32 devices in a mesh: cand: 2 (over y), gz: 4 (over x, core), yx: 4 (over z).
Axes of the slice: x: 2, y: 2, z: 4, core: 2. Of those that a mesh axis runs over, the one named last changes fastest.
Arguments:
- features: bfloat16 [128, 64, 16, 128], P(('cand', 'gz'), 'yx'), parts along dimension 0, may hold values from -20 to 20
- conv_weight: bfloat16 [3, 3, 3, 128, 128], replicated, may hold values from -0.109375 to 0.109375
- gain_mid: float32 [128], replicated, may hold values from 0.5 to 1.5
- offset_mid: float32 [128], replicated, may hold values from -3 to 3
- deep_weight: bfloat16 [3, 3, 3, 128, 256], P(None, None, None, None, 'yx'), may hold values from -0.109375 to 0.109375
- gain_deep: float32 [256], replicated, may hold values from 0.5 to 1.5
- offset_deep: float32 [256], replicated, may hold values from -3 to 3
- up_weight: bfloat16 [256, 128], replicated, may hold values from -0.375 to 0.375
Outputs:
- decoded: bfloat16 [128, 64, 16, 128], P(('cand', 'gz'), 'yx'), parts along dimension 0
The draws below stay inside these ranges and needn't reach their ends.
There are 2 independent parts, one for each index of `cand`. The reference program is written for one: setup_inputs(seed, part) draws one part's arguments, and reference() takes and returns one part's arrays. A program takes and returns all parts, laid end to end along the dimension named above; an argument that names none is the same for every part. Nothing has to cross between parts.
All inputs are finite; a program needn't handle non-finite values.
Results may differ from the reference program's by a relative error of at most 0.01.
Values may be sent and summed in bfloat16 or wider, within the bound.
No kernel may reach another device: no remote copies, remote signals or barrier semaphores. Data moves between devices by JAX's collectives and lax.ppermute only.
A program may use at most 64 MiB of HBM per device.

```python
import math
import jax
import jax.numpy as jnp
from jax import lax

C3 = 128
C4 = 256
GROUPS = 32
EDGE = 16
NZ = 64
TILE_ROWS = 64
N_YX = 4


def draw_features(key, part):
    key = jax.random.fold_in(key, 11)
    noise_key, scale_key = jax.random.split(key)
    full_shape = (NZ, TILE_ROWS, EDGE, C3)
    depth_pos = lax.broadcasted_iota(jnp.float32, full_shape, 0) / NZ
    tile_pos = lax.broadcasted_iota(jnp.float32, full_shape, 1) / TILE_ROWS
    rising = 1.0 + depth_pos + tile_pos
    local_scale = jnp.exp(jax.random.uniform(scale_key, (NZ, TILE_ROWS, EDGE, 1), jnp.float32, 0.0, 2.3))
    values = jnp.clip(jax.random.normal(noise_key, full_shape, jnp.float32), -4.0, 4.0)
    return (values * local_scale * rising / 6.0).astype(jnp.bfloat16)


def shard_levels(key, shape, cuts, low, top_value):
    def one(dim, shards_of):
        draws = jax.random.uniform(jax.random.fold_in(jax.random.fold_in(key, 6), dim), (shards_of,), jnp.float32, low / len(cuts), top_value / len(cuts))
        return jnp.repeat(jnp.exp(draws), shape[dim] // shards_of).reshape((-1,) + (1,) * (len(shape) - dim - 1))

    loudness = one(*cuts[0])
    for cut in cuts[1:]:
        loudness = loudness * one(*cut)
    return loudness


def scatter_about(key, dims, scale, bound, cuts=(), held_as=jnp.bfloat16):
    entries = scale * jax.random.normal(key, dims, jnp.float32)
    if cuts:
        entries = entries * shard_levels(key, dims, cuts, -0.22, 0.18)
    return jnp.clip(entries, -bound, bound).astype(held_as)


def setup_inputs(seed: int = 0, part: int = 0) -> dict:
    splits = jax.random.split(jax.random.key(seed), 9)
    part_keys = jax.random.split(jax.random.fold_in(splits[8], part), 9)
    return {
        "features": draw_features(jax.random.fold_in(jax.random.fold_in(splits[8], part), 71), part),
        "conv_weight": scatter_about(splits[1], (3, 3, 3, C3, C3), (27 * C3) ** -0.5, 0.109375),
        "gain_mid": jnp.clip(1.0 + 0.1 * jax.random.normal(splits[2], (C3,), jnp.float32), 0.5, 1.5),
        "offset_mid": scatter_about(splits[3], (C3,), 0.5, 3.0, (), jnp.float32),
        "deep_weight": scatter_about(splits[4], (3, 3, 3, C3, C4), (27 * C3) ** -0.5, 0.109375, ((4, 4),)),
        "gain_deep": jnp.clip(1.0 + 0.1 * jax.random.normal(splits[5], (C4,), jnp.float32), 0.5, 1.5),
        "offset_deep": scatter_about(splits[6], (C4,), 0.5, 3.0, (), jnp.float32),
        "up_weight": scatter_about(splits[7], (C4, C3), C4 ** -0.5, 0.375),
    }


EPSILON = 1e-05
LAYOUT = ('NDHWC', 'DHWIO', 'NDHWC')

def to_grid(tiled):
    side_count = math.isqrt(N_YX)
    depth_len, tile_rows, edge_len, channels = tiled.shape
    shaped = tiled.reshape(depth_len, side_count, side_count, edge_len, edge_len, channels)
    return shaped.transpose(0, 1, 3, 2, 4, 5).reshape(depth_len, side_count * edge_len, side_count * edge_len, channels)

def to_tiles(field_grid):
    side_count = math.isqrt(N_YX)
    depth_len, span_y, span_x, channels = field_grid.shape
    edge_len = span_y // side_count
    shaped = field_grid.reshape(depth_len, side_count, edge_len, side_count, edge_len, channels)
    return shaped.transpose(0, 1, 3, 2, 4, 5).reshape(depth_len, side_count * side_count * edge_len, edge_len, channels)

def convolve_same(field_grid, weight):
    result = lax.conv_general_dilated(field_grid[None], weight, (1, 1, 1), ((1, 1), (1, 1), (1, 1)), dimension_numbers=LAYOUT, preferred_element_type=jnp.float32)
    return result[0]

def group_norm(values, gain, offset_term):
    channels = values.shape[-1]
    flat = values.reshape(-1, channels)
    width = channels // GROUPS
    count = flat.shape[0] * width
    mean_value = lax.optimization_barrier(jnp.sum(flat, axis=0)).reshape(GROUPS, width).sum(axis=1) / count
    centered = flat - jnp.repeat(mean_value, width)
    spread = lax.optimization_barrier(jnp.sum(centered * centered, axis=0)).reshape(GROUPS, width).sum(axis=1) / count
    scaled = centered * jnp.repeat(lax.rsqrt(spread + EPSILON), width)
    return jax.nn.silu(scaled.reshape(values.shape) * gain + offset_term).astype(jnp.bfloat16)

def reference(features, conv_weight, gain_mid, offset_mid, deep_weight, gain_deep, offset_deep, up_weight):
    field_grid = to_grid(features)
    mid_out = group_norm(convolve_same(field_grid, conv_weight), gain_mid, offset_mid)
    depth_len, span_y, span_x, channels = mid_out.shape
    pooled = mid_out.astype(jnp.float32).reshape(depth_len // 2, 2, span_y // 2, 2, span_x // 2, 2, channels)
    pooled = pooled.mean(axis=(1, 3, 5)).astype(jnp.bfloat16)
    deep_out = group_norm(convolve_same(pooled, deep_weight), gain_deep, offset_deep)
    lifted = jnp.dot(deep_out.reshape(-1, C4), up_weight, preferred_element_type=jnp.float32)
    lifted = lifted.reshape(depth_len // 2, span_y // 2, span_x // 2, channels)
    widened = jnp.repeat(jnp.repeat(jnp.repeat(lifted, 2, axis=0), 2, axis=1), 2, axis=2)
    decoded = (mid_out.astype(jnp.float32) + widened).astype(jnp.bfloat16)
    return to_tiles(decoded)
```

```python
import math

import jax
import jax.numpy as jnp
from jax import lax
from jax.sharding import PartitionSpec as P

GROUPS = 32


EPSILON = 1e-05
LAYOUT = ("NDHWC", "DHWIO", "NDHWC")
PART = ("gz", "yx")


def send(block, axis, distance):
    size = lax.axis_size(axis)
    route = [(i, i + distance) for i in range(size) if 0 <= i + distance < size]
    return lax.ppermute(block, axis, route)


def convolve(padded, weight):
    result = lax.conv_general_dilated(
        padded[None],
        weight,
        (1, 1, 1),
        "VALID",
        dimension_numbers=LAYOUT,
        preferred_element_type=jnp.float32,
    )
    return result[0]


def extend_depth(volume):
    before = send(volume[-1:], "gz", 1)
    after = send(volume[:1], "gz", -1)
    return jnp.concatenate([before, volume, after], axis=0)


def plane_sides(low, high, place, stride, side):
    if side == 2:
        route = [(i, i + stride if (i // stride) % 2 == 0 else i - stride) for i in range(4)]
        got = lax.ppermute(jnp.where(place == 0, high, low), "yx", route)
        none = jnp.zeros_like(got)
        return jnp.where(place == 1, got, none), jnp.where(place == 0, got, none)
    before, after = send(high, "yx", stride), send(low, "yx", -stride)
    none = jnp.zeros_like(before)
    return jnp.where(place > 0, before, none), jnp.where(place < side - 1, after, none)


def extend_plane(volume):
    side = math.isqrt(lax.axis_size("yx"))
    tile = lax.axis_index("yx")
    for dim, stride, place in ((1, side, tile // side), (2, 1, tile % side)):
        length = volume.shape[dim]
        high = lax.slice_in_dim(volume, length - 1, length, axis=dim)
        low = lax.slice_in_dim(volume, 0, 1, axis=dim)
        before, after = plane_sides(low, high, place, stride, side)
        volume = jnp.concatenate([before, volume, after], axis=dim)
    return volume


def group_norm(values, gain, offset_term, width):
    channels = values.shape[-1]
    flat = values.reshape(-1, channels)
    rows = flat.shape[0]
    devices = lax.axis_size("gz") * lax.axis_size("yx")
    mean = jnp.sum(flat, axis=0) / rows
    spread = jnp.sum(jnp.square(flat - mean), axis=0)
    mine = jnp.stack([mean, spread])
    every = lax.all_to_all(jnp.broadcast_to(mine[None], (devices, 2, channels)), PART, 0, 0)
    means = every[:, 0].reshape(devices, -1, width)
    mean = means.mean(axis=(0, 2))
    total = every[:, 1].reshape(devices, -1, width).sum(axis=(0, 2))
    total = total + rows * jnp.square(means - mean[:, None]).sum(axis=(0, 2))
    scale = lax.rsqrt(total / (rows * devices * width) + EPSILON)
    scaled = (flat - jnp.repeat(mean, width)) * jnp.repeat(scale, width)
    return jax.nn.silu(scaled.reshape(values.shape) * gain + offset_term).astype(jnp.bfloat16)


def whole_kernel(weight):
    n = lax.axis_size("yx")
    shards = [weight]
    for k in range(1, n):
        shards.append(lax.ppermute(weight, "yx", [(i, (i + k) % n) for i in range(n)]))
    stack = jnp.stack(shards)
    order = (lax.axis_index("yx") - jnp.arange(n)) % n
    stack = jnp.take(stack, order, axis=0)
    return jnp.moveaxis(stack, 0, 4).reshape(weight.shape[:4] + (n * weight.shape[4],))


def body(
    features, conv_weight, gain_mid, offset_mid, deep_weight, gain_deep, offset_deep, up_weight
):
    edge_len = features.shape[0]
    channels = features.shape[3]
    deep_channels = gain_deep.shape[0]
    padded = extend_plane(extend_depth(features))
    full_kernel = whole_kernel(deep_weight)
    mid_act = convolve(padded, conv_weight)
    mid_out = group_norm(mid_act, gain_mid, offset_mid, channels // GROUPS)
    half_edge = edge_len // 2
    pooled = mid_out.astype(jnp.float32).reshape(half_edge, 2, half_edge, 2, half_edge, 2, channels)
    pooled = pooled.mean(axis=(1, 3, 5)).astype(jnp.bfloat16)
    deep_padded = extend_plane(extend_depth(pooled))
    deep_act = convolve(deep_padded, full_kernel)
    deep_out = group_norm(deep_act, gain_deep, offset_deep, deep_channels // GROUPS)
    lifted = jnp.dot(
        deep_out.reshape(-1, deep_channels), up_weight, preferred_element_type=jnp.float32
    )
    lifted = lifted.reshape(half_edge, half_edge, half_edge, channels)
    widened = jnp.broadcast_to(
        lifted[:, None, :, None, :, None, :], (half_edge, 2, half_edge, 2, half_edge, 2, channels)
    )
    widened = widened.reshape(edge_len, edge_len, edge_len, channels)
    return (mid_out.astype(jnp.float32) + widened).astype(jnp.bfloat16)


def solution(mesh):
    placed = (
        P(("cand", "gz"), "yx", None, None),
        P(),
        P(),
        P(),
        P(None, None, None, None, "yx"),
        P(),
        P(),
        P(),
    )
    return jax.shard_map(
        body,
        mesh=mesh,
        in_specs=placed,
        out_specs=P(("cand", "gz"), "yx", None, None),
        check_vma=False,
    )
```

```python
import functools
import math

import jax
import jax.numpy as jnp
from jax import lax
from jax.experimental import pallas as pl
from jax.experimental.pallas import tpu as pltpu
from jax.sharding import PartitionSpec as P

GROUPS = 32
EPSILON = 1e-05
PART = ("gz", "yx")
VMEM_BYTES = 32 * 1024 * 1024
HIGHEST = lax.Precision.HIGHEST


class Square:
    def __init__(self):
        self.tiles = lax.axis_size("yx")
        self.side = math.isqrt(self.tiles)
        tile = lax.axis_index("yx")
        self.row, self.column = tile // self.side, tile % self.side
        self.folded = self.side == 2
        self.steps = (0,) if self.folded else (-1, 1)

    def low_sides(self):
        if self.folded:
            return [self.row], [self.column]
        return [1, 0], [1, 0]

    def route(self, down, right):
        pairs = []
        for tile in range(self.tiles):
            row, column = tile // self.side + down, tile % self.side + right
            if 0 <= row < self.side and 0 <= column < self.side:
                pairs.append((tile, row * self.side + column))
        return pairs

    def swap_route(self, mask):
        return [(tile, tile ^ mask) for tile in range(self.tiles)]

    def halos(self, y_edges, x_edges, corners):
        if self.folded:
            y = lax.ppermute(y_edges[0], "yx", self.swap_route(2))
            x = lax.ppermute(x_edges[0], "yx", self.swap_route(1))
            corner = lax.ppermute(corners[0], "yx", self.swap_route(3))
            return [y], [x], [corner]
        y = [lax.ppermute(y_edges[k], "yx", self.route((1, -1)[1 - k], 0)) for k in (1, 0)]
        x = [lax.ppermute(x_edges[k], "yx", self.route(0, (1, -1)[1 - k])) for k in (1, 0)]
        corner = [
            lax.ppermute(corners[2 * k + j], "yx", self.route((1, -1)[1 - k], (1, -1)[1 - j]))
            for k in (1, 0)
            for j in (1, 0)
        ]
        return y, x, corner

    def edges(self, volume):
        if self.folded:
            low_y, low_x = self.row == 1, self.column == 1
            y = jnp.where(low_y, volume[:, 0], volume[:, -1])
            x = jnp.where(low_x, volume[:, :, 0], volume[:, :, -1])
            corner = jnp.where(low_x, y[:, 0], y[:, -1])
            return [y], [x], [corner]
        y = [volume[:, 0], volume[:, -1]]
        x = [volume[:, :, 0], volume[:, :, -1]]
        return y, x, [row[:, k] for row in y for k in (0, -1)]


def swap_depth(low, high):
    size = lax.axis_size("gz")
    up = [(i, i + 1) for i in range(size - 1)]
    return lax.ppermute(high, "gz", up), lax.ppermute(low, "gz", [(j, i) for i, j in up])


def depth_face(volume, y, x, corner, at):
    edge, channels = volume.shape[2:]
    pad = jnp.zeros((edge - len(corner), channels), volume.dtype)
    last = jnp.concatenate([piece[at][None] for piece in corner] + [pad])
    rows = [volume[at]] + [piece[at][None] for piece in y + x] + [last[None]]
    return jnp.concatenate(rows)


def gather_shards(weight):
    tiles = lax.axis_size("yx")
    half = weight.shape[1] // 2
    odd = lax.axis_index("gz") % 2
    mine = weight
    if half % 16 == 0:
        mine = jnp.where(odd == 1, weight[:, half:], weight[:, :half])
    got = [
        lax.ppermute(mine, "yx", [(i, (i + k) % tiles) for i in range(tiles)]) for k in range(1, tiles)
    ]
    return got


def swap_halves(got, whole):
    if whole:
        return got
    pairs = [(i, i ^ 1) for i in range(lax.axis_size("gz"))]
    return lax.ppermute(got, "gz", pairs)


def share(statistics):
    return lax.all_to_all(statistics, PART, 0, 0)


def call(kernel, outs, scratch, scalars, *arrays, flops=0, nbytes=0):
    smem, vmem = pl.BlockSpec(memory_space=pltpu.SMEM), pl.BlockSpec(memory_space=pltpu.VMEM)
    return pl.pallas_call(
        kernel,
        out_shape=[jax.ShapeDtypeStruct(shape, dtype) for shape, dtype in outs],
        in_specs=[smem] + [vmem] * len(arrays),
        out_specs=[vmem] * len(outs),
        scratch_shapes=[pltpu.VMEM(shape, dtype) for shape, dtype in scratch],
        compiler_params=pltpu.CompilerParams(vmem_limit_bytes=VMEM_BYTES),
        cost_estimate=pl.CostEstimate(flops=flops, bytes_accessed=nbytes, transcendentals=0),
    )(scalars, *arrays)


def mid_kernel(ny, nx, pos, x, *refs):
    y_halos, x_halos, corners = refs[0], refs[1], refs[2]
    front, back, weight, act, stats, grid, taps, column, flanks = refs[3:]
    edge = x.shape[0]
    f32 = jnp.float32
    for dz in range(3):
        for dy in range(3):
            row = (dz * 3 + dy) * 128
            for dx in range(3):
                taps[row : row + 128, dx * 128 : dx * 128 + 128] = weight[dz * 9 + dy * 3 + dx]
    grid[1 : edge + 1, 1 : edge + 1] = x[...]
    grid[0, 1 : edge + 1] = front[0:edge]
    grid[edge + 1, 1 : edge + 1] = back[0:edge]
    blank = jnp.zeros((edge + 2,) + grid.shape[2:], grid.dtype)
    grid[:, 0] = blank
    grid[:, edge + 1] = blank
    for i in range(ny):
        at = jnp.where(pos[i] == 1, 0, edge + 1)
        grid[1 : edge + 1, at] = y_halos[i]
        grid[0, at] = front[edge + i]
        grid[edge + 1, at] = back[edge + i]

    act[...] = jnp.zeros(act.shape, f32)
    flat = act.reshape(edge**3, 128)
    for j in range(nx):
        column[:, 0:8] = jnp.zeros((edge + 2, 8, 128), f32)
        column[:, 8 + edge :] = jnp.zeros((edge + 2, 8, 128), f32)
        column[1 : edge + 1, 8 : 8 + edge] = x_halos[j].astype(f32)
        column[0, 8 : 8 + edge] = front[edge + ny + j].astype(f32)
        column[edge + 1, 8 : 8 + edge] = back[edge + ny + j].astype(f32)
        rows = edge + 16
        lines = column.reshape((edge + 2) * rows, 128)
        for i in range(ny):
            k = i * nx + j
            ends = [front[edge + ny + nx, k : k + 1], corners[k], back[edge + ny + nx, k : k + 1]]
            ends = jnp.concatenate([e.astype(f32) for e in ends], axis=0)
            low = pos[i] == 1
            if ny == 1:
                lines[pl.ds(7, edge + 2, stride=rows), :] = jnp.where(low, ends, 0.0)
                lines[pl.ds(8 + edge, edge + 2, stride=rows), :] = jnp.where(low, 0.0, ends)
            else:
                lines[pl.ds(7 if i == 0 else 8 + edge, edge + 2, stride=rows), :] = ends
        for dy in range(3):
            piece = column[:, 7 + dy : 7 + dy + edge].astype(jnp.bfloat16)
            flanks[:, :, dy * 128 : dy * 128 + 128] = piece
        left = jnp.concatenate(
            [flanks[dz : dz + edge].reshape(edge * edge, 384) for dz in range(3)], axis=1
        )
        right = jnp.concatenate([taps[:, 0:128], taps[:, 256:384]], axis=1)
        extra = jnp.dot(left, right, preferred_element_type=f32)
        low = pos[ny + j] == 1
        if nx == 1:
            flat[pl.ds(0, edge * edge, stride=edge), :] = jnp.where(low, extra[:, :128], 0.0)
            flat[pl.ds(edge - 1, edge * edge, stride=edge), :] = jnp.where(low, 0.0, extra[:, 128:])
        elif j == 0:
            flat[pl.ds(0, edge * edge, stride=edge), :] = extra[:, :128]
        else:
            flat[pl.ds(edge - 1, edge * edge, stride=edge), :] = extra[:, 128:]

    planes = 2
    rows = planes * edge * edge
    place = lax.broadcasted_iota(jnp.int32, (planes * edge, edge, 128), 1)

    def step(k, carry):
        z = k * planes
        left = jnp.concatenate(
            [
                grid[pl.ds(z + dz, planes), dy : dy + edge].reshape(rows, 128)
                for dz in range(3)
                for dy in range(3)
            ],
            axis=1,
        )
        wide = jnp.dot(left, taps[...], preferred_element_type=f32)
        wide = wide.reshape(planes * edge, edge, 384)
        after = jnp.where(place > 0, pltpu.roll(wide[:, :, :128], 1, 1), 0.0)
        before = jnp.where(place < edge - 1, pltpu.roll(wide[:, :, 256:], edge - 1, 1), 0.0)
        old = act[pl.ds(z, planes)].reshape(planes * edge, edge, 128)
        new = old + wide[:, :, 128:256] + after + before
        act[pl.ds(z, planes)] = new.reshape(planes, edge, edge, 128)
        return carry + jnp.sum(new.reshape(rows // 8, 8, 128), axis=0)

    total = lax.fori_loop(0, edge // planes, step, jnp.zeros((8, 128), f32))
    mean = jnp.sum(total, axis=0, keepdims=True) / edge**3

    def spread_step(k, carry):
        off = act[pl.ds(k * planes, planes)].reshape(rows // 8, 8, 128) - mean
        return carry + jnp.sum(off * off, axis=0)

    total = lax.fori_loop(0, edge // planes, spread_step, jnp.zeros((8, 128), f32))
    spread = jnp.sum(total, axis=0, keepdims=True)
    put_stats(stats, mean, spread)


def put_stats(stats, mean, spread):
    line = lax.broadcasted_iota(jnp.int32, stats.shape[1:], 0)
    both = jnp.where(line == 0, mean, spread)
    stats[...] = jnp.broadcast_to(both[None], stats.shape)


def read_stats(stats, rows):
    devices, _, channels = stats.shape
    width = channels // GROUPS
    means = stats[:, 0, :]
    spreads = stats[:, 1, :]
    line = lax.broadcasted_iota(jnp.int32, (channels, channels), 0) // width
    same = line == lax.broadcasted_iota(jnp.int32, (channels, channels), 1) // width
    same = same.astype(jnp.float32)

    def grouped(row):
        row = jnp.broadcast_to(row, (8, channels))
        return jnp.dot(row, same, precision=HIGHEST, preferred_element_type=jnp.float32)[0:1]

    mean = grouped(jnp.sum(means, axis=0, keepdims=True)) / (devices * width)
    off = means - mean
    total = grouped(jnp.sum(spreads + rows * (off * off), axis=0, keepdims=True))
    return mean, lax.rsqrt(total / (rows * devices * width) + EPSILON)


def silu(u):
    return u / (1.0 + jnp.exp(-u))


def norm_kernel(ny, nx, pos, act, stats, gain, offset, out, pooled, *refs):
    y_edges, x_edges, corners, half, fine = refs
    edge = act.shape[0]
    deep = edge // 2
    f32 = jnp.float32
    mean, scale = read_stats(stats, float(edge**3))
    scale = scale * gain[...]
    shift = offset[...]

    def step(k, _):
        value = silu((act[pl.ds(2 * k, 2)] - mean) * scale + shift).astype(jnp.bfloat16)
        out[pl.ds(2 * k, 2)] = value
        value = value.astype(f32)
        value = value[0] + value[1]
        value = value.reshape(deep, 2, edge, 128)
        half[...] = (value[:, 0] + value[:, 1]).reshape(deep * edge, 128)
        pair = half[pl.ds(0, deep * deep, stride=2), :] + half[pl.ds(1, deep * deep, stride=2), :]
        pair = (pair * 0.125).astype(jnp.bfloat16).astype(f32)
        fine[pl.ds(k, 1)] = pair.reshape(1, deep, deep, 128)
        return 0

    lax.fori_loop(0, deep, step, 0)
    pooled[...] = fine[...]
    lines = fine.reshape(deep**3, 128)
    low, high = ((pos[0] == 1, pos[1] == 1) if ny == 1 else (None, None))
    first_x = lines[pl.ds(0, deep * deep, stride=deep), :].reshape(deep, deep, 128)
    last_x = lines[pl.ds(deep - 1, deep * deep, stride=deep), :].reshape(deep, deep, 128)
    ends = []
    for y in (0, deep - 1):
        for x in (0, deep - 1):
            ends.append(lines[pl.ds(y * deep + x, deep, stride=deep * deep), :])
    if ny == 1:
        y_edges[0] = jnp.where(low, fine[:, 0], fine[:, deep - 1])
        x_edges[0] = jnp.where(high, first_x, last_x)
        corners[0] = jnp.where(
            low, jnp.where(high, ends[0], ends[1]), jnp.where(high, ends[2], ends[3])
        )
    else:
        y_edges[0], y_edges[1] = fine[:, 0], fine[:, deep - 1]
        x_edges[0], x_edges[1] = first_x, last_x
        for k in range(4):
            corners[k] = ends[k]


def deep_kernel(ny, nx, tiles, pos, pooled, y_halos, x_halos, corners, front, back, own, got, partner, *refs):
    act, stats, grid, packed, kernel = refs
    deep = pooled.shape[0]
    f32 = jnp.float32
    shard = own.shape[1]
    part = shard // 2
    tile, odd = pos[ny + nx], pos[ny + nx + 1]

    def place(rows, at):
        for tap in range(27):
            lane = (tap % 9) * 128
            kernel[tap // 9, pl.ds(at, rows.shape[1]), lane : lane + 128] = rows[tap]

    place(own, pl.multiple_of(tile * shard, shard))
    for k in range(1, tiles):
        base = lax.rem(tile + tiles - k, tiles) * shard
        if got.shape[2] == shard:
            place(got.at[k - 1], pl.multiple_of(base, shard))
            continue
        place(got.at[k - 1], pl.multiple_of(base + odd * part, part))
        place(partner.at[k - 1], pl.multiple_of(base + (1 - odd) * part, part))

    grid[...] = jnp.zeros(grid.shape, f32)
    grid[1 : deep + 1, 1 : deep + 1, 8:16] = pooled[...]
    grid[0, 1 : deep + 1, 8:16] = front[0:deep]
    grid[deep + 1, 1 : deep + 1, 8:16] = back[0:deep]
    for i in range(ny):
        at = jnp.where(pos[i] == 1, 0, deep + 1)
        grid[1 : deep + 1, at, 8:16] = y_halos[i]
        grid[0, at, 8:16] = front[deep + i]
        grid[deep + 1, at, 8:16] = back[deep + i]
    for j in range(nx):
        for z in range(deep + 2):
            if z == 0:
                line, rim = front[deep + ny + j], front
            elif z == deep + 1:
                line, rim = back[deep + ny + j], back
            else:
                line, rim = x_halos[j, z - 1], None
            lines = grid.at[z].reshape((deep + 2) * 24, 128)
            left = pos[ny + j] == 1
            for side, here in ((7, left), (16, jnp.logical_not(left))):
                if nx == 2 and side != (7, 16)[j]:
                    continue
                kept = line if nx == 2 else jnp.where(here, line, 0.0)
                lines[pl.ds(24 + side, deep, stride=24), :] = kept
                for i in range(ny):
                    k = i * nx + j
                    end = corners[k, z - 1 : z] if rim is None else rim[deep + ny + nx, k : k + 1]
                    above = pos[i] == 1
                    for y, there in ((0, above), (deep + 1, jnp.logical_not(above))):
                        if ny == 2 and y != (0, deep + 1)[i]:
                            continue
                        kept = end
                        if nx == 1:
                            kept = jnp.where(jnp.logical_and(here, there), end, 0.0)
                        grid[z, y, side : side + 1] = kept

    for dx in range(3):
        plane = grid[:, :, 7 + dx : 15 + dx]
        for y in range(deep + 1):
            both = jnp.concatenate([plane[:, y], plane[:, y + 1]], axis=1)
            packed[:, y // 2, y % 2, :, dx * 128 : dx * 128 + 128] = both.astype(jnp.bfloat16)

    rows = deep**3
    total = None
    for dz in range(3):
        left = jnp.concatenate(
            [
                packed[dz : dz + deep, dy // 2 : dy // 2 + deep // 2, dy % 2].reshape(rows, 384)
                for dy in range(3)
            ],
            axis=1,
        )
        term = lax.dot_general(
            left, kernel[dz], (((1,), (1,)), ((), ())), preferred_element_type=f32
        )
        total = term if total is None else total + term
    act[...] = total
    mean = jnp.sum(total, axis=0, keepdims=True) / rows
    off = total - mean
    put_stats(stats, mean, jnp.sum(off * off, axis=0, keepdims=True))


def final_kernel(_, act, stats, gain, offset, up, mid, out, wide):
    edge = mid.shape[0]
    deep = edge // 2
    f32 = jnp.float32
    mean, scale = read_stats(stats, float(deep**3))
    value = silu((act[...] - mean) * (scale * gain[...]) + offset[...]).astype(jnp.bfloat16)
    lifted = jnp.dot(value, up[...], preferred_element_type=f32)
    rows = deep**3
    wide[pl.ds(0, rows, stride=2), :] = lifted
    wide[pl.ds(1, rows, stride=2), :] = lifted

    def step(k, _):
        size = deep * edge
        add = wide[pl.ds(pl.multiple_of(k * size, size), size), :].reshape(1, deep, 1, edge, 128)
        old = mid[pl.ds(2 * k, 2)].astype(f32).reshape(2, deep, 2, edge, 128)
        out[pl.ds(2 * k, 2)] = (old + add).astype(jnp.bfloat16).reshape(2, edge, edge, 128)
        return 0

    lax.fori_loop(0, deep, step, 0)


def body(
    features, conv_weight, gain_mid, offset_mid, deep_weight, gain_deep, offset_deep, up_weight
):
    f32, bf16 = jnp.float32, jnp.bfloat16
    edge, channels = features.shape[0], features.shape[3]
    deep = edge // 2
    deep_channels = gain_deep.shape[0]
    square = Square()
    tiles = square.tiles
    devices = lax.axis_size("gz") * tiles
    y_low, x_low = square.low_sides()
    ny, nx = len(y_low), len(x_low)
    pos = jnp.stack(
        [jnp.asarray(v, jnp.int32) for v in y_low + x_low + [lax.axis_index("yx"), lax.axis_index("gz") % 2]]
    )

    y, x, corner = square.halos(*square.edges(features))
    own = jnp.moveaxis(deep_weight, 4, 3).reshape(27, deep_weight.shape[4], deep_weight.shape[3])
    got = gather_shards(own)
    front, back = swap_depth(
        depth_face(features, y, x, corner, 0), depth_face(features, y, x, corner, -1)
    )
    act, stats = call(
        functools.partial(mid_kernel, ny, nx),
        [((edge, edge, edge, channels), f32), ((devices, 8, channels), f32)],
        [
            ((edge + 2, edge + 2, edge, channels), bf16),
            ((9 * channels, 3 * channels), bf16),
            ((edge + 2, edge + 16, channels), f32),
            ((edge + 2, edge, 3 * channels), bf16),
        ],
        pos,
        features,
        jnp.stack(y),
        jnp.stack(x),
        jnp.stack(corner),
        front,
        back,
        conv_weight.reshape(27, channels, channels),
        flops=2 * 27 * channels * channels * edge**3,
        nbytes=6 << 20,
    )
    stats, *got = lax.optimization_barrier((stats, *got))
    got = jnp.stack(got)
    partner = swap_halves(got, got.shape[2] == own.shape[1])
    stats = share(stats)
    out, pooled, *edges = call(
        functools.partial(norm_kernel, ny, nx),
        [
            ((edge, edge, edge, channels), bf16),
            ((deep, deep, deep, channels), f32),
            ((ny, deep, deep, channels), f32),
            ((nx, deep, deep, channels), f32),
            ((ny * nx, deep, channels), f32),
        ],
        [((deep * edge, channels), f32), ((deep, deep, deep, channels), f32)],
        pos,
        act,
        stats,
        gain_mid.reshape(1, channels),
        offset_mid.reshape(1, channels),
        flops=20 * channels * edge**3,
        nbytes=3 << 20,
    )
    y, x, corner = square.halos(*([piece[i] for i in range(piece.shape[0])] for piece in edges))
    front, back = swap_depth(
        depth_face(pooled, y, x, corner, 0), depth_face(pooled, y, x, corner, -1)
    )
    deep_act, stats = call(
        functools.partial(deep_kernel, ny, nx, tiles),
        [((deep**3, deep_channels), f32), ((devices, 8, deep_channels), f32)],
        [
            ((deep + 2, deep + 2, 24, channels), f32),
            ((deep + 2, deep // 2 + 1, 2, 16, 3 * channels), bf16),
            ((3, deep_channels, 9 * channels), bf16),
        ],
        pos,
        pooled,
        jnp.stack(y),
        jnp.stack(x),
        jnp.stack(corner),
        front,
        back,
        own,
        got,
        partner,
        flops=2 * 27 * channels * deep_channels * deep**3,
        nbytes=4 << 20,
    )
    stats = share(stats)
    (decoded,) = call(
        final_kernel,
        [((edge, edge, edge, channels), bf16)],
        [((2 * deep**3, channels), f32)],
        pos,
        deep_act,
        stats,
        gain_deep.reshape(1, deep_channels),
        offset_deep.reshape(1, deep_channels),
        up_weight,
        out,
        flops=4 * deep_channels * channels * deep**3,
        nbytes=3 << 20,
    )
    return decoded


def solution(mesh):
    placed = (
        P(("cand", "gz"), "yx", None, None),
        P(),
        P(),
        P(),
        P(None, None, None, None, "yx"),
        P(),
        P(),
        P(),
    )
    return jax.shard_map(
        body,
        mesh=mesh,
        in_specs=placed,
        out_specs=P(("cand", "gz"), "yx", None, None),
        check_vma=False,
    )
```

```python
import functools
import math

import jax
import jax.numpy as jnp
from jax import lax
from jax.experimental import pallas as pl
from jax.experimental.pallas import tpu as pltpu
from jax.sharding import PartitionSpec as P

GROUPS = 32
EPSILON = 1e-05
PART = ("gz", "yx")
VMEM_BYTES = 32 * 1024 * 1024
HIGHEST = lax.Precision.HIGHEST


class Square:
    def __init__(self):
        self.tiles = lax.axis_size("yx")
        self.side = math.isqrt(self.tiles)
        tile = lax.axis_index("yx")
        self.row, self.column = tile // self.side, tile % self.side
        self.folded = self.side == 2
        self.steps = (0,) if self.folded else (-1, 1)

    def low_sides(self):
        if self.folded:
            return [self.row], [self.column]
        return [1, 0], [1, 0]

    def route(self, down, right):
        pairs = []
        for tile in range(self.tiles):
            row, column = tile // self.side + down, tile % self.side + right
            if 0 <= row < self.side and 0 <= column < self.side:
                pairs.append((tile, row * self.side + column))
        return pairs

    def swap_route(self, mask):
        return [(tile, tile ^ mask) for tile in range(self.tiles)]

    def halos(self, y_edges, x_edges, corners):
        if self.folded:
            y = lax.ppermute(y_edges[0], "yx", self.swap_route(2))
            x = lax.ppermute(x_edges[0], "yx", self.swap_route(1))
            corner = lax.ppermute(corners[0], "yx", self.swap_route(3))
            return [y], [x], [corner]
        y = [lax.ppermute(y_edges[k], "yx", self.route((1, -1)[1 - k], 0)) for k in (1, 0)]
        x = [lax.ppermute(x_edges[k], "yx", self.route(0, (1, -1)[1 - k])) for k in (1, 0)]
        corner = [
            lax.ppermute(corners[2 * k + j], "yx", self.route((1, -1)[1 - k], (1, -1)[1 - j]))
            for k in (1, 0)
            for j in (1, 0)
        ]
        return y, x, corner

    def edges(self, volume):
        if self.folded:
            low_y, low_x = self.row == 1, self.column == 1
            y = jnp.where(low_y, volume[:, 0], volume[:, -1])
            x = jnp.where(low_x, volume[:, :, 0], volume[:, :, -1])
            corner = jnp.where(low_x, y[:, 0], y[:, -1])
            return [y], [x], [corner]
        y = [volume[:, 0], volume[:, -1]]
        x = [volume[:, :, 0], volume[:, :, -1]]
        return y, x, [row[:, k] for row in y for k in (0, -1)]


def swap_depth(low, high):
    size = lax.axis_size("gz")
    up = [(i, i + 1) for i in range(size - 1)]
    return lax.ppermute(high, "gz", up), lax.ppermute(low, "gz", [(j, i) for i, j in up])


def depth_face(volume, y, x, corner, at):
    edge, channels = volume.shape[2:]
    pad = jnp.zeros((edge - len(corner), channels), volume.dtype)
    last = jnp.concatenate([piece[at][None] for piece in corner] + [pad])
    rows = [volume[at]] + [piece[at][None] for piece in y + x] + [last[None]]
    return jnp.concatenate(rows)


def gather_shards(weight):
    depth = lax.axis_size("gz")
    part = weight.shape[1] // depth
    if part % 16:
        return lax.all_gather(weight, "yx")
    mine = lax.dynamic_slice_in_dim(weight, lax.axis_index("gz") * part, part, axis=1)
    return lax.all_gather(mine, PART)


def share(statistics):
    return lax.all_to_all(statistics, PART, 0, 0)


def share_by_axis(statistics):
    tiles = lax.all_to_all(statistics, "yx", 0, 0)
    depth = lax.axis_size("gz")
    every = lax.all_to_all(jnp.broadcast_to(tiles[None], (depth,) + tiles.shape), "gz", 0, 0)
    return every.reshape((-1,) + statistics.shape[1:])


def call(kernel, outs, scratch, scalars, *arrays, flops=0, nbytes=0):
    smem, vmem = pl.BlockSpec(memory_space=pltpu.SMEM), pl.BlockSpec(memory_space=pltpu.VMEM)
    return pl.pallas_call(
        kernel,
        out_shape=[jax.ShapeDtypeStruct(shape, dtype) for shape, dtype in outs],
        in_specs=[smem] + [vmem] * len(arrays),
        out_specs=[vmem] * len(outs),
        scratch_shapes=[pltpu.VMEM(shape, dtype) for shape, dtype in scratch],
        compiler_params=pltpu.CompilerParams(vmem_limit_bytes=VMEM_BYTES),
        cost_estimate=pl.CostEstimate(flops=flops, bytes_accessed=nbytes, transcendentals=0),
    )(scalars, *arrays)


def spread_taps(weight, taps):
    for tap in range(27):
        row, lane = tap // 3 * 128, tap % 3 * 128
        taps[row : row + 128, lane : lane + 128] = weight[tap]


def join_x(wide, edge):
    place = lax.broadcasted_iota(jnp.int32, wide.shape[:2] + (128,), 1)
    after = jnp.where(place > 0, pltpu.roll(wide[:, :, :128], 1, 1), 0.0)
    before = jnp.where(place < edge - 1, pltpu.roll(wide[:, :, 256:], edge - 1, 1), 0.0)
    return wide[:, :, 128:256] + after + before


def local_planes(x, lo, count, taps, grid, act):
    edge = x.shape[0]
    blank = jnp.zeros((count + 2,) + grid.shape[2:], grid.dtype)
    grid[:, 0] = blank
    grid[:, edge + 1] = blank
    first, last = max(lo - 1, 0), min(lo + count + 1, edge)
    if first > lo - 1:
        grid[0] = jnp.zeros(grid.shape[1:], grid.dtype)
    if last < lo + count + 1:
        grid[count + 1] = jnp.zeros(grid.shape[1:], grid.dtype)
    grid[first - lo + 1 : last - lo + 1, 1 : edge + 1] = x[first:last]
    planes = 2
    rows = planes * edge * edge
    for z in range(0, count, planes):
        left = jnp.concatenate(
            [
                grid[z + dz : z + dz + planes, dy : dy + edge].reshape(rows, 128)
                for dz in range(3)
                for dy in range(3)
            ],
            axis=1,
        )
        wide = jnp.dot(left, taps[...], preferred_element_type=jnp.float32)
        new = join_x(wide.reshape(planes * edge, edge, 384), edge)
        act[z : z + planes] = new.reshape(planes, edge, edge, 128)


def front_half_kernel(_, x, weight, act, taps, grid):
    spread_taps(weight, taps)
    local_planes(x, 0, act.shape[0], taps, grid, act)


def back_half_kernel(_, x, taps, after, act, grid):
    del after
    local_planes(x, x.shape[0] - act.shape[0], act.shape[0], taps, grid, act)


def rim_kernel(ny, nx, pos, *refs):
    near, far, y_halos, x_halos, corners, front, back, taps, act, stats, column, flanks = refs
    edge = act.shape[0]
    half = edge // 2
    f32, bf16 = jnp.float32, jnp.bfloat16
    act[0:half] = near[...]
    act[half:edge] = far[...]
    flat = act.reshape(edge**3, 128)

    for plane, face, dz in ((0, front, 0), (edge - 1, back, 2)):
        inner = face[0:edge]
        blank = jnp.zeros((1, edge, 128), bf16)
        lines = [
            jnp.concatenate([blank, inner[: edge - 1]], axis=0),
            inner,
            jnp.concatenate([inner[1:], blank], axis=0),
        ]
        left = jnp.concatenate([line.reshape(edge * edge, 128) for line in lines], axis=1)
        wide = jnp.dot(left, taps[dz * 384 : dz * 384 + 384, :], preferred_element_type=f32)
        act[plane] += join_x(wide.reshape(edge, edge, 384), edge)

    for i in range(ny):
        low = pos[i] == 1
        inner = y_halos[i]
        ends = [front[edge + i][None], back[edge + i][None]]
        lines = [
            jnp.concatenate([ends[0], inner[: edge - 1]], axis=0),
            inner,
            jnp.concatenate([inner[1:], ends[1]], axis=0),
        ]
        left = jnp.concatenate([line.reshape(edge * edge, 128) for line in lines], axis=1)
        start = jnp.where(low, 0, 256)
        right = jnp.concatenate(
            [taps[pl.ds(pl.multiple_of(start + dz * 384, 128), 128), :] for dz in range(3)], axis=0
        )
        wide = jnp.dot(left, right, preferred_element_type=f32)
        act[:, jnp.where(low, 0, edge - 1)] += join_x(wide.reshape(edge, edge, 384), edge)

    for j in range(nx):
        column[:, 0:8] = jnp.zeros((edge + 2, 8, 128), f32)
        column[:, 8 + edge :] = jnp.zeros((edge + 2, 8, 128), f32)
        column[1 : edge + 1, 8 : 8 + edge] = x_halos[j].astype(f32)
        column[0, 8 : 8 + edge] = front[edge + ny + j].astype(f32)
        column[edge + 1, 8 : 8 + edge] = back[edge + ny + j].astype(f32)
        rows = edge + 16
        lines = column.reshape((edge + 2) * rows, 128)
        for i in range(ny):
            k = i * nx + j
            ends = [front[edge + ny + nx, k : k + 1], corners[k], back[edge + ny + nx, k : k + 1]]
            ends = jnp.concatenate([e.astype(f32) for e in ends], axis=0)
            low = pos[i] == 1
            if ny == 1:
                lines[pl.ds(7, edge + 2, stride=rows), :] = jnp.where(low, ends, 0.0)
                lines[pl.ds(8 + edge, edge + 2, stride=rows), :] = jnp.where(low, 0.0, ends)
            else:
                lines[pl.ds(7 if i == 0 else 8 + edge, edge + 2, stride=rows), :] = ends
        for dy in range(3):
            piece = column[:, 7 + dy : 7 + dy + edge].astype(bf16)
            flanks[:, :, dy * 128 : dy * 128 + 128] = piece
        left = jnp.concatenate(
            [flanks[dz : dz + edge].reshape(edge * edge, 384) for dz in range(3)], axis=1
        )
        right = jnp.concatenate([taps[:, 0:128], taps[:, 256:384]], axis=1)
        extra = jnp.dot(left, right, preferred_element_type=f32)
        low = pos[ny + j] == 1
        first, last = extra[:, :128], extra[:, 128:]
        if nx == 1:
            first, last = jnp.where(low, first, 0.0), jnp.where(low, 0.0, last)
        if nx == 1 or j == 0:
            flat[pl.ds(0, edge * edge, stride=edge), :] += first
        if nx == 1 or j == 1:
            flat[pl.ds(edge - 1, edge * edge, stride=edge), :] += last

    def sum_step(k, carry):
        return carry + jnp.sum(act[k].reshape(edge * 2, 8, 128), axis=0)

    total = lax.fori_loop(0, edge, sum_step, jnp.zeros((8, 128), f32), unroll=4)
    mean = jnp.sum(total, axis=0, keepdims=True) / edge**3

    def spread_step(k, carry):
        off = act[k].reshape(edge * 2, 8, 128) - mean
        return carry + jnp.sum(off * off, axis=0)

    total = lax.fori_loop(0, edge, spread_step, jnp.zeros((8, 128), f32), unroll=4)
    put_stats(stats, mean, jnp.sum(total, axis=0, keepdims=True))


def put_stats(stats, mean, spread):
    line = lax.broadcasted_iota(jnp.int32, stats.shape[1:], 0)
    both = jnp.where(line == 0, mean, spread)
    stats[...] = jnp.broadcast_to(both[None], stats.shape)


def read_stats(stats, rows):
    devices, _, channels = stats.shape
    width = channels // GROUPS
    means = stats[:, 0, :]
    spreads = stats[:, 1, :]
    line = lax.broadcasted_iota(jnp.int32, (channels, channels), 0) // width
    same = line == lax.broadcasted_iota(jnp.int32, (channels, channels), 1) // width
    same = same.astype(jnp.float32)

    def grouped(row):
        row = jnp.broadcast_to(row, (8, channels))
        return jnp.dot(row, same, precision=HIGHEST, preferred_element_type=jnp.float32)[0:1]

    mean = grouped(jnp.sum(means, axis=0, keepdims=True)) / (devices * width)
    off = means - mean
    total = grouped(jnp.sum(spreads + rows * (off * off), axis=0, keepdims=True))
    return mean, lax.rsqrt(total / (rows * devices * width) + EPSILON)


def silu_of_double(h):
    return h + h * jnp.tanh(h)


def norm_kernel(ny, nx, pos, act, stats, gain, offset, out, pooled, *refs):
    y_edges, x_edges, corners, half, fine = refs
    edge = act.shape[0]
    deep = edge // 2
    f32 = jnp.float32
    mean, scale = read_stats(stats, float(edge**3))
    scale = scale * (0.5 * gain[...])
    shift = 0.5 * offset[...]

    def step(k, _):
        value = silu_of_double((act[pl.ds(2 * k, 2)] - mean) * scale + shift).astype(jnp.bfloat16)
        out[pl.ds(2 * k, 2)] = value
        value = value.astype(f32)
        value = value[0] + value[1]
        value = value.reshape(deep, 2, edge, 128)
        half[...] = (value[:, 0] + value[:, 1]).reshape(deep * edge, 128)
        pair = half[pl.ds(0, deep * deep, stride=2), :] + half[pl.ds(1, deep * deep, stride=2), :]
        pair = (pair * 0.125).astype(jnp.bfloat16).astype(f32)
        fine[pl.ds(k, 1)] = pair.reshape(1, deep, deep, 128)
        return 0

    lax.fori_loop(0, deep, step, 0)
    pooled[...] = fine[...]
    lines = fine.reshape(deep**3, 128)
    low, high = ((pos[0] == 1, pos[1] == 1) if ny == 1 else (None, None))
    first_x = lines[pl.ds(0, deep * deep, stride=deep), :].reshape(deep, deep, 128)
    last_x = lines[pl.ds(deep - 1, deep * deep, stride=deep), :].reshape(deep, deep, 128)
    ends = []
    for y in (0, deep - 1):
        for x in (0, deep - 1):
            ends.append(lines[pl.ds(y * deep + x, deep, stride=deep * deep), :])
    if ny == 1:
        y_edges[0] = jnp.where(low, fine[:, 0], fine[:, deep - 1])
        x_edges[0] = jnp.where(high, first_x, last_x)
        corners[0] = jnp.where(
            low, jnp.where(high, ends[0], ends[1]), jnp.where(high, ends[2], ends[3])
        )
    else:
        y_edges[0], y_edges[1] = fine[:, 0], fine[:, deep - 1]
        x_edges[0], x_edges[1] = first_x, last_x
        for k in range(4):
            corners[k] = ends[k]


def place_kernel(tiles, _, got, after, kernel):
    del after
    pieces, _, part, _ = got.shape
    for i in range(pieces):
        at = (i % tiles * (pieces // tiles) + i // tiles) * part
        for tap in range(27):
            lane = tap % 9 * 128
            kernel[tap // 9, at : at + part, lane : lane + 128] = got[i, tap]


def deep_kernel(ny, nx, pos, pooled, y_halos, x_halos, corners, front, back, kernel, *refs):
    act, stats, grid, packed = refs
    deep = pooled.shape[0]
    f32 = jnp.float32
    grid[...] = jnp.zeros(grid.shape, f32)
    grid[1 : deep + 1, 1 : deep + 1, 8:16] = pooled[...]
    grid[0, 1 : deep + 1, 8:16] = front[0:deep]
    grid[deep + 1, 1 : deep + 1, 8:16] = back[0:deep]
    for i in range(ny):
        at = jnp.where(pos[i] == 1, 0, deep + 1)
        grid[1 : deep + 1, at, 8:16] = y_halos[i]
        grid[0, at, 8:16] = front[deep + i]
        grid[deep + 1, at, 8:16] = back[deep + i]
    for j in range(nx):
        for z in range(deep + 2):
            if z == 0:
                line, rim = front[deep + ny + j], front
            elif z == deep + 1:
                line, rim = back[deep + ny + j], back
            else:
                line, rim = x_halos[j, z - 1], None
            lines = grid.at[z].reshape((deep + 2) * 24, 128)
            left = pos[ny + j] == 1
            for side, here in ((7, left), (16, jnp.logical_not(left))):
                if nx == 2 and side != (7, 16)[j]:
                    continue
                kept = line if nx == 2 else jnp.where(here, line, 0.0)
                lines[pl.ds(24 + side, deep, stride=24), :] = kept
                for i in range(ny):
                    k = i * nx + j
                    end = corners[k, z - 1 : z] if rim is None else rim[deep + ny + nx, k : k + 1]
                    above = pos[i] == 1
                    for y, there in ((0, above), (deep + 1, jnp.logical_not(above))):
                        if ny == 2 and y != (0, deep + 1)[i]:
                            continue
                        kept = end
                        if nx == 1:
                            kept = jnp.where(jnp.logical_and(here, there), end, 0.0)
                        grid[z, y, side : side + 1] = kept

    for dx in range(3):
        plane = grid[:, :, 7 + dx : 15 + dx]
        for y in range(deep + 1):
            both = jnp.concatenate([plane[:, y], plane[:, y + 1]], axis=1)
            packed[:, y // 2, y % 2, :, dx * 128 : dx * 128 + 128] = both.astype(jnp.bfloat16)

    rows = deep**3
    total = None
    for dz in range(3):
        left = jnp.concatenate(
            [
                packed[dz : dz + deep, dy // 2 : dy // 2 + deep // 2, dy % 2].reshape(rows, 384)
                for dy in range(3)
            ],
            axis=1,
        )
        term = lax.dot_general(
            left, kernel[dz], (((1,), (1,)), ((), ())), preferred_element_type=f32
        )
        total = term if total is None else total + term
    act[...] = total
    mean = jnp.sum(total, axis=0, keepdims=True) / rows
    off = total - mean
    put_stats(stats, mean, jnp.sum(off * off, axis=0, keepdims=True))


def final_kernel(_, act, stats, gain, offset, up, mid, out, wide):
    edge = mid.shape[0]
    deep = edge // 2
    f32 = jnp.float32
    mean, scale = read_stats(stats, float(deep**3))
    scale = scale * (0.5 * gain[...])
    value = silu_of_double((act[...] - mean) * scale + 0.5 * offset[...]).astype(jnp.bfloat16)
    lifted = jnp.dot(value, up[...], preferred_element_type=f32)
    rows = deep**3
    wide[pl.ds(0, rows, stride=2), :] = lifted
    wide[pl.ds(1, rows, stride=2), :] = lifted

    def step(k, _):
        size = deep * edge
        add = wide[pl.ds(pl.multiple_of(k * size, size), size), :].reshape(1, deep, 1, edge, 128)
        old = mid[pl.ds(2 * k, 2)].astype(f32).reshape(2, deep, 2, edge, 128)
        out[pl.ds(2 * k, 2)] = (old + add).astype(jnp.bfloat16).reshape(2, edge, edge, 128)
        return 0

    lax.fori_loop(0, deep, step, 0)


def body(
    features, conv_weight, gain_mid, offset_mid, deep_weight, gain_deep, offset_deep, up_weight
):
    f32, bf16 = jnp.float32, jnp.bfloat16
    edge, channels = features.shape[0], features.shape[3]
    deep = edge // 2
    deep_channels = gain_deep.shape[0]
    square = Square()
    tiles = square.tiles
    devices = lax.axis_size("gz") * tiles
    y_low, x_low = square.low_sides()
    ny, nx = len(y_low), len(x_low)
    pos = jnp.stack(
        [jnp.asarray(v, jnp.int32) for v in y_low + x_low]
    )

    y, x, corner = square.halos(*square.edges(features))
    own = jnp.moveaxis(deep_weight, 4, 3).reshape(27, deep_weight.shape[4], deep_weight.shape[3])
    got = gather_shards(own)
    front, back = swap_depth(
        depth_face(features, y, x, corner, 0), depth_face(features, y, x, corner, -1)
    )
    half_act = ((deep, edge, edge, channels), f32)
    half_grid = ((deep + 2, edge + 2, edge, channels), bf16)
    conv_flops = 27 * channels * channels * edge**3
    near, taps = call(
        front_half_kernel,
        [half_act, ((9 * channels, 3 * channels), bf16)],
        [half_grid],
        pos,
        features,
        conv_weight.reshape(27, channels, channels),
        flops=conv_flops,
        nbytes=2 << 20,
    )
    (far,) = call(
        back_half_kernel,
        [half_act],
        [half_grid],
        pos,
        features,
        taps,
        corner[0],
        flops=conv_flops,
        nbytes=2 << 20,
    )
    act, stats = call(
        functools.partial(rim_kernel, ny, nx),
        [((edge, edge, edge, channels), f32), ((devices, 8, channels), f32)],
        [((edge + 2, edge + 16, channels), f32), ((edge + 2, edge, 3 * channels), bf16)],
        pos,
        near,
        far,
        jnp.stack(y),
        jnp.stack(x),
        jnp.stack(corner),
        front,
        back,
        taps,
        flops=conv_flops // 8,
        nbytes=5 << 20,
    )
    stats = share(stats)
    out, pooled, *edges = call(
        functools.partial(norm_kernel, ny, nx),
        [
            ((edge, edge, edge, channels), bf16),
            ((deep, deep, deep, channels), f32),
            ((ny, deep, deep, channels), f32),
            ((nx, deep, deep, channels), f32),
            ((ny * nx, deep, channels), f32),
        ],
        [((deep * edge, channels), f32), ((deep, deep, deep, channels), f32)],
        pos,
        act,
        stats,
        gain_mid.reshape(1, channels),
        offset_mid.reshape(1, channels),
        flops=20 * channels * edge**3,
        nbytes=3 << 20,
    )
    y, x, corner = square.halos(*([piece[i] for i in range(piece.shape[0])] for piece in edges))
    front, back = swap_depth(
        depth_face(pooled, y, x, corner, 0), depth_face(pooled, y, x, corner, -1)
    )
    (kernel,) = call(
        functools.partial(place_kernel, tiles),
        [((3, deep_channels, 9 * channels), bf16)],
        [],
        pos,
        got,
        corner[0],
        nbytes=4 << 20,
    )
    deep_act, stats = call(
        functools.partial(deep_kernel, ny, nx),
        [((deep**3, deep_channels), f32), ((tiles, 8, deep_channels), f32)],
        [
            ((deep + 2, deep + 2, 24, channels), f32),
            ((deep + 2, deep // 2 + 1, 2, 16, 3 * channels), bf16),
        ],
        pos,
        pooled,
        jnp.stack(y),
        jnp.stack(x),
        jnp.stack(corner),
        front,
        back,
        kernel,
        flops=2 * 27 * channels * deep_channels * deep**3,
        nbytes=4 << 20,
    )
    stats = share_by_axis(stats)
    (decoded,) = call(
        final_kernel,
        [((edge, edge, edge, channels), bf16)],
        [((2 * deep**3, channels), f32)],
        pos,
        deep_act,
        stats,
        gain_deep.reshape(1, deep_channels),
        offset_deep.reshape(1, deep_channels),
        up_weight,
        out,
        flops=4 * deep_channels * channels * deep**3,
        nbytes=3 << 20,
    )
    return decoded


def solution(mesh):
    placed = (
        P(("cand", "gz"), "yx", None, None),
        P(),
        P(),
        P(),
        P(None, None, None, None, "yx"),
        P(),
        P(),
        P(),
    )
    return jax.shard_map(
        body,
        mesh=mesh,
        in_specs=placed,
        out_specs=P(("cand", "gz"), "yx", None, None),
        check_vma=False,
    )
```

```python
import functools
import math

import jax
import jax.numpy as jnp
from jax import lax
from jax.experimental import pallas as pl
from jax.experimental.pallas import tpu as pltpu
from jax.sharding import PartitionSpec as P

GROUPS = 32
EPSILON = 1e-05
PART = ("gz", "yx")
VMEM_BYTES = 32 * 1024 * 1024
HIGHEST = lax.Precision.HIGHEST


class Square:
    def __init__(self):
        self.tiles = lax.axis_size("yx")
        self.side = math.isqrt(self.tiles)
        tile = lax.axis_index("yx")
        self.row, self.column = tile // self.side, tile % self.side
        self.folded = self.side == 2
        self.steps = (0,) if self.folded else (-1, 1)

    def low_sides(self):
        if self.folded:
            return [self.row], [self.column]
        return [1, 0], [1, 0]

    def route(self, down, right):
        pairs = []
        for tile in range(self.tiles):
            row, column = tile // self.side + down, tile % self.side + right
            if 0 <= row < self.side and 0 <= column < self.side:
                pairs.append((tile, row * self.side + column))
        return pairs

    def swap_route(self, mask):
        return [(tile, tile ^ mask) for tile in range(self.tiles)]

    def halos(self, y_edges, x_edges, corners):
        if self.folded:
            y = lax.ppermute(y_edges[0], "yx", self.swap_route(2))
            x = lax.ppermute(x_edges[0], "yx", self.swap_route(1))
            corner = lax.ppermute(corners[0], "yx", self.swap_route(3))
            return [y], [x], [corner]
        y = [lax.ppermute(y_edges[k], "yx", self.route((1, -1)[1 - k], 0)) for k in (1, 0)]
        x = [lax.ppermute(x_edges[k], "yx", self.route(0, (1, -1)[1 - k])) for k in (1, 0)]
        corner = [
            lax.ppermute(corners[2 * k + j], "yx", self.route((1, -1)[1 - k], (1, -1)[1 - j]))
            for k in (1, 0)
            for j in (1, 0)
        ]
        return y, x, corner


def swap_depth(low, high):
    size = lax.axis_size("gz")
    up = [(i, i + 1) for i in range(size - 1)]
    return lax.ppermute(high, "gz", up), lax.ppermute(low, "gz", [(j, i) for i, j in up])


def depth_face(volume, y, x, corner, at):
    edge, channels = volume.shape[2:]
    pad = jnp.zeros((edge - len(corner), channels), volume.dtype)
    last = jnp.concatenate([piece[at][None] for piece in corner] + [pad])
    rows = [volume[at]] + [piece[at][None] for piece in y + x] + [last[None]]
    return jnp.concatenate(rows)


def split_axes(rows):
    return ("cand", "gz")[: 2 if rows % 64 == 0 else 0]


def share_pieces(got, axes):
    held = stack(*got)[None]
    for axis in axes:
        held = stack(held, swap(held, axis, 1))
        held = held.reshape((-1,) + held.shape[2:])
    return held


def rotate_shards(piece):
    tiles = lax.axis_size("yx")
    return [
        lax.ppermute(piece, "yx", [(i, (i + k) % tiles) for i in range(tiles)]) for k in range(1, tiles)
    ]


def swap(block, axis, mask):
    return lax.ppermute(block, axis, [(i, i ^ mask) for i in range(lax.axis_size(axis))])


def merge(stats, rows, axes):
    for axis in axes:
        mask = 1
        while mask < lax.axis_size(axis):
            other = swap(stats, axis, mask)
            off = stats[0] - other[0]
            mean = 0.5 * (stats[0] + other[0])
            stats = jnp.stack([mean, stats[1] + other[1] + (0.5 * rows) * (off * off)])
            rows, mask = 2 * rows, 2 * mask
    return stats, rows


def call(kernel, outs, scratch, scalars, *arrays, flops=0, nbytes=0, copied_out=False):
    smem, vmem = pl.BlockSpec(memory_space=pltpu.SMEM), pl.BlockSpec(memory_space=pltpu.VMEM)
    out_spec = pl.BlockSpec(memory_space=pl.ANY) if copied_out else vmem
    return pl.pallas_call(
        kernel,
        out_shape=[jax.ShapeDtypeStruct(shape, dtype) for shape, dtype in outs],
        in_specs=[smem] + [vmem] * len(arrays),
        out_specs=[out_spec] * len(outs),
        scratch_shapes=[pltpu.VMEM(*entry) if isinstance(entry, tuple) else entry for entry in scratch],
        compiler_params=pltpu.CompilerParams(vmem_limit_bytes=VMEM_BYTES),
        cost_estimate=pl.CostEstimate(flops=flops, bytes_accessed=nbytes, transcendentals=0),
    )(scalars, *arrays)


def edge_kernel(ny, nx, pos, x, y_edges, x_edges, corners, lines):
    edge = x.shape[0]
    f32, bf16 = jnp.float32, jnp.bfloat16
    for i in range(ny):
        at = jnp.where(pos[i] == 1, 0, edge - 1) if ny == 1 else (0, edge - 1)[i]
        y_edges[i] = x[:, at]
    flat = lines.reshape(edge * edge * 8, 128)
    for j in range(nx):
        first = x[:, :, 0:8].astype(f32)
        last = x[:, :, edge - 8 : edge].astype(f32)
        if nx == 1:
            low = pos[ny] == 1
            turned = pltpu.roll(last.reshape(edge * edge, 8, 128), 1, 1)
            kept = jnp.where(low, first.reshape(edge * edge, 8, 128), turned)
        else:
            kept = (first, pltpu.roll(last.reshape(edge * edge, 8, 128), 1, 1))[j]
        lines[...] = kept.reshape(edge * edge, 8, 128)
        column = flat[pl.ds(0, edge * edge, stride=8), :]
        x_edges[j] = column.astype(bf16).reshape(edge, edge, 128)
        for i in range(ny):
            first_y = flat[pl.ds(0, edge, stride=8 * edge), :]
            last_y = flat[pl.ds(8 * (edge - 1), edge, stride=8 * edge), :]
            kept = jnp.where(pos[i] == 1, first_y, last_y) if ny == 1 else (first_y, last_y)[i]
            corners[i * nx + j] = kept.astype(bf16)


def spread_taps(weight, taps):
    for tap in range(27):
        row, lane = tap // 3 * 128, tap % 3 * 128
        taps[row : row + 128, lane : lane + 128] = weight[tap]


def pair_taps(weight, pairs):
    for dz in range(3):
        for line in range(4):
            row = (dz * 4 + line) * 128
            for out in range(2):
                lane = out * 128
                if 0 <= line - out < 3:
                    block = weight[dz * 9 + (line - out) * 3 + 2]
                else:
                    block = jnp.zeros((128, 128), pairs.dtype)
                pairs[row : row + 128, lane : lane + 128] = block


def join_x(wide, edge):
    place = lax.broadcasted_iota(jnp.int32, wide.shape[:2] + (128,), 1)
    after = jnp.where(place > 0, pltpu.roll(wide[:, :, :128], 1, 1), 0.0)
    before = jnp.where(place < edge - 1, pltpu.roll(wide[:, :, 256:], edge - 1, 1), 0.0)
    return wide[:, :, 128:256] + after + before


def local_planes(x, lo, count, taps, pairs, grid, act):
    edge = x.shape[0]
    blank = jnp.zeros((count + 2,) + grid.shape[2:], grid.dtype)
    grid[:, 0] = blank
    grid[:, edge + 1] = blank
    first, last = max(lo - 1, 0), min(lo + count + 1, edge)
    if first > lo - 1:
        grid[0] = jnp.zeros(grid.shape[1:], grid.dtype)
    if last < lo + count + 1:
        grid[count + 1] = jnp.zeros(grid.shape[1:], grid.dtype)
    grid[first - lo + 1 : last - lo + 1, 1 : edge + 1] = x[first:last]
    planes = 2
    rows = planes * edge * edge
    place = lax.broadcasted_iota(jnp.int32, (planes * edge, edge, 128), 1)
    halved = grid.reshape(count + 2, edge // 2 + 1, 2, edge, 128)
    for z in range(0, count, planes):
        left = jnp.concatenate(
            [
                grid[z + dz : z + dz + planes, dy : dy + edge].reshape(rows, 128)
                for dz in range(3)
                for dy in range(3)
            ],
            axis=1,
        )
        wide = jnp.dot(left, taps[:, 0:256], preferred_element_type=jnp.float32)
        wide = wide.reshape(planes * edge, edge, 256)
        left = jnp.concatenate(
            [
                halved[z + dz : z + dz + planes, line // 2 : line // 2 + edge // 2, line % 2].reshape(
                    rows // 2, 128
                )
                for dz in range(3)
                for line in range(4)
            ],
            axis=1,
        )
        two = jnp.dot(left, pairs[...], preferred_element_type=jnp.float32)
        two = two.reshape(planes * edge // 2, edge, 256)
        two = jnp.stack([two[:, :, :128], two[:, :, 128:]], axis=1).reshape(planes * edge, edge, 128)
        after = jnp.where(place > 0, pltpu.roll(wide[:, :, :128], 1, 1), 0.0)
        before = jnp.where(place < edge - 1, pltpu.roll(two, edge - 1, 1), 0.0)
        new = wide[:, :, 128:256] + after + before
        act[z : z + planes] = new.reshape(planes, edge, edge, 128)


def front_half_kernel(pos, x, weight, deep_weight, after, act, taps, pairs, piece, grid):
    del after
    spread_taps(weight, taps)
    pair_taps(weight, pairs)
    size = piece.shape[1]
    if size < deep_weight.shape[1]:
        piece[...] = deep_weight[:, pl.ds(pl.multiple_of(pos[pos.shape[0] - 1] * size, size), size)]
    else:
        piece[...] = deep_weight[...]
    local_planes(x, 0, act.shape[0], taps, pairs, grid, act)


def back_half_kernel(_, x, taps, pairs, after, act, grid):
    del after
    local_planes(x, x.shape[0] - act.shape[0], act.shape[0], taps, pairs, grid, act)


def rim_kernel(ny, nx, pos, *refs):
    near, far, y_halos, x_halos, corners, front, back, taps, act, stats, column, flanks = refs
    edge = act.shape[0]
    half = edge // 2
    f32, bf16 = jnp.float32, jnp.bfloat16
    act[0:half] = near[...]
    act[half:edge] = far[...]
    flat = act.reshape(edge**3, 128)

    for plane, face, dz in ((0, front, 0), (edge - 1, back, 2)):
        inner = face[0:edge]
        blank = jnp.zeros((1, edge, 128), bf16)
        lines = [
            jnp.concatenate([blank, inner[: edge - 1]], axis=0),
            inner,
            jnp.concatenate([inner[1:], blank], axis=0),
        ]
        left = jnp.concatenate([line.reshape(edge * edge, 128) for line in lines], axis=1)
        wide = jnp.dot(left, taps[dz * 384 : dz * 384 + 384, :], preferred_element_type=f32)
        act[plane] += join_x(wide.reshape(edge, edge, 384), edge)

    for i in range(ny):
        low = pos[i] == 1
        inner = y_halos[i]
        ends = [front[edge + i][None], back[edge + i][None]]
        lines = [
            jnp.concatenate([ends[0], inner[: edge - 1]], axis=0),
            inner,
            jnp.concatenate([inner[1:], ends[1]], axis=0),
        ]
        left = jnp.concatenate([line.reshape(edge * edge, 128) for line in lines], axis=1)
        start = jnp.where(low, 0, 256)
        right = jnp.concatenate(
            [taps[pl.ds(pl.multiple_of(start + dz * 384, 128), 128), :] for dz in range(3)], axis=0
        )
        wide = jnp.dot(left, right, preferred_element_type=f32)
        act[:, jnp.where(low, 0, edge - 1)] += join_x(wide.reshape(edge, edge, 384), edge)

    for j in range(nx):
        column[:, 0:8] = jnp.zeros((edge + 2, 8, 128), f32)
        column[:, 8 + edge :] = jnp.zeros((edge + 2, 8, 128), f32)
        column[1 : edge + 1, 8 : 8 + edge] = x_halos[j].astype(f32)
        column[0, 8 : 8 + edge] = front[edge + ny + j].astype(f32)
        column[edge + 1, 8 : 8 + edge] = back[edge + ny + j].astype(f32)
        rows = edge + 16
        lines = column.reshape((edge + 2) * rows, 128)
        for i in range(ny):
            k = i * nx + j
            ends = [front[edge + ny + nx, k : k + 1], corners[k], back[edge + ny + nx, k : k + 1]]
            ends = jnp.concatenate([e.astype(f32) for e in ends], axis=0)
            low = pos[i] == 1
            if ny == 1:
                lines[pl.ds(7, edge + 2, stride=rows), :] = jnp.where(low, ends, 0.0)
                lines[pl.ds(8 + edge, edge + 2, stride=rows), :] = jnp.where(low, 0.0, ends)
            else:
                lines[pl.ds(7 if i == 0 else 8 + edge, edge + 2, stride=rows), :] = ends
        for dy in range(3):
            piece = column[:, 7 + dy : 7 + dy + edge].astype(bf16)
            flanks[:, :, dy * 128 : dy * 128 + 128] = piece
        left = jnp.concatenate(
            [flanks[dz : dz + edge].reshape(edge * edge, 384) for dz in range(3)], axis=1
        )
        right = jnp.concatenate([taps[:, 0:128], taps[:, 256:384]], axis=1)
        extra = jnp.dot(left, right, preferred_element_type=f32)
        low = pos[ny + j] == 1
        first, last = extra[:, :128], extra[:, 128:]
        if nx == 1:
            first, last = jnp.where(low, first, 0.0), jnp.where(low, 0.0, last)
        if nx == 1 or j == 0:
            flat[pl.ds(0, edge * edge, stride=edge), :] += first
        if nx == 1 or j == 1:
            flat[pl.ds(edge - 1, edge * edge, stride=edge), :] += last

    def sum_step(k, carry):
        return carry + jnp.sum(act[k].reshape(edge * 2, 8, 128), axis=0)

    total = lax.fori_loop(0, edge, sum_step, jnp.zeros((8, 128), f32), unroll=4)
    mean = jnp.sum(total, axis=0, keepdims=True) / edge**3

    def spread_step(k, carry):
        off = act[k].reshape(edge * 2, 8, 128) - mean
        return carry + jnp.sum(off * off, axis=0)

    total = lax.fori_loop(0, edge, spread_step, jnp.zeros((8, 128), f32), unroll=4)
    put_stats(stats, mean, jnp.sum(total, axis=0, keepdims=True))


def put_stats(stats, mean, spread):
    stats[0:1] = mean
    stats[1:2] = spread


def read_stats(stats, rows):
    channels = stats.shape[1]
    width = channels // GROUPS
    line = lax.broadcasted_iota(jnp.int32, (channels, channels), 0) // width
    same = line == lax.broadcasted_iota(jnp.int32, (channels, channels), 1) // width
    same = same.astype(jnp.float32)

    def grouped(row):
        row = jnp.broadcast_to(row, (8, channels))
        return jnp.dot(row, same, precision=HIGHEST, preferred_element_type=jnp.float32)[0:1]

    means = stats[0:1]
    mean = grouped(means) / width
    off = means - mean
    total = grouped(stats[1:2] + rows * (off * off))
    return mean, lax.rsqrt(total / (rows * width) + EPSILON)


def silu_of_double(h):
    return h + h * jnp.tanh(h)


def norm_kernel(ny, nx, rows, pos, act, stats, gain, offset, out, pooled, *refs):
    y_edges, x_edges, corners, half = refs
    edge = act.shape[0]
    deep = edge // 2
    f32, bf16 = jnp.float32, jnp.bfloat16
    mean, scale = read_stats(stats, rows)
    scale = scale * (0.5 * gain[...])
    shift = 0.5 * offset[...]
    for k in range(deep):
        value = silu_of_double((act[2 * k : 2 * k + 2] - mean) * scale + shift).astype(bf16)
        out[2 * k : 2 * k + 2] = value
        value = value.astype(f32)
        value = (value[0] + value[1]).reshape(deep, 2, edge, 128)
        half[k] = (value[:, 0] + value[:, 1]).reshape(deep * edge, 128)
        lines = half.at[k]
        pair = lines[pl.ds(0, deep * deep, stride=2), :] + lines[pl.ds(1, deep * deep, stride=2), :]
        pooled[k] = (pair * 0.125).astype(bf16).astype(f32).reshape(deep, deep, 128)
    lines = pooled.reshape(deep**3, 128)
    first_x = lines[pl.ds(0, deep * deep, stride=deep), :]
    last_x = lines[pl.ds(deep - 1, deep * deep, stride=deep), :]
    first_y, last_y = (pooled[:, y].reshape(deep * deep, 128) for y in (0, deep - 1))
    ends = []
    for y in (0, deep - 1):
        for x in (0, deep - 1):
            ends.append(lines[pl.ds(y * deep + x, deep, stride=deep * deep), :])
    if ny == 1:
        above, left = pos[0] == 1, pos[1] == 1
        y_edges[0] = jnp.where(above, first_y, last_y).astype(bf16)
        x_edges[0] = jnp.where(left, first_x, last_x).astype(bf16)
        corners[0] = jnp.where(
            above, jnp.where(left, ends[0], ends[1]), jnp.where(left, ends[2], ends[3])
        )
    else:
        y_edges[0], y_edges[1] = first_y.astype(bf16), last_y.astype(bf16)
        x_edges[0], x_edges[1] = first_x.astype(bf16), last_x.astype(bf16)
        for k in range(4):
            corners[k] = ends[k]


def stack_kernel(*refs):
    out = refs[-1]
    for k in range(out.shape[0]):
        out[k] = refs[k][...]


def stack(*arrays):
    vmem = pl.BlockSpec(memory_space=pltpu.VMEM)
    return pl.pallas_call(
        stack_kernel,
        out_shape=jax.ShapeDtypeStruct((len(arrays),) + arrays[0].shape, arrays[0].dtype),
        in_specs=[vmem] * len(arrays),
        out_specs=vmem,
        compiler_params=pltpu.CompilerParams(vmem_limit_bytes=VMEM_BYTES),
    )(*arrays)


def place_kernel(tiles, pos, own, held, kernel):
    shard, part = own.shape[1], held.shape[3]
    tile, mine = pos[pos.shape[0] - 2], pos[pos.shape[0] - 1]

    def place(rows, at):
        for tap in range(27):
            lane = tap % 9 * 128
            kernel[tap // 9, pl.ds(at, rows.shape[1]), lane : lane + 128] = rows[tap]

    place(own, pl.multiple_of(tile * shard, shard))
    for piece in range(held.shape[0]):
        at = jnp.bitwise_xor(mine, piece) * part
        for k in range(1, tiles):
            base = lax.rem(tile + tiles - k, tiles) * shard
            place(held.at[piece, k - 1], pl.multiple_of(base + at, part))


def deep_kernel(ny, nx, pos, pooled, y_halos, x_halos, corners, front, back, kernel, *refs):
    act, stats, grid, packed = refs
    deep = pooled.shape[0]
    f32 = jnp.float32
    front, back = (face[...].astype(f32).reshape(-1, deep, 128) for face in (front, back))
    y_halos = [y_halos[i].astype(f32).reshape(deep, deep, 128) for i in range(ny)]
    x_halos = [x_halos[i].astype(f32).reshape(deep, deep, 128) for i in range(nx)]
    grid[...] = jnp.zeros(grid.shape, f32)
    grid[1 : deep + 1, 1 : deep + 1, 8:16] = pooled[...]
    grid[0, 1 : deep + 1, 8:16] = front[0:deep]
    grid[deep + 1, 1 : deep + 1, 8:16] = back[0:deep]
    for i in range(ny):
        at = jnp.where(pos[i] == 1, 0, deep + 1)
        grid[1 : deep + 1, at, 8:16] = y_halos[i]
        grid[0, at, 8:16] = front[deep + i]
        grid[deep + 1, at, 8:16] = back[deep + i]
    for j in range(nx):
        for z in range(deep + 2):
            if z == 0:
                line, rim = front[deep + ny + j], front
            elif z == deep + 1:
                line, rim = back[deep + ny + j], back
            else:
                line, rim = x_halos[j][z - 1], None
            lines = grid.at[z].reshape((deep + 2) * 24, 128)
            left = pos[ny + j] == 1
            for side, here in ((7, left), (16, jnp.logical_not(left))):
                if nx == 2 and side != (7, 16)[j]:
                    continue
                kept = line if nx == 2 else jnp.where(here, line, 0.0)
                lines[pl.ds(24 + side, deep, stride=24), :] = kept
                for i in range(ny):
                    k = i * nx + j
                    end = corners[k, z - 1 : z] if rim is None else rim[deep + ny + nx, k : k + 1]
                    above = pos[i] == 1
                    for y, there in ((0, above), (deep + 1, jnp.logical_not(above))):
                        if ny == 2 and y != (0, deep + 1)[i]:
                            continue
                        kept = end
                        if nx == 1:
                            kept = jnp.where(jnp.logical_and(here, there), end, 0.0)
                        grid[z, y, side : side + 1] = kept

    for dx in range(3):
        plane = grid[:, :, 7 + dx : 15 + dx]
        for y in range(deep + 1):
            both = jnp.concatenate([plane[:, y], plane[:, y + 1]], axis=1)
            packed[:, y // 2, y % 2, :, dx * 128 : dx * 128 + 128] = both.astype(jnp.bfloat16)

    rows = deep**3
    total = None
    for dz in range(3):
        left = jnp.concatenate(
            [
                packed[dz : dz + deep, dy // 2 : dy // 2 + deep // 2, dy % 2].reshape(rows, 384)
                for dy in range(3)
            ],
            axis=1,
        )
        term = lax.dot_general(
            left, kernel[dz], (((1,), (1,)), ((), ())), preferred_element_type=f32
        )
        total = term if total is None else total + term
    act[...] = total
    mean = jnp.sum(total, axis=0, keepdims=True) / rows
    off = total - mean
    put_stats(stats, mean, jnp.sum(off * off, axis=0, keepdims=True))


def final_kernel(rows, _, act, stats, gain, offset, up, mid, out, wide, held, sems):
    edge = mid.shape[0]
    deep = edge // 2
    f32 = jnp.float32
    mean, scale = read_stats(stats, rows)
    scale = scale * (0.5 * gain[...])
    value = silu_of_double((act[...] - mean) * scale + 0.5 * offset[...]).astype(jnp.bfloat16)
    lifted = jnp.dot(value, up[...], preferred_element_type=f32)
    wide[pl.ds(0, deep**3, stride=2), :] = lifted
    wide[pl.ds(1, deep**3, stride=2), :] = lifted
    size = deep * edge
    copies = []
    for k in range(deep):
        add = wide[k * size : k * size + size, :].reshape(1, deep, 1, edge, 128)
        old = mid[2 * k : 2 * k + 2].astype(f32).reshape(2, deep, 2, edge, 128)
        held[2 * k : 2 * k + 2] = (old + add).astype(jnp.bfloat16).reshape(2, edge, edge, 128)
        copy = pltpu.make_async_copy(
            held.at[2 * k : 2 * k + 2], out.at[2 * k : 2 * k + 2], sems.at[k]
        )
        copy.start()
        copies.append(copy)
    for copy in copies:
        copy.wait()


def body(
    features, conv_weight, gain_mid, offset_mid, deep_weight, gain_deep, offset_deep, up_weight
):
    f32, bf16 = jnp.float32, jnp.bfloat16
    edge, channels = features.shape[0], features.shape[3]
    deep = edge // 2
    deep_channels = gain_deep.shape[0]
    square = Square()
    tiles = square.tiles
    devices = lax.axis_size("gz") * tiles
    y_low, x_low = square.low_sides()
    ny, nx = len(y_low), len(x_low)
    axes = split_axes(deep_weight.shape[4])
    mine = sum(lax.axis_index(axis) % 2 * 2**k for k, axis in enumerate(axes))
    pos = y_low + x_low + [lax.axis_index("yx"), mine]
    pos = jnp.stack([jnp.asarray(v, jnp.int32) for v in pos])

    edges = call(
        functools.partial(edge_kernel, ny, nx),
        [
            ((ny, edge, edge, channels), bf16),
            ((nx, edge, edge, channels), bf16),
            ((ny * nx, edge, channels), bf16),
        ],
        [((edge * edge, 8, channels), f32)],
        pos,
        features,
        nbytes=1 << 20,
    )
    halos = square.halos(*(list(piece) for piece in edges))
    own = jnp.moveaxis(deep_weight, 4, 3).reshape(27, deep_weight.shape[4], channels)
    half_act = ((deep, edge, edge, channels), f32)
    half_grid = ((deep + 2, edge + 2, edge, channels), bf16)
    conv_flops = 27 * channels * channels * edge**3
    near, taps, pairs, piece = call(
        front_half_kernel,
        [
            half_act,
            ((9 * channels, 3 * channels), bf16),
            ((12 * channels, 2 * channels), bf16),
            ((27, own.shape[1] // 2 ** len(axes), channels), bf16),
        ],
        [half_grid],
        pos,
        features,
        conv_weight.reshape(27, channels, channels),
        own,
        edges[2],
        flops=conv_flops,
        nbytes=3 << 20,
    )
    piece, (y, x, corner) = lax.optimization_barrier((piece, halos))
    front, back = swap_depth(
        depth_face(features, y, x, corner, 0), depth_face(features, y, x, corner, -1)
    )
    got = rotate_shards(piece)
    (far,) = call(
        back_half_kernel,
        [half_act],
        [half_grid],
        pos,
        features,
        taps,
        pairs,
        corner[0],
        flops=conv_flops,
        nbytes=3 << 20,
    )
    act, stats = call(
        functools.partial(rim_kernel, ny, nx),
        [((edge, edge, edge, channels), f32), ((2, channels), f32)],
        [((edge + 2, edge + 16, channels), f32), ((edge + 2, edge, 3 * channels), bf16)],
        pos,
        near,
        far,
        jnp.stack(y),
        jnp.stack(x),
        jnp.stack(corner),
        front,
        back,
        taps,
    )
    stats, *got = lax.optimization_barrier((stats, *got))
    stats, rows = merge(stats, float(edge**3), ("gz",))
    stats, _ = merge(stats, rows, ("yx",))
    held = share_pieces(got, axes)
    out, pooled, *edges = call(
        functools.partial(norm_kernel, ny, nx, float(edge**3 * devices)),
        [
            ((edge, edge, edge, channels), bf16),
            ((deep, deep, deep, channels), f32),
            ((ny, deep * deep, channels), bf16),
            ((nx, deep * deep, channels), bf16),
            ((ny * nx, deep, channels), f32),
        ],
        [((deep, deep * edge, channels), f32)],
        pos,
        act,
        stats,
        gain_mid.reshape(1, channels),
        offset_mid.reshape(1, channels),
        flops=20 * channels * edge**3,
        nbytes=3 << 20,
    )
    y, x, corner = square.halos(*(list(piece) for piece in edges))

    def face(at):
        plane = pooled[at].astype(bf16).reshape(deep * deep, channels)
        rims = [piece.reshape(deep, deep, channels)[at] for piece in y + x]
        ends = [piece[at][None].astype(bf16) for piece in corner]
        rows = deep * deep + deep * (ny + nx) + len(ends)
        pad = jnp.zeros((-rows % 16, channels), bf16)
        return jnp.concatenate([plane] + rims + ends + [pad])

    front, back = swap_depth(face(0), face(-1))
    (kernel,) = call(
        functools.partial(place_kernel, tiles),
        [((3, deep_channels, 9 * channels), bf16)],
        [],
        pos,
        own,
        held,
        nbytes=4 << 20,
    )
    deep_act, stats = call(
        functools.partial(deep_kernel, ny, nx),
        [((deep**3, deep_channels), f32), ((2, deep_channels), f32)],
        [
            ((deep + 2, deep + 2, 24, channels), f32),
            ((deep + 2, deep // 2 + 1, 2, 16, 3 * channels), bf16),
        ],
        pos,
        pooled,
        jnp.stack(y),
        jnp.stack(x),
        jnp.stack(corner),
        front,
        back,
        kernel,
        flops=2 * 27 * channels * deep_channels * deep**3,
        nbytes=4 << 20,
    )
    stats, _ = merge(stats, float(deep**3), PART)
    (decoded,) = call(
        functools.partial(final_kernel, float(deep**3 * devices)),
        [((edge, edge, edge, channels), bf16)],
        [
            ((2 * deep**3, channels), f32),
            ((edge, edge, edge, channels), bf16),
            pltpu.SemaphoreType.DMA((deep,)),
        ],
        pos,
        deep_act,
        stats,
        gain_deep.reshape(1, deep_channels),
        offset_deep.reshape(1, deep_channels),
        up_weight,
        out,
        flops=4 * deep_channels * channels * deep**3,
        nbytes=3 << 20,
        copied_out=True,
    )
    return decoded


def solution(mesh):
    placed = (
        P(("cand", "gz"), "yx", None, None),
        P(),
        P(),
        P(),
        P(None, None, None, None, "yx"),
        P(),
        P(),
        P(),
    )
    return jax.shard_map(
        body,
        mesh=mesh,
        in_specs=placed,
        out_specs=P(("cand", "gz"), "yx", None, None),
        check_vma=False,
    )
```

```python
import functools
import math

import jax
import jax.numpy as jnp
from jax import lax
from jax.experimental import pallas as pl
from jax.experimental.pallas import tpu as pltpu
from jax.sharding import PartitionSpec as P

GROUPS = 32
EPSILON = 1e-05
PART = ("gz", "yx")
VMEM_BYTES = 32 * 1024 * 1024


class Square:
    def __init__(self):
        self.tiles = lax.axis_size("yx")
        self.side = math.isqrt(self.tiles)
        tile = lax.axis_index("yx")
        self.row, self.column = tile // self.side, tile % self.side
        self.folded = self.side == 2
        self.steps = (0,) if self.folded else (-1, 1)

    def low_sides(self):
        if self.folded:
            return [self.row], [self.column]
        return [1, 0], [1, 0]

    def route(self, down, right):
        pairs = []
        for tile in range(self.tiles):
            row, column = tile // self.side + down, tile % self.side + right
            if 0 <= row < self.side and 0 <= column < self.side:
                pairs.append((tile, row * self.side + column))
        return pairs

    def swap_route(self, mask):
        return [(tile, tile ^ mask) for tile in range(self.tiles)]

    def halos(self, y_edges, x_edges, corners):
        if self.folded:
            y = lax.ppermute(y_edges[0], "yx", self.swap_route(2))
            x = lax.ppermute(x_edges[0], "yx", self.swap_route(1))
            corner = lax.ppermute(corners[0], "yx", self.swap_route(3))
            return [y], [x], [corner]
        y = [lax.ppermute(y_edges[k], "yx", self.route((1, -1)[1 - k], 0)) for k in (1, 0)]
        x = [lax.ppermute(x_edges[k], "yx", self.route(0, (1, -1)[1 - k])) for k in (1, 0)]
        corner = [
            lax.ppermute(corners[2 * k + j], "yx", self.route((1, -1)[1 - k], (1, -1)[1 - j]))
            for k in (1, 0)
            for j in (1, 0)
        ]
        return y, x, corner


def swap_depth(low, high):
    size = lax.axis_size("gz")
    up = [(i, i + 1) for i in range(size - 1)]
    return lax.ppermute(high, "gz", up), lax.ppermute(low, "gz", [(j, i) for i, j in up])


def split_axes(rows):
    return ("cand", "gz")[: 2 if rows % 64 == 0 else 0]


def rotate_shards(piece):
    tiles = lax.axis_size("yx")
    return [
        lax.ppermute(piece, "yx", [(i, (i + k) % tiles) for i in range(tiles)]) for k in range(1, tiles)
    ]


def swap(block, axis, mask):
    return lax.ppermute(block, axis, [(i, i ^ mask) for i in range(lax.axis_size(axis))])


def share(stats):
    return lax.all_to_all(stats, PART, 0, 0)


def call(kernel, outs, scratch, scalars, *arrays, flops=0, nbytes=0, in_hbm=False, out_hbm=False):
    smem, vmem, hbm = (
        pl.BlockSpec(memory_space=space) for space in (pltpu.SMEM, pltpu.VMEM, pltpu.HBM)
    )
    return pl.pallas_call(
        kernel,
        out_shape=[jax.ShapeDtypeStruct(shape, dtype) for shape, dtype in outs],
        in_specs=[smem] + [hbm if in_hbm else vmem] * len(arrays),
        out_specs=[hbm if out_hbm else vmem] * len(outs),
        scratch_shapes=[pltpu.VMEM(*entry) if isinstance(entry, tuple) else entry for entry in scratch],
        compiler_params=pltpu.CompilerParams(vmem_limit_bytes=VMEM_BYTES),
        cost_estimate=pl.CostEstimate(flops=flops, bytes_accessed=nbytes, transcendentals=0),
    )(scalars, *arrays)


def start_kernel(ny, nx, pos, x_in, w_in, d_in, y_edges, x_edges, corners, x, w, d, lines, sems):
    edge = x.shape[0]
    size = edge // 4
    first = [
        pltpu.make_async_copy(x_in.at[pl.ds(k * size, size)], x.at[pl.ds(k * size, size)], sems.at[k])
        for k in range(4)
    ]
    later = [pltpu.make_async_copy(w_in, w, sems.at[4]), pltpu.make_async_copy(d_in, d, sems.at[5])]
    for copy in first + later:
        copy.start()
    for copy in first:
        copy.wait()
    f32, bf16 = jnp.float32, jnp.bfloat16
    for i in range(ny):
        at = jnp.where(pos[i] == 1, 0, edge - 1) if ny == 1 else (0, edge - 1)[i]
        y_edges[i] = x[:, at]
    flat = lines.reshape(edge * edge * 8, 128)
    for j in range(nx):
        first = x[:, :, 0:8].astype(f32)
        last = x[:, :, edge - 8 : edge].astype(f32)
        if nx == 1:
            low = pos[ny] == 1
            turned = pltpu.roll(last.reshape(edge * edge, 8, 128), 1, 1)
            kept = jnp.where(low, first.reshape(edge * edge, 8, 128), turned)
        else:
            kept = (first, pltpu.roll(last.reshape(edge * edge, 8, 128), 1, 1))[j]
        lines[...] = kept.reshape(edge * edge, 8, 128)
        column = flat[pl.ds(0, edge * edge, stride=8), :]
        x_edges[j] = column.astype(bf16).reshape(edge, edge, 128)
        for i in range(ny):
            first_y = flat[pl.ds(0, edge, stride=8 * edge), :]
            last_y = flat[pl.ds(8 * (edge - 1), edge, stride=8 * edge), :]
            kept = jnp.where(pos[i] == 1, first_y, last_y) if ny == 1 else (first_y, last_y)[i]
            corners[i * nx + j] = kept.astype(bf16)
    for copy in later:
        copy.wait()


def face_kernel(ny, nx, _, x, y_halos, x_halos, corners, low, high):
    edge = x.shape[0]
    wide = edge + ny + nx
    for face, at in ((low, 0), (high, edge - 3)):
        for k in range(3):
            row = k * wide
            face[row : row + edge] = x[at + k]
            for i in range(ny):
                face[row + edge + i] = y_halos[i, at + k]
            for j in range(nx):
                face[row + edge + ny + j] = x_halos[j, at + k]
        for k in range(ny * nx):
            face[3 * wide + k] = corners[k]


def spread_taps(weight, taps):
    for tap in range(27):
        row, lane = tap // 3 * 128, tap % 3 * 128
        taps[row : row + 128, lane : lane + 128] = weight[tap]


def pair_taps(weight, pairs):
    for dz in range(3):
        for line in range(4):
            row = (dz * 4 + line) * 128
            for out in range(2):
                lane = out * 128
                if 0 <= line - out < 3:
                    block = weight[dz * 9 + (line - out) * 3 + 2]
                else:
                    block = jnp.zeros((128, 128), pairs.dtype)
                pairs[row : row + 128, lane : lane + 128] = block


def join_x(wide, edge):
    place = lax.broadcasted_iota(jnp.int32, wide.shape[:2] + (128,), 1)
    after = jnp.where(place > 0, pltpu.roll(wide[:, :, :128], 1, 1), 0.0)
    before = jnp.where(place < edge - 1, pltpu.roll(wide[:, :, 256:], edge - 1, 1), 0.0)
    return wide[:, :, 128:256] + after + before


def convolve(grid, count, taps, pairs, put):
    edge = grid.shape[2]
    planes = 2
    rows = planes * edge * edge
    place = lax.broadcasted_iota(jnp.int32, (planes * edge, edge, 128), 1)
    halved = grid.reshape(grid.shape[0], edge // 2 + 1, 2, edge, 128)
    for z in range(0, count, planes):
        left = jnp.concatenate(
            [
                grid[z + dz : z + dz + planes, dy : dy + edge].reshape(rows, 128)
                for dz in range(3)
                for dy in range(3)
            ],
            axis=1,
        )
        wide = jnp.dot(left, taps[:, 0:256], preferred_element_type=jnp.float32)
        wide = wide.reshape(planes * edge, edge, 256)
        left = jnp.concatenate(
            [
                halved[z + dz : z + dz + planes, line // 2 : line // 2 + edge // 2, line % 2].reshape(
                    rows // 2, 128
                )
                for dz in range(3)
                for line in range(4)
            ],
            axis=1,
        )
        two = jnp.dot(left, pairs[...], preferred_element_type=jnp.float32)
        two = two.reshape(planes * edge // 2, edge, 256)
        two = jnp.stack([two[:, :, :128], two[:, :, 128:]], axis=1).reshape(planes * edge, edge, 128)
        after = jnp.where(place > 0, pltpu.roll(wide[:, :, :128], 1, 1), 0.0)
        before = jnp.where(place < edge - 1, pltpu.roll(two, edge - 1, 1), 0.0)
        new = wide[:, :, 128:256] + after + before
        put(z, new.reshape(planes, edge, edge, 128))


def clear_sides(grid):
    blank = jnp.zeros(grid.shape[:1] + grid.shape[2:], grid.dtype)
    grid[:, 0] = blank
    grid[:, grid.shape[1] - 1] = blank


def local_planes(x, lo, count, taps, pairs, grid, act):
    edge = x.shape[0]
    clear_sides(grid)
    first, last = max(lo - 1, 0), min(lo + count + 1, edge)
    if first > lo - 1:
        grid[0] = jnp.zeros(grid.shape[1:], grid.dtype)
    if last < lo + count + 1:
        grid[count + 1] = jnp.zeros(grid.shape[1:], grid.dtype)
    grid[first - lo + 1 : last - lo + 1, 1 : edge + 1] = x[first:last]

    def put(z, new):
        act[z : z + new.shape[0]] = new

    convolve(grid, count, taps, pairs, put)


def front_half_kernel(pos, x, weight, deep_weight, act, taps, pairs, piece, grid):
    spread_taps(weight, taps)
    pair_taps(weight, pairs)
    size = piece.shape[1]
    if size < deep_weight.shape[1]:
        piece[...] = deep_weight[:, pl.ds(pl.multiple_of(pos[pos.shape[0] - 1] * size, size), size)]
    else:
        piece[...] = deep_weight[...]
    local_planes(x, 0, act.shape[0], taps, pairs, grid, act)


def back_half_kernel(_, x, taps, pairs, after, act, grid):
    del after
    local_planes(x, x.shape[0] - act.shape[0], act.shape[0], taps, pairs, grid, act)


def rim_kernel(ny, nx, pos, *refs):
    x, near, far, y_halos, x_halos, corners, front, back, taps, pairs, act, stats, grid, column, flanks = refs
    edge = x.shape[0]
    half = edge // 2
    wide_face = edge + ny + nx
    depth = edge + 4
    f32, bf16 = jnp.float32, jnp.bfloat16
    act[2 : 2 + half] = near[...]
    act[2 + half : 2 + edge] = far[...]

    clear_sides(grid)
    for face, halo_at, own_at, own, out_at, touched, dz in (
        (front, 0, 3, 0, 0, 2, 0),
        (back, 1, 0, edge - 1, depth - 2, depth - 3, 2),
    ):
        for k in range(3):
            grid[halo_at + k, 1 : edge + 1] = face[k * wide_face : k * wide_face + edge]
        grid[own_at, 1 : edge + 1] = x[own]

        def put(z, new):
            act[out_at + z : out_at + z + new.shape[0]] = new

        convolve(grid, 2, taps, pairs, put)
        beside = halo_at + (2 if dz == 0 else 0)
        left = jnp.concatenate(
            [grid[beside, dy : dy + edge].reshape(edge * edge, 128) for dy in range(3)], axis=1
        )
        wide = jnp.dot(left, taps[dz * 384 : dz * 384 + 384, :], preferred_element_type=f32)
        act[touched] += join_x(wide.reshape(edge, edge, 384), edge)

    def rim(face, row):
        return jnp.stack([face[k * wide_face + edge + row] for k in range(3)])

    for i in range(ny):
        low = pos[i] == 1
        line = jnp.concatenate([rim(front, i), y_halos[i], rim(back, i)], axis=0)
        left = jnp.concatenate(
            [line[dz : dz + depth].reshape(depth * edge, 128) for dz in range(3)], axis=1
        )
        start = jnp.where(low, 0, 256)
        right = jnp.concatenate(
            [taps[pl.ds(pl.multiple_of(start + dz * 384, 128), 128), :] for dz in range(3)], axis=0
        )
        wide = jnp.dot(left, right, preferred_element_type=f32)
        act[:, jnp.where(low, 0, edge - 1)] += join_x(wide.reshape(depth, edge, 384), edge)

    flat = act.reshape(depth * edge * edge, 128)
    for j in range(nx):
        column[:, 0:8] = jnp.zeros((depth + 2, 8, 128), f32)
        column[:, 8 + edge :] = jnp.zeros((depth + 2, 8, 128), f32)
        column[3 : edge + 3, 8 : 8 + edge] = x_halos[j].astype(f32)
        column[0:3, 8 : 8 + edge] = rim(front, ny + j).astype(f32)
        column[edge + 3 :, 8 : 8 + edge] = rim(back, ny + j).astype(f32)
        rows = edge + 16
        lines = column.reshape((depth + 2) * rows, 128)
        for i in range(ny):
            k = i * nx + j
            low = pos[i] == 1
            for at, count, ends in (
                (0, 3, front[3 * wide_face + k].astype(f32)[edge - 3 :]),
                (3, edge, corners[k].astype(f32)),
                (edge + 3, 3, back[3 * wide_face + k].astype(f32)[:3]),
            ):
                first, last = ends, ends
                if ny == 1:
                    first, last = jnp.where(low, ends, 0.0), jnp.where(low, 0.0, ends)
                if ny == 1 or i == 0:
                    lines[pl.ds(at * rows + 7, count, stride=rows), :] = first
                if ny == 1 or i == 1:
                    lines[pl.ds(at * rows + 8 + edge, count, stride=rows), :] = last
        for dy in range(3):
            piece = column[:, 7 + dy : 7 + dy + edge].astype(bf16)
            flanks[:, :, dy * 128 : dy * 128 + 128] = piece
        left = jnp.concatenate(
            [flanks[dz : dz + depth].reshape(depth * edge, 384) for dz in range(3)], axis=1
        )
        right = jnp.concatenate([taps[:, 0:128], taps[:, 256:384]], axis=1)
        extra = jnp.dot(left, right, preferred_element_type=f32)
        low = pos[ny + j] == 1
        first, last = extra[:, :128], extra[:, 128:]
        if nx == 1:
            first, last = jnp.where(low, first, 0.0), jnp.where(low, 0.0, last)
        if nx == 1 or j == 0:
            flat[pl.ds(0, depth * edge, stride=edge), :] += first
        if nx == 1 or j == 1:
            flat[pl.ds(edge - 1, depth * edge, stride=edge), :] += last

    def sum_step(k, carry):
        return carry + jnp.sum(act[k].reshape(edge * 2, 8, 128), axis=0)

    total = lax.fori_loop(2, edge + 2, sum_step, jnp.zeros((8, 128), f32), unroll=4)
    mean = jnp.sum(total, axis=0, keepdims=True) / edge**3

    def spread_step(k, carry):
        off = act[k].reshape(edge * 2, 8, 128) - mean
        return carry + jnp.sum(off * off, axis=0)

    total = lax.fori_loop(2, edge + 2, spread_step, jnp.zeros((8, 128), f32), unroll=4)
    put_stats(stats, mean, jnp.sum(total, axis=0, keepdims=True))


def put_stats(stats, mean, spread):
    both = jnp.concatenate([mean, spread], axis=0)
    stats[...] = jnp.broadcast_to(both[None], stats.shape)


def group_sums(row, width):
    lane = lax.broadcasted_iota(jnp.int32, row.shape, 1)
    size, step = row.shape[1], 1
    while step < width:
        above, below = pltpu.roll(row, size - step, 1), pltpu.roll(row, step, 1)
        row = row + jnp.where(jnp.bitwise_and(lane, step) == 0, above, below)
        step *= 2
    return row


def read_stats(stats, rows):
    devices, _, channels = stats.shape
    width = channels // GROUPS
    means, spreads = stats[:, 0, :], stats[:, 1, :]

    def grouped(row):
        return group_sums(jnp.broadcast_to(row, (8, channels)), width)[0:1]

    mean = grouped(jnp.sum(means, axis=0, keepdims=True)) / (devices * width)
    off = means - mean
    total = grouped(jnp.sum(spreads + rows * (off * off), axis=0, keepdims=True))
    return mean, lax.rsqrt(total / (rows * devices * width) + EPSILON)


def silu_of_double(h):
    return h + h * jnp.tanh(h)


def norm_kernel(ny, nx, pos, act, stats, gain, offset, out, pooled, *refs):
    y_edges, x_edges, corners, half = refs
    depth, edge = act.shape[0], act.shape[1]
    deep, deep_depth = edge // 2, depth // 2
    f32, bf16 = jnp.float32, jnp.bfloat16
    mean, scale = read_stats(stats, float(edge**3))
    scale = scale * (0.5 * gain[...])
    shift = 0.5 * offset[...]
    for k in range(deep_depth):
        value = silu_of_double((act[2 * k : 2 * k + 2] - mean) * scale + shift).astype(bf16)
        if 0 < k < deep_depth - 1:
            out[2 * k - 2 : 2 * k] = value
        value = value.astype(f32)
        value = (value[0] + value[1]).reshape(deep, 2, edge, 128)
        half[k] = (value[:, 0] + value[:, 1]).reshape(deep * edge, 128)
        lines = half.at[k]
        pair = lines[pl.ds(0, deep * deep, stride=2), :] + lines[pl.ds(1, deep * deep, stride=2), :]
        pair = (pair * 0.125).astype(bf16).astype(f32).reshape(deep, deep, 128)
        if k == 0 or k == deep_depth - 1:
            inside = pos[ny + nx + (0 if k == 0 else 1)] == 1
            pair = jnp.where(inside, pair, 0.0)
        pooled[k] = pair
    lines = pooled.reshape(deep_depth * deep * deep, 128)
    rows = deep_depth * deep
    first_x = lines[pl.ds(0, rows, stride=deep), :]
    last_x = lines[pl.ds(deep - 1, rows, stride=deep), :]
    first_y, last_y = (pooled[:, y].reshape(rows, 128) for y in (0, deep - 1))
    ends = []
    for y in (0, deep - 1):
        for x in (0, deep - 1):
            ends.append(lines[pl.ds(y * deep + x, deep_depth, stride=deep * deep), :])
    if ny == 1:
        above, left = pos[0] == 1, pos[1] == 1
        y_edges[0] = jnp.where(above, first_y, last_y).astype(bf16)
        x_edges[0] = jnp.where(left, first_x, last_x).astype(bf16)
        corners[0, 0:deep_depth] = jnp.where(
            above, jnp.where(left, ends[0], ends[1]), jnp.where(left, ends[2], ends[3])
        )
    else:
        y_edges[0], y_edges[1] = first_y.astype(bf16), last_y.astype(bf16)
        x_edges[0], x_edges[1] = first_x.astype(bf16), last_x.astype(bf16)
        for k in range(4):
            corners[k, 0:deep_depth] = ends[k]


def stack_kernel(*refs):
    out = refs[-1]
    for k in range(out.shape[0]):
        out[k] = refs[k][...]


def stack(*arrays):
    vmem = pl.BlockSpec(memory_space=pltpu.VMEM)
    return pl.pallas_call(
        stack_kernel,
        out_shape=jax.ShapeDtypeStruct((len(arrays),) + arrays[0].shape, arrays[0].dtype),
        in_specs=[vmem] * len(arrays),
        out_specs=vmem,
        compiler_params=pltpu.CompilerParams(vmem_limit_bytes=VMEM_BYTES),
    )(*arrays)


def place_kernel(tiles, pos, own, held, kernel):
    shard, part = own.shape[1], held.shape[3]
    tile, mine = pos[pos.shape[0] - 2], pos[pos.shape[0] - 1]

    def place(rows, at):
        for tap in range(27):
            lane = tap % 9 * 128
            kernel[tap // 9, pl.ds(at, rows.shape[1]), lane : lane + 128] = rows[tap]

    place(own, pl.multiple_of(tile * shard, shard))
    for piece in range(held.shape[0]):
        at = jnp.bitwise_xor(mine, piece) * part
        for k in range(1, tiles):
            base = lax.rem(tile + tiles - k, tiles) * shard
            place(held.at[piece, k - 1], pl.multiple_of(base + at, part))


def deep_kernel(ny, nx, pos, pooled, y_halos, x_halos, corners, kernel, *refs):
    act, stats, grid, packed = refs
    depth, deep = pooled.shape[0], pooled.shape[1]
    f32 = jnp.float32
    grid[...] = jnp.zeros(grid.shape, f32)
    grid[:, 1 : deep + 1, 8:16] = pooled[...]
    for i in range(ny):
        at = jnp.where(pos[i] == 1, 0, deep + 1)
        grid[:, at, 8:16] = y_halos[i].astype(f32).reshape(depth, deep, 128)
    pitch = (deep + 2) * 24
    flat = grid.reshape(depth * pitch, 128)
    for j in range(nx):
        left = pos[ny + j] == 1
        column = x_halos[j].astype(f32).reshape(depth, deep, 128)
        for side, here in ((7, left), (16, jnp.logical_not(left))):
            if nx == 2 and side != (7, 16)[j]:
                continue
            for z in range(depth):
                kept = column[z] if nx == 2 else jnp.where(here, column[z], 0.0)
                flat[pl.ds(z * pitch + 24 + side, deep, stride=24), :] = kept
            for i in range(ny):
                end = corners[i * nx + j, 0:depth]
                above = pos[i] == 1
                for y, there in ((0, above), (deep + 1, jnp.logical_not(above))):
                    if ny == 2 and y != (0, deep + 1)[i]:
                        continue
                    kept = end
                    if nx == 1:
                        kept = jnp.where(jnp.logical_and(here, there), end, 0.0)
                    flat[pl.ds(y * 24 + side, depth, stride=pitch), :] = kept

    for dx in range(3):
        plane = grid[:, :, 7 + dx : 15 + dx]
        for y in range(deep + 1):
            both = jnp.concatenate([plane[:, y], plane[:, y + 1]], axis=1)
            packed[:, y // 2, y % 2, :, dx * 128 : dx * 128 + 128] = both.astype(jnp.bfloat16)

    rows = deep**3
    total = None
    for dz in range(3):
        left = jnp.concatenate(
            [
                packed[dz : dz + deep, dy // 2 : dy // 2 + deep // 2, dy % 2].reshape(rows, 384)
                for dy in range(3)
            ],
            axis=1,
        )
        term = lax.dot_general(
            left, kernel[dz], (((1,), (1,)), ((), ())), preferred_element_type=f32
        )
        total = term if total is None else total + term
    act[...] = total
    mean = jnp.sum(total, axis=0, keepdims=True) / rows
    off = total - mean
    put_stats(stats, mean, jnp.sum(off * off, axis=0, keepdims=True))


def final_kernel(_, act, stats, gain, offset, up, mid, out, wide, held, sems):
    edge = mid.shape[0]
    deep = edge // 2
    f32 = jnp.float32
    mean, scale = read_stats(stats, float(deep**3))
    scale = scale * (0.5 * gain[...])
    value = silu_of_double((act[...] - mean) * scale + 0.5 * offset[...]).astype(jnp.bfloat16)
    lifted = jnp.dot(value, up[...], preferred_element_type=f32)
    wide[pl.ds(0, deep**3, stride=2), :] = lifted
    wide[pl.ds(1, deep**3, stride=2), :] = lifted
    size = deep * edge
    copies = []
    for k in range(deep):
        add = wide[k * size : k * size + size, :].reshape(1, deep, 1, edge, 128)
        old = mid[2 * k : 2 * k + 2].astype(f32).reshape(2, deep, 2, edge, 128)
        held[2 * k : 2 * k + 2] = (old + add).astype(jnp.bfloat16).reshape(2, edge, edge, 128)
        copy = pltpu.make_async_copy(
            held.at[2 * k : 2 * k + 2], out.at[2 * k : 2 * k + 2], sems.at[k]
        )
        copy.start()
        copies.append(copy)
    for copy in copies:
        copy.wait()


def body(
    features, conv_weight, gain_mid, offset_mid, deep_weight, gain_deep, offset_deep, up_weight
):
    f32, bf16 = jnp.float32, jnp.bfloat16
    edge, channels = features.shape[0], features.shape[3]
    deep = edge // 2
    deep_channels = gain_deep.shape[0]
    square = Square()
    tiles = square.tiles
    devices = lax.axis_size("gz") * tiles
    y_low, x_low = square.low_sides()
    ny, nx = len(y_low), len(x_low)
    axes = split_axes(deep_weight.shape[4])
    mine = sum(lax.axis_index(axis) % 2 * 2**k for k, axis in enumerate(axes))
    depth_at = lax.axis_index("gz")
    inside = [depth_at > 0, depth_at < lax.axis_size("gz") - 1]
    pos = y_low + x_low + inside + [lax.axis_index("yx"), mine]
    pos = jnp.stack([jnp.asarray(v, jnp.int32) for v in pos])

    own = jnp.moveaxis(deep_weight, 4, 3).reshape(27, deep_weight.shape[4], channels)
    conv_weight = conv_weight.reshape(27, channels, channels)
    *edges, features, conv_weight, own = call(
        functools.partial(start_kernel, ny, nx),
        [
            ((ny, edge, edge, channels), bf16),
            ((nx, edge, edge, channels), bf16),
            ((ny * nx, edge, channels), bf16),
            (features.shape, bf16),
            (conv_weight.shape, bf16),
            (own.shape, bf16),
        ],
        [((edge * edge, 8, channels), f32), pltpu.SemaphoreType.DMA((6,))],
        pos,
        features,
        conv_weight,
        own,
        nbytes=5 << 20,
        in_hbm=True,
    )
    halos = square.halos(*(list(piece) for piece in edges))
    half_act = ((deep, edge, edge, channels), f32)
    half_grid = ((deep + 2, edge + 2, edge, channels), bf16)
    conv_flops = 27 * channels * channels * edge**3
    near, taps, pairs, piece = call(
        front_half_kernel,
        [
            half_act,
            ((9 * channels, 3 * channels), bf16),
            ((12 * channels, 2 * channels), bf16),
            ((27, own.shape[1] // 2 ** len(axes), channels), bf16),
        ],
        [half_grid],
        pos,
        features,
        conv_weight,
        own,
        flops=conv_flops,
        nbytes=3 << 20,
    )
    piece, (y, x, corner) = lax.optimization_barrier((piece, halos))
    y, x, corner = jnp.stack(y), jnp.stack(x), jnp.stack(corner)
    face = ((3 * (edge + ny + nx) + ny * nx, edge, channels), bf16)
    faces = call(
        functools.partial(face_kernel, ny, nx), [face, face], [], pos, features, y, x, corner
    )
    front, back = swap_depth(*faces)
    got = rotate_shards(piece)
    (far,) = call(
        back_half_kernel,
        [half_act],
        [half_grid],
        pos,
        features,
        taps,
        pairs,
        corner,
        flops=conv_flops,
        nbytes=3 << 20,
    )
    act, stats = call(
        functools.partial(rim_kernel, ny, nx),
        [((edge + 4, edge, edge, channels), f32), ((devices, 2, channels), f32)],
        [
            ((4, edge + 2, edge, channels), bf16),
            ((edge + 6, edge + 16, channels), f32),
            ((edge + 6, edge, 3 * channels), bf16),
        ],
        pos,
        features,
        near,
        far,
        y,
        x,
        corner,
        front,
        back,
        taps,
        pairs,
    )
    stats, *got = lax.optimization_barrier((stats, *got))
    stats = share(stats)
    held = stack(*got)[None]
    for axis in axes:
        other = swap(held, axis, 1)
        if axis == "cand":
            stats, other = lax.optimization_barrier((stats, other))
        held = stack(held, other)
        held = held.reshape((-1,) + held.shape[2:])
    out, pooled, *edges = call(
        functools.partial(norm_kernel, ny, nx),
        [
            ((edge, edge, edge, channels), bf16),
            ((deep + 2, deep, deep, channels), f32),
            ((ny, (deep + 2) * deep, channels), bf16),
            ((nx, (deep + 2) * deep, channels), bf16),
            ((ny * nx, 16, channels), f32),
        ],
        [((deep + 2, deep * edge, channels), f32)],
        pos,
        act,
        stats,
        gain_mid.reshape(1, channels),
        offset_mid.reshape(1, channels),
        flops=20 * channels * edge**3,
        nbytes=3 << 20,
    )
    y, x, corner = square.halos(*(list(piece) for piece in edges))
    (kernel,) = call(
        functools.partial(place_kernel, tiles),
        [((3, deep_channels, 9 * channels), bf16)],
        [],
        pos,
        own,
        held,
        nbytes=4 << 20,
    )
    deep_act, stats = call(
        functools.partial(deep_kernel, ny, nx),
        [((deep**3, deep_channels), f32), ((devices, 2, deep_channels), f32)],
        [
            ((deep + 2, deep + 2, 24, channels), f32),
            ((deep + 2, deep // 2 + 1, 2, 16, 3 * channels), bf16),
        ],
        pos,
        pooled,
        jnp.stack(y),
        jnp.stack(x),
        jnp.stack(corner),
        kernel,
        flops=2 * 27 * channels * deep_channels * deep**3,
        nbytes=4 << 20,
    )
    stats = share(stats)
    (decoded,) = call(
        final_kernel,
        [((edge, edge, edge, channels), bf16)],
        [
            ((2 * deep**3, channels), f32),
            ((edge, edge, edge, channels), bf16),
            pltpu.SemaphoreType.DMA((deep,)),
        ],
        pos,
        deep_act,
        stats,
        gain_deep.reshape(1, deep_channels),
        offset_deep.reshape(1, deep_channels),
        up_weight,
        out,
        flops=4 * deep_channels * channels * deep**3,
        nbytes=3 << 20,
        out_hbm=True,
    )
    return decoded


def solution(mesh):
    placed = (
        P(("cand", "gz"), "yx", None, None),
        P(),
        P(),
        P(),
        P(None, None, None, None, "yx"),
        P(),
        P(),
        P(),
    )
    return jax.shard_map(
        body,
        mesh=mesh,
        in_specs=placed,
        out_specs=P(("cand", "gz"), "yx", None, None),
        check_vma=False,
    )
```

```python
import functools
import math

import jax
import jax.numpy as jnp
from jax import lax
from jax.experimental import pallas as pl
from jax.experimental.pallas import tpu as pltpu
from jax.sharding import PartitionSpec as P

GROUPS = 32
EPSILON = 1e-05
PART = ("gz", "yx")
VMEM_BYTES = 32 * 1024 * 1024


class Square:
    def __init__(self):
        self.tiles = lax.axis_size("yx")
        self.side = math.isqrt(self.tiles)
        tile = lax.axis_index("yx")
        self.row, self.column = tile // self.side, tile % self.side
        self.folded = self.side == 2
        self.steps = (0,) if self.folded else (-1, 1)

    def low_sides(self):
        if self.folded:
            return [self.row], [self.column]
        return [1, 0], [1, 0]

    def route(self, down, right):
        pairs = []
        for tile in range(self.tiles):
            row, column = tile // self.side + down, tile % self.side + right
            if 0 <= row < self.side and 0 <= column < self.side:
                pairs.append((tile, row * self.side + column))
        return pairs

    def swap_route(self, mask):
        return [(tile, tile ^ mask) for tile in range(self.tiles)]

    def halos(self, y_edges, x_edges, corners):
        if self.folded:
            y = lax.ppermute(y_edges[0], "yx", self.swap_route(2))
            x = lax.ppermute(x_edges[0], "yx", self.swap_route(1))
            corner = lax.ppermute(corners[0], "yx", self.swap_route(3))
            return [y], [x], [corner]
        y = [lax.ppermute(y_edges[k], "yx", self.route((1, -1)[1 - k], 0)) for k in (1, 0)]
        x = [lax.ppermute(x_edges[k], "yx", self.route(0, (1, -1)[1 - k])) for k in (1, 0)]
        corner = [
            lax.ppermute(corners[2 * k + j], "yx", self.route((1, -1)[1 - k], (1, -1)[1 - j]))
            for k in (1, 0)
            for j in (1, 0)
        ]
        return y, x, corner


def swap_depth(low, high):
    size = lax.axis_size("gz")
    up = [(i, i + 1) for i in range(size - 1)]
    return lax.ppermute(high, "gz", up), lax.ppermute(low, "gz", [(j, i) for i, j in up])


def split_axes(rows):
    return ("cand", "gz")[: 2 if rows % 64 == 0 else 0]


def rotate_shards(piece):
    tiles = lax.axis_size("yx")
    return [
        lax.ppermute(piece, "yx", [(i, (i + k) % tiles) for i in range(tiles)]) for k in range(1, tiles)
    ]


def swap(block, axis, mask):
    return lax.ppermute(block, axis, [(i, i ^ mask) for i in range(lax.axis_size(axis))])


def share(stats):
    return lax.all_to_all(stats, PART, 0, 0)


def call(kernel, outs, scratch, scalars, *arrays, flops=0, nbytes=0, in_hbm=False, out_hbm=False):
    smem, vmem, hbm = (
        pl.BlockSpec(memory_space=space) for space in (pltpu.SMEM, pltpu.VMEM, pltpu.HBM)
    )
    if in_hbm:
        arrays = [pltpu.with_memory_space_constraint(array, pltpu.HBM) for array in arrays]
    return pl.pallas_call(
        kernel,
        out_shape=[jax.ShapeDtypeStruct(shape, dtype) for shape, dtype in outs],
        in_specs=[smem] + [hbm if in_hbm else vmem] * len(arrays),
        out_specs=[hbm if out_hbm else vmem] * len(outs),
        scratch_shapes=[pltpu.VMEM(*entry) if isinstance(entry, tuple) else entry for entry in scratch],
        compiler_params=pltpu.CompilerParams(vmem_limit_bytes=VMEM_BYTES),
        cost_estimate=pl.CostEstimate(flops=flops, bytes_accessed=nbytes, transcendentals=0),
    )(scalars, *arrays)


def start_kernel(ny, nx, pos, x_in, w_in, d_in, y_edges, x_edges, corners, x, w, d, lines, sems):
    edge = x.shape[0]
    size = edge // 4
    first = [
        pltpu.make_async_copy(x_in.at[pl.ds(k * size, size)], x.at[pl.ds(k * size, size)], sems.at[k])
        for k in range(4)
    ]
    later = [pltpu.make_async_copy(w_in, w, sems.at[4]), pltpu.make_async_copy(d_in, d, sems.at[5])]
    for copy in first + later:
        copy.start()
    for copy in first:
        copy.wait()
    f32, bf16 = jnp.float32, jnp.bfloat16
    for i in range(ny):
        at = jnp.where(pos[i] == 1, 0, edge - 1) if ny == 1 else (0, edge - 1)[i]
        y_edges[i] = x[:, at]
    flat = lines.reshape(edge * edge * 8, 128)
    for j in range(nx):
        first = x[:, :, 0:8].astype(f32)
        last = x[:, :, edge - 8 : edge].astype(f32)
        if nx == 1:
            low = pos[ny] == 1
            turned = pltpu.roll(last.reshape(edge * edge, 8, 128), 1, 1)
            kept = jnp.where(low, first.reshape(edge * edge, 8, 128), turned)
        else:
            kept = (first, pltpu.roll(last.reshape(edge * edge, 8, 128), 1, 1))[j]
        lines[...] = kept.reshape(edge * edge, 8, 128)
        column = flat[pl.ds(0, edge * edge, stride=8), :]
        x_edges[j] = column.astype(bf16).reshape(edge, edge, 128)
        for i in range(ny):
            first_y = flat[pl.ds(0, edge, stride=8 * edge), :]
            last_y = flat[pl.ds(8 * (edge - 1), edge, stride=8 * edge), :]
            kept = jnp.where(pos[i] == 1, first_y, last_y) if ny == 1 else (first_y, last_y)[i]
            corners[i * nx + j] = kept.astype(bf16)
    for copy in later:
        copy.wait()


def face_kernel(ny, nx, _, x, y_halos, x_halos, corners, low, high):
    edge = x.shape[0]
    wide = edge + ny + nx
    for face, at in ((low, 0), (high, edge - 3)):
        for k in range(3):
            row = k * wide
            face[row : row + edge] = x[at + k]
            for i in range(ny):
                face[row + edge + i] = y_halos[i, at + k]
            for j in range(nx):
                face[row + edge + ny + j] = x_halos[j, at + k]
        for k in range(ny * nx):
            face[3 * wide + k] = corners[k]


def spread_taps(weight, taps):
    for tap in range(27):
        row, lane = tap // 3 * 128, tap % 3 * 128
        taps[row : row + 128, lane : lane + 128] = weight[tap]


def pair_taps(weight, pairs):
    for dz in range(3):
        for line in range(4):
            row = (dz * 4 + line) * 128
            for out in range(2):
                lane = out * 128
                if 0 <= line - out < 3:
                    block = weight[dz * 9 + (line - out) * 3 + 2]
                else:
                    block = jnp.zeros((128, 128), pairs.dtype)
                pairs[row : row + 128, lane : lane + 128] = block


def join_x(wide, edge):
    place = lax.broadcasted_iota(jnp.int32, wide.shape[:2] + (128,), 1)
    after = jnp.where(place > 0, pltpu.roll(wide[:, :, :128], 1, 1), 0.0)
    before = jnp.where(place < edge - 1, pltpu.roll(wide[:, :, 256:], edge - 1, 1), 0.0)
    return wide[:, :, 128:256] + after + before


def convolve(grid, count, taps, pairs, put):
    edge = grid.shape[2]
    planes = min(count, 4)
    rows = planes * edge * edge
    place = lax.broadcasted_iota(jnp.int32, (planes * edge, edge, 128), 1)
    halved = grid.reshape(grid.shape[0], edge // 2 + 1, 2, edge, 128)
    for z in range(0, count, planes):
        left = jnp.concatenate(
            [
                grid[z + dz : z + dz + planes, dy : dy + edge].reshape(rows, 128)
                for dz in range(3)
                for dy in range(3)
            ],
            axis=1,
        )
        wide = jnp.dot(left, taps[:, 0:256], preferred_element_type=jnp.float32)
        wide = wide.reshape(planes * edge, edge, 256)
        left = jnp.concatenate(
            [
                halved[z + dz : z + dz + planes, line // 2 : line // 2 + edge // 2, line % 2].reshape(
                    rows // 2, 128
                )
                for dz in range(3)
                for line in range(4)
            ],
            axis=1,
        )
        two = jnp.dot(left, pairs[...], preferred_element_type=jnp.float32)
        two = two.reshape(planes * edge // 2, edge, 256)
        two = jnp.stack([two[:, :, :128], two[:, :, 128:]], axis=1).reshape(planes * edge, edge, 128)
        after = jnp.where(place > 0, pltpu.roll(wide[:, :, :128], 1, 1), 0.0)
        before = jnp.where(place < edge - 1, pltpu.roll(two, edge - 1, 1), 0.0)
        new = wide[:, :, 128:256] + after + before
        put(z, new.reshape(planes, edge, edge, 128))


def clear_sides(grid):
    blank = jnp.zeros(grid.shape[:1] + grid.shape[2:], grid.dtype)
    grid[:, 0] = blank
    grid[:, grid.shape[1] - 1] = blank


def local_planes(x, lo, count, taps, pairs, grid, act):
    edge = x.shape[0]
    clear_sides(grid)
    first, last = max(lo - 1, 0), min(lo + count + 1, edge)
    if first > lo - 1:
        grid[0] = jnp.zeros(grid.shape[1:], grid.dtype)
    if last < lo + count + 1:
        grid[count + 1] = jnp.zeros(grid.shape[1:], grid.dtype)
    grid[first - lo + 1 : last - lo + 1, 1 : edge + 1] = x[first:last]

    def put(z, new):
        act[z : z + new.shape[0]] = new

    convolve(grid, count, taps, pairs, put)


def front_half_kernel(pos, x, weight, deep_weight, act, taps, pairs, piece, grid):
    spread_taps(weight, taps)
    pair_taps(weight, pairs)
    size = piece.shape[1]
    if size < deep_weight.shape[1]:
        piece[...] = deep_weight[:, pl.ds(pl.multiple_of(pos[pos.shape[0] - 1] * size, size), size)]
    else:
        piece[...] = deep_weight[...]
    local_planes(x, 0, act.shape[0], taps, pairs, grid, act)


def rim_kernel(ny, nx, pos, *refs):
    x, near, y_halos, x_halos, corners, front, back, taps, pairs, act, stats, half_grid, grid, column, flanks = refs
    edge = x.shape[0]
    half = edge // 2
    wide_face = edge + ny + nx
    depth = edge + 4
    f32, bf16 = jnp.float32, jnp.bfloat16
    act[2 : 2 + half] = near[...]
    local_planes(x, half, half, taps, pairs, half_grid, act.at[2 + half : 2 + edge])

    clear_sides(grid)
    for face, halo_at, own_at, own, out_at, touched, dz in (
        (front, 0, 3, 0, 0, 2, 0),
        (back, 1, 0, edge - 1, depth - 2, depth - 3, 2),
    ):
        for k in range(3):
            grid[halo_at + k, 1 : edge + 1] = face[k * wide_face : k * wide_face + edge]
        grid[own_at, 1 : edge + 1] = x[own]

        def put(z, new):
            act[out_at + z : out_at + z + new.shape[0]] = new

        convolve(grid, 2, taps, pairs, put)
        beside = halo_at + (2 if dz == 0 else 0)
        left = jnp.concatenate(
            [grid[beside, dy : dy + edge].reshape(edge * edge, 128) for dy in range(3)], axis=1
        )
        wide = jnp.dot(left, taps[dz * 384 : dz * 384 + 384, :], preferred_element_type=f32)
        act[touched] += join_x(wide.reshape(edge, edge, 384), edge)

    def rim(face, row):
        return jnp.stack([face[k * wide_face + edge + row] for k in range(3)])

    for i in range(ny):
        low = pos[i] == 1
        line = jnp.concatenate([rim(front, i), y_halos[i], rim(back, i)], axis=0)
        left = jnp.concatenate(
            [line[dz : dz + depth].reshape(depth * edge, 128) for dz in range(3)], axis=1
        )
        start = jnp.where(low, 0, 256)
        right = jnp.concatenate(
            [taps[pl.ds(pl.multiple_of(start + dz * 384, 128), 128), :] for dz in range(3)], axis=0
        )
        wide = jnp.dot(left, right, preferred_element_type=f32)
        act[:, jnp.where(low, 0, edge - 1)] += join_x(wide.reshape(depth, edge, 384), edge)

    flat = act.reshape(depth * edge * edge, 128)
    for j in range(nx):
        column[:, 0:8] = jnp.zeros((depth + 2, 8, 128), f32)
        column[:, 8 + edge :] = jnp.zeros((depth + 2, 8, 128), f32)
        column[3 : edge + 3, 8 : 8 + edge] = x_halos[j].astype(f32)
        column[0:3, 8 : 8 + edge] = rim(front, ny + j).astype(f32)
        column[edge + 3 :, 8 : 8 + edge] = rim(back, ny + j).astype(f32)
        rows = edge + 16
        lines = column.reshape((depth + 2) * rows, 128)
        for i in range(ny):
            k = i * nx + j
            low = pos[i] == 1
            for at, count, ends in (
                (0, 3, front[3 * wide_face + k].astype(f32)[edge - 3 :]),
                (3, edge, corners[k].astype(f32)),
                (edge + 3, 3, back[3 * wide_face + k].astype(f32)[:3]),
            ):
                first, last = ends, ends
                if ny == 1:
                    first, last = jnp.where(low, ends, 0.0), jnp.where(low, 0.0, ends)
                if ny == 1 or i == 0:
                    lines[pl.ds(at * rows + 7, count, stride=rows), :] = first
                if ny == 1 or i == 1:
                    lines[pl.ds(at * rows + 8 + edge, count, stride=rows), :] = last
        for dy in range(3):
            piece = column[:, 7 + dy : 7 + dy + edge].astype(bf16)
            flanks[:, :, dy * 128 : dy * 128 + 128] = piece
        left = jnp.concatenate(
            [flanks[dz : dz + depth].reshape(depth * edge, 384) for dz in range(3)], axis=1
        )
        right = jnp.concatenate([taps[:, 0:128], taps[:, 256:384]], axis=1)
        extra = jnp.dot(left, right, preferred_element_type=f32)
        low = pos[ny + j] == 1
        first, last = extra[:, :128], extra[:, 128:]
        if nx == 1:
            first, last = jnp.where(low, first, 0.0), jnp.where(low, 0.0, last)
        if nx == 1 or j == 0:
            flat[pl.ds(0, depth * edge, stride=edge), :] += first
        if nx == 1 or j == 1:
            flat[pl.ds(edge - 1, depth * edge, stride=edge), :] += last

    def sum_step(k, carry):
        return carry + jnp.sum(act[k].reshape(edge * 2, 8, 128), axis=0)

    total = lax.fori_loop(2, edge + 2, sum_step, jnp.zeros((8, 128), f32), unroll=4)
    mean = jnp.sum(total, axis=0, keepdims=True) / edge**3

    def spread_step(k, carry):
        off = act[k].reshape(edge * 2, 8, 128) - mean
        return carry + jnp.sum(off * off, axis=0)

    total = lax.fori_loop(2, edge + 2, spread_step, jnp.zeros((8, 128), f32), unroll=4)
    put_stats(stats, mean, jnp.sum(total, axis=0, keepdims=True))


def put_stats(stats, mean, spread):
    both = jnp.concatenate([mean, spread], axis=0)
    stats[...] = jnp.broadcast_to(both[None], stats.shape)


def group_sums(row, width):
    lane = lax.broadcasted_iota(jnp.int32, row.shape, 1)
    size, step = row.shape[1], 1
    while step < width:
        above, below = pltpu.roll(row, size - step, 1), pltpu.roll(row, step, 1)
        row = row + jnp.where(jnp.bitwise_and(lane, step) == 0, above, below)
        step *= 2
    return row


def read_stats(stats, rows):
    devices, _, channels = stats.shape
    width = channels // GROUPS
    means, spreads = stats[:, 0, :], stats[:, 1, :]

    def grouped(row):
        return group_sums(jnp.broadcast_to(row, (8, channels)), width)[0:1]

    mean = grouped(jnp.sum(means, axis=0, keepdims=True)) / (devices * width)
    off = means - mean
    total = grouped(jnp.sum(spreads + rows * (off * off), axis=0, keepdims=True))
    return mean, lax.rsqrt(total / (rows * devices * width) + EPSILON)


def silu_of_double(h):
    return h + h * jnp.tanh(h)


def norm_kernel(ny, nx, pos, act, stats, gain, offset, out, pooled, *refs):
    y_edges, x_edges, corners, half = refs
    depth, edge = act.shape[0], act.shape[1]
    deep, deep_depth = edge // 2, depth // 2
    f32, bf16 = jnp.float32, jnp.bfloat16
    mean, scale = read_stats(stats, float(edge**3))
    scale = scale * (0.5 * gain[...])
    shift = 0.5 * offset[...]
    for k in range(deep_depth):
        value = silu_of_double((act[2 * k : 2 * k + 2] - mean) * scale + shift).astype(bf16)
        if 0 < k < deep_depth - 1:
            out[2 * k - 2 : 2 * k] = value
        value = value.astype(f32)
        value = (value[0] + value[1]).reshape(deep, 2, edge, 128)
        half[k] = (value[:, 0] + value[:, 1]).reshape(deep * edge, 128)
        lines = half.at[k]
        pair = lines[pl.ds(0, deep * deep, stride=2), :] + lines[pl.ds(1, deep * deep, stride=2), :]
        pair = (pair * 0.125).astype(bf16).astype(f32).reshape(deep, deep, 128)
        if k == 0 or k == deep_depth - 1:
            inside = pos[ny + nx + (0 if k == 0 else 1)] == 1
            pair = jnp.where(inside, pair, 0.0)
        pooled[k] = pair
    lines = pooled.reshape(deep_depth * deep * deep, 128)
    rows = deep_depth * deep
    first_x = lines[pl.ds(0, rows, stride=deep), :]
    last_x = lines[pl.ds(deep - 1, rows, stride=deep), :]
    first_y, last_y = (pooled[:, y].reshape(rows, 128) for y in (0, deep - 1))
    ends = []
    for y in (0, deep - 1):
        for x in (0, deep - 1):
            ends.append(lines[pl.ds(y * deep + x, deep_depth, stride=deep * deep), :])
    if ny == 1:
        above, left = pos[0] == 1, pos[1] == 1
        y_edges[0] = jnp.where(above, first_y, last_y).astype(bf16)
        x_edges[0] = jnp.where(left, first_x, last_x).astype(bf16)
        corners[0, 0:deep_depth] = jnp.where(
            above, jnp.where(left, ends[0], ends[1]), jnp.where(left, ends[2], ends[3])
        )
    else:
        y_edges[0], y_edges[1] = first_y.astype(bf16), last_y.astype(bf16)
        x_edges[0], x_edges[1] = first_x.astype(bf16), last_x.astype(bf16)
        for k in range(4):
            corners[k, 0:deep_depth] = ends[k]


def stack_kernel(*refs):
    out = refs[-1]
    for k in range(out.shape[0]):
        out[k] = refs[k][...]


def stack(*arrays):
    vmem = pl.BlockSpec(memory_space=pltpu.VMEM)
    return pl.pallas_call(
        stack_kernel,
        out_shape=jax.ShapeDtypeStruct((len(arrays),) + arrays[0].shape, arrays[0].dtype),
        in_specs=[vmem] * len(arrays),
        out_specs=vmem,
        compiler_params=pltpu.CompilerParams(vmem_limit_bytes=VMEM_BYTES),
    )(*arrays)


def place_kernel(tiles, pos, own, held, kernel):
    shard, part = own.shape[1], held.shape[3]
    tile, mine = pos[pos.shape[0] - 2], pos[pos.shape[0] - 1]

    def place(rows, at):
        for tap in range(27):
            lane = tap % 9 * 128
            kernel[tap // 9, pl.ds(at, rows.shape[1]), lane : lane + 128] = rows[tap]

    place(own, pl.multiple_of(tile * shard, shard))
    for piece in range(held.shape[0]):
        at = jnp.bitwise_xor(mine, piece) * part
        for k in range(1, tiles):
            base = lax.rem(tile + tiles - k, tiles) * shard
            place(held.at[piece, k - 1], pl.multiple_of(base + at, part))


def deep_kernel(ny, nx, pos, pooled, y_halos, x_halos, corners, kernel, *refs):
    act, stats, grid, packed = refs
    depth, deep = pooled.shape[0], pooled.shape[1]
    f32 = jnp.float32
    grid[...] = jnp.zeros(grid.shape, f32)
    grid[:, 1 : deep + 1, 8:16] = pooled[...]
    for i in range(ny):
        at = jnp.where(pos[i] == 1, 0, deep + 1)
        grid[:, at, 8:16] = y_halos[i].astype(f32).reshape(depth, deep, 128)
    pitch = (deep + 2) * 24
    flat = grid.reshape(depth * pitch, 128)
    for j in range(nx):
        left = pos[ny + j] == 1
        column = x_halos[j].astype(f32).reshape(depth, deep, 128)
        for side, here in ((7, left), (16, jnp.logical_not(left))):
            if nx == 2 and side != (7, 16)[j]:
                continue
            for z in range(depth):
                kept = column[z] if nx == 2 else jnp.where(here, column[z], 0.0)
                flat[pl.ds(z * pitch + 24 + side, deep, stride=24), :] = kept
            for i in range(ny):
                end = corners[i * nx + j, 0:depth]
                above = pos[i] == 1
                for y, there in ((0, above), (deep + 1, jnp.logical_not(above))):
                    if ny == 2 and y != (0, deep + 1)[i]:
                        continue
                    kept = end
                    if nx == 1:
                        kept = jnp.where(jnp.logical_and(here, there), end, 0.0)
                    flat[pl.ds(y * 24 + side, depth, stride=pitch), :] = kept

    for dx in range(3):
        plane = grid[:, :, 7 + dx : 15 + dx]
        for y in range(deep + 1):
            both = jnp.concatenate([plane[:, y], plane[:, y + 1]], axis=1)
            packed[:, y // 2, y % 2, :, dx * 128 : dx * 128 + 128] = both.astype(jnp.bfloat16)

    rows = deep**3
    total = None
    for dz in range(3):
        left = jnp.concatenate(
            [
                packed[dz : dz + deep, dy // 2 : dy // 2 + deep // 2, dy % 2].reshape(rows, 384)
                for dy in range(3)
            ],
            axis=1,
        )
        term = lax.dot_general(
            left, kernel[dz], (((1,), (1,)), ((), ())), preferred_element_type=f32
        )
        total = term if total is None else total + term
    act[...] = total
    mean = jnp.sum(total, axis=0, keepdims=True) / rows
    off = total - mean
    put_stats(stats, mean, jnp.sum(off * off, axis=0, keepdims=True))


def final_kernel(_, act, stats, gain, offset, up, mid, out, wide, held, sems):
    edge = mid.shape[0]
    deep = edge // 2
    f32 = jnp.float32
    mean, scale = read_stats(stats, float(deep**3))
    scale = scale * (0.5 * gain[...])
    shift = 0.5 * offset[...]
    planes = 2
    size = planes * deep * deep
    copies = []
    for k in range(0, deep, planes):
        value = act[k * deep * deep : k * deep * deep + size]
        value = silu_of_double((value - mean) * scale + shift).astype(jnp.bfloat16)
        lifted = jnp.dot(value, up[...], preferred_element_type=f32)
        lines = wide.at[k // planes]
        lines[pl.ds(0, size, stride=2), :] = lifted
        lines[pl.ds(1, size, stride=2), :] = lifted
        add = lines[...].reshape(planes, 1, deep, 1, edge, 128)
        at = pl.ds(2 * k, 2 * planes)
        old = mid[at].astype(f32).reshape(planes, 2, deep, 2, edge, 128)
        held[at] = (old + add).astype(jnp.bfloat16).reshape(2 * planes, edge, edge, 128)
        copy = pltpu.make_async_copy(held.at[at], out.at[at], sems.at[k // planes])
        copy.start()
        copies.append(copy)
    for copy in copies:
        copy.wait()


def body(
    features, conv_weight, gain_mid, offset_mid, deep_weight, gain_deep, offset_deep, up_weight
):
    f32, bf16 = jnp.float32, jnp.bfloat16
    edge, channels = features.shape[0], features.shape[3]
    deep = edge // 2
    deep_channels = gain_deep.shape[0]
    square = Square()
    tiles = square.tiles
    devices = lax.axis_size("gz") * tiles
    y_low, x_low = square.low_sides()
    ny, nx = len(y_low), len(x_low)
    axes = split_axes(deep_weight.shape[4])
    mine = sum(lax.axis_index(axis) % 2 * 2**k for k, axis in enumerate(axes))
    depth_at = lax.axis_index("gz")
    inside = [depth_at > 0, depth_at < lax.axis_size("gz") - 1]
    pos = y_low + x_low + inside + [lax.axis_index("yx"), mine]
    pos = jnp.stack([jnp.asarray(v, jnp.int32) for v in pos])

    own = jnp.moveaxis(deep_weight, 4, 3).reshape(27, deep_weight.shape[4], channels)
    conv_weight = conv_weight.reshape(27, channels, channels)
    *edges, features, conv_weight, own = call(
        functools.partial(start_kernel, ny, nx),
        [
            ((ny, edge, edge, channels), bf16),
            ((nx, edge, edge, channels), bf16),
            ((ny * nx, edge, channels), bf16),
            (features.shape, bf16),
            (conv_weight.shape, bf16),
            (own.shape, bf16),
        ],
        [((edge * edge, 8, channels), f32), pltpu.SemaphoreType.DMA((6,))],
        pos,
        features,
        conv_weight,
        own,
        nbytes=5 << 20,
        in_hbm=True,
    )
    halos = square.halos(*(list(piece) for piece in edges))
    half_act = ((deep, edge, edge, channels), f32)
    half_grid = ((deep + 2, edge + 2, edge, channels), bf16)
    conv_flops = 27 * channels * channels * edge**3
    near, taps, pairs, piece = call(
        front_half_kernel,
        [
            half_act,
            ((9 * channels, 3 * channels), bf16),
            ((12 * channels, 2 * channels), bf16),
            ((27, own.shape[1] // 2 ** len(axes), channels), bf16),
        ],
        [half_grid],
        pos,
        features,
        conv_weight,
        own,
        flops=conv_flops,
        nbytes=3 << 20,
    )
    piece, (y, x, corner) = lax.optimization_barrier((piece, halos))
    y, x, corner = jnp.stack(y), jnp.stack(x), jnp.stack(corner)
    face = ((3 * (edge + ny + nx) + ny * nx, edge, channels), bf16)
    faces = call(
        functools.partial(face_kernel, ny, nx), [face, face], [], pos, features, y, x, corner
    )
    front, back = swap_depth(*faces)
    got = rotate_shards(piece)
    act, stats = call(
        functools.partial(rim_kernel, ny, nx),
        [((edge + 4, edge, edge, channels), f32), ((devices, 2, channels), f32)],
        [
            half_grid,
            ((4, edge + 2, edge, channels), bf16),
            ((edge + 6, edge + 16, channels), f32),
            ((edge + 6, edge, 3 * channels), bf16),
        ],
        pos,
        features,
        near,
        y,
        x,
        corner,
        front,
        back,
        taps,
        pairs,
    )
    stats, *got = lax.optimization_barrier((stats, *got))
    stats = share(stats)
    held = stack(*got)[None]
    for axis in axes:
        other = swap(held, axis, 1)
        if axis == "cand":
            stats, other = lax.optimization_barrier((stats, other))
        held = stack(held, other)
        held = held.reshape((-1,) + held.shape[2:])
    out, pooled, *edges = call(
        functools.partial(norm_kernel, ny, nx),
        [
            ((edge, edge, edge, channels), bf16),
            ((deep + 2, deep, deep, channels), f32),
            ((ny, (deep + 2) * deep, channels), bf16),
            ((nx, (deep + 2) * deep, channels), bf16),
            ((ny * nx, 16, channels), f32),
        ],
        [((deep + 2, deep * edge, channels), f32)],
        pos,
        act,
        stats,
        gain_mid.reshape(1, channels),
        offset_mid.reshape(1, channels),
        flops=20 * channels * edge**3,
        nbytes=3 << 20,
    )
    y, x, corner = square.halos(*(list(piece) for piece in edges))
    (kernel,) = call(
        functools.partial(place_kernel, tiles),
        [((3, deep_channels, 9 * channels), bf16)],
        [],
        pos,
        own,
        held,
        nbytes=4 << 20,
    )
    deep_act, stats = call(
        functools.partial(deep_kernel, ny, nx),
        [((deep**3, deep_channels), f32), ((devices, 2, deep_channels), f32)],
        [
            ((deep + 2, deep + 2, 24, channels), f32),
            ((deep + 2, deep // 2 + 1, 2, 16, 3 * channels), bf16),
        ],
        pos,
        pooled,
        jnp.stack(y),
        jnp.stack(x),
        jnp.stack(corner),
        kernel,
        flops=2 * 27 * channels * deep_channels * deep**3,
        nbytes=4 << 20,
    )
    stats = share(stats)
    (decoded,) = call(
        final_kernel,
        [((edge, edge, edge, channels), bf16)],
        [
            ((deep // 2, 4 * deep * deep, channels), f32),
            ((edge, edge, edge, channels), bf16),
            pltpu.SemaphoreType.DMA((deep // 2,)),
        ],
        pos,
        deep_act,
        stats,
        gain_deep.reshape(1, deep_channels),
        offset_deep.reshape(1, deep_channels),
        up_weight,
        out,
        flops=4 * deep_channels * channels * deep**3,
        nbytes=3 << 20,
        out_hbm=True,
    )
    return decoded


def solution(mesh):
    placed = (
        P(("cand", "gz"), "yx", None, None),
        P(),
        P(),
        P(),
        P(None, None, None, None, "yx"),
        P(),
        P(),
        P(),
    )
    return jax.shard_map(
        body,
        mesh=mesh,
        in_specs=placed,
        out_specs=P(("cand", "gz"), "yx", None, None),
        check_vma=False,
    )
```

```python
import functools
import math

import jax
import jax.numpy as jnp
from jax import lax
from jax.experimental import pallas as pl
from jax.experimental.pallas import tpu as pltpu
from jax.sharding import PartitionSpec as P

GROUPS = 32
EPSILON = 1e-05
PART = ("gz", "yx")
VMEM_BYTES = 32 * 1024 * 1024


class Square:
    def __init__(self):
        self.tiles = lax.axis_size("yx")
        self.side = math.isqrt(self.tiles)
        tile = lax.axis_index("yx")
        self.row, self.column = tile // self.side, tile % self.side
        self.folded = self.side == 2
        self.steps = (0,) if self.folded else (-1, 1)

    def low_sides(self):
        if self.folded:
            return [self.row], [self.column]
        return [1, 0], [1, 0]

    def route(self, down, right):
        pairs = []
        for tile in range(self.tiles):
            row, column = tile // self.side + down, tile % self.side + right
            if 0 <= row < self.side and 0 <= column < self.side:
                pairs.append((tile, row * self.side + column))
        return pairs

    def swap_route(self, mask):
        return [(tile, tile ^ mask) for tile in range(self.tiles)]

    def halos(self, y_edges, x_edges, corners):
        if self.folded:
            y = lax.ppermute(y_edges[0], "yx", self.swap_route(2))
            x = lax.ppermute(x_edges[0], "yx", self.swap_route(1))
            corner = lax.ppermute(corners[0], "yx", self.swap_route(3))
            return [y], [x], [corner]
        y = [lax.ppermute(y_edges[k], "yx", self.route((1, -1)[1 - k], 0)) for k in (1, 0)]
        x = [lax.ppermute(x_edges[k], "yx", self.route(0, (1, -1)[1 - k])) for k in (1, 0)]
        corner = [
            lax.ppermute(corners[2 * k + j], "yx", self.route((1, -1)[1 - k], (1, -1)[1 - j]))
            for k in (1, 0)
            for j in (1, 0)
        ]
        return y, x, corner


def swap_depth(low, high):
    size = lax.axis_size("gz")
    up = [(i, i + 1) for i in range(size - 1)]
    return lax.ppermute(high, "gz", up), lax.ppermute(low, "gz", [(j, i) for i, j in up])


class Riders:
    STEPS = (("cand", 1), ("gz", 2), ("gz", 1))

    def __init__(self, rows):
        self.tiles = 27 * rows // 16
        self.fits = (
            lax.axis_size("yx") == 4
            and lax.axis_size("cand") % 2 == 0
            and lax.axis_size("gz") % 4 == 0
            and self.tiles >= 8
        )
        self.size = -(-self.tiles // 8) if self.fits else 0
        self.mine = sum(
            lax.axis_index(axis) // mask % 2 * 2**k for k, (axis, mask) in enumerate(self.STEPS)
        )


def rotate_shards(piece):
    tiles = lax.axis_size("yx")
    return [
        lax.ppermute(piece, "yx", [(i, (i + k) % tiles) for i in range(tiles)]) for k in range(1, tiles)
    ]


def swap(block, axis, mask):
    return lax.ppermute(block, axis, [(i, i ^ mask) for i in range(lax.axis_size(axis))])


def share(stats):
    return lax.all_to_all(stats, PART, 0, 0)


def call(kernel, outs, scratch, scalars, *arrays, flops=0, nbytes=0, in_hbm=0, out_hbm=False):
    smem, vmem, hbm = (
        pl.BlockSpec(memory_space=space) for space in (pltpu.SMEM, pltpu.VMEM, pltpu.HBM)
    )
    far, near = arrays[:in_hbm], arrays[in_hbm:]
    far = [pltpu.with_memory_space_constraint(array, pltpu.HBM) for array in far]
    return pl.pallas_call(
        kernel,
        out_shape=[jax.ShapeDtypeStruct(shape, dtype) for shape, dtype in outs],
        in_specs=[smem] + [hbm] * len(far) + [vmem] * len(near),
        out_specs=[hbm if out_hbm else vmem] * len(outs),
        scratch_shapes=[pltpu.VMEM(*entry) if isinstance(entry, tuple) else entry for entry in scratch],
        compiler_params=pltpu.CompilerParams(vmem_limit_bytes=VMEM_BYTES),
        cost_estimate=pl.CostEstimate(flops=flops, bytes_accessed=nbytes, transcendentals=0),
    )(scalars, *far, *near)


def start_kernel(ny, nx, size, pos, x_in, w_in, d_in, y_out, x_out, corners, x, w, lines, sems):
    edge = x_in.shape[0]
    f32, bf16 = jnp.float32, jnp.bfloat16
    chunks = 4
    planes = edge // chunks
    first = [
        pltpu.make_async_copy(
            x_in.at[pl.ds(k * planes, planes)],
            x.at[pl.ds(1 + k * planes, planes), pl.ds(1, edge)],
            sems.at[k],
        )
        for k in range(chunks)
    ]
    later = [pltpu.make_async_copy(w_in, w, sems.at[chunks])]
    if size:
        at = jnp.minimum(pos[pos.shape[0] - 1] * size, d_in.shape[0] - size)
        for k, (out, begin) in enumerate(((y_out, edge), (x_out, edge), (corners, 1))):
            later.append(
                pltpu.make_async_copy(
                    d_in.at[pl.ds(at, size)], out.at[0, pl.ds(begin, size)], sems.at[chunks + 1 + k]
                )
            )
    for copy in first + later:
        copy.start()
    x[0] = jnp.zeros(x.shape[1:], bf16)
    x[edge + 1] = jnp.zeros(x.shape[1:], bf16)
    blank = jnp.zeros((edge,) + x.shape[2:], bf16)
    x[1 : edge + 1, 0] = blank
    x[1 : edge + 1, edge + 1] = blank
    flat = lines.reshape(nx * edge * edge * 8, 128)
    part = planes * edge
    for k in range(chunks):
        first[k].wait()
        at, here = pl.ds(k * planes, planes), pl.ds(1 + k * planes, planes)
        for i in range(ny):
            row = jnp.where(pos[i] == 1, 1, edge) if ny == 1 else (1, edge)[i]
            y_out[i, at] = x[here, row]
        for j in range(nx):
            low = x[here, 1 : edge + 1, 0:8].astype(f32).reshape(part, 8, 128)
            high = x[here, 1 : edge + 1, edge - 8 : edge].astype(f32).reshape(part, 8, 128)
            high = pltpu.roll(high, 1, 1)
            kept = jnp.where(pos[ny] == 1, low, high) if nx == 1 else (low, high)[j]
            lines[j, k * part : k * part + part] = kept
            begin = (j * edge * edge + k * part) * 8
            column = flat[pl.ds(begin, part, stride=8), :]
            x_out[j, at] = column.astype(bf16).reshape(planes, edge, 128)
    for i in range(ny):
        for j in range(nx):
            begin = j * edge * edge * 8
            low = flat[pl.ds(begin, edge, stride=8 * edge), :]
            high = flat[pl.ds(begin + 8 * (edge - 1), edge, stride=8 * edge), :]
            kept = jnp.where(pos[i] == 1, low, high) if ny == 1 else (low, high)[i]
            corners[i * nx + j, 0] = kept.astype(bf16)
    for copy in later:
        copy.wait()


def face_kernel(ny, nx, size, _, x, y_halos, x_halos, corners, low, high, *riders):
    edge = low.shape[1]
    wide = edge + ny + nx
    for face, at in ((low, 0), (high, edge - 3)):
        for k in range(3):
            row = k * wide
            face[row : row + edge] = x[1 + at + k, 1 : edge + 1]
            for i in range(ny):
                face[row + edge + i] = y_halos[i, at + k]
            for j in range(nx):
                face[row + edge + ny + j] = x_halos[j, at + k]
        for k in range(ny * nx):
            face[3 * wide + k] = corners[k, 0]
    if size:
        riders[0][0] = x_halos[0, edge : edge + size]
        riders[0][1] = y_halos[0, edge : edge + size]
        riders[0][2] = corners[0, 1 : 1 + size]


def spread_taps(weight, taps):
    for tap in range(27):
        row, lane = tap // 3 * 128, tap % 3 * 128
        taps[row : row + 128, lane : lane + 128] = weight[tap]


def pair_taps(weight, pairs):
    for dz in range(3):
        for line in range(4):
            row = (dz * 4 + line) * 128
            for out in range(2):
                lane = out * 128
                if 0 <= line - out < 3:
                    block = weight[dz * 9 + (line - out) * 3 + 2]
                else:
                    block = jnp.zeros((128, 128), pairs.dtype)
                pairs[row : row + 128, lane : lane + 128] = block


def join_x(wide, edge):
    place = lax.broadcasted_iota(jnp.int32, wide.shape[:2] + (128,), 1)
    after = jnp.where(place > 0, pltpu.roll(wide[:, :, :128], 1, 1), 0.0)
    before = jnp.where(place < edge - 1, pltpu.roll(wide[:, :, 256:], edge - 1, 1), 0.0)
    return wide[:, :, 128:256] + after + before


def convolve(grid, count, taps, pairs, put):
    edge = grid.shape[2]
    planes = min(count, 4)
    rows = planes * edge * edge
    place = lax.broadcasted_iota(jnp.int32, (planes * edge, edge, 128), 1)
    halved = grid.reshape(grid.shape[0], edge // 2 + 1, 2, edge, 128)
    for z in range(0, count, planes):
        left = jnp.concatenate(
            [
                grid[z + dz : z + dz + planes, dy : dy + edge].reshape(rows, 128)
                for dz in range(3)
                for dy in range(3)
            ],
            axis=1,
        )
        wide = jnp.dot(left, taps[:, 0:256], preferred_element_type=jnp.float32)
        wide = wide.reshape(planes * edge, edge, 256)
        left = jnp.concatenate(
            [
                halved[z + dz : z + dz + planes, line // 2 : line // 2 + edge // 2, line % 2].reshape(
                    rows // 2, 128
                )
                for dz in range(3)
                for line in range(4)
            ],
            axis=1,
        )
        two = jnp.dot(left, pairs[...], preferred_element_type=jnp.float32)
        two = two.reshape(planes * edge // 2, edge, 256)
        two = jnp.stack([two[:, :, :128], two[:, :, 128:]], axis=1).reshape(planes * edge, edge, 128)
        after = jnp.where(place > 0, pltpu.roll(wide[:, :, :128], 1, 1), 0.0)
        before = jnp.where(place < edge - 1, pltpu.roll(two, edge - 1, 1), 0.0)
        new = wide[:, :, 128:256] + after + before
        put(z, new.reshape(planes, edge, edge, 128))


def conv_kernel(_, x, weight, act, taps, pairs, sums):
    edge = act.shape[0]
    spread_taps(weight, taps)
    pair_taps(weight, pairs)
    totals = []

    def put(z, new):
        act[z : z + new.shape[0]] = new
        totals.append(jnp.sum(new.reshape(-1, 8, 128), axis=0))

    convolve(x, edge, taps, pairs, put)
    sums[...] = functools.reduce(jnp.add, totals)


def rim_kernel(ny, nx, pos, *refs):
    x, own, sums, y_halos, x_halos, corners, front, back, taps, pairs, act, stats, grid, column, flanks = refs
    edge = own.shape[0]
    wide_face = edge + ny + nx
    depth = edge + 4
    f32, bf16 = jnp.float32, jnp.bfloat16
    total = sums[...]
    act[2 : 2 + edge] = own[...]

    blank = jnp.zeros(grid.shape[:1] + grid.shape[2:], grid.dtype)
    grid[:, 0] = blank
    grid[:, edge + 1] = blank
    for face, halo_at, own_at, plane, out_at, touched, dz in (
        (front, 0, 3, 0, 0, 2, 0),
        (back, 1, 0, edge - 1, depth - 2, depth - 3, 2),
    ):
        for k in range(3):
            grid[halo_at + k, 1 : edge + 1] = face[k * wide_face : k * wide_face + edge]
        grid[own_at, 1 : edge + 1] = x[1 + plane, 1 : edge + 1]

        def put(z, new):
            act[out_at + z : out_at + z + new.shape[0]] = new

        convolve(grid, 2, taps, pairs, put)
        beside = halo_at + (2 if dz == 0 else 0)
        left = jnp.concatenate(
            [grid[beside, dy : dy + edge].reshape(edge * edge, 128) for dy in range(3)], axis=1
        )
        wide = jnp.dot(left, taps[dz * 384 : dz * 384 + 384, :], preferred_element_type=f32)
        new = join_x(wide.reshape(edge, edge, 384), edge)
        total = total + jnp.sum(new.reshape(-1, 8, 128), axis=0)
        act[touched] += new

    def rim(face, row):
        return jnp.stack([face[k * wide_face + edge + row] for k in range(3)])

    for i in range(ny):
        low = pos[i] == 1
        line = jnp.concatenate([rim(front, i), y_halos[i, 0:edge], rim(back, i)], axis=0)
        left = jnp.concatenate(
            [line[dz : dz + depth].reshape(depth * edge, 128) for dz in range(3)], axis=1
        )
        start = jnp.where(low, 0, 256)
        right = jnp.concatenate(
            [taps[pl.ds(pl.multiple_of(start + dz * 384, 128), 128), :] for dz in range(3)], axis=0
        )
        wide = jnp.dot(left, right, preferred_element_type=f32)
        new = join_x(wide.reshape(depth, edge, 384), edge)
        total = total + jnp.sum(new[2 : 2 + edge].reshape(-1, 8, 128), axis=0)
        act[:, jnp.where(low, 0, edge - 1)] += new

    flat = act.reshape(depth * edge * edge, 128)
    for j in range(nx):
        column[:, 0:8] = jnp.zeros((depth + 2, 8, 128), f32)
        column[:, 8 + edge :] = jnp.zeros((depth + 2, 8, 128), f32)
        column[3 : edge + 3, 8 : 8 + edge] = x_halos[j, 0:edge].astype(f32)
        column[0:3, 8 : 8 + edge] = rim(front, ny + j).astype(f32)
        column[edge + 3 :, 8 : 8 + edge] = rim(back, ny + j).astype(f32)
        rows = edge + 16
        lines = column.reshape((depth + 2) * rows, 128)
        for i in range(ny):
            k = i * nx + j
            low = pos[i] == 1
            for at, count, ends in (
                (0, 3, front[3 * wide_face + k].astype(f32)[edge - 3 :]),
                (3, edge, corners[k, 0].astype(f32)),
                (edge + 3, 3, back[3 * wide_face + k].astype(f32)[:3]),
            ):
                first, last = ends, ends
                if ny == 1:
                    first, last = jnp.where(low, ends, 0.0), jnp.where(low, 0.0, ends)
                if ny == 1 or i == 0:
                    lines[pl.ds(at * rows + 7, count, stride=rows), :] = first
                if ny == 1 or i == 1:
                    lines[pl.ds(at * rows + 8 + edge, count, stride=rows), :] = last
        for dy in range(3):
            piece = column[:, 7 + dy : 7 + dy + edge].astype(bf16)
            flanks[:, :, dy * 128 : dy * 128 + 128] = piece
        left = jnp.concatenate(
            [flanks[dz : dz + depth].reshape(depth * edge, 384) for dz in range(3)], axis=1
        )
        right = jnp.concatenate([taps[:, 0:128], taps[:, 256:384]], axis=1)
        extra = jnp.dot(left, right, preferred_element_type=f32)
        low = pos[ny + j] == 1
        first, last = extra[:, :128], extra[:, 128:]
        if nx == 1:
            first, last = jnp.where(low, first, 0.0), jnp.where(low, 0.0, last)
        line = lax.broadcasted_iota(jnp.int32, (8, 128), 0)
        inner = slice(2 * edge, 2 * edge + edge * edge)
        if nx == 1 or j == 0:
            flat[pl.ds(0, depth * edge, stride=edge), :] += first
            total = total + jnp.where(line == 0, jnp.sum(first[inner], axis=0, keepdims=True), 0.0)
        if nx == 1 or j == 1:
            flat[pl.ds(edge - 1, depth * edge, stride=edge), :] += last
            total = total + jnp.where(line == 7, jnp.sum(last[inner], axis=0, keepdims=True), 0.0)

    rows = edge**3 // 8
    mean = total / rows

    def spread_step(k, carry):
        off = act[k].reshape(edge * 2, 8, 128) - mean
        return carry + jnp.sum(off * off, axis=0)

    spread = lax.fori_loop(2, edge + 2, spread_step, jnp.zeros((8, 128), f32), unroll=4)
    put_stats(stats, mean, spread, rows)


def merge(mean, spread, rows, other_mean, other_spread):
    off = mean - other_mean
    return 0.5 * (mean + other_mean), spread + other_spread + (0.5 * rows) * (off * off)


def put_stats(stats, mean, spread, rows):
    for step in (1, 2, 4):
        others = pltpu.roll(mean, step, 0), pltpu.roll(spread, step, 0)
        mean, spread = merge(mean, spread, float(rows * step), *others)
    both = jnp.concatenate([mean[0:1], spread[0:1]], axis=0)
    stats[...] = jnp.broadcast_to(both[None], stats.shape)


def read_stats(stats, rows):
    devices, _, channels = stats.shape
    shape = (8, channels)
    means = [jnp.broadcast_to(stats[k, 0:1, :], shape) for k in range(devices)]
    spreads = [jnp.broadcast_to(stats[k, 1:2, :], shape) for k in range(devices)]
    mean = functools.reduce(jnp.add, means) / devices
    spread = functools.reduce(jnp.add, spreads)
    spread = spread + rows * functools.reduce(jnp.add, [(m - mean) * (m - mean) for m in means])
    rows = rows * devices
    lane = lax.broadcasted_iota(jnp.int32, shape, 1)
    step = 1
    while step < channels // GROUPS:
        low = jnp.bitwise_and(lane, step) == 0
        others = [
            jnp.where(low, pltpu.roll(row, channels - step, 1), pltpu.roll(row, step, 1))
            for row in (mean, spread)
        ]
        mean, spread = merge(mean, spread, rows, *others)
        rows, step = 2.0 * rows, 2 * step
    return mean, lax.rsqrt(spread / rows + EPSILON)


def silu_of_double(h):
    return h + h * jnp.tanh(h)


def norm_kernel(ny, nx, pos, act, stats, gain, offset, out, pooled, *refs):
    y_edges, x_edges, corners, half = refs
    depth, edge = act.shape[0], act.shape[1]
    deep, deep_depth = edge // 2, depth // 2
    f32, bf16 = jnp.float32, jnp.bfloat16
    mean, scale = read_stats(stats, float(edge**3))
    scale = scale * (0.5 * gain[...])
    shift = 0.5 * offset[...]
    for k in range(deep_depth):
        value = act[2 * k : 2 * k + 2].reshape(edge * edge // 4, 8, 128)
        value = silu_of_double((value - mean) * scale + shift)
        value = value.reshape(2, edge, edge, 128).astype(bf16)
        if 0 < k < deep_depth - 1:
            out[2 * k - 2 : 2 * k] = value
        value = value.astype(f32)
        value = (value[0] + value[1]).reshape(deep, 2, edge, 128)
        half[k] = (value[:, 0] + value[:, 1]).reshape(deep * edge, 128)
        lines = half.at[k]
        pair = lines[pl.ds(0, deep * deep, stride=2), :] + lines[pl.ds(1, deep * deep, stride=2), :]
        pair = (pair * 0.125).astype(bf16).astype(f32).reshape(deep, deep, 128)
        if k == 0 or k == deep_depth - 1:
            inside = pos[ny + nx + (0 if k == 0 else 1)] == 1
            pair = jnp.where(inside, pair, 0.0)
        pooled[k] = pair
    lines = pooled.reshape(deep_depth * deep * deep, 128)
    rows = deep_depth * deep
    first_x = lines[pl.ds(0, rows, stride=deep), :]
    last_x = lines[pl.ds(deep - 1, rows, stride=deep), :]
    first_y, last_y = (pooled[:, y].reshape(rows, 128) for y in (0, deep - 1))
    ends = []
    for y in (0, deep - 1):
        for x in (0, deep - 1):
            ends.append(lines[pl.ds(y * deep + x, deep_depth, stride=deep * deep), :])
    if ny == 1:
        above, left = pos[0] == 1, pos[1] == 1
        y_edges[0] = jnp.where(above, first_y, last_y).astype(bf16)
        x_edges[0] = jnp.where(left, first_x, last_x).astype(bf16)
        corners[0, 0:deep_depth] = jnp.where(
            above, jnp.where(left, ends[0], ends[1]), jnp.where(left, ends[2], ends[3])
        )
    else:
        y_edges[0], y_edges[1] = first_y.astype(bf16), last_y.astype(bf16)
        x_edges[0], x_edges[1] = first_x.astype(bf16), last_x.astype(bf16)
        for k in range(4):
            corners[k, 0:deep_depth] = ends[k]


def stack_kernel(*refs):
    out = refs[-1]
    for k in range(out.shape[0]):
        out[k] = refs[k][...]


def stack(*arrays):
    vmem = pl.BlockSpec(memory_space=pltpu.VMEM)
    return pl.pallas_call(
        stack_kernel,
        out_shape=jax.ShapeDtypeStruct((len(arrays),) + arrays[0].shape, arrays[0].dtype),
        in_specs=[vmem] * len(arrays),
        out_specs=vmem,
        compiler_params=pltpu.CompilerParams(vmem_limit_bytes=VMEM_BYTES),
    )(*arrays)


def place_kernel(pos, own, *refs):
    *held, out, sem = refs
    tile, mine = pos[pos.shape[0] - 2], pos[pos.shape[0] - 1]
    copy = pltpu.make_async_copy(own, out.at[tile], sem)
    copy.start()
    if len(held) == 1:
        pieces, others, size = held[0].shape[:3]
        for piece in range(pieces):
            at = jnp.minimum(jnp.bitwise_xor(mine, piece) * size, own.shape[0] - size)
            for k in range(others):
                out[jnp.bitwise_xor(tile, k + 1), pl.ds(at, size)] = held[0][piece, k]
    else:
        for k, shard in enumerate(held):
            out[lax.rem(tile + len(held) - k, len(held) + 1)] = shard[...]
    copy.wait()


def deep_kernel(ny, nx, pos, pooled, y_halos, x_halos, corners, kernel, *refs):
    act, stats, grid, packed = refs
    depth, deep = pooled.shape[0], pooled.shape[1]
    f32 = jnp.float32
    grid[...] = jnp.zeros(grid.shape, f32)
    grid[:, 1 : deep + 1, 8:16] = pooled[...]
    for i in range(ny):
        at = jnp.where(pos[i] == 1, 0, deep + 1)
        grid[:, at, 8:16] = y_halos[i].astype(f32).reshape(depth, deep, 128)
    pitch = (deep + 2) * 24
    flat = grid.reshape(depth * pitch, 128)
    for j in range(nx):
        left = pos[ny + j] == 1
        column = x_halos[j].astype(f32).reshape(depth, deep, 128)
        for side, here in ((7, left), (16, jnp.logical_not(left))):
            if nx == 2 and side != (7, 16)[j]:
                continue
            for z in range(depth):
                kept = column[z] if nx == 2 else jnp.where(here, column[z], 0.0)
                flat[pl.ds(z * pitch + 24 + side, deep, stride=24), :] = kept
            for i in range(ny):
                end = corners[i * nx + j, 0:depth]
                above = pos[i] == 1
                for y, there in ((0, above), (deep + 1, jnp.logical_not(above))):
                    if ny == 2 and y != (0, deep + 1)[i]:
                        continue
                    kept = end
                    if nx == 1:
                        kept = jnp.where(jnp.logical_and(here, there), end, 0.0)
                    flat[pl.ds(y * 24 + side, depth, stride=pitch), :] = kept

    for dx in range(3):
        plane = grid[:, :, 7 + dx : 15 + dx]
        for y in range(deep + 1):
            both = jnp.concatenate([plane[:, y], plane[:, y + 1]], axis=1)
            packed[:, y // 2, y % 2, :, dx * 128 : dx * 128 + 128] = both.astype(jnp.bfloat16)

    rows = deep**3
    total = None
    for dz in range(3):
        left = jnp.concatenate(
            [
                packed[dz : dz + deep, dy // 2 : dy // 2 + deep // 2, dy % 2].reshape(rows, 384)
                for dy in range(3)
            ],
            axis=1,
        )
        right = jnp.concatenate(
            [kernel[:, dz * 9 + tap].reshape(-1, 128) for tap in range(9)], axis=1
        )
        term = lax.dot_general(
            left, right, (((1,), (1,)), ((), ())), preferred_element_type=f32
        )
        total = term if total is None else total + term
    act[...] = total
    total = total.reshape(rows // 8, 8, -1)
    rows = rows // 8
    mean = jnp.sum(total, axis=0) / rows
    off = total - mean
    put_stats(stats, mean, jnp.sum(off * off, axis=0), rows)


def final_kernel(_, act, stats, gain, offset, up, mid, out, wide, held, sems):
    edge = mid.shape[0]
    deep = edge // 2
    f32 = jnp.float32
    mean, scale = read_stats(stats, float(deep**3))
    scale = scale * (0.5 * gain[...])
    shift = 0.5 * offset[...]
    planes = 2
    size = planes * deep * deep
    copies = []
    for k in range(0, deep, planes):
        value = act[k * deep * deep : k * deep * deep + size].reshape(size // 8, 8, -1)
        value = silu_of_double((value - mean) * scale + shift)
        value = value.reshape(size, -1).astype(jnp.bfloat16)
        lifted = jnp.dot(value, up[...], preferred_element_type=f32)
        lines = wide.at[k // planes]
        lines[pl.ds(0, size, stride=2), :] = lifted
        lines[pl.ds(1, size, stride=2), :] = lifted
        add = lines[...].reshape(planes, 1, deep, 1, edge, 128)
        at = pl.ds(2 * k, 2 * planes)
        old = mid[at].astype(f32).reshape(planes, 2, deep, 2, edge, 128)
        held[at] = (old + add).astype(jnp.bfloat16).reshape(2 * planes, edge, edge, 128)
        copy = pltpu.make_async_copy(held.at[at], out.at[at], sems.at[k // planes])
        copy.start()
        copies.append(copy)
    for copy in copies:
        copy.wait()


def body(
    features, conv_weight, gain_mid, offset_mid, deep_weight, gain_deep, offset_deep, up_weight
):
    f32, bf16 = jnp.float32, jnp.bfloat16
    edge, channels = features.shape[0], features.shape[3]
    deep = edge // 2
    deep_channels = gain_deep.shape[0]
    square = Square()
    tiles = square.tiles
    devices = lax.axis_size("gz") * tiles
    y_low, x_low = square.low_sides()
    ny, nx = len(y_low), len(x_low)
    riders = Riders(deep_weight.shape[4])
    depth_at = lax.axis_index("gz")
    inside = [depth_at > 0, depth_at < lax.axis_size("gz") - 1]
    pos = y_low + x_low + inside + [lax.axis_index("yx"), riders.mine]
    pos = jnp.stack([jnp.asarray(v, jnp.int32) for v in pos])

    own = jnp.moveaxis(deep_weight, 4, 3).reshape(-1, 16, channels)
    conv_weight = conv_weight.reshape(27, channels, channels)
    *edges, field, conv_weight = call(
        functools.partial(start_kernel, ny, nx, riders.size),
        [
            ((ny, edge + riders.size, edge, channels), bf16),
            ((nx, edge + riders.size, edge, channels), bf16),
            ((ny * nx, 1 + riders.size, edge, channels), bf16),
            ((edge + 2, edge + 2, edge, channels), bf16),
            (conv_weight.shape, bf16),
        ],
        [((nx, edge * edge, 8, channels), f32), pltpu.SemaphoreType.DMA((8,))],
        pos,
        features,
        conv_weight,
        own,
        nbytes=5 << 20,
        in_hbm=3,
    )
    halos = square.halos(*(list(piece) for piece in edges))
    conv_flops = 54 * channels * channels * edge**3
    act, taps, pairs, sums = call(
        conv_kernel,
        [
            ((edge, edge, edge, channels), f32),
            ((9 * channels, 3 * channels), bf16),
            ((12 * channels, 2 * channels), bf16),
            ((8, channels), f32),
        ],
        [],
        pos,
        field,
        conv_weight,
        flops=conv_flops,
        nbytes=6 << 20,
    )
    (y, x, corner), act = lax.optimization_barrier((halos, act))
    y, x, corner = jnp.stack(y), jnp.stack(x), jnp.stack(corner)
    face = ((3 * (edge + ny + nx) + ny * nx, edge, channels), bf16)
    held = [((3, riders.size, 16, channels), bf16)] if riders.size else []
    low, high, *held = call(
        functools.partial(face_kernel, ny, nx, riders.size),
        [face, face] + held,
        [],
        pos,
        field,
        y,
        x,
        corner,
    )
    front, back = swap_depth(low, high)
    if riders.size:
        held = held[0][None]
        other = swap(held, *riders.STEPS[0])
    else:
        held = rotate_shards(own)
    act, stats = call(
        functools.partial(rim_kernel, ny, nx),
        [((edge + 4, edge, edge, channels), f32), ((devices, 2, channels), f32)],
        [
            ((4, edge + 2, edge, channels), bf16),
            ((edge + 6, edge + 16, channels), f32),
            ((edge + 6, edge, 3 * channels), bf16),
        ],
        pos,
        field,
        act,
        sums,
        y,
        x,
        corner,
        front,
        back,
        taps,
        pairs,
        flops=conv_flops // 2,
        nbytes=6 << 20,
    )
    if riders.size:
        stats, other = lax.optimization_barrier((stats, other))
        held = stack(held, other).reshape((-1,) + held.shape[1:])
        other = swap(held, *riders.STEPS[1])
        stats = share(stats)
        stats, other = lax.optimization_barrier((stats, other))
        held = stack(held, other).reshape((-1,) + held.shape[1:])
        other = swap(held, *riders.STEPS[2])
        held = [stack(held, other).reshape((-1,) + held.shape[1:])]
    else:
        stats = share(stats)
    out, pooled, *edges = call(
        functools.partial(norm_kernel, ny, nx),
        [
            ((edge, edge, edge, channels), bf16),
            ((deep + 2, deep, deep, channels), f32),
            ((ny, (deep + 2) * deep, channels), bf16),
            ((nx, (deep + 2) * deep, channels), bf16),
            ((ny * nx, 16, channels), f32),
        ],
        [((deep + 2, deep * edge, channels), f32)],
        pos,
        act,
        stats,
        gain_mid.reshape(1, channels),
        offset_mid.reshape(1, channels),
        flops=20 * channels * edge**3,
        nbytes=3 << 20,
    )
    y, x, corner = square.halos(*(list(piece) for piece in edges))
    (kernel,) = call(
        place_kernel,
        [((tiles,) + own.shape, bf16)],
        [pltpu.SemaphoreType.DMA],
        pos,
        own,
        *held,
        nbytes=4 << 20,
        in_hbm=1,
    )
    kernel = kernel.reshape(tiles, 27, deep_weight.shape[4], channels)
    deep_act, stats = call(
        functools.partial(deep_kernel, ny, nx),
        [((deep**3, deep_channels), f32), ((devices, 2, deep_channels), f32)],
        [
            ((deep + 2, deep + 2, 24, channels), f32),
            ((deep + 2, deep // 2 + 1, 2, 16, 3 * channels), bf16),
        ],
        pos,
        pooled,
        jnp.stack(y),
        jnp.stack(x),
        jnp.stack(corner),
        kernel,
        flops=2 * 27 * channels * deep_channels * deep**3,
        nbytes=4 << 20,
    )
    stats = share(stats)
    (decoded,) = call(
        final_kernel,
        [((edge, edge, edge, channels), bf16)],
        [
            ((deep // 2, 4 * deep * deep, channels), f32),
            ((edge, edge, edge, channels), bf16),
            pltpu.SemaphoreType.DMA((deep // 2,)),
        ],
        pos,
        deep_act,
        stats,
        gain_deep.reshape(1, deep_channels),
        offset_deep.reshape(1, deep_channels),
        up_weight,
        out,
        flops=4 * deep_channels * channels * deep**3,
        nbytes=3 << 20,
        out_hbm=True,
    )
    return decoded


def solution(mesh):
    placed = (
        P(("cand", "gz"), "yx", None, None),
        P(),
        P(),
        P(),
        P(None, None, None, None, "yx"),
        P(),
        P(),
        P(),
    )
    return jax.shard_map(
        body,
        mesh=mesh,
        in_specs=placed,
        out_specs=P(("cand", "gz"), "yx", None, None),
        check_vma=False,
    )
```

```python
import functools
import math

import jax
import jax.numpy as jnp
from jax import lax
from jax.experimental import pallas as pl
from jax.experimental.pallas import tpu as pltpu
from jax.sharding import PartitionSpec as P

GROUPS = 32
EPSILON = 1e-05
PART = ("gz", "yx")
VMEM_BYTES = 32 * 1024 * 1024


class Square:
    def __init__(self):
        self.tiles = lax.axis_size("yx")
        self.side = math.isqrt(self.tiles)
        tile = lax.axis_index("yx")
        self.row, self.column = tile // self.side, tile % self.side
        self.folded = self.side == 2
        self.steps = (0,) if self.folded else (-1, 1)

    def low_sides(self):
        if self.folded:
            return [self.row], [self.column]
        return [1, 0], [1, 0]

    def route(self, down, right):
        pairs = []
        for tile in range(self.tiles):
            row, column = tile // self.side + down, tile % self.side + right
            if 0 <= row < self.side and 0 <= column < self.side:
                pairs.append((tile, row * self.side + column))
        return pairs

    def swap_route(self, mask):
        return [(tile, tile ^ mask) for tile in range(self.tiles)]

    def halos(self, y_edges, x_edges, corners):
        if self.folded:
            y = lax.ppermute(y_edges[0], "yx", self.swap_route(2))
            x = lax.ppermute(x_edges[0], "yx", self.swap_route(1))
            corner = lax.ppermute(corners[0], "yx", self.swap_route(3))
            return [y], [x], [corner]
        y = [lax.ppermute(y_edges[k], "yx", self.route((1, -1)[1 - k], 0)) for k in (1, 0)]
        x = [lax.ppermute(x_edges[k], "yx", self.route(0, (1, -1)[1 - k])) for k in (1, 0)]
        corner = [
            lax.ppermute(corners[2 * k + j], "yx", self.route((1, -1)[1 - k], (1, -1)[1 - j]))
            for k in (1, 0)
            for j in (1, 0)
        ]
        return y, x, corner


def swap_depth(outer, inner):
    size = lax.axis_size("gz")
    routes = [[], []]
    for low in range(size - 1):
        routes[low % 2] += [(low, low + 1), (low + 1, low)]
    return lax.ppermute(outer, "gz", routes[1]), lax.ppermute(inner, "gz", routes[0])


class Riders:
    STEPS = (("cand", 1), ("gz", 2), ("gz", 1))

    def __init__(self, rows):
        self.tiles = 27 * rows // 16
        self.fits = (
            lax.axis_size("yx") == 4
            and lax.axis_size("cand") % 2 == 0
            and lax.axis_size("gz") % 4 == 0
            and self.tiles >= 8
        )
        self.size = -(-self.tiles // 8) if self.fits else 0
        self.mine = sum(
            lax.axis_index(axis) // mask % 2 * 2**k for k, (axis, mask) in enumerate(self.STEPS)
        )


def rotate_shards(piece):
    tiles = lax.axis_size("yx")
    return [
        lax.ppermute(piece, "yx", [(i, (i + k) % tiles) for i in range(tiles)]) for k in range(1, tiles)
    ]


def swap(block, axis, mask):
    return lax.ppermute(block, axis, [(i, i ^ mask) for i in range(lax.axis_size(axis))])


def share(stats):
    return lax.all_to_all(stats, PART, 0, 0)


def call(kernel, outs, scratch, scalars, *arrays, flops=0, nbytes=0, in_hbm=0, out_hbm=False):
    smem, vmem, hbm = (
        pl.BlockSpec(memory_space=space) for space in (pltpu.SMEM, pltpu.VMEM, pltpu.HBM)
    )
    far, near = arrays[:in_hbm], arrays[in_hbm:]
    far = [pltpu.with_memory_space_constraint(array, pltpu.HBM) for array in far]
    return pl.pallas_call(
        kernel,
        out_shape=[jax.ShapeDtypeStruct(shape, dtype) for shape, dtype in outs],
        in_specs=[smem] + [hbm] * len(far) + [vmem] * len(near),
        out_specs=[hbm if out_hbm else vmem] * len(outs),
        scratch_shapes=[pltpu.VMEM(*entry) if isinstance(entry, tuple) else entry for entry in scratch],
        compiler_params=pltpu.CompilerParams(vmem_limit_bytes=VMEM_BYTES),
        cost_estimate=pl.CostEstimate(flops=flops, bytes_accessed=nbytes, transcendentals=0),
    )(scalars, *far, *near)


def start_kernel(ny, nx, size, pos, x_in, w_in, d_in, y_out, x_out, corners, x, w, lines, sems):
    edge = x_in.shape[0]
    f32, bf16 = jnp.float32, jnp.bfloat16
    chunks = 8
    planes = edge // chunks
    first = [
        pltpu.make_async_copy(
            x_in.at[pl.ds(k * planes, planes)],
            x.at[pl.ds(1 + k * planes, planes), pl.ds(1, edge)],
            sems.at[k],
        )
        for k in range(chunks)
    ]
    later = []
    if size:
        at = jnp.minimum(pos[pos.shape[0] - 1] * size, d_in.shape[0] - size)
        for k, (out, begin) in enumerate(((y_out, edge), (x_out, edge), (corners, 1))):
            later.append(
                pltpu.make_async_copy(
                    d_in.at[pl.ds(at, size)], out.at[0, pl.ds(begin, size)], sems.at[chunks + k]
                )
            )
    for k in range(9):
        three = pl.ds(3 * k, 3)
        later.append(
            pltpu.make_async_copy(w_in.at[three], w.at[three], sems.at[chunks + 3 + k])
        )
    for copy in first + later:
        copy.start()
    x[0] = jnp.zeros(x.shape[1:], bf16)
    x[edge + 1] = jnp.zeros(x.shape[1:], bf16)
    blank = jnp.zeros((edge,) + x.shape[2:], bf16)
    x[1 : edge + 1, 0] = blank
    x[1 : edge + 1, edge + 1] = blank
    flat = lines.reshape(nx * edge * edge * 8, 128)
    part = planes * edge
    for k in range(chunks):
        first[k].wait()
        at, here = pl.ds(k * planes, planes), pl.ds(1 + k * planes, planes)
        for i in range(ny):
            row = jnp.where(pos[i] == 1, 1, edge) if ny == 1 else (1, edge)[i]
            y_out[i, at] = x[here, row]
        for j in range(nx):
            low = x[here, 1 : edge + 1, 0:8].astype(f32).reshape(part, 8, 128)
            high = x[here, 1 : edge + 1, edge - 8 : edge].astype(f32).reshape(part, 8, 128)
            high = pltpu.roll(high, 1, 1)
            kept = jnp.where(pos[ny] == 1, low, high) if nx == 1 else (low, high)[j]
            lines[j, k * part : k * part + part] = kept
            begin = (j * edge * edge + k * part) * 8
            column = flat[pl.ds(begin, part, stride=8), :]
            x_out[j, at] = column.astype(bf16).reshape(planes, edge, 128)
    for i in range(ny):
        for j in range(nx):
            begin = j * edge * edge * 8
            low = flat[pl.ds(begin, edge, stride=8 * edge), :]
            high = flat[pl.ds(begin + 8 * (edge - 1), edge, stride=8 * edge), :]
            kept = jnp.where(pos[i] == 1, low, high) if ny == 1 else (low, high)[i]
            corners[i * nx + j, 0] = kept.astype(bf16)
    for copy in later:
        copy.wait()


def face_kernel(ny, nx, size, pos, x, y_halos, x_halos, corners, outer, inner, *riders):
    edge = outer.shape[1]
    wide = edge + ny + nx
    odd = pos[ny + nx + 2]
    far = edge - 3
    for face, at in ((outer, odd * far), (inner, (1 - odd) * far)):
        for k in range(3):
            row = k * wide
            face[row : row + edge] = x[1 + at + k, 1 : edge + 1]
            for i in range(ny):
                face[row + edge + i] = y_halos[i, at + k]
            for j in range(nx):
                face[row + edge + ny + j] = x_halos[j, at + k]
        for k in range(ny * nx):
            face[3 * wide + k] = corners[k, 0]
    if size:
        riders[0][0] = x_halos[0, edge : edge + size]
        riders[0][1] = y_halos[0, edge : edge + size]
        riders[0][2] = corners[0, 1 : 1 + size]


def spread_taps(weight, taps):
    for tap in range(27):
        row, lane = tap // 3 * 128, tap % 3 * 128
        taps[row : row + 128, lane : lane + 128] = weight[tap]


def pair_taps(weight, pairs):
    for dz in range(3):
        for line in range(4):
            row = (dz * 4 + line) * 128
            for out in range(2):
                lane = out * 128
                if 0 <= line - out < 3:
                    block = weight[dz * 9 + (line - out) * 3 + 2]
                else:
                    block = jnp.zeros((128, 128), pairs.dtype)
                pairs[row : row + 128, lane : lane + 128] = block


def join_x(wide, edge):
    place = lax.broadcasted_iota(jnp.int32, wide.shape[:2] + (128,), 1)
    after = jnp.where(place > 0, pltpu.roll(wide[:, :, :128], 1, 1), 0.0)
    before = jnp.where(place < edge - 1, pltpu.roll(wide[:, :, 256:], edge - 1, 1), 0.0)
    return wide[:, :, 128:256] + after + before


def convolve(grid, count, taps, pairs, put):
    edge = grid.shape[2]
    planes = min(count, 4)
    rows = planes * edge * edge
    place = lax.broadcasted_iota(jnp.int32, (planes * edge, edge, 128), 1)
    halved = grid.reshape(grid.shape[0], edge // 2 + 1, 2, edge, 128)
    for z in range(0, count, planes):
        left = jnp.concatenate(
            [
                grid[z + dz : z + dz + planes, dy : dy + edge].reshape(rows, 128)
                for dz in range(3)
                for dy in range(3)
            ],
            axis=1,
        )
        wide = jnp.dot(left, taps[:, 0:256], preferred_element_type=jnp.float32)
        wide = wide.reshape(planes * edge, edge, 256)
        left = jnp.concatenate(
            [
                halved[z + dz : z + dz + planes, line // 2 : line // 2 + edge // 2, line % 2].reshape(
                    rows // 2, 128
                )
                for dz in range(3)
                for line in range(4)
            ],
            axis=1,
        )
        two = jnp.dot(left, pairs[...], preferred_element_type=jnp.float32)
        two = two.reshape(planes * edge // 2, edge, 256)
        two = jnp.stack([two[:, :, :128], two[:, :, 128:]], axis=1).reshape(planes * edge, edge, 128)
        after = jnp.where(place > 0, pltpu.roll(wide[:, :, :128], 1, 1), 0.0)
        before = jnp.where(place < edge - 1, pltpu.roll(two, edge - 1, 1), 0.0)
        new = wide[:, :, 128:256] + after + before
        put(z, new.reshape(planes, edge, edge, 128))


def conv_kernel(_, x, weight, act, taps, pairs):
    edge = act.shape[0]
    spread_taps(weight, taps)
    pair_taps(weight, pairs)

    def put(z, new):
        act[z : z + new.shape[0]] = new

    convolve(x, edge, taps, pairs, put)


def y_terms(line, low, taps):
    planes, edge = line.shape[0] - 2, line.shape[1]
    left = jnp.concatenate(
        [line[dz : dz + planes].reshape(planes * edge, 128) for dz in range(3)], axis=1
    )
    start = jnp.where(low, 0, 256)
    right = jnp.concatenate(
        [taps[pl.ds(pl.multiple_of(start + dz * 384, 128), 128), :] for dz in range(3)], axis=0
    )
    wide = jnp.dot(left, right, preferred_element_type=jnp.float32)
    return join_x(wide.reshape(planes, edge, 384), edge)


def x_terms(column, taps):
    planes, edge = column.shape[0] - 2, column.shape[1] - 16
    lines = [column[:, 7 + dy : 7 + dy + edge].astype(jnp.bfloat16) for dy in range(3)]
    left = jnp.concatenate(
        [line[dz : dz + planes].reshape(planes * edge, 128) for dz in range(3) for line in lines],
        axis=1,
    )
    right = jnp.concatenate([taps[:, 0:128], taps[:, 256:384]], axis=1)
    both = jnp.dot(left, right, preferred_element_type=jnp.float32)
    return both[:, :128], both[:, 128:]


def fill_column(column, at, voxels, ends, above):
    count, edge = voxels.shape[:2]
    rows = edge + 16
    lines = column.reshape(column.shape[0] * rows, 128)
    column[at : at + count, 8 : 8 + edge] = voxels.astype(jnp.float32)
    for i, end in enumerate(ends):
        first = last = end.astype(jnp.float32)
        if len(ends) == 1:
            first, last = jnp.where(above[0], first, 0.0), jnp.where(above[0], 0.0, last)
        if len(ends) == 1 or i == 0:
            lines[pl.ds(at * rows + 7, count, stride=rows), :] = first
        if len(ends) == 1 or i == 1:
            lines[pl.ds(at * rows + 8 + edge, count, stride=rows), :] = last


def add_column(act, terms, j, nx, low):
    planes, edge = act.shape[:2]
    flat = act.reshape(planes * edge * edge, 128)
    first, last = terms
    if nx == 1:
        first, last = jnp.where(low, first, 0.0), jnp.where(low, 0.0, last)
    if nx == 1 or j == 0:
        flat[pl.ds(0, planes * edge, stride=edge), :] += first
    if nx == 1 or j == 1:
        flat[pl.ds(edge - 1, planes * edge, stride=edge), :] += last


def moments(planes):
    count, edge = planes.shape[:2]
    zero = jnp.zeros((8, 128), jnp.float32)

    def sum_step(k, carry):
        return carry + jnp.sum(planes[k].reshape(edge * 2, 8, 128), axis=0)

    mean = lax.fori_loop(0, count, sum_step, zero, unroll=True) / (count * edge * edge // 8)

    def spread_step(k, carry):
        off = planes[k].reshape(edge * 2, 8, 128) - mean
        return carry + jnp.sum(off * off, axis=0)

    return mean, lax.fori_loop(0, count, spread_step, zero, unroll=True)


def side_kernel(ny, nx, pos, own, y_halos, x_halos, corners, taps, inner, ends, stats, act, column):
    edge = own.shape[0]
    act[0] = jnp.zeros(act.shape[1:], jnp.float32)
    act[edge + 1] = jnp.zeros(act.shape[1:], jnp.float32)
    act[1 : edge + 1] = own[...]
    above = [pos[i] == 1 for i in range(ny)]
    blank = jnp.zeros((2, edge, 128), jnp.bfloat16)
    for i in range(ny):
        line = jnp.concatenate([blank, y_halos[i, 0:edge], blank], axis=0)
        act[:, jnp.where(above[i], 0, edge - 1)] += y_terms(line, above[i], taps)
    for j in range(nx):
        column[...] = jnp.zeros(column.shape, jnp.float32)
        fill_column(
            column, 2, x_halos[j, 0:edge], [corners[i * nx + j, 0] for i in range(ny)], above
        )
        add_column(act, x_terms(column, taps), j, nx, pos[ny + j] == 1)
    inner[...] = act[2:edge]
    ends[0:2] = act[0:2]
    ends[2:4] = act[edge : edge + 2]
    mean, spread = moments(act.at[2:edge])
    stats[0:8] = mean
    stats[8:16] = spread


def end_kernel(ny, nx, pos, *refs):
    x, inner_stats, partial, outer_face, inner_face, taps, pairs, act, stats, faces, grid, column = refs
    edge = x.shape[2]
    wide_face = edge + ny + nx
    f32 = jnp.float32
    odd = pos[ny + nx + 2] == 1
    faces[0] = jnp.where(odd, inner_face[...], outer_face[...])
    faces[1] = jnp.where(odd, outer_face[...], inner_face[...])
    above = [pos[i] == 1 for i in range(ny)]
    blank = jnp.zeros(grid.shape[:1] + grid.shape[2:], grid.dtype)
    grid[:, 0] = blank
    grid[:, edge + 1] = blank
    gap = jnp.zeros((2, edge, 128), grid.dtype)
    for side, halo_at, own_at, plane, at, beyond, own, beside, dz in (
        (0, 0, 3, 1, 0, 0, 2, 2, 0),
        (1, 1, 0, edge, 3, 4, 3, 1, 2),
    ):
        for k in range(3):
            begin = k * wide_face
            grid[halo_at + k, 1 : edge + 1] = faces[side, begin : begin + edge]
        grid[own_at, 1 : edge + 1] = x[plane, 1 : edge + 1]

        def put(z, new):
            act[beyond + z : beyond + z + new.shape[0]] = new

        convolve(grid, 2, taps, pairs, put)
        left = jnp.concatenate(
            [grid[beside, dy : dy + edge].reshape(edge * edge, 128) for dy in range(3)], axis=1
        )
        wide = jnp.dot(left, taps[dz * 384 : dz * 384 + 384, :], preferred_element_type=f32)
        own_part = partial[1 if side == 0 else 2]
        act[own] = own_part + join_x(wide.reshape(edge, edge, 384), edge)
        near = 1 if side == 0 else 4
        act[near] += partial[0 if side == 0 else 3]

        def rim(row):
            planes = [faces[side, k * wide_face + edge + row] for k in range(3)]
            return jnp.stack(planes)

        three = act.at[at : at + 3]
        for i in range(ny):
            line = [rim(i), gap] if side == 0 else [gap, rim(i)]
            three[:, jnp.where(above[i], 0, edge - 1)] += y_terms(
                jnp.concatenate(line, axis=0), above[i], taps
            )
        for j in range(nx):
            column[...] = jnp.zeros(column.shape, f32)
            ends = []
            for i in range(ny):
                tile = faces[side, 3 * wide_face + i * nx + j].astype(f32)
                ends.append(tile[edge - 3 :] if side == 0 else tile[:3])
            fill_column(column, 0 if side == 0 else 2, rim(ny + j), ends, above)
            add_column(three, x_terms(column, taps), j, nx, pos[ny + j] == 1)

    mean, spread = moments(act.at[2:4])
    few, many = edge * edge // 4, (edge - 2) * edge * edge // 8
    inner_mean, inner_spread = inner_stats[0:8], inner_stats[8:16]
    off = inner_mean - mean
    share_of = few / (few + many)
    spread = spread + inner_spread + (many * share_of) * (off * off)
    put_stats(stats, inner_mean - share_of * off, spread, few + many)


def merge(mean, spread, rows, other_mean, other_spread):
    off = mean - other_mean
    return 0.5 * (mean + other_mean), spread + other_spread + (0.5 * rows) * (off * off)


def put_stats(stats, mean, spread, rows):
    for step in (1, 2, 4):
        others = pltpu.roll(mean, step, 0), pltpu.roll(spread, step, 0)
        mean, spread = merge(mean, spread, float(rows * step), *others)
    both = jnp.concatenate([mean[0:1], spread[0:1]], axis=0)
    stats[...] = jnp.broadcast_to(both[None], stats.shape)


def read_stats(stats, rows):
    devices, _, channels = stats.shape
    shape = (8, channels)
    means = [jnp.broadcast_to(stats[k, 0:1, :], shape) for k in range(devices)]
    spreads = [jnp.broadcast_to(stats[k, 1:2, :], shape) for k in range(devices)]
    mean = functools.reduce(jnp.add, means) / devices
    spread = functools.reduce(jnp.add, spreads)
    spread = spread + rows * functools.reduce(jnp.add, [(m - mean) * (m - mean) for m in means])
    rows = rows * devices
    lane = lax.broadcasted_iota(jnp.int32, shape, 1)
    step = 1
    while step < channels // GROUPS:
        low = jnp.bitwise_and(lane, step) == 0
        others = [
            jnp.where(low, pltpu.roll(row, channels - step, 1), pltpu.roll(row, step, 1))
            for row in (mean, spread)
        ]
        mean, spread = merge(mean, spread, rows, *others)
        rows, step = 2.0 * rows, 2 * step
    return mean, lax.rsqrt(spread / rows + EPSILON)


def silu_of_double(h):
    return h + h * jnp.tanh(h)


def norm_kernel(ny, nx, pos, inner, ends, stats, gain, offset, out, pooled, *refs):
    y_edges, x_edges, corners, half = refs
    depth, edge = inner.shape[0] + 6, inner.shape[1]
    deep, deep_depth = edge // 2, depth // 2
    f32, bf16 = jnp.float32, jnp.bfloat16
    mean, scale = read_stats(stats, float(edge**3))
    scale = scale * (0.5 * gain[...])
    shift = 0.5 * offset[...]
    for k in range(deep_depth):
        value = [
            ends[z] if z < 3 else inner[z - 3] if z < depth - 3 else ends[z - depth + 6]
            for z in (2 * k, 2 * k + 1)
        ]
        value = jnp.stack(value).reshape(edge * edge // 4, 8, 128)
        value = silu_of_double((value - mean) * scale + shift)
        value = value.reshape(2, edge, edge, 128).astype(bf16)
        if 0 < k < deep_depth - 1:
            out[2 * k - 2 : 2 * k] = value
        value = value.astype(f32)
        value = (value[0] + value[1]).reshape(deep, 2, edge, 128)
        half[k] = (value[:, 0] + value[:, 1]).reshape(deep * edge, 128)
        lines = half.at[k]
        pair = lines[pl.ds(0, deep * deep, stride=2), :] + lines[pl.ds(1, deep * deep, stride=2), :]
        pair = (pair * 0.125).astype(bf16).astype(f32).reshape(deep, deep, 128)
        if k == 0 or k == deep_depth - 1:
            inside = pos[ny + nx + (0 if k == 0 else 1)] == 1
            pair = jnp.where(inside, pair, 0.0)
        pooled[k] = pair
    lines = pooled.reshape(deep_depth * deep * deep, 128)
    rows = deep_depth * deep
    first_x = lines[pl.ds(0, rows, stride=deep), :]
    last_x = lines[pl.ds(deep - 1, rows, stride=deep), :]
    first_y, last_y = (pooled[:, y].reshape(rows, 128) for y in (0, deep - 1))
    ends = []
    for y in (0, deep - 1):
        for x in (0, deep - 1):
            ends.append(lines[pl.ds(y * deep + x, deep_depth, stride=deep * deep), :])
    if ny == 1:
        above, left = pos[0] == 1, pos[1] == 1
        y_edges[0] = jnp.where(above, first_y, last_y).astype(bf16)
        x_edges[0] = jnp.where(left, first_x, last_x).astype(bf16)
        corners[0, 0:deep_depth] = jnp.where(
            above, jnp.where(left, ends[0], ends[1]), jnp.where(left, ends[2], ends[3])
        )
    else:
        y_edges[0], y_edges[1] = first_y.astype(bf16), last_y.astype(bf16)
        x_edges[0], x_edges[1] = first_x.astype(bf16), last_x.astype(bf16)
        for k in range(4):
            corners[k, 0:deep_depth] = ends[k]


def stack_kernel(*refs):
    out = refs[-1]
    for k in range(out.shape[0]):
        out[k] = refs[k][...]


def stack(*arrays):
    vmem = pl.BlockSpec(memory_space=pltpu.VMEM)
    return pl.pallas_call(
        stack_kernel,
        out_shape=jax.ShapeDtypeStruct((len(arrays),) + arrays[0].shape, arrays[0].dtype),
        in_specs=[vmem] * len(arrays),
        out_specs=vmem,
        compiler_params=pltpu.CompilerParams(vmem_limit_bytes=VMEM_BYTES),
    )(*arrays)


def place_kernel(pos, own, *refs):
    *held, out, sem = refs
    tile, mine = pos[pos.shape[0] - 2], pos[pos.shape[0] - 1]
    copy = pltpu.make_async_copy(own, out.at[tile], sem)
    copy.start()
    if len(held) == 1:
        pieces, others, size = held[0].shape[:3]
        for piece in range(pieces):
            at = jnp.minimum(jnp.bitwise_xor(mine, piece) * size, own.shape[0] - size)
            for k in range(others):
                out[jnp.bitwise_xor(tile, k + 1), pl.ds(at, size)] = held[0][piece, k]
    else:
        for k, shard in enumerate(held):
            out[lax.rem(tile + len(held) - k, len(held) + 1)] = shard[...]
    copy.wait()


def deep_kernel(ny, nx, pos, pooled, y_halos, x_halos, corners, kernel, *refs):
    act, stats, grid, packed = refs
    depth, deep = pooled.shape[0], pooled.shape[1]
    f32 = jnp.float32
    grid[...] = jnp.zeros(grid.shape, f32)
    grid[:, 1 : deep + 1, 8:16] = pooled[...]
    for i in range(ny):
        at = jnp.where(pos[i] == 1, 0, deep + 1)
        grid[:, at, 8:16] = y_halos[i].astype(f32).reshape(depth, deep, 128)
    pitch = (deep + 2) * 24
    flat = grid.reshape(depth * pitch, 128)
    for j in range(nx):
        left = pos[ny + j] == 1
        column = x_halos[j].astype(f32).reshape(depth, deep, 128)
        for side, here in ((7, left), (16, jnp.logical_not(left))):
            if nx == 2 and side != (7, 16)[j]:
                continue
            for z in range(depth):
                kept = column[z] if nx == 2 else jnp.where(here, column[z], 0.0)
                flat[pl.ds(z * pitch + 24 + side, deep, stride=24), :] = kept
            for i in range(ny):
                end = corners[i * nx + j, 0:depth]
                above = pos[i] == 1
                for y, there in ((0, above), (deep + 1, jnp.logical_not(above))):
                    if ny == 2 and y != (0, deep + 1)[i]:
                        continue
                    kept = end
                    if nx == 1:
                        kept = jnp.where(jnp.logical_and(here, there), end, 0.0)
                    flat[pl.ds(y * 24 + side, depth, stride=pitch), :] = kept

    for dx in range(3):
        plane = grid[:, :, 7 + dx : 15 + dx]
        for y in range(deep + 1):
            both = jnp.concatenate([plane[:, y], plane[:, y + 1]], axis=1)
            packed[:, y // 2, y % 2, :, dx * 128 : dx * 128 + 128] = both.astype(jnp.bfloat16)

    rows = deep**3
    total = None
    for dz in range(3):
        left = jnp.concatenate(
            [
                packed[dz : dz + deep, dy // 2 : dy // 2 + deep // 2, dy % 2].reshape(rows, 384)
                for dy in range(3)
            ],
            axis=1,
        )
        right = jnp.concatenate(
            [kernel[:, dz * 9 + tap].reshape(-1, 128) for tap in range(9)], axis=1
        )
        term = lax.dot_general(
            left, right, (((1,), (1,)), ((), ())), preferred_element_type=f32
        )
        total = term if total is None else total + term
    act[...] = total
    total = total.reshape(rows // 8, 8, -1)
    rows = rows // 8
    mean = jnp.sum(total, axis=0) / rows
    off = total - mean
    put_stats(stats, mean, jnp.sum(off * off, axis=0), rows)


def final_kernel(_, act, stats, gain, offset, up, mid, out, wide, held, sems):
    edge = mid.shape[0]
    deep = edge // 2
    f32 = jnp.float32
    mean, scale = read_stats(stats, float(deep**3))
    scale = scale * (0.5 * gain[...])
    shift = 0.5 * offset[...]
    planes = 2
    size = planes * deep * deep
    copies = []
    for k in range(0, deep, planes):
        value = act[k * deep * deep : k * deep * deep + size].reshape(size // 8, 8, -1)
        value = silu_of_double((value - mean) * scale + shift)
        value = value.reshape(size, -1).astype(jnp.bfloat16)
        lifted = jnp.dot(value, up[...], preferred_element_type=f32)
        lines = wide.at[k // planes]
        lines[pl.ds(0, size, stride=2), :] = lifted
        lines[pl.ds(1, size, stride=2), :] = lifted
        add = lines[...].reshape(planes, 1, deep, 1, edge, 128)
        at = pl.ds(2 * k, 2 * planes)
        old = mid[at].astype(f32).reshape(planes, 2, deep, 2, edge, 128)
        held[at] = (old + add).astype(jnp.bfloat16).reshape(2 * planes, edge, edge, 128)
        copy = pltpu.make_async_copy(held.at[at], out.at[at], sems.at[k // planes])
        copy.start()
        copies.append(copy)
    for copy in copies:
        copy.wait()


def body(
    features, conv_weight, gain_mid, offset_mid, deep_weight, gain_deep, offset_deep, up_weight
):
    f32, bf16 = jnp.float32, jnp.bfloat16
    edge, channels = features.shape[0], features.shape[3]
    deep = edge // 2
    deep_channels = gain_deep.shape[0]
    square = Square()
    tiles = square.tiles
    devices = lax.axis_size("gz") * tiles
    y_low, x_low = square.low_sides()
    ny, nx = len(y_low), len(x_low)
    riders = Riders(deep_weight.shape[4])
    depth_at = lax.axis_index("gz")
    inside = [depth_at > 0, depth_at < lax.axis_size("gz") - 1]
    pos = y_low + x_low + inside + [depth_at % 2, lax.axis_index("yx"), riders.mine]
    pos = jnp.stack([jnp.asarray(v, jnp.int32) for v in pos])

    own = jnp.moveaxis(deep_weight, 4, 3).reshape(-1, 16, channels)
    conv_weight = conv_weight.reshape(27, channels, channels)
    *edges, field, conv_weight = call(
        functools.partial(start_kernel, ny, nx, riders.size),
        [
            ((ny, edge + riders.size, edge, channels), bf16),
            ((nx, edge + riders.size, edge, channels), bf16),
            ((ny * nx, 1 + riders.size, edge, channels), bf16),
            ((edge + 2, edge + 2, edge, channels), bf16),
            (conv_weight.shape, bf16),
        ],
        [((nx, edge * edge, 8, channels), f32), pltpu.SemaphoreType.DMA((20,))],
        pos,
        features,
        conv_weight,
        own,
        nbytes=5 << 20,
        in_hbm=3,
    )
    halos = square.halos(*(list(piece) for piece in edges))
    conv_flops = 54 * channels * channels * edge**3
    act, taps, pairs = call(
        conv_kernel,
        [
            ((edge, edge, edge, channels), f32),
            ((9 * channels, 3 * channels), bf16),
            ((12 * channels, 2 * channels), bf16),
        ],
        [],
        pos,
        field,
        conv_weight,
        flops=conv_flops,
        nbytes=6 << 20,
    )
    (y, x, corner), act = lax.optimization_barrier((halos, act))
    y, x, corner = jnp.stack(y), jnp.stack(x), jnp.stack(corner)
    face = ((3 * (edge + ny + nx) + ny * nx, edge, channels), bf16)
    held = [((3, riders.size, 16, channels), bf16)] if riders.size else []
    outer, inner, *held = call(
        functools.partial(face_kernel, ny, nx, riders.size),
        [face, face] + held,
        [],
        pos,
        field,
        y,
        x,
        corner,
    )
    outer, inner = swap_depth(outer, inner)
    if riders.size:
        held = held[0][None]
        other = swap(held, *riders.STEPS[0])
    else:
        held = rotate_shards(own)
    six = ((6, edge, edge, channels), f32)
    column = (edge + 16, channels)
    middle, partial, stats = call(
        functools.partial(side_kernel, ny, nx),
        [
            ((edge - 2, edge, edge, channels), f32),
            ((4, edge, edge, channels), f32),
            ((16, channels), f32),
        ],
        [((edge + 2, edge, edge, channels), f32), ((edge + 4,) + column, f32)],
        pos,
        act,
        y,
        x,
        corner,
        taps,
        flops=conv_flops // 4,
        nbytes=6 << 20,
    )
    ends, stats = call(
        functools.partial(end_kernel, ny, nx),
        [six, ((devices, 2, channels), f32)],
        [
            ((2,) + face[0], bf16),
            ((4, edge + 2, edge, channels), bf16),
            ((5,) + column, f32),
        ],
        pos,
        field,
        stats,
        partial,
        outer,
        inner,
        taps,
        pairs,
        flops=conv_flops // 2,
        nbytes=3 << 20,
    )
    if riders.size:
        stats, other = lax.optimization_barrier((stats, other))
        held = stack(held, other).reshape((-1,) + held.shape[1:])
        other = swap(held, *riders.STEPS[1])
        stats = share(stats)
        stats, other = lax.optimization_barrier((stats, other))
        held = stack(held, other).reshape((-1,) + held.shape[1:])
        other = swap(held, *riders.STEPS[2])
        held = [stack(held, other).reshape((-1,) + held.shape[1:])]
    else:
        stats = share(stats)
    out, pooled, *edges = call(
        functools.partial(norm_kernel, ny, nx),
        [
            ((edge, edge, edge, channels), bf16),
            ((deep + 2, deep, deep, channels), f32),
            ((ny, (deep + 2) * deep, channels), bf16),
            ((nx, (deep + 2) * deep, channels), bf16),
            ((ny * nx, 16, channels), f32),
        ],
        [((deep + 2, deep * edge, channels), f32)],
        pos,
        middle,
        ends,
        stats,
        gain_mid.reshape(1, channels),
        offset_mid.reshape(1, channels),
        flops=20 * channels * edge**3,
        nbytes=3 << 20,
    )
    y, x, corner = square.halos(*(list(piece) for piece in edges))
    (kernel,) = call(
        place_kernel,
        [((tiles,) + own.shape, bf16)],
        [pltpu.SemaphoreType.DMA],
        pos,
        own,
        *held,
        nbytes=4 << 20,
        in_hbm=1,
    )
    kernel = kernel.reshape(tiles, 27, deep_weight.shape[4], channels)
    deep_act, stats = call(
        functools.partial(deep_kernel, ny, nx),
        [((deep**3, deep_channels), f32), ((devices, 2, deep_channels), f32)],
        [
            ((deep + 2, deep + 2, 24, channels), f32),
            ((deep + 2, deep // 2 + 1, 2, 16, 3 * channels), bf16),
        ],
        pos,
        pooled,
        jnp.stack(y),
        jnp.stack(x),
        jnp.stack(corner),
        kernel,
        flops=2 * 27 * channels * deep_channels * deep**3,
        nbytes=4 << 20,
    )
    stats = share(stats)
    (decoded,) = call(
        final_kernel,
        [((edge, edge, edge, channels), bf16)],
        [
            ((deep // 2, 4 * deep * deep, channels), f32),
            ((edge, edge, edge, channels), bf16),
            pltpu.SemaphoreType.DMA((deep // 2,)),
        ],
        pos,
        deep_act,
        stats,
        gain_deep.reshape(1, deep_channels),
        offset_deep.reshape(1, deep_channels),
        up_weight,
        out,
        flops=4 * deep_channels * channels * deep**3,
        nbytes=3 << 20,
        out_hbm=True,
    )
    return decoded


def solution(mesh):
    placed = (
        P(("cand", "gz"), "yx", None, None),
        P(),
        P(),
        P(),
        P(None, None, None, None, "yx"),
        P(),
        P(),
        P(),
    )
    return jax.shard_map(
        body,
        mesh=mesh,
        in_specs=placed,
        out_specs=P(("cand", "gz"), "yx", None, None),
        check_vma=False,
    )
```

```python
import functools
import math

import jax
import jax.numpy as jnp
from jax import lax
from jax.experimental import pallas as pl
from jax.experimental.pallas import tpu as pltpu
from jax.sharding import PartitionSpec as P

GROUPS = 32
EPSILON = 1e-05
PART = ("gz", "yx")
VMEM_BYTES = 32 * 1024 * 1024


class Square:
    def __init__(self):
        self.tiles = lax.axis_size("yx")
        self.side = math.isqrt(self.tiles)
        tile = lax.axis_index("yx")
        self.row, self.column = tile // self.side, tile % self.side
        self.folded = self.side == 2
        self.steps = (0,) if self.folded else (-1, 1)

    def low_sides(self):
        if self.folded:
            return [self.row == 1], [self.column == 1]
        return [True, False], [True, False]

    def route(self, down, right):
        pairs = []
        for tile in range(self.tiles):
            row, column = tile // self.side + down, tile % self.side + right
            if 0 <= row < self.side and 0 <= column < self.side:
                pairs.append((tile, row * self.side + column))
        return pairs

    def swap_route(self, mask):
        return [(tile, tile ^ mask) for tile in range(self.tiles)]

    def halos(self, y_edges, x_edges, corners):
        if self.folded:
            y = lax.ppermute(y_edges[0], "yx", self.swap_route(2))
            x = lax.ppermute(x_edges[0], "yx", self.swap_route(1))
            corner = lax.ppermute(corners[0], "yx", self.swap_route(3))
            return [y], [x], [corner]
        y = [lax.ppermute(y_edges[k], "yx", self.route((1, -1)[1 - k], 0)) for k in (1, 0)]
        x = [lax.ppermute(x_edges[k], "yx", self.route(0, (1, -1)[1 - k])) for k in (1, 0)]
        corner = [
            lax.ppermute(corners[2 * k + j], "yx", self.route((1, -1)[1 - k], (1, -1)[1 - j]))
            for k in (1, 0)
            for j in (1, 0)
        ]
        return y, x, corner


def swap_depth(outer, inner):
    size = lax.axis_size("gz")
    routes = [[], []]
    for low in range(size - 1):
        routes[low % 2] += [(low, low + 1), (low + 1, low)]
    return lax.ppermute(outer, "gz", routes[1]), lax.ppermute(inner, "gz", routes[0])


class Riders:
    STEPS = (("cand", 1), ("gz", 2), ("gz", 1))

    def __init__(self, rows):
        self.tiles = 27 * rows // 16
        self.fits = (
            lax.axis_size("yx") == 4
            and lax.axis_size("cand") % 2 == 0
            and lax.axis_size("gz") % 4 == 0
            and self.tiles >= 8
        )
        self.size = -(-self.tiles // 8) if self.fits else 0

    @classmethod
    def mine(cls):
        return sum(
            lax.axis_index(axis) // mask % 2 * 2**k for k, (axis, mask) in enumerate(cls.STEPS)
        )


def rotate_shards(piece):
    tiles = lax.axis_size("yx")
    return [
        lax.ppermute(piece, "yx", [(i, (i + k) % tiles) for i in range(tiles)]) for k in range(1, tiles)
    ]


def swap(block, axis, mask):
    return lax.ppermute(block, axis, [(i, i ^ mask) for i in range(lax.axis_size(axis))])


def share(stats):
    return lax.all_to_all(stats, PART, 0, 0)


def call(kernel, outs, scratch, *arrays, flops=0, nbytes=0, in_hbm=0, out_hbm=False):
    vmem, hbm = (pl.BlockSpec(memory_space=space) for space in (pltpu.VMEM, pltpu.HBM))
    far, near = arrays[:in_hbm], arrays[in_hbm:]
    far = [pltpu.with_memory_space_constraint(array, pltpu.HBM) for array in far]
    return pl.pallas_call(
        kernel,
        out_shape=[jax.ShapeDtypeStruct(shape, dtype) for shape, dtype in outs],
        in_specs=[hbm] * len(far) + [vmem] * len(near),
        out_specs=[hbm if out_hbm else vmem] * len(outs),
        scratch_shapes=[pltpu.VMEM(*entry) if isinstance(entry, tuple) else entry for entry in scratch],
        compiler_params=pltpu.CompilerParams(vmem_limit_bytes=VMEM_BYTES),
        cost_estimate=pl.CostEstimate(flops=flops, bytes_accessed=nbytes, transcendentals=0),
    )(*far, *near)


def start_kernel(ny, nx, size, x_in, w_in, d_in, y_out, x_out, corners, x, w, lines, sems):
    edge = x_in.shape[0]
    f32, bf16 = jnp.float32, jnp.bfloat16
    above, left = Square().low_sides()
    chunks = 4
    planes = edge // chunks
    first = [
        pltpu.make_async_copy(
            x_in.at[pl.ds(k * planes, planes)],
            x.at[pl.ds(1 + k * planes, planes), pl.ds(1, edge)],
            sems.at[k],
        )
        for k in range(chunks)
    ]
    later = []
    if size:
        at = jnp.minimum(Riders.mine() * size, d_in.shape[0] - size)
        for k, (out, begin) in enumerate(((y_out, edge), (x_out, edge), (corners, 1))):
            later.append(
                pltpu.make_async_copy(
                    d_in.at[pl.ds(at, size)], out.at[0, pl.ds(begin, size)], sems.at[chunks + k]
                )
            )
    later.append(pltpu.make_async_copy(w_in, w, sems.at[chunks + 3]))
    for copy in first + later:
        copy.start()
    x[0] = jnp.zeros(x.shape[1:], bf16)
    x[edge + 1] = jnp.zeros(x.shape[1:], bf16)
    blank = jnp.zeros((edge,) + x.shape[2:], bf16)
    x[1 : edge + 1, 0] = blank
    x[1 : edge + 1, edge + 1] = blank
    flat = lines.reshape(nx * edge * edge * 8, 128)
    part = planes * edge
    for k in range(chunks):
        first[k].wait()
        at, here = pl.ds(k * planes, planes), pl.ds(1 + k * planes, planes)
        for i in range(ny):
            row = jnp.where(above[i], 1, edge)
            y_out[i, at] = x[here, row]
        for j in range(nx):
            low = x[here, 1 : edge + 1, 0:8].astype(f32).reshape(part, 8, 128)
            high = x[here, 1 : edge + 1, edge - 8 : edge].astype(f32).reshape(part, 8, 128)
            high = pltpu.roll(high, 1, 1)
            kept = jnp.where(left[j], low, high)
            lines[j, k * part : k * part + part] = kept
            begin = (j * edge * edge + k * part) * 8
            column = flat[pl.ds(begin, part, stride=8), :]
            x_out[j, at] = column.astype(bf16).reshape(planes, edge, 128)
    for i in range(ny):
        for j in range(nx):
            begin = j * edge * edge * 8
            low = flat[pl.ds(begin, edge, stride=8 * edge), :]
            high = flat[pl.ds(begin + 8 * (edge - 1), edge, stride=8 * edge), :]
            kept = jnp.where(above[i], low, high)
            corners[i * nx + j, 0] = kept.astype(bf16)
    for copy in later:
        copy.wait()


def face_kernel(ny, nx, size, x, y_halos, x_halos, corners, outer, inner, *riders):
    edge = outer.shape[1]
    wide = edge + ny + nx
    odd = lax.axis_index("gz") % 2
    far = edge - 3
    for face, at in ((outer, odd * far), (inner, (1 - odd) * far)):
        for k in range(3):
            row = k * wide
            face[row : row + edge] = x[1 + at + k, 1 : edge + 1]
            for i in range(ny):
                face[row + edge + i] = y_halos[i, at + k]
            for j in range(nx):
                face[row + edge + ny + j] = x_halos[j, at + k]
        for k in range(ny * nx):
            face[3 * wide + k] = corners[k, 0]
    if size:
        riders[0][0] = x_halos[0, edge : edge + size]
        riders[0][1] = y_halos[0, edge : edge + size]
        riders[0][2] = corners[0, 1 : 1 + size]


def spread_taps(weight, taps):
    for tap in range(27):
        row, lane = tap // 3 * 128, tap % 3 * 128
        taps[row : row + 128, lane : lane + 128] = weight[tap]


def pair_taps(weight, pairs):
    for dz in range(3):
        for line in range(4):
            row = (dz * 4 + line) * 128
            for out in range(2):
                lane = out * 128
                if 0 <= line - out < 3:
                    block = weight[dz * 9 + (line - out) * 3 + 2]
                else:
                    block = jnp.zeros((128, 128), pairs.dtype)
                pairs[row : row + 128, lane : lane + 128] = block


def join_x(wide, edge):
    place = lax.broadcasted_iota(jnp.int32, wide.shape[:2] + (128,), 1)
    after = jnp.where(place > 0, pltpu.roll(wide[:, :, :128], 1, 1), 0.0)
    before = jnp.where(place < edge - 1, pltpu.roll(wide[:, :, 256:], edge - 1, 1), 0.0)
    return wide[:, :, 128:256] + after + before


def convolve(grid, count, taps, pairs, put):
    edge = grid.shape[2]
    planes = min(count, 4)
    rows = planes * edge * edge
    place = lax.broadcasted_iota(jnp.int32, (planes * edge, edge, 128), 1)
    halved = grid.reshape(grid.shape[0], edge // 2 + 1, 2, edge, 128)
    for z in range(0, count, planes):
        left = jnp.concatenate(
            [
                grid[z + dz : z + dz + planes, dy : dy + edge].reshape(rows, 128)
                for dz in range(3)
                for dy in range(3)
            ],
            axis=1,
        )
        wide = jnp.dot(left, taps[:, 0:256], preferred_element_type=jnp.float32)
        wide = wide.reshape(planes * edge, edge, 256)
        left = jnp.concatenate(
            [
                halved[z + dz : z + dz + planes, line // 2 : line // 2 + edge // 2, line % 2].reshape(
                    rows // 2, 128
                )
                for dz in range(3)
                for line in range(4)
            ],
            axis=1,
        )
        two = jnp.dot(left, pairs[...], preferred_element_type=jnp.float32)
        two = two.reshape(planes * edge // 2, edge, 256)
        two = jnp.stack([two[:, :, :128], two[:, :, 128:]], axis=1).reshape(planes * edge, edge, 128)
        after = jnp.where(place > 0, pltpu.roll(wide[:, :, :128], 1, 1), 0.0)
        before = jnp.where(place < edge - 1, pltpu.roll(two, edge - 1, 1), 0.0)
        new = wide[:, :, 128:256] + after + before
        put(z, new.reshape(planes, edge, edge, 128))


def conv_kernel(deep_in, x, weight, act, taps, pairs, deep_weight, sem):
    copy = pltpu.make_async_copy(deep_in, deep_weight, sem)
    copy.start()
    edge = act.shape[0]
    spread_taps(weight, taps)
    pair_taps(weight, pairs)

    def put(z, new):
        act[z : z + new.shape[0]] = new

    convolve(x, edge, taps, pairs, put)
    copy.wait()


def y_terms(line, low, taps):
    planes, edge = line.shape[0] - 2, line.shape[1]
    left = jnp.concatenate(
        [line[dz : dz + planes].reshape(planes * edge, 128) for dz in range(3)], axis=1
    )
    start = jnp.where(low, 0, 256)
    right = jnp.concatenate(
        [taps[pl.ds(pl.multiple_of(start + dz * 384, 128), 128), :] for dz in range(3)], axis=0
    )
    wide = jnp.dot(left, right, preferred_element_type=jnp.float32)
    return join_x(wide.reshape(planes, edge, 384), edge)


def x_terms(column, taps):
    planes, edge = column.shape[0] - 2, column.shape[1] - 16
    lines = [column[:, 7 + dy : 7 + dy + edge].astype(jnp.bfloat16) for dy in range(3)]
    left = jnp.concatenate(
        [line[dz : dz + planes].reshape(planes * edge, 128) for dz in range(3) for line in lines],
        axis=1,
    )
    right = jnp.concatenate([taps[:, 0:128], taps[:, 256:384]], axis=1)
    both = jnp.dot(left, right, preferred_element_type=jnp.float32)
    return both[:, :128], both[:, 128:]


def fill_column(column, at, voxels, ends, above):
    count, edge = voxels.shape[:2]
    rows = edge + 16
    lines = column.reshape(column.shape[0] * rows, 128)
    column[at : at + count, 8 : 8 + edge] = voxels.astype(jnp.float32)
    for i, end in enumerate(ends):
        first = last = end.astype(jnp.float32)
        if len(ends) == 1:
            first, last = jnp.where(above[0], first, 0.0), jnp.where(above[0], 0.0, last)
        if len(ends) == 1 or i == 0:
            lines[pl.ds(at * rows + 7, count, stride=rows), :] = first
        if len(ends) == 1 or i == 1:
            lines[pl.ds(at * rows + 8 + edge, count, stride=rows), :] = last


def add_column(act, terms, j, nx, low):
    planes, edge = act.shape[:2]
    flat = act.reshape(planes * edge * edge, 128)
    first, last = terms
    if nx == 1:
        first, last = jnp.where(low, first, 0.0), jnp.where(low, 0.0, last)
    if nx == 1 or j == 0:
        flat[pl.ds(0, planes * edge, stride=edge), :] += first
    if nx == 1 or j == 1:
        flat[pl.ds(edge - 1, planes * edge, stride=edge), :] += last


def moments(planes):
    count, edge = planes.shape[:2]
    zero = jnp.zeros((8, 128), jnp.float32)

    def sum_step(k, carry):
        return carry + jnp.sum(planes[k].reshape(edge * 2, 8, 128), axis=0)

    mean = lax.fori_loop(0, count, sum_step, zero, unroll=True) / (count * edge * edge // 8)

    def spread_step(k, carry):
        off = planes[k].reshape(edge * 2, 8, 128) - mean
        return carry + jnp.sum(off * off, axis=0)

    return mean, lax.fori_loop(0, count, spread_step, zero, unroll=True)


def side_kernel(ny, nx, own, y_halos, x_halos, corners, taps, inner, ends, stats, act, column):
    edge = own.shape[0]
    act[0] = jnp.zeros(act.shape[1:], jnp.float32)
    act[edge + 1] = jnp.zeros(act.shape[1:], jnp.float32)
    act[1 : edge + 1] = own[...]
    above, left = Square().low_sides()
    blank = jnp.zeros((2, edge, 128), jnp.bfloat16)
    for i in range(ny):
        line = jnp.concatenate([blank, y_halos[i, 0:edge], blank], axis=0)
        act[:, jnp.where(above[i], 0, edge - 1)] += y_terms(line, above[i], taps)
    for j in range(nx):
        column[...] = jnp.zeros(column.shape, jnp.float32)
        fill_column(
            column, 2, x_halos[j, 0:edge], [corners[i * nx + j, 0] for i in range(ny)], above
        )
        add_column(act, x_terms(column, taps), j, nx, left[j])
    inner[...] = act[2:edge]
    ends[0:2] = act[0:2]
    ends[2:4] = act[edge : edge + 2]
    mean, spread = moments(act.at[2:edge])
    stats[0:8] = mean
    stats[8:16] = spread


def end_kernel(ny, nx, *refs):
    x, inner_stats, partial, outer_face, inner_face, taps, pairs, act, stats, faces, grid, column = refs
    edge = x.shape[2]
    wide_face = edge + ny + nx
    f32 = jnp.float32
    odd = lax.axis_index("gz") % 2 == 1
    faces[0] = jnp.where(odd, inner_face[...], outer_face[...])
    faces[1] = jnp.where(odd, outer_face[...], inner_face[...])
    above, left = Square().low_sides()
    blank = jnp.zeros(grid.shape[:1] + grid.shape[2:], grid.dtype)
    grid[:, 0] = blank
    grid[:, edge + 1] = blank
    gap = jnp.zeros((2, edge, 128), grid.dtype)
    for side, halo_at, own_at, plane, at, beyond, own, beside, dz in (
        (0, 0, 3, 1, 0, 0, 2, 2, 0),
        (1, 1, 0, edge, 3, 4, 3, 1, 2),
    ):
        for k in range(3):
            begin = k * wide_face
            grid[halo_at + k, 1 : edge + 1] = faces[side, begin : begin + edge]
        grid[own_at, 1 : edge + 1] = x[plane, 1 : edge + 1]

        def put(z, new):
            act[beyond + z : beyond + z + new.shape[0]] = new

        convolve(grid, 2, taps, pairs, put)
        stacked = jnp.concatenate(
            [grid[beside, dy : dy + edge].reshape(edge * edge, 128) for dy in range(3)], axis=1
        )
        wide = jnp.dot(stacked, taps[dz * 384 : dz * 384 + 384, :], preferred_element_type=f32)
        own_part = partial[1 if side == 0 else 2]
        act[own] = own_part + join_x(wide.reshape(edge, edge, 384), edge)
        near = 1 if side == 0 else 4
        act[near] += partial[0 if side == 0 else 3]

        def rim(row):
            planes = [faces[side, k * wide_face + edge + row] for k in range(3)]
            return jnp.stack(planes)

        three = act.at[at : at + 3]
        for i in range(ny):
            line = [rim(i), gap] if side == 0 else [gap, rim(i)]
            three[:, jnp.where(above[i], 0, edge - 1)] += y_terms(
                jnp.concatenate(line, axis=0), above[i], taps
            )
        for j in range(nx):
            column[...] = jnp.zeros(column.shape, f32)
            ends = []
            for i in range(ny):
                tile = faces[side, 3 * wide_face + i * nx + j].astype(f32)
                ends.append(tile[edge - 3 :] if side == 0 else tile[:3])
            fill_column(column, 0 if side == 0 else 2, rim(ny + j), ends, above)
            add_column(three, x_terms(column, taps), j, nx, left[j])

    mean, spread = moments(act.at[2:4])
    few, many = edge * edge // 4, (edge - 2) * edge * edge // 8
    inner_mean, inner_spread = inner_stats[0:8], inner_stats[8:16]
    off = inner_mean - mean
    share_of = few / (few + many)
    spread = spread + inner_spread + (many * share_of) * (off * off)
    put_stats(stats, inner_mean - share_of * off, spread, few + many)


def merge(mean, spread, rows, other_mean, other_spread):
    off = mean - other_mean
    return 0.5 * (mean + other_mean), spread + other_spread + (0.5 * rows) * (off * off)


def put_stats(stats, mean, spread, rows):
    for step in (1, 2, 4):
        others = pltpu.roll(mean, step, 0), pltpu.roll(spread, step, 0)
        mean, spread = merge(mean, spread, float(rows * step), *others)
    both = jnp.concatenate([mean[0:1], spread[0:1]], axis=0)
    stats[...] = jnp.broadcast_to(both[None], stats.shape)


def read_stats(stats, rows):
    devices, _, channels = stats.shape
    shape = (8, channels)
    means = [jnp.broadcast_to(stats[k, 0:1, :], shape) for k in range(devices)]
    spreads = [jnp.broadcast_to(stats[k, 1:2, :], shape) for k in range(devices)]
    mean = functools.reduce(jnp.add, means) / devices
    spread = functools.reduce(jnp.add, spreads)
    spread = spread + rows * functools.reduce(jnp.add, [(m - mean) * (m - mean) for m in means])
    rows = rows * devices
    lane = lax.broadcasted_iota(jnp.int32, shape, 1)
    step = 1
    while step < channels // GROUPS:
        low = jnp.bitwise_and(lane, step) == 0
        others = [
            jnp.where(low, pltpu.roll(row, channels - step, 1), pltpu.roll(row, step, 1))
            for row in (mean, spread)
        ]
        mean, spread = merge(mean, spread, rows, *others)
        rows, step = 2.0 * rows, 2 * step
    return mean, lax.rsqrt(spread / rows + EPSILON)


def silu_of_double(h):
    return h + h * jnp.tanh(h)


def norm_kernel(ny, nx, inner, ends, stats, gain, offset, out, pooled, *refs):
    y_edges, x_edges, corners, half = refs
    depth, edge = inner.shape[0] + 6, inner.shape[1]
    deep, deep_depth = edge // 2, depth // 2
    f32, bf16 = jnp.float32, jnp.bfloat16
    above, left = Square().low_sides()
    depth_at = lax.axis_index("gz")
    mean, scale = read_stats(stats, float(edge**3))
    scale = scale * (0.5 * gain[...])
    shift = 0.5 * offset[...]
    for k in range(deep_depth):
        value = [
            ends[z] if z < 3 else inner[z - 3] if z < depth - 3 else ends[z - depth + 6]
            for z in (2 * k, 2 * k + 1)
        ]
        value = jnp.stack(value).reshape(edge * edge // 4, 8, 128)
        value = silu_of_double((value - mean) * scale + shift)
        value = value.reshape(2, edge, edge, 128).astype(bf16)
        if 0 < k < deep_depth - 1:
            out[2 * k - 2 : 2 * k] = value
        value = value.astype(f32)
        value = (value[0] + value[1]).reshape(deep, 2, edge, 128)
        half[k] = (value[:, 0] + value[:, 1]).reshape(deep * edge, 128)
        lines = half.at[k]
        pair = lines[pl.ds(0, deep * deep, stride=2), :] + lines[pl.ds(1, deep * deep, stride=2), :]
        pair = (pair * 0.125).astype(bf16).astype(f32).reshape(deep, deep, 128)
        if k == 0 or k == deep_depth - 1:
            inside = depth_at > 0 if k == 0 else depth_at < lax.axis_size("gz") - 1
            pair = jnp.where(inside, pair, 0.0)
        pooled[k] = pair
    lines = pooled.reshape(deep_depth * deep * deep, 128)
    rows = deep_depth * deep
    first_x = lines[pl.ds(0, rows, stride=deep), :]
    last_x = lines[pl.ds(deep - 1, rows, stride=deep), :]
    first_y, last_y = (pooled[:, y].reshape(rows, 128) for y in (0, deep - 1))
    ends = []
    for y in (0, deep - 1):
        for x in (0, deep - 1):
            ends.append(lines[pl.ds(y * deep + x, deep_depth, stride=deep * deep), :])
    if ny == 1:
        above, left = above[0], left[0]
        y_edges[0] = jnp.where(above, first_y, last_y).astype(bf16)
        x_edges[0] = jnp.where(left, first_x, last_x).astype(bf16)
        corners[0, 0:deep_depth] = jnp.where(
            above, jnp.where(left, ends[0], ends[1]), jnp.where(left, ends[2], ends[3])
        )
    else:
        y_edges[0], y_edges[1] = first_y.astype(bf16), last_y.astype(bf16)
        x_edges[0], x_edges[1] = first_x.astype(bf16), last_x.astype(bf16)
        for k in range(4):
            corners[k, 0:deep_depth] = ends[k]


def stack_kernel(*refs):
    out = refs[-1]
    for k in range(out.shape[0]):
        out[k] = refs[k][...]


def stack(*arrays):
    vmem = pl.BlockSpec(memory_space=pltpu.VMEM)
    return pl.pallas_call(
        stack_kernel,
        out_shape=jax.ShapeDtypeStruct((len(arrays),) + arrays[0].shape, arrays[0].dtype),
        in_specs=[vmem] * len(arrays),
        out_specs=vmem,
        compiler_params=pltpu.CompilerParams(vmem_limit_bytes=VMEM_BYTES),
    )(*arrays)


def place_weights(own, held, out):
    tile = lax.axis_index("yx")
    out[tile] = own[...]
    if len(held) == 1:
        pieces, others, size = held[0].shape[:3]
        for piece in range(pieces):
            at = jnp.minimum(jnp.bitwise_xor(Riders.mine(), piece) * size, own.shape[0] - size)
            for k in range(others):
                out[jnp.bitwise_xor(tile, k + 1), pl.ds(at, size)] = held[0][piece, k]
    else:
        for k, shard in enumerate(held):
            out[lax.rem(tile + len(held) - k, len(held) + 1)] = shard[...]


def tap_rows(weight, taps):
    per = weight.shape[1] // 27
    return jnp.concatenate(
        [weight[:, pl.ds(tap * per, per)].reshape(-1, 128) for tap in taps], axis=1
    )


def dot_rows(left, right):
    return lax.dot_general(
        left, right, (((1,), (1,)), ((), ())), preferred_element_type=jnp.float32
    )


def deep_kernel(pooled, own, *refs):
    *held, act, weight, grid, packed = refs
    depth, deep = pooled.shape[0], pooled.shape[1]
    place_weights(own, held, weight)
    grid[...] = jnp.zeros(grid.shape, jnp.float32)
    grid[:, 1 : deep + 1, 8:16] = pooled[...]
    for dx in range(3):
        plane = grid[:, :, 7 + dx : 15 + dx]
        for y in range(deep + 1):
            both = jnp.concatenate([plane[:, y], plane[:, y + 1]], axis=1)
            packed[:, y // 2, y % 2, :, dx * 128 : dx * 128 + 128] = both.astype(jnp.bfloat16)
    rows = deep**3
    total = None
    for dz in range(3):
        left = jnp.concatenate(
            [
                packed[dz : dz + deep, dy // 2 : dy // 2 + deep // 2, dy % 2].reshape(rows, 384)
                for dy in range(3)
            ],
            axis=1,
        )
        term = dot_rows(left, tap_rows(weight, range(dz * 9, dz * 9 + 9)))
        total = term if total is None else total + term
    for half in range(act.shape[0]):
        act[half] = total[:, half * 128 : half * 128 + 128]


def deep_rim_kernel(ny, nx, own, y_halos, x_halos, corners, weight, act, stats, line):
    depth, deep = line.shape[0], line.shape[1] - 16
    halves = act.shape[0]
    f32 = jnp.float32
    square = deep * deep
    above, left = Square().low_sides()
    act[...] = own[...]
    flat = line.reshape(depth * line.shape[1], 128)

    def shifts():
        return jnp.concatenate(
            [
                line[dz : dz + deep, 7 + d : 7 + d + deep].reshape(square, 128).astype(jnp.bfloat16)
                for dz in range(3)
                for d in range(3)
            ],
            axis=1,
        )

    for i in range(ny):
        line[...] = jnp.zeros(line.shape, f32)
        line[:, 8 : 8 + deep] = y_halos[i].astype(f32).reshape(depth, deep, 128)
        for j in range(nx):
            end = corners[i * nx + j, 0:depth]
            first, last = jnp.where(left[j], end, 0.0), jnp.where(left[j], 0.0, end)
            if nx == 1 or j == 0:
                flat[pl.ds(7, depth, stride=line.shape[1]), :] = first
            if nx == 1 or j == 1:
                flat[pl.ds(8 + deep, depth, stride=line.shape[1]), :] = last
        tap = jnp.where(above[i], 0, 6)
        taps = [tap + dz * 9 + dx for dz in range(3) for dx in range(3)]
        terms = dot_rows(shifts(), tap_rows(weight, taps))
        for half in range(halves):
            rows = act.at[half].reshape(deep, deep, deep, 128)
            term = terms[:, half * 128 : half * 128 + 128].reshape(deep, deep, 128)
            rows[:, jnp.where(above[i], 0, deep - 1)] += term
    for j in range(nx):
        line[...] = jnp.zeros(line.shape, f32)
        line[:, 8 : 8 + deep] = x_halos[j].astype(f32).reshape(depth, deep, 128)
        tap = jnp.where(left[j], 0, 2)
        taps = [tap + dz * 9 + dy * 3 for dz in range(3) for dy in range(3)]
        terms = dot_rows(shifts(), tap_rows(weight, taps))
        first, last = jnp.where(left[j], terms, 0.0), jnp.where(left[j], 0.0, terms)
        for half in range(halves):
            lanes, rows = slice(half * 128, half * 128 + 128), act.at[half]
            if nx == 1 or j == 0:
                rows[pl.ds(0, square, stride=deep), :] += first[:, lanes]
            if nx == 1 or j == 1:
                rows[pl.ds(deep - 1, square, stride=deep), :] += last[:, lanes]

    rows = deep**3 // 8
    means, spreads = [], []
    for half in range(halves):
        total = act[half].reshape(rows, 8, 128)
        means.append(jnp.sum(total, axis=0) / rows)
        off = total - means[-1]
        spreads.append(jnp.sum(off * off, axis=0))
    put_stats(stats, *(jnp.concatenate(part, axis=1) for part in (means, spreads)), rows)


def final_kernel(act, stats, gain, offset, up, mid, out, wide, held, sems):
    edge = mid.shape[0]
    deep = edge // 2
    f32 = jnp.float32
    mean, scale = read_stats(stats, float(deep**3))
    scale = scale * (0.5 * gain[...])
    shift = 0.5 * offset[...]
    planes = 2
    size = planes * deep * deep
    copies = []
    for k in range(0, deep, planes):
        at = slice(k * deep * deep, k * deep * deep + size)
        value = jnp.concatenate([act[half, at] for half in range(act.shape[0])], axis=1)
        value = value.reshape(size // 8, 8, -1)
        value = silu_of_double((value - mean) * scale + shift)
        value = value.reshape(size, -1).astype(jnp.bfloat16)
        lifted = jnp.dot(value, up[...], preferred_element_type=f32)
        lines = wide.at[k // planes]
        lines[pl.ds(0, size, stride=2), :] = lifted
        lines[pl.ds(1, size, stride=2), :] = lifted
        add = lines[...].reshape(planes, 1, deep, 1, edge, 128)
        at = pl.ds(2 * k, 2 * planes)
        old = mid[at].astype(f32).reshape(planes, 2, deep, 2, edge, 128)
        held[at] = (old + add).astype(jnp.bfloat16).reshape(2 * planes, edge, edge, 128)
        copy = pltpu.make_async_copy(held.at[at], out.at[at], sems.at[k // planes])
        copy.start()
        copies.append(copy)
    for copy in copies:
        copy.wait()


def body(
    features, conv_weight, gain_mid, offset_mid, deep_weight, gain_deep, offset_deep, up_weight
):
    f32, bf16 = jnp.float32, jnp.bfloat16
    edge, channels = features.shape[0], features.shape[3]
    deep = edge // 2
    deep_channels = gain_deep.shape[0]
    square = Square()
    tiles = square.tiles
    devices = lax.axis_size("gz") * tiles
    ny, nx = (len(sides) for sides in square.low_sides())
    riders = Riders(deep_weight.shape[4])

    own = jnp.moveaxis(deep_weight, 4, 3).reshape(-1, 16, channels)
    conv_weight = conv_weight.reshape(27, channels, channels)
    *edges, field, conv_weight = call(
        functools.partial(start_kernel, ny, nx, riders.size),
        [
            ((ny, edge + riders.size, edge, channels), bf16),
            ((nx, edge + riders.size, edge, channels), bf16),
            ((ny * nx, 1 + riders.size, edge, channels), bf16),
            ((edge + 2, edge + 2, edge, channels), bf16),
            (conv_weight.shape, bf16),
        ],
        [((nx, edge * edge, 8, channels), f32), pltpu.SemaphoreType.DMA((8,))],
        features,
        conv_weight,
        own,
        nbytes=5 << 20,
        in_hbm=3,
    )
    halos = square.halos(*(list(piece) for piece in edges))
    conv_flops = 54 * channels * channels * edge**3
    act, taps, pairs, own = call(
        conv_kernel,
        [
            ((edge, edge, edge, channels), f32),
            ((9 * channels, 3 * channels), bf16),
            ((12 * channels, 2 * channels), bf16),
            (own.shape, bf16),
        ],
        [pltpu.SemaphoreType.DMA],
        own,
        field,
        conv_weight,
        flops=conv_flops,
        nbytes=6 << 20,
        in_hbm=1,
    )
    (y, x, corner), act = lax.optimization_barrier((halos, act))
    y, x, corner = jnp.stack(y), jnp.stack(x), jnp.stack(corner)
    face = ((3 * (edge + ny + nx) + ny * nx, edge, channels), bf16)
    held = [((3, riders.size, 16, channels), bf16)] if riders.size else []
    outer, inner, *held = call(
        functools.partial(face_kernel, ny, nx, riders.size),
        [face, face] + held,
        [],
        field,
        y,
        x,
        corner,
    )
    outer, inner = swap_depth(outer, inner)
    if riders.size:
        held = held[0][None]
        other = swap(held, *riders.STEPS[0])
    else:
        held = rotate_shards(own)
    six = ((6, edge, edge, channels), f32)
    column = (edge + 16, channels)
    middle, partial, stats = call(
        functools.partial(side_kernel, ny, nx),
        [
            ((edge - 2, edge, edge, channels), f32),
            ((4, edge, edge, channels), f32),
            ((16, channels), f32),
        ],
        [((edge + 2, edge, edge, channels), f32), ((edge + 4,) + column, f32)],
        act,
        y,
        x,
        corner,
        taps,
        flops=conv_flops // 4,
        nbytes=6 << 20,
    )
    ends, stats = call(
        functools.partial(end_kernel, ny, nx),
        [six, ((devices, 2, channels), f32)],
        [
            ((2,) + face[0], bf16),
            ((4, edge + 2, edge, channels), bf16),
            ((5,) + column, f32),
        ],
        field,
        stats,
        partial,
        outer,
        inner,
        taps,
        pairs,
        flops=conv_flops // 2,
        nbytes=3 << 20,
    )
    if riders.size:
        stats, other = lax.optimization_barrier((stats, other))
        held = stack(held, other).reshape((-1,) + held.shape[1:])
        other = swap(held, *riders.STEPS[1])
        stats = share(stats)
        stats, other = lax.optimization_barrier((stats, other))
        held = stack(held, other).reshape((-1,) + held.shape[1:])
        other = swap(held, *riders.STEPS[2])
        held = [stack(held, other).reshape((-1,) + held.shape[1:])]
    else:
        stats = share(stats)
    out, pooled, *edges = call(
        functools.partial(norm_kernel, ny, nx),
        [
            ((edge, edge, edge, channels), bf16),
            ((deep + 2, deep, deep, channels), f32),
            ((ny, (deep + 2) * deep, channels), bf16),
            ((nx, (deep + 2) * deep, channels), bf16),
            ((ny * nx, 16, channels), f32),
        ],
        [((deep + 2, deep * edge, channels), f32)],
        middle,
        ends,
        stats,
        gain_mid.reshape(1, channels),
        offset_mid.reshape(1, channels),
        flops=20 * channels * edge**3,
        nbytes=3 << 20,
    )
    y, x, corner = square.halos(*(list(piece) for piece in edges))
    halves = ((deep_channels // 128, deep**3, 128), f32)
    deep_act, weight = call(
        deep_kernel,
        [halves, ((tiles,) + own.shape, bf16)],
        [
            ((deep + 2, deep + 2, 24, channels), f32),
            ((deep + 2, deep // 2 + 1, 2, 16, 3 * channels), bf16),
        ],
        pooled,
        own,
        *held,
        flops=54 * channels * deep_channels * deep**3,
        nbytes=4 << 20,
    )
    deep_act, stats = call(
        functools.partial(deep_rim_kernel, ny, nx),
        [halves, ((devices, 2, deep_channels), f32)],
        [((deep + 2, 24, channels), f32)],
        deep_act,
        jnp.stack(y),
        jnp.stack(x),
        jnp.stack(corner),
        weight,
        flops=4 * channels * deep_channels * deep**3,
        nbytes=3 << 20,
    )
    stats = share(stats)
    (decoded,) = call(
        final_kernel,
        [((edge, edge, edge, channels), bf16)],
        [
            ((deep // 2, 4 * deep * deep, channels), f32),
            ((edge, edge, edge, channels), bf16),
            pltpu.SemaphoreType.DMA((deep // 2,)),
        ],
        deep_act,
        stats,
        gain_deep.reshape(1, deep_channels),
        offset_deep.reshape(1, deep_channels),
        up_weight,
        out,
        flops=4 * deep_channels * channels * deep**3,
        nbytes=3 << 20,
        out_hbm=True,
    )
    return decoded


def solution(mesh):
    placed = (
        P(("cand", "gz"), "yx", None, None),
        P(),
        P(),
        P(),
        P(None, None, None, None, "yx"),
        P(),
        P(),
        P(),
    )
    return jax.shard_map(
        body,
        mesh=mesh,
        in_specs=placed,
        out_specs=P(("cand", "gz"), "yx", None, None),
        check_vma=False,
    )
```

```python
import functools
import math

import jax
import jax.numpy as jnp
from jax import lax
from jax.experimental import pallas as pl
from jax.experimental.pallas import tpu as pltpu
from jax.sharding import PartitionSpec as P

GROUPS = 32
EPSILON = 1e-05
PART = ("gz", "yx")
VMEM_BYTES = 32 * 1024 * 1024


class Square:
    def __init__(self):
        self.tiles = lax.axis_size("yx")
        self.side = math.isqrt(self.tiles)
        tile = lax.axis_index("yx")
        self.row, self.column = tile // self.side, tile % self.side
        self.folded = self.side == 2
        self.steps = (0,) if self.folded else (-1, 1)

    def low_sides(self):
        if self.folded:
            return [self.row == 1], [self.column == 1]
        return [True, False], [True, False]

    def route(self, down, right):
        pairs = []
        for tile in range(self.tiles):
            row, column = tile // self.side + down, tile % self.side + right
            if 0 <= row < self.side and 0 <= column < self.side:
                pairs.append((tile, row * self.side + column))
        return pairs

    def swap_route(self, mask):
        return [(tile, tile ^ mask) for tile in range(self.tiles)]

    def halos(self, y_edges, x_edges, corners):
        if self.folded:
            y = lax.ppermute(y_edges[0], "yx", self.swap_route(2))
            x = lax.ppermute(x_edges[0], "yx", self.swap_route(1))
            corner = lax.ppermute(corners[0], "yx", self.swap_route(3))
            return [y], [x], [corner]
        y = [lax.ppermute(y_edges[k], "yx", self.route((1, -1)[1 - k], 0)) for k in (1, 0)]
        x = [lax.ppermute(x_edges[k], "yx", self.route(0, (1, -1)[1 - k])) for k in (1, 0)]
        corner = [
            lax.ppermute(corners[2 * k + j], "yx", self.route((1, -1)[1 - k], (1, -1)[1 - j]))
            for k in (1, 0)
            for j in (1, 0)
        ]
        return y, x, corner


def swap_depth(outer, inner):
    size = lax.axis_size("gz")
    routes = [[], []]
    for low in range(size - 1):
        routes[low % 2] += [(low, low + 1), (low + 1, low)]
    return lax.ppermute(outer, "gz", routes[1]), lax.ppermute(inner, "gz", routes[0])


class Riders:
    STEPS = (("cand", 1), ("gz", 2), ("gz", 1))

    def __init__(self, rows):
        self.tiles = 27 * rows // 16
        self.fits = (
            lax.axis_size("yx") == 4
            and lax.axis_size("cand") % 2 == 0
            and lax.axis_size("gz") % 4 == 0
            and self.tiles >= 8
        )
        self.size = -(-self.tiles // 8) if self.fits else 0

    @classmethod
    def mine(cls):
        return sum(
            lax.axis_index(axis) // mask % 2 * 2**k for k, (axis, mask) in enumerate(cls.STEPS)
        )


def rotate_shards(piece):
    tiles = lax.axis_size("yx")
    return [
        lax.ppermute(piece, "yx", [(i, (i + k) % tiles) for i in range(tiles)]) for k in range(1, tiles)
    ]


def swap(block, axis, mask):
    return lax.ppermute(block, axis, [(i, i ^ mask) for i in range(lax.axis_size(axis))])


def share(stats):
    return lax.all_to_all(stats, PART, 0, 0)


def call(kernel, outs, scratch, *arrays, flops=0, nbytes=0, in_hbm=0, out_hbm=False):
    vmem, hbm = (pl.BlockSpec(memory_space=space) for space in (pltpu.VMEM, pltpu.HBM))
    far, near = arrays[:in_hbm], arrays[in_hbm:]
    far = [pltpu.with_memory_space_constraint(array, pltpu.HBM) for array in far]
    return pl.pallas_call(
        kernel,
        out_shape=[jax.ShapeDtypeStruct(shape, dtype) for shape, dtype in outs],
        in_specs=[hbm] * len(far) + [vmem] * len(near),
        out_specs=[hbm if out_hbm else vmem] * len(outs),
        scratch_shapes=[pltpu.VMEM(*entry) if isinstance(entry, tuple) else entry for entry in scratch],
        compiler_params=pltpu.CompilerParams(vmem_limit_bytes=VMEM_BYTES),
        cost_estimate=pl.CostEstimate(flops=flops, bytes_accessed=nbytes, transcendentals=0),
    )(*far, *near)


def start_kernel(ny, size, x_in, w_in, d_in, y_out, rider, x, w, sems):
    edge = x_in.shape[0]
    bf16 = jnp.bfloat16
    above, _ = Square().low_sides()
    chunks = 4
    planes = edge // chunks
    first = [
        pltpu.make_async_copy(
            x_in.at[pl.ds(k * planes, planes)],
            x.at[pl.ds(1 + k * planes, planes), pl.ds(1, edge)],
            sems.at[k],
        )
        for k in range(chunks)
    ]
    later = []
    if size:
        at = jnp.minimum(Riders.mine() * size, d_in.shape[0] - size)
        later.append(pltpu.make_async_copy(d_in.at[pl.ds(at, size)], rider, sems.at[chunks]))
    later.append(pltpu.make_async_copy(w_in, w, sems.at[chunks + 1]))
    for copy in first + later:
        copy.start()
    x[0] = jnp.zeros(x.shape[1:], bf16)
    x[edge + 1] = jnp.zeros(x.shape[1:], bf16)
    blank = jnp.zeros((edge,) + x.shape[2:], bf16)
    x[1 : edge + 1, 0] = blank
    x[1 : edge + 1, edge + 1] = blank
    if not size:
        rider[...] = jnp.zeros(rider.shape, bf16)
    for k in range(chunks):
        first[k].wait()
        at, here = pl.ds(k * planes, planes), pl.ds(1 + k * planes, planes)
        for i in range(ny):
            y_out[i, at] = x[here, jnp.where(above[i], 1, edge)]
    for copy in later:
        copy.wait()
    if size:
        y_out[0, edge : edge + size] = rider[...]


def flank_kernel(ny, nx, size, x, rider, x_out, corners, lines):
    edge = x.shape[2]
    f32, bf16 = jnp.float32, jnp.bfloat16
    above, left = Square().low_sides()
    flat = lines.reshape(nx * edge * edge * 8, 128)
    planes = edge // 4
    part = planes * edge
    for k in range(4):
        at, here = pl.ds(k * planes, planes), pl.ds(1 + k * planes, planes)
        for j in range(nx):
            low = x[here, 1 : edge + 1, 0:8].astype(f32).reshape(part, 8, 128)
            high = x[here, 1 : edge + 1, edge - 8 : edge].astype(f32).reshape(part, 8, 128)
            high = pltpu.roll(high, 1, 1)
            lines[j, k * part : k * part + part] = jnp.where(left[j], low, high)
            begin = (j * edge * edge + k * part) * 8
            column = flat[pl.ds(begin, part, stride=8), :]
            x_out[j, at] = column.astype(bf16).reshape(planes, edge, 128)
    for i in range(ny):
        for j in range(nx):
            begin = j * edge * edge * 8
            low = flat[pl.ds(begin, edge, stride=8 * edge), :]
            high = flat[pl.ds(begin + 8 * (edge - 1), edge, stride=8 * edge), :]
            corners[i * nx + j, 0] = jnp.where(above[i], low, high).astype(bf16)
    if size:
        x_out[0, edge : edge + size] = rider[...]
        corners[0, 1 : 1 + size] = rider[...]


def face_kernel(ny, nx, size, x, y_halos, x_halos, corners, outer, inner, *riders):
    edge = outer.shape[1]
    wide = edge + ny + nx
    odd = lax.axis_index("gz") % 2
    far = edge - 3
    for face, at in ((outer, odd * far), (inner, (1 - odd) * far)):
        for k in range(3):
            row = k * wide
            face[row : row + edge] = x[1 + at + k, 1 : edge + 1]
            for i in range(ny):
                face[row + edge + i] = y_halos[i, at + k]
            for j in range(nx):
                face[row + edge + ny + j] = x_halos[j, at + k]
        for k in range(ny * nx):
            face[3 * wide + k] = corners[k, 0]
    if size:
        riders[0][0] = x_halos[0, edge : edge + size]
        riders[0][1] = y_halos[0, edge : edge + size]
        riders[0][2] = corners[0, 1 : 1 + size]


def spread_taps(weight, taps):
    for tap in range(27):
        row, lane = tap // 3 * 128, tap % 3 * 128
        taps[row : row + 128, lane : lane + 128] = weight[tap]


def pair_taps(weight, pairs):
    for dz in range(3):
        for line in range(4):
            row = (dz * 4 + line) * 128
            for out in range(2):
                lane = out * 128
                if 0 <= line - out < 3:
                    block = weight[dz * 9 + (line - out) * 3 + 2]
                else:
                    block = jnp.zeros((128, 128), pairs.dtype)
                pairs[row : row + 128, lane : lane + 128] = block


def join_x(wide, edge):
    place = lax.broadcasted_iota(jnp.int32, wide.shape[:2] + (128,), 1)
    after = jnp.where(place > 0, pltpu.roll(wide[:, :, :128], 1, 1), 0.0)
    before = jnp.where(place < edge - 1, pltpu.roll(wide[:, :, 256:], edge - 1, 1), 0.0)
    return wide[:, :, 128:256] + after + before


def convolve(grid, count, taps, pairs, put):
    edge = grid.shape[2]
    planes = min(count, 4)
    rows = planes * edge * edge
    place = lax.broadcasted_iota(jnp.int32, (planes * edge, edge, 128), 1)
    halved = grid.reshape(grid.shape[0], edge // 2 + 1, 2, edge, 128)
    for z in range(0, count, planes):
        left = jnp.concatenate(
            [
                grid[z + dz : z + dz + planes, dy : dy + edge].reshape(rows, 128)
                for dz in range(3)
                for dy in range(3)
            ],
            axis=1,
        )
        wide = jnp.dot(left, taps[:, 0:256], preferred_element_type=jnp.float32)
        wide = wide.reshape(planes * edge, edge, 256)
        left = jnp.concatenate(
            [
                halved[z + dz : z + dz + planes, line // 2 : line // 2 + edge // 2, line % 2].reshape(
                    rows // 2, 128
                )
                for dz in range(3)
                for line in range(4)
            ],
            axis=1,
        )
        two = jnp.dot(left, pairs[...], preferred_element_type=jnp.float32)
        two = two.reshape(planes * edge // 2, edge, 256)
        two = jnp.stack([two[:, :, :128], two[:, :, 128:]], axis=1).reshape(planes * edge, edge, 128)
        after = jnp.where(place > 0, pltpu.roll(wide[:, :, :128], 1, 1), 0.0)
        before = jnp.where(place < edge - 1, pltpu.roll(two, edge - 1, 1), 0.0)
        new = wide[:, :, 128:256] + after + before
        put(z, new.reshape(planes, edge, edge, 128))


def conv_kernel(deep_in, x, weight, act, taps, pairs, deep_weight, sem):
    copy = pltpu.make_async_copy(deep_in, deep_weight, sem)
    copy.start()
    edge = act.shape[0]
    spread_taps(weight, taps)
    pair_taps(weight, pairs)

    def put(z, new):
        act[z : z + new.shape[0]] = new

    convolve(x, edge, taps, pairs, put)
    copy.wait()


def y_terms(line, low, taps):
    planes, edge = line.shape[0] - 2, line.shape[1]
    left = jnp.concatenate(
        [line[dz : dz + planes].reshape(planes * edge, 128) for dz in range(3)], axis=1
    )
    start = jnp.where(low, 0, 256)
    right = jnp.concatenate(
        [taps[pl.ds(pl.multiple_of(start + dz * 384, 128), 128), :] for dz in range(3)], axis=0
    )
    wide = jnp.dot(left, right, preferred_element_type=jnp.float32)
    return join_x(wide.reshape(planes, edge, 384), edge)


def x_terms(column, taps):
    planes, edge = column.shape[0] - 2, column.shape[1] - 16
    lines = [column[:, 7 + dy : 7 + dy + edge].astype(jnp.bfloat16) for dy in range(3)]
    left = jnp.concatenate(
        [line[dz : dz + planes].reshape(planes * edge, 128) for dz in range(3) for line in lines],
        axis=1,
    )
    right = jnp.concatenate([taps[:, 0:128], taps[:, 256:384]], axis=1)
    both = jnp.dot(left, right, preferred_element_type=jnp.float32)
    return both[:, :128], both[:, 128:]


def fill_column(column, at, voxels, ends, above):
    count, edge = voxels.shape[:2]
    rows = edge + 16
    lines = column.reshape(column.shape[0] * rows, 128)
    column[at : at + count, 8 : 8 + edge] = voxels.astype(jnp.float32)
    for i, end in enumerate(ends):
        first = last = end.astype(jnp.float32)
        if len(ends) == 1:
            first, last = jnp.where(above[0], first, 0.0), jnp.where(above[0], 0.0, last)
        if len(ends) == 1 or i == 0:
            lines[pl.ds(at * rows + 7, count, stride=rows), :] = first
        if len(ends) == 1 or i == 1:
            lines[pl.ds(at * rows + 8 + edge, count, stride=rows), :] = last


def add_column(act, terms, j, nx, low):
    planes, edge = act.shape[:2]
    flat = act.reshape(planes * edge * edge, 128)
    first, last = terms
    if nx == 1:
        first, last = jnp.where(low, first, 0.0), jnp.where(low, 0.0, last)
    if nx == 1 or j == 0:
        flat[pl.ds(0, planes * edge, stride=edge), :] += first
    if nx == 1 or j == 1:
        flat[pl.ds(edge - 1, planes * edge, stride=edge), :] += last


def moments(planes):
    count, edge = planes.shape[:2]
    zero = jnp.zeros((8, 128), jnp.float32)

    def sum_step(k, carry):
        return carry + jnp.sum(planes[k].reshape(edge * 2, 8, 128), axis=0)

    mean = lax.fori_loop(0, count, sum_step, zero, unroll=True) / (count * edge * edge // 8)

    def spread_step(k, carry):
        off = planes[k].reshape(edge * 2, 8, 128) - mean
        return carry + jnp.sum(off * off, axis=0)

    return mean, lax.fori_loop(0, count, spread_step, zero, unroll=True)


def side_kernel(ny, nx, own, y_halos, x_halos, corners, taps, inner, ends, stats, act, column):
    edge = own.shape[0]
    act[0] = jnp.zeros(act.shape[1:], jnp.float32)
    act[edge + 1] = jnp.zeros(act.shape[1:], jnp.float32)
    act[1 : edge + 1] = own[...]
    above, left = Square().low_sides()
    blank = jnp.zeros((2, edge, 128), jnp.bfloat16)
    for i in range(ny):
        line = jnp.concatenate([blank, y_halos[i, 0:edge], blank], axis=0)
        act[:, jnp.where(above[i], 0, edge - 1)] += y_terms(line, above[i], taps)
    for j in range(nx):
        column[...] = jnp.zeros(column.shape, jnp.float32)
        fill_column(
            column, 2, x_halos[j, 0:edge], [corners[i * nx + j, 0] for i in range(ny)], above
        )
        add_column(act, x_terms(column, taps), j, nx, left[j])
    inner[...] = act[2:edge]
    ends[0:2] = act[0:2]
    ends[2:4] = act[edge : edge + 2]
    mean, spread = moments(act.at[2:edge])
    stats[0:8] = mean
    stats[8:16] = spread


def end_kernel(ny, nx, *refs):
    x, inner_stats, partial, outer_face, inner_face, taps, pairs, act, stats, faces, grid, column = refs
    edge = x.shape[2]
    wide_face = edge + ny + nx
    f32 = jnp.float32
    odd = lax.axis_index("gz") % 2 == 1
    faces[0] = jnp.where(odd, inner_face[...], outer_face[...])
    faces[1] = jnp.where(odd, outer_face[...], inner_face[...])
    above, left = Square().low_sides()
    blank = jnp.zeros(grid.shape[:1] + grid.shape[2:], grid.dtype)
    grid[:, 0] = blank
    grid[:, edge + 1] = blank
    gap = jnp.zeros((2, edge, 128), grid.dtype)
    for side, halo_at, own_at, plane, at, beyond, own, beside, dz in (
        (0, 0, 3, 1, 0, 0, 2, 2, 0),
        (1, 1, 0, edge, 3, 4, 3, 1, 2),
    ):
        for k in range(3):
            begin = k * wide_face
            grid[halo_at + k, 1 : edge + 1] = faces[side, begin : begin + edge]
        grid[own_at, 1 : edge + 1] = x[plane, 1 : edge + 1]

        def put(z, new):
            act[beyond + z : beyond + z + new.shape[0]] = new

        convolve(grid, 2, taps, pairs, put)
        stacked = jnp.concatenate(
            [grid[beside, dy : dy + edge].reshape(edge * edge, 128) for dy in range(3)], axis=1
        )
        wide = jnp.dot(stacked, taps[dz * 384 : dz * 384 + 384, :], preferred_element_type=f32)
        own_part = partial[1 if side == 0 else 2]
        act[own] = own_part + join_x(wide.reshape(edge, edge, 384), edge)
        near = 1 if side == 0 else 4
        act[near] += partial[0 if side == 0 else 3]

        def rim(row):
            planes = [faces[side, k * wide_face + edge + row] for k in range(3)]
            return jnp.stack(planes)

        three = act.at[at : at + 3]
        for i in range(ny):
            line = [rim(i), gap] if side == 0 else [gap, rim(i)]
            three[:, jnp.where(above[i], 0, edge - 1)] += y_terms(
                jnp.concatenate(line, axis=0), above[i], taps
            )
        for j in range(nx):
            column[...] = jnp.zeros(column.shape, f32)
            ends = []
            for i in range(ny):
                tile = faces[side, 3 * wide_face + i * nx + j].astype(f32)
                ends.append(tile[edge - 3 :] if side == 0 else tile[:3])
            fill_column(column, 0 if side == 0 else 2, rim(ny + j), ends, above)
            add_column(three, x_terms(column, taps), j, nx, left[j])

    mean, spread = moments(act.at[2:4])
    few, many = edge * edge // 4, (edge - 2) * edge * edge // 8
    inner_mean, inner_spread = inner_stats[0:8], inner_stats[8:16]
    off = inner_mean - mean
    share_of = few / (few + many)
    spread = spread + inner_spread + (many * share_of) * (off * off)
    put_stats(stats, inner_mean - share_of * off, spread, few + many)


def merge(mean, spread, rows, other_mean, other_spread):
    off = mean - other_mean
    return 0.5 * (mean + other_mean), spread + other_spread + (0.5 * rows) * (off * off)


def put_stats(stats, mean, spread, rows):
    for step in (1, 2, 4):
        others = pltpu.roll(mean, step, 0), pltpu.roll(spread, step, 0)
        mean, spread = merge(mean, spread, float(rows * step), *others)
    both = jnp.concatenate([mean[0:1], spread[0:1]], axis=0)
    stats[...] = jnp.broadcast_to(both[None], stats.shape)


def read_stats(stats, rows):
    devices, _, channels = stats.shape
    shape = (8, channels)
    means = [jnp.broadcast_to(stats[k, 0:1, :], shape) for k in range(devices)]
    spreads = [jnp.broadcast_to(stats[k, 1:2, :], shape) for k in range(devices)]
    mean = functools.reduce(jnp.add, means) / devices
    spread = functools.reduce(jnp.add, spreads)
    spread = spread + rows * functools.reduce(jnp.add, [(m - mean) * (m - mean) for m in means])
    rows = rows * devices
    lane = lax.broadcasted_iota(jnp.int32, shape, 1)
    step = 1
    while step < channels // GROUPS:
        low = jnp.bitwise_and(lane, step) == 0
        others = [
            jnp.where(low, pltpu.roll(row, channels - step, 1), pltpu.roll(row, step, 1))
            for row in (mean, spread)
        ]
        mean, spread = merge(mean, spread, rows, *others)
        rows, step = 2.0 * rows, 2 * step
    return mean, lax.rsqrt(spread / rows + EPSILON)


def silu_of_double(h):
    return h + h * jnp.tanh(h)


def norm_kernel(ny, nx, inner, ends, stats, gain, offset, out, pooled, *refs):
    y_edges, x_edges, corners, half = refs
    depth, edge = inner.shape[0] + 6, inner.shape[1]
    deep, deep_depth = edge // 2, depth // 2
    f32, bf16 = jnp.float32, jnp.bfloat16
    above, left = Square().low_sides()
    depth_at = lax.axis_index("gz")
    mean, scale = read_stats(stats, float(edge**3))
    scale = scale * (0.5 * gain[...])
    shift = 0.5 * offset[...]
    for k in range(deep_depth):
        value = [
            ends[z] if z < 3 else inner[z - 3] if z < depth - 3 else ends[z - depth + 6]
            for z in (2 * k, 2 * k + 1)
        ]
        value = jnp.stack(value).reshape(edge * edge // 4, 8, 128)
        value = silu_of_double((value - mean) * scale + shift)
        value = value.reshape(2, edge, edge, 128).astype(bf16)
        if 0 < k < deep_depth - 1:
            out[2 * k - 2 : 2 * k] = value
        value = value.astype(f32)
        value = (value[0] + value[1]).reshape(deep, 2, edge, 128)
        half[k] = (value[:, 0] + value[:, 1]).reshape(deep * edge, 128)
        lines = half.at[k]
        pair = lines[pl.ds(0, deep * deep, stride=2), :] + lines[pl.ds(1, deep * deep, stride=2), :]
        pair = (pair * 0.125).astype(bf16).astype(f32).reshape(deep, deep, 128)
        if k == 0 or k == deep_depth - 1:
            inside = depth_at > 0 if k == 0 else depth_at < lax.axis_size("gz") - 1
            pair = jnp.where(inside, pair, 0.0)
        pooled[k] = pair
    lines = pooled.reshape(deep_depth * deep * deep, 128)
    rows = deep_depth * deep
    first_x = lines[pl.ds(0, rows, stride=deep), :]
    last_x = lines[pl.ds(deep - 1, rows, stride=deep), :]
    first_y, last_y = (pooled[:, y].reshape(rows, 128) for y in (0, deep - 1))
    ends = []
    for y in (0, deep - 1):
        for x in (0, deep - 1):
            ends.append(lines[pl.ds(y * deep + x, deep_depth, stride=deep * deep), :])
    if ny == 1:
        above, left = above[0], left[0]
        y_edges[0] = jnp.where(above, first_y, last_y).astype(bf16)
        x_edges[0] = jnp.where(left, first_x, last_x).astype(bf16)
        corners[0, 0:deep_depth] = jnp.where(
            above, jnp.where(left, ends[0], ends[1]), jnp.where(left, ends[2], ends[3])
        )
    else:
        y_edges[0], y_edges[1] = first_y.astype(bf16), last_y.astype(bf16)
        x_edges[0], x_edges[1] = first_x.astype(bf16), last_x.astype(bf16)
        for k in range(4):
            corners[k, 0:deep_depth] = ends[k]


def stack_kernel(*refs):
    out = refs[-1]
    for k in range(out.shape[0]):
        out[k] = refs[k][...]


def stack(*arrays):
    vmem = pl.BlockSpec(memory_space=pltpu.VMEM)
    return pl.pallas_call(
        stack_kernel,
        out_shape=jax.ShapeDtypeStruct((len(arrays),) + arrays[0].shape, arrays[0].dtype),
        in_specs=[vmem] * len(arrays),
        out_specs=vmem,
        compiler_params=pltpu.CompilerParams(vmem_limit_bytes=VMEM_BYTES),
    )(*arrays)


def place_weights(own, held, out):
    tile = lax.axis_index("yx")
    out[tile] = own[...]
    if len(held) == 1:
        pieces, others, size = held[0].shape[:3]
        for piece in range(pieces):
            at = jnp.minimum(jnp.bitwise_xor(Riders.mine(), piece) * size, own.shape[0] - size)
            for k in range(others):
                out[jnp.bitwise_xor(tile, k + 1), pl.ds(at, size)] = held[0][piece, k]
    else:
        for k, shard in enumerate(held):
            out[lax.rem(tile + len(held) - k, len(held) + 1)] = shard[...]


def tap_rows(weight, taps):
    per = weight.shape[1] // 27
    return jnp.concatenate(
        [weight[:, pl.ds(tap * per, per)].reshape(-1, 128) for tap in taps], axis=1
    )


def dot_rows(left, right):
    return lax.dot_general(
        left, right, (((1,), (1,)), ((), ())), preferred_element_type=jnp.float32
    )


def deep_kernel(pooled, own, *refs):
    *held, act, weight, grid, packed = refs
    depth, deep = pooled.shape[0], pooled.shape[1]
    place_weights(own, held, weight)
    grid[...] = jnp.zeros(grid.shape, jnp.float32)
    grid[:, 1 : deep + 1, 8:16] = pooled[...]
    for dx in range(3):
        plane = grid[:, :, 7 + dx : 15 + dx]
        for y in range(deep + 1):
            both = jnp.concatenate([plane[:, y], plane[:, y + 1]], axis=1)
            packed[:, y // 2, y % 2, :, dx * 128 : dx * 128 + 128] = both.astype(jnp.bfloat16)
    rows = deep**3
    total = None
    for dz in range(3):
        left = jnp.concatenate(
            [
                packed[dz : dz + deep, dy // 2 : dy // 2 + deep // 2, dy % 2].reshape(rows, 384)
                for dy in range(3)
            ],
            axis=1,
        )
        term = dot_rows(left, tap_rows(weight, range(dz * 9, dz * 9 + 9)))
        total = term if total is None else total + term
    for half in range(act.shape[0]):
        act[half] = total[:, half * 128 : half * 128 + 128]


def deep_rim_kernel(ny, nx, own, y_halos, x_halos, corners, weight, act, stats, line):
    depth, deep = line.shape[0], line.shape[1] - 16
    halves = act.shape[0]
    f32 = jnp.float32
    square = deep * deep
    above, left = Square().low_sides()
    act[...] = own[...]
    flat = line.reshape(depth * line.shape[1], 128)

    def shifts():
        return jnp.concatenate(
            [
                line[dz : dz + deep, 7 + d : 7 + d + deep].reshape(square, 128).astype(jnp.bfloat16)
                for dz in range(3)
                for d in range(3)
            ],
            axis=1,
        )

    for i in range(ny):
        line[...] = jnp.zeros(line.shape, f32)
        line[:, 8 : 8 + deep] = y_halos[i].astype(f32).reshape(depth, deep, 128)
        for j in range(nx):
            end = corners[i * nx + j, 0:depth]
            first, last = jnp.where(left[j], end, 0.0), jnp.where(left[j], 0.0, end)
            if nx == 1 or j == 0:
                flat[pl.ds(7, depth, stride=line.shape[1]), :] = first
            if nx == 1 or j == 1:
                flat[pl.ds(8 + deep, depth, stride=line.shape[1]), :] = last
        tap = jnp.where(above[i], 0, 6)
        taps = [tap + dz * 9 + dx for dz in range(3) for dx in range(3)]
        terms = dot_rows(shifts(), tap_rows(weight, taps))
        for half in range(halves):
            rows = act.at[half].reshape(deep, deep, deep, 128)
            term = terms[:, half * 128 : half * 128 + 128].reshape(deep, deep, 128)
            rows[:, jnp.where(above[i], 0, deep - 1)] += term
    for j in range(nx):
        line[...] = jnp.zeros(line.shape, f32)
        line[:, 8 : 8 + deep] = x_halos[j].astype(f32).reshape(depth, deep, 128)
        tap = jnp.where(left[j], 0, 2)
        taps = [tap + dz * 9 + dy * 3 for dz in range(3) for dy in range(3)]
        terms = dot_rows(shifts(), tap_rows(weight, taps))
        first, last = jnp.where(left[j], terms, 0.0), jnp.where(left[j], 0.0, terms)
        for half in range(halves):
            lanes, rows = slice(half * 128, half * 128 + 128), act.at[half]
            if nx == 1 or j == 0:
                rows[pl.ds(0, square, stride=deep), :] += first[:, lanes]
            if nx == 1 or j == 1:
                rows[pl.ds(deep - 1, square, stride=deep), :] += last[:, lanes]

    rows = deep**3 // 8
    means, spreads = [], []
    for half in range(halves):
        total = act[half].reshape(rows, 8, 128)
        means.append(jnp.sum(total, axis=0) / rows)
        off = total - means[-1]
        spreads.append(jnp.sum(off * off, axis=0))
    put_stats(stats, *(jnp.concatenate(part, axis=1) for part in (means, spreads)), rows)


def final_kernel(act, stats, gain, offset, up, mid, out, wide, held, sems):
    edge = mid.shape[0]
    deep = edge // 2
    f32 = jnp.float32
    mean, scale = read_stats(stats, float(deep**3))
    scale = scale * (0.5 * gain[...])
    shift = 0.5 * offset[...]
    planes = 2
    size = planes * deep * deep
    copies = []
    for k in range(0, deep, planes):
        at = slice(k * deep * deep, k * deep * deep + size)
        value = jnp.concatenate([act[half, at] for half in range(act.shape[0])], axis=1)
        value = value.reshape(size // 8, 8, -1)
        value = silu_of_double((value - mean) * scale + shift)
        value = value.reshape(size, -1).astype(jnp.bfloat16)
        lifted = jnp.dot(value, up[...], preferred_element_type=f32)
        lines = wide.at[k // planes]
        lines[pl.ds(0, size, stride=2), :] = lifted
        lines[pl.ds(1, size, stride=2), :] = lifted
        add = lines[...].reshape(planes, 1, deep, 1, edge, 128)
        at = pl.ds(2 * k, 2 * planes)
        old = mid[at].astype(f32).reshape(planes, 2, deep, 2, edge, 128)
        held[at] = (old + add).astype(jnp.bfloat16).reshape(2 * planes, edge, edge, 128)
        copy = pltpu.make_async_copy(held.at[at], out.at[at], sems.at[k // planes])
        copy.start()
        copies.append(copy)
    for copy in copies:
        copy.wait()


def body(
    features, conv_weight, gain_mid, offset_mid, deep_weight, gain_deep, offset_deep, up_weight
):
    f32, bf16 = jnp.float32, jnp.bfloat16
    edge, channels = features.shape[0], features.shape[3]
    deep = edge // 2
    deep_channels = gain_deep.shape[0]
    square = Square()
    tiles = square.tiles
    devices = lax.axis_size("gz") * tiles
    ny, nx = (len(sides) for sides in square.low_sides())
    riders = Riders(deep_weight.shape[4])

    own = jnp.moveaxis(deep_weight, 4, 3).reshape(-1, 16, channels)
    conv_weight = conv_weight.reshape(27, channels, channels)
    y, rider, field, conv_weight = call(
        functools.partial(start_kernel, ny, riders.size),
        [
            ((ny, edge + riders.size, edge, channels), bf16),
            ((max(riders.size, 1), 16, channels), bf16),
            ((edge + 2, edge + 2, edge, channels), bf16),
            (conv_weight.shape, bf16),
        ],
        [pltpu.SemaphoreType.DMA((6,))],
        features,
        conv_weight,
        own,
        nbytes=5 << 20,
        in_hbm=3,
    )
    x, corner = call(
        functools.partial(flank_kernel, ny, nx, riders.size),
        [
            ((nx, edge + riders.size, edge, channels), bf16),
            ((ny * nx, 1 + riders.size, edge, channels), bf16),
        ],
        [((nx, edge * edge, 8, channels), f32)],
        field,
        rider,
        nbytes=2 << 20,
    )
    edges = y, x, corner
    halos = square.halos(*(list(piece) for piece in edges))
    conv_flops = 54 * channels * channels * edge**3
    act, taps, pairs, own = call(
        conv_kernel,
        [
            ((edge, edge, edge, channels), f32),
            ((9 * channels, 3 * channels), bf16),
            ((12 * channels, 2 * channels), bf16),
            (own.shape, bf16),
        ],
        [pltpu.SemaphoreType.DMA],
        own,
        field,
        conv_weight,
        flops=conv_flops,
        nbytes=6 << 20,
        in_hbm=1,
    )
    (y, x, corner), act = lax.optimization_barrier((halos, act))
    y, x, corner = jnp.stack(y), jnp.stack(x), jnp.stack(corner)
    face = ((3 * (edge + ny + nx) + ny * nx, edge, channels), bf16)
    held = [((3, riders.size, 16, channels), bf16)] if riders.size else []
    outer, inner, *held = call(
        functools.partial(face_kernel, ny, nx, riders.size),
        [face, face] + held,
        [],
        field,
        y,
        x,
        corner,
    )
    outer, inner = swap_depth(outer, inner)
    if riders.size:
        held = held[0][None]
        other = swap(held, *riders.STEPS[0])
        act, other = lax.optimization_barrier((act, other))
        held = stack(held, other).reshape((-1,) + held.shape[1:])
        other = swap(held, *riders.STEPS[1])
    else:
        held = rotate_shards(own)
    six = ((6, edge, edge, channels), f32)
    column = (edge + 16, channels)
    middle, partial, stats = call(
        functools.partial(side_kernel, ny, nx),
        [
            ((edge - 2, edge, edge, channels), f32),
            ((4, edge, edge, channels), f32),
            ((16, channels), f32),
        ],
        [((edge + 2, edge, edge, channels), f32), ((edge + 4,) + column, f32)],
        act,
        y,
        x,
        corner,
        taps,
        flops=conv_flops // 4,
        nbytes=6 << 20,
    )
    ends, stats = call(
        functools.partial(end_kernel, ny, nx),
        [six, ((devices, 2, channels), f32)],
        [
            ((2,) + face[0], bf16),
            ((4, edge + 2, edge, channels), bf16),
            ((5,) + column, f32),
        ],
        field,
        stats,
        partial,
        outer,
        inner,
        taps,
        pairs,
        flops=conv_flops // 2,
        nbytes=3 << 20,
    )
    stats = share(stats)
    if riders.size:
        stats, other = lax.optimization_barrier((stats, other))
        held = stack(held, other).reshape((-1,) + held.shape[1:])
        other = swap(held, *riders.STEPS[2])
        held = [stack(held, other).reshape((-1,) + held.shape[1:])]
    out, pooled, *edges = call(
        functools.partial(norm_kernel, ny, nx),
        [
            ((edge, edge, edge, channels), bf16),
            ((deep + 2, deep, deep, channels), f32),
            ((ny, (deep + 2) * deep, channels), bf16),
            ((nx, (deep + 2) * deep, channels), bf16),
            ((ny * nx, 16, channels), f32),
        ],
        [((deep + 2, deep * edge, channels), f32)],
        middle,
        ends,
        stats,
        gain_mid.reshape(1, channels),
        offset_mid.reshape(1, channels),
        flops=20 * channels * edge**3,
        nbytes=3 << 20,
    )
    y, x, corner = square.halos(*(list(piece) for piece in edges))
    halves = ((deep_channels // 128, deep**3, 128), f32)
    deep_act, weight = call(
        deep_kernel,
        [halves, ((tiles,) + own.shape, bf16)],
        [
            ((deep + 2, deep + 2, 24, channels), f32),
            ((deep + 2, deep // 2 + 1, 2, 16, 3 * channels), bf16),
        ],
        pooled,
        own,
        *held,
        flops=54 * channels * deep_channels * deep**3,
        nbytes=4 << 20,
    )
    deep_act, stats = call(
        functools.partial(deep_rim_kernel, ny, nx),
        [halves, ((devices, 2, deep_channels), f32)],
        [((deep + 2, 24, channels), f32)],
        deep_act,
        jnp.stack(y),
        jnp.stack(x),
        jnp.stack(corner),
        weight,
        flops=4 * channels * deep_channels * deep**3,
        nbytes=3 << 20,
    )
    stats = share(stats)
    (decoded,) = call(
        final_kernel,
        [((edge, edge, edge, channels), bf16)],
        [
            ((deep // 2, 4 * deep * deep, channels), f32),
            ((edge, edge, edge, channels), bf16),
            pltpu.SemaphoreType.DMA((deep // 2,)),
        ],
        deep_act,
        stats,
        gain_deep.reshape(1, deep_channels),
        offset_deep.reshape(1, deep_channels),
        up_weight,
        out,
        flops=4 * deep_channels * channels * deep**3,
        nbytes=3 << 20,
        out_hbm=True,
    )
    return decoded


def solution(mesh):
    placed = (
        P(("cand", "gz"), "yx", None, None),
        P(),
        P(),
        P(),
        P(None, None, None, None, "yx"),
        P(),
        P(),
        P(),
    )
    return jax.shard_map(
        body,
        mesh=mesh,
        in_specs=placed,
        out_specs=P(("cand", "gz"), "yx", None, None),
        check_vma=False,
    )
```

```python
import functools
import math

import jax
import jax.numpy as jnp
from jax import lax
from jax.experimental import pallas as pl
from jax.experimental.pallas import tpu as pltpu
from jax.sharding import PartitionSpec as P

GROUPS = 32
EPSILON = 1e-05
PART = ("gz", "yx")
VMEM_BYTES = 32 * 1024 * 1024


class Square:
    def __init__(self):
        self.tiles = lax.axis_size("yx")
        self.side = math.isqrt(self.tiles)
        tile = lax.axis_index("yx")
        self.row, self.column = tile // self.side, tile % self.side
        self.folded = self.side == 2
        self.steps = (0,) if self.folded else (-1, 1)

    def low_sides(self):
        if self.folded:
            return [self.row == 1], [self.column == 1]
        return [True, False], [True, False]

    def route(self, down, right):
        pairs = []
        for tile in range(self.tiles):
            row, column = tile // self.side + down, tile % self.side + right
            if 0 <= row < self.side and 0 <= column < self.side:
                pairs.append((tile, row * self.side + column))
        return pairs

    def swap_route(self, mask):
        return [(tile, tile ^ mask) for tile in range(self.tiles)]

    def halos(self, y_edges, x_edges, corners):
        if self.folded:
            y = lax.ppermute(y_edges[0], "yx", self.swap_route(2))
            x = lax.ppermute(x_edges[0], "yx", self.swap_route(1))
            corner = lax.ppermute(corners[0], "yx", self.swap_route(3))
            return [y], [x], [corner]
        y = [lax.ppermute(y_edges[k], "yx", self.route((1, -1)[1 - k], 0)) for k in (1, 0)]
        x = [lax.ppermute(x_edges[k], "yx", self.route(0, (1, -1)[1 - k])) for k in (1, 0)]
        corner = [
            lax.ppermute(corners[2 * k + j], "yx", self.route((1, -1)[1 - k], (1, -1)[1 - j]))
            for k in (1, 0)
            for j in (1, 0)
        ]
        return y, x, corner


def swap_depth(outer, inner):
    size = lax.axis_size("gz")
    routes = [[], []]
    for low in range(size - 1):
        routes[low % 2] += [(low, low + 1), (low + 1, low)]
    return lax.ppermute(outer, "gz", routes[1]), lax.ppermute(inner, "gz", routes[0])


class Riders:
    STEPS = (("cand", 1), ("gz", 2), ("gz", 1))

    def __init__(self, rows):
        self.tiles = 27 * rows // 16
        self.fits = (
            lax.axis_size("yx") == 4
            and lax.axis_size("cand") % 2 == 0
            and lax.axis_size("gz") % 4 == 0
            and self.tiles >= 8
        )
        self.size = -(-self.tiles // 8) if self.fits else 0

    @classmethod
    def mine(cls):
        return sum(
            lax.axis_index(axis) // mask % 2 * 2**k for k, (axis, mask) in enumerate(cls.STEPS)
        )


def rotate_shards(piece):
    tiles = lax.axis_size("yx")
    return [
        lax.ppermute(piece, "yx", [(i, (i + k) % tiles) for i in range(tiles)]) for k in range(1, tiles)
    ]


def swap(block, axis, mask):
    return lax.ppermute(block, axis, [(i, i ^ mask) for i in range(lax.axis_size(axis))])


def share(stats):
    return lax.all_to_all(stats, PART, 0, 0)


def call(kernel, outs, scratch, *arrays, flops=0, nbytes=0, in_hbm=0, out_hbm=False):
    vmem, hbm = (pl.BlockSpec(memory_space=space) for space in (pltpu.VMEM, pltpu.HBM))
    far, near = arrays[:in_hbm], arrays[in_hbm:]
    far = [pltpu.with_memory_space_constraint(array, pltpu.HBM) for array in far]
    return pl.pallas_call(
        kernel,
        out_shape=[jax.ShapeDtypeStruct(shape, dtype) for shape, dtype in outs],
        in_specs=[hbm] * len(far) + [vmem] * len(near),
        out_specs=[hbm if out_hbm else vmem] * len(outs),
        scratch_shapes=[pltpu.VMEM(*entry) if isinstance(entry, tuple) else entry for entry in scratch],
        compiler_params=pltpu.CompilerParams(vmem_limit_bytes=VMEM_BYTES),
        cost_estimate=pl.CostEstimate(flops=flops, bytes_accessed=nbytes, transcendentals=0),
    )(*far, *near)


def start_kernel(ny, nx, size, x_in, w_in, d_in, y_out, x_out, corners, x, w, lines, sems):
    edge = x_in.shape[0]
    f32, bf16 = jnp.float32, jnp.bfloat16
    above, left = Square().low_sides()
    chunks = 4
    planes = edge // chunks
    first = [
        pltpu.make_async_copy(
            x_in.at[pl.ds(k * planes, planes)],
            x.at[pl.ds(1 + k * planes, planes), pl.ds(1, edge)],
            sems.at[k],
        )
        for k in range(chunks)
    ]
    later = []
    if size:
        at = jnp.minimum(Riders.mine() * size, d_in.shape[0] - size)
        for k, (out, begin) in enumerate(((y_out, edge), (x_out, edge), (corners, 1))):
            later.append(
                pltpu.make_async_copy(
                    d_in.at[pl.ds(at, size)], out.at[0, pl.ds(begin, size)], sems.at[chunks + k]
                )
            )
    later.append(pltpu.make_async_copy(w_in, w, sems.at[chunks + 3]))
    for copy in first + later:
        copy.start()
    x[0] = jnp.zeros(x.shape[1:], bf16)
    x[edge + 1] = jnp.zeros(x.shape[1:], bf16)
    blank = jnp.zeros((edge,) + x.shape[2:], bf16)
    x[1 : edge + 1, 0] = blank
    x[1 : edge + 1, edge + 1] = blank
    flat = lines.reshape(nx * edge * edge * 8, 128)
    part = planes * edge
    for k in range(chunks):
        first[k].wait()
        at, here = pl.ds(k * planes, planes), pl.ds(1 + k * planes, planes)
        for i in range(ny):
            row = jnp.where(above[i], 1, edge)
            y_out[i, at] = x[here, row]
        for j in range(nx):
            low = x[here, 1 : edge + 1, 0:8].astype(f32).reshape(part, 8, 128)
            high = x[here, 1 : edge + 1, edge - 8 : edge].astype(f32).reshape(part, 8, 128)
            high = pltpu.roll(high, 1, 1)
            kept = jnp.where(left[j], low, high)
            lines[j, k * part : k * part + part] = kept
            begin = (j * edge * edge + k * part) * 8
            column = flat[pl.ds(begin, part, stride=8), :]
            x_out[j, at] = column.astype(bf16).reshape(planes, edge, 128)
    for i in range(ny):
        for j in range(nx):
            begin = j * edge * edge * 8
            low = flat[pl.ds(begin, edge, stride=8 * edge), :]
            high = flat[pl.ds(begin + 8 * (edge - 1), edge, stride=8 * edge), :]
            kept = jnp.where(above[i], low, high)
            corners[i * nx + j, 0] = kept.astype(bf16)
    for copy in later:
        copy.wait()


def face_kernel(ny, nx, size, x, y_halos, x_halos, corners, outer, inner, *riders):
    edge = outer.shape[1]
    wide = edge + ny + nx
    odd = lax.axis_index("gz") % 2
    far = edge - 3
    for face, at in ((outer, odd * far), (inner, (1 - odd) * far)):
        for k in range(3):
            row = k * wide
            face[row : row + edge] = x[1 + at + k, 1 : edge + 1]
            for i in range(ny):
                face[row + edge + i] = y_halos[i, at + k]
            for j in range(nx):
                face[row + edge + ny + j] = x_halos[j, at + k]
        for k in range(ny * nx):
            face[3 * wide + k] = corners[k, 0]
    if size:
        riders[0][0] = x_halos[0, edge : edge + size]
        riders[0][1] = y_halos[0, edge : edge + size]
        riders[0][2] = corners[0, 1 : 1 + size]
        riders[0][3] = corners[0, 1 : 1 + size]


def spread_taps(weight, taps):
    for tap in range(27):
        row, lane = tap // 3 * 128, tap % 3 * 128
        taps[row : row + 128, lane : lane + 128] = weight[tap]


def pair_taps(weight, pairs):
    for dz in range(3):
        for line in range(4):
            row = (dz * 4 + line) * 128
            for out in range(2):
                lane = out * 128
                if 0 <= line - out < 3:
                    block = weight[dz * 9 + (line - out) * 3 + 2]
                else:
                    block = jnp.zeros((128, 128), pairs.dtype)
                pairs[row : row + 128, lane : lane + 128] = block


def join_x(wide, edge):
    place = lax.broadcasted_iota(jnp.int32, wide.shape[:2] + (128,), 1)
    after = jnp.where(place > 0, pltpu.roll(wide[:, :, :128], 1, 1), 0.0)
    before = jnp.where(place < edge - 1, pltpu.roll(wide[:, :, 256:], edge - 1, 1), 0.0)
    return wide[:, :, 128:256] + after + before


def convolve(grid, count, taps, pairs, put):
    edge = grid.shape[2]
    planes = min(count, 4)
    rows = planes * edge * edge
    place = lax.broadcasted_iota(jnp.int32, (planes * edge, edge, 128), 1)
    halved = grid.reshape(grid.shape[0], edge // 2 + 1, 2, edge, 128)
    for z in range(0, count, planes):
        left = jnp.concatenate(
            [
                grid[z + dz : z + dz + planes, dy : dy + edge].reshape(rows, 128)
                for dz in range(3)
                for dy in range(3)
            ],
            axis=1,
        )
        wide = jnp.dot(left, taps[:, 0:256], preferred_element_type=jnp.float32)
        wide = wide.reshape(planes * edge, edge, 256)
        left = jnp.concatenate(
            [
                halved[z + dz : z + dz + planes, line // 2 : line // 2 + edge // 2, line % 2].reshape(
                    rows // 2, 128
                )
                for dz in range(3)
                for line in range(4)
            ],
            axis=1,
        )
        two = jnp.dot(left, pairs[...], preferred_element_type=jnp.float32)
        two = two.reshape(planes * edge // 2, edge, 256)
        two = jnp.stack([two[:, :, :128], two[:, :, 128:]], axis=1).reshape(planes * edge, edge, 128)
        after = jnp.where(place > 0, pltpu.roll(wide[:, :, :128], 1, 1), 0.0)
        before = jnp.where(place < edge - 1, pltpu.roll(two, edge - 1, 1), 0.0)
        new = wide[:, :, 128:256] + after + before
        put(z, new.reshape(planes, edge, edge, 128))


def conv_kernel(deep_in, x, weight, act, taps, pairs, deep_weight, sem):
    copy = pltpu.make_async_copy(deep_in, deep_weight, sem)
    copy.start()
    edge = act.shape[0]
    spread_taps(weight, taps)
    pair_taps(weight, pairs)

    def put(z, new):
        act[z : z + new.shape[0]] = new

    convolve(x, edge, taps, pairs, put)
    copy.wait()


def y_terms(line, low, taps):
    planes, edge = line.shape[0] - 2, line.shape[1]
    left = jnp.concatenate(
        [line[dz : dz + planes].reshape(planes * edge, 128) for dz in range(3)], axis=1
    )
    start = jnp.where(low, 0, 256)
    right = jnp.concatenate(
        [taps[pl.ds(pl.multiple_of(start + dz * 384, 128), 128), :] for dz in range(3)], axis=0
    )
    wide = jnp.dot(left, right, preferred_element_type=jnp.float32)
    return join_x(wide.reshape(planes, edge, 384), edge)


def x_terms(column, taps):
    planes, edge = column.shape[0] - 2, column.shape[1] - 16
    lines = [column[:, 7 + dy : 7 + dy + edge].astype(jnp.bfloat16) for dy in range(3)]
    left = jnp.concatenate(
        [line[dz : dz + planes].reshape(planes * edge, 128) for dz in range(3) for line in lines],
        axis=1,
    )
    right = jnp.concatenate([taps[:, 0:128], taps[:, 256:384]], axis=1)
    both = jnp.dot(left, right, preferred_element_type=jnp.float32)
    return both[:, :128], both[:, 128:]


def fill_column(column, at, voxels, ends, above):
    count, edge = voxels.shape[:2]
    rows = edge + 16
    lines = column.reshape(column.shape[0] * rows, 128)
    column[at : at + count, 8 : 8 + edge] = voxels.astype(jnp.float32)
    for i, end in enumerate(ends):
        first = last = end.astype(jnp.float32)
        if len(ends) == 1:
            first, last = jnp.where(above[0], first, 0.0), jnp.where(above[0], 0.0, last)
        if len(ends) == 1 or i == 0:
            lines[pl.ds(at * rows + 7, count, stride=rows), :] = first
        if len(ends) == 1 or i == 1:
            lines[pl.ds(at * rows + 8 + edge, count, stride=rows), :] = last


def add_column(act, terms, j, nx, low):
    planes, edge = act.shape[:2]
    flat = act.reshape(planes * edge * edge, 128)
    first, last = terms
    if nx == 1:
        first, last = jnp.where(low, first, 0.0), jnp.where(low, 0.0, last)
    if nx == 1 or j == 0:
        flat[pl.ds(0, planes * edge, stride=edge), :] += first
    if nx == 1 or j == 1:
        flat[pl.ds(edge - 1, planes * edge, stride=edge), :] += last


def moments(planes):
    count, edge = planes.shape[:2]
    zero = jnp.zeros((8, 128), jnp.float32)

    def sum_step(k, carry):
        return carry + jnp.sum(planes[k].reshape(edge * 2, 8, 128), axis=0)

    mean = lax.fori_loop(0, count, sum_step, zero, unroll=True) / (count * edge * edge // 8)

    def spread_step(k, carry):
        off = planes[k].reshape(edge * 2, 8, 128) - mean
        return carry + jnp.sum(off * off, axis=0)

    return mean, lax.fori_loop(0, count, spread_step, zero, unroll=True)


def side_kernel(ny, nx, own, y_halos, x_halos, corners, taps, inner, ends, stats, act, column):
    edge = own.shape[0]
    act[0] = jnp.zeros(act.shape[1:], jnp.float32)
    act[edge + 1] = jnp.zeros(act.shape[1:], jnp.float32)
    act[1 : edge + 1] = own[...]
    above, left = Square().low_sides()
    blank = jnp.zeros((2, edge, 128), jnp.bfloat16)
    for i in range(ny):
        line = jnp.concatenate([blank, y_halos[i, 0:edge], blank], axis=0)
        act[:, jnp.where(above[i], 0, edge - 1)] += y_terms(line, above[i], taps)
    for j in range(nx):
        column[...] = jnp.zeros(column.shape, jnp.float32)
        fill_column(
            column, 2, x_halos[j, 0:edge], [corners[i * nx + j, 0] for i in range(ny)], above
        )
        add_column(act, x_terms(column, taps), j, nx, left[j])
    inner[...] = act[2:edge]
    ends[0:2] = act[0:2]
    ends[2:4] = act[edge : edge + 2]
    mean, spread = moments(act.at[2:edge])
    stats[0:8] = mean
    stats[8:16] = spread


def end_kernel(ny, nx, *refs):
    x, inner_stats, partial, outer_face, inner_face, taps, pairs, act, stats, faces, grid, column = refs
    edge = x.shape[2]
    wide_face = edge + ny + nx
    f32 = jnp.float32
    odd = lax.axis_index("gz") % 2 == 1
    faces[0] = jnp.where(odd, inner_face[...], outer_face[...])
    faces[1] = jnp.where(odd, outer_face[...], inner_face[...])
    above, left = Square().low_sides()
    blank = jnp.zeros(grid.shape[:1] + grid.shape[2:], grid.dtype)
    grid[:, 0] = blank
    grid[:, edge + 1] = blank
    gap = jnp.zeros((2, edge, 128), grid.dtype)
    for side, halo_at, own_at, plane, at, beyond, own, beside, dz in (
        (0, 0, 3, 1, 0, 0, 2, 2, 0),
        (1, 1, 0, edge, 3, 4, 3, 1, 2),
    ):
        for k in range(3):
            begin = k * wide_face
            grid[halo_at + k, 1 : edge + 1] = faces[side, begin : begin + edge]
        grid[own_at, 1 : edge + 1] = x[plane, 1 : edge + 1]

        def put(z, new):
            act[beyond + z : beyond + z + new.shape[0]] = new

        convolve(grid, 2, taps, pairs, put)
        stacked = jnp.concatenate(
            [grid[beside, dy : dy + edge].reshape(edge * edge, 128) for dy in range(3)], axis=1
        )
        wide = jnp.dot(stacked, taps[dz * 384 : dz * 384 + 384, :], preferred_element_type=f32)
        own_part = partial[1 if side == 0 else 2]
        act[own] = own_part + join_x(wide.reshape(edge, edge, 384), edge)
        near = 1 if side == 0 else 4
        act[near] += partial[0 if side == 0 else 3]

        def rim(row):
            planes = [faces[side, k * wide_face + edge + row] for k in range(3)]
            return jnp.stack(planes)

        three = act.at[at : at + 3]
        for i in range(ny):
            line = [rim(i), gap] if side == 0 else [gap, rim(i)]
            three[:, jnp.where(above[i], 0, edge - 1)] += y_terms(
                jnp.concatenate(line, axis=0), above[i], taps
            )
        for j in range(nx):
            column[...] = jnp.zeros(column.shape, f32)
            ends = []
            for i in range(ny):
                tile = faces[side, 3 * wide_face + i * nx + j].astype(f32)
                ends.append(tile[edge - 3 :] if side == 0 else tile[:3])
            fill_column(column, 0 if side == 0 else 2, rim(ny + j), ends, above)
            add_column(three, x_terms(column, taps), j, nx, left[j])

    mean, spread = moments(act.at[2:4])
    few, many = edge * edge // 4, (edge - 2) * edge * edge // 8
    inner_mean, inner_spread = inner_stats[0:8], inner_stats[8:16]
    off = inner_mean - mean
    share_of = few / (few + many)
    spread = spread + inner_spread + (many * share_of) * (off * off)
    put_stats(stats, inner_mean - share_of * off, spread, few + many)


def merge(mean, spread, rows, other_mean, other_spread):
    off = mean - other_mean
    return 0.5 * (mean + other_mean), spread + other_spread + (0.5 * rows) * (off * off)


def put_stats(stats, mean, spread, rows):
    for step in (1, 2, 4):
        others = pltpu.roll(mean, step, 0), pltpu.roll(spread, step, 0)
        mean, spread = merge(mean, spread, float(rows * step), *others)
    both = jnp.concatenate([mean[0:1], spread[0:1]], axis=0)
    stats[...] = jnp.broadcast_to(both[None], stats.shape)


def read_stats(stats, rows):
    devices, _, channels = stats.shape
    shape = (8, channels)
    means = [jnp.broadcast_to(stats[k, 0:1, :], shape) for k in range(devices)]
    spreads = [jnp.broadcast_to(stats[k, 1:2, :], shape) for k in range(devices)]
    mean = functools.reduce(jnp.add, means) / devices
    spread = functools.reduce(jnp.add, spreads)
    spread = spread + rows * functools.reduce(jnp.add, [(m - mean) * (m - mean) for m in means])
    rows = rows * devices
    lane = lax.broadcasted_iota(jnp.int32, shape, 1)
    step = 1
    while step < channels // GROUPS:
        low = jnp.bitwise_and(lane, step) == 0
        others = [
            jnp.where(low, pltpu.roll(row, channels - step, 1), pltpu.roll(row, step, 1))
            for row in (mean, spread)
        ]
        mean, spread = merge(mean, spread, rows, *others)
        rows, step = 2.0 * rows, 2 * step
    return mean, lax.rsqrt(spread / rows + EPSILON)


def silu_of_double(h):
    return h + h * jnp.tanh(h)


def norm_kernel(ny, nx, inner, ends, stats, gain, offset, out, pooled, *refs):
    y_edges, x_edges, corners, half = refs
    depth, edge = inner.shape[0] + 6, inner.shape[1]
    deep, deep_depth = edge // 2, depth // 2
    f32, bf16 = jnp.float32, jnp.bfloat16
    above, left = Square().low_sides()
    depth_at = lax.axis_index("gz")
    mean, scale = read_stats(stats, float(edge**3))
    scale = scale * (0.5 * gain[...])
    shift = 0.5 * offset[...]
    for k in range(deep_depth):
        value = [
            ends[z] if z < 3 else inner[z - 3] if z < depth - 3 else ends[z - depth + 6]
            for z in (2 * k, 2 * k + 1)
        ]
        value = jnp.stack(value).reshape(edge * edge // 4, 8, 128)
        value = silu_of_double((value - mean) * scale + shift)
        value = value.reshape(2, edge, edge, 128).astype(bf16)
        if 0 < k < deep_depth - 1:
            out[2 * k - 2 : 2 * k] = value
        value = value.astype(f32)
        value = (value[0] + value[1]).reshape(deep, 2, edge, 128)
        half[k] = (value[:, 0] + value[:, 1]).reshape(deep * edge, 128)
        lines = half.at[k]
        pair = lines[pl.ds(0, deep * deep, stride=2), :] + lines[pl.ds(1, deep * deep, stride=2), :]
        pair = (pair * 0.125).astype(bf16).astype(f32).reshape(deep, deep, 128)
        if k == 0 or k == deep_depth - 1:
            inside = depth_at > 0 if k == 0 else depth_at < lax.axis_size("gz") - 1
            pair = jnp.where(inside, pair, 0.0)
        pooled[k] = pair
    lines = pooled.reshape(deep_depth * deep * deep, 128)
    rows = deep_depth * deep
    first_x = lines[pl.ds(0, rows, stride=deep), :]
    last_x = lines[pl.ds(deep - 1, rows, stride=deep), :]
    first_y, last_y = (pooled[:, y].reshape(rows, 128) for y in (0, deep - 1))
    ends = []
    for y in (0, deep - 1):
        for x in (0, deep - 1):
            ends.append(lines[pl.ds(y * deep + x, deep_depth, stride=deep * deep), :])
    if ny == 1:
        above, left = above[0], left[0]
        y_edges[0] = jnp.where(above, first_y, last_y).astype(bf16)
        x_edges[0] = jnp.where(left, first_x, last_x).astype(bf16)
        corners[0, 0:deep_depth] = jnp.where(
            above, jnp.where(left, ends[0], ends[1]), jnp.where(left, ends[2], ends[3])
        )
    else:
        y_edges[0], y_edges[1] = first_y.astype(bf16), last_y.astype(bf16)
        x_edges[0], x_edges[1] = first_x.astype(bf16), last_x.astype(bf16)
        for k in range(4):
            corners[k, 0:deep_depth] = ends[k]


def stack_kernel(*refs):
    out = refs[-1]
    for k in range(out.shape[0]):
        out[k] = refs[k][: out.shape[1], : out.shape[2]]


def stack(*arrays, part=None):
    vmem = pl.BlockSpec(memory_space=pltpu.VMEM)
    shape = (part or arrays[0].shape[:2]) + arrays[0].shape[2:]
    return pl.pallas_call(
        stack_kernel,
        out_shape=jax.ShapeDtypeStruct((len(arrays),) + shape, arrays[0].dtype),
        in_specs=[vmem] * len(arrays),
        out_specs=vmem,
        compiler_params=pltpu.CompilerParams(vmem_limit_bytes=VMEM_BYTES),
    )(*arrays)


def place_weights(own, held, out):
    tile = lax.axis_index("yx")
    out[tile] = own[...]
    if len(held) == 1:
        pieces, others, size = held[0].shape[:3]
        for piece in range(pieces):
            at = jnp.minimum(jnp.bitwise_xor(Riders.mine(), piece) * size, own.shape[0] - size)
            for k in range(others):
                out[jnp.bitwise_xor(tile, k + 1), pl.ds(at, size)] = held[0][piece, k]
    else:
        for k, shard in enumerate(held):
            out[lax.rem(tile + len(held) - k, len(held) + 1)] = shard[...]


def tap_rows(weight, taps):
    per = weight.shape[1] // 27
    return jnp.concatenate(
        [weight[:, pl.ds(tap * per, per)].reshape(-1, 128) for tap in taps], axis=1
    )


def dot_rows(left, right):
    return lax.dot_general(
        left, right, (((1,), (1,)), ((), ())), preferred_element_type=jnp.float32
    )


def deep_kernel(pooled, own, *refs):
    *held, act, weight, grid, packed = refs
    depth, deep = pooled.shape[0], pooled.shape[1]
    place_weights(own, held, weight)
    grid[...] = jnp.zeros(grid.shape, jnp.float32)
    grid[:, 1 : deep + 1, 8:16] = pooled[...]
    for dx in range(3):
        plane = grid[:, :, 7 + dx : 15 + dx]
        for y in range(deep + 1):
            both = jnp.concatenate([plane[:, y], plane[:, y + 1]], axis=1)
            packed[:, y // 2, y % 2, :, dx * 128 : dx * 128 + 128] = both.astype(jnp.bfloat16)
    rows = deep**3
    total = None
    for dz in range(3):
        left = jnp.concatenate(
            [
                packed[dz : dz + deep, dy // 2 : dy // 2 + deep // 2, dy % 2].reshape(rows, 384)
                for dy in range(3)
            ],
            axis=1,
        )
        term = dot_rows(left, tap_rows(weight, range(dz * 9, dz * 9 + 9)))
        total = term if total is None else total + term
    for half in range(act.shape[0]):
        act[half] = total[:, half * 128 : half * 128 + 128]


def deep_rim_kernel(ny, nx, own, y_halos, x_halos, corners, weight, act, stats, line):
    depth, deep = line.shape[0], line.shape[1] - 16
    halves = act.shape[0]
    f32 = jnp.float32
    square = deep * deep
    above, left = Square().low_sides()
    act[...] = own[...]
    flat = line.reshape(depth * line.shape[1], 128)

    def shifts():
        return jnp.concatenate(
            [
                line[dz : dz + deep, 7 + d : 7 + d + deep].reshape(square, 128).astype(jnp.bfloat16)
                for dz in range(3)
                for d in range(3)
            ],
            axis=1,
        )

    for i in range(ny):
        line[...] = jnp.zeros(line.shape, f32)
        line[:, 8 : 8 + deep] = y_halos[i].astype(f32).reshape(depth, deep, 128)
        for j in range(nx):
            end = corners[i * nx + j, 0:depth]
            first, last = jnp.where(left[j], end, 0.0), jnp.where(left[j], 0.0, end)
            if nx == 1 or j == 0:
                flat[pl.ds(7, depth, stride=line.shape[1]), :] = first
            if nx == 1 or j == 1:
                flat[pl.ds(8 + deep, depth, stride=line.shape[1]), :] = last
        tap = jnp.where(above[i], 0, 6)
        taps = [tap + dz * 9 + dx for dz in range(3) for dx in range(3)]
        terms = dot_rows(shifts(), tap_rows(weight, taps))
        for half in range(halves):
            rows = act.at[half].reshape(deep, deep, deep, 128)
            term = terms[:, half * 128 : half * 128 + 128].reshape(deep, deep, 128)
            rows[:, jnp.where(above[i], 0, deep - 1)] += term
    for j in range(nx):
        line[...] = jnp.zeros(line.shape, f32)
        line[:, 8 : 8 + deep] = x_halos[j].astype(f32).reshape(depth, deep, 128)
        tap = jnp.where(left[j], 0, 2)
        taps = [tap + dz * 9 + dy * 3 for dz in range(3) for dy in range(3)]
        terms = dot_rows(shifts(), tap_rows(weight, taps))
        first, last = jnp.where(left[j], terms, 0.0), jnp.where(left[j], 0.0, terms)
        for half in range(halves):
            lanes, rows = slice(half * 128, half * 128 + 128), act.at[half]
            if nx == 1 or j == 0:
                rows[pl.ds(0, square, stride=deep), :] += first[:, lanes]
            if nx == 1 or j == 1:
                rows[pl.ds(deep - 1, square, stride=deep), :] += last[:, lanes]

    rows = deep**3 // 8
    means, spreads = [], []
    for half in range(halves):
        total = act[half].reshape(rows, 8, 128)
        means.append(jnp.sum(total, axis=0) / rows)
        off = total - means[-1]
        spreads.append(jnp.sum(off * off, axis=0))
    put_stats(stats, *(jnp.concatenate(part, axis=1) for part in (means, spreads)), rows)


def final_kernel(act, stats, gain, offset, up, mid, out, wide, held, sems):
    edge = mid.shape[0]
    deep = edge // 2
    f32 = jnp.float32
    mean, scale = read_stats(stats, float(deep**3))
    scale = scale * (0.5 * gain[...])
    shift = 0.5 * offset[...]
    planes = 2
    size = planes * deep * deep
    copies = []
    for k in range(0, deep, planes):
        at = slice(k * deep * deep, k * deep * deep + size)
        value = jnp.concatenate([act[half, at] for half in range(act.shape[0])], axis=1)
        value = value.reshape(size // 8, 8, -1)
        value = silu_of_double((value - mean) * scale + shift)
        value = value.reshape(size, -1).astype(jnp.bfloat16)
        lifted = jnp.dot(value, up[...], preferred_element_type=f32)
        lines = wide.at[k // planes]
        lines[pl.ds(0, size, stride=2), :] = lifted
        lines[pl.ds(1, size, stride=2), :] = lifted
        add = lines[...].reshape(planes, 1, deep, 1, edge, 128)
        at = pl.ds(2 * k, 2 * planes)
        old = mid[at].astype(f32).reshape(planes, 2, deep, 2, edge, 128)
        held[at] = (old + add).astype(jnp.bfloat16).reshape(2 * planes, edge, edge, 128)
        copy = pltpu.make_async_copy(held.at[at], out.at[at], sems.at[k // planes])
        copy.start()
        copies.append(copy)
    for copy in copies:
        copy.wait()


def body(
    features, conv_weight, gain_mid, offset_mid, deep_weight, gain_deep, offset_deep, up_weight
):
    f32, bf16 = jnp.float32, jnp.bfloat16
    edge, channels = features.shape[0], features.shape[3]
    deep = edge // 2
    deep_channels = gain_deep.shape[0]
    square = Square()
    tiles = square.tiles
    devices = lax.axis_size("gz") * tiles
    ny, nx = (len(sides) for sides in square.low_sides())
    riders = Riders(deep_weight.shape[4])

    own = jnp.moveaxis(deep_weight, 4, 3).reshape(-1, 16, channels)
    conv_weight = conv_weight.reshape(27, channels, channels)
    *edges, field, conv_weight = call(
        functools.partial(start_kernel, ny, nx, riders.size),
        [
            ((ny, edge + riders.size, edge, channels), bf16),
            ((nx, edge + riders.size, edge, channels), bf16),
            ((ny * nx, 1 + riders.size, edge, channels), bf16),
            ((edge + 2, edge + 2, edge, channels), bf16),
            (conv_weight.shape, bf16),
        ],
        [((nx, edge * edge, 8, channels), f32), pltpu.SemaphoreType.DMA((8,))],
        features,
        conv_weight,
        own,
        nbytes=5 << 20,
        in_hbm=3,
    )
    halos = square.halos(*(list(piece) for piece in edges))
    conv_flops = 54 * channels * channels * edge**3
    act, taps, pairs, own = call(
        conv_kernel,
        [
            ((edge, edge, edge, channels), f32),
            ((9 * channels, 3 * channels), bf16),
            ((12 * channels, 2 * channels), bf16),
            (own.shape, bf16),
        ],
        [pltpu.SemaphoreType.DMA],
        own,
        field,
        conv_weight,
        flops=conv_flops,
        nbytes=6 << 20,
        in_hbm=1,
    )
    (y, x, corner), act = lax.optimization_barrier((halos, act))
    y, x, corner = jnp.stack(y), jnp.stack(x), jnp.stack(corner)
    face = ((3 * (edge + ny + nx) + ny * nx, edge, channels), bf16)
    held = [((4, riders.size, 16, channels), bf16)] if riders.size else []
    outer, inner, *held = call(
        functools.partial(face_kernel, ny, nx, riders.size),
        [face, face] + held,
        [],
        field,
        y,
        x,
        corner,
    )
    outer, inner = swap_depth(outer, inner)
    if riders.size:
        held = held[0][None]
        other = swap(held, *riders.STEPS[0])
    else:
        held = rotate_shards(own)
    six = ((6, edge, edge, channels), f32)
    column = (edge + 16, channels)
    middle, partial, stats = call(
        functools.partial(side_kernel, ny, nx),
        [
            ((edge - 2, edge, edge, channels), f32),
            ((4, edge, edge, channels), f32),
            ((16, channels), f32),
        ],
        [((edge + 2, edge, edge, channels), f32), ((edge + 4,) + column, f32)],
        act,
        y,
        x,
        corner,
        taps,
    )
    ends, stats = call(
        functools.partial(end_kernel, ny, nx),
        [six, ((devices, 2, channels), f32)],
        [
            ((2,) + face[0], bf16),
            ((4, edge + 2, edge, channels), bf16),
            ((5,) + column, f32),
        ],
        field,
        stats,
        partial,
        outer,
        inner,
        taps,
        pairs,
    )
    if riders.size:
        stats, other = lax.optimization_barrier((stats, other))
        held = stack(held, other, part=(1, 3)).reshape((2, 3) + held.shape[2:])
        other = swap(held, *riders.STEPS[1])
        stats = share(stats)
        stats, other = lax.optimization_barrier((stats, other))
        held = stack(held, other).reshape((-1,) + held.shape[1:])
        other = swap(held, *riders.STEPS[2])
        held = [stack(held, other).reshape((-1,) + held.shape[1:])]
    else:
        stats = share(stats)
    out, pooled, *edges = call(
        functools.partial(norm_kernel, ny, nx),
        [
            ((edge, edge, edge, channels), bf16),
            ((deep + 2, deep, deep, channels), f32),
            ((ny, (deep + 2) * deep, channels), bf16),
            ((nx, (deep + 2) * deep, channels), bf16),
            ((ny * nx, 16, channels), f32),
        ],
        [((deep + 2, deep * edge, channels), f32)],
        middle,
        ends,
        stats,
        gain_mid.reshape(1, channels),
        offset_mid.reshape(1, channels),
        flops=20 * channels * edge**3,
        nbytes=3 << 20,
    )
    y, x, corner = square.halos(*(list(piece) for piece in edges))
    halves = ((deep_channels // 128, deep**3, 128), f32)
    deep_act, weight = call(
        deep_kernel,
        [halves, ((tiles,) + own.shape, bf16)],
        [
            ((deep + 2, deep + 2, 24, channels), f32),
            ((deep + 2, deep // 2 + 1, 2, 16, 3 * channels), bf16),
        ],
        pooled,
        own,
        *held,
        flops=54 * channels * deep_channels * deep**3,
        nbytes=4 << 20,
    )
    deep_act, stats = call(
        functools.partial(deep_rim_kernel, ny, nx),
        [halves, ((devices, 2, deep_channels), f32)],
        [((deep + 2, 24, channels), f32)],
        deep_act,
        jnp.stack(y),
        jnp.stack(x),
        jnp.stack(corner),
        weight,
        flops=4 * channels * deep_channels * deep**3,
        nbytes=3 << 20,
    )
    stats = share(stats)
    (decoded,) = call(
        final_kernel,
        [((edge, edge, edge, channels), bf16)],
        [
            ((deep // 2, 4 * deep * deep, channels), f32),
            ((edge, edge, edge, channels), bf16),
            pltpu.SemaphoreType.DMA((deep // 2,)),
        ],
        deep_act,
        stats,
        gain_deep.reshape(1, deep_channels),
        offset_deep.reshape(1, deep_channels),
        up_weight,
        out,
        flops=4 * deep_channels * channels * deep**3,
        nbytes=3 << 20,
        out_hbm=True,
    )
    return decoded


def solution(mesh):
    placed = (
        P(("cand", "gz"), "yx", None, None),
        P(),
        P(),
        P(),
        P(None, None, None, None, "yx"),
        P(),
        P(),
        P(),
    )
    return jax.shard_map(
        body,
        mesh=mesh,
        in_specs=placed,
        out_specs=P(("cand", "gz"), "yx", None, None),
        check_vma=False,
    )
```

```python
import functools
import math

import jax
import jax.numpy as jnp
from jax import lax
from jax.experimental import pallas as pl
from jax.experimental.pallas import tpu as pltpu
from jax.sharding import PartitionSpec as P

GROUPS = 32
EPSILON = 1e-05
PART = ("gz", "yx")
VMEM_BYTES = 32 * 1024 * 1024


class Square:
    def __init__(self):
        self.tiles = lax.axis_size("yx")
        self.side = math.isqrt(self.tiles)
        tile = lax.axis_index("yx")
        self.row, self.column = tile // self.side, tile % self.side
        self.folded = self.side == 2
        self.steps = (0,) if self.folded else (-1, 1)

    def low_sides(self):
        if self.folded:
            return [self.row == 1], [self.column == 1]
        return [True, False], [True, False]

    def route(self, down, right):
        pairs = []
        for tile in range(self.tiles):
            row, column = tile // self.side + down, tile % self.side + right
            if 0 <= row < self.side and 0 <= column < self.side:
                pairs.append((tile, row * self.side + column))
        return pairs

    def swap_route(self, mask):
        return [(tile, tile ^ mask) for tile in range(self.tiles)]

    def halos(self, y_edges, x_edges, corners):
        if self.folded:
            y = lax.ppermute(y_edges[0], "yx", self.swap_route(2))
            x = lax.ppermute(x_edges[0], "yx", self.swap_route(1))
            corner = lax.ppermute(corners[0], "yx", self.swap_route(3))
            return [y], [x], [corner]
        y = [lax.ppermute(y_edges[k], "yx", self.route((1, -1)[1 - k], 0)) for k in (1, 0)]
        x = [lax.ppermute(x_edges[k], "yx", self.route(0, (1, -1)[1 - k])) for k in (1, 0)]
        corner = [
            lax.ppermute(corners[2 * k + j], "yx", self.route((1, -1)[1 - k], (1, -1)[1 - j]))
            for k in (1, 0)
            for j in (1, 0)
        ]
        return y, x, corner


def swap_depth(outer, inner):
    size = lax.axis_size("gz")
    routes = [[], []]
    for low in range(size - 1):
        routes[low % 2] += [(low, low + 1), (low + 1, low)]
    return lax.ppermute(outer, "gz", routes[1]), lax.ppermute(inner, "gz", routes[0])


class Riders:
    STEPS = (("cand", 1), ("gz", 2), ("gz", 1))

    def __init__(self, rows):
        self.tiles = 27 * rows // 16
        self.fits = (
            lax.axis_size("yx") == 4
            and lax.axis_size("cand") % 2 == 0
            and lax.axis_size("gz") % 4 == 0
            and self.tiles >= 8
        )
        self.size = -(-self.tiles // 8) if self.fits else 0

    @classmethod
    def mine(cls):
        return sum(
            lax.axis_index(axis) // mask % 2 * 2**k for k, (axis, mask) in enumerate(cls.STEPS)
        )


def rotate_shards(piece):
    tiles = lax.axis_size("yx")
    return [
        lax.ppermute(piece, "yx", [(i, (i + k) % tiles) for i in range(tiles)]) for k in range(1, tiles)
    ]


def swap(block, axis, mask):
    return lax.ppermute(block, axis, [(i, i ^ mask) for i in range(lax.axis_size(axis))])


def share(stats):
    return lax.all_to_all(stats, PART, 0, 0)


def call(kernel, outs, scratch, *arrays, flops=0, nbytes=0, in_hbm=0, out_hbm=False):
    vmem, hbm = (pl.BlockSpec(memory_space=space) for space in (pltpu.VMEM, pltpu.HBM))
    far, near = arrays[:in_hbm], arrays[in_hbm:]
    far = [pltpu.with_memory_space_constraint(array, pltpu.HBM) for array in far]
    return pl.pallas_call(
        kernel,
        out_shape=[jax.ShapeDtypeStruct(shape, dtype) for shape, dtype in outs],
        in_specs=[hbm] * len(far) + [vmem] * len(near),
        out_specs=[hbm if out_hbm else vmem] * len(outs),
        scratch_shapes=[pltpu.VMEM(*entry) if isinstance(entry, tuple) else entry for entry in scratch],
        compiler_params=pltpu.CompilerParams(vmem_limit_bytes=VMEM_BYTES),
        cost_estimate=pl.CostEstimate(flops=flops, bytes_accessed=nbytes, transcendentals=0),
    )(*far, *near)


def start_kernel(ny, nx, size, x_in, w_in, d_in, y_out, x_out, corners, outer, inner, x, w, lines, sems):
    edge = x_in.shape[0]
    f32, bf16 = jnp.float32, jnp.bfloat16
    above, left = Square().low_sides()
    chunks = 4
    planes = edge // chunks
    first = [
        pltpu.make_async_copy(
            x_in.at[pl.ds(k * planes, planes)],
            x.at[pl.ds(1 + k * planes, planes), pl.ds(1, edge)],
            sems.at[k],
        )
        for k in range(chunks)
    ]
    later = []
    if size:
        at = jnp.minimum(Riders.mine() * size, d_in.shape[0] - size)
        for k, (out, begin) in enumerate(((y_out, edge), (x_out, edge), (corners, 1))):
            later.append(
                pltpu.make_async_copy(
                    d_in.at[pl.ds(at, size)], out.at[0, pl.ds(begin, size)], sems.at[chunks + k]
                )
            )
    later.append(pltpu.make_async_copy(w_in, w, sems.at[chunks + 3]))
    for copy in first + later:
        copy.start()
    x[0] = jnp.zeros(x.shape[1:], bf16)
    x[edge + 1] = jnp.zeros(x.shape[1:], bf16)
    blank = jnp.zeros((edge,) + x.shape[2:], bf16)
    x[1 : edge + 1, 0] = blank
    x[1 : edge + 1, edge + 1] = blank
    flat = lines.reshape(nx * edge * edge * 8, 128)
    part = planes * edge
    for k in range(chunks):
        first[k].wait()
        at, here = pl.ds(k * planes, planes), pl.ds(1 + k * planes, planes)
        for i in range(ny):
            row = jnp.where(above[i], 1, edge)
            y_out[i, at] = x[here, row]
        for j in range(nx):
            low = x[here, 1 : edge + 1, 0:8].astype(f32).reshape(part, 8, 128)
            high = x[here, 1 : edge + 1, edge - 8 : edge].astype(f32).reshape(part, 8, 128)
            high = pltpu.roll(high, 1, 1)
            kept = jnp.where(left[j], low, high)
            lines[j, k * part : k * part + part] = kept
            begin = (j * edge * edge + k * part) * 8
            column = flat[pl.ds(begin, part, stride=8), :]
            x_out[j, at] = column.astype(bf16).reshape(planes, edge, 128)
    for i in range(ny):
        for j in range(nx):
            begin = j * edge * edge * 8
            low = flat[pl.ds(begin, edge, stride=8 * edge), :]
            high = flat[pl.ds(begin + 8 * (edge - 1), edge, stride=8 * edge), :]
            kept = jnp.where(above[i], low, high)
            corners[i * nx + j, 0] = kept.astype(bf16)
    odd, far = lax.axis_index("gz") % 2, edge - 3
    for face, at in ((outer, odd * far), (inner, (1 - odd) * far)):
        for k in range(3):
            face[k] = x[1 + at + k, 1 : edge + 1]
    for copy in later:
        copy.wait()


def turn_kernel(ny, nx, size, y_halos, x_halos, corners, outer, inner, *riders):
    edge = outer.shape[1]
    wide = ny + nx
    odd, far = lax.axis_index("gz") % 2, edge - 3
    for face, at in ((outer, odd * far), (inner, (1 - odd) * far)):
        for k in range(3):
            row = k * wide
            for i in range(ny):
                face[row + i] = y_halos[i, at + k]
            for j in range(nx):
                face[row + ny + j] = x_halos[j, at + k]
        for k in range(ny * nx):
            face[3 * wide + k] = corners[k, 0]
    if size:
        riders[0][0] = x_halos[0, edge : edge + size]
        riders[0][1] = y_halos[0, edge : edge + size]
        riders[0][2] = corners[0, 1 : 1 + size]


def in_order(odd, outer, inner):
    return jnp.where(odd, inner, outer), jnp.where(odd, outer, inner)


def spread_taps(weight, taps):
    for tap in range(27):
        row, lane = tap // 3 * 128, tap % 3 * 128
        taps[row : row + 128, lane : lane + 128] = weight[tap]


def pair_taps(weight, pairs):
    for dz in range(3):
        for line in range(4):
            row = (dz * 4 + line) * 128
            for out in range(2):
                lane = out * 128
                if 0 <= line - out < 3:
                    block = weight[dz * 9 + (line - out) * 3 + 2]
                else:
                    block = jnp.zeros((128, 128), pairs.dtype)
                pairs[row : row + 128, lane : lane + 128] = block


def join_x(wide, edge):
    place = lax.broadcasted_iota(jnp.int32, wide.shape[:2] + (128,), 1)
    after = jnp.where(place > 0, pltpu.roll(wide[:, :, :128], 1, 1), 0.0)
    before = jnp.where(place < edge - 1, pltpu.roll(wide[:, :, 256:], edge - 1, 1), 0.0)
    return wide[:, :, 128:256] + after + before


def convolve(grid, count, taps, pairs, put):
    edge = grid.shape[2]
    planes = min(count, 4)
    rows = planes * edge * edge
    place = lax.broadcasted_iota(jnp.int32, (planes * edge, edge, 128), 1)
    halved = grid.reshape(grid.shape[0], edge // 2 + 1, 2, edge, 128)
    for z in range(0, count, planes):
        left = jnp.concatenate(
            [
                grid[z + dz : z + dz + planes, dy : dy + edge].reshape(rows, 128)
                for dz in range(3)
                for dy in range(3)
            ],
            axis=1,
        )
        wide = jnp.dot(left, taps[:, 0:256], preferred_element_type=jnp.float32)
        wide = wide.reshape(planes * edge, edge, 256)
        left = jnp.concatenate(
            [
                halved[z + dz : z + dz + planes, line // 2 : line // 2 + edge // 2, line % 2].reshape(
                    rows // 2, 128
                )
                for dz in range(3)
                for line in range(4)
            ],
            axis=1,
        )
        two = jnp.dot(left, pairs[...], preferred_element_type=jnp.float32)
        two = two.reshape(planes * edge // 2, edge, 256)
        two = jnp.stack([two[:, :, :128], two[:, :, 128:]], axis=1).reshape(planes * edge, edge, 128)
        after = jnp.where(place > 0, pltpu.roll(wide[:, :, :128], 1, 1), 0.0)
        before = jnp.where(place < edge - 1, pltpu.roll(two, edge - 1, 1), 0.0)
        new = wide[:, :, 128:256] + after + before
        put(z, new.reshape(planes, edge, edge, 128))


def conv_kernel(deep_in, x, weight, act, taps, pairs, deep_weight, sem):
    copy = pltpu.make_async_copy(deep_in, deep_weight, sem)
    copy.start()
    edge = act.shape[0]
    spread_taps(weight, taps)
    pair_taps(weight, pairs)

    def put(z, new):
        act[z : z + new.shape[0]] = new

    convolve(x, edge, taps, pairs, put)
    copy.wait()


def y_terms(line, low, taps):
    planes, edge = line.shape[0] - 2, line.shape[1]
    left = jnp.concatenate(
        [line[dz : dz + planes].reshape(planes * edge, 128) for dz in range(3)], axis=1
    )
    start = jnp.where(low, 0, 256)
    right = jnp.concatenate(
        [taps[pl.ds(pl.multiple_of(start + dz * 384, 128), 128), :] for dz in range(3)], axis=0
    )
    wide = jnp.dot(left, right, preferred_element_type=jnp.float32)
    return join_x(wide.reshape(planes, edge, 384), edge)


def x_terms(column, taps):
    planes, edge = column.shape[0] - 2, column.shape[1] - 16
    lines = [column[:, 7 + dy : 7 + dy + edge].astype(jnp.bfloat16) for dy in range(3)]
    left = jnp.concatenate(
        [line[dz : dz + planes].reshape(planes * edge, 128) for dz in range(3) for line in lines],
        axis=1,
    )
    right = jnp.concatenate([taps[:, 0:128], taps[:, 256:384]], axis=1)
    both = jnp.dot(left, right, preferred_element_type=jnp.float32)
    return both[:, :128], both[:, 128:]


def fill_column(column, at, voxels, ends, above):
    count, edge = voxels.shape[:2]
    rows = edge + 16
    lines = column.reshape(column.shape[0] * rows, 128)
    column[at : at + count, 8 : 8 + edge] = voxels.astype(jnp.float32)
    for i, end in enumerate(ends):
        first = last = end.astype(jnp.float32)
        if len(ends) == 1:
            first, last = jnp.where(above[0], first, 0.0), jnp.where(above[0], 0.0, last)
        if len(ends) == 1 or i == 0:
            lines[pl.ds(at * rows + 7, count, stride=rows), :] = first
        if len(ends) == 1 or i == 1:
            lines[pl.ds(at * rows + 8 + edge, count, stride=rows), :] = last


def add_column(act, terms, j, nx, low):
    planes, edge = act.shape[:2]
    flat = act.reshape(planes * edge * edge, 128)
    first, last = terms
    if nx == 1:
        first, last = jnp.where(low, first, 0.0), jnp.where(low, 0.0, last)
    if nx == 1 or j == 0:
        flat[pl.ds(0, planes * edge, stride=edge), :] += first
    if nx == 1 or j == 1:
        flat[pl.ds(edge - 1, planes * edge, stride=edge), :] += last


def moments(planes):
    count, edge = planes.shape[:2]
    zero = jnp.zeros((8, 128), jnp.float32)

    def sum_step(k, carry):
        return carry + jnp.sum(planes[k].reshape(edge * 2, 8, 128), axis=0)

    mean = lax.fori_loop(0, count, sum_step, zero, unroll=True) / (count * edge * edge // 8)

    def spread_step(k, carry):
        off = planes[k].reshape(edge * 2, 8, 128) - mean
        return carry + jnp.sum(off * off, axis=0)

    return mean, lax.fori_loop(0, count, spread_step, zero, unroll=True)


def side_kernel(ny, nx, *refs):
    x, own, y_halos, x_halos, corners, outer, inner, taps, pairs, middle, ends, stats, act, grid, column = refs
    edge = own.shape[0]
    depth = edge + 4
    f32 = jnp.float32
    above, left = Square().low_sides()
    odd = lax.axis_index("gz") % 2 == 1
    act[2 : 2 + edge] = own[...]
    blank = jnp.zeros(grid.shape[:1] + grid.shape[2:], grid.dtype)
    grid[:, 0] = blank
    grid[:, edge + 1] = blank
    faces = in_order(odd, outer[...], inner[...])
    for face, halo_at, own_at, plane, beyond, at, beside, dz in (
        (faces[0], 0, 3, 1, 0, 2, 2, 0),
        (faces[1], 1, 0, edge, edge + 2, edge + 1, 1, 2),
    ):
        grid[halo_at : halo_at + 3, 1 : edge + 1] = face
        grid[own_at, 1 : edge + 1] = x[plane, 1 : edge + 1]

        def put(z, new):
            act[beyond + z : beyond + z + new.shape[0]] = new

        convolve(grid, 2, taps, pairs, put)
        stacked = jnp.concatenate(
            [grid[beside, dy : dy + edge].reshape(edge * edge, 128) for dy in range(3)], axis=1
        )
        wide = jnp.dot(stacked, taps[dz * 384 : dz * 384 + 384, :], preferred_element_type=f32)
        act[at] += join_x(wide.reshape(edge, edge, 384), edge)

    gap = jnp.zeros((2, edge, 128), grid.dtype)
    reached = act.at[1 : depth - 1]
    for i in range(ny):
        line = jnp.concatenate([gap, y_halos[i, 0:edge], gap], axis=0)
        reached[:, jnp.where(above[i], 0, edge - 1)] += y_terms(line, above[i], taps)
    for j in range(nx):
        column[...] = jnp.zeros(column.shape, f32)
        fill_column(
            column, 2, x_halos[j, 0:edge], [corners[i * nx + j, 0] for i in range(ny)], above
        )
        add_column(reached, x_terms(column, taps), j, nx, left[j])
    middle[...] = act[3 : depth - 3]
    ends[0:3] = act[0:3]
    ends[3:6] = act[depth - 3 :]
    mean, spread = moments(act.at[3 : depth - 3])
    stats[0:8] = mean
    stats[8:16] = spread


def end_kernel(ny, nx, middle_stats, ends, outer, inner, taps, act, stats, faces, column):
    edge = act.shape[1]
    wide = ny + nx
    f32 = jnp.float32
    above, left = Square().low_sides()
    odd = lax.axis_index("gz") % 2 == 1
    faces[0], faces[1] = in_order(odd, outer[...], inner[...])
    act[...] = ends[...]
    gap = jnp.zeros((2, edge, 128), faces.dtype)
    for side in range(2):

        def rim(row):
            return jnp.stack([faces[side, k * wide + row] for k in range(3)])

        three = act.at[3 * side : 3 * side + 3]
        for i in range(ny):
            line = [rim(i), gap] if side == 0 else [gap, rim(i)]
            line = jnp.concatenate(line, axis=0)
            three[:, jnp.where(above[i], 0, edge - 1)] += y_terms(line, above[i], taps)
        for j in range(nx):
            column[...] = jnp.zeros(column.shape, f32)
            tails = []
            for i in range(ny):
                tile = faces[side, 3 * wide + i * nx + j].astype(f32)
                tails.append(tile[edge - 3 :] if side == 0 else tile[:3])
            fill_column(column, 0 if side == 0 else 2, rim(ny + j), tails, above)
            add_column(three, x_terms(column, taps), j, nx, left[j])

    mean, spread = moments(act.at[2:4])
    few, many = edge * edge // 4, (edge - 2) * edge * edge // 8
    middle_mean, middle_spread = middle_stats[0:8], middle_stats[8:16]
    off = middle_mean - mean
    part = few / (few + many)
    spread = spread + middle_spread + (many * part) * (off * off)
    put_stats(stats, middle_mean - part * off, spread, few + many)


def merge(mean, spread, rows, other_mean, other_spread):
    off = mean - other_mean
    return 0.5 * (mean + other_mean), spread + other_spread + (0.5 * rows) * (off * off)


def put_stats(stats, mean, spread, rows):
    for step in (1, 2, 4):
        others = pltpu.roll(mean, step, 0), pltpu.roll(spread, step, 0)
        mean, spread = merge(mean, spread, float(rows * step), *others)
    both = jnp.concatenate([mean[0:1], spread[0:1]], axis=0)
    stats[...] = jnp.broadcast_to(both[None], stats.shape)


def read_stats(stats, rows):
    devices, _, channels = stats.shape
    shape = (8, channels)
    means = [jnp.broadcast_to(stats[k, 0:1, :], shape) for k in range(devices)]
    spreads = [jnp.broadcast_to(stats[k, 1:2, :], shape) for k in range(devices)]
    mean = functools.reduce(jnp.add, means) / devices
    spread = functools.reduce(jnp.add, spreads)
    spread = spread + rows * functools.reduce(jnp.add, [(m - mean) * (m - mean) for m in means])
    rows = rows * devices
    lane = lax.broadcasted_iota(jnp.int32, shape, 1)
    step = 1
    while step < channels // GROUPS:
        low = jnp.bitwise_and(lane, step) == 0
        others = [
            jnp.where(low, pltpu.roll(row, channels - step, 1), pltpu.roll(row, step, 1))
            for row in (mean, spread)
        ]
        mean, spread = merge(mean, spread, rows, *others)
        rows, step = 2.0 * rows, 2 * step
    return mean, lax.rsqrt(spread / rows + EPSILON)


def silu_of_double(h):
    return h + h * jnp.tanh(h)


def norm_kernel(ny, nx, inner, ends, stats, gain, offset, out, pooled, *refs):
    y_edges, x_edges, corners, half = refs
    depth, edge = inner.shape[0] + 6, inner.shape[1]
    deep, deep_depth = edge // 2, depth // 2
    f32, bf16 = jnp.float32, jnp.bfloat16
    above, left = Square().low_sides()
    depth_at = lax.axis_index("gz")
    mean, scale = read_stats(stats, float(edge**3))
    scale = scale * (0.5 * gain[...])
    shift = 0.5 * offset[...]
    for k in range(deep_depth):
        value = [
            ends[z] if z < 3 else inner[z - 3] if z < depth - 3 else ends[z - depth + 6]
            for z in (2 * k, 2 * k + 1)
        ]
        value = jnp.stack(value).reshape(edge * edge // 4, 8, 128)
        value = silu_of_double((value - mean) * scale + shift)
        value = value.reshape(2, edge, edge, 128).astype(bf16)
        if 0 < k < deep_depth - 1:
            out[2 * k - 2 : 2 * k] = value
        value = value.astype(f32)
        value = (value[0] + value[1]).reshape(deep, 2, edge, 128)
        half[k] = (value[:, 0] + value[:, 1]).reshape(deep * edge, 128)
        lines = half.at[k]
        pair = lines[pl.ds(0, deep * deep, stride=2), :] + lines[pl.ds(1, deep * deep, stride=2), :]
        pair = (pair * 0.125).astype(bf16).astype(f32).reshape(deep, deep, 128)
        if k == 0 or k == deep_depth - 1:
            inside = depth_at > 0 if k == 0 else depth_at < lax.axis_size("gz") - 1
            pair = jnp.where(inside, pair, 0.0)
        pooled[k] = pair
    lines = pooled.reshape(deep_depth * deep * deep, 128)
    rows = deep_depth * deep
    first_x = lines[pl.ds(0, rows, stride=deep), :]
    last_x = lines[pl.ds(deep - 1, rows, stride=deep), :]
    first_y, last_y = (pooled[:, y].reshape(rows, 128) for y in (0, deep - 1))
    ends = []
    for y in (0, deep - 1):
        for x in (0, deep - 1):
            ends.append(lines[pl.ds(y * deep + x, deep_depth, stride=deep * deep), :])
    if ny == 1:
        above, left = above[0], left[0]
        y_edges[0] = jnp.where(above, first_y, last_y).astype(bf16)
        x_edges[0] = jnp.where(left, first_x, last_x).astype(bf16)
        corners[0, 0:deep_depth] = jnp.where(
            above, jnp.where(left, ends[0], ends[1]), jnp.where(left, ends[2], ends[3])
        )
    else:
        y_edges[0], y_edges[1] = first_y.astype(bf16), last_y.astype(bf16)
        x_edges[0], x_edges[1] = first_x.astype(bf16), last_x.astype(bf16)
        for k in range(4):
            corners[k, 0:deep_depth] = ends[k]


def stack_kernel(*refs):
    out = refs[-1]
    for k in range(out.shape[0]):
        out[k] = refs[k][...]


def stack(*arrays):
    vmem = pl.BlockSpec(memory_space=pltpu.VMEM)
    return pl.pallas_call(
        stack_kernel,
        out_shape=jax.ShapeDtypeStruct((len(arrays),) + arrays[0].shape, arrays[0].dtype),
        in_specs=[vmem] * len(arrays),
        out_specs=vmem,
        compiler_params=pltpu.CompilerParams(vmem_limit_bytes=VMEM_BYTES),
    )(*arrays)


def place_weights(own, held, out):
    tile = lax.axis_index("yx")
    out[tile] = own[...]
    if len(held) == 1:
        pieces, others, size = held[0].shape[:3]
        for piece in range(pieces):
            at = jnp.minimum(jnp.bitwise_xor(Riders.mine(), piece) * size, own.shape[0] - size)
            for k in range(others):
                out[jnp.bitwise_xor(tile, k + 1), pl.ds(at, size)] = held[0][piece, k]
    else:
        for k, shard in enumerate(held):
            out[lax.rem(tile + len(held) - k, len(held) + 1)] = shard[...]


def tap_rows(weight, taps):
    per = weight.shape[1] // 27
    return jnp.concatenate(
        [weight[:, pl.ds(tap * per, per)].reshape(-1, 128) for tap in taps], axis=1
    )


def dot_rows(left, right):
    return lax.dot_general(
        left, right, (((1,), (1,)), ((), ())), preferred_element_type=jnp.float32
    )


def deep_kernel(pooled, own, *refs):
    *held, act, weight, grid, packed = refs
    depth, deep = pooled.shape[0], pooled.shape[1]
    place_weights(own, held, weight)
    grid[...] = jnp.zeros(grid.shape, jnp.float32)
    grid[:, 1 : deep + 1, 8:16] = pooled[...]
    for dx in range(3):
        plane = grid[:, :, 7 + dx : 15 + dx]
        for y in range(deep + 1):
            both = jnp.concatenate([plane[:, y], plane[:, y + 1]], axis=1)
            packed[:, y // 2, y % 2, :, dx * 128 : dx * 128 + 128] = both.astype(jnp.bfloat16)
    rows = deep**3
    total = None
    for dz in range(3):
        left = jnp.concatenate(
            [
                packed[dz : dz + deep, dy // 2 : dy // 2 + deep // 2, dy % 2].reshape(rows, 384)
                for dy in range(3)
            ],
            axis=1,
        )
        term = dot_rows(left, tap_rows(weight, range(dz * 9, dz * 9 + 9)))
        total = term if total is None else total + term
    for half in range(act.shape[0]):
        act[half] = total[:, half * 128 : half * 128 + 128]


def deep_rim_kernel(ny, nx, own, y_halos, x_halos, corners, weight, act, stats, line):
    depth, deep = line.shape[0], line.shape[1] - 16
    halves = act.shape[0]
    f32 = jnp.float32
    square = deep * deep
    above, left = Square().low_sides()
    act[...] = own[...]
    flat = line.reshape(depth * line.shape[1], 128)

    def shifts():
        return jnp.concatenate(
            [
                line[dz : dz + deep, 7 + d : 7 + d + deep].reshape(square, 128).astype(jnp.bfloat16)
                for dz in range(3)
                for d in range(3)
            ],
            axis=1,
        )

    for i in range(ny):
        line[...] = jnp.zeros(line.shape, f32)
        line[:, 8 : 8 + deep] = y_halos[i].astype(f32).reshape(depth, deep, 128)
        for j in range(nx):
            end = corners[i * nx + j, 0:depth]
            first, last = jnp.where(left[j], end, 0.0), jnp.where(left[j], 0.0, end)
            if nx == 1 or j == 0:
                flat[pl.ds(7, depth, stride=line.shape[1]), :] = first
            if nx == 1 or j == 1:
                flat[pl.ds(8 + deep, depth, stride=line.shape[1]), :] = last
        tap = jnp.where(above[i], 0, 6)
        taps = [tap + dz * 9 + dx for dz in range(3) for dx in range(3)]
        terms = dot_rows(shifts(), tap_rows(weight, taps))
        for half in range(halves):
            rows = act.at[half].reshape(deep, deep, deep, 128)
            term = terms[:, half * 128 : half * 128 + 128].reshape(deep, deep, 128)
            rows[:, jnp.where(above[i], 0, deep - 1)] += term
    for j in range(nx):
        line[...] = jnp.zeros(line.shape, f32)
        line[:, 8 : 8 + deep] = x_halos[j].astype(f32).reshape(depth, deep, 128)
        tap = jnp.where(left[j], 0, 2)
        taps = [tap + dz * 9 + dy * 3 for dz in range(3) for dy in range(3)]
        terms = dot_rows(shifts(), tap_rows(weight, taps))
        first, last = jnp.where(left[j], terms, 0.0), jnp.where(left[j], 0.0, terms)
        for half in range(halves):
            lanes, rows = slice(half * 128, half * 128 + 128), act.at[half]
            if nx == 1 or j == 0:
                rows[pl.ds(0, square, stride=deep), :] += first[:, lanes]
            if nx == 1 or j == 1:
                rows[pl.ds(deep - 1, square, stride=deep), :] += last[:, lanes]

    rows = deep**3 // 8
    means, spreads = [], []
    for half in range(halves):
        total = act[half].reshape(rows, 8, 128)
        means.append(jnp.sum(total, axis=0) / rows)
        off = total - means[-1]
        spreads.append(jnp.sum(off * off, axis=0))
    put_stats(stats, *(jnp.concatenate(part, axis=1) for part in (means, spreads)), rows)


def final_kernel(act, stats, gain, offset, up, mid, out, wide, held, sems):
    edge = mid.shape[0]
    deep = edge // 2
    f32 = jnp.float32
    mean, scale = read_stats(stats, float(deep**3))
    scale = scale * (0.5 * gain[...])
    shift = 0.5 * offset[...]
    planes = 2
    size = planes * deep * deep
    copies = []
    for k in range(0, deep, planes):
        at = slice(k * deep * deep, k * deep * deep + size)
        value = jnp.concatenate([act[half, at] for half in range(act.shape[0])], axis=1)
        value = value.reshape(size // 8, 8, -1)
        value = silu_of_double((value - mean) * scale + shift)
        value = value.reshape(size, -1).astype(jnp.bfloat16)
        lifted = jnp.dot(value, up[...], preferred_element_type=f32)
        lines = wide.at[k // planes]
        lines[pl.ds(0, size, stride=2), :] = lifted
        lines[pl.ds(1, size, stride=2), :] = lifted
        add = lines[...].reshape(planes, 1, deep, 1, edge, 128)
        at = pl.ds(2 * k, 2 * planes)
        old = mid[at].astype(f32).reshape(planes, 2, deep, 2, edge, 128)
        held[at] = (old + add).astype(jnp.bfloat16).reshape(2 * planes, edge, edge, 128)
        copy = pltpu.make_async_copy(held.at[at], out.at[at], sems.at[k // planes])
        copy.start()
        copies.append(copy)
    for copy in copies:
        copy.wait()


def body(
    features, conv_weight, gain_mid, offset_mid, deep_weight, gain_deep, offset_deep, up_weight
):
    f32, bf16 = jnp.float32, jnp.bfloat16
    edge, channels = features.shape[0], features.shape[3]
    deep = edge // 2
    deep_channels = gain_deep.shape[0]
    square = Square()
    tiles = square.tiles
    devices = lax.axis_size("gz") * tiles
    ny, nx = (len(sides) for sides in square.low_sides())
    riders = Riders(deep_weight.shape[4])

    own = jnp.moveaxis(deep_weight, 4, 3).reshape(-1, 16, channels)
    conv_weight = conv_weight.reshape(27, channels, channels)
    three = ((3, edge, edge, channels), bf16)
    *edges, outer, inner, field, conv_weight = call(
        functools.partial(start_kernel, ny, nx, riders.size),
        [
            ((ny, edge + riders.size, edge, channels), bf16),
            ((nx, edge + riders.size, edge, channels), bf16),
            ((ny * nx, 1 + riders.size, edge, channels), bf16),
            three,
            three,
            ((edge + 2, edge + 2, edge, channels), bf16),
            (conv_weight.shape, bf16),
        ],
        [((nx, edge * edge, 8, channels), f32), pltpu.SemaphoreType.DMA((8,))],
        features,
        conv_weight,
        own,
        nbytes=5 << 20,
        in_hbm=3,
    )
    halos = square.halos(*(list(piece) for piece in edges))
    outer, inner = swap_depth(outer, inner)
    conv_flops = 54 * channels * channels * edge**3
    act, taps, pairs, own = call(
        conv_kernel,
        [
            ((edge, edge, edge, channels), f32),
            ((9 * channels, 3 * channels), bf16),
            ((12 * channels, 2 * channels), bf16),
            (own.shape, bf16),
        ],
        [pltpu.SemaphoreType.DMA],
        own,
        field,
        conv_weight,
        flops=conv_flops,
        nbytes=6 << 20,
        in_hbm=1,
    )
    (y, x, corner), act = lax.optimization_barrier((halos, act))
    y, x, corner = jnp.stack(y), jnp.stack(x), jnp.stack(corner)
    turn = ((3 * (ny + nx) + ny * nx, edge, channels), bf16)
    held = [((3, riders.size, 16, channels), bf16)] if riders.size else []
    turns = call(
        functools.partial(turn_kernel, ny, nx, riders.size), [turn, turn] + held, [], y, x, corner
    )
    turns, held = swap_depth(*turns[:2]), turns[2:]
    if riders.size:
        held = held[0][None]
        other = swap(held, *riders.STEPS[0])
    else:
        held = rotate_shards(own)
    six = ((6, edge, edge, channels), f32)
    column = (edge + 16, channels)
    middle, ends, stats = call(
        functools.partial(side_kernel, ny, nx),
        [((edge - 2, edge, edge, channels), f32), six, ((16, channels), f32)],
        [
            ((edge + 4, edge, edge, channels), f32),
            ((4, edge + 2, edge, channels), bf16),
            ((edge + 4,) + column, f32),
        ],
        field,
        act,
        y,
        x,
        corner,
        outer,
        inner,
        taps,
        pairs,
    )
    ends, stats = call(
        functools.partial(end_kernel, ny, nx),
        [six, ((devices, 2, channels), f32)],
        [((2,) + turn[0], bf16), ((5,) + column, f32)],
        stats,
        ends,
        *turns,
        taps,
    )
    if riders.size:
        stats, other = lax.optimization_barrier((stats, other))
        held = stack(held, other).reshape((-1,) + held.shape[1:])
        other = swap(held, *riders.STEPS[1])
        stats = share(stats)
        stats, other = lax.optimization_barrier((stats, other))
        held = stack(held, other).reshape((-1,) + held.shape[1:])
        other = swap(held, *riders.STEPS[2])
        held = [stack(held, other).reshape((-1,) + held.shape[1:])]
    else:
        stats = share(stats)
    out, pooled, *edges = call(
        functools.partial(norm_kernel, ny, nx),
        [
            ((edge, edge, edge, channels), bf16),
            ((deep + 2, deep, deep, channels), f32),
            ((ny, (deep + 2) * deep, channels), bf16),
            ((nx, (deep + 2) * deep, channels), bf16),
            ((ny * nx, 16, channels), f32),
        ],
        [((deep + 2, deep * edge, channels), f32)],
        middle,
        ends,
        stats,
        gain_mid.reshape(1, channels),
        offset_mid.reshape(1, channels),
        flops=20 * channels * edge**3,
        nbytes=3 << 20,
    )
    y, x, corner = square.halos(*(list(piece) for piece in edges))
    halves = ((deep_channels // 128, deep**3, 128), f32)
    deep_act, weight = call(
        deep_kernel,
        [halves, ((tiles,) + own.shape, bf16)],
        [
            ((deep + 2, deep + 2, 24, channels), f32),
            ((deep + 2, deep // 2 + 1, 2, 16, 3 * channels), bf16),
        ],
        pooled,
        own,
        *held,
        flops=54 * channels * deep_channels * deep**3,
        nbytes=4 << 20,
    )
    deep_act, stats = call(
        functools.partial(deep_rim_kernel, ny, nx),
        [halves, ((devices, 2, deep_channels), f32)],
        [((deep + 2, 24, channels), f32)],
        deep_act,
        jnp.stack(y),
        jnp.stack(x),
        jnp.stack(corner),
        weight,
        flops=4 * channels * deep_channels * deep**3,
        nbytes=3 << 20,
    )
    stats = share(stats)
    (decoded,) = call(
        final_kernel,
        [((edge, edge, edge, channels), bf16)],
        [
            ((deep // 2, 4 * deep * deep, channels), f32),
            ((edge, edge, edge, channels), bf16),
            pltpu.SemaphoreType.DMA((deep // 2,)),
        ],
        deep_act,
        stats,
        gain_deep.reshape(1, deep_channels),
        offset_deep.reshape(1, deep_channels),
        up_weight,
        out,
        flops=4 * deep_channels * channels * deep**3,
        nbytes=3 << 20,
        out_hbm=True,
    )
    return decoded


def solution(mesh):
    placed = (
        P(("cand", "gz"), "yx", None, None),
        P(),
        P(),
        P(),
        P(None, None, None, None, "yx"),
        P(),
        P(),
        P(),
    )
    return jax.shard_map(
        body,
        mesh=mesh,
        in_specs=placed,
        out_specs=P(("cand", "gz"), "yx", None, None),
        check_vma=False,
    )
```

```python
import functools
import math

import jax
import jax.numpy as jnp
from jax import lax
from jax.experimental import pallas as pl
from jax.experimental.pallas import tpu as pltpu
from jax.sharding import PartitionSpec as P

GROUPS = 32
EPSILON = 1e-05
PART = ("gz", "yx")
VMEM_BYTES = 32 * 1024 * 1024


class Square:
    def __init__(self):
        self.tiles = lax.axis_size("yx")
        self.side = math.isqrt(self.tiles)
        tile = lax.axis_index("yx")
        self.row, self.column = tile // self.side, tile % self.side
        self.folded = self.side == 2
        self.steps = (0,) if self.folded else (-1, 1)

    def low_sides(self):
        if self.folded:
            return [self.row == 1], [self.column == 1]
        return [True, False], [True, False]

    def route(self, down, right):
        pairs = []
        for tile in range(self.tiles):
            row, column = tile // self.side + down, tile % self.side + right
            if 0 <= row < self.side and 0 <= column < self.side:
                pairs.append((tile, row * self.side + column))
        return pairs

    def swap_route(self, mask):
        return [(tile, tile ^ mask) for tile in range(self.tiles)]

    def halos(self, y_edges, x_edges, corners):
        if self.folded:
            y = lax.ppermute(y_edges[0], "yx", self.swap_route(2))
            x = lax.ppermute(x_edges[0], "yx", self.swap_route(1))
            corner = lax.ppermute(corners[0], "yx", self.swap_route(3))
            return [y], [x], [corner]
        y = [lax.ppermute(y_edges[k], "yx", self.route((1, -1)[1 - k], 0)) for k in (1, 0)]
        x = [lax.ppermute(x_edges[k], "yx", self.route(0, (1, -1)[1 - k])) for k in (1, 0)]
        corner = [
            lax.ppermute(corners[2 * k + j], "yx", self.route((1, -1)[1 - k], (1, -1)[1 - j]))
            for k in (1, 0)
            for j in (1, 0)
        ]
        return y, x, corner


def swap_depth(outer, inner):
    size = lax.axis_size("gz")
    routes = [[], []]
    for low in range(size - 1):
        routes[low % 2] += [(low, low + 1), (low + 1, low)]
    return lax.ppermute(outer, "gz", routes[1]), lax.ppermute(inner, "gz", routes[0])


class Riders:
    STEPS = (("gz", 2), ("cand", 1), ("gz", 1))

    def __init__(self, rows):
        self.tiles = 27 * rows // 16
        self.fits = (
            lax.axis_size("yx") == 4
            and lax.axis_size("cand") % 2 == 0
            and lax.axis_size("gz") % 4 == 0
            and self.tiles >= 8
        )
        self.size = -(-self.tiles // 8) if self.fits else 0

    @classmethod
    def mine(cls):
        return sum(
            lax.axis_index(axis) // mask % 2 * 2**k for k, (axis, mask) in enumerate(cls.STEPS)
        )


def rotate_shards(piece):
    tiles = lax.axis_size("yx")
    return [
        lax.ppermute(piece, "yx", [(i, (i + k) % tiles) for i in range(tiles)]) for k in range(1, tiles)
    ]


def swap(block, axis, mask):
    return lax.ppermute(block, axis, [(i, i ^ mask) for i in range(lax.axis_size(axis))])


def share(stats):
    return lax.all_to_all(stats, PART, 0, 0)


def call(kernel, outs, scratch, *arrays, flops=0, nbytes=0, in_hbm=0, out_hbm=False):
    vmem, hbm = (pl.BlockSpec(memory_space=space) for space in (pltpu.VMEM, pltpu.HBM))
    far, near = arrays[:in_hbm], arrays[in_hbm:]
    far = [pltpu.with_memory_space_constraint(array, pltpu.HBM) for array in far]
    return pl.pallas_call(
        kernel,
        out_shape=[jax.ShapeDtypeStruct(shape, dtype) for shape, dtype in outs],
        in_specs=[hbm] * len(far) + [vmem] * len(near),
        out_specs=[hbm if out_hbm else vmem] * len(outs),
        scratch_shapes=[pltpu.VMEM(*entry) if isinstance(entry, tuple) else entry for entry in scratch],
        compiler_params=pltpu.CompilerParams(vmem_limit_bytes=VMEM_BYTES),
        cost_estimate=pl.CostEstimate(flops=flops, bytes_accessed=nbytes, transcendentals=0),
    )(*far, *near)


def start_kernel(ny, nx, size, x_in, w_in, d_in, y_out, x_out, corners, outer, inner, x, w, lines, sems):
    edge = x_in.shape[0]
    f32, bf16 = jnp.float32, jnp.bfloat16
    above, left = Square().low_sides()
    chunks = 4
    planes = edge // chunks
    first = [
        pltpu.make_async_copy(
            x_in.at[pl.ds(k * planes, planes)],
            x.at[pl.ds(1 + k * planes, planes), pl.ds(1, edge)],
            sems.at[k],
        )
        for k in range(chunks)
    ]
    later = []
    if size:
        at = jnp.minimum(Riders.mine() * size, d_in.shape[0] - size)
        for k, (out, begin) in enumerate(((y_out, edge), (x_out, edge), (corners, 1))):
            later.append(
                pltpu.make_async_copy(
                    d_in.at[pl.ds(at, size)], out.at[0, pl.ds(begin, size)], sems.at[chunks + k]
                )
            )
    later.append(pltpu.make_async_copy(w_in, w, sems.at[chunks + 3]))
    for copy in first + later:
        copy.start()
    x[0] = jnp.zeros(x.shape[1:], bf16)
    x[edge + 1] = jnp.zeros(x.shape[1:], bf16)
    blank = jnp.zeros((edge,) + x.shape[2:], bf16)
    x[1 : edge + 1, 0] = blank
    x[1 : edge + 1, edge + 1] = blank
    flat = lines.reshape(nx * edge * edge * 8, 128)
    part = planes * edge
    for k in range(chunks):
        first[k].wait()
        at, here = pl.ds(k * planes, planes), pl.ds(1 + k * planes, planes)
        for i in range(ny):
            row = jnp.where(above[i], 1, edge)
            y_out[i, at] = x[here, row]
        for j in range(nx):
            low = x[here, 1 : edge + 1, 0:8].astype(f32).reshape(part, 8, 128)
            high = x[here, 1 : edge + 1, edge - 8 : edge].astype(f32).reshape(part, 8, 128)
            high = pltpu.roll(high, 1, 1)
            kept = jnp.where(left[j], low, high)
            lines[j, k * part : k * part + part] = kept
            begin = (j * edge * edge + k * part) * 8
            column = flat[pl.ds(begin, part, stride=8), :]
            x_out[j, at] = column.astype(bf16).reshape(planes, edge, 128)
    for i in range(ny):
        for j in range(nx):
            begin = j * edge * edge * 8
            low = flat[pl.ds(begin, edge, stride=8 * edge), :]
            high = flat[pl.ds(begin + 8 * (edge - 1), edge, stride=8 * edge), :]
            kept = jnp.where(above[i], low, high)
            corners[i * nx + j, 0] = kept.astype(bf16)
    odd, far = lax.axis_index("gz") % 2, edge - 3
    for face, at in ((outer, odd * far), (inner, (1 - odd) * far)):
        for k in range(3):
            face[k] = x[1 + at + k, 1 : edge + 1]
    for copy in later:
        copy.wait()


def turn_kernel(ny, nx, size, y_halos, x_halos, corners, outer, inner, *riders):
    edge = outer.shape[1]
    wide = ny + nx
    odd, far = lax.axis_index("gz") % 2, edge - 3
    for face, at in ((outer, odd * far), (inner, (1 - odd) * far)):
        for k in range(3):
            row = k * wide
            for i in range(ny):
                face[row + i] = y_halos[i, at + k]
            for j in range(nx):
                face[row + ny + j] = x_halos[j, at + k]
        for k in range(ny * nx):
            face[3 * wide + k] = corners[k, 0]
    if size:
        riders[0][0] = x_halos[0, edge : edge + size]
        riders[0][1] = y_halos[0, edge : edge + size]
        riders[0][2] = corners[0, 1 : 1 + size]


def in_order(odd, outer, inner):
    return jnp.where(odd, inner, outer), jnp.where(odd, outer, inner)


def spread_taps(weight, taps):
    for tap in range(27):
        row, lane = tap // 3 * 128, tap % 3 * 128
        taps[row : row + 128, lane : lane + 128] = weight[tap]


def pair_taps(weight, pairs):
    for dz in range(3):
        for line in range(4):
            row = (dz * 4 + line) * 128
            for out in range(2):
                lane = out * 128
                if 0 <= line - out < 3:
                    block = weight[dz * 9 + (line - out) * 3 + 2]
                else:
                    block = jnp.zeros((128, 128), pairs.dtype)
                pairs[row : row + 128, lane : lane + 128] = block


def join_x(wide, edge):
    place = lax.broadcasted_iota(jnp.int32, wide.shape[:2] + (128,), 1)
    after = jnp.where(place > 0, pltpu.roll(wide[:, :, :128], 1, 1), 0.0)
    before = jnp.where(place < edge - 1, pltpu.roll(wide[:, :, 256:], edge - 1, 1), 0.0)
    return wide[:, :, 128:256] + after + before


def convolve(grid, count, taps, pairs, put):
    edge = grid.shape[2]
    planes = min(count, 4)
    rows = planes * edge * edge
    place = lax.broadcasted_iota(jnp.int32, (planes * edge, edge, 128), 1)
    halved = grid.reshape(grid.shape[0], edge // 2 + 1, 2, edge, 128)
    for z in range(0, count, planes):
        left = jnp.concatenate(
            [
                grid[z + dz : z + dz + planes, dy : dy + edge].reshape(rows, 128)
                for dz in range(3)
                for dy in range(3)
            ],
            axis=1,
        )
        wide = jnp.dot(left, taps[:, 0:256], preferred_element_type=jnp.float32)
        wide = wide.reshape(planes * edge, edge, 256)
        left = jnp.concatenate(
            [
                halved[z + dz : z + dz + planes, line // 2 : line // 2 + edge // 2, line % 2].reshape(
                    rows // 2, 128
                )
                for dz in range(3)
                for line in range(4)
            ],
            axis=1,
        )
        two = jnp.dot(left, pairs[...], preferred_element_type=jnp.float32)
        two = two.reshape(planes * edge // 2, edge, 256)
        two = jnp.stack([two[:, :, :128], two[:, :, 128:]], axis=1).reshape(planes * edge, edge, 128)
        after = jnp.where(place > 0, pltpu.roll(wide[:, :, :128], 1, 1), 0.0)
        before = jnp.where(place < edge - 1, pltpu.roll(two, edge - 1, 1), 0.0)
        new = wide[:, :, 128:256] + after + before
        put(z, new.reshape(planes, edge, edge, 128))


def conv_kernel(deep_in, x, weight, act, taps, pairs, deep_weight, sem):
    copy = pltpu.make_async_copy(deep_in, deep_weight, sem)
    copy.start()
    edge = act.shape[0]
    spread_taps(weight, taps)
    pair_taps(weight, pairs)

    def put(z, new):
        act[z : z + new.shape[0]] = new

    convolve(x, edge, taps, pairs, put)
    copy.wait()


def y_terms(line, low, taps):
    planes, edge = line.shape[0] - 2, line.shape[1]
    left = jnp.concatenate(
        [line[dz : dz + planes].reshape(planes * edge, 128) for dz in range(3)], axis=1
    )
    start = jnp.where(low, 0, 256)
    right = jnp.concatenate(
        [taps[pl.ds(pl.multiple_of(start + dz * 384, 128), 128), :] for dz in range(3)], axis=0
    )
    wide = jnp.dot(left, right, preferred_element_type=jnp.float32)
    return join_x(wide.reshape(planes, edge, 384), edge)


def x_terms(column, taps):
    planes, edge = column.shape[0] - 2, column.shape[1] - 16
    lines = [column[:, 7 + dy : 7 + dy + edge].astype(jnp.bfloat16) for dy in range(3)]
    left = jnp.concatenate(
        [line[dz : dz + planes].reshape(planes * edge, 128) for dz in range(3) for line in lines],
        axis=1,
    )
    right = jnp.concatenate([taps[:, 0:128], taps[:, 256:384]], axis=1)
    both = jnp.dot(left, right, preferred_element_type=jnp.float32)
    return both[:, :128], both[:, 128:]


def fill_column(column, at, voxels, ends, above):
    count, edge = voxels.shape[:2]
    rows = edge + 16
    lines = column.reshape(column.shape[0] * rows, 128)
    column[at : at + count, 8 : 8 + edge] = voxels.astype(jnp.float32)
    for i, end in enumerate(ends):
        first = last = end.astype(jnp.float32)
        if len(ends) == 1:
            first, last = jnp.where(above[0], first, 0.0), jnp.where(above[0], 0.0, last)
        if len(ends) == 1 or i == 0:
            lines[pl.ds(at * rows + 7, count, stride=rows), :] = first
        if len(ends) == 1 or i == 1:
            lines[pl.ds(at * rows + 8 + edge, count, stride=rows), :] = last


def add_column(act, terms, j, nx, low):
    planes, edge = act.shape[:2]
    flat = act.reshape(planes * edge * edge, 128)
    first, last = terms
    if nx == 1:
        first, last = jnp.where(low, first, 0.0), jnp.where(low, 0.0, last)
    if nx == 1 or j == 0:
        flat[pl.ds(0, planes * edge, stride=edge), :] += first
    if nx == 1 or j == 1:
        flat[pl.ds(edge - 1, planes * edge, stride=edge), :] += last


def moments(planes):
    count, edge = planes.shape[:2]
    zero = jnp.zeros((8, 128), jnp.float32)

    def sum_step(k, carry):
        return carry + jnp.sum(planes[k].reshape(edge * 2, 8, 128), axis=0)

    mean = lax.fori_loop(0, count, sum_step, zero, unroll=True) / (count * edge * edge // 8)

    def spread_step(k, carry):
        off = planes[k].reshape(edge * 2, 8, 128) - mean
        return carry + jnp.sum(off * off, axis=0)

    return mean, lax.fori_loop(0, count, spread_step, zero, unroll=True)


def side_kernel(ny, nx, *refs):
    x, own, y_halos, x_halos, corners, outer, inner, taps, pairs, middle, ends, stats, act, grid, column = refs
    edge = own.shape[0]
    depth = edge + 4
    f32 = jnp.float32
    above, left = Square().low_sides()
    odd = lax.axis_index("gz") % 2 == 1
    act[2 : 2 + edge] = own[...]
    blank = jnp.zeros(grid.shape[:1] + grid.shape[2:], grid.dtype)
    grid[:, 0] = blank
    grid[:, edge + 1] = blank
    faces = in_order(odd, outer[...], inner[...])
    for face, halo_at, own_at, plane, beyond, at, beside, dz in (
        (faces[0], 0, 3, 1, 0, 2, 2, 0),
        (faces[1], 1, 0, edge, edge + 2, edge + 1, 1, 2),
    ):
        grid[halo_at : halo_at + 3, 1 : edge + 1] = face
        grid[own_at, 1 : edge + 1] = x[plane, 1 : edge + 1]

        def put(z, new):
            act[beyond + z : beyond + z + new.shape[0]] = new

        convolve(grid, 2, taps, pairs, put)
        stacked = jnp.concatenate(
            [grid[beside, dy : dy + edge].reshape(edge * edge, 128) for dy in range(3)], axis=1
        )
        wide = jnp.dot(stacked, taps[dz * 384 : dz * 384 + 384, :], preferred_element_type=f32)
        act[at] += join_x(wide.reshape(edge, edge, 384), edge)

    gap = jnp.zeros((2, edge, 128), grid.dtype)
    reached = act.at[1 : depth - 1]
    for i in range(ny):
        line = jnp.concatenate([gap, y_halos[i, 0:edge], gap], axis=0)
        reached[:, jnp.where(above[i], 0, edge - 1)] += y_terms(line, above[i], taps)
    for j in range(nx):
        column[...] = jnp.zeros(column.shape, f32)
        fill_column(
            column, 2, x_halos[j, 0:edge], [corners[i * nx + j, 0] for i in range(ny)], above
        )
        add_column(reached, x_terms(column, taps), j, nx, left[j])
    middle[...] = act[3 : depth - 3]
    ends[0:3] = act[0:3]
    ends[3:6] = act[depth - 3 :]
    mean, spread = moments(act.at[3 : depth - 3])
    stats[0:8] = mean
    stats[8:16] = spread


def end_kernel(ny, nx, middle_stats, ends, outer, inner, taps, act, stats, faces, column):
    edge = act.shape[1]
    wide = ny + nx
    f32 = jnp.float32
    above, left = Square().low_sides()
    odd = lax.axis_index("gz") % 2 == 1
    faces[0], faces[1] = in_order(odd, outer[...], inner[...])
    act[...] = ends[...]
    gap = jnp.zeros((2, edge, 128), faces.dtype)
    for side in range(2):

        def rim(row):
            return jnp.stack([faces[side, k * wide + row] for k in range(3)])

        three = act.at[3 * side : 3 * side + 3]
        for i in range(ny):
            line = [rim(i), gap] if side == 0 else [gap, rim(i)]
            line = jnp.concatenate(line, axis=0)
            three[:, jnp.where(above[i], 0, edge - 1)] += y_terms(line, above[i], taps)
        for j in range(nx):
            column[...] = jnp.zeros(column.shape, f32)
            tails = []
            for i in range(ny):
                tile = faces[side, 3 * wide + i * nx + j].astype(f32)
                tails.append(tile[edge - 3 :] if side == 0 else tile[:3])
            fill_column(column, 0 if side == 0 else 2, rim(ny + j), tails, above)
            add_column(three, x_terms(column, taps), j, nx, left[j])

    mean, spread = moments(act.at[2:4])
    few, many = edge * edge // 4, (edge - 2) * edge * edge // 8
    middle_mean, middle_spread = middle_stats[0:8], middle_stats[8:16]
    off = middle_mean - mean
    part = few / (few + many)
    spread = spread + middle_spread + (many * part) * (off * off)
    put_stats(stats, middle_mean - part * off, spread, few + many)


def merge(mean, spread, rows, other_mean, other_spread):
    off = mean - other_mean
    return 0.5 * (mean + other_mean), spread + other_spread + (0.5 * rows) * (off * off)


def put_stats(stats, mean, spread, rows):
    for step in (1, 2, 4):
        others = pltpu.roll(mean, step, 0), pltpu.roll(spread, step, 0)
        mean, spread = merge(mean, spread, float(rows * step), *others)
    both = jnp.concatenate([mean[0:1], spread[0:1]], axis=0)
    stats[...] = jnp.broadcast_to(both[None], stats.shape)


def read_stats(stats, rows):
    devices, _, channels = stats.shape
    shape = (8, channels)
    means = [jnp.broadcast_to(stats[k, 0:1, :], shape) for k in range(devices)]
    spreads = [jnp.broadcast_to(stats[k, 1:2, :], shape) for k in range(devices)]
    mean = functools.reduce(jnp.add, means) / devices
    spread = functools.reduce(jnp.add, spreads)
    spread = spread + rows * functools.reduce(jnp.add, [(m - mean) * (m - mean) for m in means])
    rows = rows * devices
    lane = lax.broadcasted_iota(jnp.int32, shape, 1)
    step = 1
    while step < channels // GROUPS:
        low = jnp.bitwise_and(lane, step) == 0
        others = [
            jnp.where(low, pltpu.roll(row, channels - step, 1), pltpu.roll(row, step, 1))
            for row in (mean, spread)
        ]
        mean, spread = merge(mean, spread, rows, *others)
        rows, step = 2.0 * rows, 2 * step
    return mean, lax.rsqrt(spread / rows + EPSILON)


def silu_of_double(h):
    return h + h * jnp.tanh(h)


def norm_kernel(ny, nx, inner, ends, stats, gain, offset, out, pooled, *refs):
    y_edges, x_edges, corners, half = refs
    depth, edge = inner.shape[0] + 6, inner.shape[1]
    deep, deep_depth = edge // 2, depth // 2
    f32, bf16 = jnp.float32, jnp.bfloat16
    above, left = Square().low_sides()
    depth_at = lax.axis_index("gz")
    mean, scale = read_stats(stats, float(edge**3))
    scale = scale * (0.5 * gain[...])
    shift = 0.5 * offset[...]
    for k in range(deep_depth):
        value = [
            ends[z] if z < 3 else inner[z - 3] if z < depth - 3 else ends[z - depth + 6]
            for z in (2 * k, 2 * k + 1)
        ]
        value = jnp.stack(value).reshape(edge * edge // 4, 8, 128)
        value = silu_of_double((value - mean) * scale + shift)
        value = value.reshape(2, edge, edge, 128).astype(bf16)
        if 0 < k < deep_depth - 1:
            out[2 * k - 2 : 2 * k] = value
        value = value.astype(f32)
        value = (value[0] + value[1]).reshape(deep, 2, edge, 128)
        half[k] = (value[:, 0] + value[:, 1]).reshape(deep * edge, 128)
        lines = half.at[k]
        pair = lines[pl.ds(0, deep * deep, stride=2), :] + lines[pl.ds(1, deep * deep, stride=2), :]
        pair = (pair * 0.125).astype(bf16).astype(f32).reshape(deep, deep, 128)
        if k == 0 or k == deep_depth - 1:
            inside = depth_at > 0 if k == 0 else depth_at < lax.axis_size("gz") - 1
            pair = jnp.where(inside, pair, 0.0)
        pooled[k] = pair
    lines = pooled.reshape(deep_depth * deep * deep, 128)
    rows = deep_depth * deep
    first_x = lines[pl.ds(0, rows, stride=deep), :]
    last_x = lines[pl.ds(deep - 1, rows, stride=deep), :]
    first_y, last_y = (pooled[:, y].reshape(rows, 128) for y in (0, deep - 1))
    ends = []
    for y in (0, deep - 1):
        for x in (0, deep - 1):
            ends.append(lines[pl.ds(y * deep + x, deep_depth, stride=deep * deep), :])
    if ny == 1:
        above, left = above[0], left[0]
        y_edges[0] = jnp.where(above, first_y, last_y).astype(bf16)
        x_edges[0] = jnp.where(left, first_x, last_x).astype(bf16)
        corners[0, 0:deep_depth] = jnp.where(
            above, jnp.where(left, ends[0], ends[1]), jnp.where(left, ends[2], ends[3])
        )
    else:
        y_edges[0], y_edges[1] = first_y.astype(bf16), last_y.astype(bf16)
        x_edges[0], x_edges[1] = first_x.astype(bf16), last_x.astype(bf16)
        for k in range(4):
            corners[k, 0:deep_depth] = ends[k]


def stack_kernel(*refs):
    out = refs[-1]
    for k in range(out.shape[0]):
        out[k] = refs[k][...]


def stack(*arrays):
    vmem = pl.BlockSpec(memory_space=pltpu.VMEM)
    return pl.pallas_call(
        stack_kernel,
        out_shape=jax.ShapeDtypeStruct((len(arrays),) + arrays[0].shape, arrays[0].dtype),
        in_specs=[vmem] * len(arrays),
        out_specs=vmem,
        compiler_params=pltpu.CompilerParams(vmem_limit_bytes=VMEM_BYTES),
    )(*arrays)


def place_weights(own, held, out):
    tile = lax.axis_index("yx")
    out[tile] = own[...]
    if len(held) == 1:
        pieces, others, size = held[0].shape[:3]
        for piece in range(pieces):
            at = jnp.minimum(jnp.bitwise_xor(Riders.mine(), piece) * size, own.shape[0] - size)
            for k in range(others):
                out[jnp.bitwise_xor(tile, k + 1), pl.ds(at, size)] = held[0][piece, k]
    else:
        for k, shard in enumerate(held):
            out[lax.rem(tile + len(held) - k, len(held) + 1)] = shard[...]


def tap_rows(weight, taps):
    per = weight.shape[1] // 27
    return jnp.concatenate(
        [weight[:, pl.ds(tap * per, per)].reshape(-1, 128) for tap in taps], axis=1
    )


def dot_rows(left, right):
    return lax.dot_general(
        left, right, (((1,), (1,)), ((), ())), preferred_element_type=jnp.float32
    )


def deep_kernel(pooled, own, *refs):
    *held, act, weight, grid, packed = refs
    depth, deep = pooled.shape[0], pooled.shape[1]
    place_weights(own, held, weight)
    grid[...] = jnp.zeros(grid.shape, jnp.float32)
    grid[:, 1 : deep + 1, 8:16] = pooled[...]
    for dx in range(3):
        plane = grid[:, :, 7 + dx : 15 + dx]
        for y in range(deep + 1):
            both = jnp.concatenate([plane[:, y], plane[:, y + 1]], axis=1)
            packed[:, y // 2, y % 2, :, dx * 128 : dx * 128 + 128] = both.astype(jnp.bfloat16)
    rows = deep**3
    total = None
    for dz in range(3):
        left = jnp.concatenate(
            [
                packed[dz : dz + deep, dy // 2 : dy // 2 + deep // 2, dy % 2].reshape(rows, 384)
                for dy in range(3)
            ],
            axis=1,
        )
        term = dot_rows(left, tap_rows(weight, range(dz * 9, dz * 9 + 9)))
        total = term if total is None else total + term
    for half in range(act.shape[0]):
        act[half] = total[:, half * 128 : half * 128 + 128]


def deep_rim_kernel(ny, nx, own, y_halos, x_halos, corners, weight, act, stats, line):
    depth, deep = line.shape[0], line.shape[1] - 16
    halves = act.shape[0]
    f32 = jnp.float32
    square = deep * deep
    above, left = Square().low_sides()
    act[...] = own[...]
    flat = line.reshape(depth * line.shape[1], 128)

    def shifts():
        return jnp.concatenate(
            [
                line[dz : dz + deep, 7 + d : 7 + d + deep].reshape(square, 128).astype(jnp.bfloat16)
                for dz in range(3)
                for d in range(3)
            ],
            axis=1,
        )

    for i in range(ny):
        line[...] = jnp.zeros(line.shape, f32)
        line[:, 8 : 8 + deep] = y_halos[i].astype(f32).reshape(depth, deep, 128)
        for j in range(nx):
            end = corners[i * nx + j, 0:depth]
            first, last = jnp.where(left[j], end, 0.0), jnp.where(left[j], 0.0, end)
            if nx == 1 or j == 0:
                flat[pl.ds(7, depth, stride=line.shape[1]), :] = first
            if nx == 1 or j == 1:
                flat[pl.ds(8 + deep, depth, stride=line.shape[1]), :] = last
        tap = jnp.where(above[i], 0, 6)
        taps = [tap + dz * 9 + dx for dz in range(3) for dx in range(3)]
        terms = dot_rows(shifts(), tap_rows(weight, taps))
        for half in range(halves):
            rows = act.at[half].reshape(deep, deep, deep, 128)
            term = terms[:, half * 128 : half * 128 + 128].reshape(deep, deep, 128)
            rows[:, jnp.where(above[i], 0, deep - 1)] += term
    for j in range(nx):
        line[...] = jnp.zeros(line.shape, f32)
        line[:, 8 : 8 + deep] = x_halos[j].astype(f32).reshape(depth, deep, 128)
        tap = jnp.where(left[j], 0, 2)
        taps = [tap + dz * 9 + dy * 3 for dz in range(3) for dy in range(3)]
        terms = dot_rows(shifts(), tap_rows(weight, taps))
        first, last = jnp.where(left[j], terms, 0.0), jnp.where(left[j], 0.0, terms)
        for half in range(halves):
            lanes, rows = slice(half * 128, half * 128 + 128), act.at[half]
            if nx == 1 or j == 0:
                rows[pl.ds(0, square, stride=deep), :] += first[:, lanes]
            if nx == 1 or j == 1:
                rows[pl.ds(deep - 1, square, stride=deep), :] += last[:, lanes]

    rows = deep**3 // 8
    means, spreads = [], []
    for half in range(halves):
        total = act[half].reshape(rows, 8, 128)
        means.append(jnp.sum(total, axis=0) / rows)
        off = total - means[-1]
        spreads.append(jnp.sum(off * off, axis=0))
    put_stats(stats, *(jnp.concatenate(part, axis=1) for part in (means, spreads)), rows)


def final_kernel(act, stats, gain, offset, up, mid, out, wide, held, sems):
    edge = mid.shape[0]
    deep = edge // 2
    f32 = jnp.float32
    mean, scale = read_stats(stats, float(deep**3))
    scale = scale * (0.5 * gain[...])
    shift = 0.5 * offset[...]
    planes = 2
    size = planes * deep * deep
    copies = []
    for k in range(0, deep, planes):
        at = slice(k * deep * deep, k * deep * deep + size)
        value = jnp.concatenate([act[half, at] for half in range(act.shape[0])], axis=1)
        value = value.reshape(size // 8, 8, -1)
        value = silu_of_double((value - mean) * scale + shift)
        value = value.reshape(size, -1).astype(jnp.bfloat16)
        lifted = jnp.dot(value, up[...], preferred_element_type=f32)
        lines = wide.at[k // planes]
        lines[pl.ds(0, size, stride=2), :] = lifted
        lines[pl.ds(1, size, stride=2), :] = lifted
        add = lines[...].reshape(planes, 1, deep, 1, edge, 128)
        at = pl.ds(2 * k, 2 * planes)
        old = mid[at].astype(f32).reshape(planes, 2, deep, 2, edge, 128)
        held[at] = (old + add).astype(jnp.bfloat16).reshape(2 * planes, edge, edge, 128)
        copy = pltpu.make_async_copy(held.at[at], out.at[at], sems.at[k // planes])
        copy.start()
        copies.append(copy)
    for copy in copies:
        copy.wait()


def body(
    features, conv_weight, gain_mid, offset_mid, deep_weight, gain_deep, offset_deep, up_weight
):
    f32, bf16 = jnp.float32, jnp.bfloat16
    edge, channels = features.shape[0], features.shape[3]
    deep = edge // 2
    deep_channels = gain_deep.shape[0]
    square = Square()
    tiles = square.tiles
    devices = lax.axis_size("gz") * tiles
    ny, nx = (len(sides) for sides in square.low_sides())
    riders = Riders(deep_weight.shape[4])

    own = jnp.moveaxis(deep_weight, 4, 3).reshape(-1, 16, channels)
    conv_weight = conv_weight.reshape(27, channels, channels)
    three = ((3, edge, edge, channels), bf16)
    *edges, outer, inner, field, conv_weight = call(
        functools.partial(start_kernel, ny, nx, riders.size),
        [
            ((ny, edge + riders.size, edge, channels), bf16),
            ((nx, edge + riders.size, edge, channels), bf16),
            ((ny * nx, 1 + riders.size, edge, channels), bf16),
            three,
            three,
            ((edge + 2, edge + 2, edge, channels), bf16),
            (conv_weight.shape, bf16),
        ],
        [((nx, edge * edge, 8, channels), f32), pltpu.SemaphoreType.DMA((8,))],
        features,
        conv_weight,
        own,
        nbytes=5 << 20,
        in_hbm=3,
    )
    halos = square.halos(*(list(piece) for piece in edges))
    outer, inner = swap_depth(outer, inner)
    conv_flops = 54 * channels * channels * edge**3
    act, taps, pairs, own = call(
        conv_kernel,
        [
            ((edge, edge, edge, channels), f32),
            ((9 * channels, 3 * channels), bf16),
            ((12 * channels, 2 * channels), bf16),
            (own.shape, bf16),
        ],
        [pltpu.SemaphoreType.DMA],
        own,
        field,
        conv_weight,
        flops=conv_flops,
        nbytes=6 << 20,
        in_hbm=1,
    )
    (y, x, corner), act = lax.optimization_barrier((halos, act))
    y, x, corner = jnp.stack(y), jnp.stack(x), jnp.stack(corner)
    turn = ((3 * (ny + nx) + ny * nx, edge, channels), bf16)
    held = [((3, riders.size, 16, channels), bf16)] if riders.size else []
    turns = call(
        functools.partial(turn_kernel, ny, nx, riders.size), [turn, turn] + held, [], y, x, corner
    )
    turns, held = swap_depth(*turns[:2]), turns[2:]
    if riders.size:
        held = held[0][None]
        other = swap(held, *riders.STEPS[0])
    else:
        held = rotate_shards(own)
    six = ((6, edge, edge, channels), f32)
    column = (edge + 16, channels)
    middle, ends, stats = call(
        functools.partial(side_kernel, ny, nx),
        [((edge - 2, edge, edge, channels), f32), six, ((16, channels), f32)],
        [
            ((edge + 4, edge, edge, channels), f32),
            ((4, edge + 2, edge, channels), bf16),
            ((edge + 4,) + column, f32),
        ],
        field,
        act,
        y,
        x,
        corner,
        outer,
        inner,
        taps,
        pairs,
    )
    ends, stats = call(
        functools.partial(end_kernel, ny, nx),
        [six, ((devices, 2, channels), f32)],
        [((2,) + turn[0], bf16), ((5,) + column, f32)],
        stats,
        ends,
        *turns,
        taps,
    )
    if riders.size:
        stats, other = lax.optimization_barrier((stats, other))
        held = stack(held, other).reshape((-1,) + held.shape[1:])
        other = swap(held, *riders.STEPS[1])
        stats = share(stats)
        stats, other = lax.optimization_barrier((stats, other))
        held = stack(held, other).reshape((-1,) + held.shape[1:])
        other = swap(held, *riders.STEPS[2])
        held = [stack(held, other).reshape((-1,) + held.shape[1:])]
    else:
        stats = share(stats)
    out, pooled, *edges = call(
        functools.partial(norm_kernel, ny, nx),
        [
            ((edge, edge, edge, channels), bf16),
            ((deep + 2, deep, deep, channels), f32),
            ((ny, (deep + 2) * deep, channels), bf16),
            ((nx, (deep + 2) * deep, channels), bf16),
            ((ny * nx, 16, channels), f32),
        ],
        [((deep + 2, deep * edge, channels), f32)],
        middle,
        ends,
        stats,
        gain_mid.reshape(1, channels),
        offset_mid.reshape(1, channels),
        flops=20 * channels * edge**3,
        nbytes=3 << 20,
    )
    y, x, corner = square.halos(*(list(piece) for piece in edges))
    halves = ((deep_channels // 128, deep**3, 128), f32)
    deep_act, weight = call(
        deep_kernel,
        [halves, ((tiles,) + own.shape, bf16)],
        [
            ((deep + 2, deep + 2, 24, channels), f32),
            ((deep + 2, deep // 2 + 1, 2, 16, 3 * channels), bf16),
        ],
        pooled,
        own,
        *held,
        flops=54 * channels * deep_channels * deep**3,
        nbytes=4 << 20,
    )
    deep_act, stats = call(
        functools.partial(deep_rim_kernel, ny, nx),
        [halves, ((devices, 2, deep_channels), f32)],
        [((deep + 2, 24, channels), f32)],
        deep_act,
        jnp.stack(y),
        jnp.stack(x),
        jnp.stack(corner),
        weight,
        flops=4 * channels * deep_channels * deep**3,
        nbytes=3 << 20,
    )
    stats = share(stats)
    (decoded,) = call(
        final_kernel,
        [((edge, edge, edge, channels), bf16)],
        [
            ((deep // 2, 4 * deep * deep, channels), f32),
            ((edge, edge, edge, channels), bf16),
            pltpu.SemaphoreType.DMA((deep // 2,)),
        ],
        deep_act,
        stats,
        gain_deep.reshape(1, deep_channels),
        offset_deep.reshape(1, deep_channels),
        up_weight,
        out,
        flops=4 * deep_channels * channels * deep**3,
        nbytes=3 << 20,
        out_hbm=True,
    )
    return decoded


def solution(mesh):
    placed = (
        P(("cand", "gz"), "yx", None, None),
        P(),
        P(),
        P(),
        P(None, None, None, None, "yx"),
        P(),
        P(),
        P(),
    )
    return jax.shard_map(
        body,
        mesh=mesh,
        in_specs=placed,
        out_specs=P(("cand", "gz"), "yx", None, None),
        check_vma=False,
    )
```

```python
import functools
import math

import jax
import jax.numpy as jnp
from jax import lax
from jax.experimental import pallas as pl
from jax.experimental.pallas import tpu as pltpu
from jax.sharding import PartitionSpec as P

GROUPS = 32
EPSILON = 1e-05
PART = ("gz", "yx")
VMEM_BYTES = 32 * 1024 * 1024


class Square:
    def __init__(self):
        self.tiles = lax.axis_size("yx")
        self.side = math.isqrt(self.tiles)
        tile = lax.axis_index("yx")
        self.row, self.column = tile // self.side, tile % self.side
        self.folded = self.side == 2
        self.steps = (0,) if self.folded else (-1, 1)

    def low_sides(self):
        if self.folded:
            return [self.row == 1], [self.column == 1]
        return [True, False], [True, False]

    def route(self, down, right):
        pairs = []
        for tile in range(self.tiles):
            row, column = tile // self.side + down, tile % self.side + right
            if 0 <= row < self.side and 0 <= column < self.side:
                pairs.append((tile, row * self.side + column))
        return pairs

    def swap_route(self, mask):
        return [(tile, tile ^ mask) for tile in range(self.tiles)]

    def halos(self, y_edges, x_edges, corners):
        if self.folded:
            y = lax.ppermute(y_edges[0], "yx", self.swap_route(2))
            x = lax.ppermute(x_edges[0], "yx", self.swap_route(1))
            corner = lax.ppermute(corners[0], "yx", self.swap_route(3))
            return [y], [x], [corner]
        y = [lax.ppermute(y_edges[k], "yx", self.route((1, -1)[1 - k], 0)) for k in (1, 0)]
        x = [lax.ppermute(x_edges[k], "yx", self.route(0, (1, -1)[1 - k])) for k in (1, 0)]
        corner = [
            lax.ppermute(corners[2 * k + j], "yx", self.route((1, -1)[1 - k], (1, -1)[1 - j]))
            for k in (1, 0)
            for j in (1, 0)
        ]
        return y, x, corner


def swap_depth(outer, inner):
    size = lax.axis_size("gz")
    routes = [[], []]
    for low in range(size - 1):
        routes[low % 2] += [(low, low + 1), (low + 1, low)]
    inner = lax.ppermute(inner, "gz", routes[0])
    return lax.ppermute(outer, "gz", routes[1]), inner


class Riders:
    STEPS = (("gz", 2), ("cand", 1), ("gz", 1))

    def __init__(self, rows):
        self.tiles = 27 * rows // 16
        self.fits = (
            lax.axis_size("yx") == 4
            and lax.axis_size("cand") % 2 == 0
            and lax.axis_size("gz") % 4 == 0
            and self.tiles >= 8
        )
        self.size = -(-self.tiles // 8) if self.fits else 0

    @classmethod
    def mine(cls):
        return sum(
            lax.axis_index(axis) // mask % 2 * 2**k for k, (axis, mask) in enumerate(cls.STEPS)
        )


def rotate_shards(piece):
    tiles = lax.axis_size("yx")
    return [
        lax.ppermute(piece, "yx", [(i, (i + k) % tiles) for i in range(tiles)]) for k in range(1, tiles)
    ]


def swap(block, axis, mask):
    return lax.ppermute(block, axis, [(i, i ^ mask) for i in range(lax.axis_size(axis))])


def share(stats):
    return lax.all_to_all(stats, PART, 0, 0)


def call(kernel, outs, scratch, *arrays, flops=0, nbytes=0, in_hbm=0, out_hbm=False):
    vmem, hbm = (pl.BlockSpec(memory_space=space) for space in (pltpu.VMEM, pltpu.HBM))
    far, near = arrays[:in_hbm], arrays[in_hbm:]
    far = [pltpu.with_memory_space_constraint(array, pltpu.HBM) for array in far]
    return pl.pallas_call(
        kernel,
        out_shape=[jax.ShapeDtypeStruct(shape, dtype) for shape, dtype in outs],
        in_specs=[hbm] * len(far) + [vmem] * len(near),
        out_specs=[hbm if out_hbm else vmem] * len(outs),
        scratch_shapes=[pltpu.VMEM(*entry) if isinstance(entry, tuple) else entry for entry in scratch],
        compiler_params=pltpu.CompilerParams(vmem_limit_bytes=VMEM_BYTES),
        cost_estimate=pl.CostEstimate(flops=flops, bytes_accessed=nbytes, transcendentals=0),
    )(*far, *near)


def start_kernel(ny, nx, size, x_in, w_in, d_in, y_out, x_out, corners, outer, inner, x, w, lines, sems):
    edge = x_in.shape[0]
    f32, bf16 = jnp.float32, jnp.bfloat16
    above, left = Square().low_sides()
    chunks = 4
    planes = edge // chunks
    first = [
        pltpu.make_async_copy(
            x_in.at[pl.ds(k * planes, planes)],
            x.at[pl.ds(1 + k * planes, planes), pl.ds(1, edge)],
            sems.at[k],
        )
        for k in range(chunks)
    ]
    later = []
    if size:
        at = jnp.minimum(Riders.mine() * size, d_in.shape[0] - size)
        for k, (out, begin) in enumerate(((y_out, edge), (x_out, edge), (corners, 1))):
            later.append(
                pltpu.make_async_copy(
                    d_in.at[pl.ds(at, size)], out.at[0, pl.ds(begin, size)], sems.at[chunks + k]
                )
            )
    later.append(pltpu.make_async_copy(w_in, w, sems.at[chunks + 3]))
    for copy in first + later:
        copy.start()
    x[0] = jnp.zeros(x.shape[1:], bf16)
    x[edge + 1] = jnp.zeros(x.shape[1:], bf16)
    blank = jnp.zeros((edge,) + x.shape[2:], bf16)
    x[1 : edge + 1, 0] = blank
    x[1 : edge + 1, edge + 1] = blank
    flat = lines.reshape(nx * edge * edge * 8, 128)
    part = planes * edge
    for k in range(chunks):
        first[k].wait()
        at, here = pl.ds(k * planes, planes), pl.ds(1 + k * planes, planes)
        for i in range(ny):
            row = jnp.where(above[i], 1, edge)
            y_out[i, at] = x[here, row]
        for j in range(nx):
            low = x[here, 1 : edge + 1, 0:8].astype(f32).reshape(part, 8, 128)
            high = x[here, 1 : edge + 1, edge - 8 : edge].astype(f32).reshape(part, 8, 128)
            high = pltpu.roll(high, 1, 1)
            kept = jnp.where(left[j], low, high)
            lines[j, k * part : k * part + part] = kept
            begin = (j * edge * edge + k * part) * 8
            column = flat[pl.ds(begin, part, stride=8), :]
            x_out[j, at] = column.astype(bf16).reshape(planes, edge, 128)
    for i in range(ny):
        for j in range(nx):
            begin = j * edge * edge * 8
            low = flat[pl.ds(begin, edge, stride=8 * edge), :]
            high = flat[pl.ds(begin + 8 * (edge - 1), edge, stride=8 * edge), :]
            kept = jnp.where(above[i], low, high)
            corners[i * nx + j, 0] = kept.astype(bf16)
    odd, far = lax.axis_index("gz") % 2, edge - 3
    for face, at in ((outer, odd * far), (inner, (1 - odd) * far)):
        for k in range(3):
            face[k] = x[1 + at + k, 1 : edge + 1]
    for copy in later:
        copy.wait()


def turn_kernel(ny, nx, size, y_halos, x_halos, corners, outer, inner, *riders):
    edge = outer.shape[1]
    wide = ny + nx
    odd, far = lax.axis_index("gz") % 2, edge - 3
    for face, at in ((outer, odd * far), (inner, (1 - odd) * far)):
        for k in range(3):
            row = k * wide
            for i in range(ny):
                face[row + i] = y_halos[i, at + k]
            for j in range(nx):
                face[row + ny + j] = x_halos[j, at + k]
        for k in range(ny * nx):
            face[3 * wide + k] = corners[k, 0]
    if size:
        riders[0][0] = x_halos[0, edge : edge + size]
        riders[0][1] = y_halos[0, edge : edge + size]
        riders[0][2] = corners[0, 1 : 1 + size]


def in_order(odd, outer, inner):
    return jnp.where(odd, inner, outer), jnp.where(odd, outer, inner)


def spread_taps(weight, taps):
    for tap in range(27):
        row, lane = tap // 3 * 128, tap % 3 * 128
        taps[row : row + 128, lane : lane + 128] = weight[tap]


def pair_taps(weight, pairs):
    for dz in range(3):
        for line in range(4):
            row = (dz * 4 + line) * 128
            for out in range(2):
                lane = out * 128
                if 0 <= line - out < 3:
                    block = weight[dz * 9 + (line - out) * 3 + 2]
                else:
                    block = jnp.zeros((128, 128), pairs.dtype)
                pairs[row : row + 128, lane : lane + 128] = block


def join_x(wide, edge):
    place = lax.broadcasted_iota(jnp.int32, wide.shape[:2] + (128,), 1)
    after = jnp.where(place > 0, pltpu.roll(wide[:, :, :128], 1, 1), 0.0)
    before = jnp.where(place < edge - 1, pltpu.roll(wide[:, :, 256:], edge - 1, 1), 0.0)
    return wide[:, :, 128:256] + after + before


def convolve(grid, count, taps, pairs, put):
    edge = grid.shape[2]
    planes = min(count, 4)
    rows = planes * edge * edge
    place = lax.broadcasted_iota(jnp.int32, (planes * edge, edge, 128), 1)
    halved = grid.reshape(grid.shape[0], edge // 2 + 1, 2, edge, 128)
    for z in range(0, count, planes):
        left = jnp.concatenate(
            [
                grid[z + dz : z + dz + planes, dy : dy + edge].reshape(rows, 128)
                for dz in range(3)
                for dy in range(3)
            ],
            axis=1,
        )
        wide = jnp.dot(left, taps[:, 0:256], preferred_element_type=jnp.float32)
        wide = wide.reshape(planes * edge, edge, 256)
        left = jnp.concatenate(
            [
                halved[z + dz : z + dz + planes, line // 2 : line // 2 + edge // 2, line % 2].reshape(
                    rows // 2, 128
                )
                for dz in range(3)
                for line in range(4)
            ],
            axis=1,
        )
        two = jnp.dot(left, pairs[...], preferred_element_type=jnp.float32)
        two = two.reshape(planes * edge // 2, edge, 256)
        two = jnp.stack([two[:, :, :128], two[:, :, 128:]], axis=1).reshape(planes * edge, edge, 128)
        after = jnp.where(place > 0, pltpu.roll(wide[:, :, :128], 1, 1), 0.0)
        before = jnp.where(place < edge - 1, pltpu.roll(two, edge - 1, 1), 0.0)
        new = wide[:, :, 128:256] + after + before
        put(z, new.reshape(planes, edge, edge, 128))


def conv_kernel(deep_in, x, weight, act, taps, pairs, deep_weight, sem):
    copy = pltpu.make_async_copy(deep_in, deep_weight, sem)
    copy.start()
    edge = act.shape[0]
    spread_taps(weight, taps)
    pair_taps(weight, pairs)

    def put(z, new):
        act[z : z + new.shape[0]] = new

    convolve(x, edge, taps, pairs, put)
    copy.wait()


def y_terms(line, low, taps):
    planes, edge = line.shape[0] - 2, line.shape[1]
    left = jnp.concatenate(
        [line[dz : dz + planes].reshape(planes * edge, 128) for dz in range(3)], axis=1
    )
    start = jnp.where(low, 0, 256)
    right = jnp.concatenate(
        [taps[pl.ds(pl.multiple_of(start + dz * 384, 128), 128), :] for dz in range(3)], axis=0
    )
    wide = jnp.dot(left, right, preferred_element_type=jnp.float32)
    return join_x(wide.reshape(planes, edge, 384), edge)


def x_terms(column, taps):
    planes, edge = column.shape[0] - 2, column.shape[1] - 16
    lines = [column[:, 7 + dy : 7 + dy + edge].astype(jnp.bfloat16) for dy in range(3)]
    left = jnp.concatenate(
        [line[dz : dz + planes].reshape(planes * edge, 128) for dz in range(3) for line in lines],
        axis=1,
    )
    right = jnp.concatenate([taps[:, 0:128], taps[:, 256:384]], axis=1)
    both = jnp.dot(left, right, preferred_element_type=jnp.float32)
    return both[:, :128], both[:, 128:]


def fill_column(column, at, voxels, ends, above):
    count, edge = voxels.shape[:2]
    rows = edge + 16
    lines = column.reshape(column.shape[0] * rows, 128)
    column[at : at + count, 8 : 8 + edge] = voxels.astype(jnp.float32)
    for i, end in enumerate(ends):
        first = last = end.astype(jnp.float32)
        if len(ends) == 1:
            first, last = jnp.where(above[0], first, 0.0), jnp.where(above[0], 0.0, last)
        if len(ends) == 1 or i == 0:
            lines[pl.ds(at * rows + 7, count, stride=rows), :] = first
        if len(ends) == 1 or i == 1:
            lines[pl.ds(at * rows + 8 + edge, count, stride=rows), :] = last


def add_column(act, terms, j, nx, low):
    planes, edge = act.shape[:2]
    flat = act.reshape(planes * edge * edge, 128)
    first, last = terms
    if nx == 1:
        first, last = jnp.where(low, first, 0.0), jnp.where(low, 0.0, last)
    if nx == 1 or j == 0:
        flat[pl.ds(0, planes * edge, stride=edge), :] += first
    if nx == 1 or j == 1:
        flat[pl.ds(edge - 1, planes * edge, stride=edge), :] += last


def moments(planes):
    count, edge = planes.shape[:2]
    zero = jnp.zeros((8, 128), jnp.float32)

    def sum_step(k, carry):
        return carry + jnp.sum(planes[k].reshape(edge * 2, 8, 128), axis=0)

    mean = lax.fori_loop(0, count, sum_step, zero, unroll=True) / (count * edge * edge // 8)

    def spread_step(k, carry):
        off = planes[k].reshape(edge * 2, 8, 128) - mean
        return carry + jnp.sum(off * off, axis=0)

    return mean, lax.fori_loop(0, count, spread_step, zero, unroll=True)


def side_kernel(ny, nx, *refs):
    x, own, y_halos, x_halos, corners, inner, outer, taps, pairs, middle, ends, stats, act, grid, column = refs
    edge = own.shape[0]
    depth = edge + 4
    f32 = jnp.float32
    above, left = Square().low_sides()
    odd = lax.axis_index("gz") % 2 == 1
    act[2 : 2 + edge] = own[...]
    blank = jnp.zeros(grid.shape[:1] + grid.shape[2:], grid.dtype)
    grid[:, 0] = blank
    grid[:, edge + 1] = blank
    faces = in_order(odd, outer[...], inner[...])
    for face, halo_at, own_at, plane, beyond, at, beside, dz in (
        (faces[0], 0, 3, 1, 0, 2, 2, 0),
        (faces[1], 1, 0, edge, edge + 2, edge + 1, 1, 2),
    ):
        grid[halo_at : halo_at + 3, 1 : edge + 1] = face
        grid[own_at, 1 : edge + 1] = x[plane, 1 : edge + 1]

        def put(z, new):
            act[beyond + z : beyond + z + new.shape[0]] = new

        convolve(grid, 2, taps, pairs, put)
        stacked = jnp.concatenate(
            [grid[beside, dy : dy + edge].reshape(edge * edge, 128) for dy in range(3)], axis=1
        )
        wide = jnp.dot(stacked, taps[dz * 384 : dz * 384 + 384, :], preferred_element_type=f32)
        act[at] += join_x(wide.reshape(edge, edge, 384), edge)

    gap = jnp.zeros((2, edge, 128), grid.dtype)
    reached = act.at[1 : depth - 1]
    for i in range(ny):
        line = jnp.concatenate([gap, y_halos[i, 0:edge], gap], axis=0)
        reached[:, jnp.where(above[i], 0, edge - 1)] += y_terms(line, above[i], taps)
    for j in range(nx):
        column[...] = jnp.zeros(column.shape, f32)
        fill_column(
            column, 2, x_halos[j, 0:edge], [corners[i * nx + j, 0] for i in range(ny)], above
        )
        add_column(reached, x_terms(column, taps), j, nx, left[j])
    middle[...] = act[3 : depth - 3]
    ends[0:3] = act[0:3]
    ends[3:6] = act[depth - 3 :]
    mean, spread = moments(act.at[3 : depth - 3])
    stats[0:8] = mean
    stats[8:16] = spread


def end_kernel(ny, nx, middle_stats, ends, inner, outer, taps, act, stats, faces, column):
    edge = act.shape[1]
    wide = ny + nx
    f32 = jnp.float32
    above, left = Square().low_sides()
    odd = lax.axis_index("gz") % 2 == 1
    faces[0], faces[1] = in_order(odd, outer[...], inner[...])
    act[...] = ends[...]
    gap = jnp.zeros((2, edge, 128), faces.dtype)
    for side in range(2):

        def rim(row):
            return jnp.stack([faces[side, k * wide + row] for k in range(3)])

        three = act.at[3 * side : 3 * side + 3]
        for i in range(ny):
            line = [rim(i), gap] if side == 0 else [gap, rim(i)]
            line = jnp.concatenate(line, axis=0)
            three[:, jnp.where(above[i], 0, edge - 1)] += y_terms(line, above[i], taps)
        for j in range(nx):
            column[...] = jnp.zeros(column.shape, f32)
            tails = []
            for i in range(ny):
                tile = faces[side, 3 * wide + i * nx + j].astype(f32)
                tails.append(tile[edge - 3 :] if side == 0 else tile[:3])
            fill_column(column, 0 if side == 0 else 2, rim(ny + j), tails, above)
            add_column(three, x_terms(column, taps), j, nx, left[j])

    mean, spread = moments(act.at[2:4])
    few, many = edge * edge // 4, (edge - 2) * edge * edge // 8
    middle_mean, middle_spread = middle_stats[0:8], middle_stats[8:16]
    off = middle_mean - mean
    part = few / (few + many)
    spread = spread + middle_spread + (many * part) * (off * off)
    put_stats(stats, middle_mean - part * off, spread, few + many)


def merge(mean, spread, rows, other_mean, other_spread):
    off = mean - other_mean
    return 0.5 * (mean + other_mean), spread + other_spread + (0.5 * rows) * (off * off)


def put_stats(stats, mean, spread, rows):
    for step in (1, 2, 4):
        others = pltpu.roll(mean, step, 0), pltpu.roll(spread, step, 0)
        mean, spread = merge(mean, spread, float(rows * step), *others)
    both = jnp.concatenate([mean[0:1], spread[0:1]], axis=0)
    stats[...] = jnp.broadcast_to(both[None], stats.shape)


def read_stats(stats, rows):
    devices, _, channels = stats.shape
    shape = (8, channels)
    means = [jnp.broadcast_to(stats[k, 0:1, :], shape) for k in range(devices)]
    spreads = [jnp.broadcast_to(stats[k, 1:2, :], shape) for k in range(devices)]
    mean = functools.reduce(jnp.add, means) / devices
    spread = functools.reduce(jnp.add, spreads)
    spread = spread + rows * functools.reduce(jnp.add, [(m - mean) * (m - mean) for m in means])
    rows = rows * devices
    lane = lax.broadcasted_iota(jnp.int32, shape, 1)
    step = 1
    while step < channels // GROUPS:
        low = jnp.bitwise_and(lane, step) == 0
        others = [
            jnp.where(low, pltpu.roll(row, channels - step, 1), pltpu.roll(row, step, 1))
            for row in (mean, spread)
        ]
        mean, spread = merge(mean, spread, rows, *others)
        rows, step = 2.0 * rows, 2 * step
    return mean, lax.rsqrt(spread / rows + EPSILON)


def silu_of_double(h):
    return h + h * jnp.tanh(h)


def norm_kernel(ny, nx, inner, ends, stats, gain, offset, out, pooled, *refs):
    y_edges, x_edges, corners, half = refs
    depth, edge = inner.shape[0] + 6, inner.shape[1]
    deep, deep_depth = edge // 2, depth // 2
    f32, bf16 = jnp.float32, jnp.bfloat16
    above, left = Square().low_sides()
    depth_at = lax.axis_index("gz")
    mean, scale = read_stats(stats, float(edge**3))
    scale = scale * (0.5 * gain[...])
    shift = 0.5 * offset[...]
    for k in range(deep_depth):
        value = [
            ends[z] if z < 3 else inner[z - 3] if z < depth - 3 else ends[z - depth + 6]
            for z in (2 * k, 2 * k + 1)
        ]
        value = jnp.stack(value).reshape(edge * edge // 4, 8, 128)
        value = silu_of_double((value - mean) * scale + shift)
        value = value.reshape(2, edge, edge, 128).astype(bf16)
        if 0 < k < deep_depth - 1:
            out[2 * k - 2 : 2 * k] = value
        value = value.astype(f32)
        value = (value[0] + value[1]).reshape(deep, 2, edge, 128)
        half[k] = (value[:, 0] + value[:, 1]).reshape(deep * edge, 128)
        lines = half.at[k]
        pair = lines[pl.ds(0, deep * deep, stride=2), :] + lines[pl.ds(1, deep * deep, stride=2), :]
        pair = (pair * 0.125).astype(bf16).astype(f32).reshape(deep, deep, 128)
        if k == 0 or k == deep_depth - 1:
            inside = depth_at > 0 if k == 0 else depth_at < lax.axis_size("gz") - 1
            pair = jnp.where(inside, pair, 0.0)
        pooled[k] = pair
    lines = pooled.reshape(deep_depth * deep * deep, 128)
    rows = deep_depth * deep
    first_x = lines[pl.ds(0, rows, stride=deep), :]
    last_x = lines[pl.ds(deep - 1, rows, stride=deep), :]
    first_y, last_y = (pooled[:, y].reshape(rows, 128) for y in (0, deep - 1))
    ends = []
    for y in (0, deep - 1):
        for x in (0, deep - 1):
            ends.append(lines[pl.ds(y * deep + x, deep_depth, stride=deep * deep), :])
    if ny == 1:
        above, left = above[0], left[0]
        y_edges[0] = jnp.where(above, first_y, last_y).astype(bf16)
        x_edges[0] = jnp.where(left, first_x, last_x).astype(bf16)
        corners[0, 0:deep_depth] = jnp.where(
            above, jnp.where(left, ends[0], ends[1]), jnp.where(left, ends[2], ends[3])
        )
    else:
        y_edges[0], y_edges[1] = first_y.astype(bf16), last_y.astype(bf16)
        x_edges[0], x_edges[1] = first_x.astype(bf16), last_x.astype(bf16)
        for k in range(4):
            corners[k, 0:deep_depth] = ends[k]


def stack_kernel(*refs):
    out = refs[-1]
    for k in range(out.shape[0]):
        out[k] = refs[k][...]


def stack(*arrays):
    vmem = pl.BlockSpec(memory_space=pltpu.VMEM)
    return pl.pallas_call(
        stack_kernel,
        out_shape=jax.ShapeDtypeStruct((len(arrays),) + arrays[0].shape, arrays[0].dtype),
        in_specs=[vmem] * len(arrays),
        out_specs=vmem,
        compiler_params=pltpu.CompilerParams(vmem_limit_bytes=VMEM_BYTES),
    )(*arrays)


def place_weights(own, held, out):
    tile = lax.axis_index("yx")
    out[tile] = own[...]
    if len(held) == 1:
        pieces, others, size = held[0].shape[:3]
        for piece in range(pieces):
            at = jnp.minimum(jnp.bitwise_xor(Riders.mine(), piece) * size, own.shape[0] - size)
            for k in range(others):
                out[jnp.bitwise_xor(tile, k + 1), pl.ds(at, size)] = held[0][piece, k]
    else:
        for k, shard in enumerate(held):
            out[lax.rem(tile + len(held) - k, len(held) + 1)] = shard[...]


def tap_rows(weight, taps):
    per = weight.shape[1] // 27
    return jnp.concatenate(
        [weight[:, pl.ds(tap * per, per)].reshape(-1, 128) for tap in taps], axis=1
    )


def dot_rows(left, right):
    return lax.dot_general(
        left, right, (((1,), (1,)), ((), ())), preferred_element_type=jnp.float32
    )


def deep_kernel(pooled, own, *refs):
    *held, act, weight, grid, packed = refs
    depth, deep = pooled.shape[0], pooled.shape[1]
    place_weights(own, held, weight)
    grid[...] = jnp.zeros(grid.shape, jnp.float32)
    grid[:, 1 : deep + 1, 8:16] = pooled[...]
    for dx in range(3):
        plane = grid[:, :, 7 + dx : 15 + dx]
        for y in range(deep + 1):
            both = jnp.concatenate([plane[:, y], plane[:, y + 1]], axis=1)
            packed[:, y // 2, y % 2, :, dx * 128 : dx * 128 + 128] = both.astype(jnp.bfloat16)
    rows = deep**3
    total = None
    for dz in range(3):
        left = jnp.concatenate(
            [
                packed[dz : dz + deep, dy // 2 : dy // 2 + deep // 2, dy % 2].reshape(rows, 384)
                for dy in range(3)
            ],
            axis=1,
        )
        term = dot_rows(left, tap_rows(weight, range(dz * 9, dz * 9 + 9)))
        total = term if total is None else total + term
    for half in range(act.shape[0]):
        act[half] = total[:, half * 128 : half * 128 + 128]


def deep_rim_kernel(ny, nx, own, y_halos, x_halos, corners, weight, act, stats, line):
    depth, deep = line.shape[0], line.shape[1] - 16
    halves = act.shape[0]
    f32 = jnp.float32
    square = deep * deep
    above, left = Square().low_sides()
    act[...] = own[...]
    flat = line.reshape(depth * line.shape[1], 128)

    def shifts():
        return jnp.concatenate(
            [
                line[dz : dz + deep, 7 + d : 7 + d + deep].reshape(square, 128).astype(jnp.bfloat16)
                for dz in range(3)
                for d in range(3)
            ],
            axis=1,
        )

    for i in range(ny):
        line[...] = jnp.zeros(line.shape, f32)
        line[:, 8 : 8 + deep] = y_halos[i].astype(f32).reshape(depth, deep, 128)
        for j in range(nx):
            end = corners[i * nx + j, 0:depth]
            first, last = jnp.where(left[j], end, 0.0), jnp.where(left[j], 0.0, end)
            if nx == 1 or j == 0:
                flat[pl.ds(7, depth, stride=line.shape[1]), :] = first
            if nx == 1 or j == 1:
                flat[pl.ds(8 + deep, depth, stride=line.shape[1]), :] = last
        tap = jnp.where(above[i], 0, 6)
        taps = [tap + dz * 9 + dx for dz in range(3) for dx in range(3)]
        terms = dot_rows(shifts(), tap_rows(weight, taps))
        for half in range(halves):
            rows = act.at[half].reshape(deep, deep, deep, 128)
            term = terms[:, half * 128 : half * 128 + 128].reshape(deep, deep, 128)
            rows[:, jnp.where(above[i], 0, deep - 1)] += term
    for j in range(nx):
        line[...] = jnp.zeros(line.shape, f32)
        line[:, 8 : 8 + deep] = x_halos[j].astype(f32).reshape(depth, deep, 128)
        tap = jnp.where(left[j], 0, 2)
        taps = [tap + dz * 9 + dy * 3 for dz in range(3) for dy in range(3)]
        terms = dot_rows(shifts(), tap_rows(weight, taps))
        first, last = jnp.where(left[j], terms, 0.0), jnp.where(left[j], 0.0, terms)
        for half in range(halves):
            lanes, rows = slice(half * 128, half * 128 + 128), act.at[half]
            if nx == 1 or j == 0:
                rows[pl.ds(0, square, stride=deep), :] += first[:, lanes]
            if nx == 1 or j == 1:
                rows[pl.ds(deep - 1, square, stride=deep), :] += last[:, lanes]

    rows = deep**3 // 8
    means, spreads = [], []
    for half in range(halves):
        total = act[half].reshape(rows, 8, 128)
        means.append(jnp.sum(total, axis=0) / rows)
        off = total - means[-1]
        spreads.append(jnp.sum(off * off, axis=0))
    put_stats(stats, *(jnp.concatenate(part, axis=1) for part in (means, spreads)), rows)


def final_kernel(act, stats, gain, offset, up, mid, out, wide, held, sems):
    edge = mid.shape[0]
    deep = edge // 2
    f32 = jnp.float32
    mean, scale = read_stats(stats, float(deep**3))
    scale = scale * (0.5 * gain[...])
    shift = 0.5 * offset[...]
    planes = 2
    size = planes * deep * deep
    copies = []
    for k in range(0, deep, planes):
        at = slice(k * deep * deep, k * deep * deep + size)
        value = jnp.concatenate([act[half, at] for half in range(act.shape[0])], axis=1)
        value = value.reshape(size // 8, 8, -1)
        value = silu_of_double((value - mean) * scale + shift)
        value = value.reshape(size, -1).astype(jnp.bfloat16)
        lifted = jnp.dot(value, up[...], preferred_element_type=f32)
        lines = wide.at[k // planes]
        lines[pl.ds(0, size, stride=2), :] = lifted
        lines[pl.ds(1, size, stride=2), :] = lifted
        add = lines[...].reshape(planes, 1, deep, 1, edge, 128)
        at = pl.ds(2 * k, 2 * planes)
        old = mid[at].astype(f32).reshape(planes, 2, deep, 2, edge, 128)
        held[at] = (old + add).astype(jnp.bfloat16).reshape(2 * planes, edge, edge, 128)
        copy = pltpu.make_async_copy(held.at[at], out.at[at], sems.at[k // planes])
        copy.start()
        copies.append(copy)
    for copy in copies:
        copy.wait()


def body(
    features, conv_weight, gain_mid, offset_mid, deep_weight, gain_deep, offset_deep, up_weight
):
    f32, bf16 = jnp.float32, jnp.bfloat16
    edge, channels = features.shape[0], features.shape[3]
    deep = edge // 2
    deep_channels = gain_deep.shape[0]
    square = Square()
    tiles = square.tiles
    devices = lax.axis_size("gz") * tiles
    ny, nx = (len(sides) for sides in square.low_sides())
    riders = Riders(deep_weight.shape[4])

    own = jnp.moveaxis(deep_weight, 4, 3).reshape(-1, 16, channels)
    conv_weight = conv_weight.reshape(27, channels, channels)
    three = ((3, edge, edge, channels), bf16)
    *edges, outer, inner, field, conv_weight = call(
        functools.partial(start_kernel, ny, nx, riders.size),
        [
            ((ny, edge + riders.size, edge, channels), bf16),
            ((nx, edge + riders.size, edge, channels), bf16),
            ((ny * nx, 1 + riders.size, edge, channels), bf16),
            three,
            three,
            ((edge + 2, edge + 2, edge, channels), bf16),
            (conv_weight.shape, bf16),
        ],
        [((nx, edge * edge, 8, channels), f32), pltpu.SemaphoreType.DMA((8,))],
        features,
        conv_weight,
        own,
        nbytes=5 << 20,
        in_hbm=3,
    )
    halos = square.halos(*(list(piece) for piece in edges))
    outer, inner = swap_depth(outer, inner)
    conv_flops = 54 * channels * channels * edge**3
    act, taps, pairs, own = call(
        conv_kernel,
        [
            ((edge, edge, edge, channels), f32),
            ((9 * channels, 3 * channels), bf16),
            ((12 * channels, 2 * channels), bf16),
            (own.shape, bf16),
        ],
        [pltpu.SemaphoreType.DMA],
        own,
        field,
        conv_weight,
        flops=conv_flops,
        nbytes=6 << 20,
        in_hbm=1,
    )
    (y, x, corner), act = lax.optimization_barrier((halos, act))
    y, x, corner = jnp.stack(y), jnp.stack(x), jnp.stack(corner)
    turn = ((3 * (ny + nx) + ny * nx, edge, channels), bf16)
    held = [((3, riders.size, 16, channels), bf16)] if riders.size else []
    turns = call(
        functools.partial(turn_kernel, ny, nx, riders.size), [turn, turn] + held, [], y, x, corner
    )
    turns, held = swap_depth(*turns[:2]), turns[2:]
    if riders.size:
        held = held[0][None]
        other = swap(held, *riders.STEPS[0])
    else:
        held = rotate_shards(own)
    six = ((6, edge, edge, channels), f32)
    column = (edge + 16, channels)
    middle, ends, stats = call(
        functools.partial(side_kernel, ny, nx),
        [((edge - 2, edge, edge, channels), f32), six, ((16, channels), f32)],
        [
            ((edge + 4, edge, edge, channels), f32),
            ((4, edge + 2, edge, channels), bf16),
            ((edge + 4,) + column, f32),
        ],
        field,
        act,
        y,
        x,
        corner,
        inner,
        outer,
        taps,
        pairs,
    )
    ends, stats = call(
        functools.partial(end_kernel, ny, nx),
        [six, ((devices, 2, channels), f32)],
        [((2,) + turn[0], bf16), ((5,) + column, f32)],
        stats,
        ends,
        *turns[::-1],
        taps,
    )
    if riders.size:
        stats, other = lax.optimization_barrier((stats, other))
        held = stack(held, other).reshape((-1,) + held.shape[1:])
        other = swap(held, *riders.STEPS[1])
        stats = share(stats)
        stats, other = lax.optimization_barrier((stats, other))
        held = stack(held, other).reshape((-1,) + held.shape[1:])
        other = swap(held, *riders.STEPS[2])
        held = [stack(held, other).reshape((-1,) + held.shape[1:])]
    else:
        stats = share(stats)
    out, pooled, *edges = call(
        functools.partial(norm_kernel, ny, nx),
        [
            ((edge, edge, edge, channels), bf16),
            ((deep + 2, deep, deep, channels), f32),
            ((ny, (deep + 2) * deep, channels), bf16),
            ((nx, (deep + 2) * deep, channels), bf16),
            ((ny * nx, 16, channels), f32),
        ],
        [((deep + 2, deep * edge, channels), f32)],
        middle,
        ends,
        stats,
        gain_mid.reshape(1, channels),
        offset_mid.reshape(1, channels),
        flops=20 * channels * edge**3,
        nbytes=3 << 20,
    )
    y, x, corner = square.halos(*(list(piece) for piece in edges))
    halves = ((deep_channels // 128, deep**3, 128), f32)
    deep_act, weight = call(
        deep_kernel,
        [halves, ((tiles,) + own.shape, bf16)],
        [
            ((deep + 2, deep + 2, 24, channels), f32),
            ((deep + 2, deep // 2 + 1, 2, 16, 3 * channels), bf16),
        ],
        pooled,
        own,
        *held,
        flops=54 * channels * deep_channels * deep**3,
        nbytes=4 << 20,
    )
    deep_act, stats = call(
        functools.partial(deep_rim_kernel, ny, nx),
        [halves, ((devices, 2, deep_channels), f32)],
        [((deep + 2, 24, channels), f32)],
        deep_act,
        jnp.stack(y),
        jnp.stack(x),
        jnp.stack(corner),
        weight,
        flops=4 * channels * deep_channels * deep**3,
        nbytes=3 << 20,
    )
    stats = share(stats)
    (decoded,) = call(
        final_kernel,
        [((edge, edge, edge, channels), bf16)],
        [
            ((deep // 2, 4 * deep * deep, channels), f32),
            ((edge, edge, edge, channels), bf16),
            pltpu.SemaphoreType.DMA((deep // 2,)),
        ],
        deep_act,
        stats,
        gain_deep.reshape(1, deep_channels),
        offset_deep.reshape(1, deep_channels),
        up_weight,
        out,
        flops=4 * deep_channels * channels * deep**3,
        nbytes=3 << 20,
        out_hbm=True,
    )
    return decoded


def solution(mesh):
    placed = (
        P(("cand", "gz"), "yx", None, None),
        P(),
        P(),
        P(),
        P(None, None, None, None, "yx"),
        P(),
        P(),
        P(),
    )
    return jax.shard_map(
        body,
        mesh=mesh,
        in_specs=placed,
        out_specs=P(("cand", "gz"), "yx", None, None),
        check_vma=False,
    )
```

```python
import functools
import math

import jax
import jax.numpy as jnp
from jax import lax
from jax.experimental import pallas as pl
from jax.experimental.pallas import tpu as pltpu
from jax.sharding import PartitionSpec as P

GROUPS = 32
EPSILON = 1e-05
PART = ("gz", "yx")
VMEM_BYTES = 32 * 1024 * 1024


class Square:
    def __init__(self):
        self.tiles = lax.axis_size("yx")
        self.side = math.isqrt(self.tiles)
        tile = lax.axis_index("yx")
        self.row, self.column = tile // self.side, tile % self.side
        self.folded = self.side == 2
        self.steps = (0,) if self.folded else (-1, 1)

    def low_sides(self):
        if self.folded:
            return [self.row == 1], [self.column == 1]
        return [True, False], [True, False]

    def route(self, down, right):
        pairs = []
        for tile in range(self.tiles):
            row, column = tile // self.side + down, tile % self.side + right
            if 0 <= row < self.side and 0 <= column < self.side:
                pairs.append((tile, row * self.side + column))
        return pairs

    def swap_route(self, mask):
        return [(tile, tile ^ mask) for tile in range(self.tiles)]

    def halos(self, y_edges, x_edges, corners):
        if self.folded:
            y = lax.ppermute(y_edges[0], "yx", self.swap_route(2))
            x = lax.ppermute(x_edges[0], "yx", self.swap_route(1))
            corner = lax.ppermute(corners[0], "yx", self.swap_route(3))
            return [y], [x], [corner]
        y = [lax.ppermute(y_edges[k], "yx", self.route((1, -1)[1 - k], 0)) for k in (1, 0)]
        x = [lax.ppermute(x_edges[k], "yx", self.route(0, (1, -1)[1 - k])) for k in (1, 0)]
        corner = [
            lax.ppermute(corners[2 * k + j], "yx", self.route((1, -1)[1 - k], (1, -1)[1 - j]))
            for k in (1, 0)
            for j in (1, 0)
        ]
        return y, x, corner


def swap_depth(face, outer):
    size = lax.axis_size("gz")
    pairs = [(low, low + 1) for low in range(int(outer), size - 1, 2)]
    return lax.ppermute(face, "gz", pairs + [pair[::-1] for pair in pairs])


class Riders:
    STEPS = (("gz", 2), ("cand", 1), ("gz", 1))

    def __init__(self, rows):
        self.tiles = 27 * rows // 16
        self.fits = (
            lax.axis_size("yx") == 4
            and lax.axis_size("cand") % 2 == 0
            and lax.axis_size("gz") % 4 == 0
            and self.tiles >= 8
        )
        self.size = -(-self.tiles // 8) if self.fits else 0

    @classmethod
    def mine(cls):
        return sum(
            lax.axis_index(axis) // mask % 2 * 2**k for k, (axis, mask) in enumerate(cls.STEPS)
        )


def rotate_shards(piece):
    tiles = lax.axis_size("yx")
    return [
        lax.ppermute(piece, "yx", [(i, (i + k) % tiles) for i in range(tiles)]) for k in range(1, tiles)
    ]


def swap(block, axis, mask):
    return lax.ppermute(block, axis, [(i, i ^ mask) for i in range(lax.axis_size(axis))])


def share(stats):
    return lax.all_to_all(stats, PART, 0, 0)


def call(kernel, outs, scratch, *arrays, flops=0, nbytes=0, in_hbm=0, out_hbm=False):
    vmem, hbm = (pl.BlockSpec(memory_space=space) for space in (pltpu.VMEM, pltpu.HBM))
    far, near = arrays[:in_hbm], arrays[in_hbm:]
    far = [pltpu.with_memory_space_constraint(array, pltpu.HBM) for array in far]
    return pl.pallas_call(
        kernel,
        out_shape=[jax.ShapeDtypeStruct(shape, dtype) for shape, dtype in outs],
        in_specs=[hbm] * len(far) + [vmem] * len(near),
        out_specs=[hbm if out_hbm else vmem] * len(outs),
        scratch_shapes=[pltpu.VMEM(*entry) if isinstance(entry, tuple) else entry for entry in scratch],
        compiler_params=pltpu.CompilerParams(vmem_limit_bytes=VMEM_BYTES),
        cost_estimate=pl.CostEstimate(flops=flops, bytes_accessed=nbytes, transcendentals=0),
    )(*far, *near)


def start_kernel(ny, nx, size, x_in, w_in, d_in, y_out, x_out, corners, outer, x, w, lines, sems):
    edge = x_in.shape[0]
    f32, bf16 = jnp.float32, jnp.bfloat16
    above, left = Square().low_sides()
    chunks = 4
    planes = edge // chunks
    first = [
        pltpu.make_async_copy(
            x_in.at[pl.ds(k * planes, planes)],
            x.at[pl.ds(1 + k * planes, planes), pl.ds(1, edge)],
            sems.at[k],
        )
        for k in range(chunks)
    ]
    later = []
    if size:
        at = jnp.minimum(Riders.mine() * size, d_in.shape[0] - size)
        for k, (out, begin) in enumerate(((y_out, edge), (x_out, edge), (corners, 1))):
            later.append(
                pltpu.make_async_copy(
                    d_in.at[pl.ds(at, size)], out.at[0, pl.ds(begin, size)], sems.at[chunks + k]
                )
            )
    later.append(pltpu.make_async_copy(w_in, w, sems.at[chunks + 3]))
    for copy in first + later:
        copy.start()
    x[0] = jnp.zeros(x.shape[1:], bf16)
    x[edge + 1] = jnp.zeros(x.shape[1:], bf16)
    blank = jnp.zeros((edge,) + x.shape[2:], bf16)
    x[1 : edge + 1, 0] = blank
    x[1 : edge + 1, edge + 1] = blank
    flat = lines.reshape(nx * edge * edge * 8, 128)
    part = planes * edge
    for k in range(chunks):
        first[k].wait()
        at, here = pl.ds(k * planes, planes), pl.ds(1 + k * planes, planes)
        for i in range(ny):
            row = jnp.where(above[i], 1, edge)
            y_out[i, at] = x[here, row]
        for j in range(nx):
            low = x[here, 1 : edge + 1, 0:8].astype(f32).reshape(part, 8, 128)
            high = x[here, 1 : edge + 1, edge - 8 : edge].astype(f32).reshape(part, 8, 128)
            high = pltpu.roll(high, 1, 1)
            kept = jnp.where(left[j], low, high)
            lines[j, k * part : k * part + part] = kept
            begin = (j * edge * edge + k * part) * 8
            column = flat[pl.ds(begin, part, stride=8), :]
            x_out[j, at] = column.astype(bf16).reshape(planes, edge, 128)
    for i in range(ny):
        for j in range(nx):
            begin = j * edge * edge * 8
            low = flat[pl.ds(begin, edge, stride=8 * edge), :]
            high = flat[pl.ds(begin + 8 * (edge - 1), edge, stride=8 * edge), :]
            kept = jnp.where(above[i], low, high)
            corners[i * nx + j, 0] = kept.astype(bf16)
    odd, far = lax.axis_index("gz") % 2, edge - 3
    for k in range(3):
        outer[k] = x[1 + odd * far + k, 1 : edge + 1]
    for copy in later:
        copy.wait()


def turn_kernel(ny, nx, size, x, y_halos, x_halos, corners, outer, inner, *riders):
    edge = outer.shape[1]
    wide = ny + nx
    odd, far = lax.axis_index("gz") % 2, edge - 3
    for face, at, begin in ((outer, odd * far, 0), (inner, (1 - odd) * far, 3 * edge)):
        for k in range(3):
            row = begin + k * wide
            for i in range(ny):
                face[row + i] = y_halos[i, at + k]
            for j in range(nx):
                face[row + ny + j] = x_halos[j, at + k]
            if begin:
                face[k * edge : k * edge + edge] = x[1 + at + k, 1 : edge + 1]
        for k in range(ny * nx):
            face[begin + 3 * wide + k] = corners[k, 0]
    if size:
        riders[0][0] = x_halos[0, edge : edge + size]
        riders[0][1] = y_halos[0, edge : edge + size]
        riders[0][2] = corners[0, 1 : 1 + size]


def in_order(odd, outer, inner):
    return jnp.where(odd, inner, outer), jnp.where(odd, outer, inner)


def spread_taps(weight, taps):
    for tap in range(27):
        row, lane = tap // 3 * 128, tap % 3 * 128
        taps[row : row + 128, lane : lane + 128] = weight[tap]


def pair_taps(weight, pairs):
    for dz in range(3):
        for line in range(4):
            row = (dz * 4 + line) * 128
            for out in range(2):
                lane = out * 128
                if 0 <= line - out < 3:
                    block = weight[dz * 9 + (line - out) * 3 + 2]
                else:
                    block = jnp.zeros((128, 128), pairs.dtype)
                pairs[row : row + 128, lane : lane + 128] = block


def join_x(wide, edge):
    place = lax.broadcasted_iota(jnp.int32, wide.shape[:2] + (128,), 1)
    after = jnp.where(place > 0, pltpu.roll(wide[:, :, :128], 1, 1), 0.0)
    before = jnp.where(place < edge - 1, pltpu.roll(wide[:, :, 256:], edge - 1, 1), 0.0)
    return wide[:, :, 128:256] + after + before


def convolve(grid, count, taps, pairs, put):
    edge = grid.shape[2]
    planes = min(count, 4)
    rows = planes * edge * edge
    place = lax.broadcasted_iota(jnp.int32, (planes * edge, edge, 128), 1)
    halved = grid.reshape(grid.shape[0], edge // 2 + 1, 2, edge, 128)
    for z in range(0, count, planes):
        left = jnp.concatenate(
            [
                grid[z + dz : z + dz + planes, dy : dy + edge].reshape(rows, 128)
                for dz in range(3)
                for dy in range(3)
            ],
            axis=1,
        )
        wide = jnp.dot(left, taps[:, 0:256], preferred_element_type=jnp.float32)
        wide = wide.reshape(planes * edge, edge, 256)
        left = jnp.concatenate(
            [
                halved[z + dz : z + dz + planes, line // 2 : line // 2 + edge // 2, line % 2].reshape(
                    rows // 2, 128
                )
                for dz in range(3)
                for line in range(4)
            ],
            axis=1,
        )
        two = jnp.dot(left, pairs[...], preferred_element_type=jnp.float32)
        two = two.reshape(planes * edge // 2, edge, 256)
        two = jnp.stack([two[:, :, :128], two[:, :, 128:]], axis=1).reshape(planes * edge, edge, 128)
        after = jnp.where(place > 0, pltpu.roll(wide[:, :, :128], 1, 1), 0.0)
        before = jnp.where(place < edge - 1, pltpu.roll(two, edge - 1, 1), 0.0)
        new = wide[:, :, 128:256] + after + before
        put(z, new.reshape(planes, edge, edge, 128))


def conv_kernel(deep_in, x, weight, act, taps, pairs, deep_weight, sem):
    copy = pltpu.make_async_copy(deep_in, deep_weight, sem)
    copy.start()
    edge = act.shape[0]
    spread_taps(weight, taps)
    pair_taps(weight, pairs)

    def put(z, new):
        act[z : z + new.shape[0]] = new

    convolve(x, edge, taps, pairs, put)
    copy.wait()


def y_terms(line, low, taps):
    planes, edge = line.shape[0] - 2, line.shape[1]
    left = jnp.concatenate(
        [line[dz : dz + planes].reshape(planes * edge, 128) for dz in range(3)], axis=1
    )
    start = jnp.where(low, 0, 256)
    right = jnp.concatenate(
        [taps[pl.ds(pl.multiple_of(start + dz * 384, 128), 128), :] for dz in range(3)], axis=0
    )
    wide = jnp.dot(left, right, preferred_element_type=jnp.float32)
    return join_x(wide.reshape(planes, edge, 384), edge)


def x_terms(column, taps):
    planes, edge = column.shape[0] - 2, column.shape[1] - 16
    lines = [column[:, 7 + dy : 7 + dy + edge].astype(jnp.bfloat16) for dy in range(3)]
    left = jnp.concatenate(
        [line[dz : dz + planes].reshape(planes * edge, 128) for dz in range(3) for line in lines],
        axis=1,
    )
    right = jnp.concatenate([taps[:, 0:128], taps[:, 256:384]], axis=1)
    both = jnp.dot(left, right, preferred_element_type=jnp.float32)
    return both[:, :128], both[:, 128:]


def fill_column(column, at, voxels, ends, above):
    count, edge = voxels.shape[:2]
    rows = edge + 16
    lines = column.reshape(column.shape[0] * rows, 128)
    column[at : at + count, 8 : 8 + edge] = voxels.astype(jnp.float32)
    for i, end in enumerate(ends):
        first = last = end.astype(jnp.float32)
        if len(ends) == 1:
            first, last = jnp.where(above[0], first, 0.0), jnp.where(above[0], 0.0, last)
        if len(ends) == 1 or i == 0:
            lines[pl.ds(at * rows + 7, count, stride=rows), :] = first
        if len(ends) == 1 or i == 1:
            lines[pl.ds(at * rows + 8 + edge, count, stride=rows), :] = last


def add_column(act, terms, j, nx, low):
    planes, edge = act.shape[:2]
    flat = act.reshape(planes * edge * edge, 128)
    first, last = terms
    if nx == 1:
        first, last = jnp.where(low, first, 0.0), jnp.where(low, 0.0, last)
    if nx == 1 or j == 0:
        flat[pl.ds(0, planes * edge, stride=edge), :] += first
    if nx == 1 or j == 1:
        flat[pl.ds(edge - 1, planes * edge, stride=edge), :] += last


def moments(planes):
    count, edge = planes.shape[:2]
    zero = jnp.zeros((8, 128), jnp.float32)

    def sum_step(k, carry):
        return carry + jnp.sum(planes[k].reshape(edge * 2, 8, 128), axis=0)

    mean = lax.fori_loop(0, count, sum_step, zero, unroll=True) / (count * edge * edge // 8)

    def spread_step(k, carry):
        off = planes[k].reshape(edge * 2, 8, 128) - mean
        return carry + jnp.sum(off * off, axis=0)

    return mean, lax.fori_loop(0, count, spread_step, zero, unroll=True)


def add_beyond(behind, face, x, grid, taps, pairs, ends):
    edge = x.shape[2]
    grid[pl.ds(jnp.where(behind, 1, 0), 3), 1 : edge + 1] = face
    own = jnp.where(behind, edge, 1)
    grid[jnp.where(behind, 0, 3), 1 : edge + 1] = x[own, 1 : edge + 1]
    blank = jnp.zeros(grid.shape[:1] + grid.shape[2:], grid.dtype)
    grid[:, 0] = blank
    grid[:, edge + 1] = blank
    begin = jnp.where(behind, 4, 0)

    def put(z, new):
        ends[pl.ds(begin + z, new.shape[0])] += new

    convolve(grid, 2, taps, pairs, put)
    beside = jnp.where(behind, 1, 2)
    stacked = jnp.concatenate(
        [grid[beside, dy : dy + edge].reshape(edge * edge, 128) for dy in range(3)], axis=1
    )
    rows = taps[pl.ds(pl.multiple_of(jnp.where(behind, 768, 0), 128), 384), :]
    wide = jnp.dot(stacked, rows, preferred_element_type=jnp.float32)
    ends[jnp.where(behind, 3, 2)] += join_x(wide.reshape(edge, edge, 384), edge)


def side_kernel(ny, nx, x, own, y_halos, x_halos, corners, outer, taps, pairs, *refs):
    middle, ends, stats, grid, column = refs
    edge = own.shape[0]
    f32 = jnp.float32
    above, left = Square().low_sides()
    zero = jnp.zeros((2, edge, edge, 128), f32)
    ends[0:2] = zero
    ends[2] = own[0]
    ends[3] = own[edge - 1]
    ends[4:6] = zero
    total = jnp.zeros((8, 128), f32)
    for z in range(edge - 2):
        plane = own[1 + z]
        middle[z] = plane
        total = total + jnp.sum(plane.reshape(edge * 2, 8, 128), axis=0)
    odd = lax.axis_index("gz") % 2 == 1
    add_beyond(odd, outer[...], x, grid, taps, pairs, ends)

    parts = ((ends.at[1:3], 0), (middle, 2), (ends.at[3:5], edge))
    gap = jnp.zeros((2, edge, 128), grid.dtype)
    for i in range(ny):
        line = jnp.concatenate([gap, y_halos[i, 0:edge], gap], axis=0)
        new = y_terms(line, above[i], taps)
        row = jnp.where(above[i], 0, edge - 1)
        for ref, at in parts:
            ref[:, row] += new[at : at + ref.shape[0]]
        total = total + jnp.sum(new[2:edge].reshape(-1, 8, 128), axis=0)
    line = lax.broadcasted_iota(jnp.int32, (8, 128), 0)
    for j in range(nx):
        column[...] = jnp.zeros(column.shape, f32)
        fill_column(
            column, 2, x_halos[j, 0:edge], [corners[i * nx + j, 0] for i in range(ny)], above
        )
        terms = x_terms(column, taps)
        for ref, at in parts:
            rows = slice(at * edge, (at + ref.shape[0]) * edge)
            add_column(ref, [term[rows] for term in terms], j, nx, left[j])
        first, last = (
            jnp.sum(term[2 * edge : edge * edge], axis=0, keepdims=True) for term in terms
        )
        total = total + jnp.where(
            left[j], jnp.where(line == 0, first, 0.0), jnp.where(line == 7, last, 0.0)
        )
    mean = total / ((edge - 2) * edge * edge // 8)
    spread = jnp.zeros((8, 128), f32)
    for z in range(edge - 2):
        off = middle[z].reshape(edge * 2, 8, 128) - mean
        spread = spread + jnp.sum(off * off, axis=0)
    stats[0:8] = mean
    stats[8:16] = spread


def end_kernel(ny, nx, x, middle_stats, ends, inner, outer, taps, pairs, act, stats, faces, grid, column):
    edge = act.shape[1]
    wide = ny + nx
    f32 = jnp.float32
    above, left = Square().low_sides()
    odd = lax.axis_index("gz") % 2 == 1
    faces[0], faces[1] = in_order(odd, outer[...], inner[3 * edge :])
    act[...] = ends[...]
    add_beyond(
        jnp.logical_not(odd),
        inner[0 : 3 * edge].reshape(3, edge, edge, 128),
        x,
        grid,
        taps,
        pairs,
        act,
    )
    gap = jnp.zeros((2, edge, 128), faces.dtype)
    for side in range(2):

        def rim(row):
            return jnp.stack([faces[side, k * wide + row] for k in range(3)])

        three = act.at[3 * side : 3 * side + 3]
        for i in range(ny):
            line = [rim(i), gap] if side == 0 else [gap, rim(i)]
            line = jnp.concatenate(line, axis=0)
            three[:, jnp.where(above[i], 0, edge - 1)] += y_terms(line, above[i], taps)
        for j in range(nx):
            column[...] = jnp.zeros(column.shape, f32)
            tails = []
            for i in range(ny):
                tile = faces[side, 3 * wide + i * nx + j].astype(f32)
                tails.append(tile[edge - 3 :] if side == 0 else tile[:3])
            fill_column(column, 0 if side == 0 else 2, rim(ny + j), tails, above)
            add_column(three, x_terms(column, taps), j, nx, left[j])

    mean, spread = moments(act.at[2:4])
    few, many = edge * edge // 4, (edge - 2) * edge * edge // 8
    middle_mean, middle_spread = middle_stats[0:8], middle_stats[8:16]
    off = middle_mean - mean
    part = few / (few + many)
    spread = spread + middle_spread + (many * part) * (off * off)
    put_stats(stats, middle_mean - part * off, spread, few + many)


def merge(mean, spread, rows, other_mean, other_spread):
    off = mean - other_mean
    return 0.5 * (mean + other_mean), spread + other_spread + (0.5 * rows) * (off * off)


def put_stats(stats, mean, spread, rows):
    for step in (1, 2, 4):
        others = pltpu.roll(mean, step, 0), pltpu.roll(spread, step, 0)
        mean, spread = merge(mean, spread, float(rows * step), *others)
    both = jnp.concatenate([mean[0:1], spread[0:1]], axis=0)
    stats[...] = jnp.broadcast_to(both[None], stats.shape)


def read_stats(stats, rows):
    devices, _, channels = stats.shape
    shape = (8, channels)
    means = [jnp.broadcast_to(stats[k, 0:1, :], shape) for k in range(devices)]
    spreads = [jnp.broadcast_to(stats[k, 1:2, :], shape) for k in range(devices)]
    mean = functools.reduce(jnp.add, means) / devices
    spread = functools.reduce(jnp.add, spreads)
    spread = spread + rows * functools.reduce(jnp.add, [(m - mean) * (m - mean) for m in means])
    rows = rows * devices
    lane = lax.broadcasted_iota(jnp.int32, shape, 1)
    step = 1
    while step < channels // GROUPS:
        low = jnp.bitwise_and(lane, step) == 0
        others = [
            jnp.where(low, pltpu.roll(row, channels - step, 1), pltpu.roll(row, step, 1))
            for row in (mean, spread)
        ]
        mean, spread = merge(mean, spread, rows, *others)
        rows, step = 2.0 * rows, 2 * step
    return mean, lax.rsqrt(spread / rows + EPSILON)


def silu_of_double(h):
    return h + h * jnp.tanh(h)


def norm_kernel(ny, nx, inner, ends, stats, gain, offset, out, pooled, *refs):
    y_edges, x_edges, corners, half = refs
    depth, edge = inner.shape[0] + 6, inner.shape[1]
    deep, deep_depth = edge // 2, depth // 2
    f32, bf16 = jnp.float32, jnp.bfloat16
    above, left = Square().low_sides()
    depth_at = lax.axis_index("gz")
    mean, scale = read_stats(stats, float(edge**3))
    scale = scale * (0.5 * gain[...])
    shift = 0.5 * offset[...]
    for k in range(deep_depth):
        value = [
            ends[z] if z < 3 else inner[z - 3] if z < depth - 3 else ends[z - depth + 6]
            for z in (2 * k, 2 * k + 1)
        ]
        value = jnp.stack(value).reshape(edge * edge // 4, 8, 128)
        value = silu_of_double((value - mean) * scale + shift)
        value = value.reshape(2, edge, edge, 128).astype(bf16)
        if 0 < k < deep_depth - 1:
            out[2 * k - 2 : 2 * k] = value
        value = value.astype(f32)
        value = (value[0] + value[1]).reshape(deep, 2, edge, 128)
        half[k] = (value[:, 0] + value[:, 1]).reshape(deep * edge, 128)
        lines = half.at[k]
        pair = lines[pl.ds(0, deep * deep, stride=2), :] + lines[pl.ds(1, deep * deep, stride=2), :]
        pair = (pair * 0.125).astype(bf16).astype(f32).reshape(deep, deep, 128)
        if k == 0 or k == deep_depth - 1:
            inside = depth_at > 0 if k == 0 else depth_at < lax.axis_size("gz") - 1
            pair = jnp.where(inside, pair, 0.0)
        pooled[k] = pair
    lines = pooled.reshape(deep_depth * deep * deep, 128)
    rows = deep_depth * deep
    first_x = lines[pl.ds(0, rows, stride=deep), :]
    last_x = lines[pl.ds(deep - 1, rows, stride=deep), :]
    first_y, last_y = (pooled[:, y].reshape(rows, 128) for y in (0, deep - 1))
    ends = []
    for y in (0, deep - 1):
        for x in (0, deep - 1):
            ends.append(lines[pl.ds(y * deep + x, deep_depth, stride=deep * deep), :])
    if ny == 1:
        above, left = above[0], left[0]
        y_edges[0] = jnp.where(above, first_y, last_y).astype(bf16)
        x_edges[0] = jnp.where(left, first_x, last_x).astype(bf16)
        corners[0, 0:deep_depth] = jnp.where(
            above, jnp.where(left, ends[0], ends[1]), jnp.where(left, ends[2], ends[3])
        )
    else:
        y_edges[0], y_edges[1] = first_y.astype(bf16), last_y.astype(bf16)
        x_edges[0], x_edges[1] = first_x.astype(bf16), last_x.astype(bf16)
        for k in range(4):
            corners[k, 0:deep_depth] = ends[k]


def stack_kernel(*refs):
    out = refs[-1]
    for k in range(out.shape[0]):
        out[k] = refs[k][...]


def stack(*arrays):
    vmem = pl.BlockSpec(memory_space=pltpu.VMEM)
    return pl.pallas_call(
        stack_kernel,
        out_shape=jax.ShapeDtypeStruct((len(arrays),) + arrays[0].shape, arrays[0].dtype),
        in_specs=[vmem] * len(arrays),
        out_specs=vmem,
        compiler_params=pltpu.CompilerParams(vmem_limit_bytes=VMEM_BYTES),
    )(*arrays)


def place_weights(own, held, out):
    tile = lax.axis_index("yx")
    out[tile] = own[...]
    if len(held) == 1:
        pieces, others, size = held[0].shape[:3]
        for piece in range(pieces):
            at = jnp.minimum(jnp.bitwise_xor(Riders.mine(), piece) * size, own.shape[0] - size)
            for k in range(others):
                out[jnp.bitwise_xor(tile, k + 1), pl.ds(at, size)] = held[0][piece, k]
    else:
        for k, shard in enumerate(held):
            out[lax.rem(tile + len(held) - k, len(held) + 1)] = shard[...]


def tap_rows(weight, taps):
    per = weight.shape[1] // 27
    return jnp.concatenate(
        [weight[:, pl.ds(tap * per, per)].reshape(-1, 128) for tap in taps], axis=1
    )


def dot_rows(left, right):
    return lax.dot_general(
        left, right, (((1,), (1,)), ((), ())), preferred_element_type=jnp.float32
    )


def deep_kernel(pooled, own, *refs):
    *held, act, weight, grid, packed = refs
    depth, deep = pooled.shape[0], pooled.shape[1]
    place_weights(own, held, weight)
    grid[...] = jnp.zeros(grid.shape, jnp.float32)
    grid[:, 1 : deep + 1, 8:16] = pooled[...]
    for dx in range(3):
        plane = grid[:, :, 7 + dx : 15 + dx]
        for y in range(deep + 1):
            both = jnp.concatenate([plane[:, y], plane[:, y + 1]], axis=1)
            packed[:, y // 2, y % 2, :, dx * 128 : dx * 128 + 128] = both.astype(jnp.bfloat16)
    rows = deep**3
    total = None
    for dz in range(3):
        left = jnp.concatenate(
            [
                packed[dz : dz + deep, dy // 2 : dy // 2 + deep // 2, dy % 2].reshape(rows, 384)
                for dy in range(3)
            ],
            axis=1,
        )
        term = dot_rows(left, tap_rows(weight, range(dz * 9, dz * 9 + 9)))
        total = term if total is None else total + term
    for half in range(act.shape[0]):
        act[half] = total[:, half * 128 : half * 128 + 128]


def deep_rim_kernel(ny, nx, own, y_halos, x_halos, corners, weight, act, stats, line):
    depth, deep = line.shape[0], line.shape[1] - 16
    halves = act.shape[0]
    f32 = jnp.float32
    square = deep * deep
    above, left = Square().low_sides()
    act[...] = own[...]
    flat = line.reshape(depth * line.shape[1], 128)

    def shifts():
        return jnp.concatenate(
            [
                line[dz : dz + deep, 7 + d : 7 + d + deep].reshape(square, 128).astype(jnp.bfloat16)
                for dz in range(3)
                for d in range(3)
            ],
            axis=1,
        )

    for i in range(ny):
        line[...] = jnp.zeros(line.shape, f32)
        line[:, 8 : 8 + deep] = y_halos[i].astype(f32).reshape(depth, deep, 128)
        for j in range(nx):
            end = corners[i * nx + j, 0:depth]
            first, last = jnp.where(left[j], end, 0.0), jnp.where(left[j], 0.0, end)
            if nx == 1 or j == 0:
                flat[pl.ds(7, depth, stride=line.shape[1]), :] = first
            if nx == 1 or j == 1:
                flat[pl.ds(8 + deep, depth, stride=line.shape[1]), :] = last
        tap = jnp.where(above[i], 0, 6)
        taps = [tap + dz * 9 + dx for dz in range(3) for dx in range(3)]
        terms = dot_rows(shifts(), tap_rows(weight, taps))
        for half in range(halves):
            rows = act.at[half].reshape(deep, deep, deep, 128)
            term = terms[:, half * 128 : half * 128 + 128].reshape(deep, deep, 128)
            rows[:, jnp.where(above[i], 0, deep - 1)] += term
    for j in range(nx):
        line[...] = jnp.zeros(line.shape, f32)
        line[:, 8 : 8 + deep] = x_halos[j].astype(f32).reshape(depth, deep, 128)
        tap = jnp.where(left[j], 0, 2)
        taps = [tap + dz * 9 + dy * 3 for dz in range(3) for dy in range(3)]
        terms = dot_rows(shifts(), tap_rows(weight, taps))
        first, last = jnp.where(left[j], terms, 0.0), jnp.where(left[j], 0.0, terms)
        for half in range(halves):
            lanes, rows = slice(half * 128, half * 128 + 128), act.at[half]
            if nx == 1 or j == 0:
                rows[pl.ds(0, square, stride=deep), :] += first[:, lanes]
            if nx == 1 or j == 1:
                rows[pl.ds(deep - 1, square, stride=deep), :] += last[:, lanes]

    rows = deep**3 // 8
    means, spreads = [], []
    for half in range(halves):
        total = act[half].reshape(rows, 8, 128)
        means.append(jnp.sum(total, axis=0) / rows)
        off = total - means[-1]
        spreads.append(jnp.sum(off * off, axis=0))
    put_stats(stats, *(jnp.concatenate(part, axis=1) for part in (means, spreads)), rows)


def final_kernel(act, stats, gain, offset, up, mid, out, wide, held, sems):
    edge = mid.shape[0]
    deep = edge // 2
    f32 = jnp.float32
    mean, scale = read_stats(stats, float(deep**3))
    scale = scale * (0.5 * gain[...])
    shift = 0.5 * offset[...]
    planes = 2
    size = planes * deep * deep
    copies = []
    for k in range(0, deep, planes):
        at = slice(k * deep * deep, k * deep * deep + size)
        value = jnp.concatenate([act[half, at] for half in range(act.shape[0])], axis=1)
        value = value.reshape(size // 8, 8, -1)
        value = silu_of_double((value - mean) * scale + shift)
        value = value.reshape(size, -1).astype(jnp.bfloat16)
        lifted = jnp.dot(value, up[...], preferred_element_type=f32)
        lines = wide.at[k // planes]
        lines[pl.ds(0, size, stride=2), :] = lifted
        lines[pl.ds(1, size, stride=2), :] = lifted
        add = lines[...].reshape(planes, 1, deep, 1, edge, 128)
        at = pl.ds(2 * k, 2 * planes)
        old = mid[at].astype(f32).reshape(planes, 2, deep, 2, edge, 128)
        held[at] = (old + add).astype(jnp.bfloat16).reshape(2 * planes, edge, edge, 128)
        copy = pltpu.make_async_copy(held.at[at], out.at[at], sems.at[k // planes])
        copy.start()
        copies.append(copy)
    for copy in copies:
        copy.wait()


def body(
    features, conv_weight, gain_mid, offset_mid, deep_weight, gain_deep, offset_deep, up_weight
):
    f32, bf16 = jnp.float32, jnp.bfloat16
    edge, channels = features.shape[0], features.shape[3]
    deep = edge // 2
    deep_channels = gain_deep.shape[0]
    square = Square()
    tiles = square.tiles
    devices = lax.axis_size("gz") * tiles
    ny, nx = (len(sides) for sides in square.low_sides())
    riders = Riders(deep_weight.shape[4])

    own = jnp.moveaxis(deep_weight, 4, 3).reshape(-1, 16, channels)
    conv_weight = conv_weight.reshape(27, channels, channels)
    three = ((3, edge, edge, channels), bf16)
    *edges, outer, field, conv_weight = call(
        functools.partial(start_kernel, ny, nx, riders.size),
        [
            ((ny, edge + riders.size, edge, channels), bf16),
            ((nx, edge + riders.size, edge, channels), bf16),
            ((ny * nx, 1 + riders.size, edge, channels), bf16),
            three,
            ((edge + 2, edge + 2, edge, channels), bf16),
            (conv_weight.shape, bf16),
        ],
        [((nx, edge * edge, 8, channels), f32), pltpu.SemaphoreType.DMA((8,))],
        features,
        conv_weight,
        own,
        nbytes=5 << 20,
        in_hbm=3,
    )
    halos = square.halos(*(list(piece) for piece in edges))
    outer = swap_depth(outer, True)
    conv_flops = 54 * channels * channels * edge**3
    act, taps, pairs, own = call(
        conv_kernel,
        [
            ((edge, edge, edge, channels), f32),
            ((9 * channels, 3 * channels), bf16),
            ((12 * channels, 2 * channels), bf16),
            (own.shape, bf16),
        ],
        [pltpu.SemaphoreType.DMA],
        own,
        field,
        conv_weight,
        flops=conv_flops,
        nbytes=6 << 20,
        in_hbm=1,
    )
    (y, x, corner), act, outer = lax.optimization_barrier((halos, act, outer))
    y, x, corner = jnp.stack(y), jnp.stack(x), jnp.stack(corner)
    turn = ((3 * (ny + nx) + ny * nx, edge, channels), bf16)
    full = ((3 * edge + turn[0][0], edge, channels), bf16)
    held = [((3, riders.size, 16, channels), bf16)] if riders.size else []
    outer_rim, inner, *held = call(
        functools.partial(turn_kernel, ny, nx, riders.size),
        [turn, full] + held,
        [],
        field,
        y,
        x,
        corner,
    )
    outer_rim, inner = swap_depth(outer_rim, True), swap_depth(inner, False)
    if riders.size:
        held = held[0][None]
        other = swap(held, *riders.STEPS[0])
    else:
        held = rotate_shards(own)
    six = ((6, edge, edge, channels), f32)
    column = (edge + 16, channels)
    middle, ends, stats = call(
        functools.partial(side_kernel, ny, nx),
        [((edge - 2, edge, edge, channels), f32), six, ((16, channels), f32)],
        [
            ((4, edge + 2, edge, channels), bf16),
            ((edge + 4,) + column, f32),
        ],
        field,
        act,
        y,
        x,
        corner,
        outer,
        taps,
        pairs,
    )
    ends, stats = call(
        functools.partial(end_kernel, ny, nx),
        [six, ((devices, 2, channels), f32)],
        [
            ((2,) + turn[0], bf16),
            ((4, edge + 2, edge, channels), bf16),
            ((5,) + column, f32),
        ],
        field,
        stats,
        ends,
        inner,
        outer_rim,
        taps,
        pairs,
    )
    if riders.size:
        stats, other = lax.optimization_barrier((stats, other))
        held = stack(held, other).reshape((-1,) + held.shape[1:])
        other = swap(held, *riders.STEPS[1])
        stats = share(stats)
        stats, other = lax.optimization_barrier((stats, other))
        held = stack(held, other).reshape((-1,) + held.shape[1:])
        other = swap(held, *riders.STEPS[2])
        held = [stack(held, other).reshape((-1,) + held.shape[1:])]
    else:
        stats = share(stats)
    out, pooled, *edges = call(
        functools.partial(norm_kernel, ny, nx),
        [
            ((edge, edge, edge, channels), bf16),
            ((deep + 2, deep, deep, channels), f32),
            ((ny, (deep + 2) * deep, channels), bf16),
            ((nx, (deep + 2) * deep, channels), bf16),
            ((ny * nx, 16, channels), f32),
        ],
        [((deep + 2, deep * edge, channels), f32)],
        middle,
        ends,
        stats,
        gain_mid.reshape(1, channels),
        offset_mid.reshape(1, channels),
        flops=20 * channels * edge**3,
        nbytes=3 << 20,
    )
    y, x, corner = square.halos(*(list(piece) for piece in edges))
    halves = ((deep_channels // 128, deep**3, 128), f32)
    deep_act, weight = call(
        deep_kernel,
        [halves, ((tiles,) + own.shape, bf16)],
        [
            ((deep + 2, deep + 2, 24, channels), f32),
            ((deep + 2, deep // 2 + 1, 2, 16, 3 * channels), bf16),
        ],
        pooled,
        own,
        *held,
        flops=54 * channels * deep_channels * deep**3,
        nbytes=4 << 20,
    )
    deep_act, stats = call(
        functools.partial(deep_rim_kernel, ny, nx),
        [halves, ((devices, 2, deep_channels), f32)],
        [((deep + 2, 24, channels), f32)],
        deep_act,
        jnp.stack(y),
        jnp.stack(x),
        jnp.stack(corner),
        weight,
        flops=4 * channels * deep_channels * deep**3,
        nbytes=3 << 20,
    )
    stats = share(stats)
    (decoded,) = call(
        final_kernel,
        [((edge, edge, edge, channels), bf16)],
        [
            ((deep // 2, 4 * deep * deep, channels), f32),
            ((edge, edge, edge, channels), bf16),
            pltpu.SemaphoreType.DMA((deep // 2,)),
        ],
        deep_act,
        stats,
        gain_deep.reshape(1, deep_channels),
        offset_deep.reshape(1, deep_channels),
        up_weight,
        out,
        flops=4 * deep_channels * channels * deep**3,
        nbytes=3 << 20,
        out_hbm=True,
    )
    return decoded


def solution(mesh):
    placed = (
        P(("cand", "gz"), "yx", None, None),
        P(),
        P(),
        P(),
        P(None, None, None, None, "yx"),
        P(),
        P(),
        P(),
    )
    return jax.shard_map(
        body,
        mesh=mesh,
        in_specs=placed,
        out_specs=P(("cand", "gz"), "yx", None, None),
        check_vma=False,
    )
```

```python
import functools
import math

import jax
import jax.numpy as jnp
from jax import lax
from jax.experimental import pallas as pl
from jax.experimental.pallas import tpu as pltpu
from jax.sharding import PartitionSpec as P

GROUPS = 32
EPSILON = 1e-05
PART = ("gz", "yx")
VMEM_BYTES = 32 * 1024 * 1024


class Square:
    def __init__(self):
        self.tiles = lax.axis_size("yx")
        self.side = math.isqrt(self.tiles)
        tile = lax.axis_index("yx")
        self.row, self.column = tile // self.side, tile % self.side
        self.folded = self.side == 2
        self.steps = (0,) if self.folded else (-1, 1)

    def low_sides(self):
        if self.folded:
            return [self.row == 1], [self.column == 1]
        return [True, False], [True, False]

    def route(self, down, right):
        pairs = []
        for tile in range(self.tiles):
            row, column = tile // self.side + down, tile % self.side + right
            if 0 <= row < self.side and 0 <= column < self.side:
                pairs.append((tile, row * self.side + column))
        return pairs

    def swap_route(self, mask):
        return [(tile, tile ^ mask) for tile in range(self.tiles)]

    def halos(self, y_edges, x_edges, corners):
        if self.folded:
            y = lax.ppermute(y_edges[0], "yx", self.swap_route(2))
            x = lax.ppermute(x_edges[0], "yx", self.swap_route(1))
            corner = lax.ppermute(corners[0], "yx", self.swap_route(3))
            return [y], [x], [corner]
        y = [lax.ppermute(y_edges[k], "yx", self.route((1, -1)[1 - k], 0)) for k in (1, 0)]
        x = [lax.ppermute(x_edges[k], "yx", self.route(0, (1, -1)[1 - k])) for k in (1, 0)]
        corner = [
            lax.ppermute(corners[2 * k + j], "yx", self.route((1, -1)[1 - k], (1, -1)[1 - j]))
            for k in (1, 0)
            for j in (1, 0)
        ]
        return y, x, corner


def swap_depth(outer, inner):
    size = lax.axis_size("gz")
    routes = [[], []]
    for low in range(size - 1):
        routes[low % 2] += [(low, low + 1), (low + 1, low)]
    return lax.ppermute(outer, "gz", routes[1]), lax.ppermute(inner, "gz", routes[0])


class Riders:
    STEPS = (("cand", 1), ("gz", 2), ("gz", 1))

    def __init__(self, rows):
        self.tiles = 27 * rows // 16
        self.fits = (
            lax.axis_size("yx") == 4
            and lax.axis_size("cand") % 2 == 0
            and lax.axis_size("gz") % 4 == 0
            and self.tiles >= 8
        )
        self.size = -(-self.tiles // 8) if self.fits else 0

    @classmethod
    def mine(cls):
        return sum(
            lax.axis_index(axis) // mask % 2 * 2**k for k, (axis, mask) in enumerate(cls.STEPS)
        )


def rotate_shards(piece):
    tiles = lax.axis_size("yx")
    return [
        lax.ppermute(piece, "yx", [(i, (i + k) % tiles) for i in range(tiles)]) for k in range(1, tiles)
    ]


def swap(block, axis, mask):
    return lax.ppermute(block, axis, [(i, i ^ mask) for i in range(lax.axis_size(axis))])


def share(stats):
    return lax.all_to_all(stats, PART, 0, 0)


def call(kernel, outs, scratch, *arrays, flops=0, nbytes=0, in_hbm=0, out_hbm=False):
    vmem, hbm = (pl.BlockSpec(memory_space=space) for space in (pltpu.VMEM, pltpu.HBM))
    far, near = arrays[:in_hbm], arrays[in_hbm:]
    far = [pltpu.with_memory_space_constraint(array, pltpu.HBM) for array in far]
    return pl.pallas_call(
        kernel,
        out_shape=[jax.ShapeDtypeStruct(shape, dtype) for shape, dtype in outs],
        in_specs=[hbm] * len(far) + [vmem] * len(near),
        out_specs=[hbm if out_hbm else vmem] * len(outs),
        scratch_shapes=[pltpu.VMEM(*entry) if isinstance(entry, tuple) else entry for entry in scratch],
        compiler_params=pltpu.CompilerParams(vmem_limit_bytes=VMEM_BYTES),
        cost_estimate=pl.CostEstimate(flops=flops, bytes_accessed=nbytes, transcendentals=0),
    )(*far, *near)


def start_kernel(ny, nx, size, x_in, w_in, d_in, y_out, x_out, corners, x, w, lines, sems):
    edge = x_in.shape[0]
    f32, bf16 = jnp.float32, jnp.bfloat16
    above, left = Square().low_sides()
    chunks = 4
    planes = edge // chunks
    first = [
        pltpu.make_async_copy(
            x_in.at[pl.ds(k * planes, planes)],
            x.at[pl.ds(1 + k * planes, planes), pl.ds(1, edge)],
            sems.at[k],
        )
        for k in range(chunks)
    ]
    later = []
    if size:
        at = jnp.minimum(Riders.mine() * size, d_in.shape[0] - size)
        for k, (out, begin) in enumerate(((y_out, edge), (x_out, edge), (corners, 1))):
            later.append(
                pltpu.make_async_copy(
                    d_in.at[pl.ds(at, size)], out.at[0, pl.ds(begin, size)], sems.at[chunks + k]
                )
            )
    later.append(pltpu.make_async_copy(w_in, w, sems.at[chunks + 3]))
    for copy in first + later:
        copy.start()
    x[0] = jnp.zeros(x.shape[1:], bf16)
    x[edge + 1] = jnp.zeros(x.shape[1:], bf16)
    blank = jnp.zeros((edge,) + x.shape[2:], bf16)
    x[1 : edge + 1, 0] = blank
    x[1 : edge + 1, edge + 1] = blank
    flat = lines.reshape(nx * edge * edge * 8, 128)
    part = planes * edge
    for k in range(chunks):
        first[k].wait()
        at, here = pl.ds(k * planes, planes), pl.ds(1 + k * planes, planes)
        for i in range(ny):
            row = jnp.where(above[i], 1, edge)
            y_out[i, at] = x[here, row]
        for j in range(nx):
            low = x[here, 1 : edge + 1, 0:8].astype(f32).reshape(part, 8, 128)
            high = x[here, 1 : edge + 1, edge - 8 : edge].astype(f32).reshape(part, 8, 128)
            high = pltpu.roll(high, 1, 1)
            kept = jnp.where(left[j], low, high)
            lines[j, k * part : k * part + part] = kept
            begin = (j * edge * edge + k * part) * 8
            column = flat[pl.ds(begin, part, stride=8), :]
            x_out[j, at] = column.astype(bf16).reshape(planes, edge, 128)
    for i in range(ny):
        for j in range(nx):
            begin = j * edge * edge * 8
            low = flat[pl.ds(begin, edge, stride=8 * edge), :]
            high = flat[pl.ds(begin + 8 * (edge - 1), edge, stride=8 * edge), :]
            kept = jnp.where(above[i], low, high)
            corners[i * nx + j, 0] = kept.astype(bf16)
    for copy in later:
        copy.wait()


def face_kernel(ny, nx, size, x, y_halos, x_halos, corners, outer, inner, *riders):
    edge = outer.shape[1]
    wide = edge + ny + nx
    odd = lax.axis_index("gz") % 2
    far = edge - 3
    for face, at in ((outer, odd * far), (inner, (1 - odd) * far)):
        for k in range(3):
            row = k * wide
            face[row : row + edge] = x[1 + at + k, 1 : edge + 1]
            for i in range(ny):
                face[row + edge + i] = y_halos[i, at + k]
            for j in range(nx):
                face[row + edge + ny + j] = x_halos[j, at + k]
        for k in range(ny * nx):
            face[3 * wide + k] = corners[k, 0]
    if size:
        riders[0][0] = x_halos[0, edge : edge + size]
        riders[0][1] = y_halos[0, edge : edge + size]
        riders[0][2] = corners[0, 1 : 1 + size]


def spread_taps(weight, taps):
    for tap in range(27):
        row, lane = tap // 3 * 128, tap % 3 * 128
        taps[row : row + 128, lane : lane + 128] = weight[tap]


def pair_taps(weight, pairs):
    for dz in range(3):
        for line in range(4):
            row = (dz * 4 + line) * 128
            for out in range(2):
                lane = out * 128
                if 0 <= line - out < 3:
                    block = weight[dz * 9 + (line - out) * 3 + 2]
                else:
                    block = jnp.zeros((128, 128), pairs.dtype)
                pairs[row : row + 128, lane : lane + 128] = block


def join_x(wide, edge):
    place = lax.broadcasted_iota(jnp.int32, wide.shape[:2] + (128,), 1)
    after = jnp.where(place > 0, pltpu.roll(wide[:, :, :128], 1, 1), 0.0)
    before = jnp.where(place < edge - 1, pltpu.roll(wide[:, :, 256:], edge - 1, 1), 0.0)
    return wide[:, :, 128:256] + after + before


def convolve(grid, spans, taps, pairs):
    edge = grid.shape[2]
    rows = sum(count for _, count in spans) * edge * edge
    halved = grid.reshape(grid.shape[0], edge // 2 + 1, 2, edge, 128)

    def stacked(pieces):
        return jnp.concatenate([piece.reshape(-1, 128) for piece in pieces], axis=0)

    left = jnp.concatenate(
        [
            stacked([grid[z + dz : z + dz + n, dy : dy + edge] for z, n in spans])
            for dz in range(3)
            for dy in range(3)
        ],
        axis=1,
    )
    wide = jnp.dot(left, taps[:, 0:256], preferred_element_type=jnp.float32)
    wide = wide.reshape(rows // edge, edge, 256)
    left = jnp.concatenate(
        [
            stacked(
                [
                    halved[z + dz : z + dz + n, line // 2 : line // 2 + edge // 2, line % 2]
                    for z, n in spans
                ]
            )
            for dz in range(3)
            for line in range(4)
        ],
        axis=1,
    )
    two = jnp.dot(left, pairs[...], preferred_element_type=jnp.float32)
    two = two.reshape(rows // edge // 2, edge, 256)
    two = jnp.stack([two[:, :, :128], two[:, :, 128:]], axis=1).reshape(rows // edge, edge, 128)
    place = lax.broadcasted_iota(jnp.int32, two.shape, 1)
    after = jnp.where(place > 0, pltpu.roll(wide[:, :, :128], 1, 1), 0.0)
    before = jnp.where(place < edge - 1, pltpu.roll(two, edge - 1, 1), 0.0)
    return (wide[:, :, 128:256] + after + before).reshape(-1, edge, edge, 128)


def conv_kernel(deep_in, x, weight, act, taps, pairs, deep_weight, sem):
    copy = pltpu.make_async_copy(deep_in, deep_weight, sem)
    copy.start()
    edge = act.shape[0]
    spread_taps(weight, taps)
    pair_taps(weight, pairs)
    planes = 4
    for z in range(0, edge, planes):
        act[z : z + planes] = convolve(x, [(z, planes)], taps, pairs)
    copy.wait()


def y_terms(line, low, taps):
    planes, edge = line.shape[0] - 2, line.shape[1]
    left = jnp.concatenate(
        [line[dz : dz + planes].reshape(planes * edge, 128) for dz in range(3)], axis=1
    )
    start = jnp.where(low, 0, 256)
    right = jnp.concatenate(
        [taps[pl.ds(pl.multiple_of(start + dz * 384, 128), 128), :] for dz in range(3)], axis=0
    )
    wide = jnp.dot(left, right, preferred_element_type=jnp.float32)
    return join_x(wide.reshape(planes, edge, 384), edge)


def x_terms(column, taps):
    planes, edge = column.shape[0] - 2, column.shape[1] - 16
    lines = [column[:, 7 + dy : 7 + dy + edge].astype(jnp.bfloat16) for dy in range(3)]
    left = jnp.concatenate(
        [line[dz : dz + planes].reshape(planes * edge, 128) for dz in range(3) for line in lines],
        axis=1,
    )
    right = jnp.concatenate([taps[:, 0:128], taps[:, 256:384]], axis=1)
    both = jnp.dot(left, right, preferred_element_type=jnp.float32)
    return both[:, :128], both[:, 128:]


def fill_column(column, at, voxels, ends, above):
    count, edge = voxels.shape[:2]
    rows = edge + 16
    lines = column.reshape(column.shape[0] * rows, 128)
    column[at : at + count, 8 : 8 + edge] = voxels.astype(jnp.float32)
    for i, end in enumerate(ends):
        first = last = end.astype(jnp.float32)
        if len(ends) == 1:
            first, last = jnp.where(above[0], first, 0.0), jnp.where(above[0], 0.0, last)
        if len(ends) == 1 or i == 0:
            lines[pl.ds(at * rows + 7, count, stride=rows), :] = first
        if len(ends) == 1 or i == 1:
            lines[pl.ds(at * rows + 8 + edge, count, stride=rows), :] = last


def add_column(act, terms, j, nx, low):
    planes, edge = act.shape[:2]
    flat = act.reshape(planes * edge * edge, 128)
    first, last = terms
    if nx == 1:
        first, last = jnp.where(low, first, 0.0), jnp.where(low, 0.0, last)
    if nx == 1 or j == 0:
        flat[pl.ds(0, planes * edge, stride=edge), :] += first
    if nx == 1 or j == 1:
        flat[pl.ds(edge - 1, planes * edge, stride=edge), :] += last


def moments(planes):
    count, edge = planes.shape[:2]
    zero = jnp.zeros((8, 128), jnp.float32)

    def sum_step(k, carry):
        return carry + jnp.sum(planes[k].reshape(edge * 2, 8, 128), axis=0)

    mean = lax.fori_loop(0, count, sum_step, zero, unroll=True) / (count * edge * edge // 8)

    def spread_step(k, carry):
        off = planes[k].reshape(edge * 2, 8, 128) - mean
        return carry + jnp.sum(off * off, axis=0)

    return mean, lax.fori_loop(0, count, spread_step, zero, unroll=True)


def side_kernel(ny, nx, own, y_halos, x_halos, corners, taps, inner, ends, stats, act, column):
    edge = own.shape[0]
    act[0] = jnp.zeros(act.shape[1:], jnp.float32)
    act[edge + 1] = jnp.zeros(act.shape[1:], jnp.float32)
    act[1 : edge + 1] = own[...]
    above, left = Square().low_sides()
    blank = jnp.zeros((2, edge, 128), jnp.bfloat16)
    for i in range(ny):
        line = jnp.concatenate([blank, y_halos[i, 0:edge], blank], axis=0)
        act[:, jnp.where(above[i], 0, edge - 1)] += y_terms(line, above[i], taps)
    for j in range(nx):
        column[...] = jnp.zeros(column.shape, jnp.float32)
        fill_column(
            column, 2, x_halos[j, 0:edge], [corners[i * nx + j, 0] for i in range(ny)], above
        )
        add_column(act, x_terms(column, taps), j, nx, left[j])
    inner[...] = act[2:edge]
    ends[0:2] = act[0:2]
    ends[2:4] = act[edge : edge + 2]
    mean, spread = moments(act.at[2:edge])
    stats[0:8] = mean
    stats[8:16] = spread


def end_kernel(ny, nx, *refs):
    x, inner_stats, partial, outer_face, inner_face, taps, pairs, act, stats, rims, grid, column = refs
    edge = x.shape[2]
    wide_face = edge + ny + nx
    f32 = jnp.float32
    above, left = Square().low_sides()
    odd = lax.axis_index("gz") % 2 == 1
    blank = jnp.zeros(grid.shape[:1] + grid.shape[2:], grid.dtype)
    grid[:, 0] = blank
    grid[:, edge + 1] = blank
    act[0] = jnp.zeros(act.shape[1:], f32)
    act[1:5] = partial[...]
    act[5] = jnp.zeros(act.shape[1:], f32)
    sides = ((outer_face, odd, 0), (inner_face, jnp.logical_not(odd), 4))
    for face, behind, base in sides:
        first = base + jnp.where(behind, 1, 0)
        side = jnp.where(behind, 1, 0)
        for k in range(3):
            begin = k * wide_face
            grid[first + k, 1 : edge + 1] = face[begin : begin + edge]
            rims[side, k * (ny + nx) : (k + 1) * (ny + nx)] = face[begin + edge : begin + wide_face]
        rims[side, 3 * (ny + nx) :] = face[3 * wide_face :]
        grid[base + jnp.where(behind, 0, 3), 1 : edge + 1] = x[
            jnp.where(behind, edge, 1), 1 : edge + 1
        ]
    beyond = convolve(grid, [(0, 2), (4, 2)], taps, pairs)
    for (_, behind, base), new in zip(sides, (beyond[0:2], beyond[2:4])):
        act[pl.ds(jnp.where(behind, 4, 0), 2)] += new
        beside = base + jnp.where(behind, 1, 2)
        lines = [grid[beside, dy : dy + edge].reshape(edge * edge, 128) for dy in range(3)]
        rows = taps[pl.ds(pl.multiple_of(jnp.where(behind, 768, 0), 128), 384), :]
        wide = jnp.dot(jnp.concatenate(lines, axis=1), rows, preferred_element_type=f32)
        act[jnp.where(behind, 3, 2)] += join_x(wide.reshape(edge, edge, 384), edge)

    gap = jnp.zeros((2, edge, 128), grid.dtype)
    for side in range(2):

        def rim(row):
            return jnp.stack([rims[side, k * (ny + nx) + row] for k in range(3)])

        three = act.at[3 * side : 3 * side + 3]
        for i in range(ny):
            line = [rim(i), gap] if side == 0 else [gap, rim(i)]
            three[:, jnp.where(above[i], 0, edge - 1)] += y_terms(
                jnp.concatenate(line, axis=0), above[i], taps
            )
        for j in range(nx):
            column[...] = jnp.zeros(column.shape, f32)
            ends = []
            for i in range(ny):
                tile = rims[side, 3 * (ny + nx) + i * nx + j].astype(f32)
                ends.append(tile[edge - 3 :] if side == 0 else tile[:3])
            fill_column(column, 0 if side == 0 else 2, rim(ny + j), ends, above)
            add_column(three, x_terms(column, taps), j, nx, left[j])

    mean, spread = moments(act.at[2:4])
    few, many = edge * edge // 4, (edge - 2) * edge * edge // 8
    inner_mean, inner_spread = inner_stats[0:8], inner_stats[8:16]
    off = inner_mean - mean
    share_of = few / (few + many)
    spread = spread + inner_spread + (many * share_of) * (off * off)
    put_stats(stats, inner_mean - share_of * off, spread, few + many)


def merge(mean, spread, rows, other_mean, other_spread):
    off = mean - other_mean
    return 0.5 * (mean + other_mean), spread + other_spread + (0.5 * rows) * (off * off)


def put_stats(stats, mean, spread, rows):
    for step in (1, 2, 4):
        others = pltpu.roll(mean, step, 0), pltpu.roll(spread, step, 0)
        mean, spread = merge(mean, spread, float(rows * step), *others)
    both = jnp.concatenate([mean[0:1], spread[0:1]], axis=0)
    stats[...] = jnp.broadcast_to(both[None], stats.shape)


def read_stats(stats, rows):
    devices, _, channels = stats.shape
    shape = (8, channels)
    means = [jnp.broadcast_to(stats[k, 0:1, :], shape) for k in range(devices)]
    spreads = [jnp.broadcast_to(stats[k, 1:2, :], shape) for k in range(devices)]
    mean = functools.reduce(jnp.add, means) / devices
    spread = functools.reduce(jnp.add, spreads)
    spread = spread + rows * functools.reduce(jnp.add, [(m - mean) * (m - mean) for m in means])
    rows = rows * devices
    lane = lax.broadcasted_iota(jnp.int32, shape, 1)
    step = 1
    while step < channels // GROUPS:
        low = jnp.bitwise_and(lane, step) == 0
        others = [
            jnp.where(low, pltpu.roll(row, channels - step, 1), pltpu.roll(row, step, 1))
            for row in (mean, spread)
        ]
        mean, spread = merge(mean, spread, rows, *others)
        rows, step = 2.0 * rows, 2 * step
    return mean, lax.rsqrt(spread / rows + EPSILON)


def silu_of_double(h):
    return h + h * jnp.tanh(h)


def norm_kernel(ny, nx, inner, ends, stats, gain, offset, out, pooled, *refs):
    y_edges, x_edges, corners, half = refs
    depth, edge = inner.shape[0] + 6, inner.shape[1]
    deep, deep_depth = edge // 2, depth // 2
    f32, bf16 = jnp.float32, jnp.bfloat16
    above, left = Square().low_sides()
    depth_at = lax.axis_index("gz")
    mean, scale = read_stats(stats, float(edge**3))
    scale = scale * (0.5 * gain[...])
    shift = 0.5 * offset[...]
    for k in range(deep_depth):
        value = [
            ends[z] if z < 3 else inner[z - 3] if z < depth - 3 else ends[z - depth + 6]
            for z in (2 * k, 2 * k + 1)
        ]
        value = jnp.stack(value).reshape(edge * edge // 4, 8, 128)
        value = silu_of_double((value - mean) * scale + shift)
        value = value.reshape(2, edge, edge, 128).astype(bf16)
        if 0 < k < deep_depth - 1:
            out[2 * k - 2 : 2 * k] = value
        value = value.astype(f32)
        value = (value[0] + value[1]).reshape(deep, 2, edge, 128)
        half[k] = (value[:, 0] + value[:, 1]).reshape(deep * edge, 128)
        lines = half.at[k]
        pair = lines[pl.ds(0, deep * deep, stride=2), :] + lines[pl.ds(1, deep * deep, stride=2), :]
        pair = (pair * 0.125).astype(bf16).astype(f32).reshape(deep, deep, 128)
        if k == 0 or k == deep_depth - 1:
            inside = depth_at > 0 if k == 0 else depth_at < lax.axis_size("gz") - 1
            pair = jnp.where(inside, pair, 0.0)
        pooled[k] = pair
    lines = pooled.reshape(deep_depth * deep * deep, 128)
    rows = deep_depth * deep
    first_x = lines[pl.ds(0, rows, stride=deep), :]
    last_x = lines[pl.ds(deep - 1, rows, stride=deep), :]
    first_y, last_y = (pooled[:, y].reshape(rows, 128) for y in (0, deep - 1))
    ends = []
    for y in (0, deep - 1):
        for x in (0, deep - 1):
            ends.append(lines[pl.ds(y * deep + x, deep_depth, stride=deep * deep), :])
    if ny == 1:
        above, left = above[0], left[0]
        y_edges[0] = jnp.where(above, first_y, last_y).astype(bf16)
        x_edges[0] = jnp.where(left, first_x, last_x).astype(bf16)
        corners[0, 0:deep_depth] = jnp.where(
            above, jnp.where(left, ends[0], ends[1]), jnp.where(left, ends[2], ends[3])
        )
    else:
        y_edges[0], y_edges[1] = first_y.astype(bf16), last_y.astype(bf16)
        x_edges[0], x_edges[1] = first_x.astype(bf16), last_x.astype(bf16)
        for k in range(4):
            corners[k, 0:deep_depth] = ends[k]


def stack_kernel(*refs):
    out = refs[-1]
    for k in range(out.shape[0]):
        out[k] = refs[k][...]


def stack(*arrays):
    vmem = pl.BlockSpec(memory_space=pltpu.VMEM)
    return pl.pallas_call(
        stack_kernel,
        out_shape=jax.ShapeDtypeStruct((len(arrays),) + arrays[0].shape, arrays[0].dtype),
        in_specs=[vmem] * len(arrays),
        out_specs=vmem,
        compiler_params=pltpu.CompilerParams(vmem_limit_bytes=VMEM_BYTES),
    )(*arrays)


def place_weights(own, held, out):
    tile = lax.axis_index("yx")
    out[tile] = own[...]
    if len(held) == 1:
        pieces, others, size = held[0].shape[:3]
        for piece in range(pieces):
            at = jnp.minimum(jnp.bitwise_xor(Riders.mine(), piece) * size, own.shape[0] - size)
            for k in range(others):
                out[jnp.bitwise_xor(tile, k + 1), pl.ds(at, size)] = held[0][piece, k]
    else:
        for k, shard in enumerate(held):
            out[lax.rem(tile + len(held) - k, len(held) + 1)] = shard[...]


def tap_rows(weight, taps):
    per = weight.shape[1] // 27
    return jnp.concatenate(
        [weight[:, pl.ds(tap * per, per)].reshape(-1, 128) for tap in taps], axis=1
    )


def dot_rows(left, right):
    return lax.dot_general(
        left, right, (((1,), (1,)), ((), ())), preferred_element_type=jnp.float32
    )


def deep_kernel(pooled, own, *refs):
    *held, act, weight, grid, packed = refs
    depth, deep = pooled.shape[0], pooled.shape[1]
    place_weights(own, held, weight)
    grid[...] = jnp.zeros(grid.shape, jnp.float32)
    grid[:, 1 : deep + 1, 8:16] = pooled[...]
    for dx in range(3):
        plane = grid[:, :, 7 + dx : 15 + dx]
        for y in range(deep + 1):
            both = jnp.concatenate([plane[:, y], plane[:, y + 1]], axis=1)
            packed[:, y // 2, y % 2, :, dx * 128 : dx * 128 + 128] = both.astype(jnp.bfloat16)
    rows = deep**3
    total = None
    for dz in range(3):
        left = jnp.concatenate(
            [
                packed[dz : dz + deep, dy // 2 : dy // 2 + deep // 2, dy % 2].reshape(rows, 384)
                for dy in range(3)
            ],
            axis=1,
        )
        term = dot_rows(left, tap_rows(weight, range(dz * 9, dz * 9 + 9)))
        total = term if total is None else total + term
    for half in range(act.shape[0]):
        act[half] = total[:, half * 128 : half * 128 + 128]


def deep_rim_kernel(ny, nx, own, y_halos, x_halos, corners, weight, act, stats, line):
    depth, deep = line.shape[0], line.shape[1] - 16
    halves = act.shape[0]
    f32 = jnp.float32
    square = deep * deep
    above, left = Square().low_sides()
    act[...] = own[...]
    flat = line.reshape(depth * line.shape[1], 128)

    def shifts():
        return jnp.concatenate(
            [
                line[dz : dz + deep, 7 + d : 7 + d + deep].reshape(square, 128).astype(jnp.bfloat16)
                for dz in range(3)
                for d in range(3)
            ],
            axis=1,
        )

    for i in range(ny):
        line[...] = jnp.zeros(line.shape, f32)
        line[:, 8 : 8 + deep] = y_halos[i].astype(f32).reshape(depth, deep, 128)
        for j in range(nx):
            end = corners[i * nx + j, 0:depth]
            first, last = jnp.where(left[j], end, 0.0), jnp.where(left[j], 0.0, end)
            if nx == 1 or j == 0:
                flat[pl.ds(7, depth, stride=line.shape[1]), :] = first
            if nx == 1 or j == 1:
                flat[pl.ds(8 + deep, depth, stride=line.shape[1]), :] = last
        tap = jnp.where(above[i], 0, 6)
        taps = [tap + dz * 9 + dx for dz in range(3) for dx in range(3)]
        terms = dot_rows(shifts(), tap_rows(weight, taps))
        for half in range(halves):
            rows = act.at[half].reshape(deep, deep, deep, 128)
            term = terms[:, half * 128 : half * 128 + 128].reshape(deep, deep, 128)
            rows[:, jnp.where(above[i], 0, deep - 1)] += term
    for j in range(nx):
        line[...] = jnp.zeros(line.shape, f32)
        line[:, 8 : 8 + deep] = x_halos[j].astype(f32).reshape(depth, deep, 128)
        tap = jnp.where(left[j], 0, 2)
        taps = [tap + dz * 9 + dy * 3 for dz in range(3) for dy in range(3)]
        terms = dot_rows(shifts(), tap_rows(weight, taps))
        first, last = jnp.where(left[j], terms, 0.0), jnp.where(left[j], 0.0, terms)
        for half in range(halves):
            lanes, rows = slice(half * 128, half * 128 + 128), act.at[half]
            if nx == 1 or j == 0:
                rows[pl.ds(0, square, stride=deep), :] += first[:, lanes]
            if nx == 1 or j == 1:
                rows[pl.ds(deep - 1, square, stride=deep), :] += last[:, lanes]

    rows = deep**3 // 8
    means, spreads = [], []
    for half in range(halves):
        total = act[half].reshape(rows, 8, 128)
        means.append(jnp.sum(total, axis=0) / rows)
        off = total - means[-1]
        spreads.append(jnp.sum(off * off, axis=0))
    put_stats(stats, *(jnp.concatenate(part, axis=1) for part in (means, spreads)), rows)


def final_kernel(act, stats, gain, offset, up, mid, out, wide, held, sems):
    edge = mid.shape[0]
    deep = edge // 2
    f32 = jnp.float32
    mean, scale = read_stats(stats, float(deep**3))
    scale = scale * (0.5 * gain[...])
    shift = 0.5 * offset[...]
    planes = 2
    size = planes * deep * deep
    copies = []
    for k in range(0, deep, planes):
        at = slice(k * deep * deep, k * deep * deep + size)
        value = jnp.concatenate([act[half, at] for half in range(act.shape[0])], axis=1)
        value = value.reshape(size // 8, 8, -1)
        value = silu_of_double((value - mean) * scale + shift)
        value = value.reshape(size, -1).astype(jnp.bfloat16)
        lifted = jnp.dot(value, up[...], preferred_element_type=f32)
        lines = wide.at[k // planes]
        lines[pl.ds(0, size, stride=2), :] = lifted
        lines[pl.ds(1, size, stride=2), :] = lifted
        add = lines[...].reshape(planes, 1, deep, 1, edge, 128)
        at = pl.ds(2 * k, 2 * planes)
        old = mid[at].astype(f32).reshape(planes, 2, deep, 2, edge, 128)
        held[at] = (old + add).astype(jnp.bfloat16).reshape(2 * planes, edge, edge, 128)
        copy = pltpu.make_async_copy(held.at[at], out.at[at], sems.at[k // planes])
        copy.start()
        copies.append(copy)
    for copy in copies:
        copy.wait()


def body(
    features, conv_weight, gain_mid, offset_mid, deep_weight, gain_deep, offset_deep, up_weight
):
    f32, bf16 = jnp.float32, jnp.bfloat16
    edge, channels = features.shape[0], features.shape[3]
    deep = edge // 2
    deep_channels = gain_deep.shape[0]
    square = Square()
    tiles = square.tiles
    devices = lax.axis_size("gz") * tiles
    ny, nx = (len(sides) for sides in square.low_sides())
    riders = Riders(deep_weight.shape[4])

    own = jnp.moveaxis(deep_weight, 4, 3).reshape(-1, 16, channels)
    conv_weight = conv_weight.reshape(27, channels, channels)
    *edges, field, conv_weight = call(
        functools.partial(start_kernel, ny, nx, riders.size),
        [
            ((ny, edge + riders.size, edge, channels), bf16),
            ((nx, edge + riders.size, edge, channels), bf16),
            ((ny * nx, 1 + riders.size, edge, channels), bf16),
            ((edge + 2, edge + 2, edge, channels), bf16),
            (conv_weight.shape, bf16),
        ],
        [((nx, edge * edge, 8, channels), f32), pltpu.SemaphoreType.DMA((8,))],
        features,
        conv_weight,
        own,
        nbytes=5 << 20,
        in_hbm=3,
    )
    halos = square.halos(*(list(piece) for piece in edges))
    conv_flops = 54 * channels * channels * edge**3
    act, taps, pairs, own = call(
        conv_kernel,
        [
            ((edge, edge, edge, channels), f32),
            ((9 * channels, 3 * channels), bf16),
            ((12 * channels, 2 * channels), bf16),
            (own.shape, bf16),
        ],
        [pltpu.SemaphoreType.DMA],
        own,
        field,
        conv_weight,
        flops=conv_flops,
        nbytes=6 << 20,
        in_hbm=1,
    )
    (y, x, corner), act = lax.optimization_barrier((halos, act))
    y, x, corner = jnp.stack(y), jnp.stack(x), jnp.stack(corner)
    face = ((3 * (edge + ny + nx) + ny * nx, edge, channels), bf16)
    held = [((3, riders.size, 16, channels), bf16)] if riders.size else []
    outer, inner, *held = call(
        functools.partial(face_kernel, ny, nx, riders.size),
        [face, face] + held,
        [],
        field,
        y,
        x,
        corner,
    )
    outer, inner = swap_depth(outer, inner)
    if riders.size:
        held = held[0][None]
        other = swap(held, *riders.STEPS[0])
    else:
        held = rotate_shards(own)
    six = ((6, edge, edge, channels), f32)
    column = (edge + 16, channels)
    middle, partial, stats = call(
        functools.partial(side_kernel, ny, nx),
        [
            ((edge - 2, edge, edge, channels), f32),
            ((4, edge, edge, channels), f32),
            ((16, channels), f32),
        ],
        [((edge + 2, edge, edge, channels), f32), ((edge + 4,) + column, f32)],
        act,
        y,
        x,
        corner,
        taps,
        flops=conv_flops // 4,
        nbytes=6 << 20,
    )
    ends, stats = call(
        functools.partial(end_kernel, ny, nx),
        [six, ((devices, 2, channels), f32)],
        [
            ((2, 3 * (ny + nx) + ny * nx, edge, channels), bf16),
            ((8, edge + 2, edge, channels), bf16),
            ((5,) + column, f32),
        ],
        field,
        stats,
        partial,
        outer,
        inner,
        taps,
        pairs,
        flops=conv_flops // 2,
        nbytes=3 << 20,
    )
    if riders.size:
        stats, other = lax.optimization_barrier((stats, other))
        held = stack(held, other).reshape((-1,) + held.shape[1:])
        other = swap(held, *riders.STEPS[1])
        stats = share(stats)
        stats, other = lax.optimization_barrier((stats, other))
        held = stack(held, other).reshape((-1,) + held.shape[1:])
        other = swap(held, *riders.STEPS[2])
        held = [stack(held, other).reshape((-1,) + held.shape[1:])]
    else:
        stats = share(stats)
    out, pooled, *edges = call(
        functools.partial(norm_kernel, ny, nx),
        [
            ((edge, edge, edge, channels), bf16),
            ((deep + 2, deep, deep, channels), f32),
            ((ny, (deep + 2) * deep, channels), bf16),
            ((nx, (deep + 2) * deep, channels), bf16),
            ((ny * nx, 16, channels), f32),
        ],
        [((deep + 2, deep * edge, channels), f32)],
        middle,
        ends,
        stats,
        gain_mid.reshape(1, channels),
        offset_mid.reshape(1, channels),
        flops=20 * channels * edge**3,
        nbytes=3 << 20,
    )
    y, x, corner = square.halos(*(list(piece) for piece in edges))
    halves = ((deep_channels // 128, deep**3, 128), f32)
    deep_act, weight = call(
        deep_kernel,
        [halves, ((tiles,) + own.shape, bf16)],
        [
            ((deep + 2, deep + 2, 24, channels), f32),
            ((deep + 2, deep // 2 + 1, 2, 16, 3 * channels), bf16),
        ],
        pooled,
        own,
        *held,
        flops=54 * channels * deep_channels * deep**3,
        nbytes=4 << 20,
    )
    deep_act, stats = call(
        functools.partial(deep_rim_kernel, ny, nx),
        [halves, ((devices, 2, deep_channels), f32)],
        [((deep + 2, 24, channels), f32)],
        deep_act,
        jnp.stack(y),
        jnp.stack(x),
        jnp.stack(corner),
        weight,
        flops=4 * channels * deep_channels * deep**3,
        nbytes=3 << 20,
    )
    stats = share(stats)
    (decoded,) = call(
        final_kernel,
        [((edge, edge, edge, channels), bf16)],
        [
            ((deep // 2, 4 * deep * deep, channels), f32),
            ((edge, edge, edge, channels), bf16),
            pltpu.SemaphoreType.DMA((deep // 2,)),
        ],
        deep_act,
        stats,
        gain_deep.reshape(1, deep_channels),
        offset_deep.reshape(1, deep_channels),
        up_weight,
        out,
        flops=4 * deep_channels * channels * deep**3,
        nbytes=3 << 20,
        out_hbm=True,
    )
    return decoded


def solution(mesh):
    placed = (
        P(("cand", "gz"), "yx", None, None),
        P(),
        P(),
        P(),
        P(None, None, None, None, "yx"),
        P(),
        P(),
        P(),
    )
    return jax.shard_map(
        body,
        mesh=mesh,
        in_specs=placed,
        out_specs=P(("cand", "gz"), "yx", None, None),
        check_vma=False,
    )
```

```python
import functools
import math

import jax
import jax.numpy as jnp
from jax import lax
from jax.experimental import pallas as pl
from jax.experimental.pallas import tpu as pltpu
from jax.sharding import PartitionSpec as P

GROUPS = 32
EPSILON = 1e-05
PART = ("gz", "yx")
VMEM_BYTES = 32 * 1024 * 1024


class Square:
    def __init__(self):
        self.tiles = lax.axis_size("yx")
        self.side = math.isqrt(self.tiles)
        tile = lax.axis_index("yx")
        self.row, self.column = tile // self.side, tile % self.side
        self.folded = self.side == 2
        self.steps = (0,) if self.folded else (-1, 1)

    def low_sides(self):
        if self.folded:
            return [self.row == 1], [self.column == 1]
        return [True, False], [True, False]

    def route(self, down, right):
        pairs = []
        for tile in range(self.tiles):
            row, column = tile // self.side + down, tile % self.side + right
            if 0 <= row < self.side and 0 <= column < self.side:
                pairs.append((tile, row * self.side + column))
        return pairs

    def swap_route(self, mask):
        return [(tile, tile ^ mask) for tile in range(self.tiles)]

    def halos(self, y_edges, x_edges, corners):
        if self.folded:
            y = lax.ppermute(y_edges[0], "yx", self.swap_route(2))
            x = lax.ppermute(x_edges[0], "yx", self.swap_route(1))
            corner = lax.ppermute(corners[0], "yx", self.swap_route(3))
            return [y], [x], [corner]
        y = [lax.ppermute(y_edges[k], "yx", self.route((1, -1)[1 - k], 0)) for k in (1, 0)]
        x = [lax.ppermute(x_edges[k], "yx", self.route(0, (1, -1)[1 - k])) for k in (1, 0)]
        corner = [
            lax.ppermute(corners[2 * k + j], "yx", self.route((1, -1)[1 - k], (1, -1)[1 - j]))
            for k in (1, 0)
            for j in (1, 0)
        ]
        return y, x, corner


def swap_depth(outer, inner):
    size = lax.axis_size("gz")
    routes = [[], []]
    for low in range(size - 1):
        routes[low % 2] += [(low, low + 1), (low + 1, low)]
    return lax.ppermute(outer, "gz", routes[1]), lax.ppermute(inner, "gz", routes[0])


class Riders:
    STEPS = (("cand", 1), ("gz", 2), ("gz", 1))

    def __init__(self, rows):
        self.tiles = 27 * rows // 16
        self.fits = (
            lax.axis_size("yx") == 4
            and lax.axis_size("cand") % 2 == 0
            and lax.axis_size("gz") % 4 == 0
            and self.tiles >= 8
        )
        self.size = -(-self.tiles // 8) if self.fits else 0

    @classmethod
    def mine(cls):
        return sum(
            lax.axis_index(axis) // mask % 2 * 2**k for k, (axis, mask) in enumerate(cls.STEPS)
        )


def rotate_shards(piece):
    tiles = lax.axis_size("yx")
    return [
        lax.ppermute(piece, "yx", [(i, (i + k) % tiles) for i in range(tiles)]) for k in range(1, tiles)
    ]


def swap(block, axis, mask):
    return lax.ppermute(block, axis, [(i, i ^ mask) for i in range(lax.axis_size(axis))])


def share(stats):
    return lax.all_to_all(stats, PART, 0, 0)


def call(kernel, outs, scratch, *arrays, flops=0, nbytes=0, in_hbm=0, out_hbm=False):
    vmem, hbm = (pl.BlockSpec(memory_space=space) for space in (pltpu.VMEM, pltpu.HBM))
    far, near = arrays[:in_hbm], arrays[in_hbm:]
    far = [pltpu.with_memory_space_constraint(array, pltpu.HBM) for array in far]
    return pl.pallas_call(
        kernel,
        out_shape=[jax.ShapeDtypeStruct(shape, dtype) for shape, dtype in outs],
        in_specs=[hbm] * len(far) + [vmem] * len(near),
        out_specs=[hbm if out_hbm else vmem] * len(outs),
        scratch_shapes=[pltpu.VMEM(*entry) if isinstance(entry, tuple) else entry for entry in scratch],
        compiler_params=pltpu.CompilerParams(vmem_limit_bytes=VMEM_BYTES),
        cost_estimate=pl.CostEstimate(flops=flops, bytes_accessed=nbytes, transcendentals=0),
    )(*far, *near)


def start_kernel(ny, nx, size, x_in, w_in, d_in, y_out, x_out, corners, x, w, lines, sems):
    edge = x_in.shape[0]
    f32, bf16 = jnp.float32, jnp.bfloat16
    above, left = Square().low_sides()
    chunks = 4
    planes = edge // chunks
    first = [
        pltpu.make_async_copy(
            x_in.at[pl.ds(k * planes, planes)],
            x.at[pl.ds(1 + k * planes, planes), pl.ds(1, edge)],
            sems.at[k],
        )
        for k in range(chunks)
    ]
    later = []
    if size:
        at = jnp.minimum(Riders.mine() * size, d_in.shape[0] - size)
        for k, (out, begin) in enumerate(((y_out, edge), (x_out, edge), (corners, 1))):
            later.append(
                pltpu.make_async_copy(
                    d_in.at[pl.ds(at, size)], out.at[0, pl.ds(begin, size)], sems.at[chunks + k]
                )
            )
    later.append(pltpu.make_async_copy(w_in, w, sems.at[chunks + 3]))
    for copy in first + later:
        copy.start()
    x[0] = jnp.zeros(x.shape[1:], bf16)
    x[edge + 1] = jnp.zeros(x.shape[1:], bf16)
    blank = jnp.zeros((edge,) + x.shape[2:], bf16)
    x[1 : edge + 1, 0] = blank
    x[1 : edge + 1, edge + 1] = blank
    flat = lines.reshape(nx * edge * edge * 8, 128)
    part = planes * edge
    for k in range(chunks):
        first[k].wait()
        at, here = pl.ds(k * planes, planes), pl.ds(1 + k * planes, planes)
        for i in range(ny):
            row = jnp.where(above[i], 1, edge)
            y_out[i, at] = x[here, row]
        for j in range(nx):
            low = x[here, 1 : edge + 1, 0:8].astype(f32).reshape(part, 8, 128)
            high = x[here, 1 : edge + 1, edge - 8 : edge].astype(f32).reshape(part, 8, 128)
            high = pltpu.roll(high, 1, 1)
            kept = jnp.where(left[j], low, high)
            lines[j, k * part : k * part + part] = kept
            begin = (j * edge * edge + k * part) * 8
            column = flat[pl.ds(begin, part, stride=8), :]
            x_out[j, at] = column.astype(bf16).reshape(planes, edge, 128)
    for i in range(ny):
        for j in range(nx):
            begin = j * edge * edge * 8
            low = flat[pl.ds(begin, edge, stride=8 * edge), :]
            high = flat[pl.ds(begin + 8 * (edge - 1), edge, stride=8 * edge), :]
            kept = jnp.where(above[i], low, high)
            corners[i * nx + j, 0] = kept.astype(bf16)
    for copy in later:
        copy.wait()


def face_kernel(ny, nx, size, x, y_halos, x_halos, corners, outer, inner, *riders):
    edge = outer.shape[1]
    wide = edge + ny + nx
    odd = lax.axis_index("gz") % 2
    far = edge - 3
    for face, at in ((outer, odd * far), (inner, (1 - odd) * far)):
        for k in range(3):
            row = k * wide
            face[row : row + edge] = x[1 + at + k, 1 : edge + 1]
            for i in range(ny):
                face[row + edge + i] = y_halos[i, at + k]
            for j in range(nx):
                face[row + edge + ny + j] = x_halos[j, at + k]
        for k in range(ny * nx):
            face[3 * wide + k] = corners[k, 0]
    for k in range(inner.shape[0], outer.shape[0]):
        outer[k] = corners[0, 0]
    if size:
        riders[0][0] = x_halos[0, edge : edge + size]
        riders[0][1] = y_halos[0, edge : edge + size]
        riders[0][2] = corners[0, 1 : 1 + size]
        riders[0][3] = corners[0, 1 : 1 + size]


def spread_taps(weight, taps):
    for tap in range(27):
        row, lane = tap // 3 * 128, tap % 3 * 128
        taps[row : row + 128, lane : lane + 128] = weight[tap]


def pair_taps(weight, pairs):
    for dz in range(3):
        for line in range(4):
            row = (dz * 4 + line) * 128
            for out in range(2):
                lane = out * 128
                if 0 <= line - out < 3:
                    block = weight[dz * 9 + (line - out) * 3 + 2]
                else:
                    block = jnp.zeros((128, 128), pairs.dtype)
                pairs[row : row + 128, lane : lane + 128] = block


def join_x(wide, edge):
    place = lax.broadcasted_iota(jnp.int32, wide.shape[:2] + (128,), 1)
    after = jnp.where(place > 0, pltpu.roll(wide[:, :, :128], 1, 1), 0.0)
    before = jnp.where(place < edge - 1, pltpu.roll(wide[:, :, 256:], edge - 1, 1), 0.0)
    return wide[:, :, 128:256] + after + before


def convolve(grid, count, taps, pairs, put):
    edge = grid.shape[2]
    planes = min(count, 4)
    rows = planes * edge * edge
    place = lax.broadcasted_iota(jnp.int32, (planes * edge, edge, 128), 1)
    halved = grid.reshape(grid.shape[0], edge // 2 + 1, 2, edge, 128)
    for z in range(0, count, planes):
        left = jnp.concatenate(
            [
                grid[z + dz : z + dz + planes, dy : dy + edge].reshape(rows, 128)
                for dz in range(3)
                for dy in range(3)
            ],
            axis=1,
        )
        wide = jnp.dot(left, taps[:, 0:256], preferred_element_type=jnp.float32)
        wide = wide.reshape(planes * edge, edge, 256)
        left = jnp.concatenate(
            [
                halved[z + dz : z + dz + planes, line // 2 : line // 2 + edge // 2, line % 2].reshape(
                    rows // 2, 128
                )
                for dz in range(3)
                for line in range(4)
            ],
            axis=1,
        )
        two = jnp.dot(left, pairs[...], preferred_element_type=jnp.float32)
        two = two.reshape(planes * edge // 2, edge, 256)
        two = jnp.stack([two[:, :, :128], two[:, :, 128:]], axis=1).reshape(planes * edge, edge, 128)
        after = jnp.where(place > 0, pltpu.roll(wide[:, :, :128], 1, 1), 0.0)
        before = jnp.where(place < edge - 1, pltpu.roll(two, edge - 1, 1), 0.0)
        new = wide[:, :, 128:256] + after + before
        put(z, new.reshape(planes, edge, edge, 128))


def conv_kernel(deep_in, x, weight, act, taps, pairs, deep_weight, sem):
    copy = pltpu.make_async_copy(deep_in, deep_weight, sem)
    copy.start()
    edge = act.shape[0]
    spread_taps(weight, taps)
    pair_taps(weight, pairs)

    def put(z, new):
        act[z : z + new.shape[0]] = new

    convolve(x, edge, taps, pairs, put)
    copy.wait()


def y_terms(line, low, taps):
    planes, edge = line.shape[0] - 2, line.shape[1]
    left = jnp.concatenate(
        [line[dz : dz + planes].reshape(planes * edge, 128) for dz in range(3)], axis=1
    )
    start = jnp.where(low, 0, 256)
    right = jnp.concatenate(
        [taps[pl.ds(pl.multiple_of(start + dz * 384, 128), 128), :] for dz in range(3)], axis=0
    )
    wide = jnp.dot(left, right, preferred_element_type=jnp.float32)
    return join_x(wide.reshape(planes, edge, 384), edge)


def x_terms(column, taps):
    planes, edge = column.shape[0] - 2, column.shape[1] - 16
    lines = [column[:, 7 + dy : 7 + dy + edge].astype(jnp.bfloat16) for dy in range(3)]
    left = jnp.concatenate(
        [line[dz : dz + planes].reshape(planes * edge, 128) for dz in range(3) for line in lines],
        axis=1,
    )
    right = jnp.concatenate([taps[:, 0:128], taps[:, 256:384]], axis=1)
    both = jnp.dot(left, right, preferred_element_type=jnp.float32)
    return both[:, :128], both[:, 128:]


def fill_column(column, at, voxels, ends, above):
    count, edge = voxels.shape[:2]
    rows = edge + 16
    lines = column.reshape(column.shape[0] * rows, 128)
    column[at : at + count, 8 : 8 + edge] = voxels.astype(jnp.float32)
    for i, end in enumerate(ends):
        first = last = end.astype(jnp.float32)
        if len(ends) == 1:
            first, last = jnp.where(above[0], first, 0.0), jnp.where(above[0], 0.0, last)
        if len(ends) == 1 or i == 0:
            lines[pl.ds(at * rows + 7, count, stride=rows), :] = first
        if len(ends) == 1 or i == 1:
            lines[pl.ds(at * rows + 8 + edge, count, stride=rows), :] = last


def add_column(act, terms, j, nx, low):
    planes, edge = act.shape[:2]
    flat = act.reshape(planes * edge * edge, 128)
    first, last = terms
    if nx == 1:
        first, last = jnp.where(low, first, 0.0), jnp.where(low, 0.0, last)
    if nx == 1 or j == 0:
        flat[pl.ds(0, planes * edge, stride=edge), :] += first
    if nx == 1 or j == 1:
        flat[pl.ds(edge - 1, planes * edge, stride=edge), :] += last


def moments(planes):
    count, edge = planes.shape[:2]
    zero = jnp.zeros((8, 128), jnp.float32)

    def sum_step(k, carry):
        return carry + jnp.sum(planes[k].reshape(edge * 2, 8, 128), axis=0)

    mean = lax.fori_loop(0, count, sum_step, zero, unroll=True) / (count * edge * edge // 8)

    def spread_step(k, carry):
        off = planes[k].reshape(edge * 2, 8, 128) - mean
        return carry + jnp.sum(off * off, axis=0)

    return mean, lax.fori_loop(0, count, spread_step, zero, unroll=True)


def side_kernel(ny, nx, own, y_halos, x_halos, corners, taps, inner, ends, stats, act, column):
    edge = own.shape[0]
    act[0] = jnp.zeros(act.shape[1:], jnp.float32)
    act[edge + 1] = jnp.zeros(act.shape[1:], jnp.float32)
    act[1 : edge + 1] = own[...]
    above, left = Square().low_sides()
    blank = jnp.zeros((2, edge, 128), jnp.bfloat16)
    for i in range(ny):
        line = jnp.concatenate([blank, y_halos[i, 0:edge], blank], axis=0)
        act[:, jnp.where(above[i], 0, edge - 1)] += y_terms(line, above[i], taps)
    for j in range(nx):
        column[...] = jnp.zeros(column.shape, jnp.float32)
        fill_column(
            column, 2, x_halos[j, 0:edge], [corners[i * nx + j, 0] for i in range(ny)], above
        )
        add_column(act, x_terms(column, taps), j, nx, left[j])
    inner[...] = act[2:edge]
    ends[0:2] = act[0:2]
    ends[2:4] = act[edge : edge + 2]
    mean, spread = moments(act.at[2:edge])
    stats[0:8] = mean
    stats[8:16] = spread


def end_kernel(ny, nx, *refs):
    x, inner_stats, partial, outer_face, inner_face, taps, pairs, act, stats, faces, grid, column = refs
    edge = x.shape[2]
    wide_face = edge + ny + nx
    f32 = jnp.float32
    odd = lax.axis_index("gz") % 2 == 1
    size = inner_face.shape[0]
    faces[0] = jnp.where(odd, inner_face[...], outer_face[0:size])
    faces[1] = jnp.where(odd, outer_face[0:size], inner_face[...])
    above, left = Square().low_sides()
    blank = jnp.zeros(grid.shape[:1] + grid.shape[2:], grid.dtype)
    grid[:, 0] = blank
    grid[:, edge + 1] = blank
    gap = jnp.zeros((2, edge, 128), grid.dtype)
    for side, halo_at, own_at, plane, at, beyond, own, beside, dz in (
        (0, 0, 3, 1, 0, 0, 2, 2, 0),
        (1, 1, 0, edge, 3, 4, 3, 1, 2),
    ):
        for k in range(3):
            begin = k * wide_face
            grid[halo_at + k, 1 : edge + 1] = faces[side, begin : begin + edge]
        grid[own_at, 1 : edge + 1] = x[plane, 1 : edge + 1]

        def put(z, new):
            act[beyond + z : beyond + z + new.shape[0]] = new

        convolve(grid, 2, taps, pairs, put)
        stacked = jnp.concatenate(
            [grid[beside, dy : dy + edge].reshape(edge * edge, 128) for dy in range(3)], axis=1
        )
        wide = jnp.dot(stacked, taps[dz * 384 : dz * 384 + 384, :], preferred_element_type=f32)
        own_part = partial[1 if side == 0 else 2]
        act[own] = own_part + join_x(wide.reshape(edge, edge, 384), edge)
        near = 1 if side == 0 else 4
        act[near] += partial[0 if side == 0 else 3]

        def rim(row):
            planes = [faces[side, k * wide_face + edge + row] for k in range(3)]
            return jnp.stack(planes)

        three = act.at[at : at + 3]
        for i in range(ny):
            line = [rim(i), gap] if side == 0 else [gap, rim(i)]
            three[:, jnp.where(above[i], 0, edge - 1)] += y_terms(
                jnp.concatenate(line, axis=0), above[i], taps
            )
        for j in range(nx):
            column[...] = jnp.zeros(column.shape, f32)
            ends = []
            for i in range(ny):
                tile = faces[side, 3 * wide_face + i * nx + j].astype(f32)
                ends.append(tile[edge - 3 :] if side == 0 else tile[:3])
            fill_column(column, 0 if side == 0 else 2, rim(ny + j), ends, above)
            add_column(three, x_terms(column, taps), j, nx, left[j])

    mean, spread = moments(act.at[2:4])
    few, many = edge * edge // 4, (edge - 2) * edge * edge // 8
    inner_mean, inner_spread = inner_stats[0:8], inner_stats[8:16]
    off = inner_mean - mean
    share_of = few / (few + many)
    spread = spread + inner_spread + (many * share_of) * (off * off)
    put_stats(stats, inner_mean - share_of * off, spread, few + many)


def merge(mean, spread, rows, other_mean, other_spread):
    off = mean - other_mean
    return 0.5 * (mean + other_mean), spread + other_spread + (0.5 * rows) * (off * off)


def put_stats(stats, mean, spread, rows):
    for step in (1, 2, 4):
        others = pltpu.roll(mean, step, 0), pltpu.roll(spread, step, 0)
        mean, spread = merge(mean, spread, float(rows * step), *others)
    both = jnp.concatenate([mean[0:1], spread[0:1]], axis=0)
    stats[...] = jnp.broadcast_to(both[None], stats.shape)


def read_stats(stats, rows):
    devices, _, channels = stats.shape
    shape = (8, channels)
    means = [jnp.broadcast_to(stats[k, 0:1, :], shape) for k in range(devices)]
    spreads = [jnp.broadcast_to(stats[k, 1:2, :], shape) for k in range(devices)]
    mean = functools.reduce(jnp.add, means) / devices
    spread = functools.reduce(jnp.add, spreads)
    spread = spread + rows * functools.reduce(jnp.add, [(m - mean) * (m - mean) for m in means])
    rows = rows * devices
    lane = lax.broadcasted_iota(jnp.int32, shape, 1)
    step = 1
    while step < channels // GROUPS:
        low = jnp.bitwise_and(lane, step) == 0
        others = [
            jnp.where(low, pltpu.roll(row, channels - step, 1), pltpu.roll(row, step, 1))
            for row in (mean, spread)
        ]
        mean, spread = merge(mean, spread, rows, *others)
        rows, step = 2.0 * rows, 2 * step
    return mean, lax.rsqrt(spread / rows + EPSILON)


def silu_of_double(h):
    return h + h * jnp.tanh(h)


def norm_kernel(ny, nx, inner, ends, stats, gain, offset, out, pooled, *refs):
    y_edges, x_edges, corners, half = refs
    depth, edge = inner.shape[0] + 6, inner.shape[1]
    deep, deep_depth = edge // 2, depth // 2
    f32, bf16 = jnp.float32, jnp.bfloat16
    above, left = Square().low_sides()
    depth_at = lax.axis_index("gz")
    mean, scale = read_stats(stats, float(edge**3))
    scale = scale * (0.5 * gain[...])
    shift = 0.5 * offset[...]
    for k in range(deep_depth):
        value = [
            ends[z] if z < 3 else inner[z - 3] if z < depth - 3 else ends[z - depth + 6]
            for z in (2 * k, 2 * k + 1)
        ]
        value = jnp.stack(value).reshape(edge * edge // 4, 8, 128)
        value = silu_of_double((value - mean) * scale + shift)
        value = value.reshape(2, edge, edge, 128).astype(bf16)
        if 0 < k < deep_depth - 1:
            out[2 * k - 2 : 2 * k] = value
        value = value.astype(f32)
        value = (value[0] + value[1]).reshape(deep, 2, edge, 128)
        half[k] = (value[:, 0] + value[:, 1]).reshape(deep * edge, 128)
        lines = half.at[k]
        pair = lines[pl.ds(0, deep * deep, stride=2), :] + lines[pl.ds(1, deep * deep, stride=2), :]
        pair = (pair * 0.125).astype(bf16).astype(f32).reshape(deep, deep, 128)
        if k == 0 or k == deep_depth - 1:
            inside = depth_at > 0 if k == 0 else depth_at < lax.axis_size("gz") - 1
            pair = jnp.where(inside, pair, 0.0)
        pooled[k] = pair
    lines = pooled.reshape(deep_depth * deep * deep, 128)
    rows = deep_depth * deep
    first_x = lines[pl.ds(0, rows, stride=deep), :]
    last_x = lines[pl.ds(deep - 1, rows, stride=deep), :]
    first_y, last_y = (pooled[:, y].reshape(rows, 128) for y in (0, deep - 1))
    ends = []
    for y in (0, deep - 1):
        for x in (0, deep - 1):
            ends.append(lines[pl.ds(y * deep + x, deep_depth, stride=deep * deep), :])
    if ny == 1:
        above, left = above[0], left[0]
        y_edges[0] = jnp.where(above, first_y, last_y).astype(bf16)
        x_edges[0] = jnp.where(left, first_x, last_x).astype(bf16)
        corners[0, 0:deep_depth] = jnp.where(
            above, jnp.where(left, ends[0], ends[1]), jnp.where(left, ends[2], ends[3])
        )
    else:
        y_edges[0], y_edges[1] = first_y.astype(bf16), last_y.astype(bf16)
        x_edges[0], x_edges[1] = first_x.astype(bf16), last_x.astype(bf16)
        for k in range(4):
            corners[k, 0:deep_depth] = ends[k]


def stack_kernel(*refs):
    out = refs[-1]
    for k in range(out.shape[0]):
        out[k] = refs[k][: out.shape[1], : out.shape[2]]


def stack(*arrays, part=None):
    vmem = pl.BlockSpec(memory_space=pltpu.VMEM)
    shape = (part or arrays[0].shape[:2]) + arrays[0].shape[2:]
    return pl.pallas_call(
        stack_kernel,
        out_shape=jax.ShapeDtypeStruct((len(arrays),) + shape, arrays[0].dtype),
        in_specs=[vmem] * len(arrays),
        out_specs=vmem,
        compiler_params=pltpu.CompilerParams(vmem_limit_bytes=VMEM_BYTES),
    )(*arrays)


def place_weights(own, held, out):
    tile = lax.axis_index("yx")
    out[tile] = own[...]
    if len(held) == 1:
        pieces, others, size = held[0].shape[:3]
        for piece in range(pieces):
            at = jnp.minimum(jnp.bitwise_xor(Riders.mine(), piece) * size, own.shape[0] - size)
            for k in range(others):
                out[jnp.bitwise_xor(tile, k + 1), pl.ds(at, size)] = held[0][piece, k]
    else:
        for k, shard in enumerate(held):
            out[lax.rem(tile + len(held) - k, len(held) + 1)] = shard[...]


def tap_rows(weight, taps):
    per = weight.shape[1] // 27
    return jnp.concatenate(
        [weight[:, pl.ds(tap * per, per)].reshape(-1, 128) for tap in taps], axis=1
    )


def dot_rows(left, right):
    return lax.dot_general(
        left, right, (((1,), (1,)), ((), ())), preferred_element_type=jnp.float32
    )


def deep_kernel(pooled, own, *refs):
    *held, act, weight, grid, packed = refs
    depth, deep = pooled.shape[0], pooled.shape[1]
    place_weights(own, held, weight)
    grid[...] = jnp.zeros(grid.shape, jnp.float32)
    grid[:, 1 : deep + 1, 8:16] = pooled[...]
    for dx in range(3):
        plane = grid[:, :, 7 + dx : 15 + dx]
        for y in range(deep + 1):
            both = jnp.concatenate([plane[:, y], plane[:, y + 1]], axis=1)
            packed[:, y // 2, y % 2, :, dx * 128 : dx * 128 + 128] = both.astype(jnp.bfloat16)
    rows = deep**3
    total = None
    for dz in range(3):
        left = jnp.concatenate(
            [
                packed[dz : dz + deep, dy // 2 : dy // 2 + deep // 2, dy % 2].reshape(rows, 384)
                for dy in range(3)
            ],
            axis=1,
        )
        term = dot_rows(left, tap_rows(weight, range(dz * 9, dz * 9 + 9)))
        total = term if total is None else total + term
    for half in range(act.shape[0]):
        act[half] = total[:, half * 128 : half * 128 + 128]


def deep_rim_kernel(ny, nx, own, y_halos, x_halos, corners, weight, act, stats, line):
    depth, deep = line.shape[0], line.shape[1] - 16
    halves = act.shape[0]
    f32 = jnp.float32
    square = deep * deep
    above, left = Square().low_sides()
    act[...] = own[...]
    flat = line.reshape(depth * line.shape[1], 128)

    def shifts():
        return jnp.concatenate(
            [
                line[dz : dz + deep, 7 + d : 7 + d + deep].reshape(square, 128).astype(jnp.bfloat16)
                for dz in range(3)
                for d in range(3)
            ],
            axis=1,
        )

    for i in range(ny):
        line[...] = jnp.zeros(line.shape, f32)
        line[:, 8 : 8 + deep] = y_halos[i].astype(f32).reshape(depth, deep, 128)
        for j in range(nx):
            end = corners[i * nx + j, 0:depth]
            first, last = jnp.where(left[j], end, 0.0), jnp.where(left[j], 0.0, end)
            if nx == 1 or j == 0:
                flat[pl.ds(7, depth, stride=line.shape[1]), :] = first
            if nx == 1 or j == 1:
                flat[pl.ds(8 + deep, depth, stride=line.shape[1]), :] = last
        tap = jnp.where(above[i], 0, 6)
        taps = [tap + dz * 9 + dx for dz in range(3) for dx in range(3)]
        terms = dot_rows(shifts(), tap_rows(weight, taps))
        for half in range(halves):
            rows = act.at[half].reshape(deep, deep, deep, 128)
            term = terms[:, half * 128 : half * 128 + 128].reshape(deep, deep, 128)
            rows[:, jnp.where(above[i], 0, deep - 1)] += term
    for j in range(nx):
        line[...] = jnp.zeros(line.shape, f32)
        line[:, 8 : 8 + deep] = x_halos[j].astype(f32).reshape(depth, deep, 128)
        tap = jnp.where(left[j], 0, 2)
        taps = [tap + dz * 9 + dy * 3 for dz in range(3) for dy in range(3)]
        terms = dot_rows(shifts(), tap_rows(weight, taps))
        first, last = jnp.where(left[j], terms, 0.0), jnp.where(left[j], 0.0, terms)
        for half in range(halves):
            lanes, rows = slice(half * 128, half * 128 + 128), act.at[half]
            if nx == 1 or j == 0:
                rows[pl.ds(0, square, stride=deep), :] += first[:, lanes]
            if nx == 1 or j == 1:
                rows[pl.ds(deep - 1, square, stride=deep), :] += last[:, lanes]

    rows = deep**3 // 8
    means, spreads = [], []
    for half in range(halves):
        total = act[half].reshape(rows, 8, 128)
        means.append(jnp.sum(total, axis=0) / rows)
        off = total - means[-1]
        spreads.append(jnp.sum(off * off, axis=0))
    put_stats(stats, *(jnp.concatenate(part, axis=1) for part in (means, spreads)), rows)


def final_kernel(act, stats, gain, offset, up, mid, out, wide, held, sems):
    edge = mid.shape[0]
    deep = edge // 2
    f32 = jnp.float32
    mean, scale = read_stats(stats, float(deep**3))
    scale = scale * (0.5 * gain[...])
    shift = 0.5 * offset[...]
    planes = 2
    size = planes * deep * deep
    copies = []
    for k in range(0, deep, planes):
        at = slice(k * deep * deep, k * deep * deep + size)
        value = jnp.concatenate([act[half, at] for half in range(act.shape[0])], axis=1)
        value = value.reshape(size // 8, 8, -1)
        value = silu_of_double((value - mean) * scale + shift)
        value = value.reshape(size, -1).astype(jnp.bfloat16)
        lifted = jnp.dot(value, up[...], preferred_element_type=f32)
        lines = wide.at[k // planes]
        lines[pl.ds(0, size, stride=2), :] = lifted
        lines[pl.ds(1, size, stride=2), :] = lifted
        add = lines[...].reshape(planes, 1, deep, 1, edge, 128)
        at = pl.ds(2 * k, 2 * planes)
        old = mid[at].astype(f32).reshape(planes, 2, deep, 2, edge, 128)
        held[at] = (old + add).astype(jnp.bfloat16).reshape(2 * planes, edge, edge, 128)
        copy = pltpu.make_async_copy(held.at[at], out.at[at], sems.at[k // planes])
        copy.start()
        copies.append(copy)
    for copy in copies:
        copy.wait()


def body(
    features, conv_weight, gain_mid, offset_mid, deep_weight, gain_deep, offset_deep, up_weight
):
    f32, bf16 = jnp.float32, jnp.bfloat16
    edge, channels = features.shape[0], features.shape[3]
    deep = edge // 2
    deep_channels = gain_deep.shape[0]
    square = Square()
    tiles = square.tiles
    devices = lax.axis_size("gz") * tiles
    ny, nx = (len(sides) for sides in square.low_sides())
    riders = Riders(deep_weight.shape[4])

    own = jnp.moveaxis(deep_weight, 4, 3).reshape(-1, 16, channels)
    conv_weight = conv_weight.reshape(27, channels, channels)
    *edges, field, conv_weight = call(
        functools.partial(start_kernel, ny, nx, riders.size),
        [
            ((ny, edge + riders.size, edge, channels), bf16),
            ((nx, edge + riders.size, edge, channels), bf16),
            ((ny * nx, 1 + riders.size, edge, channels), bf16),
            ((edge + 2, edge + 2, edge, channels), bf16),
            (conv_weight.shape, bf16),
        ],
        [((nx, edge * edge, 8, channels), f32), pltpu.SemaphoreType.DMA((8,))],
        features,
        conv_weight,
        own,
        nbytes=5 << 20,
        in_hbm=3,
    )
    halos = square.halos(*(list(piece) for piece in edges))
    conv_flops = 54 * channels * channels * edge**3
    act, taps, pairs, own = call(
        conv_kernel,
        [
            ((edge, edge, edge, channels), f32),
            ((9 * channels, 3 * channels), bf16),
            ((12 * channels, 2 * channels), bf16),
            (own.shape, bf16),
        ],
        [pltpu.SemaphoreType.DMA],
        own,
        field,
        conv_weight,
        flops=conv_flops,
        nbytes=6 << 20,
        in_hbm=1,
    )
    (y, x, corner), act = lax.optimization_barrier((halos, act))
    y, x, corner = jnp.stack(y), jnp.stack(x), jnp.stack(corner)
    face = ((3 * (edge + ny + nx) + ny * nx, edge, channels), bf16)
    held = [((4, riders.size, 16, channels), bf16)] if riders.size else []
    outer, inner, *held = call(
        functools.partial(face_kernel, ny, nx, riders.size),
        [((face[0][0] + 2,) + face[0][1:], bf16), face] + held,
        [],
        field,
        y,
        x,
        corner,
    )
    outer, inner = swap_depth(outer, inner)
    if riders.size:
        held = held[0][None]
        other = swap(held, *riders.STEPS[0])
    else:
        held = rotate_shards(own)
    six = ((6, edge, edge, channels), f32)
    column = (edge + 16, channels)
    middle, partial, stats = call(
        functools.partial(side_kernel, ny, nx),
        [
            ((edge - 2, edge, edge, channels), f32),
            ((4, edge, edge, channels), f32),
            ((16, channels), f32),
        ],
        [((edge + 2, edge, edge, channels), f32), ((edge + 4,) + column, f32)],
        act,
        y,
        x,
        corner,
        taps,
    )
    ends, stats = call(
        functools.partial(end_kernel, ny, nx),
        [six, ((devices, 2, channels), f32)],
        [
            ((2,) + face[0], bf16),
            ((4, edge + 2, edge, channels), bf16),
            ((5,) + column, f32),
        ],
        field,
        stats,
        partial,
        outer,
        inner,
        taps,
        pairs,
    )
    if riders.size:
        stats, other = lax.optimization_barrier((stats, other))
        held = stack(held, other, part=(1, 3)).reshape((2, 3) + held.shape[2:])
        other = swap(held, *riders.STEPS[1])
        stats = share(stats)
        stats, other = lax.optimization_barrier((stats, other))
        held = stack(held, other).reshape((-1,) + held.shape[1:])
        other = swap(held, *riders.STEPS[2])
        held = [stack(held, other).reshape((-1,) + held.shape[1:])]
    else:
        stats = share(stats)
    out, pooled, *edges = call(
        functools.partial(norm_kernel, ny, nx),
        [
            ((edge, edge, edge, channels), bf16),
            ((deep + 2, deep, deep, channels), f32),
            ((ny, (deep + 2) * deep, channels), bf16),
            ((nx, (deep + 2) * deep, channels), bf16),
            ((ny * nx, 16, channels), f32),
        ],
        [((deep + 2, deep * edge, channels), f32)],
        middle,
        ends,
        stats,
        gain_mid.reshape(1, channels),
        offset_mid.reshape(1, channels),
        flops=20 * channels * edge**3,
        nbytes=3 << 20,
    )
    y, x, corner = square.halos(*(list(piece) for piece in edges))
    halves = ((deep_channels // 128, deep**3, 128), f32)
    deep_act, weight = call(
        deep_kernel,
        [halves, ((tiles,) + own.shape, bf16)],
        [
            ((deep + 2, deep + 2, 24, channels), f32),
            ((deep + 2, deep // 2 + 1, 2, 16, 3 * channels), bf16),
        ],
        pooled,
        own,
        *held,
        flops=54 * channels * deep_channels * deep**3,
        nbytes=4 << 20,
    )
    deep_act, stats = call(
        functools.partial(deep_rim_kernel, ny, nx),
        [halves, ((devices, 2, deep_channels), f32)],
        [((deep + 2, 24, channels), f32)],
        deep_act,
        jnp.stack(y),
        jnp.stack(x),
        jnp.stack(corner),
        weight,
        flops=4 * channels * deep_channels * deep**3,
        nbytes=3 << 20,
    )
    stats = share(stats)
    (decoded,) = call(
        final_kernel,
        [((edge, edge, edge, channels), bf16)],
        [
            ((deep // 2, 4 * deep * deep, channels), f32),
            ((edge, edge, edge, channels), bf16),
            pltpu.SemaphoreType.DMA((deep // 2,)),
        ],
        deep_act,
        stats,
        gain_deep.reshape(1, deep_channels),
        offset_deep.reshape(1, deep_channels),
        up_weight,
        out,
        flops=4 * deep_channels * channels * deep**3,
        nbytes=3 << 20,
        out_hbm=True,
    )
    return decoded


def solution(mesh):
    placed = (
        P(("cand", "gz"), "yx", None, None),
        P(),
        P(),
        P(),
        P(None, None, None, None, "yx"),
        P(),
        P(),
        P(),
    )
    return jax.shard_map(
        body,
        mesh=mesh,
        in_specs=placed,
        out_specs=P(("cand", "gz"), "yx", None, None),
        check_vma=False,
    )
```

```python
import functools
import math

import jax
import jax.numpy as jnp
from jax import lax
from jax.experimental import pallas as pl
from jax.experimental.pallas import tpu as pltpu
from jax.sharding import PartitionSpec as P

GROUPS = 32
EPSILON = 1e-05
PART = ("gz", "yx")
VMEM_BYTES = 32 * 1024 * 1024


class Square:
    def __init__(self):
        self.tiles = lax.axis_size("yx")
        self.side = math.isqrt(self.tiles)
        tile = lax.axis_index("yx")
        self.row, self.column = tile // self.side, tile % self.side
        self.folded = self.side == 2
        self.steps = (0,) if self.folded else (-1, 1)

    def low_sides(self):
        if self.folded:
            return [self.row == 1], [self.column == 1]
        return [True, False], [True, False]

    def route(self, down, right):
        pairs = []
        for tile in range(self.tiles):
            row, column = tile // self.side + down, tile % self.side + right
            if 0 <= row < self.side and 0 <= column < self.side:
                pairs.append((tile, row * self.side + column))
        return pairs

    def swap_route(self, mask):
        return [(tile, tile ^ mask) for tile in range(self.tiles)]

    def halos(self, y_edges, x_edges, corners):
        if self.folded:
            y = lax.ppermute(y_edges[0], "yx", self.swap_route(2))
            x = lax.ppermute(x_edges[0], "yx", self.swap_route(1))
            corner = lax.ppermute(corners[0], "yx", self.swap_route(3))
            return [y], [x], [corner]
        y = [lax.ppermute(y_edges[k], "yx", self.route((1, -1)[1 - k], 0)) for k in (1, 0)]
        x = [lax.ppermute(x_edges[k], "yx", self.route(0, (1, -1)[1 - k])) for k in (1, 0)]
        corner = [
            lax.ppermute(corners[2 * k + j], "yx", self.route((1, -1)[1 - k], (1, -1)[1 - j]))
            for k in (1, 0)
            for j in (1, 0)
        ]
        return y, x, corner


def swap_depth(outer, inner):
    size = lax.axis_size("gz")
    routes = [[], []]
    for low in range(size - 1):
        routes[low % 2] += [(low, low + 1), (low + 1, low)]
    return lax.ppermute(outer, "gz", routes[1]), lax.ppermute(inner, "gz", routes[0])


class Riders:
    STEPS = (("cand", 1), ("gz", 2), ("gz", 1))

    def __init__(self, rows):
        self.tiles = 27 * rows // 16
        self.fits = (
            lax.axis_size("yx") == 4
            and lax.axis_size("cand") % 2 == 0
            and lax.axis_size("gz") % 4 == 0
            and self.tiles >= 8
        )
        self.size = -(-self.tiles // 8) if self.fits else 0

    @classmethod
    def mine(cls):
        return sum(
            lax.axis_index(axis) // mask % 2 * 2**k for k, (axis, mask) in enumerate(cls.STEPS)
        )


def rotate_shards(piece):
    tiles = lax.axis_size("yx")
    return [
        lax.ppermute(piece, "yx", [(i, (i + k) % tiles) for i in range(tiles)]) for k in range(1, tiles)
    ]


def swap(block, axis, mask):
    return lax.ppermute(block, axis, [(i, i ^ mask) for i in range(lax.axis_size(axis))])


def share(stats):
    return lax.all_to_all(stats, PART, 0, 0)


def call(kernel, outs, scratch, *arrays, flops=0, nbytes=0, in_hbm=0, out_hbm=False):
    vmem, hbm = (pl.BlockSpec(memory_space=space) for space in (pltpu.VMEM, pltpu.HBM))
    far, near = arrays[:in_hbm], arrays[in_hbm:]
    far = [pltpu.with_memory_space_constraint(array, pltpu.HBM) for array in far]
    return pl.pallas_call(
        kernel,
        out_shape=[jax.ShapeDtypeStruct(shape, dtype) for shape, dtype in outs],
        in_specs=[hbm] * len(far) + [vmem] * len(near),
        out_specs=[hbm if out_hbm else vmem] * len(outs),
        scratch_shapes=[pltpu.VMEM(*entry) if isinstance(entry, tuple) else entry for entry in scratch],
        compiler_params=pltpu.CompilerParams(vmem_limit_bytes=VMEM_BYTES),
        cost_estimate=pl.CostEstimate(flops=flops, bytes_accessed=nbytes, transcendentals=0),
    )(*far, *near)


def start_kernel(ny, nx, size, x_in, w_in, d_in, y_out, x_out, corners, x, w, lines, sems):
    edge = x_in.shape[0]
    f32, bf16 = jnp.float32, jnp.bfloat16
    above, left = Square().low_sides()
    chunks = 4
    planes = edge // chunks
    first = [
        pltpu.make_async_copy(
            x_in.at[pl.ds(k * planes, planes)],
            x.at[pl.ds(1 + k * planes, planes), pl.ds(1, edge)],
            sems.at[k],
        )
        for k in range(chunks)
    ]
    later = []
    if size:
        at = jnp.minimum(Riders.mine() * size, d_in.shape[0] - size)
        for k, (out, begin) in enumerate(((y_out, edge), (x_out, edge), (corners, 1))):
            later.append(
                pltpu.make_async_copy(
                    d_in.at[pl.ds(at, size)], out.at[0, pl.ds(begin, size)], sems.at[chunks + k]
                )
            )
    later.append(pltpu.make_async_copy(w_in, w, sems.at[chunks + 3]))
    for copy in first + later:
        copy.start()
    x[0] = jnp.zeros(x.shape[1:], bf16)
    x[edge + 1] = jnp.zeros(x.shape[1:], bf16)
    blank = jnp.zeros((edge,) + x.shape[2:], bf16)
    x[1 : edge + 1, 0] = blank
    x[1 : edge + 1, edge + 1] = blank
    flat = lines.reshape(nx * edge * edge * 8, 128)
    part = planes * edge
    for k in range(chunks):
        first[k].wait()
        at, here = pl.ds(k * planes, planes), pl.ds(1 + k * planes, planes)
        for i in range(ny):
            row = jnp.where(above[i], 1, edge)
            y_out[i, at] = x[here, row]
        for j in range(nx):
            low = x[here, 1 : edge + 1, 0:8].astype(f32).reshape(part, 8, 128)
            high = x[here, 1 : edge + 1, edge - 8 : edge].astype(f32).reshape(part, 8, 128)
            high = pltpu.roll(high, 1, 1)
            kept = jnp.where(left[j], low, high)
            lines[j, k * part : k * part + part] = kept
            begin = (j * edge * edge + k * part) * 8
            column = flat[pl.ds(begin, part, stride=8), :]
            x_out[j, at] = column.astype(bf16).reshape(planes, edge, 128)
    for i in range(ny):
        for j in range(nx):
            begin = j * edge * edge * 8
            low = flat[pl.ds(begin, edge, stride=8 * edge), :]
            high = flat[pl.ds(begin + 8 * (edge - 1), edge, stride=8 * edge), :]
            kept = jnp.where(above[i], low, high)
            corners[i * nx + j, 0] = kept.astype(bf16)
    for copy in later:
        copy.wait()


def face_kernel(ny, nx, size, x, y_halos, x_halos, corners, outer, inner, *riders):
    edge = outer.shape[1]
    wide = edge + ny + nx
    odd = lax.axis_index("gz") % 2
    far = edge - 3
    for face, at in ((outer, odd * far), (inner, (1 - odd) * far)):
        for k in range(3):
            row = k * wide
            face[row : row + edge] = x[1 + at + k, 1 : edge + 1]
            for i in range(ny):
                face[row + edge + i] = y_halos[i, at + k]
            for j in range(nx):
                face[row + edge + ny + j] = x_halos[j, at + k]
        for k in range(ny * nx):
            face[3 * wide + k] = corners[k, 0]
    for k in range(inner.shape[0], outer.shape[0]):
        outer[k] = corners[0, 0]
    if size:
        riders[0][0] = x_halos[0, edge : edge + size]
        riders[0][1] = y_halos[0, edge : edge + size]
        riders[0][2] = corners[0, 1 : 1 + size]
        riders[0][3] = corners[0, 1 : 1 + size]


def spread_taps(weight, taps):
    for tap in range(27):
        row, lane = tap // 3 * 128, tap % 3 * 128
        taps[row : row + 128, lane : lane + 128] = weight[tap]


def pair_taps(weight, pairs):
    for dz in range(3):
        for line in range(4):
            row = (dz * 4 + line) * 128
            for out in range(2):
                lane = out * 128
                if 0 <= line - out < 3:
                    block = weight[dz * 9 + (line - out) * 3 + 2]
                else:
                    block = jnp.zeros((128, 128), pairs.dtype)
                pairs[row : row + 128, lane : lane + 128] = block


def join_x(wide, edge):
    place = lax.broadcasted_iota(jnp.int32, wide.shape[:2] + (128,), 1)
    after = jnp.where(place > 0, pltpu.roll(wide[:, :, :128], 1, 1), 0.0)
    before = jnp.where(place < edge - 1, pltpu.roll(wide[:, :, 256:], edge - 1, 1), 0.0)
    return wide[:, :, 128:256] + after + before


def convolve(grid, count, taps, pairs, put):
    edge = grid.shape[2]
    planes = min(count, 4)
    rows = planes * edge * edge
    place = lax.broadcasted_iota(jnp.int32, (planes * edge, edge, 128), 1)
    halved = grid.reshape(grid.shape[0], edge // 2 + 1, 2, edge, 128)
    for z in range(0, count, planes):
        left = jnp.concatenate(
            [
                grid[z + dz : z + dz + planes, dy : dy + edge].reshape(rows, 128)
                for dz in range(3)
                for dy in range(3)
            ],
            axis=1,
        )
        wide = jnp.dot(left, taps[:, 0:256], preferred_element_type=jnp.float32)
        wide = wide.reshape(planes * edge, edge, 256)
        left = jnp.concatenate(
            [
                halved[z + dz : z + dz + planes, line // 2 : line // 2 + edge // 2, line % 2].reshape(
                    rows // 2, 128
                )
                for dz in range(3)
                for line in range(4)
            ],
            axis=1,
        )
        two = jnp.dot(left, pairs[...], preferred_element_type=jnp.float32)
        two = two.reshape(planes * edge // 2, edge, 256)
        two = jnp.stack([two[:, :, :128], two[:, :, 128:]], axis=1).reshape(planes * edge, edge, 128)
        after = jnp.where(place > 0, pltpu.roll(wide[:, :, :128], 1, 1), 0.0)
        before = jnp.where(place < edge - 1, pltpu.roll(two, edge - 1, 1), 0.0)
        new = wide[:, :, 128:256] + after + before
        put(z, new.reshape(planes, edge, edge, 128))


def conv_kernel(deep_in, x, weight, act, taps, pairs, deep_weight, sem):
    copy = pltpu.make_async_copy(deep_in, deep_weight, sem)
    copy.start()
    edge = act.shape[0]
    spread_taps(weight, taps)
    pair_taps(weight, pairs)

    def put(z, new):
        act[z : z + new.shape[0]] = new

    convolve(x, edge, taps, pairs, put)
    copy.wait()


def y_terms(line, low, taps):
    planes, edge = line.shape[0] - 2, line.shape[1]
    left = jnp.concatenate(
        [line[dz : dz + planes].reshape(planes * edge, 128) for dz in range(3)], axis=1
    )
    start = jnp.where(low, 0, 256)
    right = jnp.concatenate(
        [taps[pl.ds(pl.multiple_of(start + dz * 384, 128), 128), :] for dz in range(3)], axis=0
    )
    wide = jnp.dot(left, right, preferred_element_type=jnp.float32)
    return join_x(wide.reshape(planes, edge, 384), edge)


def x_terms(column, taps):
    planes, edge = column.shape[0] - 2, column.shape[1] - 16
    lines = [column[:, 7 + dy : 7 + dy + edge].astype(jnp.bfloat16) for dy in range(3)]
    left = jnp.concatenate(
        [line[dz : dz + planes].reshape(planes * edge, 128) for dz in range(3) for line in lines],
        axis=1,
    )
    right = jnp.concatenate([taps[:, 0:128], taps[:, 256:384]], axis=1)
    both = jnp.dot(left, right, preferred_element_type=jnp.float32)
    return both[:, :128], both[:, 128:]


def fill_column(column, at, voxels, ends, above):
    count, edge = voxels.shape[:2]
    rows = edge + 16
    lines = column.reshape(column.shape[0] * rows, 128)
    column[at : at + count, 8 : 8 + edge] = voxels.astype(jnp.float32)
    for i, end in enumerate(ends):
        first = last = end.astype(jnp.float32)
        if len(ends) == 1:
            first, last = jnp.where(above[0], first, 0.0), jnp.where(above[0], 0.0, last)
        if len(ends) == 1 or i == 0:
            lines[pl.ds(at * rows + 7, count, stride=rows), :] = first
        if len(ends) == 1 or i == 1:
            lines[pl.ds(at * rows + 8 + edge, count, stride=rows), :] = last


def add_column(act, terms, j, nx, low):
    planes, edge = act.shape[:2]
    flat = act.reshape(planes * edge * edge, 128)
    first, last = terms
    if nx == 1:
        first, last = jnp.where(low, first, 0.0), jnp.where(low, 0.0, last)
    if nx == 1 or j == 0:
        flat[pl.ds(0, planes * edge, stride=edge), :] += first
    if nx == 1 or j == 1:
        flat[pl.ds(edge - 1, planes * edge, stride=edge), :] += last


def moments(planes):
    count, edge = planes.shape[:2]
    zero = jnp.zeros((8, 128), jnp.float32)

    def sum_step(k, carry):
        return carry + jnp.sum(planes[k].reshape(edge * 2, 8, 128), axis=0)

    mean = lax.fori_loop(0, count, sum_step, zero, unroll=True) / (count * edge * edge // 8)

    def spread_step(k, carry):
        off = planes[k].reshape(edge * 2, 8, 128) - mean
        return carry + jnp.sum(off * off, axis=0)

    return mean, lax.fori_loop(0, count, spread_step, zero, unroll=True)


def side_kernel(ny, nx, own, y_halos, x_halos, corners, taps, inner, ends, stats, act, column):
    edge = own.shape[0]
    act[0] = jnp.zeros(act.shape[1:], jnp.float32)
    act[edge + 1] = jnp.zeros(act.shape[1:], jnp.float32)
    act[1 : edge + 1] = own[...]
    above, left = Square().low_sides()
    blank = jnp.zeros((2, edge, 128), jnp.bfloat16)
    for i in range(ny):
        line = jnp.concatenate([blank, y_halos[i, 0:edge], blank], axis=0)
        act[:, jnp.where(above[i], 0, edge - 1)] += y_terms(line, above[i], taps)
    for j in range(nx):
        column[...] = jnp.zeros(column.shape, jnp.float32)
        fill_column(
            column, 2, x_halos[j, 0:edge], [corners[i * nx + j, 0] for i in range(ny)], above
        )
        add_column(act, x_terms(column, taps), j, nx, left[j])
    inner[...] = act[2:edge]
    ends[0:2] = act[0:2]
    ends[2:4] = act[edge : edge + 2]
    mean, spread = moments(act.at[2:edge])
    stats[0:8] = mean
    stats[8:16] = spread


def add_face(ny, nx, behind, face, x, taps, pairs, ends, three, grid, column):
    edge = x.shape[2]
    wide_face = edge + ny + nx
    f32 = jnp.float32
    above, left = Square().low_sides()
    end = pl.ds(jnp.where(behind, 3, 0), 3)
    three[...] = ends[end]
    blank = jnp.zeros(grid.shape[:1] + grid.shape[2:], grid.dtype)
    grid[:, 0] = blank
    grid[:, edge + 1] = blank
    first = jnp.where(behind, 1, 0)
    for k in range(3):
        grid[first + k, 1 : edge + 1] = face[k * wide_face : k * wide_face + edge]
    grid[jnp.where(behind, 0, 3), 1 : edge + 1] = x[jnp.where(behind, edge, 1), 1 : edge + 1]

    def put(z, new):
        three[pl.ds(first + z, new.shape[0])] += new

    convolve(grid, 2, taps, pairs, put)
    beside = jnp.where(behind, 1, 2)
    lines = [grid[beside, dy : dy + edge].reshape(edge * edge, 128) for dy in range(3)]
    rows = taps[pl.ds(pl.multiple_of(jnp.where(behind, 768, 0), 128), 384), :]
    wide = jnp.dot(jnp.concatenate(lines, axis=1), rows, preferred_element_type=f32)
    three[jnp.where(behind, 0, 2)] += join_x(wide.reshape(edge, edge, 384), edge)

    def five(voxels):
        gap = jnp.zeros((2,) + voxels.shape[1:], voxels.dtype)
        return jnp.where(
            behind,
            jnp.concatenate([gap, voxels], axis=0),
            jnp.concatenate([voxels, gap], axis=0),
        )

    def rim(row):
        return five(jnp.stack([face[k * wide_face + edge + row] for k in range(3)]).astype(f32))

    for i in range(ny):
        terms = y_terms(rim(i).astype(jnp.bfloat16), above[i], taps)
        three[:, jnp.where(above[i], 0, edge - 1)] += terms
    for j in range(nx):
        column[...] = jnp.zeros(column.shape, f32)
        tails = []
        for i in range(ny):
            tile = face[3 * wide_face + i * nx + j].astype(f32)
            tails.append(five(jnp.where(behind, tile[:3], tile[edge - 3 :])))
        fill_column(column, 0, rim(ny + j), tails, above)
        add_column(three, x_terms(column, taps), j, nx, left[j])
    ends[end] = three[...]


def inner_kernel(ny, nx, x, partial, face, taps, pairs, ends, three, grid, column):
    blank = jnp.zeros(ends.shape[1:], jnp.float32)
    ends[0] = blank
    ends[1:5] = partial[...]
    ends[5] = blank
    behind = lax.axis_index("gz") % 2 == 0
    add_face(ny, nx, behind, face, x, taps, pairs, ends, three, grid, column)


def outer_kernel(ny, nx, x, middle_stats, ends, face, taps, pairs, act, stats, three, grid, column):
    edge = x.shape[2]
    act[...] = ends[...]
    behind = lax.axis_index("gz") % 2 == 1
    add_face(ny, nx, behind, face, x, taps, pairs, act, three, grid, column)
    mean, spread = moments(act.at[2:4])
    few, many = edge * edge // 4, (edge - 2) * edge * edge // 8
    middle_mean, middle_spread = middle_stats[0:8], middle_stats[8:16]
    off = middle_mean - mean
    part = few / (few + many)
    spread = spread + middle_spread + (many * part) * (off * off)
    put_stats(stats, middle_mean - part * off, spread, few + many)


def merge(mean, spread, rows, other_mean, other_spread):
    off = mean - other_mean
    return 0.5 * (mean + other_mean), spread + other_spread + (0.5 * rows) * (off * off)


def put_stats(stats, mean, spread, rows):
    for step in (1, 2, 4):
        others = pltpu.roll(mean, step, 0), pltpu.roll(spread, step, 0)
        mean, spread = merge(mean, spread, float(rows * step), *others)
    both = jnp.concatenate([mean[0:1], spread[0:1]], axis=0)
    stats[...] = jnp.broadcast_to(both[None], stats.shape)


def read_stats(stats, rows):
    devices, _, channels = stats.shape
    shape = (8, channels)
    means = [jnp.broadcast_to(stats[k, 0:1, :], shape) for k in range(devices)]
    spreads = [jnp.broadcast_to(stats[k, 1:2, :], shape) for k in range(devices)]
    mean = functools.reduce(jnp.add, means) / devices
    spread = functools.reduce(jnp.add, spreads)
    spread = spread + rows * functools.reduce(jnp.add, [(m - mean) * (m - mean) for m in means])
    rows = rows * devices
    lane = lax.broadcasted_iota(jnp.int32, shape, 1)
    step = 1
    while step < channels // GROUPS:
        low = jnp.bitwise_and(lane, step) == 0
        others = [
            jnp.where(low, pltpu.roll(row, channels - step, 1), pltpu.roll(row, step, 1))
            for row in (mean, spread)
        ]
        mean, spread = merge(mean, spread, rows, *others)
        rows, step = 2.0 * rows, 2 * step
    return mean, lax.rsqrt(spread / rows + EPSILON)


def silu_of_double(h):
    return h + h * jnp.tanh(h)


def norm_kernel(ny, nx, inner, ends, stats, gain, offset, out, pooled, *refs):
    y_edges, x_edges, corners, half = refs
    depth, edge = inner.shape[0] + 6, inner.shape[1]
    deep, deep_depth = edge // 2, depth // 2
    f32, bf16 = jnp.float32, jnp.bfloat16
    above, left = Square().low_sides()
    depth_at = lax.axis_index("gz")
    mean, scale = read_stats(stats, float(edge**3))
    scale = scale * (0.5 * gain[...])
    shift = 0.5 * offset[...]
    for k in range(deep_depth):
        value = [
            ends[z] if z < 3 else inner[z - 3] if z < depth - 3 else ends[z - depth + 6]
            for z in (2 * k, 2 * k + 1)
        ]
        value = jnp.stack(value).reshape(edge * edge // 4, 8, 128)
        value = silu_of_double((value - mean) * scale + shift)
        value = value.reshape(2, edge, edge, 128).astype(bf16)
        if 0 < k < deep_depth - 1:
            out[2 * k - 2 : 2 * k] = value
        value = value.astype(f32)
        value = (value[0] + value[1]).reshape(deep, 2, edge, 128)
        half[k] = (value[:, 0] + value[:, 1]).reshape(deep * edge, 128)
        lines = half.at[k]
        pair = lines[pl.ds(0, deep * deep, stride=2), :] + lines[pl.ds(1, deep * deep, stride=2), :]
        pair = (pair * 0.125).astype(bf16).astype(f32).reshape(deep, deep, 128)
        if k == 0 or k == deep_depth - 1:
            inside = depth_at > 0 if k == 0 else depth_at < lax.axis_size("gz") - 1
            pair = jnp.where(inside, pair, 0.0)
        pooled[k] = pair
    lines = pooled.reshape(deep_depth * deep * deep, 128)
    rows = deep_depth * deep
    first_x = lines[pl.ds(0, rows, stride=deep), :]
    last_x = lines[pl.ds(deep - 1, rows, stride=deep), :]
    first_y, last_y = (pooled[:, y].reshape(rows, 128) for y in (0, deep - 1))
    ends = []
    for y in (0, deep - 1):
        for x in (0, deep - 1):
            ends.append(lines[pl.ds(y * deep + x, deep_depth, stride=deep * deep), :])
    if ny == 1:
        above, left = above[0], left[0]
        y_edges[0] = jnp.where(above, first_y, last_y).astype(bf16)
        x_edges[0] = jnp.where(left, first_x, last_x).astype(bf16)
        corners[0, 0:deep_depth] = jnp.where(
            above, jnp.where(left, ends[0], ends[1]), jnp.where(left, ends[2], ends[3])
        )
    else:
        y_edges[0], y_edges[1] = first_y.astype(bf16), last_y.astype(bf16)
        x_edges[0], x_edges[1] = first_x.astype(bf16), last_x.astype(bf16)
        for k in range(4):
            corners[k, 0:deep_depth] = ends[k]


def stack_kernel(*refs):
    out = refs[-1]
    for k in range(out.shape[0]):
        out[k] = refs[k][: out.shape[1], : out.shape[2]]


def stack(*arrays, part=None):
    vmem = pl.BlockSpec(memory_space=pltpu.VMEM)
    shape = (part or arrays[0].shape[:2]) + arrays[0].shape[2:]
    return pl.pallas_call(
        stack_kernel,
        out_shape=jax.ShapeDtypeStruct((len(arrays),) + shape, arrays[0].dtype),
        in_specs=[vmem] * len(arrays),
        out_specs=vmem,
        compiler_params=pltpu.CompilerParams(vmem_limit_bytes=VMEM_BYTES),
    )(*arrays)


def place_weights(own, held, out):
    tile = lax.axis_index("yx")
    out[tile] = own[...]
    if len(held) == 1:
        pieces, others, size = held[0].shape[:3]
        for piece in range(pieces):
            at = jnp.minimum(jnp.bitwise_xor(Riders.mine(), piece) * size, own.shape[0] - size)
            for k in range(others):
                out[jnp.bitwise_xor(tile, k + 1), pl.ds(at, size)] = held[0][piece, k]
    else:
        for k, shard in enumerate(held):
            out[lax.rem(tile + len(held) - k, len(held) + 1)] = shard[...]


def tap_rows(weight, taps):
    per = weight.shape[1] // 27
    return jnp.concatenate(
        [weight[:, pl.ds(tap * per, per)].reshape(-1, 128) for tap in taps], axis=1
    )


def dot_rows(left, right):
    return lax.dot_general(
        left, right, (((1,), (1,)), ((), ())), preferred_element_type=jnp.float32
    )


def deep_kernel(pooled, own, *refs):
    *held, act, weight, grid, packed = refs
    depth, deep = pooled.shape[0], pooled.shape[1]
    place_weights(own, held, weight)
    grid[...] = jnp.zeros(grid.shape, jnp.float32)
    grid[:, 1 : deep + 1, 8:16] = pooled[...]
    for dx in range(3):
        plane = grid[:, :, 7 + dx : 15 + dx]
        for y in range(deep + 1):
            both = jnp.concatenate([plane[:, y], plane[:, y + 1]], axis=1)
            packed[:, y // 2, y % 2, :, dx * 128 : dx * 128 + 128] = both.astype(jnp.bfloat16)
    rows = deep**3
    total = None
    for dz in range(3):
        left = jnp.concatenate(
            [
                packed[dz : dz + deep, dy // 2 : dy // 2 + deep // 2, dy % 2].reshape(rows, 384)
                for dy in range(3)
            ],
            axis=1,
        )
        term = dot_rows(left, tap_rows(weight, range(dz * 9, dz * 9 + 9)))
        total = term if total is None else total + term
    for half in range(act.shape[0]):
        act[half] = total[:, half * 128 : half * 128 + 128]


def deep_rim_kernel(ny, nx, own, y_halos, x_halos, corners, weight, act, stats, line):
    depth, deep = line.shape[0], line.shape[1] - 16
    halves = act.shape[0]
    f32 = jnp.float32
    square = deep * deep
    above, left = Square().low_sides()
    act[...] = own[...]
    flat = line.reshape(depth * line.shape[1], 128)

    def shifts():
        return jnp.concatenate(
            [
                line[dz : dz + deep, 7 + d : 7 + d + deep].reshape(square, 128).astype(jnp.bfloat16)
                for dz in range(3)
                for d in range(3)
            ],
            axis=1,
        )

    for i in range(ny):
        line[...] = jnp.zeros(line.shape, f32)
        line[:, 8 : 8 + deep] = y_halos[i].astype(f32).reshape(depth, deep, 128)
        for j in range(nx):
            end = corners[i * nx + j, 0:depth]
            first, last = jnp.where(left[j], end, 0.0), jnp.where(left[j], 0.0, end)
            if nx == 1 or j == 0:
                flat[pl.ds(7, depth, stride=line.shape[1]), :] = first
            if nx == 1 or j == 1:
                flat[pl.ds(8 + deep, depth, stride=line.shape[1]), :] = last
        tap = jnp.where(above[i], 0, 6)
        taps = [tap + dz * 9 + dx for dz in range(3) for dx in range(3)]
        terms = dot_rows(shifts(), tap_rows(weight, taps))
        for half in range(halves):
            rows = act.at[half].reshape(deep, deep, deep, 128)
            term = terms[:, half * 128 : half * 128 + 128].reshape(deep, deep, 128)
            rows[:, jnp.where(above[i], 0, deep - 1)] += term
    for j in range(nx):
        line[...] = jnp.zeros(line.shape, f32)
        line[:, 8 : 8 + deep] = x_halos[j].astype(f32).reshape(depth, deep, 128)
        tap = jnp.where(left[j], 0, 2)
        taps = [tap + dz * 9 + dy * 3 for dz in range(3) for dy in range(3)]
        terms = dot_rows(shifts(), tap_rows(weight, taps))
        first, last = jnp.where(left[j], terms, 0.0), jnp.where(left[j], 0.0, terms)
        for half in range(halves):
            lanes, rows = slice(half * 128, half * 128 + 128), act.at[half]
            if nx == 1 or j == 0:
                rows[pl.ds(0, square, stride=deep), :] += first[:, lanes]
            if nx == 1 or j == 1:
                rows[pl.ds(deep - 1, square, stride=deep), :] += last[:, lanes]

    rows = deep**3 // 8
    means, spreads = [], []
    for half in range(halves):
        total = act[half].reshape(rows, 8, 128)
        means.append(jnp.sum(total, axis=0) / rows)
        off = total - means[-1]
        spreads.append(jnp.sum(off * off, axis=0))
    put_stats(stats, *(jnp.concatenate(part, axis=1) for part in (means, spreads)), rows)


def final_kernel(act, stats, gain, offset, up, mid, out, wide, held, sems):
    edge = mid.shape[0]
    deep = edge // 2
    f32 = jnp.float32
    mean, scale = read_stats(stats, float(deep**3))
    scale = scale * (0.5 * gain[...])
    shift = 0.5 * offset[...]
    planes = 2
    size = planes * deep * deep
    copies = []
    for k in range(0, deep, planes):
        at = slice(k * deep * deep, k * deep * deep + size)
        value = jnp.concatenate([act[half, at] for half in range(act.shape[0])], axis=1)
        value = value.reshape(size // 8, 8, -1)
        value = silu_of_double((value - mean) * scale + shift)
        value = value.reshape(size, -1).astype(jnp.bfloat16)
        lifted = jnp.dot(value, up[...], preferred_element_type=f32)
        lines = wide.at[k // planes]
        lines[pl.ds(0, size, stride=2), :] = lifted
        lines[pl.ds(1, size, stride=2), :] = lifted
        add = lines[...].reshape(planes, 1, deep, 1, edge, 128)
        at = pl.ds(2 * k, 2 * planes)
        old = mid[at].astype(f32).reshape(planes, 2, deep, 2, edge, 128)
        held[at] = (old + add).astype(jnp.bfloat16).reshape(2 * planes, edge, edge, 128)
        copy = pltpu.make_async_copy(held.at[at], out.at[at], sems.at[k // planes])
        copy.start()
        copies.append(copy)
    for copy in copies:
        copy.wait()


def body(
    features, conv_weight, gain_mid, offset_mid, deep_weight, gain_deep, offset_deep, up_weight
):
    f32, bf16 = jnp.float32, jnp.bfloat16
    edge, channels = features.shape[0], features.shape[3]
    deep = edge // 2
    deep_channels = gain_deep.shape[0]
    square = Square()
    tiles = square.tiles
    devices = lax.axis_size("gz") * tiles
    ny, nx = (len(sides) for sides in square.low_sides())
    riders = Riders(deep_weight.shape[4])

    own = jnp.moveaxis(deep_weight, 4, 3).reshape(-1, 16, channels)
    conv_weight = conv_weight.reshape(27, channels, channels)
    *edges, field, conv_weight = call(
        functools.partial(start_kernel, ny, nx, riders.size),
        [
            ((ny, edge + riders.size, edge, channels), bf16),
            ((nx, edge + riders.size, edge, channels), bf16),
            ((ny * nx, 1 + riders.size, edge, channels), bf16),
            ((edge + 2, edge + 2, edge, channels), bf16),
            (conv_weight.shape, bf16),
        ],
        [((nx, edge * edge, 8, channels), f32), pltpu.SemaphoreType.DMA((8,))],
        features,
        conv_weight,
        own,
        nbytes=5 << 20,
        in_hbm=3,
    )
    halos = square.halos(*(list(piece) for piece in edges))
    conv_flops = 54 * channels * channels * edge**3
    act, taps, pairs, own = call(
        conv_kernel,
        [
            ((edge, edge, edge, channels), f32),
            ((9 * channels, 3 * channels), bf16),
            ((12 * channels, 2 * channels), bf16),
            (own.shape, bf16),
        ],
        [pltpu.SemaphoreType.DMA],
        own,
        field,
        conv_weight,
        flops=conv_flops,
        nbytes=6 << 20,
        in_hbm=1,
    )
    (y, x, corner), act = lax.optimization_barrier((halos, act))
    y, x, corner = jnp.stack(y), jnp.stack(x), jnp.stack(corner)
    face = ((3 * (edge + ny + nx) + ny * nx, edge, channels), bf16)
    held = [((4, riders.size, 16, channels), bf16)] if riders.size else []
    outer, inner, *held = call(
        functools.partial(face_kernel, ny, nx, riders.size),
        [((face[0][0] + 2,) + face[0][1:], bf16), face] + held,
        [],
        field,
        y,
        x,
        corner,
    )
    outer, inner = swap_depth(outer, inner)
    if riders.size:
        held = held[0][None]
        other = swap(held, *riders.STEPS[0])
    else:
        held = rotate_shards(own)
    six = ((6, edge, edge, channels), f32)
    column = (edge + 16, channels)
    middle, partial, stats = call(
        functools.partial(side_kernel, ny, nx),
        [
            ((edge - 2, edge, edge, channels), f32),
            ((4, edge, edge, channels), f32),
            ((16, channels), f32),
        ],
        [((edge + 2, edge, edge, channels), f32), ((edge + 4,) + column, f32)],
        act,
        y,
        x,
        corner,
        taps,
    )
    room = [
        ((3, edge, edge, channels), f32),
        ((4, edge + 2, edge, channels), bf16),
        ((5,) + column, f32),
    ]
    (ends,) = call(
        functools.partial(inner_kernel, ny, nx), [six], room, field, partial, inner, taps, pairs
    )
    ends, stats = call(
        functools.partial(outer_kernel, ny, nx),
        [six, ((devices, 2, channels), f32)],
        room,
        field,
        stats,
        ends,
        outer,
        taps,
        pairs,
    )
    if riders.size:
        stats, other = lax.optimization_barrier((stats, other))
        held = stack(held, other, part=(1, 3)).reshape((2, 3) + held.shape[2:])
        other = swap(held, *riders.STEPS[1])
        stats = share(stats)
        stats, other = lax.optimization_barrier((stats, other))
        held = stack(held, other).reshape((-1,) + held.shape[1:])
        other = swap(held, *riders.STEPS[2])
        held = [stack(held, other).reshape((-1,) + held.shape[1:])]
    else:
        stats = share(stats)
    out, pooled, *edges = call(
        functools.partial(norm_kernel, ny, nx),
        [
            ((edge, edge, edge, channels), bf16),
            ((deep + 2, deep, deep, channels), f32),
            ((ny, (deep + 2) * deep, channels), bf16),
            ((nx, (deep + 2) * deep, channels), bf16),
            ((ny * nx, 16, channels), f32),
        ],
        [((deep + 2, deep * edge, channels), f32)],
        middle,
        ends,
        stats,
        gain_mid.reshape(1, channels),
        offset_mid.reshape(1, channels),
        flops=20 * channels * edge**3,
        nbytes=3 << 20,
    )
    y, x, corner = square.halos(*(list(piece) for piece in edges))
    halves = ((deep_channels // 128, deep**3, 128), f32)
    deep_act, weight = call(
        deep_kernel,
        [halves, ((tiles,) + own.shape, bf16)],
        [
            ((deep + 2, deep + 2, 24, channels), f32),
            ((deep + 2, deep // 2 + 1, 2, 16, 3 * channels), bf16),
        ],
        pooled,
        own,
        *held,
        flops=54 * channels * deep_channels * deep**3,
        nbytes=4 << 20,
    )
    deep_act, stats = call(
        functools.partial(deep_rim_kernel, ny, nx),
        [halves, ((devices, 2, deep_channels), f32)],
        [((deep + 2, 24, channels), f32)],
        deep_act,
        jnp.stack(y),
        jnp.stack(x),
        jnp.stack(corner),
        weight,
        flops=4 * channels * deep_channels * deep**3,
        nbytes=3 << 20,
    )
    stats = share(stats)
    (decoded,) = call(
        final_kernel,
        [((edge, edge, edge, channels), bf16)],
        [
            ((deep // 2, 4 * deep * deep, channels), f32),
            ((edge, edge, edge, channels), bf16),
            pltpu.SemaphoreType.DMA((deep // 2,)),
        ],
        deep_act,
        stats,
        gain_deep.reshape(1, deep_channels),
        offset_deep.reshape(1, deep_channels),
        up_weight,
        out,
        flops=4 * deep_channels * channels * deep**3,
        nbytes=3 << 20,
        out_hbm=True,
    )
    return decoded


def solution(mesh):
    placed = (
        P(("cand", "gz"), "yx", None, None),
        P(),
        P(),
        P(),
        P(None, None, None, None, "yx"),
        P(),
        P(),
        P(),
    )
    return jax.shard_map(
        body,
        mesh=mesh,
        in_specs=placed,
        out_specs=P(("cand", "gz"), "yx", None, None),
        check_vma=False,
    )
```

```python
import functools
import math

import jax
import jax.numpy as jnp
from jax import lax
from jax.experimental import pallas as pl
from jax.experimental.pallas import tpu as pltpu
from jax.sharding import PartitionSpec as P

GROUPS = 32
EPSILON = 1e-05
PART = ("gz", "yx")
VMEM_BYTES = 32 * 1024 * 1024


class Square:
    def __init__(self):
        self.tiles = lax.axis_size("yx")
        self.side = math.isqrt(self.tiles)
        tile = lax.axis_index("yx")
        self.row, self.column = tile // self.side, tile % self.side
        self.folded = self.side == 2
        self.steps = (0,) if self.folded else (-1, 1)

    def low_sides(self):
        if self.folded:
            return [self.row == 1], [self.column == 1]
        return [True, False], [True, False]

    def route(self, down, right):
        pairs = []
        for tile in range(self.tiles):
            row, column = tile // self.side + down, tile % self.side + right
            if 0 <= row < self.side and 0 <= column < self.side:
                pairs.append((tile, row * self.side + column))
        return pairs

    def swap_route(self, mask):
        return [(tile, tile ^ mask) for tile in range(self.tiles)]

    def halos(self, y_edges, x_edges, corners):
        if self.folded:
            y = lax.ppermute(y_edges[0], "yx", self.swap_route(2))
            x = lax.ppermute(x_edges[0], "yx", self.swap_route(1))
            corner = lax.ppermute(corners[0], "yx", self.swap_route(3))
            return [y], [x], [corner]
        y = [lax.ppermute(y_edges[k], "yx", self.route((1, -1)[1 - k], 0)) for k in (1, 0)]
        x = [lax.ppermute(x_edges[k], "yx", self.route(0, (1, -1)[1 - k])) for k in (1, 0)]
        corner = [
            lax.ppermute(corners[2 * k + j], "yx", self.route((1, -1)[1 - k], (1, -1)[1 - j]))
            for k in (1, 0)
            for j in (1, 0)
        ]
        return y, x, corner


def swap_depth(outer, inner):
    size = lax.axis_size("gz")
    routes = [[], []]
    for low in range(size - 1):
        routes[low % 2] += [(low, low + 1), (low + 1, low)]
    return lax.ppermute(outer, "gz", routes[1]), lax.ppermute(inner, "gz", routes[0])


class Riders:
    STEPS = (("cand", 1), ("gz", 2), ("gz", 1))

    def __init__(self, rows):
        self.tiles = 27 * rows // 16
        self.fits = (
            lax.axis_size("yx") == 4
            and lax.axis_size("cand") % 2 == 0
            and lax.axis_size("gz") % 4 == 0
            and self.tiles >= 8
        )
        self.size = -(-self.tiles // 8) if self.fits else 0

    @classmethod
    def mine(cls):
        return sum(
            lax.axis_index(axis) // mask % 2 * 2**k for k, (axis, mask) in enumerate(cls.STEPS)
        )


def rotate_shards(piece):
    tiles = lax.axis_size("yx")
    return [
        lax.ppermute(piece, "yx", [(i, (i + k) % tiles) for i in range(tiles)]) for k in range(1, tiles)
    ]


def swap(block, axis, mask):
    return lax.ppermute(block, axis, [(i, i ^ mask) for i in range(lax.axis_size(axis))])


def share(stats):
    return lax.all_to_all(stats, PART, 0, 0)


def call(kernel, outs, scratch, *arrays, flops=0, nbytes=0, in_hbm=0, out_hbm=False):
    vmem, hbm = (pl.BlockSpec(memory_space=space) for space in (pltpu.VMEM, pltpu.HBM))
    far, near = arrays[:in_hbm], arrays[in_hbm:]
    far = [pltpu.with_memory_space_constraint(array, pltpu.HBM) for array in far]
    return pl.pallas_call(
        kernel,
        out_shape=[jax.ShapeDtypeStruct(shape, dtype) for shape, dtype in outs],
        in_specs=[hbm] * len(far) + [vmem] * len(near),
        out_specs=[hbm if out_hbm else vmem] * len(outs),
        scratch_shapes=[pltpu.VMEM(*entry) if isinstance(entry, tuple) else entry for entry in scratch],
        compiler_params=pltpu.CompilerParams(vmem_limit_bytes=VMEM_BYTES),
        cost_estimate=pl.CostEstimate(flops=flops, bytes_accessed=nbytes, transcendentals=0),
    )(*far, *near)


def start_kernel(ny, size, x_in, w_in, d_in, y_out, rider, x, w, sems):
    edge = x_in.shape[0]
    bf16 = jnp.bfloat16
    above, _ = Square().low_sides()
    chunks = 4
    planes = edge // chunks
    first = [
        pltpu.make_async_copy(
            x_in.at[pl.ds(k * planes, planes)],
            x.at[pl.ds(1 + k * planes, planes), pl.ds(1, edge)],
            sems.at[k],
        )
        for k in range(chunks)
    ]
    later = []
    if size:
        at = jnp.minimum(Riders.mine() * size, d_in.shape[0] - size)
        later.append(pltpu.make_async_copy(d_in.at[pl.ds(at, size)], rider, sems.at[chunks]))
    later.append(pltpu.make_async_copy(w_in, w, sems.at[chunks + 1]))
    for copy in first + later:
        copy.start()
    x[0] = jnp.zeros(x.shape[1:], bf16)
    x[edge + 1] = jnp.zeros(x.shape[1:], bf16)
    blank = jnp.zeros((edge,) + x.shape[2:], bf16)
    x[1 : edge + 1, 0] = blank
    x[1 : edge + 1, edge + 1] = blank
    if not size:
        rider[...] = jnp.zeros(rider.shape, bf16)
    for k in range(chunks):
        first[k].wait()
        at, here = pl.ds(k * planes, planes), pl.ds(1 + k * planes, planes)
        for i in range(ny):
            y_out[i, at] = x[here, jnp.where(above[i], 1, edge)]
    for copy in later:
        copy.wait()
    if size:
        y_out[0, edge : edge + size] = rider[...]


def flank_kernel(ny, nx, size, x, rider, after, x_out, corners, lines):
    del after
    edge = x.shape[2]
    f32, bf16 = jnp.float32, jnp.bfloat16
    above, left = Square().low_sides()
    flat = lines.reshape(nx * edge * edge * 8, 128)
    planes = edge // 4
    part = planes * edge
    for k in range(4):
        at, here = pl.ds(k * planes, planes), pl.ds(1 + k * planes, planes)
        for j in range(nx):
            low = x[here, 1 : edge + 1, 0:8].astype(f32).reshape(part, 8, 128)
            high = x[here, 1 : edge + 1, edge - 8 : edge].astype(f32).reshape(part, 8, 128)
            high = pltpu.roll(high, 1, 1)
            lines[j, k * part : k * part + part] = jnp.where(left[j], low, high)
            begin = (j * edge * edge + k * part) * 8
            column = flat[pl.ds(begin, part, stride=8), :]
            x_out[j, at] = column.astype(bf16).reshape(planes, edge, 128)
    for i in range(ny):
        for j in range(nx):
            begin = j * edge * edge * 8
            low = flat[pl.ds(begin, edge, stride=8 * edge), :]
            high = flat[pl.ds(begin + 8 * (edge - 1), edge, stride=8 * edge), :]
            corners[i * nx + j, 0] = jnp.where(above[i], low, high).astype(bf16)
    if size:
        x_out[0, edge : edge + size] = rider[...]
        corners[0, 1 : 1 + size] = rider[...]


def face_kernel(ny, nx, size, x, y_halos, x_halos, corners, outer, inner, *riders):
    edge = outer.shape[1]
    wide = edge + ny + nx
    odd = lax.axis_index("gz") % 2
    far = edge - 3
    for face, at in ((outer, odd * far), (inner, (1 - odd) * far)):
        for k in range(3):
            row = k * wide
            face[row : row + edge] = x[1 + at + k, 1 : edge + 1]
            for i in range(ny):
                face[row + edge + i] = y_halos[i, at + k]
            for j in range(nx):
                face[row + edge + ny + j] = x_halos[j, at + k]
        for k in range(ny * nx):
            face[3 * wide + k] = corners[k, 0]
    for k in range(inner.shape[0], outer.shape[0]):
        outer[k] = corners[0, 0]
    if size:
        riders[0][0] = x_halos[0, edge : edge + size]
        riders[0][1] = y_halos[0, edge : edge + size]
        riders[0][2] = corners[0, 1 : 1 + size]
        riders[0][3] = corners[0, 1 : 1 + size]


def spread_taps(weight, taps):
    for tap in range(27):
        row, lane = tap // 3 * 128, tap % 3 * 128
        taps[row : row + 128, lane : lane + 128] = weight[tap]


def pair_taps(weight, pairs):
    for dz in range(3):
        for line in range(4):
            row = (dz * 4 + line) * 128
            for out in range(2):
                lane = out * 128
                if 0 <= line - out < 3:
                    block = weight[dz * 9 + (line - out) * 3 + 2]
                else:
                    block = jnp.zeros((128, 128), pairs.dtype)
                pairs[row : row + 128, lane : lane + 128] = block


def join_x(wide, edge):
    place = lax.broadcasted_iota(jnp.int32, wide.shape[:2] + (128,), 1)
    after = jnp.where(place > 0, pltpu.roll(wide[:, :, :128], 1, 1), 0.0)
    before = jnp.where(place < edge - 1, pltpu.roll(wide[:, :, 256:], edge - 1, 1), 0.0)
    return wide[:, :, 128:256] + after + before


def convolve(grid, count, taps, pairs, put):
    edge = grid.shape[2]
    planes = min(count, 4)
    rows = planes * edge * edge
    place = lax.broadcasted_iota(jnp.int32, (planes * edge, edge, 128), 1)
    halved = grid.reshape(grid.shape[0], edge // 2 + 1, 2, edge, 128)
    for z in range(0, count, planes):
        left = jnp.concatenate(
            [
                grid[z + dz : z + dz + planes, dy : dy + edge].reshape(rows, 128)
                for dz in range(3)
                for dy in range(3)
            ],
            axis=1,
        )
        wide = jnp.dot(left, taps[:, 0:256], preferred_element_type=jnp.float32)
        wide = wide.reshape(planes * edge, edge, 256)
        left = jnp.concatenate(
            [
                halved[z + dz : z + dz + planes, line // 2 : line // 2 + edge // 2, line % 2].reshape(
                    rows // 2, 128
                )
                for dz in range(3)
                for line in range(4)
            ],
            axis=1,
        )
        two = jnp.dot(left, pairs[...], preferred_element_type=jnp.float32)
        two = two.reshape(planes * edge // 2, edge, 256)
        two = jnp.stack([two[:, :, :128], two[:, :, 128:]], axis=1).reshape(planes * edge, edge, 128)
        after = jnp.where(place > 0, pltpu.roll(wide[:, :, :128], 1, 1), 0.0)
        before = jnp.where(place < edge - 1, pltpu.roll(two, edge - 1, 1), 0.0)
        new = wide[:, :, 128:256] + after + before
        put(z, new.reshape(planes, edge, edge, 128))


def near_kernel(deep_in, x, weight, act, taps, pairs, deep_weight, sem):
    copy = pltpu.make_async_copy(deep_in, deep_weight, sem)
    copy.start()
    spread_taps(weight, taps)
    pair_taps(weight, pairs)

    def put(z, new):
        act[z : z + new.shape[0]] = new

    convolve(x, act.shape[0], taps, pairs, put)
    copy.wait()


def far_kernel(x, taps, pairs, after, act):
    del after
    half = act.shape[0]

    def put(z, new):
        act[z : z + new.shape[0]] = new

    convolve(x.at[half : 2 * half + 2], half, taps, pairs, put)


def y_terms(line, low, taps):
    planes, edge = line.shape[0] - 2, line.shape[1]
    left = jnp.concatenate(
        [line[dz : dz + planes].reshape(planes * edge, 128) for dz in range(3)], axis=1
    )
    start = jnp.where(low, 0, 256)
    right = jnp.concatenate(
        [taps[pl.ds(pl.multiple_of(start + dz * 384, 128), 128), :] for dz in range(3)], axis=0
    )
    wide = jnp.dot(left, right, preferred_element_type=jnp.float32)
    return join_x(wide.reshape(planes, edge, 384), edge)


def x_terms(column, taps):
    planes, edge = column.shape[0] - 2, column.shape[1] - 16
    lines = [column[:, 7 + dy : 7 + dy + edge].astype(jnp.bfloat16) for dy in range(3)]
    left = jnp.concatenate(
        [line[dz : dz + planes].reshape(planes * edge, 128) for dz in range(3) for line in lines],
        axis=1,
    )
    right = jnp.concatenate([taps[:, 0:128], taps[:, 256:384]], axis=1)
    both = jnp.dot(left, right, preferred_element_type=jnp.float32)
    return both[:, :128], both[:, 128:]


def fill_column(column, at, voxels, ends, above):
    count, edge = voxels.shape[:2]
    rows = edge + 16
    lines = column.reshape(column.shape[0] * rows, 128)
    column[at : at + count, 8 : 8 + edge] = voxels.astype(jnp.float32)
    for i, end in enumerate(ends):
        first = last = end.astype(jnp.float32)
        if len(ends) == 1:
            first, last = jnp.where(above[0], first, 0.0), jnp.where(above[0], 0.0, last)
        if len(ends) == 1 or i == 0:
            lines[pl.ds(at * rows + 7, count, stride=rows), :] = first
        if len(ends) == 1 or i == 1:
            lines[pl.ds(at * rows + 8 + edge, count, stride=rows), :] = last


def add_column(act, terms, j, nx, low):
    planes, edge = act.shape[:2]
    flat = act.reshape(planes * edge * edge, 128)
    first, last = terms
    if nx == 1:
        first, last = jnp.where(low, first, 0.0), jnp.where(low, 0.0, last)
    if nx == 1 or j == 0:
        flat[pl.ds(0, planes * edge, stride=edge), :] += first
    if nx == 1 or j == 1:
        flat[pl.ds(edge - 1, planes * edge, stride=edge), :] += last


def moments(planes):
    count, edge = planes.shape[:2]
    zero = jnp.zeros((8, 128), jnp.float32)

    def sum_step(k, carry):
        return carry + jnp.sum(planes[k].reshape(edge * 2, 8, 128), axis=0)

    mean = lax.fori_loop(0, count, sum_step, zero, unroll=True) / (count * edge * edge // 8)

    def spread_step(k, carry):
        off = planes[k].reshape(edge * 2, 8, 128) - mean
        return carry + jnp.sum(off * off, axis=0)

    return mean, lax.fori_loop(0, count, spread_step, zero, unroll=True)


def side_kernel(ny, nx, near, far, y_halos, x_halos, corners, taps, inner, ends, stats, act, column):
    edge = near.shape[1]
    half = edge // 2
    act[0] = jnp.zeros(act.shape[1:], jnp.float32)
    act[edge + 1] = jnp.zeros(act.shape[1:], jnp.float32)
    act[1 : half + 1] = near[...]
    act[half + 1 : edge + 1] = far[...]
    above, left = Square().low_sides()
    blank = jnp.zeros((2, edge, 128), jnp.bfloat16)
    for i in range(ny):
        line = jnp.concatenate([blank, y_halos[i, 0:edge], blank], axis=0)
        act[:, jnp.where(above[i], 0, edge - 1)] += y_terms(line, above[i], taps)
    for j in range(nx):
        column[...] = jnp.zeros(column.shape, jnp.float32)
        fill_column(
            column, 2, x_halos[j, 0:edge], [corners[i * nx + j, 0] for i in range(ny)], above
        )
        add_column(act, x_terms(column, taps), j, nx, left[j])
    inner[...] = act[2:edge]
    ends[0:2] = act[0:2]
    ends[2:4] = act[edge : edge + 2]
    mean, spread = moments(act.at[2:edge])
    stats[0:8] = mean
    stats[8:16] = spread


def add_face(ny, nx, behind, face, x, taps, pairs, ends, three, grid, column):
    edge = x.shape[2]
    wide_face = edge + ny + nx
    f32 = jnp.float32
    above, left = Square().low_sides()
    end = pl.ds(jnp.where(behind, 3, 0), 3)
    three[...] = ends[end]
    blank = jnp.zeros(grid.shape[:1] + grid.shape[2:], grid.dtype)
    grid[:, 0] = blank
    grid[:, edge + 1] = blank
    first = jnp.where(behind, 1, 0)
    for k in range(3):
        grid[first + k, 1 : edge + 1] = face[k * wide_face : k * wide_face + edge]
    grid[jnp.where(behind, 0, 3), 1 : edge + 1] = x[jnp.where(behind, edge, 1), 1 : edge + 1]

    def put(z, new):
        three[pl.ds(first + z, new.shape[0])] += new

    convolve(grid, 2, taps, pairs, put)
    beside = jnp.where(behind, 1, 2)
    lines = [grid[beside, dy : dy + edge].reshape(edge * edge, 128) for dy in range(3)]
    rows = taps[pl.ds(pl.multiple_of(jnp.where(behind, 768, 0), 128), 384), :]
    wide = jnp.dot(jnp.concatenate(lines, axis=1), rows, preferred_element_type=f32)
    three[jnp.where(behind, 0, 2)] += join_x(wide.reshape(edge, edge, 384), edge)

    def five(voxels):
        gap = jnp.zeros((2,) + voxels.shape[1:], voxels.dtype)
        return jnp.where(
            behind,
            jnp.concatenate([gap, voxels], axis=0),
            jnp.concatenate([voxels, gap], axis=0),
        )

    def rim(row):
        return five(jnp.stack([face[k * wide_face + edge + row] for k in range(3)]).astype(f32))

    for i in range(ny):
        terms = y_terms(rim(i).astype(jnp.bfloat16), above[i], taps)
        three[:, jnp.where(above[i], 0, edge - 1)] += terms
    for j in range(nx):
        column[...] = jnp.zeros(column.shape, f32)
        tails = []
        for i in range(ny):
            tile = face[3 * wide_face + i * nx + j].astype(f32)
            tails.append(five(jnp.where(behind, tile[:3], tile[edge - 3 :])))
        fill_column(column, 0, rim(ny + j), tails, above)
        add_column(three, x_terms(column, taps), j, nx, left[j])
    ends[end] = three[...]


def inner_kernel(ny, nx, x, partial, face, taps, pairs, ends, three, grid, column):
    blank = jnp.zeros(ends.shape[1:], jnp.float32)
    ends[0] = blank
    ends[1:5] = partial[...]
    ends[5] = blank
    behind = lax.axis_index("gz") % 2 == 0
    add_face(ny, nx, behind, face, x, taps, pairs, ends, three, grid, column)


def outer_kernel(ny, nx, x, middle_stats, ends, face, taps, pairs, act, stats, three, grid, column):
    edge = x.shape[2]
    act[...] = ends[...]
    behind = lax.axis_index("gz") % 2 == 1
    add_face(ny, nx, behind, face, x, taps, pairs, act, three, grid, column)
    mean, spread = moments(act.at[2:4])
    few, many = edge * edge // 4, (edge - 2) * edge * edge // 8
    middle_mean, middle_spread = middle_stats[0:8], middle_stats[8:16]
    off = middle_mean - mean
    part = few / (few + many)
    spread = spread + middle_spread + (many * part) * (off * off)
    put_stats(stats, middle_mean - part * off, spread, few + many)


def merge(mean, spread, rows, other_mean, other_spread):
    off = mean - other_mean
    return 0.5 * (mean + other_mean), spread + other_spread + (0.5 * rows) * (off * off)


def put_stats(stats, mean, spread, rows):
    for step in (1, 2, 4):
        others = pltpu.roll(mean, step, 0), pltpu.roll(spread, step, 0)
        mean, spread = merge(mean, spread, float(rows * step), *others)
    both = jnp.concatenate([mean[0:1], spread[0:1]], axis=0)
    stats[...] = jnp.broadcast_to(both[None], stats.shape)


def read_stats(stats, rows):
    devices, _, channels = stats.shape
    shape = (8, channels)
    means = [jnp.broadcast_to(stats[k, 0:1, :], shape) for k in range(devices)]
    spreads = [jnp.broadcast_to(stats[k, 1:2, :], shape) for k in range(devices)]
    mean = functools.reduce(jnp.add, means) / devices
    spread = functools.reduce(jnp.add, spreads)
    spread = spread + rows * functools.reduce(jnp.add, [(m - mean) * (m - mean) for m in means])
    rows = rows * devices
    lane = lax.broadcasted_iota(jnp.int32, shape, 1)
    step = 1
    while step < channels // GROUPS:
        low = jnp.bitwise_and(lane, step) == 0
        others = [
            jnp.where(low, pltpu.roll(row, channels - step, 1), pltpu.roll(row, step, 1))
            for row in (mean, spread)
        ]
        mean, spread = merge(mean, spread, rows, *others)
        rows, step = 2.0 * rows, 2 * step
    return mean, lax.rsqrt(spread / rows + EPSILON)


def silu_of_double(h):
    return h + h * jnp.tanh(h)


def norm_kernel(ny, nx, inner, ends, stats, gain, offset, out, pooled, *refs):
    y_edges, x_edges, corners, half = refs
    depth, edge = inner.shape[0] + 6, inner.shape[1]
    deep, deep_depth = edge // 2, depth // 2
    f32, bf16 = jnp.float32, jnp.bfloat16
    above, left = Square().low_sides()
    depth_at = lax.axis_index("gz")
    mean, scale = read_stats(stats, float(edge**3))
    scale = scale * (0.5 * gain[...])
    shift = 0.5 * offset[...]
    for k in range(deep_depth):
        value = [
            ends[z] if z < 3 else inner[z - 3] if z < depth - 3 else ends[z - depth + 6]
            for z in (2 * k, 2 * k + 1)
        ]
        value = jnp.stack(value).reshape(edge * edge // 4, 8, 128)
        value = silu_of_double((value - mean) * scale + shift)
        value = value.reshape(2, edge, edge, 128).astype(bf16)
        if 0 < k < deep_depth - 1:
            out[2 * k - 2 : 2 * k] = value
        value = value.astype(f32)
        value = (value[0] + value[1]).reshape(deep, 2, edge, 128)
        half[k] = (value[:, 0] + value[:, 1]).reshape(deep * edge, 128)
        lines = half.at[k]
        pair = lines[pl.ds(0, deep * deep, stride=2), :] + lines[pl.ds(1, deep * deep, stride=2), :]
        pair = (pair * 0.125).astype(bf16).astype(f32).reshape(deep, deep, 128)
        if k == 0 or k == deep_depth - 1:
            inside = depth_at > 0 if k == 0 else depth_at < lax.axis_size("gz") - 1
            pair = jnp.where(inside, pair, 0.0)
        pooled[k] = pair
    lines = pooled.reshape(deep_depth * deep * deep, 128)
    rows = deep_depth * deep
    first_x = lines[pl.ds(0, rows, stride=deep), :]
    last_x = lines[pl.ds(deep - 1, rows, stride=deep), :]
    first_y, last_y = (pooled[:, y].reshape(rows, 128) for y in (0, deep - 1))
    ends = []
    for y in (0, deep - 1):
        for x in (0, deep - 1):
            ends.append(lines[pl.ds(y * deep + x, deep_depth, stride=deep * deep), :])
    if ny == 1:
        above, left = above[0], left[0]
        y_edges[0] = jnp.where(above, first_y, last_y).astype(bf16)
        x_edges[0] = jnp.where(left, first_x, last_x).astype(bf16)
        corners[0, 0:deep_depth] = jnp.where(
            above, jnp.where(left, ends[0], ends[1]), jnp.where(left, ends[2], ends[3])
        )
    else:
        y_edges[0], y_edges[1] = first_y.astype(bf16), last_y.astype(bf16)
        x_edges[0], x_edges[1] = first_x.astype(bf16), last_x.astype(bf16)
        for k in range(4):
            corners[k, 0:deep_depth] = ends[k]


def stack_kernel(*refs):
    out = refs[-1]
    for k in range(out.shape[0]):
        out[k] = refs[k][: out.shape[1], : out.shape[2]]


def stack(*arrays, part=None):
    vmem = pl.BlockSpec(memory_space=pltpu.VMEM)
    shape = (part or arrays[0].shape[:2]) + arrays[0].shape[2:]
    return pl.pallas_call(
        stack_kernel,
        out_shape=jax.ShapeDtypeStruct((len(arrays),) + shape, arrays[0].dtype),
        in_specs=[vmem] * len(arrays),
        out_specs=vmem,
        compiler_params=pltpu.CompilerParams(vmem_limit_bytes=VMEM_BYTES),
    )(*arrays)


def place_weights(own, held, out):
    tile = lax.axis_index("yx")
    out[tile] = own[...]
    if len(held) == 1:
        pieces, others, size = held[0].shape[:3]
        for piece in range(pieces):
            at = jnp.minimum(jnp.bitwise_xor(Riders.mine(), piece) * size, own.shape[0] - size)
            for k in range(others):
                out[jnp.bitwise_xor(tile, k + 1), pl.ds(at, size)] = held[0][piece, k]
    else:
        for k, shard in enumerate(held):
            out[lax.rem(tile + len(held) - k, len(held) + 1)] = shard[...]


def tap_rows(weight, taps):
    per = weight.shape[1] // 27
    return jnp.concatenate(
        [weight[:, pl.ds(tap * per, per)].reshape(-1, 128) for tap in taps], axis=1
    )


def dot_rows(left, right):
    return lax.dot_general(
        left, right, (((1,), (1,)), ((), ())), preferred_element_type=jnp.float32
    )


def deep_kernel(pooled, own, *refs):
    *held, act, weight, grid, packed = refs
    depth, deep = pooled.shape[0], pooled.shape[1]
    place_weights(own, held, weight)
    grid[...] = jnp.zeros(grid.shape, jnp.float32)
    grid[:, 1 : deep + 1, 8:16] = pooled[...]
    for dx in range(3):
        plane = grid[:, :, 7 + dx : 15 + dx]
        for y in range(deep + 1):
            both = jnp.concatenate([plane[:, y], plane[:, y + 1]], axis=1)
            packed[:, y // 2, y % 2, :, dx * 128 : dx * 128 + 128] = both.astype(jnp.bfloat16)
    rows = deep**3
    total = None
    for dz in range(3):
        left = jnp.concatenate(
            [
                packed[dz : dz + deep, dy // 2 : dy // 2 + deep // 2, dy % 2].reshape(rows, 384)
                for dy in range(3)
            ],
            axis=1,
        )
        term = dot_rows(left, tap_rows(weight, range(dz * 9, dz * 9 + 9)))
        total = term if total is None else total + term
    for half in range(act.shape[0]):
        act[half] = total[:, half * 128 : half * 128 + 128]


def deep_rim_kernel(ny, nx, own, y_halos, x_halos, corners, weight, act, stats, line):
    depth, deep = line.shape[0], line.shape[1] - 16
    halves = act.shape[0]
    f32 = jnp.float32
    square = deep * deep
    above, left = Square().low_sides()
    act[...] = own[...]
    flat = line.reshape(depth * line.shape[1], 128)

    def shifts():
        return jnp.concatenate(
            [
                line[dz : dz + deep, 7 + d : 7 + d + deep].reshape(square, 128).astype(jnp.bfloat16)
                for dz in range(3)
                for d in range(3)
            ],
            axis=1,
        )

    for i in range(ny):
        line[...] = jnp.zeros(line.shape, f32)
        line[:, 8 : 8 + deep] = y_halos[i].astype(f32).reshape(depth, deep, 128)
        for j in range(nx):
            end = corners[i * nx + j, 0:depth]
            first, last = jnp.where(left[j], end, 0.0), jnp.where(left[j], 0.0, end)
            if nx == 1 or j == 0:
                flat[pl.ds(7, depth, stride=line.shape[1]), :] = first
            if nx == 1 or j == 1:
                flat[pl.ds(8 + deep, depth, stride=line.shape[1]), :] = last
        tap = jnp.where(above[i], 0, 6)
        taps = [tap + dz * 9 + dx for dz in range(3) for dx in range(3)]
        terms = dot_rows(shifts(), tap_rows(weight, taps))
        for half in range(halves):
            rows = act.at[half].reshape(deep, deep, deep, 128)
            term = terms[:, half * 128 : half * 128 + 128].reshape(deep, deep, 128)
            rows[:, jnp.where(above[i], 0, deep - 1)] += term
    for j in range(nx):
        line[...] = jnp.zeros(line.shape, f32)
        line[:, 8 : 8 + deep] = x_halos[j].astype(f32).reshape(depth, deep, 128)
        tap = jnp.where(left[j], 0, 2)
        taps = [tap + dz * 9 + dy * 3 for dz in range(3) for dy in range(3)]
        terms = dot_rows(shifts(), tap_rows(weight, taps))
        first, last = jnp.where(left[j], terms, 0.0), jnp.where(left[j], 0.0, terms)
        for half in range(halves):
            lanes, rows = slice(half * 128, half * 128 + 128), act.at[half]
            if nx == 1 or j == 0:
                rows[pl.ds(0, square, stride=deep), :] += first[:, lanes]
            if nx == 1 or j == 1:
                rows[pl.ds(deep - 1, square, stride=deep), :] += last[:, lanes]

    rows = deep**3 // 8
    means, spreads = [], []
    for half in range(halves):
        total = act[half].reshape(rows, 8, 128)
        means.append(jnp.sum(total, axis=0) / rows)
        off = total - means[-1]
        spreads.append(jnp.sum(off * off, axis=0))
    put_stats(stats, *(jnp.concatenate(part, axis=1) for part in (means, spreads)), rows)


def final_kernel(act, stats, gain, offset, up, mid, out, wide, held, sems):
    edge = mid.shape[0]
    deep = edge // 2
    f32 = jnp.float32
    mean, scale = read_stats(stats, float(deep**3))
    scale = scale * (0.5 * gain[...])
    shift = 0.5 * offset[...]
    planes = 2
    size = planes * deep * deep
    copies = []
    for k in range(0, deep, planes):
        at = slice(k * deep * deep, k * deep * deep + size)
        value = jnp.concatenate([act[half, at] for half in range(act.shape[0])], axis=1)
        value = value.reshape(size // 8, 8, -1)
        value = silu_of_double((value - mean) * scale + shift)
        value = value.reshape(size, -1).astype(jnp.bfloat16)
        lifted = jnp.dot(value, up[...], preferred_element_type=f32)
        lines = wide.at[k // planes]
        lines[pl.ds(0, size, stride=2), :] = lifted
        lines[pl.ds(1, size, stride=2), :] = lifted
        add = lines[...].reshape(planes, 1, deep, 1, edge, 128)
        at = pl.ds(2 * k, 2 * planes)
        old = mid[at].astype(f32).reshape(planes, 2, deep, 2, edge, 128)
        held[at] = (old + add).astype(jnp.bfloat16).reshape(2 * planes, edge, edge, 128)
        copy = pltpu.make_async_copy(held.at[at], out.at[at], sems.at[k // planes])
        copy.start()
        copies.append(copy)
    for copy in copies:
        copy.wait()


def body(
    features, conv_weight, gain_mid, offset_mid, deep_weight, gain_deep, offset_deep, up_weight
):
    f32, bf16 = jnp.float32, jnp.bfloat16
    edge, channels = features.shape[0], features.shape[3]
    deep = edge // 2
    deep_channels = gain_deep.shape[0]
    square = Square()
    tiles = square.tiles
    devices = lax.axis_size("gz") * tiles
    ny, nx = (len(sides) for sides in square.low_sides())
    riders = Riders(deep_weight.shape[4])

    own = jnp.moveaxis(deep_weight, 4, 3).reshape(-1, 16, channels)
    conv_weight = conv_weight.reshape(27, channels, channels)
    y, rider, field, conv_weight = call(
        functools.partial(start_kernel, ny, riders.size),
        [
            ((ny, edge + riders.size, edge, channels), bf16),
            ((max(riders.size, 1), 16, channels), bf16),
            ((edge + 2, edge + 2, edge, channels), bf16),
            (conv_weight.shape, bf16),
        ],
        [pltpu.SemaphoreType.DMA((6,))],
        features,
        conv_weight,
        own,
        nbytes=5 << 20,
        in_hbm=3,
    )
    half_act = ((deep, edge, edge, channels), f32)
    conv_flops = 54 * channels * channels * edge**3
    near, taps, pairs, own = call(
        near_kernel,
        [
            half_act,
            ((9 * channels, 3 * channels), bf16),
            ((12 * channels, 2 * channels), bf16),
            (own.shape, bf16),
        ],
        [pltpu.SemaphoreType.DMA],
        own,
        field,
        conv_weight,
        flops=conv_flops // 2,
        nbytes=4 << 20,
        in_hbm=1,
    )
    x, corner = call(
        functools.partial(flank_kernel, ny, nx, riders.size),
        [
            ((nx, edge + riders.size, edge, channels), bf16),
            ((ny * nx, 1 + riders.size, edge, channels), bf16),
        ],
        [((nx, edge * edge, 8, channels), f32)],
        field,
        rider,
        taps,
        nbytes=2 << 20,
    )
    halos = square.halos(list(y), list(x), list(corner))
    (far,) = call(
        far_kernel,
        [half_act],
        [],
        field,
        taps,
        pairs,
        corner,
        flops=conv_flops // 2,
        nbytes=4 << 20,
    )
    (y, x, corner), far = lax.optimization_barrier((halos, far))
    y, x, corner = jnp.stack(y), jnp.stack(x), jnp.stack(corner)
    face = ((3 * (edge + ny + nx) + ny * nx, edge, channels), bf16)
    held = [((4, riders.size, 16, channels), bf16)] if riders.size else []
    outer, inner, *held = call(
        functools.partial(face_kernel, ny, nx, riders.size),
        [((face[0][0] + 2,) + face[0][1:], bf16), face] + held,
        [],
        field,
        y,
        x,
        corner,
    )
    outer, inner = swap_depth(outer, inner)
    if riders.size:
        held = held[0][None]
        other = swap(held, *riders.STEPS[0])
    else:
        held = rotate_shards(own)
    six = ((6, edge, edge, channels), f32)
    column = (edge + 16, channels)
    middle, partial, stats = call(
        functools.partial(side_kernel, ny, nx),
        [
            ((edge - 2, edge, edge, channels), f32),
            ((4, edge, edge, channels), f32),
            ((16, channels), f32),
        ],
        [((edge + 2, edge, edge, channels), f32), ((edge + 4,) + column, f32)],
        near,
        far,
        y,
        x,
        corner,
        taps,
    )
    room = [
        ((3, edge, edge, channels), f32),
        ((4, edge + 2, edge, channels), bf16),
        ((5,) + column, f32),
    ]
    (ends,) = call(
        functools.partial(inner_kernel, ny, nx), [six], room, field, partial, inner, taps, pairs
    )
    ends, stats = call(
        functools.partial(outer_kernel, ny, nx),
        [six, ((devices, 2, channels), f32)],
        room,
        field,
        stats,
        ends,
        outer,
        taps,
        pairs,
    )
    if riders.size:
        stats, other = lax.optimization_barrier((stats, other))
        held = stack(held, other, part=(1, 3)).reshape((2, 3) + held.shape[2:])
        other = swap(held, *riders.STEPS[1])
        stats = share(stats)
        stats, other = lax.optimization_barrier((stats, other))
        held = stack(held, other).reshape((-1,) + held.shape[1:])
        other = swap(held, *riders.STEPS[2])
        held = [stack(held, other).reshape((-1,) + held.shape[1:])]
    else:
        stats = share(stats)
    out, pooled, *edges = call(
        functools.partial(norm_kernel, ny, nx),
        [
            ((edge, edge, edge, channels), bf16),
            ((deep + 2, deep, deep, channels), f32),
            ((ny, (deep + 2) * deep, channels), bf16),
            ((nx, (deep + 2) * deep, channels), bf16),
            ((ny * nx, 16, channels), f32),
        ],
        [((deep + 2, deep * edge, channels), f32)],
        middle,
        ends,
        stats,
        gain_mid.reshape(1, channels),
        offset_mid.reshape(1, channels),
        flops=20 * channels * edge**3,
        nbytes=3 << 20,
    )
    y, x, corner = square.halos(*(list(piece) for piece in edges))
    halves = ((deep_channels // 128, deep**3, 128), f32)
    deep_act, weight = call(
        deep_kernel,
        [halves, ((tiles,) + own.shape, bf16)],
        [
            ((deep + 2, deep + 2, 24, channels), f32),
            ((deep + 2, deep // 2 + 1, 2, 16, 3 * channels), bf16),
        ],
        pooled,
        own,
        *held,
        flops=54 * channels * deep_channels * deep**3,
        nbytes=4 << 20,
    )
    deep_act, stats = call(
        functools.partial(deep_rim_kernel, ny, nx),
        [halves, ((devices, 2, deep_channels), f32)],
        [((deep + 2, 24, channels), f32)],
        deep_act,
        jnp.stack(y),
        jnp.stack(x),
        jnp.stack(corner),
        weight,
        flops=4 * channels * deep_channels * deep**3,
        nbytes=3 << 20,
    )
    stats = share(stats)
    (decoded,) = call(
        final_kernel,
        [((edge, edge, edge, channels), bf16)],
        [
            ((deep // 2, 4 * deep * deep, channels), f32),
            ((edge, edge, edge, channels), bf16),
            pltpu.SemaphoreType.DMA((deep // 2,)),
        ],
        deep_act,
        stats,
        gain_deep.reshape(1, deep_channels),
        offset_deep.reshape(1, deep_channels),
        up_weight,
        out,
        flops=4 * deep_channels * channels * deep**3,
        nbytes=3 << 20,
        out_hbm=True,
    )
    return decoded


def solution(mesh):
    placed = (
        P(("cand", "gz"), "yx", None, None),
        P(),
        P(),
        P(),
        P(None, None, None, None, "yx"),
        P(),
        P(),
        P(),
    )
    return jax.shard_map(
        body,
        mesh=mesh,
        in_specs=placed,
        out_specs=P(("cand", "gz"), "yx", None, None),
        check_vma=False,
    )
```

```python
import functools
import math

import jax
import jax.numpy as jnp
from jax import lax
from jax.experimental import pallas as pl
from jax.experimental.pallas import tpu as pltpu
from jax.sharding import PartitionSpec as P

GROUPS = 32
EPSILON = 1e-05
PART = ("gz", "yx")
VMEM_BYTES = 32 * 1024 * 1024


class Square:
    def __init__(self):
        self.tiles = lax.axis_size("yx")
        self.side = math.isqrt(self.tiles)
        tile = lax.axis_index("yx")
        self.row, self.column = tile // self.side, tile % self.side
        self.folded = self.side == 2
        self.steps = (0,) if self.folded else (-1, 1)

    def low_sides(self):
        if self.folded:
            return [self.row == 1], [self.column == 1]
        return [True, False], [True, False]

    def route(self, down, right):
        pairs = []
        for tile in range(self.tiles):
            row, column = tile // self.side + down, tile % self.side + right
            if 0 <= row < self.side and 0 <= column < self.side:
                pairs.append((tile, row * self.side + column))
        return pairs

    def swap_route(self, mask):
        return [(tile, tile ^ mask) for tile in range(self.tiles)]

    def halos(self, y_edges, x_edges, corners):
        if self.folded:
            y = lax.ppermute(y_edges[0], "yx", self.swap_route(2))
            x = lax.ppermute(x_edges[0], "yx", self.swap_route(1))
            corner = lax.ppermute(corners[0], "yx", self.swap_route(3))
            return [y], [x], [corner]
        y = [lax.ppermute(y_edges[k], "yx", self.route((1, -1)[1 - k], 0)) for k in (1, 0)]
        x = [lax.ppermute(x_edges[k], "yx", self.route(0, (1, -1)[1 - k])) for k in (1, 0)]
        corner = [
            lax.ppermute(corners[2 * k + j], "yx", self.route((1, -1)[1 - k], (1, -1)[1 - j]))
            for k in (1, 0)
            for j in (1, 0)
        ]
        return y, x, corner


def swap_depth(outer, inner):
    size = lax.axis_size("gz")
    routes = [[], []]
    for low in range(size - 1):
        routes[low % 2] += [(low, low + 1), (low + 1, low)]
    return lax.ppermute(outer, "gz", routes[1]), lax.ppermute(inner, "gz", routes[0])


class Riders:
    STEPS = (("cand", 1), ("gz", 2), ("gz", 1))

    def __init__(self, rows):
        self.tiles = 27 * rows // 16
        self.fits = (
            lax.axis_size("yx") == 4
            and lax.axis_size("cand") % 2 == 0
            and lax.axis_size("gz") % 4 == 0
            and self.tiles >= 8
        )
        self.size = -(-self.tiles // 8) if self.fits else 0

    @classmethod
    def mine(cls):
        return sum(
            lax.axis_index(axis) // mask % 2 * 2**k for k, (axis, mask) in enumerate(cls.STEPS)
        )


def rotate_shards(piece):
    tiles = lax.axis_size("yx")
    return [
        lax.ppermute(piece, "yx", [(i, (i + k) % tiles) for i in range(tiles)]) for k in range(1, tiles)
    ]


def swap(block, axis, mask):
    return lax.ppermute(block, axis, [(i, i ^ mask) for i in range(lax.axis_size(axis))])


def share(stats):
    return lax.all_to_all(stats, PART, 0, 0)


def call(kernel, outs, scratch, *arrays, flops=0, nbytes=0, in_hbm=0, out_hbm=False):
    vmem, hbm = (pl.BlockSpec(memory_space=space) for space in (pltpu.VMEM, pltpu.HBM))
    far, near = arrays[:in_hbm], arrays[in_hbm:]
    far = [pltpu.with_memory_space_constraint(array, pltpu.HBM) for array in far]
    return pl.pallas_call(
        kernel,
        out_shape=[jax.ShapeDtypeStruct(shape, dtype) for shape, dtype in outs],
        in_specs=[hbm] * len(far) + [vmem] * len(near),
        out_specs=[hbm if out_hbm else vmem] * len(outs),
        scratch_shapes=[pltpu.VMEM(*entry) if isinstance(entry, tuple) else entry for entry in scratch],
        compiler_params=pltpu.CompilerParams(vmem_limit_bytes=VMEM_BYTES),
        cost_estimate=pl.CostEstimate(flops=flops, bytes_accessed=nbytes, transcendentals=0),
    )(*far, *near)


def start_kernel(ny, nx, size, x_in, w_in, d_in, y_out, x_out, corners, x, w, lines, sems):
    edge = x_in.shape[0]
    f32, bf16 = jnp.float32, jnp.bfloat16
    above, left = Square().low_sides()
    chunks = 4
    planes = edge // chunks
    first = [
        pltpu.make_async_copy(
            x_in.at[pl.ds(k * planes, planes)],
            x.at[pl.ds(1 + k * planes, planes), pl.ds(1, edge)],
            sems.at[k],
        )
        for k in range(chunks)
    ]
    later = []
    if size:
        at = jnp.minimum(Riders.mine() * size, d_in.shape[0] - size)
        for k, (out, begin) in enumerate(((y_out, edge), (x_out, edge), (corners, 1))):
            later.append(
                pltpu.make_async_copy(
                    d_in.at[pl.ds(at, size)], out.at[0, pl.ds(begin, size)], sems.at[chunks + k]
                )
            )
    later.append(pltpu.make_async_copy(w_in, w, sems.at[chunks + 3]))
    for copy in first + later:
        copy.start()
    x[0] = jnp.zeros(x.shape[1:], bf16)
    x[edge + 1] = jnp.zeros(x.shape[1:], bf16)
    blank = jnp.zeros((edge,) + x.shape[2:], bf16)
    x[1 : edge + 1, 0] = blank
    x[1 : edge + 1, edge + 1] = blank
    flat = lines.reshape(nx * edge * edge * 8, 128)
    part = planes * edge
    for k in range(chunks):
        first[k].wait()
        at, here = pl.ds(k * planes, planes), pl.ds(1 + k * planes, planes)
        for i in range(ny):
            row = jnp.where(above[i], 1, edge)
            y_out[i, at] = x[here, row]
        for j in range(nx):
            low = x[here, 1 : edge + 1, 0:8].astype(f32).reshape(part, 8, 128)
            high = x[here, 1 : edge + 1, edge - 8 : edge].astype(f32).reshape(part, 8, 128)
            high = pltpu.roll(high, 1, 1)
            kept = jnp.where(left[j], low, high)
            lines[j, k * part : k * part + part] = kept
            begin = (j * edge * edge + k * part) * 8
            column = flat[pl.ds(begin, part, stride=8), :]
            x_out[j, at] = column.astype(bf16).reshape(planes, edge, 128)
    for i in range(ny):
        for j in range(nx):
            begin = j * edge * edge * 8
            low = flat[pl.ds(begin, edge, stride=8 * edge), :]
            high = flat[pl.ds(begin + 8 * (edge - 1), edge, stride=8 * edge), :]
            kept = jnp.where(above[i], low, high)
            corners[i * nx + j, 0] = kept.astype(bf16)
    for copy in later:
        copy.wait()


def face_kernel(ny, nx, size, x, y_halos, x_halos, corners, outer, inner, *riders):
    edge = outer.shape[1]
    wide = edge + ny + nx
    odd = lax.axis_index("gz") % 2
    far = edge - 3
    for face, at in ((outer, odd * far), (inner, (1 - odd) * far)):
        for k in range(3):
            row = k * wide
            face[row : row + edge] = x[1 + at + k, 1 : edge + 1]
            for i in range(ny):
                face[row + edge + i] = y_halos[i, at + k]
            for j in range(nx):
                face[row + edge + ny + j] = x_halos[j, at + k]
        for k in range(ny * nx):
            face[3 * wide + k] = corners[k, 0]
    for k in range(inner.shape[0], outer.shape[0]):
        outer[k] = corners[0, 0]
    if size:
        riders[0][0] = x_halos[0, edge : edge + size]
        riders[0][1] = y_halos[0, edge : edge + size]
        riders[0][2] = corners[0, 1 : 1 + size]
        riders[0][3] = corners[0, 1 : 1 + size]


def spread_taps(weight, taps):
    for tap in range(27):
        row, lane = tap // 3 * 128, tap % 3 * 128
        taps[row : row + 128, lane : lane + 128] = weight[tap]


def pair_taps(weight, pairs):
    for dz in range(3):
        for line in range(4):
            row = (dz * 4 + line) * 128
            for out in range(2):
                lane = out * 128
                if 0 <= line - out < 3:
                    block = weight[dz * 9 + (line - out) * 3 + 2]
                else:
                    block = jnp.zeros((128, 128), pairs.dtype)
                pairs[row : row + 128, lane : lane + 128] = block


def join_x(wide, edge):
    place = lax.broadcasted_iota(jnp.int32, wide.shape[:2] + (128,), 1)
    after = jnp.where(place > 0, pltpu.roll(wide[:, :, :128], 1, 1), 0.0)
    before = jnp.where(place < edge - 1, pltpu.roll(wide[:, :, 256:], edge - 1, 1), 0.0)
    return wide[:, :, 128:256] + after + before


def convolve(grid, count, taps, pairs, put):
    edge = grid.shape[2]
    planes = min(count, 4)
    rows = planes * edge * edge
    place = lax.broadcasted_iota(jnp.int32, (planes * edge, edge, 128), 1)
    halved = grid.reshape(grid.shape[0], edge // 2 + 1, 2, edge, 128)
    for z in range(0, count, planes):
        left = jnp.concatenate(
            [
                grid[z + dz : z + dz + planes, dy : dy + edge].reshape(rows, 128)
                for dz in range(3)
                for dy in range(3)
            ],
            axis=1,
        )
        wide = jnp.dot(left, taps[:, 0:256], preferred_element_type=jnp.float32)
        wide = wide.reshape(planes * edge, edge, 256)
        left = jnp.concatenate(
            [
                halved[z + dz : z + dz + planes, line // 2 : line // 2 + edge // 2, line % 2].reshape(
                    rows // 2, 128
                )
                for dz in range(3)
                for line in range(4)
            ],
            axis=1,
        )
        two = jnp.dot(left, pairs[...], preferred_element_type=jnp.float32)
        two = two.reshape(planes * edge // 2, edge, 256)
        two = jnp.stack([two[:, :, :128], two[:, :, 128:]], axis=1).reshape(planes * edge, edge, 128)
        after = jnp.where(place > 0, pltpu.roll(wide[:, :, :128], 1, 1), 0.0)
        before = jnp.where(place < edge - 1, pltpu.roll(two, edge - 1, 1), 0.0)
        new = wide[:, :, 128:256] + after + before
        put(z, new.reshape(planes, edge, edge, 128))


def conv_kernel(deep_in, x, weight, act, taps, pairs, deep_weight, sem):
    copy = pltpu.make_async_copy(deep_in, deep_weight, sem)
    copy.start()
    edge = act.shape[0]
    spread_taps(weight, taps)
    pair_taps(weight, pairs)

    def put(z, new):
        act[z : z + new.shape[0]] = new

    convolve(x, edge, taps, pairs, put)
    copy.wait()


def y_terms(line, low, taps):
    planes, edge = line.shape[0] - 2, line.shape[1]
    left = jnp.concatenate(
        [line[dz : dz + planes].reshape(planes * edge, 128) for dz in range(3)], axis=1
    )
    start = jnp.where(low, 0, 256)
    right = jnp.concatenate(
        [taps[pl.ds(pl.multiple_of(start + dz * 384, 128), 128), :] for dz in range(3)], axis=0
    )
    wide = jnp.dot(left, right, preferred_element_type=jnp.float32)
    return join_x(wide.reshape(planes, edge, 384), edge)


def x_terms(column, taps):
    planes, edge = column.shape[0] - 2, column.shape[1] - 16
    lines = [column[:, 7 + dy : 7 + dy + edge].astype(jnp.bfloat16) for dy in range(3)]
    left = jnp.concatenate(
        [line[dz : dz + planes].reshape(planes * edge, 128) for dz in range(3) for line in lines],
        axis=1,
    )
    right = jnp.concatenate([taps[:, 0:128], taps[:, 256:384]], axis=1)
    both = jnp.dot(left, right, preferred_element_type=jnp.float32)
    return both[:, :128], both[:, 128:]


def fill_column(column, at, voxels, ends, above):
    count, edge = voxels.shape[:2]
    rows = edge + 16
    lines = column.reshape(column.shape[0] * rows, 128)
    column[at : at + count, 8 : 8 + edge] = voxels.astype(jnp.float32)
    for i, end in enumerate(ends):
        first = last = end.astype(jnp.float32)
        if len(ends) == 1:
            first, last = jnp.where(above[0], first, 0.0), jnp.where(above[0], 0.0, last)
        if len(ends) == 1 or i == 0:
            lines[pl.ds(at * rows + 7, count, stride=rows), :] = first
        if len(ends) == 1 or i == 1:
            lines[pl.ds(at * rows + 8 + edge, count, stride=rows), :] = last


def add_column(act, terms, j, nx, low):
    planes, edge = act.shape[:2]
    flat = act.reshape(planes * edge * edge, 128)
    first, last = terms
    if nx == 1:
        first, last = jnp.where(low, first, 0.0), jnp.where(low, 0.0, last)
    if nx == 1 or j == 0:
        flat[pl.ds(0, planes * edge, stride=edge), :] += first
    if nx == 1 or j == 1:
        flat[pl.ds(edge - 1, planes * edge, stride=edge), :] += last


def moments(planes):
    count, edge = planes.shape[:2]
    zero = jnp.zeros((8, 128), jnp.float32)

    def sum_step(k, carry):
        return carry + jnp.sum(planes[k].reshape(edge * 2, 8, 128), axis=0)

    mean = lax.fori_loop(0, count, sum_step, zero, unroll=True) / (count * edge * edge // 8)

    def spread_step(k, carry):
        off = planes[k].reshape(edge * 2, 8, 128) - mean
        return carry + jnp.sum(off * off, axis=0)

    return mean, lax.fori_loop(0, count, spread_step, zero, unroll=True)


def side_kernel(ny, nx, own, y_halos, x_halos, corners, taps, inner, ends, stats, act, column):
    edge = own.shape[0]
    act[0] = jnp.zeros(act.shape[1:], jnp.float32)
    act[edge + 1] = jnp.zeros(act.shape[1:], jnp.float32)
    act[1 : edge + 1] = own[...]
    above, left = Square().low_sides()
    blank = jnp.zeros((2, edge, 128), jnp.bfloat16)
    for i in range(ny):
        line = jnp.concatenate([blank, y_halos[i, 0:edge], blank], axis=0)
        act[:, jnp.where(above[i], 0, edge - 1)] += y_terms(line, above[i], taps)
    for j in range(nx):
        column[...] = jnp.zeros(column.shape, jnp.float32)
        fill_column(
            column, 2, x_halos[j, 0:edge], [corners[i * nx + j, 0] for i in range(ny)], above
        )
        add_column(act, x_terms(column, taps), j, nx, left[j])
    inner[...] = act[2:edge]
    ends[0:2] = act[0:2]
    ends[2:4] = act[edge : edge + 2]
    mean, spread = moments(act.at[2:edge])
    stats[0:8] = mean
    stats[8:16] = spread


def add_face(ny, nx, behind, face, x, taps, pairs, ends, three, grid, column):
    edge = x.shape[2]
    wide_face = edge + ny + nx
    f32 = jnp.float32
    above, left = Square().low_sides()
    end = pl.ds(jnp.where(behind, 3, 0), 3)
    three[...] = ends[end]
    blank = jnp.zeros(grid.shape[:1] + grid.shape[2:], grid.dtype)
    grid[:, 0] = blank
    grid[:, edge + 1] = blank
    first = jnp.where(behind, 1, 0)
    for k in range(3):
        grid[first + k, 1 : edge + 1] = face[k * wide_face : k * wide_face + edge]
    grid[jnp.where(behind, 0, 3), 1 : edge + 1] = x[jnp.where(behind, edge, 1), 1 : edge + 1]

    def put(z, new):
        three[pl.ds(first + z, new.shape[0])] += new

    convolve(grid, 2, taps, pairs, put)
    beside = jnp.where(behind, 1, 2)
    lines = [grid[beside, dy : dy + edge].reshape(edge * edge, 128) for dy in range(3)]
    rows = taps[pl.ds(pl.multiple_of(jnp.where(behind, 768, 0), 128), 384), :]
    wide = jnp.dot(jnp.concatenate(lines, axis=1), rows, preferred_element_type=f32)
    three[jnp.where(behind, 0, 2)] += join_x(wide.reshape(edge, edge, 384), edge)

    def five(voxels):
        gap = jnp.zeros((2,) + voxels.shape[1:], voxels.dtype)
        return jnp.where(
            behind,
            jnp.concatenate([gap, voxels], axis=0),
            jnp.concatenate([voxels, gap], axis=0),
        )

    def rim(row):
        return five(jnp.stack([face[k * wide_face + edge + row] for k in range(3)]).astype(f32))

    for i in range(ny):
        terms = y_terms(rim(i).astype(jnp.bfloat16), above[i], taps)
        three[:, jnp.where(above[i], 0, edge - 1)] += terms
    for j in range(nx):
        column[...] = jnp.zeros(column.shape, f32)
        tails = []
        for i in range(ny):
            tile = face[3 * wide_face + i * nx + j].astype(f32)
            tails.append(five(jnp.where(behind, tile[:3], tile[edge - 3 :])))
        fill_column(column, 0, rim(ny + j), tails, above)
        add_column(three, x_terms(column, taps), j, nx, left[j])
    ends[end] = three[...]


def inner_kernel(ny, nx, x, partial, face, taps, pairs, ends, three, grid, column):
    blank = jnp.zeros(ends.shape[1:], jnp.float32)
    ends[0] = blank
    ends[1:5] = partial[...]
    ends[5] = blank
    behind = lax.axis_index("gz") % 2 == 0
    add_face(ny, nx, behind, face, x, taps, pairs, ends, three, grid, column)


def outer_kernel(ny, nx, x, middle_stats, ends, face, taps, pairs, act, stats, three, grid, column):
    edge = x.shape[2]
    act[...] = ends[...]
    behind = lax.axis_index("gz") % 2 == 1
    add_face(ny, nx, behind, face, x, taps, pairs, act, three, grid, column)
    mean, spread = moments(act.at[2:4])
    few, many = edge * edge // 4, (edge - 2) * edge * edge // 8
    middle_mean, middle_spread = middle_stats[0:8], middle_stats[8:16]
    off = middle_mean - mean
    part = few / (few + many)
    spread = spread + middle_spread + (many * part) * (off * off)
    put_stats(stats, middle_mean - part * off, spread, few + many)


def merge(mean, spread, rows, other_mean, other_spread):
    off = mean - other_mean
    return 0.5 * (mean + other_mean), spread + other_spread + (0.5 * rows) * (off * off)


def put_stats(stats, mean, spread, rows):
    for step in (1, 2, 4):
        others = pltpu.roll(mean, step, 0), pltpu.roll(spread, step, 0)
        mean, spread = merge(mean, spread, float(rows * step), *others)
    both = jnp.concatenate([mean[0:1], spread[0:1]], axis=0)
    stats[...] = jnp.broadcast_to(both[None], stats.shape)


def read_stats(stats, rows):
    devices, _, channels = stats.shape
    shape = (8, channels)
    means = [jnp.broadcast_to(stats[k, 0:1, :], shape) for k in range(devices)]
    spreads = [jnp.broadcast_to(stats[k, 1:2, :], shape) for k in range(devices)]
    mean = functools.reduce(jnp.add, means) / devices
    spread = functools.reduce(jnp.add, spreads)
    spread = spread + rows * functools.reduce(jnp.add, [(m - mean) * (m - mean) for m in means])
    rows = rows * devices
    lane = lax.broadcasted_iota(jnp.int32, shape, 1)
    step = 1
    while step < channels // GROUPS:
        low = jnp.bitwise_and(lane, step) == 0
        others = [
            jnp.where(low, pltpu.roll(row, channels - step, 1), pltpu.roll(row, step, 1))
            for row in (mean, spread)
        ]
        mean, spread = merge(mean, spread, rows, *others)
        rows, step = 2.0 * rows, 2 * step
    return mean, lax.rsqrt(spread / rows + EPSILON)


def silu_of_double(h):
    return h + h * jnp.tanh(h)


def norm_kernel(ny, nx, inner, ends, stats, gain, offset, out, pooled, *refs):
    y_edges, x_edges, corners, half = refs
    depth, edge = inner.shape[0] + 6, inner.shape[1]
    deep, deep_depth = edge // 2, depth // 2
    f32, bf16 = jnp.float32, jnp.bfloat16
    above, left = Square().low_sides()
    depth_at = lax.axis_index("gz")
    mean, scale = read_stats(stats, float(edge**3))
    scale = scale * (0.5 * gain[...])
    shift = 0.5 * offset[...]
    for k in range(deep_depth):
        value = [
            ends[z] if z < 3 else inner[z - 3] if z < depth - 3 else ends[z - depth + 6]
            for z in (2 * k, 2 * k + 1)
        ]
        value = jnp.stack(value).reshape(edge * edge // 4, 8, 128)
        value = silu_of_double((value - mean) * scale + shift)
        value = value.reshape(2, edge, edge, 128).astype(bf16)
        if 0 < k < deep_depth - 1:
            out[2 * k - 2 : 2 * k] = value
        value = value.astype(f32)
        value = (value[0] + value[1]).reshape(deep, 2, edge, 128)
        half[k] = (value[:, 0] + value[:, 1]).reshape(deep * edge, 128)
        lines = half.at[k]
        pair = lines[pl.ds(0, deep * deep, stride=2), :] + lines[pl.ds(1, deep * deep, stride=2), :]
        pair = (pair * 0.125).astype(bf16).astype(f32).reshape(deep, deep, 128)
        if k == 0 or k == deep_depth - 1:
            inside = depth_at > 0 if k == 0 else depth_at < lax.axis_size("gz") - 1
            pair = jnp.where(inside, pair, 0.0)
        pooled[k] = pair
    lines = pooled.reshape(deep_depth * deep * deep, 128)
    rows = deep_depth * deep
    first_x = lines[pl.ds(0, rows, stride=deep), :]
    last_x = lines[pl.ds(deep - 1, rows, stride=deep), :]
    first_y, last_y = (pooled[:, y].reshape(rows, 128) for y in (0, deep - 1))
    ends = []
    for y in (0, deep - 1):
        for x in (0, deep - 1):
            ends.append(lines[pl.ds(y * deep + x, deep_depth, stride=deep * deep), :])
    if ny == 1:
        above, left = above[0], left[0]
        y_edges[0] = jnp.where(above, first_y, last_y).astype(bf16)
        x_edges[0] = jnp.where(left, first_x, last_x).astype(bf16)
        corners[0, 0:deep_depth] = jnp.where(
            above, jnp.where(left, ends[0], ends[1]), jnp.where(left, ends[2], ends[3])
        )
    else:
        y_edges[0], y_edges[1] = first_y.astype(bf16), last_y.astype(bf16)
        x_edges[0], x_edges[1] = first_x.astype(bf16), last_x.astype(bf16)
        for k in range(4):
            corners[k, 0:deep_depth] = ends[k]


def stack_kernel(*refs):
    out = refs[-1]
    for k in range(out.shape[0]):
        out[k] = refs[k][: out.shape[1], : out.shape[2]]


def stack(*arrays, part=None):
    vmem = pl.BlockSpec(memory_space=pltpu.VMEM)
    shape = (part or arrays[0].shape[:2]) + arrays[0].shape[2:]
    return pl.pallas_call(
        stack_kernel,
        out_shape=jax.ShapeDtypeStruct((len(arrays),) + shape, arrays[0].dtype),
        in_specs=[vmem] * len(arrays),
        out_specs=vmem,
        compiler_params=pltpu.CompilerParams(vmem_limit_bytes=VMEM_BYTES),
    )(*arrays)


def place_weights(own, held, out):
    tile = lax.axis_index("yx")
    out[tile] = own[...]
    if len(held) == 1:
        pieces, others, size = held[0].shape[:3]
        for piece in range(pieces):
            at = jnp.minimum(jnp.bitwise_xor(Riders.mine(), piece) * size, own.shape[0] - size)
            for k in range(others):
                out[jnp.bitwise_xor(tile, k + 1), pl.ds(at, size)] = held[0][piece, k]
    else:
        for k, shard in enumerate(held):
            out[lax.rem(tile + len(held) - k, len(held) + 1)] = shard[...]


def tap_rows(weight, taps):
    per = weight.shape[1] // 27
    return jnp.concatenate(
        [weight[:, pl.ds(tap * per, per)].reshape(-1, 128) for tap in taps], axis=1
    )


def dot_rows(left, right):
    return lax.dot_general(
        left, right, (((1,), (1,)), ((), ())), preferred_element_type=jnp.float32
    )


def deep_kernel(pooled, own, *refs):
    *held, act, weight, grid, packed = refs
    depth, deep = pooled.shape[0], pooled.shape[1]
    place_weights(own, held, weight)
    grid[...] = jnp.zeros(grid.shape, jnp.float32)
    grid[:, 1 : deep + 1, 8:16] = pooled[...]
    for dx in range(3):
        plane = grid[:, :, 7 + dx : 15 + dx]
        for y in range(deep + 1):
            both = jnp.concatenate([plane[:, y], plane[:, y + 1]], axis=1)
            packed[:, y // 2, y % 2, :, dx * 128 : dx * 128 + 128] = both.astype(jnp.bfloat16)
    rows = deep**3
    total = None
    for dz in range(3):
        left = jnp.concatenate(
            [
                packed[dz : dz + deep, dy // 2 : dy // 2 + deep // 2, dy % 2].reshape(rows, 384)
                for dy in range(3)
            ],
            axis=1,
        )
        term = dot_rows(left, tap_rows(weight, range(dz * 9, dz * 9 + 9)))
        total = term if total is None else total + term
    for half in range(act.shape[0]):
        act[half] = total[:, half * 128 : half * 128 + 128]


def deep_rim_kernel(ny, nx, own, y_halos, x_halos, corners, weight, act, stats, line):
    depth, deep = line.shape[0], line.shape[1] - 16
    halves = act.shape[0]
    f32 = jnp.float32
    square = deep * deep
    above, left = Square().low_sides()
    act[...] = own[...]
    flat = line.reshape(depth * line.shape[1], 128)

    def shifts():
        return jnp.concatenate(
            [
                line[dz : dz + deep, 7 + d : 7 + d + deep].reshape(square, 128).astype(jnp.bfloat16)
                for dz in range(3)
                for d in range(3)
            ],
            axis=1,
        )

    for i in range(ny):
        line[...] = jnp.zeros(line.shape, f32)
        line[:, 8 : 8 + deep] = y_halos[i].astype(f32).reshape(depth, deep, 128)
        for j in range(nx):
            end = corners[i * nx + j, 0:depth]
            first, last = jnp.where(left[j], end, 0.0), jnp.where(left[j], 0.0, end)
            if nx == 1 or j == 0:
                flat[pl.ds(7, depth, stride=line.shape[1]), :] = first
            if nx == 1 or j == 1:
                flat[pl.ds(8 + deep, depth, stride=line.shape[1]), :] = last
        tap = jnp.where(above[i], 0, 6)
        taps = [tap + dz * 9 + dx for dz in range(3) for dx in range(3)]
        terms = dot_rows(shifts(), tap_rows(weight, taps))
        for half in range(halves):
            rows = act.at[half].reshape(deep, deep, deep, 128)
            term = terms[:, half * 128 : half * 128 + 128].reshape(deep, deep, 128)
            rows[:, jnp.where(above[i], 0, deep - 1)] += term
    for j in range(nx):
        line[...] = jnp.zeros(line.shape, f32)
        line[:, 8 : 8 + deep] = x_halos[j].astype(f32).reshape(depth, deep, 128)
        tap = jnp.where(left[j], 0, 2)
        taps = [tap + dz * 9 + dy * 3 for dz in range(3) for dy in range(3)]
        terms = dot_rows(shifts(), tap_rows(weight, taps))
        first, last = jnp.where(left[j], terms, 0.0), jnp.where(left[j], 0.0, terms)
        for half in range(halves):
            lanes, rows = slice(half * 128, half * 128 + 128), act.at[half]
            if nx == 1 or j == 0:
                rows[pl.ds(0, square, stride=deep), :] += first[:, lanes]
            if nx == 1 or j == 1:
                rows[pl.ds(deep - 1, square, stride=deep), :] += last[:, lanes]

    rows = deep**3 // 8
    means, spreads = [], []
    for half in range(halves):
        total = act[half].reshape(rows, 8, 128)
        means.append(jnp.sum(total, axis=0) / rows)
        off = total - means[-1]
        spreads.append(jnp.sum(off * off, axis=0))
    put_stats(stats, *(jnp.concatenate(part, axis=1) for part in (means, spreads)), rows)


def final_kernel(act, stats, gain, offset, up, mid, out, wide, held, sems):
    edge = mid.shape[0]
    deep = edge // 2
    f32 = jnp.float32
    mean, scale = read_stats(stats, float(deep**3))
    scale = scale * (0.5 * gain[...])
    shift = 0.5 * offset[...]
    planes = 2
    size = planes * deep * deep
    copies = []
    for k in range(0, deep, planes):
        at = slice(k * deep * deep, k * deep * deep + size)
        value = jnp.concatenate([act[half, at] for half in range(act.shape[0])], axis=1)
        value = value.reshape(size // 8, 8, -1)
        value = silu_of_double((value - mean) * scale + shift)
        value = value.reshape(size, -1).astype(jnp.bfloat16)
        lifted = jnp.dot(value, up[...], preferred_element_type=f32)
        lines = wide.at[k // planes]
        lines[pl.ds(0, size, stride=2), :] = lifted
        lines[pl.ds(1, size, stride=2), :] = lifted
        add = lines[...].reshape(planes, 1, deep, 1, edge, 128)
        at = pl.ds(2 * k, 2 * planes)
        old = mid[at].astype(f32).reshape(planes, 2, deep, 2, edge, 128)
        held[at] = (old + add).astype(jnp.bfloat16).reshape(2 * planes, edge, edge, 128)
        copy = pltpu.make_async_copy(held.at[at], out.at[at], sems.at[k // planes])
        copy.start()
        copies.append(copy)
    for copy in copies:
        copy.wait()


def body(
    features, conv_weight, gain_mid, offset_mid, deep_weight, gain_deep, offset_deep, up_weight
):
    f32, bf16 = jnp.float32, jnp.bfloat16
    edge, channels = features.shape[0], features.shape[3]
    deep = edge // 2
    deep_channels = gain_deep.shape[0]
    square = Square()
    tiles = square.tiles
    devices = lax.axis_size("gz") * tiles
    ny, nx = (len(sides) for sides in square.low_sides())
    riders = Riders(deep_weight.shape[4])

    own = jnp.moveaxis(deep_weight, 4, 3).reshape(-1, 16, channels)
    conv_weight = conv_weight.reshape(27, channels, channels)
    *edges, field, conv_weight = call(
        functools.partial(start_kernel, ny, nx, riders.size),
        [
            ((ny, edge + riders.size, edge, channels), bf16),
            ((nx, edge + riders.size, edge, channels), bf16),
            ((ny * nx, 1 + riders.size, edge, channels), bf16),
            ((edge + 2, edge + 2, edge, channels), bf16),
            (conv_weight.shape, bf16),
        ],
        [((nx, edge * edge, 8, channels), f32), pltpu.SemaphoreType.DMA((8,))],
        features,
        conv_weight,
        own,
        nbytes=5 << 20,
        in_hbm=3,
    )
    halos = square.halos(*(list(piece) for piece in edges))
    conv_flops = 54 * channels * channels * edge**3
    act, taps, pairs, own = call(
        conv_kernel,
        [
            ((edge, edge, edge, channels), f32),
            ((9 * channels, 3 * channels), bf16),
            ((12 * channels, 2 * channels), bf16),
            (own.shape, bf16),
        ],
        [pltpu.SemaphoreType.DMA],
        own,
        field,
        conv_weight,
        flops=conv_flops,
        nbytes=6 << 20,
        in_hbm=1,
    )
    (y, x, corner), act = lax.optimization_barrier((halos, act))
    y, x, corner = jnp.stack(y), jnp.stack(x), jnp.stack(corner)
    face = ((3 * (edge + ny + nx) + ny * nx, edge, channels), bf16)
    held = [((4, riders.size, 16, channels), bf16)] if riders.size else []
    outer, inner, *held = call(
        functools.partial(face_kernel, ny, nx, riders.size),
        [((face[0][0] + 2,) + face[0][1:], bf16), face] + held,
        [],
        field,
        y,
        x,
        corner,
    )
    outer, inner = swap_depth(outer, inner)
    if riders.size:
        held = held[0][None]
        other = swap(held, *riders.STEPS[0])
    else:
        held = rotate_shards(own)
    six = ((6, edge, edge, channels), f32)
    column = (edge + 16, channels)
    middle, partial, stats = call(
        functools.partial(side_kernel, ny, nx),
        [
            ((edge - 2, edge, edge, channels), f32),
            ((4, edge, edge, channels), f32),
            ((16, channels), f32),
        ],
        [((edge + 2, edge, edge, channels), f32), ((edge + 4,) + column, f32)],
        act,
        y,
        x,
        corner,
        taps,
    )
    room = [
        ((3, edge, edge, channels), f32),
        ((4, edge + 2, edge, channels), bf16),
        ((5,) + column, f32),
    ]
    (ends,) = call(
        functools.partial(inner_kernel, ny, nx), [six], room, field, partial, inner, taps, pairs
    )
    if riders.size:
        ends, other = lax.optimization_barrier((ends, other))
        held = stack(held, other, part=(1, 3)).reshape((2, 3) + held.shape[2:])
        other = swap(held, *riders.STEPS[1])
    ends, stats = call(
        functools.partial(outer_kernel, ny, nx),
        [six, ((devices, 2, channels), f32)],
        room,
        field,
        stats,
        ends,
        outer,
        taps,
        pairs,
        flops=conv_flops,
    )
    stats = share(stats)
    if riders.size:
        stats, other = lax.optimization_barrier((stats, other))
        held = stack(held, other).reshape((-1,) + held.shape[1:])
        other = swap(held, *riders.STEPS[2])
        held = [stack(held, other).reshape((-1,) + held.shape[1:])]
    out, pooled, *edges = call(
        functools.partial(norm_kernel, ny, nx),
        [
            ((edge, edge, edge, channels), bf16),
            ((deep + 2, deep, deep, channels), f32),
            ((ny, (deep + 2) * deep, channels), bf16),
            ((nx, (deep + 2) * deep, channels), bf16),
            ((ny * nx, 16, channels), f32),
        ],
        [((deep + 2, deep * edge, channels), f32)],
        middle,
        ends,
        stats,
        gain_mid.reshape(1, channels),
        offset_mid.reshape(1, channels),
        flops=20 * channels * edge**3,
        nbytes=3 << 20,
    )
    y, x, corner = square.halos(*(list(piece) for piece in edges))
    halves = ((deep_channels // 128, deep**3, 128), f32)
    deep_act, weight = call(
        deep_kernel,
        [halves, ((tiles,) + own.shape, bf16)],
        [
            ((deep + 2, deep + 2, 24, channels), f32),
            ((deep + 2, deep // 2 + 1, 2, 16, 3 * channels), bf16),
        ],
        pooled,
        own,
        *held,
        flops=54 * channels * deep_channels * deep**3,
        nbytes=4 << 20,
    )
    deep_act, stats = call(
        functools.partial(deep_rim_kernel, ny, nx),
        [halves, ((devices, 2, deep_channels), f32)],
        [((deep + 2, 24, channels), f32)],
        deep_act,
        jnp.stack(y),
        jnp.stack(x),
        jnp.stack(corner),
        weight,
        flops=4 * channels * deep_channels * deep**3,
        nbytes=3 << 20,
    )
    stats = share(stats)
    (decoded,) = call(
        final_kernel,
        [((edge, edge, edge, channels), bf16)],
        [
            ((deep // 2, 4 * deep * deep, channels), f32),
            ((edge, edge, edge, channels), bf16),
            pltpu.SemaphoreType.DMA((deep // 2,)),
        ],
        deep_act,
        stats,
        gain_deep.reshape(1, deep_channels),
        offset_deep.reshape(1, deep_channels),
        up_weight,
        out,
        flops=4 * deep_channels * channels * deep**3,
        nbytes=3 << 20,
        out_hbm=True,
    )
    return decoded


def solution(mesh):
    placed = (
        P(("cand", "gz"), "yx", None, None),
        P(),
        P(),
        P(),
        P(None, None, None, None, "yx"),
        P(),
        P(),
        P(),
    )
    return jax.shard_map(
        body,
        mesh=mesh,
        in_specs=placed,
        out_specs=P(("cand", "gz"), "yx", None, None),
        check_vma=False,
    )
```

```python
import functools
import math

import jax
import jax.numpy as jnp
from jax import lax
from jax.experimental import pallas as pl
from jax.experimental.pallas import tpu as pltpu
from jax.sharding import PartitionSpec as P

GROUPS = 32
EPSILON = 1e-05
PART = ("gz", "yx")
VMEM_BYTES = 32 * 1024 * 1024


class Square:
    def __init__(self):
        self.tiles = lax.axis_size("yx")
        self.side = math.isqrt(self.tiles)
        tile = lax.axis_index("yx")
        self.row, self.column = tile // self.side, tile % self.side
        self.folded = self.side == 2
        self.steps = (0,) if self.folded else (-1, 1)

    def low_sides(self):
        if self.folded:
            return [self.row == 1], [self.column == 1]
        return [True, False], [True, False]

    def route(self, down, right):
        pairs = []
        for tile in range(self.tiles):
            row, column = tile // self.side + down, tile % self.side + right
            if 0 <= row < self.side and 0 <= column < self.side:
                pairs.append((tile, row * self.side + column))
        return pairs

    def swap_route(self, mask):
        return [(tile, tile ^ mask) for tile in range(self.tiles)]

    def halos(self, y_edges, x_edges, corners):
        if self.folded:
            y = lax.ppermute(y_edges[0], "yx", self.swap_route(2))
            x = lax.ppermute(x_edges[0], "yx", self.swap_route(1))
            corner = lax.ppermute(corners[0], "yx", self.swap_route(3))
            return [y], [x], [corner]
        y = [lax.ppermute(y_edges[k], "yx", self.route((1, -1)[1 - k], 0)) for k in (1, 0)]
        x = [lax.ppermute(x_edges[k], "yx", self.route(0, (1, -1)[1 - k])) for k in (1, 0)]
        corner = [
            lax.ppermute(corners[2 * k + j], "yx", self.route((1, -1)[1 - k], (1, -1)[1 - j]))
            for k in (1, 0)
            for j in (1, 0)
        ]
        return y, x, corner


def swap_depth(outer, inner):
    size = lax.axis_size("gz")
    routes = [[], []]
    for low in range(size - 1):
        routes[low % 2] += [(low, low + 1), (low + 1, low)]
    return lax.ppermute(outer, "gz", routes[1]), lax.ppermute(inner, "gz", routes[0])


class Riders:
    STEPS = (("cand", 1), ("gz", 2), ("gz", 1))

    def __init__(self, rows):
        self.tiles = 27 * rows // 16
        self.fits = (
            lax.axis_size("yx") == 4
            and lax.axis_size("cand") % 2 == 0
            and lax.axis_size("gz") % 4 == 0
            and self.tiles >= 8
        )
        self.size = -(-self.tiles // 8) if self.fits else 0

    @classmethod
    def mine(cls):
        return sum(
            lax.axis_index(axis) // mask % 2 * 2**k for k, (axis, mask) in enumerate(cls.STEPS)
        )


def rotate_shards(piece):
    tiles = lax.axis_size("yx")
    return [
        lax.ppermute(piece, "yx", [(i, (i + k) % tiles) for i in range(tiles)]) for k in range(1, tiles)
    ]


def swap(block, axis, mask):
    return lax.ppermute(block, axis, [(i, i ^ mask) for i in range(lax.axis_size(axis))])


def share(stats):
    return lax.all_gather(stats[0], PART)


def call(kernel, outs, scratch, *arrays, flops=0, nbytes=0, in_hbm=0, out_hbm=False):
    vmem, hbm = (pl.BlockSpec(memory_space=space) for space in (pltpu.VMEM, pltpu.HBM))
    far, near = arrays[:in_hbm], arrays[in_hbm:]
    far = [pltpu.with_memory_space_constraint(array, pltpu.HBM) for array in far]
    return pl.pallas_call(
        kernel,
        out_shape=[jax.ShapeDtypeStruct(shape, dtype) for shape, dtype in outs],
        in_specs=[hbm] * len(far) + [vmem] * len(near),
        out_specs=[hbm if out_hbm else vmem] * len(outs),
        scratch_shapes=[pltpu.VMEM(*entry) if isinstance(entry, tuple) else entry for entry in scratch],
        compiler_params=pltpu.CompilerParams(vmem_limit_bytes=VMEM_BYTES),
        cost_estimate=pl.CostEstimate(flops=flops, bytes_accessed=nbytes, transcendentals=0),
    )(*far, *near)


def start_kernel(ny, nx, size, x_in, w_in, d_in, y_out, x_out, corners, x, w, lines, sems):
    edge = x_in.shape[0]
    f32, bf16 = jnp.float32, jnp.bfloat16
    above, left = Square().low_sides()
    chunks = 4
    planes = edge // chunks
    first = [
        pltpu.make_async_copy(
            x_in.at[pl.ds(k * planes, planes)],
            x.at[pl.ds(1 + k * planes, planes), pl.ds(1, edge)],
            sems.at[k],
        )
        for k in range(chunks)
    ]
    later = []
    if size:
        at = jnp.minimum(Riders.mine() * size, d_in.shape[0] - size)
        for k, (out, begin) in enumerate(((y_out, edge), (x_out, edge), (corners, 1))):
            later.append(
                pltpu.make_async_copy(
                    d_in.at[pl.ds(at, size)], out.at[0, pl.ds(begin, size)], sems.at[chunks + k]
                )
            )
    later.append(pltpu.make_async_copy(w_in, w, sems.at[chunks + 3]))
    for copy in first + later:
        copy.start()
    x[0] = jnp.zeros(x.shape[1:], bf16)
    x[edge + 1] = jnp.zeros(x.shape[1:], bf16)
    blank = jnp.zeros((edge,) + x.shape[2:], bf16)
    x[1 : edge + 1, 0] = blank
    x[1 : edge + 1, edge + 1] = blank
    flat = lines.reshape(nx * edge * edge * 8, 128)
    part = planes * edge
    for k in range(chunks):
        first[k].wait()
        at, here = pl.ds(k * planes, planes), pl.ds(1 + k * planes, planes)
        for i in range(ny):
            row = jnp.where(above[i], 1, edge)
            y_out[i, at] = x[here, row]
        for j in range(nx):
            low = x[here, 1 : edge + 1, 0:8].astype(f32).reshape(part, 8, 128)
            high = x[here, 1 : edge + 1, edge - 8 : edge].astype(f32).reshape(part, 8, 128)
            high = pltpu.roll(high, 1, 1)
            kept = jnp.where(left[j], low, high)
            lines[j, k * part : k * part + part] = kept
            begin = (j * edge * edge + k * part) * 8
            column = flat[pl.ds(begin, part, stride=8), :]
            x_out[j, at] = column.astype(bf16).reshape(planes, edge, 128)
    for i in range(ny):
        for j in range(nx):
            begin = j * edge * edge * 8
            low = flat[pl.ds(begin, edge, stride=8 * edge), :]
            high = flat[pl.ds(begin + 8 * (edge - 1), edge, stride=8 * edge), :]
            kept = jnp.where(above[i], low, high)
            corners[i * nx + j, 0] = kept.astype(bf16)
    for copy in later:
        copy.wait()


def face_kernel(ny, nx, size, x, y_halos, x_halos, corners, outer, inner, *riders):
    edge = outer.shape[1]
    wide = edge + ny + nx
    odd = lax.axis_index("gz") % 2
    far = edge - 3
    for face, at in ((outer, odd * far), (inner, (1 - odd) * far)):
        for k in range(3):
            row = k * wide
            face[row : row + edge] = x[1 + at + k, 1 : edge + 1]
            for i in range(ny):
                face[row + edge + i] = y_halos[i, at + k]
            for j in range(nx):
                face[row + edge + ny + j] = x_halos[j, at + k]
        for k in range(ny * nx):
            face[3 * wide + k] = corners[k, 0]
    for k in range(inner.shape[0], outer.shape[0]):
        outer[k] = corners[0, 0]
    if size:
        riders[0][0] = x_halos[0, edge : edge + size]
        riders[0][1] = y_halos[0, edge : edge + size]
        riders[0][2] = corners[0, 1 : 1 + size]
        riders[0][3] = corners[0, 1 : 1 + size]


def spread_taps(weight, taps):
    for tap in range(27):
        row, lane = tap // 3 * 128, tap % 3 * 128
        taps[row : row + 128, lane : lane + 128] = weight[tap]


def pair_taps(weight, pairs):
    for dz in range(3):
        for line in range(4):
            row = (dz * 4 + line) * 128
            for out in range(2):
                lane = out * 128
                if 0 <= line - out < 3:
                    block = weight[dz * 9 + (line - out) * 3 + 2]
                else:
                    block = jnp.zeros((128, 128), pairs.dtype)
                pairs[row : row + 128, lane : lane + 128] = block


def join_x(wide, edge):
    place = lax.broadcasted_iota(jnp.int32, wide.shape[:2] + (128,), 1)
    after = jnp.where(place > 0, pltpu.roll(wide[:, :, :128], 1, 1), 0.0)
    before = jnp.where(place < edge - 1, pltpu.roll(wide[:, :, 256:], edge - 1, 1), 0.0)
    return wide[:, :, 128:256] + after + before


def convolve(grid, count, taps, pairs, put):
    edge = grid.shape[2]
    planes = min(count, 4)
    rows = planes * edge * edge
    place = lax.broadcasted_iota(jnp.int32, (planes * edge, edge, 128), 1)
    halved = grid.reshape(grid.shape[0], edge // 2 + 1, 2, edge, 128)
    for z in range(0, count, planes):
        left = jnp.concatenate(
            [
                grid[z + dz : z + dz + planes, dy : dy + edge].reshape(rows, 128)
                for dz in range(3)
                for dy in range(3)
            ],
            axis=1,
        )
        wide = jnp.dot(left, taps[:, 0:256], preferred_element_type=jnp.float32)
        wide = wide.reshape(planes * edge, edge, 256)
        left = jnp.concatenate(
            [
                halved[z + dz : z + dz + planes, line // 2 : line // 2 + edge // 2, line % 2].reshape(
                    rows // 2, 128
                )
                for dz in range(3)
                for line in range(4)
            ],
            axis=1,
        )
        two = jnp.dot(left, pairs[...], preferred_element_type=jnp.float32)
        two = two.reshape(planes * edge // 2, edge, 256)
        two = jnp.stack([two[:, :, :128], two[:, :, 128:]], axis=1).reshape(planes * edge, edge, 128)
        after = jnp.where(place > 0, pltpu.roll(wide[:, :, :128], 1, 1), 0.0)
        before = jnp.where(place < edge - 1, pltpu.roll(two, edge - 1, 1), 0.0)
        new = wide[:, :, 128:256] + after + before
        put(z, new.reshape(planes, edge, edge, 128))


def conv_kernel(deep_in, x, weight, act, taps, pairs, deep_weight, sem):
    copy = pltpu.make_async_copy(deep_in, deep_weight, sem)
    copy.start()
    edge = act.shape[0]
    spread_taps(weight, taps)
    pair_taps(weight, pairs)

    def put(z, new):
        act[z : z + new.shape[0]] = new

    convolve(x, edge, taps, pairs, put)
    copy.wait()


def y_terms(line, low, taps):
    planes, edge = line.shape[0] - 2, line.shape[1]
    left = jnp.concatenate(
        [line[dz : dz + planes].reshape(planes * edge, 128) for dz in range(3)], axis=1
    )
    start = jnp.where(low, 0, 256)
    right = jnp.concatenate(
        [taps[pl.ds(pl.multiple_of(start + dz * 384, 128), 128), :] for dz in range(3)], axis=0
    )
    wide = jnp.dot(left, right, preferred_element_type=jnp.float32)
    return join_x(wide.reshape(planes, edge, 384), edge)


def x_terms(column, taps):
    planes, edge = column.shape[0] - 2, column.shape[1] - 16
    lines = [column[:, 7 + dy : 7 + dy + edge].astype(jnp.bfloat16) for dy in range(3)]
    left = jnp.concatenate(
        [line[dz : dz + planes].reshape(planes * edge, 128) for dz in range(3) for line in lines],
        axis=1,
    )
    right = jnp.concatenate([taps[:, 0:128], taps[:, 256:384]], axis=1)
    both = jnp.dot(left, right, preferred_element_type=jnp.float32)
    return both[:, :128], both[:, 128:]


def fill_column(column, at, voxels, ends, above):
    count, edge = voxels.shape[:2]
    rows = edge + 16
    lines = column.reshape(column.shape[0] * rows, 128)
    column[at : at + count, 8 : 8 + edge] = voxels.astype(jnp.float32)
    for i, end in enumerate(ends):
        first = last = end.astype(jnp.float32)
        if len(ends) == 1:
            first, last = jnp.where(above[0], first, 0.0), jnp.where(above[0], 0.0, last)
        if len(ends) == 1 or i == 0:
            lines[pl.ds(at * rows + 7, count, stride=rows), :] = first
        if len(ends) == 1 or i == 1:
            lines[pl.ds(at * rows + 8 + edge, count, stride=rows), :] = last


def add_column(act, terms, j, nx, low):
    planes, edge = act.shape[:2]
    flat = act.reshape(planes * edge * edge, 128)
    first, last = terms
    if nx == 1:
        first, last = jnp.where(low, first, 0.0), jnp.where(low, 0.0, last)
    if nx == 1 or j == 0:
        flat[pl.ds(0, planes * edge, stride=edge), :] += first
    if nx == 1 or j == 1:
        flat[pl.ds(edge - 1, planes * edge, stride=edge), :] += last


def moments(planes):
    count, edge = planes.shape[:2]
    zero = jnp.zeros((8, 128), jnp.float32)

    def sum_step(k, carry):
        return carry + jnp.sum(planes[k].reshape(edge * 2, 8, 128), axis=0)

    mean = lax.fori_loop(0, count, sum_step, zero, unroll=True) / (count * edge * edge // 8)

    def spread_step(k, carry):
        off = planes[k].reshape(edge * 2, 8, 128) - mean
        return carry + jnp.sum(off * off, axis=0)

    return mean, lax.fori_loop(0, count, spread_step, zero, unroll=True)


def side_kernel(ny, nx, own, y_halos, x_halos, corners, taps, inner, ends, stats, act, column):
    edge = own.shape[0]
    act[0] = jnp.zeros(act.shape[1:], jnp.float32)
    act[edge + 1] = jnp.zeros(act.shape[1:], jnp.float32)
    act[1 : edge + 1] = own[...]
    above, left = Square().low_sides()
    blank = jnp.zeros((2, edge, 128), jnp.bfloat16)
    for i in range(ny):
        line = jnp.concatenate([blank, y_halos[i, 0:edge], blank], axis=0)
        act[:, jnp.where(above[i], 0, edge - 1)] += y_terms(line, above[i], taps)
    for j in range(nx):
        column[...] = jnp.zeros(column.shape, jnp.float32)
        fill_column(
            column, 2, x_halos[j, 0:edge], [corners[i * nx + j, 0] for i in range(ny)], above
        )
        add_column(act, x_terms(column, taps), j, nx, left[j])
    inner[...] = act[2:edge]
    ends[0:2] = act[0:2]
    ends[2:4] = act[edge : edge + 2]
    mean, spread = moments(act.at[2:edge])
    stats[0:8] = mean
    stats[8:16] = spread


def add_face(ny, nx, behind, face, x, taps, pairs, ends, three, grid, column):
    edge = x.shape[2]
    wide_face = edge + ny + nx
    f32 = jnp.float32
    above, left = Square().low_sides()
    end = pl.ds(jnp.where(behind, 3, 0), 3)
    three[...] = ends[end]
    blank = jnp.zeros(grid.shape[:1] + grid.shape[2:], grid.dtype)
    grid[:, 0] = blank
    grid[:, edge + 1] = blank
    first = jnp.where(behind, 1, 0)
    for k in range(3):
        grid[first + k, 1 : edge + 1] = face[k * wide_face : k * wide_face + edge]
    grid[jnp.where(behind, 0, 3), 1 : edge + 1] = x[jnp.where(behind, edge, 1), 1 : edge + 1]

    def put(z, new):
        three[pl.ds(first + z, new.shape[0])] += new

    convolve(grid, 2, taps, pairs, put)
    beside = jnp.where(behind, 1, 2)
    lines = [grid[beside, dy : dy + edge].reshape(edge * edge, 128) for dy in range(3)]
    rows = taps[pl.ds(pl.multiple_of(jnp.where(behind, 768, 0), 128), 384), :]
    wide = jnp.dot(jnp.concatenate(lines, axis=1), rows, preferred_element_type=f32)
    three[jnp.where(behind, 0, 2)] += join_x(wide.reshape(edge, edge, 384), edge)

    def five(voxels):
        gap = jnp.zeros((2,) + voxels.shape[1:], voxels.dtype)
        return jnp.where(
            behind,
            jnp.concatenate([gap, voxels], axis=0),
            jnp.concatenate([voxels, gap], axis=0),
        )

    def rim(row):
        return five(jnp.stack([face[k * wide_face + edge + row] for k in range(3)]).astype(f32))

    for i in range(ny):
        terms = y_terms(rim(i).astype(jnp.bfloat16), above[i], taps)
        three[:, jnp.where(above[i], 0, edge - 1)] += terms
    for j in range(nx):
        column[...] = jnp.zeros(column.shape, f32)
        tails = []
        for i in range(ny):
            tile = face[3 * wide_face + i * nx + j].astype(f32)
            tails.append(five(jnp.where(behind, tile[:3], tile[edge - 3 :])))
        fill_column(column, 0, rim(ny + j), tails, above)
        add_column(three, x_terms(column, taps), j, nx, left[j])
    ends[end] = three[...]


def inner_kernel(ny, nx, x, partial, face, taps, pairs, ends, three, grid, column):
    blank = jnp.zeros(ends.shape[1:], jnp.float32)
    ends[0] = blank
    ends[1:5] = partial[...]
    ends[5] = blank
    behind = lax.axis_index("gz") % 2 == 0
    add_face(ny, nx, behind, face, x, taps, pairs, ends, three, grid, column)


def outer_kernel(ny, nx, x, middle_stats, ends, face, taps, pairs, act, stats, three, grid, column):
    edge = x.shape[2]
    act[...] = ends[...]
    behind = lax.axis_index("gz") % 2 == 1
    add_face(ny, nx, behind, face, x, taps, pairs, act, three, grid, column)
    mean, spread = moments(act.at[2:4])
    few, many = edge * edge // 4, (edge - 2) * edge * edge // 8
    middle_mean, middle_spread = middle_stats[0:8], middle_stats[8:16]
    off = middle_mean - mean
    part = few / (few + many)
    spread = spread + middle_spread + (many * part) * (off * off)
    put_stats(stats, middle_mean - part * off, spread, few + many)


def merge(mean, spread, rows, other_mean, other_spread):
    off = mean - other_mean
    return 0.5 * (mean + other_mean), spread + other_spread + (0.5 * rows) * (off * off)


def put_stats(stats, mean, spread, rows):
    for step in (1, 2, 4):
        others = pltpu.roll(mean, step, 0), pltpu.roll(spread, step, 0)
        mean, spread = merge(mean, spread, float(rows * step), *others)
    both = jnp.concatenate([mean[0:1], spread[0:1]], axis=0)
    stats[...] = jnp.broadcast_to(both[None], stats.shape)


def read_stats(stats, rows):
    devices, _, channels = stats.shape
    shape = (8, channels)
    means = [jnp.broadcast_to(stats[k, 0:1, :], shape) for k in range(devices)]
    spreads = [jnp.broadcast_to(stats[k, 1:2, :], shape) for k in range(devices)]
    mean = functools.reduce(jnp.add, means) / devices
    spread = functools.reduce(jnp.add, spreads)
    spread = spread + rows * functools.reduce(jnp.add, [(m - mean) * (m - mean) for m in means])
    rows = rows * devices
    lane = lax.broadcasted_iota(jnp.int32, shape, 1)
    step = 1
    while step < channels // GROUPS:
        low = jnp.bitwise_and(lane, step) == 0
        others = [
            jnp.where(low, pltpu.roll(row, channels - step, 1), pltpu.roll(row, step, 1))
            for row in (mean, spread)
        ]
        mean, spread = merge(mean, spread, rows, *others)
        rows, step = 2.0 * rows, 2 * step
    return mean, lax.rsqrt(spread / rows + EPSILON)


def silu_of_double(h):
    return h + h * jnp.tanh(h)


def norm_kernel(ny, nx, inner, ends, stats, gain, offset, out, pooled, *refs):
    y_edges, x_edges, corners, half = refs
    depth, edge = inner.shape[0] + 6, inner.shape[1]
    deep, deep_depth = edge // 2, depth // 2
    f32, bf16 = jnp.float32, jnp.bfloat16
    above, left = Square().low_sides()
    depth_at = lax.axis_index("gz")
    mean, scale = read_stats(stats, float(edge**3))
    scale = scale * (0.5 * gain[...])
    shift = 0.5 * offset[...]
    for k in range(deep_depth):
        value = [
            ends[z] if z < 3 else inner[z - 3] if z < depth - 3 else ends[z - depth + 6]
            for z in (2 * k, 2 * k + 1)
        ]
        value = jnp.stack(value).reshape(edge * edge // 4, 8, 128)
        value = silu_of_double((value - mean) * scale + shift)
        value = value.reshape(2, edge, edge, 128).astype(bf16)
        if 0 < k < deep_depth - 1:
            out[2 * k - 2 : 2 * k] = value
        value = value.astype(f32)
        value = (value[0] + value[1]).reshape(deep, 2, edge, 128)
        half[k] = (value[:, 0] + value[:, 1]).reshape(deep * edge, 128)
        lines = half.at[k]
        pair = lines[pl.ds(0, deep * deep, stride=2), :] + lines[pl.ds(1, deep * deep, stride=2), :]
        pair = (pair * 0.125).astype(bf16).astype(f32).reshape(deep, deep, 128)
        if k == 0 or k == deep_depth - 1:
            inside = depth_at > 0 if k == 0 else depth_at < lax.axis_size("gz") - 1
            pair = jnp.where(inside, pair, 0.0)
        pooled[k] = pair
    lines = pooled.reshape(deep_depth * deep * deep, 128)
    rows = deep_depth * deep
    first_x = lines[pl.ds(0, rows, stride=deep), :]
    last_x = lines[pl.ds(deep - 1, rows, stride=deep), :]
    first_y, last_y = (pooled[:, y].reshape(rows, 128) for y in (0, deep - 1))
    ends = []
    for y in (0, deep - 1):
        for x in (0, deep - 1):
            ends.append(lines[pl.ds(y * deep + x, deep_depth, stride=deep * deep), :])
    if ny == 1:
        above, left = above[0], left[0]
        y_edges[0] = jnp.where(above, first_y, last_y).astype(bf16)
        x_edges[0] = jnp.where(left, first_x, last_x).astype(bf16)
        corners[0, 0:deep_depth] = jnp.where(
            above, jnp.where(left, ends[0], ends[1]), jnp.where(left, ends[2], ends[3])
        )
    else:
        y_edges[0], y_edges[1] = first_y.astype(bf16), last_y.astype(bf16)
        x_edges[0], x_edges[1] = first_x.astype(bf16), last_x.astype(bf16)
        for k in range(4):
            corners[k, 0:deep_depth] = ends[k]


def stack_kernel(*refs):
    out = refs[-1]
    for k in range(out.shape[0]):
        out[k] = refs[k][: out.shape[1], : out.shape[2]]


def stack(*arrays, part=None):
    vmem = pl.BlockSpec(memory_space=pltpu.VMEM)
    shape = (part or arrays[0].shape[:2]) + arrays[0].shape[2:]
    return pl.pallas_call(
        stack_kernel,
        out_shape=jax.ShapeDtypeStruct((len(arrays),) + shape, arrays[0].dtype),
        in_specs=[vmem] * len(arrays),
        out_specs=vmem,
        compiler_params=pltpu.CompilerParams(vmem_limit_bytes=VMEM_BYTES),
    )(*arrays)


def place_weights(own, held, out):
    tile = lax.axis_index("yx")
    out[tile] = own[...]
    if len(held) == 1:
        pieces, others, size = held[0].shape[:3]
        for piece in range(pieces):
            at = jnp.minimum(jnp.bitwise_xor(Riders.mine(), piece) * size, own.shape[0] - size)
            for k in range(others):
                out[jnp.bitwise_xor(tile, k + 1), pl.ds(at, size)] = held[0][piece, k]
    else:
        for k, shard in enumerate(held):
            out[lax.rem(tile + len(held) - k, len(held) + 1)] = shard[...]


def tap_rows(weight, taps):
    per = weight.shape[1] // 27
    return jnp.concatenate(
        [weight[:, pl.ds(tap * per, per)].reshape(-1, 128) for tap in taps], axis=1
    )


def dot_rows(left, right):
    return lax.dot_general(
        left, right, (((1,), (1,)), ((), ())), preferred_element_type=jnp.float32
    )


def deep_kernel(pooled, own, *refs):
    *held, act, weight, grid, packed = refs
    depth, deep = pooled.shape[0], pooled.shape[1]
    place_weights(own, held, weight)
    grid[...] = jnp.zeros(grid.shape, jnp.float32)
    grid[:, 1 : deep + 1, 8:16] = pooled[...]
    for dx in range(3):
        plane = grid[:, :, 7 + dx : 15 + dx]
        for y in range(deep + 1):
            both = jnp.concatenate([plane[:, y], plane[:, y + 1]], axis=1)
            packed[:, y // 2, y % 2, :, dx * 128 : dx * 128 + 128] = both.astype(jnp.bfloat16)
    rows = deep**3
    total = None
    for dz in range(3):
        left = jnp.concatenate(
            [
                packed[dz : dz + deep, dy // 2 : dy // 2 + deep // 2, dy % 2].reshape(rows, 384)
                for dy in range(3)
            ],
            axis=1,
        )
        term = dot_rows(left, tap_rows(weight, range(dz * 9, dz * 9 + 9)))
        total = term if total is None else total + term
    for half in range(act.shape[0]):
        act[half] = total[:, half * 128 : half * 128 + 128]


def deep_rim_kernel(ny, nx, own, y_halos, x_halos, corners, weight, act, stats, line):
    depth, deep = line.shape[0], line.shape[1] - 16
    halves = act.shape[0]
    f32 = jnp.float32
    square = deep * deep
    above, left = Square().low_sides()
    act[...] = own[...]
    flat = line.reshape(depth * line.shape[1], 128)

    def shifts():
        return jnp.concatenate(
            [
                line[dz : dz + deep, 7 + d : 7 + d + deep].reshape(square, 128).astype(jnp.bfloat16)
                for dz in range(3)
                for d in range(3)
            ],
            axis=1,
        )

    for i in range(ny):
        line[...] = jnp.zeros(line.shape, f32)
        line[:, 8 : 8 + deep] = y_halos[i].astype(f32).reshape(depth, deep, 128)
        for j in range(nx):
            end = corners[i * nx + j, 0:depth]
            first, last = jnp.where(left[j], end, 0.0), jnp.where(left[j], 0.0, end)
            if nx == 1 or j == 0:
                flat[pl.ds(7, depth, stride=line.shape[1]), :] = first
            if nx == 1 or j == 1:
                flat[pl.ds(8 + deep, depth, stride=line.shape[1]), :] = last
        tap = jnp.where(above[i], 0, 6)
        taps = [tap + dz * 9 + dx for dz in range(3) for dx in range(3)]
        terms = dot_rows(shifts(), tap_rows(weight, taps))
        for half in range(halves):
            rows = act.at[half].reshape(deep, deep, deep, 128)
            term = terms[:, half * 128 : half * 128 + 128].reshape(deep, deep, 128)
            rows[:, jnp.where(above[i], 0, deep - 1)] += term
    for j in range(nx):
        line[...] = jnp.zeros(line.shape, f32)
        line[:, 8 : 8 + deep] = x_halos[j].astype(f32).reshape(depth, deep, 128)
        tap = jnp.where(left[j], 0, 2)
        taps = [tap + dz * 9 + dy * 3 for dz in range(3) for dy in range(3)]
        terms = dot_rows(shifts(), tap_rows(weight, taps))
        first, last = jnp.where(left[j], terms, 0.0), jnp.where(left[j], 0.0, terms)
        for half in range(halves):
            lanes, rows = slice(half * 128, half * 128 + 128), act.at[half]
            if nx == 1 or j == 0:
                rows[pl.ds(0, square, stride=deep), :] += first[:, lanes]
            if nx == 1 or j == 1:
                rows[pl.ds(deep - 1, square, stride=deep), :] += last[:, lanes]

    rows = deep**3 // 8
    means, spreads = [], []
    for half in range(halves):
        total = act[half].reshape(rows, 8, 128)
        means.append(jnp.sum(total, axis=0) / rows)
        off = total - means[-1]
        spreads.append(jnp.sum(off * off, axis=0))
    put_stats(stats, *(jnp.concatenate(part, axis=1) for part in (means, spreads)), rows)


def final_kernel(act, stats, gain, offset, up, mid, out, wide, held, sems):
    edge = mid.shape[0]
    deep = edge // 2
    f32 = jnp.float32
    mean, scale = read_stats(stats, float(deep**3))
    scale = scale * (0.5 * gain[...])
    shift = 0.5 * offset[...]
    planes = 2
    size = planes * deep * deep
    copies = []
    for k in range(0, deep, planes):
        at = slice(k * deep * deep, k * deep * deep + size)
        value = jnp.concatenate([act[half, at] for half in range(act.shape[0])], axis=1)
        value = value.reshape(size // 8, 8, -1)
        value = silu_of_double((value - mean) * scale + shift)
        value = value.reshape(size, -1).astype(jnp.bfloat16)
        lifted = jnp.dot(value, up[...], preferred_element_type=f32)
        lines = wide.at[k // planes]
        lines[pl.ds(0, size, stride=2), :] = lifted
        lines[pl.ds(1, size, stride=2), :] = lifted
        add = lines[...].reshape(planes, 1, deep, 1, edge, 128)
        at = pl.ds(2 * k, 2 * planes)
        old = mid[at].astype(f32).reshape(planes, 2, deep, 2, edge, 128)
        held[at] = (old + add).astype(jnp.bfloat16).reshape(2 * planes, edge, edge, 128)
        copy = pltpu.make_async_copy(held.at[at], out.at[at], sems.at[k // planes])
        copy.start()
        copies.append(copy)
    for copy in copies:
        copy.wait()


def body(
    features, conv_weight, gain_mid, offset_mid, deep_weight, gain_deep, offset_deep, up_weight
):
    f32, bf16 = jnp.float32, jnp.bfloat16
    edge, channels = features.shape[0], features.shape[3]
    deep = edge // 2
    deep_channels = gain_deep.shape[0]
    square = Square()
    tiles = square.tiles
    devices = lax.axis_size("gz") * tiles
    ny, nx = (len(sides) for sides in square.low_sides())
    riders = Riders(deep_weight.shape[4])

    own = jnp.moveaxis(deep_weight, 4, 3).reshape(-1, 16, channels)
    conv_weight = conv_weight.reshape(27, channels, channels)
    *edges, field, conv_weight = call(
        functools.partial(start_kernel, ny, nx, riders.size),
        [
            ((ny, edge + riders.size, edge, channels), bf16),
            ((nx, edge + riders.size, edge, channels), bf16),
            ((ny * nx, 1 + riders.size, edge, channels), bf16),
            ((edge + 2, edge + 2, edge, channels), bf16),
            (conv_weight.shape, bf16),
        ],
        [((nx, edge * edge, 8, channels), f32), pltpu.SemaphoreType.DMA((8,))],
        features,
        conv_weight,
        own,
        nbytes=5 << 20,
        in_hbm=3,
    )
    halos = square.halos(*(list(piece) for piece in edges))
    conv_flops = 54 * channels * channels * edge**3
    act, taps, pairs, own = call(
        conv_kernel,
        [
            ((edge, edge, edge, channels), f32),
            ((9 * channels, 3 * channels), bf16),
            ((12 * channels, 2 * channels), bf16),
            (own.shape, bf16),
        ],
        [pltpu.SemaphoreType.DMA],
        own,
        field,
        conv_weight,
        flops=conv_flops,
        nbytes=6 << 20,
        in_hbm=1,
    )
    (y, x, corner), act = lax.optimization_barrier((halos, act))
    y, x, corner = jnp.stack(y), jnp.stack(x), jnp.stack(corner)
    face = ((3 * (edge + ny + nx) + ny * nx, edge, channels), bf16)
    held = [((4, riders.size, 16, channels), bf16)] if riders.size else []
    outer, inner, *held = call(
        functools.partial(face_kernel, ny, nx, riders.size),
        [((face[0][0] + 2,) + face[0][1:], bf16), face] + held,
        [],
        field,
        y,
        x,
        corner,
    )
    outer, inner = swap_depth(outer, inner)
    if riders.size:
        held = held[0][None]
        other = swap(held, *riders.STEPS[0])
    else:
        held = rotate_shards(own)
    six = ((6, edge, edge, channels), f32)
    column = (edge + 16, channels)
    middle, partial, stats = call(
        functools.partial(side_kernel, ny, nx),
        [
            ((edge - 2, edge, edge, channels), f32),
            ((4, edge, edge, channels), f32),
            ((16, channels), f32),
        ],
        [((edge + 2, edge, edge, channels), f32), ((edge + 4,) + column, f32)],
        act,
        y,
        x,
        corner,
        taps,
    )
    room = [
        ((3, edge, edge, channels), f32),
        ((4, edge + 2, edge, channels), bf16),
        ((5,) + column, f32),
    ]
    (ends,) = call(
        functools.partial(inner_kernel, ny, nx), [six], room, field, partial, inner, taps, pairs
    )
    ends, stats = call(
        functools.partial(outer_kernel, ny, nx),
        [six, ((devices, 2, channels), f32)],
        room,
        field,
        stats,
        ends,
        outer,
        taps,
        pairs,
    )
    if riders.size:
        stats, other = lax.optimization_barrier((stats, other))
        held = stack(held, other, part=(1, 3)).reshape((2, 3) + held.shape[2:])
        other = swap(held, *riders.STEPS[1])
        stats = share(stats)
        stats, other = lax.optimization_barrier((stats, other))
        held = stack(held, other).reshape((-1,) + held.shape[1:])
        other = swap(held, *riders.STEPS[2])
        held = [stack(held, other).reshape((-1,) + held.shape[1:])]
    else:
        stats = share(stats)
    out, pooled, *edges = call(
        functools.partial(norm_kernel, ny, nx),
        [
            ((edge, edge, edge, channels), bf16),
            ((deep + 2, deep, deep, channels), f32),
            ((ny, (deep + 2) * deep, channels), bf16),
            ((nx, (deep + 2) * deep, channels), bf16),
            ((ny * nx, 16, channels), f32),
        ],
        [((deep + 2, deep * edge, channels), f32)],
        middle,
        ends,
        stats,
        gain_mid.reshape(1, channels),
        offset_mid.reshape(1, channels),
        flops=20 * channels * edge**3,
        nbytes=3 << 20,
    )
    y, x, corner = square.halos(*(list(piece) for piece in edges))
    halves = ((deep_channels // 128, deep**3, 128), f32)
    deep_act, weight = call(
        deep_kernel,
        [halves, ((tiles,) + own.shape, bf16)],
        [
            ((deep + 2, deep + 2, 24, channels), f32),
            ((deep + 2, deep // 2 + 1, 2, 16, 3 * channels), bf16),
        ],
        pooled,
        own,
        *held,
        flops=54 * channels * deep_channels * deep**3,
        nbytes=4 << 20,
    )
    deep_act, stats = call(
        functools.partial(deep_rim_kernel, ny, nx),
        [halves, ((devices, 2, deep_channels), f32)],
        [((deep + 2, 24, channels), f32)],
        deep_act,
        jnp.stack(y),
        jnp.stack(x),
        jnp.stack(corner),
        weight,
        flops=4 * channels * deep_channels * deep**3,
        nbytes=3 << 20,
    )
    stats = share(stats)
    (decoded,) = call(
        final_kernel,
        [((edge, edge, edge, channels), bf16)],
        [
            ((deep // 2, 4 * deep * deep, channels), f32),
            ((edge, edge, edge, channels), bf16),
            pltpu.SemaphoreType.DMA((deep // 2,)),
        ],
        deep_act,
        stats,
        gain_deep.reshape(1, deep_channels),
        offset_deep.reshape(1, deep_channels),
        up_weight,
        out,
        flops=4 * deep_channels * channels * deep**3,
        nbytes=3 << 20,
        out_hbm=True,
    )
    return decoded


def solution(mesh):
    placed = (
        P(("cand", "gz"), "yx", None, None),
        P(),
        P(),
        P(),
        P(None, None, None, None, "yx"),
        P(),
        P(),
        P(),
    )
    return jax.shard_map(
        body,
        mesh=mesh,
        in_specs=placed,
        out_specs=P(("cand", "gz"), "yx", None, None),
        check_vma=False,
    )
```

```python
import functools
import math

import jax
import jax.numpy as jnp
from jax import lax
from jax.experimental import pallas as pl
from jax.experimental.pallas import tpu as pltpu
from jax.sharding import PartitionSpec as P

GROUPS = 32
EPSILON = 1e-05
PART = ("gz", "yx")
VMEM_BYTES = 32 * 1024 * 1024


class Square:
    def __init__(self):
        self.tiles = lax.axis_size("yx")
        self.side = math.isqrt(self.tiles)
        tile = lax.axis_index("yx")
        self.row, self.column = tile // self.side, tile % self.side
        self.folded = self.side == 2
        self.steps = (0,) if self.folded else (-1, 1)

    def low_sides(self):
        if self.folded:
            return [self.row == 1], [self.column == 1]
        return [True, False], [True, False]

    def route(self, down, right):
        pairs = []
        for tile in range(self.tiles):
            row, column = tile // self.side + down, tile % self.side + right
            if 0 <= row < self.side and 0 <= column < self.side:
                pairs.append((tile, row * self.side + column))
        return pairs

    def swap_route(self, mask):
        return [(tile, tile ^ mask) for tile in range(self.tiles)]

    def halos(self, y_edges, x_edges, corners):
        if self.folded:
            y = lax.ppermute(y_edges[0], "yx", self.swap_route(2))
            x = lax.ppermute(x_edges[0], "yx", self.swap_route(1))
            corner = lax.ppermute(corners[0], "yx", self.swap_route(3))
            return [y], [x], [corner]
        y = [lax.ppermute(y_edges[k], "yx", self.route((1, -1)[1 - k], 0)) for k in (1, 0)]
        x = [lax.ppermute(x_edges[k], "yx", self.route(0, (1, -1)[1 - k])) for k in (1, 0)]
        corner = [
            lax.ppermute(corners[2 * k + j], "yx", self.route((1, -1)[1 - k], (1, -1)[1 - j]))
            for k in (1, 0)
            for j in (1, 0)
        ]
        return y, x, corner


def swap_depth(outer, inner):
    size = lax.axis_size("gz")
    routes = [[], []]
    for low in range(size - 1):
        routes[low % 2] += [(low, low + 1), (low + 1, low)]
    return lax.ppermute(outer, "gz", routes[1]), lax.ppermute(inner, "gz", routes[0])


class Riders:
    STEPS = (("cand", 1), ("gz", 2), ("gz", 1))

    def __init__(self, rows):
        self.tiles = 27 * rows // 16
        self.fits = (
            lax.axis_size("yx") == 4
            and lax.axis_size("cand") % 2 == 0
            and lax.axis_size("gz") % 4 == 0
            and self.tiles >= 8
        )
        self.size = -(-self.tiles // 8) if self.fits else 0

    @classmethod
    def mine(cls):
        return sum(
            lax.axis_index(axis) // mask % 2 * 2**k for k, (axis, mask) in enumerate(cls.STEPS)
        )


def rotate_shards(piece):
    tiles = lax.axis_size("yx")
    return [
        lax.ppermute(piece, "yx", [(i, (i + k) % tiles) for i in range(tiles)]) for k in range(1, tiles)
    ]


def swap(block, axis, mask):
    return lax.ppermute(block, axis, [(i, i ^ mask) for i in range(lax.axis_size(axis))])


def share(stats):
    return lax.all_to_all(stats, PART, 0, 0)


def call(kernel, outs, scratch, *arrays, flops=0, nbytes=0, in_hbm=0, out_hbm=False):
    vmem, hbm = (pl.BlockSpec(memory_space=space) for space in (pltpu.VMEM, pltpu.HBM))
    far, near = arrays[:in_hbm], arrays[in_hbm:]
    far = [pltpu.with_memory_space_constraint(array, pltpu.HBM) for array in far]
    return pl.pallas_call(
        kernel,
        out_shape=[jax.ShapeDtypeStruct(shape, dtype) for shape, dtype in outs],
        in_specs=[hbm] * len(far) + [vmem] * len(near),
        out_specs=[hbm if out_hbm else vmem] * len(outs),
        scratch_shapes=[pltpu.VMEM(*entry) if isinstance(entry, tuple) else entry for entry in scratch],
        compiler_params=pltpu.CompilerParams(vmem_limit_bytes=VMEM_BYTES),
        cost_estimate=pl.CostEstimate(flops=flops, bytes_accessed=nbytes, transcendentals=0),
    )(*far, *near)


def start_kernel(ny, nx, size, x_in, w_in, d_in, y_out, x_out, corners, x, w, lines, sems):
    edge = x_in.shape[0]
    f32, bf16 = jnp.float32, jnp.bfloat16
    above, left = Square().low_sides()
    chunks = 4
    planes = edge // chunks
    first = [
        pltpu.make_async_copy(
            x_in.at[pl.ds(k * planes, planes)],
            x.at[pl.ds(1 + k * planes, planes), pl.ds(1, edge)],
            sems.at[k],
        )
        for k in range(chunks)
    ]
    later = []
    if size:
        at = jnp.minimum(Riders.mine() * size, d_in.shape[0] - size)
        for k, (out, begin) in enumerate(((y_out, edge), (x_out, edge), (corners, 1))):
            later.append(
                pltpu.make_async_copy(
                    d_in.at[pl.ds(at, size)], out.at[0, pl.ds(begin, size)], sems.at[chunks + k]
                )
            )
    later.append(pltpu.make_async_copy(w_in, w, sems.at[chunks + 3]))
    for copy in first + later:
        copy.start()
    x[0] = jnp.zeros(x.shape[1:], bf16)
    x[edge + 1] = jnp.zeros(x.shape[1:], bf16)
    blank = jnp.zeros((edge,) + x.shape[2:], bf16)
    x[1 : edge + 1, 0] = blank
    x[1 : edge + 1, edge + 1] = blank
    flat = lines.reshape(nx * edge * edge * 8, 128)
    part = planes * edge
    for k in range(chunks):
        first[k].wait()
        at, here = pl.ds(k * planes, planes), pl.ds(1 + k * planes, planes)
        for i in range(ny):
            row = jnp.where(above[i], 1, edge)
            y_out[i, at] = x[here, row]
        for j in range(nx):
            low = x[here, 1 : edge + 1, 0:8].astype(f32).reshape(part, 8, 128)
            high = x[here, 1 : edge + 1, edge - 8 : edge].astype(f32).reshape(part, 8, 128)
            high = pltpu.roll(high, 1, 1)
            kept = jnp.where(left[j], low, high)
            lines[j, k * part : k * part + part] = kept
            begin = (j * edge * edge + k * part) * 8
            column = flat[pl.ds(begin, part, stride=8), :]
            x_out[j, at] = column.astype(bf16).reshape(planes, edge, 128)
    for i in range(ny):
        for j in range(nx):
            begin = j * edge * edge * 8
            low = flat[pl.ds(begin, edge, stride=8 * edge), :]
            high = flat[pl.ds(begin + 8 * (edge - 1), edge, stride=8 * edge), :]
            kept = jnp.where(above[i], low, high)
            corners[i * nx + j, 0] = kept.astype(bf16)
    for copy in later:
        copy.wait()


def face_kernel(ny, nx, size, x, y_halos, x_halos, corners, outer, inner, *riders):
    edge = outer.shape[1]
    wide = edge + ny + nx
    odd = lax.axis_index("gz") % 2
    far = edge - 3
    for face, at in ((outer, odd * far), (inner, (1 - odd) * far)):
        for k in range(3):
            row = k * wide
            face[row : row + edge] = x[1 + at + k, 1 : edge + 1]
            for i in range(ny):
                face[row + edge + i] = y_halos[i, at + k]
            for j in range(nx):
                face[row + edge + ny + j] = x_halos[j, at + k]
        for k in range(ny * nx):
            face[3 * wide + k] = corners[k, 0]
    for k in range(inner.shape[0], outer.shape[0]):
        outer[k] = corners[0, 0]
    if size:
        riders[0][0] = x_halos[0, edge : edge + size]
        riders[0][1] = y_halos[0, edge : edge + size]
        riders[0][2] = corners[0, 1 : 1 + size]
        riders[0][3] = corners[0, 1 : 1 + size]


def spread_taps(weight, taps):
    for tap in range(27):
        row, lane = tap // 3 * 128, tap % 3 * 128
        taps[row : row + 128, lane : lane + 128] = weight[tap]


def pair_taps(weight, pairs):
    for dz in range(3):
        for line in range(4):
            row = (dz * 4 + line) * 128
            for out in range(2):
                lane = out * 128
                if 0 <= line - out < 3:
                    block = weight[dz * 9 + (line - out) * 3 + 2]
                else:
                    block = jnp.zeros((128, 128), pairs.dtype)
                pairs[row : row + 128, lane : lane + 128] = block


def join_x(wide, edge):
    place = lax.broadcasted_iota(jnp.int32, wide.shape[:2] + (128,), 1)
    after = jnp.where(place > 0, pltpu.roll(wide[:, :, :128], 1, 1), 0.0)
    before = jnp.where(place < edge - 1, pltpu.roll(wide[:, :, 256:], edge - 1, 1), 0.0)
    return wide[:, :, 128:256] + after + before


def convolve(grid, count, taps, pairs, put):
    edge = grid.shape[2]
    planes = min(count, 4)
    rows = planes * edge * edge
    place = lax.broadcasted_iota(jnp.int32, (planes * edge, edge, 128), 1)
    halved = grid.reshape(grid.shape[0], edge // 2 + 1, 2, edge, 128)
    for z in range(0, count, planes):
        left = jnp.concatenate(
            [
                grid[z + dz : z + dz + planes, dy : dy + edge].reshape(rows, 128)
                for dz in range(3)
                for dy in range(3)
            ],
            axis=1,
        )
        wide = jnp.dot(left, taps[:, 0:256], preferred_element_type=jnp.float32)
        wide = wide.reshape(planes * edge, edge, 256)
        left = jnp.concatenate(
            [
                halved[z + dz : z + dz + planes, line // 2 : line // 2 + edge // 2, line % 2].reshape(
                    rows // 2, 128
                )
                for dz in range(3)
                for line in range(4)
            ],
            axis=1,
        )
        two = jnp.dot(left, pairs[...], preferred_element_type=jnp.float32)
        two = two.reshape(planes * edge // 2, edge, 256)
        two = jnp.stack([two[:, :, :128], two[:, :, 128:]], axis=1).reshape(planes * edge, edge, 128)
        after = jnp.where(place > 0, pltpu.roll(wide[:, :, :128], 1, 1), 0.0)
        before = jnp.where(place < edge - 1, pltpu.roll(two, edge - 1, 1), 0.0)
        new = wide[:, :, 128:256] + after + before
        put(z, new.reshape(planes, edge, edge, 128))


def conv_kernel(deep_in, x, weight, act, taps, pairs, deep_weight, sem):
    copy = pltpu.make_async_copy(deep_in, deep_weight, sem)
    copy.start()
    edge = act.shape[0]
    spread_taps(weight, taps)
    pair_taps(weight, pairs)

    def put(z, new):
        act[z : z + new.shape[0]] = new

    convolve(x, edge, taps, pairs, put)
    copy.wait()


def y_terms(line, low, taps):
    planes, edge = line.shape[0] - 2, line.shape[1]
    left = jnp.concatenate(
        [line[dz : dz + planes].reshape(planes * edge, 128) for dz in range(3)], axis=1
    )
    start = jnp.where(low, 0, 256)
    right = jnp.concatenate(
        [taps[pl.ds(pl.multiple_of(start + dz * 384, 128), 128), :] for dz in range(3)], axis=0
    )
    wide = jnp.dot(left, right, preferred_element_type=jnp.float32)
    return join_x(wide.reshape(planes, edge, 384), edge)


def x_terms(column, taps):
    planes, edge = column.shape[0] - 2, column.shape[1] - 16
    lines = [column[:, 7 + dy : 7 + dy + edge].astype(jnp.bfloat16) for dy in range(3)]
    left = jnp.concatenate(
        [line[dz : dz + planes].reshape(planes * edge, 128) for dz in range(3) for line in lines],
        axis=1,
    )
    right = jnp.concatenate([taps[:, 0:128], taps[:, 256:384]], axis=1)
    both = jnp.dot(left, right, preferred_element_type=jnp.float32)
    return both[:, :128], both[:, 128:]


def fill_column(column, at, voxels, ends, above):
    count, edge = voxels.shape[:2]
    rows = edge + 16
    lines = column.reshape(column.shape[0] * rows, 128)
    column[at : at + count, 8 : 8 + edge] = voxels.astype(jnp.float32)
    for i, end in enumerate(ends):
        first = last = end.astype(jnp.float32)
        if len(ends) == 1:
            first, last = jnp.where(above[0], first, 0.0), jnp.where(above[0], 0.0, last)
        if len(ends) == 1 or i == 0:
            lines[pl.ds(at * rows + 7, count, stride=rows), :] = first
        if len(ends) == 1 or i == 1:
            lines[pl.ds(at * rows + 8 + edge, count, stride=rows), :] = last


def add_column(act, terms, j, nx, low):
    planes, edge = act.shape[:2]
    flat = act.reshape(planes * edge * edge, 128)
    first, last = terms
    if nx == 1:
        first, last = jnp.where(low, first, 0.0), jnp.where(low, 0.0, last)
    if nx == 1 or j == 0:
        flat[pl.ds(0, planes * edge, stride=edge), :] += first
    if nx == 1 or j == 1:
        flat[pl.ds(edge - 1, planes * edge, stride=edge), :] += last


def moments(planes):
    count, edge = planes.shape[:2]
    zero = jnp.zeros((8, 128), jnp.float32)

    def sum_step(k, carry):
        return carry + jnp.sum(planes[k].reshape(edge * 2, 8, 128), axis=0)

    mean = lax.fori_loop(0, count, sum_step, zero, unroll=True) / (count * edge * edge // 8)

    def spread_step(k, carry):
        off = planes[k].reshape(edge * 2, 8, 128) - mean
        return carry + jnp.sum(off * off, axis=0)

    return mean, lax.fori_loop(0, count, spread_step, zero, unroll=True)


def side_kernel(ny, nx, own, y_halos, x_halos, corners, taps, inner, ends, stats, act, column):
    edge = own.shape[0]
    act[0] = jnp.zeros(act.shape[1:], jnp.float32)
    act[edge + 1] = jnp.zeros(act.shape[1:], jnp.float32)
    act[1 : edge + 1] = own[...]
    above, left = Square().low_sides()
    blank = jnp.zeros((2, edge, 128), jnp.bfloat16)
    for i in range(ny):
        line = jnp.concatenate([blank, y_halos[i, 0:edge], blank], axis=0)
        act[:, jnp.where(above[i], 0, edge - 1)] += y_terms(line, above[i], taps)
    for j in range(nx):
        column[...] = jnp.zeros(column.shape, jnp.float32)
        fill_column(
            column, 2, x_halos[j, 0:edge], [corners[i * nx + j, 0] for i in range(ny)], above
        )
        add_column(act, x_terms(column, taps), j, nx, left[j])
    inner[...] = act[2:edge]
    ends[0:2] = act[0:2]
    ends[2:4] = act[edge : edge + 2]
    mean, spread = moments(act.at[2:edge])
    stats[0:8] = mean
    stats[8:16] = spread


def add_face(ny, nx, behind, face, x, taps, pairs, ends, three, grid, column, beyond=True):
    edge = x.shape[2]
    wide_face = edge + ny + nx
    f32 = jnp.float32
    above, left = Square().low_sides()
    end = pl.ds(jnp.where(behind, 3, 0), 3)
    three[...] = ends[end]
    blank = jnp.zeros(grid.shape[:1] + grid.shape[2:], grid.dtype)
    grid[:, 0] = blank
    grid[:, edge + 1] = blank
    first = jnp.where(behind, 1, 0)
    for k in range(3):
        grid[first + k, 1 : edge + 1] = face[k * wide_face : k * wide_face + edge]
    grid[jnp.where(behind, 0, 3), 1 : edge + 1] = x[jnp.where(behind, edge, 1), 1 : edge + 1]

    def put(z, new):
        three[pl.ds(first + z, new.shape[0])] += new

    if beyond:
        convolve(grid, 2, taps, pairs, put)
    beside = jnp.where(behind, 1, 2)
    lines = [grid[beside, dy : dy + edge].reshape(edge * edge, 128) for dy in range(3)]
    rows = taps[pl.ds(pl.multiple_of(jnp.where(behind, 768, 0), 128), 384), :]
    wide = jnp.dot(jnp.concatenate(lines, axis=1), rows, preferred_element_type=f32)
    three[jnp.where(behind, 0, 2)] += join_x(wide.reshape(edge, edge, 384), edge)

    def five(voxels):
        gap = jnp.zeros((2,) + voxels.shape[1:], voxels.dtype)
        return jnp.where(
            behind,
            jnp.concatenate([gap, voxels], axis=0),
            jnp.concatenate([voxels, gap], axis=0),
        )

    def rim(row):
        return five(jnp.stack([face[k * wide_face + edge + row] for k in range(3)]).astype(f32))

    for i in range(ny):
        terms = y_terms(rim(i).astype(jnp.bfloat16), above[i], taps)
        three[:, jnp.where(above[i], 0, edge - 1)] += terms
    for j in range(nx):
        column[...] = jnp.zeros(column.shape, f32)
        tails = []
        for i in range(ny):
            tile = face[3 * wide_face + i * nx + j].astype(f32)
            tails.append(five(jnp.where(behind, tile[:3], tile[edge - 3 :])))
        fill_column(column, 0, rim(ny + j), tails, above)
        add_column(three, x_terms(column, taps), j, nx, left[j])
    ends[end] = three[...]


def inner_kernel(ny, nx, x, partial, face, taps, pairs, ends, three, grid, column):
    blank = jnp.zeros(ends.shape[1:], jnp.float32)
    ends[0] = blank
    ends[1:5] = partial[...]
    ends[5] = blank
    behind = lax.axis_index("gz") % 2 == 0
    add_face(ny, nx, behind, face, x, taps, pairs, ends, three, grid, column)


def outer_kernel(ny, nx, x, middle_stats, ends, face, taps, pairs, act, stats, three, grid, column):
    edge = x.shape[2]
    act[...] = ends[...]
    behind = lax.axis_index("gz") % 2 == 1
    add_face(ny, nx, behind, face, x, taps, pairs, act, three, grid, column, beyond=False)
    mean, spread = moments(act.at[2:4])
    few, many = edge * edge // 4, (edge - 2) * edge * edge // 8
    middle_mean, middle_spread = middle_stats[0:8], middle_stats[8:16]
    off = middle_mean - mean
    part = few / (few + many)
    spread = spread + middle_spread + (many * part) * (off * off)
    put_stats(stats, middle_mean - part * off, spread, few + many)


def beyond_kernel(ny, nx, x, ends, face, taps, pairs, act, grid):
    edge = x.shape[2]
    wide_face = edge + ny + nx
    depth_at = lax.axis_index("gz")
    behind = depth_at % 2 == 1
    act[...] = ends[...]

    @pl.when(jnp.where(behind, depth_at < lax.axis_size("gz") - 1, depth_at > 0))
    def _():
        blank = jnp.zeros(grid.shape[:1] + grid.shape[2:], grid.dtype)
        grid[:, 0] = blank
        grid[:, edge + 1] = blank
        first = jnp.where(behind, 1, 0)
        for k in range(3):
            grid[first + k, 1 : edge + 1] = face[k * wide_face : k * wide_face + edge]
        own = jnp.where(behind, edge, 1)
        grid[jnp.where(behind, 0, 3), 1 : edge + 1] = x[own, 1 : edge + 1]

        def put(z, new):
            act[pl.ds(jnp.where(behind, 4, 0) + z, new.shape[0])] += new

        convolve(grid, 2, taps, pairs, put)


def merge(mean, spread, rows, other_mean, other_spread):
    off = mean - other_mean
    return 0.5 * (mean + other_mean), spread + other_spread + (0.5 * rows) * (off * off)


def put_stats(stats, mean, spread, rows):
    for step in (1, 2, 4):
        others = pltpu.roll(mean, step, 0), pltpu.roll(spread, step, 0)
        mean, spread = merge(mean, spread, float(rows * step), *others)
    both = jnp.concatenate([mean[0:1], spread[0:1]], axis=0)
    stats[...] = jnp.broadcast_to(both[None], stats.shape)


def read_stats(stats, rows):
    devices, _, channels = stats.shape
    shape = (8, channels)
    means = [jnp.broadcast_to(stats[k, 0:1, :], shape) for k in range(devices)]
    spreads = [jnp.broadcast_to(stats[k, 1:2, :], shape) for k in range(devices)]
    mean = functools.reduce(jnp.add, means) / devices
    spread = functools.reduce(jnp.add, spreads)
    spread = spread + rows * functools.reduce(jnp.add, [(m - mean) * (m - mean) for m in means])
    rows = rows * devices
    lane = lax.broadcasted_iota(jnp.int32, shape, 1)
    step = 1
    while step < channels // GROUPS:
        low = jnp.bitwise_and(lane, step) == 0
        others = [
            jnp.where(low, pltpu.roll(row, channels - step, 1), pltpu.roll(row, step, 1))
            for row in (mean, spread)
        ]
        mean, spread = merge(mean, spread, rows, *others)
        rows, step = 2.0 * rows, 2 * step
    return mean, lax.rsqrt(spread / rows + EPSILON)


def silu_of_double(h):
    return h + h * jnp.tanh(h)


def norm_kernel(ny, nx, inner, ends, stats, gain, offset, out, pooled, *refs):
    y_edges, x_edges, corners, half = refs
    depth, edge = inner.shape[0] + 6, inner.shape[1]
    deep, deep_depth = edge // 2, depth // 2
    f32, bf16 = jnp.float32, jnp.bfloat16
    above, left = Square().low_sides()
    depth_at = lax.axis_index("gz")
    mean, scale = read_stats(stats, float(edge**3))
    scale = scale * (0.5 * gain[...])
    shift = 0.5 * offset[...]
    for k in range(deep_depth):
        value = [
            ends[z] if z < 3 else inner[z - 3] if z < depth - 3 else ends[z - depth + 6]
            for z in (2 * k, 2 * k + 1)
        ]
        value = jnp.stack(value).reshape(edge * edge // 4, 8, 128)
        value = silu_of_double((value - mean) * scale + shift)
        value = value.reshape(2, edge, edge, 128).astype(bf16)
        if 0 < k < deep_depth - 1:
            out[2 * k - 2 : 2 * k] = value
        value = value.astype(f32)
        value = (value[0] + value[1]).reshape(deep, 2, edge, 128)
        half[k] = (value[:, 0] + value[:, 1]).reshape(deep * edge, 128)
        lines = half.at[k]
        pair = lines[pl.ds(0, deep * deep, stride=2), :] + lines[pl.ds(1, deep * deep, stride=2), :]
        pair = (pair * 0.125).astype(bf16).astype(f32).reshape(deep, deep, 128)
        if k == 0 or k == deep_depth - 1:
            inside = depth_at > 0 if k == 0 else depth_at < lax.axis_size("gz") - 1
            pair = jnp.where(inside, pair, 0.0)
        pooled[k] = pair
    lines = pooled.reshape(deep_depth * deep * deep, 128)
    rows = deep_depth * deep
    first_x = lines[pl.ds(0, rows, stride=deep), :]
    last_x = lines[pl.ds(deep - 1, rows, stride=deep), :]
    first_y, last_y = (pooled[:, y].reshape(rows, 128) for y in (0, deep - 1))
    ends = []
    for y in (0, deep - 1):
        for x in (0, deep - 1):
            ends.append(lines[pl.ds(y * deep + x, deep_depth, stride=deep * deep), :])
    if ny == 1:
        above, left = above[0], left[0]
        y_edges[0] = jnp.where(above, first_y, last_y).astype(bf16)
        x_edges[0] = jnp.where(left, first_x, last_x).astype(bf16)
        corners[0, 0:deep_depth] = jnp.where(
            above, jnp.where(left, ends[0], ends[1]), jnp.where(left, ends[2], ends[3])
        )
    else:
        y_edges[0], y_edges[1] = first_y.astype(bf16), last_y.astype(bf16)
        x_edges[0], x_edges[1] = first_x.astype(bf16), last_x.astype(bf16)
        for k in range(4):
            corners[k, 0:deep_depth] = ends[k]


def stack_kernel(*refs):
    out = refs[-1]
    for k in range(out.shape[0]):
        out[k] = refs[k][: out.shape[1], : out.shape[2]]


def stack(*arrays, part=None):
    vmem = pl.BlockSpec(memory_space=pltpu.VMEM)
    shape = (part or arrays[0].shape[:2]) + arrays[0].shape[2:]
    return pl.pallas_call(
        stack_kernel,
        out_shape=jax.ShapeDtypeStruct((len(arrays),) + shape, arrays[0].dtype),
        in_specs=[vmem] * len(arrays),
        out_specs=vmem,
        compiler_params=pltpu.CompilerParams(vmem_limit_bytes=VMEM_BYTES),
    )(*arrays)


def place_weights(own, held, out):
    tile = lax.axis_index("yx")
    out[tile] = own[...]
    if len(held) == 1:
        pieces, others, size = held[0].shape[:3]
        for piece in range(pieces):
            at = jnp.minimum(jnp.bitwise_xor(Riders.mine(), piece) * size, own.shape[0] - size)
            for k in range(others):
                out[jnp.bitwise_xor(tile, k + 1), pl.ds(at, size)] = held[0][piece, k]
    else:
        for k, shard in enumerate(held):
            out[lax.rem(tile + len(held) - k, len(held) + 1)] = shard[...]


def tap_rows(weight, taps):
    per = weight.shape[1] // 27
    return jnp.concatenate(
        [weight[:, pl.ds(tap * per, per)].reshape(-1, 128) for tap in taps], axis=1
    )


def dot_rows(left, right):
    return lax.dot_general(
        left, right, (((1,), (1,)), ((), ())), preferred_element_type=jnp.float32
    )


def deep_kernel(pooled, own, *refs):
    *held, act, weight, grid, packed = refs
    depth, deep = pooled.shape[0], pooled.shape[1]
    place_weights(own, held, weight)
    grid[...] = jnp.zeros(grid.shape, jnp.float32)
    grid[:, 1 : deep + 1, 8:16] = pooled[...]
    for dx in range(3):
        plane = grid[:, :, 7 + dx : 15 + dx]
        for y in range(deep + 1):
            both = jnp.concatenate([plane[:, y], plane[:, y + 1]], axis=1)
            packed[:, y // 2, y % 2, :, dx * 128 : dx * 128 + 128] = both.astype(jnp.bfloat16)
    rows = deep**3
    total = None
    for dz in range(3):
        left = jnp.concatenate(
            [
                packed[dz : dz + deep, dy // 2 : dy // 2 + deep // 2, dy % 2].reshape(rows, 384)
                for dy in range(3)
            ],
            axis=1,
        )
        term = dot_rows(left, tap_rows(weight, range(dz * 9, dz * 9 + 9)))
        total = term if total is None else total + term
    for half in range(act.shape[0]):
        act[half] = total[:, half * 128 : half * 128 + 128]


def deep_rim_kernel(ny, nx, own, y_halos, x_halos, corners, weight, act, stats, line):
    depth, deep = line.shape[0], line.shape[1] - 16
    halves = act.shape[0]
    f32 = jnp.float32
    square = deep * deep
    above, left = Square().low_sides()
    act[...] = own[...]
    flat = line.reshape(depth * line.shape[1], 128)

    def shifts():
        return jnp.concatenate(
            [
                line[dz : dz + deep, 7 + d : 7 + d + deep].reshape(square, 128).astype(jnp.bfloat16)
                for dz in range(3)
                for d in range(3)
            ],
            axis=1,
        )

    for i in range(ny):
        line[...] = jnp.zeros(line.shape, f32)
        line[:, 8 : 8 + deep] = y_halos[i].astype(f32).reshape(depth, deep, 128)
        for j in range(nx):
            end = corners[i * nx + j, 0:depth]
            first, last = jnp.where(left[j], end, 0.0), jnp.where(left[j], 0.0, end)
            if nx == 1 or j == 0:
                flat[pl.ds(7, depth, stride=line.shape[1]), :] = first
            if nx == 1 or j == 1:
                flat[pl.ds(8 + deep, depth, stride=line.shape[1]), :] = last
        tap = jnp.where(above[i], 0, 6)
        taps = [tap + dz * 9 + dx for dz in range(3) for dx in range(3)]
        terms = dot_rows(shifts(), tap_rows(weight, taps))
        for half in range(halves):
            rows = act.at[half].reshape(deep, deep, deep, 128)
            term = terms[:, half * 128 : half * 128 + 128].reshape(deep, deep, 128)
            rows[:, jnp.where(above[i], 0, deep - 1)] += term
    for j in range(nx):
        line[...] = jnp.zeros(line.shape, f32)
        line[:, 8 : 8 + deep] = x_halos[j].astype(f32).reshape(depth, deep, 128)
        tap = jnp.where(left[j], 0, 2)
        taps = [tap + dz * 9 + dy * 3 for dz in range(3) for dy in range(3)]
        terms = dot_rows(shifts(), tap_rows(weight, taps))
        first, last = jnp.where(left[j], terms, 0.0), jnp.where(left[j], 0.0, terms)
        for half in range(halves):
            lanes, rows = slice(half * 128, half * 128 + 128), act.at[half]
            if nx == 1 or j == 0:
                rows[pl.ds(0, square, stride=deep), :] += first[:, lanes]
            if nx == 1 or j == 1:
                rows[pl.ds(deep - 1, square, stride=deep), :] += last[:, lanes]

    rows = deep**3 // 8
    means, spreads = [], []
    for half in range(halves):
        total = act[half].reshape(rows, 8, 128)
        means.append(jnp.sum(total, axis=0) / rows)
        off = total - means[-1]
        spreads.append(jnp.sum(off * off, axis=0))
    put_stats(stats, *(jnp.concatenate(part, axis=1) for part in (means, spreads)), rows)


def final_kernel(act, stats, gain, offset, up, mid, out, wide, held, sems):
    edge = mid.shape[0]
    deep = edge // 2
    f32 = jnp.float32
    mean, scale = read_stats(stats, float(deep**3))
    scale = scale * (0.5 * gain[...])
    shift = 0.5 * offset[...]
    planes = 2
    size = planes * deep * deep
    copies = []
    for k in range(0, deep, planes):
        at = slice(k * deep * deep, k * deep * deep + size)
        value = jnp.concatenate([act[half, at] for half in range(act.shape[0])], axis=1)
        value = value.reshape(size // 8, 8, -1)
        value = silu_of_double((value - mean) * scale + shift)
        value = value.reshape(size, -1).astype(jnp.bfloat16)
        lifted = jnp.dot(value, up[...], preferred_element_type=f32)
        lines = wide.at[k // planes]
        lines[pl.ds(0, size, stride=2), :] = lifted
        lines[pl.ds(1, size, stride=2), :] = lifted
        add = lines[...].reshape(planes, 1, deep, 1, edge, 128)
        at = pl.ds(2 * k, 2 * planes)
        old = mid[at].astype(f32).reshape(planes, 2, deep, 2, edge, 128)
        held[at] = (old + add).astype(jnp.bfloat16).reshape(2 * planes, edge, edge, 128)
        copy = pltpu.make_async_copy(held.at[at], out.at[at], sems.at[k // planes])
        copy.start()
        copies.append(copy)
    for copy in copies:
        copy.wait()


def body(
    features, conv_weight, gain_mid, offset_mid, deep_weight, gain_deep, offset_deep, up_weight
):
    f32, bf16 = jnp.float32, jnp.bfloat16
    edge, channels = features.shape[0], features.shape[3]
    deep = edge // 2
    deep_channels = gain_deep.shape[0]
    square = Square()
    tiles = square.tiles
    devices = lax.axis_size("gz") * tiles
    ny, nx = (len(sides) for sides in square.low_sides())
    riders = Riders(deep_weight.shape[4])

    own = jnp.moveaxis(deep_weight, 4, 3).reshape(-1, 16, channels)
    conv_weight = conv_weight.reshape(27, channels, channels)
    *edges, field, conv_weight = call(
        functools.partial(start_kernel, ny, nx, riders.size),
        [
            ((ny, edge + riders.size, edge, channels), bf16),
            ((nx, edge + riders.size, edge, channels), bf16),
            ((ny * nx, 1 + riders.size, edge, channels), bf16),
            ((edge + 2, edge + 2, edge, channels), bf16),
            (conv_weight.shape, bf16),
        ],
        [((nx, edge * edge, 8, channels), f32), pltpu.SemaphoreType.DMA((8,))],
        features,
        conv_weight,
        own,
        nbytes=5 << 20,
        in_hbm=3,
    )
    halos = square.halos(*(list(piece) for piece in edges))
    conv_flops = 54 * channels * channels * edge**3
    act, taps, pairs, own = call(
        conv_kernel,
        [
            ((edge, edge, edge, channels), f32),
            ((9 * channels, 3 * channels), bf16),
            ((12 * channels, 2 * channels), bf16),
            (own.shape, bf16),
        ],
        [pltpu.SemaphoreType.DMA],
        own,
        field,
        conv_weight,
        flops=conv_flops,
        nbytes=6 << 20,
        in_hbm=1,
    )
    (y, x, corner), act = lax.optimization_barrier((halos, act))
    y, x, corner = jnp.stack(y), jnp.stack(x), jnp.stack(corner)
    face = ((3 * (edge + ny + nx) + ny * nx, edge, channels), bf16)
    held = [((4, riders.size, 16, channels), bf16)] if riders.size else []
    outer, inner, *held = call(
        functools.partial(face_kernel, ny, nx, riders.size),
        [((face[0][0] + 2,) + face[0][1:], bf16), face] + held,
        [],
        field,
        y,
        x,
        corner,
    )
    outer, inner = swap_depth(outer, inner)
    if riders.size:
        held = held[0][None]
        other = swap(held, *riders.STEPS[0])
    else:
        held = rotate_shards(own)
    six = ((6, edge, edge, channels), f32)
    column = (edge + 16, channels)
    middle, partial, stats = call(
        functools.partial(side_kernel, ny, nx),
        [
            ((edge - 2, edge, edge, channels), f32),
            ((4, edge, edge, channels), f32),
            ((16, channels), f32),
        ],
        [((edge + 2, edge, edge, channels), f32), ((edge + 4,) + column, f32)],
        act,
        y,
        x,
        corner,
        taps,
    )
    room = [
        ((3, edge, edge, channels), f32),
        ((4, edge + 2, edge, channels), bf16),
        ((5,) + column, f32),
    ]
    (ends,) = call(
        functools.partial(inner_kernel, ny, nx), [six], room, field, partial, inner, taps, pairs
    )
    ends, stats = call(
        functools.partial(outer_kernel, ny, nx),
        [six, ((devices, 2, channels), f32)],
        room,
        field,
        stats,
        ends,
        outer,
        taps,
        pairs,
    )
    if riders.size:
        stats, other = lax.optimization_barrier((stats, other))
        held = stack(held, other, part=(1, 3)).reshape((2, 3) + held.shape[2:])
        other = swap(held, *riders.STEPS[1])
    (ends,) = call(
        functools.partial(beyond_kernel, ny, nx),
        [six],
        room[1:2],
        field,
        ends,
        outer,
        taps,
        pairs,
        flops=conv_flops,
        nbytes=4 << 20,
    )
    stats, ends = lax.optimization_barrier((stats, ends))
    stats = share(stats)
    if riders.size:
        stats, other = lax.optimization_barrier((stats, other))
        held = stack(held, other).reshape((-1,) + held.shape[1:])
        other = swap(held, *riders.STEPS[2])
        held = [stack(held, other).reshape((-1,) + held.shape[1:])]
    out, pooled, *edges = call(
        functools.partial(norm_kernel, ny, nx),
        [
            ((edge, edge, edge, channels), bf16),
            ((deep + 2, deep, deep, channels), f32),
            ((ny, (deep + 2) * deep, channels), bf16),
            ((nx, (deep + 2) * deep, channels), bf16),
            ((ny * nx, 16, channels), f32),
        ],
        [((deep + 2, deep * edge, channels), f32)],
        middle,
        ends,
        stats,
        gain_mid.reshape(1, channels),
        offset_mid.reshape(1, channels),
        flops=20 * channels * edge**3,
        nbytes=3 << 20,
    )
    y, x, corner = square.halos(*(list(piece) for piece in edges))
    halves = ((deep_channels // 128, deep**3, 128), f32)
    deep_act, weight = call(
        deep_kernel,
        [halves, ((tiles,) + own.shape, bf16)],
        [
            ((deep + 2, deep + 2, 24, channels), f32),
            ((deep + 2, deep // 2 + 1, 2, 16, 3 * channels), bf16),
        ],
        pooled,
        own,
        *held,
        flops=54 * channels * deep_channels * deep**3,
        nbytes=4 << 20,
    )
    deep_act, stats = call(
        functools.partial(deep_rim_kernel, ny, nx),
        [halves, ((devices, 2, deep_channels), f32)],
        [((deep + 2, 24, channels), f32)],
        deep_act,
        jnp.stack(y),
        jnp.stack(x),
        jnp.stack(corner),
        weight,
        flops=4 * channels * deep_channels * deep**3,
        nbytes=3 << 20,
    )
    stats = share(stats)
    (decoded,) = call(
        final_kernel,
        [((edge, edge, edge, channels), bf16)],
        [
            ((deep // 2, 4 * deep * deep, channels), f32),
            ((edge, edge, edge, channels), bf16),
            pltpu.SemaphoreType.DMA((deep // 2,)),
        ],
        deep_act,
        stats,
        gain_deep.reshape(1, deep_channels),
        offset_deep.reshape(1, deep_channels),
        up_weight,
        out,
        flops=4 * deep_channels * channels * deep**3,
        nbytes=3 << 20,
        out_hbm=True,
    )
    return decoded


def solution(mesh):
    placed = (
        P(("cand", "gz"), "yx", None, None),
        P(),
        P(),
        P(),
        P(None, None, None, None, "yx"),
        P(),
        P(),
        P(),
    )
    return jax.shard_map(
        body,
        mesh=mesh,
        in_specs=placed,
        out_specs=P(("cand", "gz"), "yx", None, None),
        check_vma=False,
    )
```

```python
import functools
import math

import jax
import jax.numpy as jnp
from jax import lax
from jax.experimental import pallas as pl
from jax.experimental.pallas import tpu as pltpu
from jax.sharding import PartitionSpec as P

GROUPS = 32
EPSILON = 1e-05
PART = ("gz", "yx")
VMEM_BYTES = 32 * 1024 * 1024


class Square:
    def __init__(self):
        self.tiles = lax.axis_size("yx")
        self.side = math.isqrt(self.tiles)
        tile = lax.axis_index("yx")
        self.row, self.column = tile // self.side, tile % self.side
        self.folded = self.side == 2
        self.steps = (0,) if self.folded else (-1, 1)

    def low_sides(self):
        if self.folded:
            return [self.row == 1], [self.column == 1]
        return [True, False], [True, False]

    def route(self, down, right):
        pairs = []
        for tile in range(self.tiles):
            row, column = tile // self.side + down, tile % self.side + right
            if 0 <= row < self.side and 0 <= column < self.side:
                pairs.append((tile, row * self.side + column))
        return pairs

    def swap_route(self, mask):
        return [(tile, tile ^ mask) for tile in range(self.tiles)]

    def halos(self, y_edges, x_edges, corners):
        if self.folded:
            y = lax.ppermute(y_edges[0], "yx", self.swap_route(2))
            x = lax.ppermute(x_edges[0], "yx", self.swap_route(1))
            corner = lax.ppermute(corners[0], "yx", self.swap_route(3))
            return [y], [x], [corner]
        y = [lax.ppermute(y_edges[k], "yx", self.route((1, -1)[1 - k], 0)) for k in (1, 0)]
        x = [lax.ppermute(x_edges[k], "yx", self.route(0, (1, -1)[1 - k])) for k in (1, 0)]
        corner = [
            lax.ppermute(corners[2 * k + j], "yx", self.route((1, -1)[1 - k], (1, -1)[1 - j]))
            for k in (1, 0)
            for j in (1, 0)
        ]
        return y, x, corner


def swap_depth(outer, inner):
    size = lax.axis_size("gz")
    routes = [[], []]
    for low in range(size - 1):
        routes[low % 2] += [(low, low + 1), (low + 1, low)]
    return lax.ppermute(outer, "gz", routes[1]), lax.ppermute(inner, "gz", routes[0])


class Riders:
    STEPS = (("cand", 1), ("gz", 2), ("gz", 1))

    def __init__(self, rows):
        self.tiles = 27 * rows // 16
        self.fits = (
            lax.axis_size("yx") == 4
            and lax.axis_size("cand") % 2 == 0
            and lax.axis_size("gz") % 4 == 0
            and self.tiles >= 8
        )
        self.size = -(-self.tiles // 8) if self.fits else 0

    @classmethod
    def mine(cls):
        return sum(
            lax.axis_index(axis) // mask % 2 * 2**k for k, (axis, mask) in enumerate(cls.STEPS)
        )


def rotate_shards(piece):
    tiles = lax.axis_size("yx")
    return [
        lax.ppermute(piece, "yx", [(i, (i + k) % tiles) for i in range(tiles)]) for k in range(1, tiles)
    ]


def swap(block, axis, mask):
    return lax.ppermute(block, axis, [(i, i ^ mask) for i in range(lax.axis_size(axis))])


def share(stats):
    return lax.all_to_all(stats, PART, 0, 0)


def call(kernel, outs, scratch, *arrays, flops=0, nbytes=0, in_hbm=0, out_hbm=False):
    vmem, hbm = (pl.BlockSpec(memory_space=space) for space in (pltpu.VMEM, pltpu.HBM))
    far, near = arrays[:in_hbm], arrays[in_hbm:]
    far = [pltpu.with_memory_space_constraint(array, pltpu.HBM) for array in far]
    return pl.pallas_call(
        kernel,
        out_shape=[jax.ShapeDtypeStruct(shape, dtype) for shape, dtype in outs],
        in_specs=[hbm] * len(far) + [vmem] * len(near),
        out_specs=[hbm if out_hbm else vmem] * len(outs),
        scratch_shapes=[pltpu.VMEM(*entry) if isinstance(entry, tuple) else entry for entry in scratch],
        compiler_params=pltpu.CompilerParams(vmem_limit_bytes=VMEM_BYTES),
        cost_estimate=pl.CostEstimate(flops=flops, bytes_accessed=nbytes, transcendentals=0),
    )(*far, *near)


def start_kernel(ny, nx, size, x_in, w_in, d_in, y_out, x_out, corners, x, w, lines, sems):
    edge = x_in.shape[0]
    f32, bf16 = jnp.float32, jnp.bfloat16
    above, left = Square().low_sides()
    chunks = 4
    planes = edge // chunks
    first = [
        pltpu.make_async_copy(
            x_in.at[pl.ds(k * planes, planes)],
            x.at[pl.ds(1 + k * planes, planes), pl.ds(1, edge)],
            sems.at[k],
        )
        for k in range(chunks)
    ]
    later = []
    if size:
        at = jnp.minimum(Riders.mine() * size, d_in.shape[0] - size)
        for k, (out, begin) in enumerate(((y_out, edge), (x_out, edge), (corners, 1))):
            later.append(
                pltpu.make_async_copy(
                    d_in.at[pl.ds(at, size)], out.at[0, pl.ds(begin, size)], sems.at[chunks + k]
                )
            )
    later.append(pltpu.make_async_copy(w_in, w, sems.at[chunks + 3]))
    for k, copy in enumerate(first + later):
        copy.start(priority=k % 2)
    x[0] = jnp.zeros(x.shape[1:], bf16)
    x[edge + 1] = jnp.zeros(x.shape[1:], bf16)
    blank = jnp.zeros((edge,) + x.shape[2:], bf16)
    x[1 : edge + 1, 0] = blank
    x[1 : edge + 1, edge + 1] = blank
    flat = lines.reshape(nx * edge * edge * 8, 128)
    part = planes * edge
    for k in range(chunks):
        first[k].wait()
        at, here = pl.ds(k * planes, planes), pl.ds(1 + k * planes, planes)
        for i in range(ny):
            row = jnp.where(above[i], 1, edge)
            y_out[i, at] = x[here, row]
        for j in range(nx):
            low = x[here, 1 : edge + 1, 0:8].astype(f32).reshape(part, 8, 128)
            high = x[here, 1 : edge + 1, edge - 8 : edge].astype(f32).reshape(part, 8, 128)
            high = pltpu.roll(high, 1, 1)
            kept = jnp.where(left[j], low, high)
            lines[j, k * part : k * part + part] = kept
            begin = (j * edge * edge + k * part) * 8
            column = flat[pl.ds(begin, part, stride=8), :]
            x_out[j, at] = column.astype(bf16).reshape(planes, edge, 128)
    for i in range(ny):
        for j in range(nx):
            begin = j * edge * edge * 8
            low = flat[pl.ds(begin, edge, stride=8 * edge), :]
            high = flat[pl.ds(begin + 8 * (edge - 1), edge, stride=8 * edge), :]
            kept = jnp.where(above[i], low, high)
            corners[i * nx + j, 0] = kept.astype(bf16)
    for copy in later:
        copy.wait()


def face_kernel(ny, nx, size, x, y_halos, x_halos, corners, outer, inner, *riders):
    edge = outer.shape[1]
    wide = edge + ny + nx
    odd = lax.axis_index("gz") % 2
    far = edge - 3
    for face, at in ((outer, odd * far), (inner, (1 - odd) * far)):
        for k in range(3):
            row = k * wide
            face[row : row + edge] = x[1 + at + k, 1 : edge + 1]
            for i in range(ny):
                face[row + edge + i] = y_halos[i, at + k]
            for j in range(nx):
                face[row + edge + ny + j] = x_halos[j, at + k]
        for k in range(ny * nx):
            face[3 * wide + k] = corners[k, 0]
    for k in range(inner.shape[0], outer.shape[0]):
        outer[k] = corners[0, 0]
    if size:
        riders[0][0] = x_halos[0, edge : edge + size]
        riders[0][1] = y_halos[0, edge : edge + size]
        riders[0][2] = corners[0, 1 : 1 + size]
        riders[0][3] = corners[0, 1 : 1 + size]


def spread_taps(weight, taps):
    for tap in range(27):
        row, lane = tap // 3 * 128, tap % 3 * 128
        taps[row : row + 128, lane : lane + 128] = weight[tap]


def pair_taps(weight, pairs):
    for dz in range(3):
        for line in range(4):
            row = (dz * 4 + line) * 128
            for out in range(2):
                lane = out * 128
                if 0 <= line - out < 3:
                    block = weight[dz * 9 + (line - out) * 3 + 2]
                else:
                    block = jnp.zeros((128, 128), pairs.dtype)
                pairs[row : row + 128, lane : lane + 128] = block


def join_x(wide, edge):
    place = lax.broadcasted_iota(jnp.int32, wide.shape[:2] + (128,), 1)
    after = jnp.where(place > 0, pltpu.roll(wide[:, :, :128], 1, 1), 0.0)
    before = jnp.where(place < edge - 1, pltpu.roll(wide[:, :, 256:], edge - 1, 1), 0.0)
    return wide[:, :, 128:256] + after + before


def convolve(grid, count, taps, pairs, put):
    edge = grid.shape[2]
    planes = min(count, 4)
    rows = planes * edge * edge
    place = lax.broadcasted_iota(jnp.int32, (planes * edge, edge, 128), 1)
    halved = grid.reshape(grid.shape[0], edge // 2 + 1, 2, edge, 128)
    for z in range(0, count, planes):
        left = jnp.concatenate(
            [
                grid[z + dz : z + dz + planes, dy : dy + edge].reshape(rows, 128)
                for dz in range(3)
                for dy in range(3)
            ],
            axis=1,
        )
        wide = jnp.dot(left, taps[:, 0:256], preferred_element_type=jnp.float32)
        wide = wide.reshape(planes * edge, edge, 256)
        left = jnp.concatenate(
            [
                halved[z + dz : z + dz + planes, line // 2 : line // 2 + edge // 2, line % 2].reshape(
                    rows // 2, 128
                )
                for dz in range(3)
                for line in range(4)
            ],
            axis=1,
        )
        two = jnp.dot(left, pairs[...], preferred_element_type=jnp.float32)
        two = two.reshape(planes * edge // 2, edge, 256)
        two = jnp.stack([two[:, :, :128], two[:, :, 128:]], axis=1).reshape(planes * edge, edge, 128)
        after = jnp.where(place > 0, pltpu.roll(wide[:, :, :128], 1, 1), 0.0)
        before = jnp.where(place < edge - 1, pltpu.roll(two, edge - 1, 1), 0.0)
        new = wide[:, :, 128:256] + after + before
        put(z, new.reshape(planes, edge, edge, 128))


def conv_kernel(deep_in, x, weight, act, taps, pairs, deep_weight, sem):
    copy = pltpu.make_async_copy(deep_in, deep_weight, sem)
    copy.start()
    edge = act.shape[0]
    spread_taps(weight, taps)
    pair_taps(weight, pairs)

    def put(z, new):
        act[z : z + new.shape[0]] = new

    convolve(x, edge, taps, pairs, put)
    copy.wait()


def y_terms(line, low, taps):
    planes, edge = line.shape[0] - 2, line.shape[1]
    left = jnp.concatenate(
        [line[dz : dz + planes].reshape(planes * edge, 128) for dz in range(3)], axis=1
    )
    start = jnp.where(low, 0, 256)
    right = jnp.concatenate(
        [taps[pl.ds(pl.multiple_of(start + dz * 384, 128), 128), :] for dz in range(3)], axis=0
    )
    wide = jnp.dot(left, right, preferred_element_type=jnp.float32)
    return join_x(wide.reshape(planes, edge, 384), edge)


def x_terms(column, taps):
    planes, edge = column.shape[0] - 2, column.shape[1] - 16
    lines = [column[:, 7 + dy : 7 + dy + edge].astype(jnp.bfloat16) for dy in range(3)]
    left = jnp.concatenate(
        [line[dz : dz + planes].reshape(planes * edge, 128) for dz in range(3) for line in lines],
        axis=1,
    )
    right = jnp.concatenate([taps[:, 0:128], taps[:, 256:384]], axis=1)
    both = jnp.dot(left, right, preferred_element_type=jnp.float32)
    return both[:, :128], both[:, 128:]


def fill_column(column, at, voxels, ends, above):
    count, edge = voxels.shape[:2]
    rows = edge + 16
    lines = column.reshape(column.shape[0] * rows, 128)
    column[at : at + count, 8 : 8 + edge] = voxels.astype(jnp.float32)
    for i, end in enumerate(ends):
        first = last = end.astype(jnp.float32)
        if len(ends) == 1:
            first, last = jnp.where(above[0], first, 0.0), jnp.where(above[0], 0.0, last)
        if len(ends) == 1 or i == 0:
            lines[pl.ds(at * rows + 7, count, stride=rows), :] = first
        if len(ends) == 1 or i == 1:
            lines[pl.ds(at * rows + 8 + edge, count, stride=rows), :] = last


def add_column(act, terms, j, nx, low):
    planes, edge = act.shape[:2]
    flat = act.reshape(planes * edge * edge, 128)
    first, last = terms
    if nx == 1:
        first, last = jnp.where(low, first, 0.0), jnp.where(low, 0.0, last)
    if nx == 1 or j == 0:
        flat[pl.ds(0, planes * edge, stride=edge), :] += first
    if nx == 1 or j == 1:
        flat[pl.ds(edge - 1, planes * edge, stride=edge), :] += last


def moments(planes):
    count, edge = planes.shape[:2]
    zero = jnp.zeros((8, 128), jnp.float32)

    def sum_step(k, carry):
        return carry + jnp.sum(planes[k].reshape(edge * 2, 8, 128), axis=0)

    mean = lax.fori_loop(0, count, sum_step, zero, unroll=True) / (count * edge * edge // 8)

    def spread_step(k, carry):
        off = planes[k].reshape(edge * 2, 8, 128) - mean
        return carry + jnp.sum(off * off, axis=0)

    return mean, lax.fori_loop(0, count, spread_step, zero, unroll=True)


def side_kernel(ny, nx, own, y_halos, x_halos, corners, taps, inner, ends, stats, act, column):
    edge = own.shape[0]
    act[0] = jnp.zeros(act.shape[1:], jnp.float32)
    act[edge + 1] = jnp.zeros(act.shape[1:], jnp.float32)
    act[1 : edge + 1] = own[...]
    above, left = Square().low_sides()
    blank = jnp.zeros((2, edge, 128), jnp.bfloat16)
    for i in range(ny):
        line = jnp.concatenate([blank, y_halos[i, 0:edge], blank], axis=0)
        act[:, jnp.where(above[i], 0, edge - 1)] += y_terms(line, above[i], taps)
    for j in range(nx):
        column[...] = jnp.zeros(column.shape, jnp.float32)
        fill_column(
            column, 2, x_halos[j, 0:edge], [corners[i * nx + j, 0] for i in range(ny)], above
        )
        add_column(act, x_terms(column, taps), j, nx, left[j])
    inner[...] = act[2:edge]
    ends[0:2] = act[0:2]
    ends[2:4] = act[edge : edge + 2]
    mean, spread = moments(act.at[2:edge])
    stats[0:8] = mean
    stats[8:16] = spread


def add_face(ny, nx, behind, face, x, taps, pairs, ends, three, grid, column, beyond=True):
    edge = x.shape[2]
    wide_face = edge + ny + nx
    f32 = jnp.float32
    above, left = Square().low_sides()
    end = pl.ds(jnp.where(behind, 3, 0), 3)
    three[...] = ends[end]
    blank = jnp.zeros(grid.shape[:1] + grid.shape[2:], grid.dtype)
    grid[:, 0] = blank
    grid[:, edge + 1] = blank
    first = jnp.where(behind, 1, 0)
    for k in range(3):
        grid[first + k, 1 : edge + 1] = face[k * wide_face : k * wide_face + edge]
    grid[jnp.where(behind, 0, 3), 1 : edge + 1] = x[jnp.where(behind, edge, 1), 1 : edge + 1]

    def put(z, new):
        three[pl.ds(first + z, new.shape[0])] += new

    if beyond:
        convolve(grid, 2, taps, pairs, put)
    beside = jnp.where(behind, 1, 2)
    lines = [grid[beside, dy : dy + edge].reshape(edge * edge, 128) for dy in range(3)]
    rows = taps[pl.ds(pl.multiple_of(jnp.where(behind, 768, 0), 128), 384), :]
    wide = jnp.dot(jnp.concatenate(lines, axis=1), rows, preferred_element_type=f32)
    three[jnp.where(behind, 0, 2)] += join_x(wide.reshape(edge, edge, 384), edge)

    def five(voxels):
        gap = jnp.zeros((2,) + voxels.shape[1:], voxels.dtype)
        return jnp.where(
            behind,
            jnp.concatenate([gap, voxels], axis=0),
            jnp.concatenate([voxels, gap], axis=0),
        )

    def rim(row):
        return five(jnp.stack([face[k * wide_face + edge + row] for k in range(3)]).astype(f32))

    for i in range(ny):
        terms = y_terms(rim(i).astype(jnp.bfloat16), above[i], taps)
        three[:, jnp.where(above[i], 0, edge - 1)] += terms
    for j in range(nx):
        column[...] = jnp.zeros(column.shape, f32)
        tails = []
        for i in range(ny):
            tile = face[3 * wide_face + i * nx + j].astype(f32)
            tails.append(five(jnp.where(behind, tile[:3], tile[edge - 3 :])))
        fill_column(column, 0, rim(ny + j), tails, above)
        add_column(three, x_terms(column, taps), j, nx, left[j])
    ends[end] = three[...]


def inner_kernel(ny, nx, x, partial, face, taps, pairs, ends, three, grid, column):
    blank = jnp.zeros(ends.shape[1:], jnp.float32)
    ends[0] = blank
    ends[1:5] = partial[...]
    ends[5] = blank
    behind = lax.axis_index("gz") % 2 == 0
    add_face(ny, nx, behind, face, x, taps, pairs, ends, three, grid, column)


def outer_kernel(ny, nx, x, middle_stats, ends, face, taps, pairs, act, stats, three, grid, column):
    edge = x.shape[2]
    act[...] = ends[...]
    behind = lax.axis_index("gz") % 2 == 1
    add_face(ny, nx, behind, face, x, taps, pairs, act, three, grid, column, beyond=False)
    mean, spread = moments(act.at[2:4])
    few, many = edge * edge // 4, (edge - 2) * edge * edge // 8
    middle_mean, middle_spread = middle_stats[0:8], middle_stats[8:16]
    off = middle_mean - mean
    part = few / (few + many)
    spread = spread + middle_spread + (many * part) * (off * off)
    put_stats(stats, middle_mean - part * off, spread, few + many)


def beyond_kernel(ny, nx, x, ends, face, taps, pairs, act, grid):
    edge = x.shape[2]
    wide_face = edge + ny + nx
    depth_at = lax.axis_index("gz")
    behind = depth_at % 2 == 1
    act[...] = ends[...]

    @pl.when(jnp.where(behind, depth_at < lax.axis_size("gz") - 1, depth_at > 0))
    def _():
        blank = jnp.zeros(grid.shape[:1] + grid.shape[2:], grid.dtype)
        grid[:, 0] = blank
        grid[:, edge + 1] = blank
        first = jnp.where(behind, 1, 0)
        for k in range(3):
            grid[first + k, 1 : edge + 1] = face[k * wide_face : k * wide_face + edge]
        own = jnp.where(behind, edge, 1)
        grid[jnp.where(behind, 0, 3), 1 : edge + 1] = x[own, 1 : edge + 1]

        def put(z, new):
            act[pl.ds(jnp.where(behind, 4, 0) + z, new.shape[0])] += new

        convolve(grid, 2, taps, pairs, put)


def merge(mean, spread, rows, other_mean, other_spread):
    off = mean - other_mean
    return 0.5 * (mean + other_mean), spread + other_spread + (0.5 * rows) * (off * off)


def put_stats(stats, mean, spread, rows):
    for step in (1, 2, 4):
        others = pltpu.roll(mean, step, 0), pltpu.roll(spread, step, 0)
        mean, spread = merge(mean, spread, float(rows * step), *others)
    both = jnp.concatenate([mean[0:1], spread[0:1]], axis=0)
    stats[...] = jnp.broadcast_to(both[None], stats.shape)


def read_stats(stats, rows):
    devices, _, channels = stats.shape
    shape = (8, channels)
    means = [jnp.broadcast_to(stats[k, 0:1, :], shape) for k in range(devices)]
    spreads = [jnp.broadcast_to(stats[k, 1:2, :], shape) for k in range(devices)]
    mean = functools.reduce(jnp.add, means) / devices
    spread = functools.reduce(jnp.add, spreads)
    spread = spread + rows * functools.reduce(jnp.add, [(m - mean) * (m - mean) for m in means])
    rows = rows * devices
    lane = lax.broadcasted_iota(jnp.int32, shape, 1)
    step = 1
    while step < channels // GROUPS:
        low = jnp.bitwise_and(lane, step) == 0
        others = [
            jnp.where(low, pltpu.roll(row, channels - step, 1), pltpu.roll(row, step, 1))
            for row in (mean, spread)
        ]
        mean, spread = merge(mean, spread, rows, *others)
        rows, step = 2.0 * rows, 2 * step
    return mean, lax.rsqrt(spread / rows + EPSILON)


def silu_of_double(h):
    return h + h * jnp.tanh(h)


def norm_kernel(ny, nx, inner, ends, stats, gain, offset, out, pooled, *refs):
    y_edges, x_edges, corners, half = refs
    depth, edge = inner.shape[0] + 6, inner.shape[1]
    deep, deep_depth = edge // 2, depth // 2
    f32, bf16 = jnp.float32, jnp.bfloat16
    above, left = Square().low_sides()
    depth_at = lax.axis_index("gz")
    mean, scale = read_stats(stats, float(edge**3))
    scale = scale * (0.5 * gain[...])
    shift = 0.5 * offset[...]
    for k in range(deep_depth):
        value = [
            ends[z] if z < 3 else inner[z - 3] if z < depth - 3 else ends[z - depth + 6]
            for z in (2 * k, 2 * k + 1)
        ]
        value = jnp.stack(value).reshape(edge * edge // 4, 8, 128)
        value = silu_of_double((value - mean) * scale + shift)
        value = value.reshape(2, edge, edge, 128).astype(bf16)
        if 0 < k < deep_depth - 1:
            out[2 * k - 2 : 2 * k] = value
        value = value.astype(f32)
        value = (value[0] + value[1]).reshape(deep, 2, edge, 128)
        half[k] = (value[:, 0] + value[:, 1]).reshape(deep * edge, 128)
        lines = half.at[k]
        pair = lines[pl.ds(0, deep * deep, stride=2), :] + lines[pl.ds(1, deep * deep, stride=2), :]
        pair = (pair * 0.125).astype(bf16).astype(f32).reshape(deep, deep, 128)
        if k == 0 or k == deep_depth - 1:
            inside = depth_at > 0 if k == 0 else depth_at < lax.axis_size("gz") - 1
            pair = jnp.where(inside, pair, 0.0)
        pooled[k] = pair
    lines = pooled.reshape(deep_depth * deep * deep, 128)
    rows = deep_depth * deep
    first_x = lines[pl.ds(0, rows, stride=deep), :]
    last_x = lines[pl.ds(deep - 1, rows, stride=deep), :]
    first_y, last_y = (pooled[:, y].reshape(rows, 128) for y in (0, deep - 1))
    ends = []
    for y in (0, deep - 1):
        for x in (0, deep - 1):
            ends.append(lines[pl.ds(y * deep + x, deep_depth, stride=deep * deep), :])
    if ny == 1:
        above, left = above[0], left[0]
        y_edges[0] = jnp.where(above, first_y, last_y).astype(bf16)
        x_edges[0] = jnp.where(left, first_x, last_x).astype(bf16)
        corners[0, 0:deep_depth] = jnp.where(
            above, jnp.where(left, ends[0], ends[1]), jnp.where(left, ends[2], ends[3])
        )
    else:
        y_edges[0], y_edges[1] = first_y.astype(bf16), last_y.astype(bf16)
        x_edges[0], x_edges[1] = first_x.astype(bf16), last_x.astype(bf16)
        for k in range(4):
            corners[k, 0:deep_depth] = ends[k]


def stack_kernel(*refs):
    out = refs[-1]
    for k in range(out.shape[0]):
        out[k] = refs[k][: out.shape[1], : out.shape[2]]


def stack(*arrays, part=None):
    vmem = pl.BlockSpec(memory_space=pltpu.VMEM)
    shape = (part or arrays[0].shape[:2]) + arrays[0].shape[2:]
    return pl.pallas_call(
        stack_kernel,
        out_shape=jax.ShapeDtypeStruct((len(arrays),) + shape, arrays[0].dtype),
        in_specs=[vmem] * len(arrays),
        out_specs=vmem,
        compiler_params=pltpu.CompilerParams(vmem_limit_bytes=VMEM_BYTES),
    )(*arrays)


def place_weights(own, held, out):
    tile = lax.axis_index("yx")
    out[tile] = own[...]
    if len(held) == 1:
        pieces, others, size = held[0].shape[:3]
        for piece in range(pieces):
            at = jnp.minimum(jnp.bitwise_xor(Riders.mine(), piece) * size, own.shape[0] - size)
            for k in range(others):
                out[jnp.bitwise_xor(tile, k + 1), pl.ds(at, size)] = held[0][piece, k]
    else:
        for k, shard in enumerate(held):
            out[lax.rem(tile + len(held) - k, len(held) + 1)] = shard[...]


def tap_rows(weight, taps):
    per = weight.shape[1] // 27
    return jnp.concatenate(
        [weight[:, pl.ds(tap * per, per)].reshape(-1, 128) for tap in taps], axis=1
    )


def dot_rows(left, right):
    return lax.dot_general(
        left, right, (((1,), (1,)), ((), ())), preferred_element_type=jnp.float32
    )


def deep_kernel(pooled, own, *refs):
    *held, act, weight, grid, packed = refs
    depth, deep = pooled.shape[0], pooled.shape[1]
    place_weights(own, held, weight)
    grid[...] = jnp.zeros(grid.shape, jnp.float32)
    grid[:, 1 : deep + 1, 8:16] = pooled[...]
    for dx in range(3):
        plane = grid[:, :, 7 + dx : 15 + dx]
        for y in range(deep + 1):
            both = jnp.concatenate([plane[:, y], plane[:, y + 1]], axis=1)
            packed[:, y // 2, y % 2, :, dx * 128 : dx * 128 + 128] = both.astype(jnp.bfloat16)
    rows = deep**3
    total = None
    for dz in range(3):
        left = jnp.concatenate(
            [
                packed[dz : dz + deep, dy // 2 : dy // 2 + deep // 2, dy % 2].reshape(rows, 384)
                for dy in range(3)
            ],
            axis=1,
        )
        term = dot_rows(left, tap_rows(weight, range(dz * 9, dz * 9 + 9)))
        total = term if total is None else total + term
    for half in range(act.shape[0]):
        act[half] = total[:, half * 128 : half * 128 + 128]


def deep_rim_kernel(ny, nx, own, y_halos, x_halos, corners, weight, act, stats, line):
    depth, deep = line.shape[0], line.shape[1] - 16
    halves = act.shape[0]
    f32 = jnp.float32
    square = deep * deep
    above, left = Square().low_sides()
    act[...] = own[...]
    flat = line.reshape(depth * line.shape[1], 128)

    def shifts():
        return jnp.concatenate(
            [
                line[dz : dz + deep, 7 + d : 7 + d + deep].reshape(square, 128).astype(jnp.bfloat16)
                for dz in range(3)
                for d in range(3)
            ],
            axis=1,
        )

    for i in range(ny):
        line[...] = jnp.zeros(line.shape, f32)
        line[:, 8 : 8 + deep] = y_halos[i].astype(f32).reshape(depth, deep, 128)
        for j in range(nx):
            end = corners[i * nx + j, 0:depth]
            first, last = jnp.where(left[j], end, 0.0), jnp.where(left[j], 0.0, end)
            if nx == 1 or j == 0:
                flat[pl.ds(7, depth, stride=line.shape[1]), :] = first
            if nx == 1 or j == 1:
                flat[pl.ds(8 + deep, depth, stride=line.shape[1]), :] = last
        tap = jnp.where(above[i], 0, 6)
        taps = [tap + dz * 9 + dx for dz in range(3) for dx in range(3)]
        terms = dot_rows(shifts(), tap_rows(weight, taps))
        for half in range(halves):
            rows = act.at[half].reshape(deep, deep, deep, 128)
            term = terms[:, half * 128 : half * 128 + 128].reshape(deep, deep, 128)
            rows[:, jnp.where(above[i], 0, deep - 1)] += term
    for j in range(nx):
        line[...] = jnp.zeros(line.shape, f32)
        line[:, 8 : 8 + deep] = x_halos[j].astype(f32).reshape(depth, deep, 128)
        tap = jnp.where(left[j], 0, 2)
        taps = [tap + dz * 9 + dy * 3 for dz in range(3) for dy in range(3)]
        terms = dot_rows(shifts(), tap_rows(weight, taps))
        first, last = jnp.where(left[j], terms, 0.0), jnp.where(left[j], 0.0, terms)
        for half in range(halves):
            lanes, rows = slice(half * 128, half * 128 + 128), act.at[half]
            if nx == 1 or j == 0:
                rows[pl.ds(0, square, stride=deep), :] += first[:, lanes]
            if nx == 1 or j == 1:
                rows[pl.ds(deep - 1, square, stride=deep), :] += last[:, lanes]

    rows = deep**3 // 8
    means, spreads = [], []
    for half in range(halves):
        total = act[half].reshape(rows, 8, 128)
        means.append(jnp.sum(total, axis=0) / rows)
        off = total - means[-1]
        spreads.append(jnp.sum(off * off, axis=0))
    put_stats(stats, *(jnp.concatenate(part, axis=1) for part in (means, spreads)), rows)


def final_kernel(act, stats, gain, offset, up, mid, out, wide, held, sems):
    edge = mid.shape[0]
    deep = edge // 2
    f32 = jnp.float32
    mean, scale = read_stats(stats, float(deep**3))
    scale = scale * (0.5 * gain[...])
    shift = 0.5 * offset[...]
    planes = 2
    size = planes * deep * deep
    copies = []
    for k in range(0, deep, planes):
        at = slice(k * deep * deep, k * deep * deep + size)
        value = jnp.concatenate([act[half, at] for half in range(act.shape[0])], axis=1)
        value = value.reshape(size // 8, 8, -1)
        value = silu_of_double((value - mean) * scale + shift)
        value = value.reshape(size, -1).astype(jnp.bfloat16)
        lifted = jnp.dot(value, up[...], preferred_element_type=f32)
        lines = wide.at[k // planes]
        lines[pl.ds(0, size, stride=2), :] = lifted
        lines[pl.ds(1, size, stride=2), :] = lifted
        add = lines[...].reshape(planes, 1, deep, 1, edge, 128)
        at = pl.ds(2 * k, 2 * planes)
        old = mid[at].astype(f32).reshape(planes, 2, deep, 2, edge, 128)
        held[at] = (old + add).astype(jnp.bfloat16).reshape(2 * planes, edge, edge, 128)
        copy = pltpu.make_async_copy(held.at[at], out.at[at], sems.at[k // planes])
        copy.start(priority=k // planes % 2)
        copies.append(copy)
    for copy in copies:
        copy.wait()


def body(
    features, conv_weight, gain_mid, offset_mid, deep_weight, gain_deep, offset_deep, up_weight
):
    f32, bf16 = jnp.float32, jnp.bfloat16
    edge, channels = features.shape[0], features.shape[3]
    deep = edge // 2
    deep_channels = gain_deep.shape[0]
    square = Square()
    tiles = square.tiles
    devices = lax.axis_size("gz") * tiles
    ny, nx = (len(sides) for sides in square.low_sides())
    riders = Riders(deep_weight.shape[4])

    own = jnp.moveaxis(deep_weight, 4, 3).reshape(-1, 16, channels)
    conv_weight = conv_weight.reshape(27, channels, channels)
    *edges, field, conv_weight = call(
        functools.partial(start_kernel, ny, nx, riders.size),
        [
            ((ny, edge + riders.size, edge, channels), bf16),
            ((nx, edge + riders.size, edge, channels), bf16),
            ((ny * nx, 1 + riders.size, edge, channels), bf16),
            ((edge + 2, edge + 2, edge, channels), bf16),
            (conv_weight.shape, bf16),
        ],
        [((nx, edge * edge, 8, channels), f32), pltpu.SemaphoreType.DMA((8,))],
        features,
        conv_weight,
        own,
        nbytes=5 << 20,
        in_hbm=3,
    )
    halos = square.halos(*(list(piece) for piece in edges))
    conv_flops = 54 * channels * channels * edge**3
    act, taps, pairs, own = call(
        conv_kernel,
        [
            ((edge, edge, edge, channels), f32),
            ((9 * channels, 3 * channels), bf16),
            ((12 * channels, 2 * channels), bf16),
            (own.shape, bf16),
        ],
        [pltpu.SemaphoreType.DMA],
        own,
        field,
        conv_weight,
        flops=conv_flops,
        nbytes=6 << 20,
        in_hbm=1,
    )
    (y, x, corner), act = lax.optimization_barrier((halos, act))
    y, x, corner = jnp.stack(y), jnp.stack(x), jnp.stack(corner)
    face = ((3 * (edge + ny + nx) + ny * nx, edge, channels), bf16)
    held = [((4, riders.size, 16, channels), bf16)] if riders.size else []
    outer, inner, *held = call(
        functools.partial(face_kernel, ny, nx, riders.size),
        [((face[0][0] + 2,) + face[0][1:], bf16), face] + held,
        [],
        field,
        y,
        x,
        corner,
    )
    outer, inner = swap_depth(outer, inner)
    if riders.size:
        held = held[0][None]
        other = swap(held, *riders.STEPS[0])
    else:
        held = rotate_shards(own)
    six = ((6, edge, edge, channels), f32)
    column = (edge + 16, channels)
    middle, partial, stats = call(
        functools.partial(side_kernel, ny, nx),
        [
            ((edge - 2, edge, edge, channels), f32),
            ((4, edge, edge, channels), f32),
            ((16, channels), f32),
        ],
        [((edge + 2, edge, edge, channels), f32), ((edge + 4,) + column, f32)],
        act,
        y,
        x,
        corner,
        taps,
    )
    room = [
        ((3, edge, edge, channels), f32),
        ((4, edge + 2, edge, channels), bf16),
        ((5,) + column, f32),
    ]
    (ends,) = call(
        functools.partial(inner_kernel, ny, nx), [six], room, field, partial, inner, taps, pairs
    )
    ends, stats = call(
        functools.partial(outer_kernel, ny, nx),
        [six, ((devices, 2, channels), f32)],
        room,
        field,
        stats,
        ends,
        outer,
        taps,
        pairs,
    )
    if riders.size:
        stats, other = lax.optimization_barrier((stats, other))
        held = stack(held, other, part=(1, 3)).reshape((2, 3) + held.shape[2:])
        other = swap(held, *riders.STEPS[1])
    (ends,) = call(
        functools.partial(beyond_kernel, ny, nx),
        [six],
        room[1:2],
        field,
        ends,
        outer,
        taps,
        pairs,
        flops=conv_flops,
        nbytes=4 << 20,
    )
    stats, ends = lax.optimization_barrier((stats, ends))
    stats = share(stats)
    if riders.size:
        stats, other = lax.optimization_barrier((stats, other))
        held = stack(held, other).reshape((-1,) + held.shape[1:])
        other = swap(held, *riders.STEPS[2])
        held = [stack(held, other).reshape((-1,) + held.shape[1:])]
    out, pooled, *edges = call(
        functools.partial(norm_kernel, ny, nx),
        [
            ((edge, edge, edge, channels), bf16),
            ((deep + 2, deep, deep, channels), f32),
            ((ny, (deep + 2) * deep, channels), bf16),
            ((nx, (deep + 2) * deep, channels), bf16),
            ((ny * nx, 16, channels), f32),
        ],
        [((deep + 2, deep * edge, channels), f32)],
        middle,
        ends,
        stats,
        gain_mid.reshape(1, channels),
        offset_mid.reshape(1, channels),
        flops=20 * channels * edge**3,
        nbytes=3 << 20,
    )
    y, x, corner = square.halos(*(list(piece) for piece in edges))
    halves = ((deep_channels // 128, deep**3, 128), f32)
    deep_act, weight = call(
        deep_kernel,
        [halves, ((tiles,) + own.shape, bf16)],
        [
            ((deep + 2, deep + 2, 24, channels), f32),
            ((deep + 2, deep // 2 + 1, 2, 16, 3 * channels), bf16),
        ],
        pooled,
        own,
        *held,
        flops=54 * channels * deep_channels * deep**3,
        nbytes=4 << 20,
    )
    deep_act, stats = call(
        functools.partial(deep_rim_kernel, ny, nx),
        [halves, ((devices, 2, deep_channels), f32)],
        [((deep + 2, 24, channels), f32)],
        deep_act,
        jnp.stack(y),
        jnp.stack(x),
        jnp.stack(corner),
        weight,
        flops=4 * channels * deep_channels * deep**3,
        nbytes=3 << 20,
    )
    stats = share(stats)
    (decoded,) = call(
        final_kernel,
        [((edge, edge, edge, channels), bf16)],
        [
            ((deep // 2, 4 * deep * deep, channels), f32),
            ((edge, edge, edge, channels), bf16),
            pltpu.SemaphoreType.DMA((deep // 2,)),
        ],
        deep_act,
        stats,
        gain_deep.reshape(1, deep_channels),
        offset_deep.reshape(1, deep_channels),
        up_weight,
        out,
        flops=4 * deep_channels * channels * deep**3,
        nbytes=3 << 20,
        out_hbm=True,
    )
    return decoded


def solution(mesh):
    placed = (
        P(("cand", "gz"), "yx", None, None),
        P(),
        P(),
        P(),
        P(None, None, None, None, "yx"),
        P(),
        P(),
        P(),
    )
    return jax.shard_map(
        body,
        mesh=mesh,
        in_specs=placed,
        out_specs=P(("cand", "gz"), "yx", None, None),
        check_vma=False,
    )
```

```python
import functools
import math

import jax
import jax.numpy as jnp
from jax import lax
from jax.experimental import pallas as pl
from jax.experimental.pallas import tpu as pltpu
from jax.sharding import PartitionSpec as P

GROUPS = 32
EPSILON = 1e-05
PART = ("gz", "yx")
VMEM_BYTES = 32 * 1024 * 1024


class Square:
    def __init__(self):
        self.tiles = lax.axis_size("yx")
        self.side = math.isqrt(self.tiles)
        tile = lax.axis_index("yx")
        self.row, self.column = tile // self.side, tile % self.side
        self.folded = self.side == 2
        self.steps = (0,) if self.folded else (-1, 1)

    def low_sides(self):
        if self.folded:
            return [self.row == 1], [self.column == 1]
        return [True, False], [True, False]

    def route(self, down, right):
        pairs = []
        for tile in range(self.tiles):
            row, column = tile // self.side + down, tile % self.side + right
            if 0 <= row < self.side and 0 <= column < self.side:
                pairs.append((tile, row * self.side + column))
        return pairs

    def swap_route(self, mask):
        return [(tile, tile ^ mask) for tile in range(self.tiles)]

    def halos(self, y_edges, x_edges, corners):
        if self.folded:
            y = lax.ppermute(y_edges[0], "yx", self.swap_route(2))
            x = lax.ppermute(x_edges[0], "yx", self.swap_route(1))
            corner = lax.ppermute(corners[0], "yx", self.swap_route(3))
            return [y], [x], [corner]
        y = [lax.ppermute(y_edges[k], "yx", self.route((1, -1)[1 - k], 0)) for k in (1, 0)]
        x = [lax.ppermute(x_edges[k], "yx", self.route(0, (1, -1)[1 - k])) for k in (1, 0)]
        corner = [
            lax.ppermute(corners[2 * k + j], "yx", self.route((1, -1)[1 - k], (1, -1)[1 - j]))
            for k in (1, 0)
            for j in (1, 0)
        ]
        return y, x, corner


def swap_depth(outer, inner):
    size = lax.axis_size("gz")
    routes = [[], []]
    for low in range(size - 1):
        routes[low % 2] += [(low, low + 1), (low + 1, low)]
    return lax.ppermute(outer, "gz", routes[1]), lax.ppermute(inner, "gz", routes[0])


class Riders:
    STEPS = (("cand", 1), ("gz", 2), ("gz", 1))

    def __init__(self, rows):
        self.tiles = 27 * rows // 16
        self.fits = (
            lax.axis_size("yx") == 4
            and lax.axis_size("cand") % 2 == 0
            and lax.axis_size("gz") % 4 == 0
            and self.tiles >= 8
        )
        self.size = -(-self.tiles // 8) if self.fits else 0

    @classmethod
    def mine(cls):
        return sum(
            lax.axis_index(axis) // mask % 2 * 2**k for k, (axis, mask) in enumerate(cls.STEPS)
        )


def rotate_shards(piece):
    tiles = lax.axis_size("yx")
    return [
        lax.ppermute(piece, "yx", [(i, (i + k) % tiles) for i in range(tiles)]) for k in range(1, tiles)
    ]


def swap(block, axis, mask):
    return lax.ppermute(block, axis, [(i, i ^ mask) for i in range(lax.axis_size(axis))])


def share(stats):
    return lax.all_to_all(stats, PART, 0, 0)


def call(kernel, outs, scratch, *arrays, flops=0, nbytes=0, in_hbm=0, out_hbm=False):
    vmem, hbm = (pl.BlockSpec(memory_space=space) for space in (pltpu.VMEM, pltpu.HBM))
    far, near = arrays[:in_hbm], arrays[in_hbm:]
    far = [pltpu.with_memory_space_constraint(array, pltpu.HBM) for array in far]
    return pl.pallas_call(
        kernel,
        out_shape=[jax.ShapeDtypeStruct(shape, dtype) for shape, dtype in outs],
        in_specs=[hbm] * len(far) + [vmem] * len(near),
        out_specs=[hbm if out_hbm else vmem] * len(outs),
        scratch_shapes=[pltpu.VMEM(*entry) if isinstance(entry, tuple) else entry for entry in scratch],
        compiler_params=pltpu.CompilerParams(vmem_limit_bytes=VMEM_BYTES),
        cost_estimate=pl.CostEstimate(flops=flops, bytes_accessed=nbytes, transcendentals=0),
    )(*far, *near)


def start_kernel(ny, nx, size, x_in, w_in, d_in, y_out, x_out, corners, x, w, lines, sems):
    edge = x_in.shape[0]
    f32, bf16 = jnp.float32, jnp.bfloat16
    above, left = Square().low_sides()
    chunks = 4
    planes = edge // chunks
    first = [
        pltpu.make_async_copy(
            x_in.at[pl.ds(k * planes, planes)],
            x.at[pl.ds(1 + k * planes, planes), pl.ds(1, edge)],
            sems.at[k],
        )
        for k in range(chunks)
    ]
    later = []
    if size:
        at = jnp.minimum(Riders.mine() * size, d_in.shape[0] - size)
        for k, (out, begin) in enumerate(((y_out, edge), (x_out, edge), (corners, 1))):
            later.append(
                pltpu.make_async_copy(
                    d_in.at[pl.ds(at, size)], out.at[0, pl.ds(begin, size)], sems.at[chunks + k]
                )
            )
    later.append(pltpu.make_async_copy(w_in, w, sems.at[chunks + 3]))
    for copy in first + later:
        copy.start()
    x[0] = jnp.zeros(x.shape[1:], bf16)
    x[edge + 1] = jnp.zeros(x.shape[1:], bf16)
    blank = jnp.zeros((edge,) + x.shape[2:], bf16)
    x[1 : edge + 1, 0] = blank
    x[1 : edge + 1, edge + 1] = blank
    flat = lines.reshape(nx * edge * edge * 8, 128)
    part = planes * edge
    for k in range(chunks):
        first[k].wait()
        at, here = pl.ds(k * planes, planes), pl.ds(1 + k * planes, planes)
        for i in range(ny):
            row = jnp.where(above[i], 1, edge)
            y_out[i, at] = x[here, row]
        for j in range(nx):
            low = x[here, 1 : edge + 1, 0:8].astype(f32).reshape(part, 8, 128)
            high = x[here, 1 : edge + 1, edge - 8 : edge].astype(f32).reshape(part, 8, 128)
            high = pltpu.roll(high, 1, 1)
            kept = jnp.where(left[j], low, high)
            lines[j, k * part : k * part + part] = kept
            begin = (j * edge * edge + k * part) * 8
            column = flat[pl.ds(begin, part, stride=8), :]
            x_out[j, at] = column.astype(bf16).reshape(planes, edge, 128)
    for i in range(ny):
        for j in range(nx):
            begin = j * edge * edge * 8
            low = flat[pl.ds(begin, edge, stride=8 * edge), :]
            high = flat[pl.ds(begin + 8 * (edge - 1), edge, stride=8 * edge), :]
            kept = jnp.where(above[i], low, high)
            corners[i * nx + j, 0] = kept.astype(bf16)
    for copy in later:
        copy.wait()


def face_kernel(ny, nx, size, x, y_halos, x_halos, corners, outer, inner, *riders):
    edge = outer.shape[1]
    wide = edge + ny + nx
    odd = lax.axis_index("gz") % 2
    far = edge - 3
    for face, at in ((outer, odd * far), (inner, (1 - odd) * far)):
        for k in range(3):
            row = k * wide
            face[row : row + edge] = x[1 + at + k, 1 : edge + 1]
            for i in range(ny):
                face[row + edge + i] = y_halos[i, at + k]
            for j in range(nx):
                face[row + edge + ny + j] = x_halos[j, at + k]
        for k in range(ny * nx):
            face[3 * wide + k] = corners[k, 0]
    for k in range(inner.shape[0], outer.shape[0]):
        outer[k] = corners[0, 0]
    if size:
        riders[0][0] = x_halos[0, edge : edge + size]
        riders[0][1] = y_halos[0, edge : edge + size]
        riders[0][2] = corners[0, 1 : 1 + size]
        riders[0][3] = corners[0, 1 : 1 + size]


def spread_taps(weight, taps):
    for tap in range(27):
        row, lane = tap // 3 * 128, tap % 3 * 128
        taps[row : row + 128, lane : lane + 128] = weight[tap]


def pair_taps(weight, pairs):
    for dz in range(3):
        for line in range(4):
            row = (dz * 4 + line) * 128
            for out in range(2):
                lane = out * 128
                if 0 <= line - out < 3:
                    block = weight[dz * 9 + (line - out) * 3 + 2]
                else:
                    block = jnp.zeros((128, 128), pairs.dtype)
                pairs[row : row + 128, lane : lane + 128] = block


def join_x(wide, edge):
    place = lax.broadcasted_iota(jnp.int32, wide.shape[:2] + (128,), 1)
    after = jnp.where(place > 0, pltpu.roll(wide[:, :, :128], 1, 1), 0.0)
    before = jnp.where(place < edge - 1, pltpu.roll(wide[:, :, 256:], edge - 1, 1), 0.0)
    return wide[:, :, 128:256] + after + before


def convolve(grid, count, taps, pairs, put):
    edge = grid.shape[2]
    planes = min(count, 4)
    rows = planes * edge * edge
    place = lax.broadcasted_iota(jnp.int32, (planes * edge, edge, 128), 1)
    halved = grid.reshape(grid.shape[0], edge // 2 + 1, 2, edge, 128)
    for z in range(0, count, planes):
        left = jnp.concatenate(
            [
                grid[z + dz : z + dz + planes, dy : dy + edge].reshape(rows, 128)
                for dz in range(3)
                for dy in range(3)
            ],
            axis=1,
        )
        wide = jnp.dot(left, taps[:, 0:256], preferred_element_type=jnp.float32)
        wide = wide.reshape(planes * edge, edge, 256)
        left = jnp.concatenate(
            [
                halved[z + dz : z + dz + planes, line // 2 : line // 2 + edge // 2, line % 2].reshape(
                    rows // 2, 128
                )
                for dz in range(3)
                for line in range(4)
            ],
            axis=1,
        )
        two = jnp.dot(left, pairs[...], preferred_element_type=jnp.float32)
        two = two.reshape(planes * edge // 2, edge, 256)
        two = jnp.stack([two[:, :, :128], two[:, :, 128:]], axis=1).reshape(planes * edge, edge, 128)
        after = jnp.where(place > 0, pltpu.roll(wide[:, :, :128], 1, 1), 0.0)
        before = jnp.where(place < edge - 1, pltpu.roll(two, edge - 1, 1), 0.0)
        new = wide[:, :, 128:256] + after + before
        put(z, new.reshape(planes, edge, edge, 128))


def conv_kernel(deep_in, x, weight, act, taps, pairs, deep_weight, sem):
    copy = pltpu.make_async_copy(deep_in, deep_weight, sem)
    copy.start()
    edge = act.shape[0]
    spread_taps(weight, taps)
    pair_taps(weight, pairs)

    def put(z, new):
        act[z : z + new.shape[0]] = new

    convolve(x, edge, taps, pairs, put)
    copy.wait()


def y_terms(line, low, taps):
    planes, edge = line.shape[0] - 2, line.shape[1]
    left = jnp.concatenate(
        [line[dz : dz + planes].reshape(planes * edge, 128) for dz in range(3)], axis=1
    )
    start = jnp.where(low, 0, 256)
    right = jnp.concatenate(
        [taps[pl.ds(pl.multiple_of(start + dz * 384, 128), 128), :] for dz in range(3)], axis=0
    )
    wide = jnp.dot(left, right, preferred_element_type=jnp.float32)
    return join_x(wide.reshape(planes, edge, 384), edge)


def x_terms(column, taps):
    planes, edge = column.shape[0] - 2, column.shape[1] - 16
    lines = [column[:, 7 + dy : 7 + dy + edge].astype(jnp.bfloat16) for dy in range(3)]
    left = jnp.concatenate(
        [line[dz : dz + planes].reshape(planes * edge, 128) for dz in range(3) for line in lines],
        axis=1,
    )
    right = jnp.concatenate([taps[:, 0:128], taps[:, 256:384]], axis=1)
    both = jnp.dot(left, right, preferred_element_type=jnp.float32)
    return both[:, :128], both[:, 128:]


def fill_column(column, at, voxels, ends, above):
    count, edge = voxels.shape[:2]
    rows = edge + 16
    lines = column.reshape(column.shape[0] * rows, 128)
    column[at : at + count, 8 : 8 + edge] = voxels.astype(jnp.float32)
    for i, end in enumerate(ends):
        first = last = end.astype(jnp.float32)
        if len(ends) == 1:
            first, last = jnp.where(above[0], first, 0.0), jnp.where(above[0], 0.0, last)
        if len(ends) == 1 or i == 0:
            lines[pl.ds(at * rows + 7, count, stride=rows), :] = first
        if len(ends) == 1 or i == 1:
            lines[pl.ds(at * rows + 8 + edge, count, stride=rows), :] = last


def add_column(act, terms, j, nx, low):
    planes, edge = act.shape[:2]
    flat = act.reshape(planes * edge * edge, 128)
    first, last = terms
    if nx == 1:
        first, last = jnp.where(low, first, 0.0), jnp.where(low, 0.0, last)
    if nx == 1 or j == 0:
        flat[pl.ds(0, planes * edge, stride=edge), :] += first
    if nx == 1 or j == 1:
        flat[pl.ds(edge - 1, planes * edge, stride=edge), :] += last


def moments(planes):
    count, edge = planes.shape[:2]
    zero = jnp.zeros((8, 128), jnp.float32)

    def sum_step(k, carry):
        return carry + jnp.sum(planes[k].reshape(edge * 2, 8, 128), axis=0)

    mean = lax.fori_loop(0, count, sum_step, zero, unroll=True) / (count * edge * edge // 8)

    def spread_step(k, carry):
        off = planes[k].reshape(edge * 2, 8, 128) - mean
        return carry + jnp.sum(off * off, axis=0)

    return mean, lax.fori_loop(0, count, spread_step, zero, unroll=True)


def side_kernel(ny, nx, own, y_halos, x_halos, corners, taps, inner, ends, stats, act, column):
    edge = own.shape[0]
    act[0] = jnp.zeros(act.shape[1:], jnp.float32)
    act[edge + 1] = jnp.zeros(act.shape[1:], jnp.float32)
    act[1 : edge + 1] = own[...]
    above, left = Square().low_sides()
    blank = jnp.zeros((2, edge, 128), jnp.bfloat16)
    for i in range(ny):
        line = jnp.concatenate([blank, y_halos[i, 0:edge], blank], axis=0)
        act[:, jnp.where(above[i], 0, edge - 1)] += y_terms(line, above[i], taps)
    for j in range(nx):
        column[...] = jnp.zeros(column.shape, jnp.float32)
        fill_column(
            column, 2, x_halos[j, 0:edge], [corners[i * nx + j, 0] for i in range(ny)], above
        )
        add_column(act, x_terms(column, taps), j, nx, left[j])
    inner[...] = act[2:edge]
    ends[0:2] = act[0:2]
    ends[2:4] = act[edge : edge + 2]
    mean, spread = moments(act.at[2:edge])
    stats[0:8] = mean
    stats[8:16] = spread


def add_face(ny, nx, behind, face, x, taps, pairs, ends, three, grid, column, beyond=True):
    edge = x.shape[2]
    wide_face = edge + ny + nx
    f32 = jnp.float32
    above, left = Square().low_sides()
    end = pl.ds(jnp.where(behind, 3, 0), 3)
    three[...] = ends[end]
    blank = jnp.zeros(grid.shape[:1] + grid.shape[2:], grid.dtype)
    grid[:, 0] = blank
    grid[:, edge + 1] = blank
    first = jnp.where(behind, 1, 0)
    for k in range(3):
        grid[first + k, 1 : edge + 1] = face[k * wide_face : k * wide_face + edge]
    grid[jnp.where(behind, 0, 3), 1 : edge + 1] = x[jnp.where(behind, edge, 1), 1 : edge + 1]

    def put(z, new):
        three[pl.ds(first + z, new.shape[0])] += new

    if beyond:
        convolve(grid, 2, taps, pairs, put)
    beside = jnp.where(behind, 1, 2)
    lines = [grid[beside, dy : dy + edge].reshape(edge * edge, 128) for dy in range(3)]
    rows = taps[pl.ds(pl.multiple_of(jnp.where(behind, 768, 0), 128), 384), :]
    wide = jnp.dot(jnp.concatenate(lines, axis=1), rows, preferred_element_type=f32)
    three[jnp.where(behind, 0, 2)] += join_x(wide.reshape(edge, edge, 384), edge)

    def five(voxels):
        gap = jnp.zeros((2,) + voxels.shape[1:], voxels.dtype)
        return jnp.where(
            behind,
            jnp.concatenate([gap, voxels], axis=0),
            jnp.concatenate([voxels, gap], axis=0),
        )

    def rim(row):
        return five(jnp.stack([face[k * wide_face + edge + row] for k in range(3)]).astype(f32))

    for i in range(ny):
        terms = y_terms(rim(i).astype(jnp.bfloat16), above[i], taps)
        three[:, jnp.where(above[i], 0, edge - 1)] += terms
    for j in range(nx):
        column[...] = jnp.zeros(column.shape, f32)
        tails = []
        for i in range(ny):
            tile = face[3 * wide_face + i * nx + j].astype(f32)
            tails.append(five(jnp.where(behind, tile[:3], tile[edge - 3 :])))
        fill_column(column, 0, rim(ny + j), tails, above)
        add_column(three, x_terms(column, taps), j, nx, left[j])
    ends[end] = three[...]


def inner_kernel(ny, nx, x, partial, face, taps, pairs, ends, three, grid, column):
    blank = jnp.zeros(ends.shape[1:], jnp.float32)
    ends[0] = blank
    ends[1:5] = partial[...]
    ends[5] = blank
    behind = lax.axis_index("gz") % 2 == 0
    add_face(ny, nx, behind, face, x, taps, pairs, ends, three, grid, column)


def outer_kernel(ny, nx, x, middle_stats, ends, face, taps, pairs, act, stats, three, grid, column):
    edge = x.shape[2]
    act[...] = ends[...]
    behind = lax.axis_index("gz") % 2 == 1
    add_face(ny, nx, behind, face, x, taps, pairs, act, three, grid, column, beyond=False)
    mean, spread = moments(act.at[2:4])
    few, many = edge * edge // 4, (edge - 2) * edge * edge // 8
    middle_mean, middle_spread = middle_stats[0:8], middle_stats[8:16]
    off = middle_mean - mean
    part = few / (few + many)
    spread = spread + middle_spread + (many * part) * (off * off)
    put_stats(stats, middle_mean - part * off, spread, few + many)


def beyond_kernel(ny, nx, x, ends, face, taps, pairs, act, grid):
    edge = x.shape[2]
    wide_face = edge + ny + nx
    depth_at = lax.axis_index("gz")
    behind = depth_at % 2 == 1
    act[...] = ends[...]

    @pl.when(jnp.where(behind, depth_at < lax.axis_size("gz") - 1, depth_at > 0))
    def _():
        blank = jnp.zeros(grid.shape[:1] + grid.shape[2:], grid.dtype)
        grid[:, 0] = blank
        grid[:, edge + 1] = blank
        first = jnp.where(behind, 1, 0)
        for k in range(3):
            grid[first + k, 1 : edge + 1] = face[k * wide_face : k * wide_face + edge]
        own = jnp.where(behind, edge, 1)
        grid[jnp.where(behind, 0, 3), 1 : edge + 1] = x[own, 1 : edge + 1]

        def put(z, new):
            act[pl.ds(jnp.where(behind, 4, 0) + z, new.shape[0])] += new

        convolve(grid, 2, taps, pairs, put)


def merge(mean, spread, rows, other_mean, other_spread):
    off = mean - other_mean
    return 0.5 * (mean + other_mean), spread + other_spread + (0.5 * rows) * (off * off)


def put_stats(stats, mean, spread, rows):
    for step in (1, 2, 4):
        others = pltpu.roll(mean, step, 0), pltpu.roll(spread, step, 0)
        mean, spread = merge(mean, spread, float(rows * step), *others)
    both = jnp.concatenate([mean[0:1], spread[0:1]], axis=0)
    stats[...] = jnp.broadcast_to(both[None], stats.shape)


def read_stats(stats, rows):
    devices, _, channels = stats.shape
    shape = (8, channels)
    means = [jnp.broadcast_to(stats[k, 0:1, :], shape) for k in range(devices)]
    spreads = [jnp.broadcast_to(stats[k, 1:2, :], shape) for k in range(devices)]
    mean = functools.reduce(jnp.add, means) / devices
    spread = functools.reduce(jnp.add, spreads)
    spread = spread + rows * functools.reduce(jnp.add, [(m - mean) * (m - mean) for m in means])
    rows = rows * devices
    lane = lax.broadcasted_iota(jnp.int32, shape, 1)
    step = 1
    while step < channels // GROUPS:
        low = jnp.bitwise_and(lane, step) == 0
        others = [
            jnp.where(low, pltpu.roll(row, channels - step, 1), pltpu.roll(row, step, 1))
            for row in (mean, spread)
        ]
        mean, spread = merge(mean, spread, rows, *others)
        rows, step = 2.0 * rows, 2 * step
    return mean, lax.rsqrt(spread / rows + EPSILON)


def silu_of_double(h):
    return h + h * jnp.tanh(h)


def sixteen(rows):
    pad = jnp.zeros((16 - rows.shape[0], 128), rows.dtype)
    return jnp.concatenate([rows, pad], axis=0).astype(jnp.bfloat16)


def norm_kernel(ny, nx, inner, ends, stats, gain, offset, out, pooled, *refs):
    y_edges, x_edges, corners, half = refs
    depth, edge = inner.shape[0] + 6, inner.shape[1]
    deep, deep_depth = edge // 2, depth // 2
    f32, bf16 = jnp.float32, jnp.bfloat16
    above, left = Square().low_sides()
    depth_at = lax.axis_index("gz")
    mean, scale = read_stats(stats, float(edge**3))
    scale = scale * (0.5 * gain[...])
    shift = 0.5 * offset[...]
    for k in range(deep_depth):
        value = [
            ends[z] if z < 3 else inner[z - 3] if z < depth - 3 else ends[z - depth + 6]
            for z in (2 * k, 2 * k + 1)
        ]
        value = jnp.stack(value).reshape(edge * edge // 4, 8, 128)
        value = silu_of_double((value - mean) * scale + shift)
        value = value.reshape(2, edge, edge, 128).astype(bf16)
        if 0 < k < deep_depth - 1:
            out[2 * k - 2 : 2 * k] = value
        value = value.astype(f32)
        value = (value[0] + value[1]).reshape(deep, 2, edge, 128)
        half[k] = (value[:, 0] + value[:, 1]).reshape(deep * edge, 128)
        lines = half.at[k]
        pair = lines[pl.ds(0, deep * deep, stride=2), :] + lines[pl.ds(1, deep * deep, stride=2), :]
        pair = (pair * 0.125).astype(bf16).astype(f32).reshape(deep, deep, 128)
        if k == 0 or k == deep_depth - 1:
            inside = depth_at > 0 if k == 0 else depth_at < lax.axis_size("gz") - 1
            pair = jnp.where(inside, pair, 0.0)
        pooled[k] = pair
    lines = pooled.reshape(deep_depth * deep * deep, 128)
    rows = deep_depth * deep
    first_x = lines[pl.ds(0, rows, stride=deep), :]
    last_x = lines[pl.ds(deep - 1, rows, stride=deep), :]
    first_y, last_y = (pooled[:, y].reshape(rows, 128) for y in (0, deep - 1))
    ends = []
    for y in (0, deep - 1):
        for x in (0, deep - 1):
            ends.append(lines[pl.ds(y * deep + x, deep_depth, stride=deep * deep), :])
    if ny == 1:
        above, left = above[0], left[0]
        y_edges[0] = jnp.where(above, first_y, last_y).astype(bf16)
        x_edges[0] = jnp.where(left, first_x, last_x).astype(bf16)
        end = jnp.where(
            above, jnp.where(left, ends[0], ends[1]), jnp.where(left, ends[2], ends[3])
        )
        corners[0, 0:16] = sixteen(end)
    else:
        y_edges[0], y_edges[1] = first_y.astype(bf16), last_y.astype(bf16)
        x_edges[0], x_edges[1] = first_x.astype(bf16), last_x.astype(bf16)
        for k in range(4):
            corners[k, 0:16] = sixteen(ends[k])


def stack_kernel(*refs):
    out = refs[-1]
    for k in range(out.shape[0]):
        out[k] = refs[k][: out.shape[1], : out.shape[2]]


def stack(*arrays, part=None):
    vmem = pl.BlockSpec(memory_space=pltpu.VMEM)
    shape = (part or arrays[0].shape[:2]) + arrays[0].shape[2:]
    return pl.pallas_call(
        stack_kernel,
        out_shape=jax.ShapeDtypeStruct((len(arrays),) + shape, arrays[0].dtype),
        in_specs=[vmem] * len(arrays),
        out_specs=vmem,
        compiler_params=pltpu.CompilerParams(vmem_limit_bytes=VMEM_BYTES),
    )(*arrays)


def place_weights(own, held, out):
    tile = lax.axis_index("yx")
    out[tile] = own[...]
    if len(held) == 1:
        pieces, others, size = held[0].shape[:3]
        for piece in range(pieces):
            at = jnp.minimum(jnp.bitwise_xor(Riders.mine(), piece) * size, own.shape[0] - size)
            for k in range(others):
                out[jnp.bitwise_xor(tile, k + 1), pl.ds(at, size)] = held[0][piece, k]
    else:
        for k, shard in enumerate(held):
            out[lax.rem(tile + len(held) - k, len(held) + 1)] = shard[...]


def tap_rows(weight, taps):
    per = weight.shape[1] // 27
    return jnp.concatenate(
        [weight[:, pl.ds(tap * per, per)].reshape(-1, 128) for tap in taps], axis=1
    )


def dot_rows(left, right):
    return lax.dot_general(
        left, right, (((1,), (1,)), ((), ())), preferred_element_type=jnp.float32
    )


def deep_kernel(pooled, own, *refs):
    *held, act, weight, grid, packed = refs
    depth, deep = pooled.shape[0], pooled.shape[1]
    place_weights(own, held, weight)
    grid[...] = jnp.zeros(grid.shape, jnp.float32)
    grid[:, 1 : deep + 1, 8:16] = pooled[...]
    for dx in range(3):
        plane = grid[:, :, 7 + dx : 15 + dx]
        for y in range(deep + 1):
            both = jnp.concatenate([plane[:, y], plane[:, y + 1]], axis=1)
            packed[:, y // 2, y % 2, :, dx * 128 : dx * 128 + 128] = both.astype(jnp.bfloat16)
    rows = deep**3
    total = None
    for dz in range(3):
        left = jnp.concatenate(
            [
                packed[dz : dz + deep, dy // 2 : dy // 2 + deep // 2, dy % 2].reshape(rows, 384)
                for dy in range(3)
            ],
            axis=1,
        )
        term = dot_rows(left, tap_rows(weight, range(dz * 9, dz * 9 + 9)))
        total = term if total is None else total + term
    for half in range(act.shape[0]):
        act[half] = total[:, half * 128 : half * 128 + 128]


def deep_rim_kernel(ny, nx, own, y_halos, corners, x_halos, weight, act, stats, line):
    depth, deep = line.shape[0], line.shape[1] - 16
    halves = act.shape[0]
    f32 = jnp.float32
    square = deep * deep
    above, left = Square().low_sides()
    act[...] = own[...]
    flat = line.reshape(depth * line.shape[1], 128)

    def shifts():
        return jnp.concatenate(
            [
                line[dz : dz + deep, 7 + d : 7 + d + deep].reshape(square, 128).astype(jnp.bfloat16)
                for dz in range(3)
                for d in range(3)
            ],
            axis=1,
        )

    for i in range(ny):
        line[...] = jnp.zeros(line.shape, f32)
        line[:, 8 : 8 + deep] = y_halos[i].astype(f32).reshape(depth, deep, 128)
        for j in range(nx):
            end = corners[i * nx + j, 0:16].astype(f32)[:depth]
            first, last = jnp.where(left[j], end, 0.0), jnp.where(left[j], 0.0, end)
            if nx == 1 or j == 0:
                flat[pl.ds(7, depth, stride=line.shape[1]), :] = first
            if nx == 1 or j == 1:
                flat[pl.ds(8 + deep, depth, stride=line.shape[1]), :] = last
        tap = jnp.where(above[i], 0, 6)
        taps = [tap + dz * 9 + dx for dz in range(3) for dx in range(3)]
        terms = dot_rows(shifts(), tap_rows(weight, taps))
        for half in range(halves):
            rows = act.at[half].reshape(deep, deep, deep, 128)
            term = terms[:, half * 128 : half * 128 + 128].reshape(deep, deep, 128)
            rows[:, jnp.where(above[i], 0, deep - 1)] += term
    for j in range(nx):
        line[...] = jnp.zeros(line.shape, f32)
        line[:, 8 : 8 + deep] = x_halos[j].astype(f32).reshape(depth, deep, 128)
        tap = jnp.where(left[j], 0, 2)
        taps = [tap + dz * 9 + dy * 3 for dz in range(3) for dy in range(3)]
        terms = dot_rows(shifts(), tap_rows(weight, taps))
        first, last = jnp.where(left[j], terms, 0.0), jnp.where(left[j], 0.0, terms)
        for half in range(halves):
            lanes, rows = slice(half * 128, half * 128 + 128), act.at[half]
            if nx == 1 or j == 0:
                rows[pl.ds(0, square, stride=deep), :] += first[:, lanes]
            if nx == 1 or j == 1:
                rows[pl.ds(deep - 1, square, stride=deep), :] += last[:, lanes]

    rows = deep**3 // 8
    means, spreads = [], []
    for half in range(halves):
        total = act[half].reshape(rows, 8, 128)
        means.append(jnp.sum(total, axis=0) / rows)
        off = total - means[-1]
        spreads.append(jnp.sum(off * off, axis=0))
    put_stats(stats, *(jnp.concatenate(part, axis=1) for part in (means, spreads)), rows)


def final_kernel(act, stats, gain, offset, up, mid, out, wide, held, sems):
    edge = mid.shape[0]
    deep = edge // 2
    f32 = jnp.float32
    mean, scale = read_stats(stats, float(deep**3))
    scale = scale * (0.5 * gain[...])
    shift = 0.5 * offset[...]
    planes = 2
    size = planes * deep * deep
    copies = []
    for k in range(0, deep, planes):
        at = slice(k * deep * deep, k * deep * deep + size)
        value = jnp.concatenate([act[half, at] for half in range(act.shape[0])], axis=1)
        value = value.reshape(size // 8, 8, -1)
        value = silu_of_double((value - mean) * scale + shift)
        value = value.reshape(size, -1).astype(jnp.bfloat16)
        lifted = jnp.dot(value, up[...], preferred_element_type=f32)
        lines = wide.at[k // planes]
        lines[pl.ds(0, size, stride=2), :] = lifted
        lines[pl.ds(1, size, stride=2), :] = lifted
        add = lines[...].reshape(planes, 1, deep, 1, edge, 128)
        at = pl.ds(2 * k, 2 * planes)
        old = mid[at].astype(f32).reshape(planes, 2, deep, 2, edge, 128)
        held[at] = (old + add).astype(jnp.bfloat16).reshape(2 * planes, edge, edge, 128)
        copy = pltpu.make_async_copy(held.at[at], out.at[at], sems.at[k // planes])
        copy.start()
        copies.append(copy)
    for copy in copies:
        copy.wait()


def body(
    features, conv_weight, gain_mid, offset_mid, deep_weight, gain_deep, offset_deep, up_weight
):
    f32, bf16 = jnp.float32, jnp.bfloat16
    edge, channels = features.shape[0], features.shape[3]
    deep = edge // 2
    deep_channels = gain_deep.shape[0]
    square = Square()
    tiles = square.tiles
    devices = lax.axis_size("gz") * tiles
    ny, nx = (len(sides) for sides in square.low_sides())
    riders = Riders(deep_weight.shape[4])

    own = jnp.moveaxis(deep_weight, 4, 3).reshape(-1, 16, channels)
    conv_weight = conv_weight.reshape(27, channels, channels)
    *edges, field, conv_weight = call(
        functools.partial(start_kernel, ny, nx, riders.size),
        [
            ((ny, edge + riders.size, edge, channels), bf16),
            ((nx, edge + riders.size, edge, channels), bf16),
            ((ny * nx, 1 + riders.size, edge, channels), bf16),
            ((edge + 2, edge + 2, edge, channels), bf16),
            (conv_weight.shape, bf16),
        ],
        [((nx, edge * edge, 8, channels), f32), pltpu.SemaphoreType.DMA((8,))],
        features,
        conv_weight,
        own,
        nbytes=5 << 20,
        in_hbm=3,
    )
    halos = square.halos(*(list(piece) for piece in edges))
    conv_flops = 54 * channels * channels * edge**3
    act, taps, pairs, own = call(
        conv_kernel,
        [
            ((edge, edge, edge, channels), f32),
            ((9 * channels, 3 * channels), bf16),
            ((12 * channels, 2 * channels), bf16),
            (own.shape, bf16),
        ],
        [pltpu.SemaphoreType.DMA],
        own,
        field,
        conv_weight,
        flops=conv_flops,
        nbytes=6 << 20,
        in_hbm=1,
    )
    (y, x, corner), act = lax.optimization_barrier((halos, act))
    y, x, corner = jnp.stack(y), jnp.stack(x), jnp.stack(corner)
    face = ((3 * (edge + ny + nx) + ny * nx, edge, channels), bf16)
    held = [((4, riders.size, 16, channels), bf16)] if riders.size else []
    outer, inner, *held = call(
        functools.partial(face_kernel, ny, nx, riders.size),
        [((face[0][0] + 2,) + face[0][1:], bf16), face] + held,
        [],
        field,
        y,
        x,
        corner,
    )
    outer, inner = swap_depth(outer, inner)
    if riders.size:
        held = held[0][None]
        other = swap(held, *riders.STEPS[0])
    else:
        held = rotate_shards(own)
    six = ((6, edge, edge, channels), f32)
    column = (edge + 16, channels)
    middle, partial, stats = call(
        functools.partial(side_kernel, ny, nx),
        [
            ((edge - 2, edge, edge, channels), f32),
            ((4, edge, edge, channels), f32),
            ((16, channels), f32),
        ],
        [((edge + 2, edge, edge, channels), f32), ((edge + 4,) + column, f32)],
        act,
        y,
        x,
        corner,
        taps,
    )
    room = [
        ((3, edge, edge, channels), f32),
        ((4, edge + 2, edge, channels), bf16),
        ((5,) + column, f32),
    ]
    (ends,) = call(
        functools.partial(inner_kernel, ny, nx), [six], room, field, partial, inner, taps, pairs
    )
    ends, stats = call(
        functools.partial(outer_kernel, ny, nx),
        [six, ((devices, 2, channels), f32)],
        room,
        field,
        stats,
        ends,
        outer,
        taps,
        pairs,
    )
    if riders.size:
        stats, other = lax.optimization_barrier((stats, other))
        held = stack(held, other, part=(1, 3)).reshape((2, 3) + held.shape[2:])
        other = swap(held, *riders.STEPS[1])
    (ends,) = call(
        functools.partial(beyond_kernel, ny, nx),
        [six],
        room[1:2],
        field,
        ends,
        outer,
        taps,
        pairs,
        flops=conv_flops,
        nbytes=4 << 20,
    )
    stats, ends = lax.optimization_barrier((stats, ends))
    stats = share(stats)
    if riders.size:
        stats, other = lax.optimization_barrier((stats, other))
        held = stack(held, other).reshape((-1,) + held.shape[1:])
        other = swap(held, *riders.STEPS[2])
        held = [stack(held, other).reshape((-1,) + held.shape[1:])]
    out, pooled, *edges = call(
        functools.partial(norm_kernel, ny, nx),
        [
            ((edge, edge, edge, channels), bf16),
            ((deep + 2, deep, deep, channels), f32),
            ((ny, (deep + 2) * deep, channels), bf16),
            ((nx, (deep + 2) * deep, channels), bf16),
            ((ny * nx, (deep + 2) * deep, channels), bf16),
        ],
        [((deep + 2, deep * edge, channels), f32)],
        middle,
        ends,
        stats,
        gain_mid.reshape(1, channels),
        offset_mid.reshape(1, channels),
        flops=20 * channels * edge**3,
        nbytes=3 << 20,
    )
    y, x, corner = square.halos(*(list(piece) for piece in edges))
    halves = ((deep_channels // 128, deep**3, 128), f32)
    deep_act, weight = call(
        deep_kernel,
        [halves, ((tiles,) + own.shape, bf16)],
        [
            ((deep + 2, deep + 2, 24, channels), f32),
            ((deep + 2, deep // 2 + 1, 2, 16, 3 * channels), bf16),
        ],
        pooled,
        own,
        *held,
        flops=54 * channels * deep_channels * deep**3,
        nbytes=4 << 20,
    )
    deep_act, stats = call(
        functools.partial(deep_rim_kernel, ny, nx),
        [halves, ((devices, 2, deep_channels), f32)],
        [((deep + 2, 24, channels), f32)],
        deep_act,
        jnp.stack(y),
        jnp.stack(corner),
        jnp.stack(x),
        weight,
        flops=4 * channels * deep_channels * deep**3,
        nbytes=3 << 20,
    )
    stats = share(stats)
    (decoded,) = call(
        final_kernel,
        [((edge, edge, edge, channels), bf16)],
        [
            ((deep // 2, 4 * deep * deep, channels), f32),
            ((edge, edge, edge, channels), bf16),
            pltpu.SemaphoreType.DMA((deep // 2,)),
        ],
        deep_act,
        stats,
        gain_deep.reshape(1, deep_channels),
        offset_deep.reshape(1, deep_channels),
        up_weight,
        out,
        flops=4 * deep_channels * channels * deep**3,
        nbytes=3 << 20,
        out_hbm=True,
    )
    return decoded


def solution(mesh):
    placed = (
        P(("cand", "gz"), "yx", None, None),
        P(),
        P(),
        P(),
        P(None, None, None, None, "yx"),
        P(),
        P(),
        P(),
    )
    return jax.shard_map(
        body,
        mesh=mesh,
        in_specs=placed,
        out_specs=P(("cand", "gz"), "yx", None, None),
        check_vma=False,
    )
```

```python
import functools
import math

import jax
import jax.numpy as jnp
from jax import lax
from jax.experimental import pallas as pl
from jax.experimental.pallas import tpu as pltpu
from jax.sharding import PartitionSpec as P

GROUPS = 32
EPSILON = 1e-05
PART = ("gz", "yx")
VMEM_BYTES = 32 * 1024 * 1024


class Square:
    def __init__(self):
        self.tiles = lax.axis_size("yx")
        self.side = math.isqrt(self.tiles)
        tile = lax.axis_index("yx")
        self.row, self.column = tile // self.side, tile % self.side
        self.folded = self.side == 2
        self.steps = (0,) if self.folded else (-1, 1)

    def low_sides(self):
        if self.folded:
            return [self.row == 1], [self.column == 1]
        return [True, False], [True, False]

    def route(self, down, right):
        pairs = []
        for tile in range(self.tiles):
            row, column = tile // self.side + down, tile % self.side + right
            if 0 <= row < self.side and 0 <= column < self.side:
                pairs.append((tile, row * self.side + column))
        return pairs

    def swap_route(self, mask):
        return [(tile, tile ^ mask) for tile in range(self.tiles)]

    def halos(self, y_edges, x_edges, corners):
        if self.folded:
            y = lax.ppermute(y_edges[0], "yx", self.swap_route(2))
            x = lax.ppermute(x_edges[0], "yx", self.swap_route(1))
            corner = lax.ppermute(corners[0], "yx", self.swap_route(3))
            return [y], [x], [corner]
        y = [lax.ppermute(y_edges[k], "yx", self.route((1, -1)[1 - k], 0)) for k in (1, 0)]
        x = [lax.ppermute(x_edges[k], "yx", self.route(0, (1, -1)[1 - k])) for k in (1, 0)]
        corner = [
            lax.ppermute(corners[2 * k + j], "yx", self.route((1, -1)[1 - k], (1, -1)[1 - j]))
            for k in (1, 0)
            for j in (1, 0)
        ]
        return y, x, corner


def swap_depth(outer, inner):
    size = lax.axis_size("gz")
    routes = [[], []]
    for low in range(size - 1):
        routes[low % 2] += [(low, low + 1), (low + 1, low)]
    return lax.ppermute(outer, "gz", routes[1]), lax.ppermute(inner, "gz", routes[0])


class Riders:
    STEPS = (("cand", 1), ("gz", 2), ("gz", 1))

    def __init__(self, rows):
        self.tiles = 27 * rows // 16
        self.fits = (
            lax.axis_size("yx") == 4
            and lax.axis_size("cand") % 2 == 0
            and lax.axis_size("gz") % 4 == 0
            and self.tiles >= 8
        )
        self.size = -(-self.tiles // 8) if self.fits else 0

    @classmethod
    def mine(cls):
        return sum(
            lax.axis_index(axis) // mask % 2 * 2**k for k, (axis, mask) in enumerate(cls.STEPS)
        )


def rotate_shards(piece):
    tiles = lax.axis_size("yx")
    return [
        lax.ppermute(piece, "yx", [(i, (i + k) % tiles) for i in range(tiles)]) for k in range(1, tiles)
    ]


def swap(block, axis, mask):
    return lax.ppermute(block, axis, [(i, i ^ mask) for i in range(lax.axis_size(axis))])


def share(stats):
    return lax.all_to_all(stats, PART, 0, 0)


def call(kernel, outs, scratch, *arrays, flops=0, nbytes=0, in_hbm=0, out_hbm=False):
    vmem, hbm = (pl.BlockSpec(memory_space=space) for space in (pltpu.VMEM, pltpu.HBM))
    far, near = arrays[:in_hbm], arrays[in_hbm:]
    far = [pltpu.with_memory_space_constraint(array, pltpu.HBM) for array in far]
    return pl.pallas_call(
        kernel,
        out_shape=[jax.ShapeDtypeStruct(shape, dtype) for shape, dtype in outs],
        in_specs=[hbm] * len(far) + [vmem] * len(near),
        out_specs=[hbm if out_hbm else vmem] * len(outs),
        scratch_shapes=[pltpu.VMEM(*entry) if isinstance(entry, tuple) else entry for entry in scratch],
        compiler_params=pltpu.CompilerParams(vmem_limit_bytes=VMEM_BYTES),
        cost_estimate=pl.CostEstimate(flops=flops, bytes_accessed=nbytes, transcendentals=0),
    )(*far, *near)


def start_kernel(ny, nx, size, x_in, w_in, d_in, y_out, x_out, corners, x, w, lines, sems):
    edge = x_in.shape[0]
    f32, bf16 = jnp.float32, jnp.bfloat16
    above, left = Square().low_sides()
    chunks = 4
    planes = edge // chunks
    first = [
        pltpu.make_async_copy(
            x_in.at[pl.ds(k * planes, planes)],
            x.at[pl.ds(1 + k * planes, planes), pl.ds(1, edge)],
            sems.at[k],
        )
        for k in range(chunks)
    ]
    later = []
    if size:
        at = jnp.minimum(Riders.mine() * size, d_in.shape[0] - size)
        for k, (out, begin) in enumerate(((y_out, edge), (x_out, edge), (corners, 1))):
            later.append(
                pltpu.make_async_copy(
                    d_in.at[pl.ds(at, size)], out.at[0, pl.ds(begin, size)], sems.at[chunks + k]
                )
            )
    later.append(pltpu.make_async_copy(w_in, w, sems.at[chunks + 3]))
    for copy in first + later:
        copy.start()
    x[0] = jnp.zeros(x.shape[1:], bf16)
    x[edge + 1] = jnp.zeros(x.shape[1:], bf16)
    blank = jnp.zeros((edge,) + x.shape[2:], bf16)
    x[1 : edge + 1, 0] = blank
    x[1 : edge + 1, edge + 1] = blank
    flat = lines.reshape(nx * edge * edge * 8, 128)
    part = planes * edge
    for k in range(chunks):
        first[k].wait()
        at, here = pl.ds(k * planes, planes), pl.ds(1 + k * planes, planes)
        for i in range(ny):
            row = jnp.where(above[i], 1, edge)
            y_out[i, at] = x[here, row]
        for j in range(nx):
            low = x[here, 1 : edge + 1, 0:8].astype(f32).reshape(part, 8, 128)
            high = x[here, 1 : edge + 1, edge - 8 : edge].astype(f32).reshape(part, 8, 128)
            high = pltpu.roll(high, 1, 1)
            kept = jnp.where(left[j], low, high)
            lines[j, k * part : k * part + part] = kept
            begin = (j * edge * edge + k * part) * 8
            column = flat[pl.ds(begin, part, stride=8), :]
            x_out[j, at] = column.astype(bf16).reshape(planes, edge, 128)
    for i in range(ny):
        for j in range(nx):
            begin = j * edge * edge * 8
            low = flat[pl.ds(begin, edge, stride=8 * edge), :]
            high = flat[pl.ds(begin + 8 * (edge - 1), edge, stride=8 * edge), :]
            kept = jnp.where(above[i], low, high)
            corners[i * nx + j, 0] = kept.astype(bf16)
    for copy in later:
        copy.wait()


def face_kernel(ny, nx, size, x, y_halos, x_halos, corners, outer, inner, *riders):
    edge = outer.shape[1]
    wide = edge + ny + nx
    odd = lax.axis_index("gz") % 2
    far = edge - 3
    for face, at in ((outer, odd * far), (inner, (1 - odd) * far)):
        for k in range(3):
            row = k * wide
            face[row : row + edge] = x[1 + at + k, 1 : edge + 1]
            for i in range(ny):
                face[row + edge + i] = y_halos[i, at + k]
            for j in range(nx):
                face[row + edge + ny + j] = x_halos[j, at + k]
        for k in range(ny * nx):
            face[3 * wide + k] = corners[k, 0]
    for k in range(inner.shape[0], outer.shape[0]):
        outer[k] = corners[0, 0]
    if size:
        riders[0][0] = x_halos[0, edge : edge + size]
        riders[0][1] = y_halos[0, edge : edge + size]
        riders[0][2] = corners[0, 1 : 1 + size]
        riders[0][3] = corners[0, 1 : 1 + size]


def spread_taps(weight, taps):
    for tap in range(27):
        row, lane = tap // 3 * 128, tap % 3 * 128
        taps[row : row + 128, lane : lane + 128] = weight[tap]


def pair_taps(weight, pairs):
    for dz in range(3):
        for line in range(4):
            row = (dz * 4 + line) * 128
            for out in range(2):
                lane = out * 128
                if 0 <= line - out < 3:
                    block = weight[dz * 9 + (line - out) * 3 + 2]
                else:
                    block = jnp.zeros((128, 128), pairs.dtype)
                pairs[row : row + 128, lane : lane + 128] = block


def join_x(wide, edge):
    place = lax.broadcasted_iota(jnp.int32, wide.shape[:2] + (128,), 1)
    after = jnp.where(place > 0, pltpu.roll(wide[:, :, :128], 1, 1), 0.0)
    before = jnp.where(place < edge - 1, pltpu.roll(wide[:, :, 256:], edge - 1, 1), 0.0)
    return wide[:, :, 128:256] + after + before


def convolve(grid, count, taps, pairs, put):
    edge = grid.shape[2]
    planes = min(count, 4)
    rows = planes * edge * edge
    place = lax.broadcasted_iota(jnp.int32, (planes * edge, edge, 128), 1)
    halved = grid.reshape(grid.shape[0], edge // 2 + 1, 2, edge, 128)
    for z in range(0, count, planes):
        left = jnp.concatenate(
            [
                grid[z + dz : z + dz + planes, dy : dy + edge].reshape(rows, 128)
                for dz in range(3)
                for dy in range(3)
            ],
            axis=1,
        )
        wide = jnp.dot(left, taps[:, 0:256], preferred_element_type=jnp.float32)
        wide = wide.reshape(planes * edge, edge, 256)
        left = jnp.concatenate(
            [
                halved[z + dz : z + dz + planes, line // 2 : line // 2 + edge // 2, line % 2].reshape(
                    rows // 2, 128
                )
                for dz in range(3)
                for line in range(4)
            ],
            axis=1,
        )
        two = jnp.dot(left, pairs[...], preferred_element_type=jnp.float32)
        two = two.reshape(planes * edge // 2, edge, 256)
        two = jnp.stack([two[:, :, :128], two[:, :, 128:]], axis=1).reshape(planes * edge, edge, 128)
        after = jnp.where(place > 0, pltpu.roll(wide[:, :, :128], 1, 1), 0.0)
        before = jnp.where(place < edge - 1, pltpu.roll(two, edge - 1, 1), 0.0)
        new = wide[:, :, 128:256] + after + before
        put(z, new.reshape(planes, edge, edge, 128))


def conv_kernel(deep_in, x, weight, act, taps, pairs, deep_weight, sem):
    copy = pltpu.make_async_copy(deep_in, deep_weight, sem)
    copy.start()
    edge = act.shape[0]
    spread_taps(weight, taps)
    pair_taps(weight, pairs)

    def put(z, new):
        act[z : z + new.shape[0]] = new

    convolve(x, edge, taps, pairs, put)
    copy.wait()


def y_terms(line, low, taps):
    planes, edge = line.shape[0] - 2, line.shape[1]
    left = jnp.concatenate(
        [line[dz : dz + planes].reshape(planes * edge, 128) for dz in range(3)], axis=1
    )
    start = jnp.where(low, 0, 256)
    right = jnp.concatenate(
        [taps[pl.ds(pl.multiple_of(start + dz * 384, 128), 128), :] for dz in range(3)], axis=0
    )
    wide = jnp.dot(left, right, preferred_element_type=jnp.float32)
    return join_x(wide.reshape(planes, edge, 384), edge)


def x_terms(column, taps):
    planes, edge = column.shape[0] - 2, column.shape[1] - 16
    lines = [column[:, 7 + dy : 7 + dy + edge].astype(jnp.bfloat16) for dy in range(3)]
    left = jnp.concatenate(
        [line[dz : dz + planes].reshape(planes * edge, 128) for dz in range(3) for line in lines],
        axis=1,
    )
    right = jnp.concatenate([taps[:, 0:128], taps[:, 256:384]], axis=1)
    both = jnp.dot(left, right, preferred_element_type=jnp.float32)
    return both[:, :128], both[:, 128:]


def fill_column(column, at, voxels, ends, above):
    count, edge = voxels.shape[:2]
    rows = edge + 16
    lines = column.reshape(column.shape[0] * rows, 128)
    column[at : at + count, 8 : 8 + edge] = voxels.astype(jnp.float32)
    for i, end in enumerate(ends):
        first = last = end.astype(jnp.float32)
        if len(ends) == 1:
            first, last = jnp.where(above[0], first, 0.0), jnp.where(above[0], 0.0, last)
        if len(ends) == 1 or i == 0:
            lines[pl.ds(at * rows + 7, count, stride=rows), :] = first
        if len(ends) == 1 or i == 1:
            lines[pl.ds(at * rows + 8 + edge, count, stride=rows), :] = last


def add_column(act, terms, j, nx, low):
    planes, edge = act.shape[:2]
    flat = act.reshape(planes * edge * edge, 128)
    first, last = terms
    if nx == 1:
        first, last = jnp.where(low, first, 0.0), jnp.where(low, 0.0, last)
    if nx == 1 or j == 0:
        flat[pl.ds(0, planes * edge, stride=edge), :] += first
    if nx == 1 or j == 1:
        flat[pl.ds(edge - 1, planes * edge, stride=edge), :] += last


def moments(planes):
    count, edge = planes.shape[:2]
    zero = jnp.zeros((8, 128), jnp.float32)

    def sum_step(k, carry):
        return carry + jnp.sum(planes[k].reshape(edge * 2, 8, 128), axis=0)

    mean = lax.fori_loop(0, count, sum_step, zero, unroll=True) / (count * edge * edge // 8)

    def spread_step(k, carry):
        off = planes[k].reshape(edge * 2, 8, 128) - mean
        return carry + jnp.sum(off * off, axis=0)

    return mean, lax.fori_loop(0, count, spread_step, zero, unroll=True)


def side_kernel(ny, nx, own, y_halos, x_halos, corners, taps, inner, ends, stats, act, column):
    edge = own.shape[0]
    act[0] = jnp.zeros(act.shape[1:], jnp.float32)
    act[edge + 1] = jnp.zeros(act.shape[1:], jnp.float32)
    act[1 : edge + 1] = own[...]
    above, left = Square().low_sides()
    blank = jnp.zeros((2, edge, 128), jnp.bfloat16)
    for i in range(ny):
        line = jnp.concatenate([blank, y_halos[i, 0:edge], blank], axis=0)
        act[:, jnp.where(above[i], 0, edge - 1)] += y_terms(line, above[i], taps)
    for j in range(nx):
        column[...] = jnp.zeros(column.shape, jnp.float32)
        fill_column(
            column, 2, x_halos[j, 0:edge], [corners[i * nx + j, 0] for i in range(ny)], above
        )
        add_column(act, x_terms(column, taps), j, nx, left[j])
    inner[...] = act[2:edge]
    ends[0:2] = act[0:2]
    ends[2:4] = act[edge : edge + 2]
    mean, spread = moments(act.at[2:edge])
    stats[0:8] = mean
    stats[8:16] = spread


def add_face(ny, nx, behind, face, x, taps, pairs, ends, three, grid, column, beyond=True):
    edge = x.shape[2]
    wide_face = edge + ny + nx
    f32 = jnp.float32
    above, left = Square().low_sides()
    end = pl.ds(jnp.where(behind, 3, 0), 3)
    three[...] = ends[end]
    blank = jnp.zeros(grid.shape[:1] + grid.shape[2:], grid.dtype)
    grid[:, 0] = blank
    grid[:, edge + 1] = blank
    first = jnp.where(behind, 1, 0)
    for k in range(3):
        grid[first + k, 1 : edge + 1] = face[k * wide_face : k * wide_face + edge]
    grid[jnp.where(behind, 0, 3), 1 : edge + 1] = x[jnp.where(behind, edge, 1), 1 : edge + 1]

    def put(z, new):
        three[pl.ds(first + z, new.shape[0])] += new

    if beyond:
        convolve(grid, 2, taps, pairs, put)
    beside = jnp.where(behind, 1, 2)
    lines = [grid[beside, dy : dy + edge].reshape(edge * edge, 128) for dy in range(3)]
    rows = taps[pl.ds(pl.multiple_of(jnp.where(behind, 768, 0), 128), 384), :]
    wide = jnp.dot(jnp.concatenate(lines, axis=1), rows, preferred_element_type=f32)
    three[jnp.where(behind, 0, 2)] += join_x(wide.reshape(edge, edge, 384), edge)

    def five(voxels):
        gap = jnp.zeros((2,) + voxels.shape[1:], voxels.dtype)
        return jnp.where(
            behind,
            jnp.concatenate([gap, voxels], axis=0),
            jnp.concatenate([voxels, gap], axis=0),
        )

    def rim(row):
        return five(jnp.stack([face[k * wide_face + edge + row] for k in range(3)]).astype(f32))

    for i in range(ny):
        terms = y_terms(rim(i).astype(jnp.bfloat16), above[i], taps)
        three[:, jnp.where(above[i], 0, edge - 1)] += terms
    for j in range(nx):
        column[...] = jnp.zeros(column.shape, f32)
        tails = []
        for i in range(ny):
            tile = face[3 * wide_face + i * nx + j].astype(f32)
            tails.append(five(jnp.where(behind, tile[:3], tile[edge - 3 :])))
        fill_column(column, 0, rim(ny + j), tails, above)
        add_column(three, x_terms(column, taps), j, nx, left[j])
    ends[end] = three[...]


def inner_kernel(ny, nx, x, partial, face, taps, pairs, ends, three, grid, column):
    blank = jnp.zeros(ends.shape[1:], jnp.float32)
    ends[0] = blank
    ends[1:5] = partial[...]
    ends[5] = blank
    behind = lax.axis_index("gz") % 2 == 0
    add_face(ny, nx, behind, face, x, taps, pairs, ends, three, grid, column)


def outer_kernel(ny, nx, x, middle_stats, ends, face, taps, pairs, act, stats, three, grid, column):
    edge = x.shape[2]
    act[...] = ends[...]
    behind = lax.axis_index("gz") % 2 == 1
    add_face(ny, nx, behind, face, x, taps, pairs, act, three, grid, column, beyond=False)
    mean, spread = moments(act.at[2:4])
    few, many = edge * edge // 4, (edge - 2) * edge * edge // 8
    middle_mean, middle_spread = middle_stats[0:8], middle_stats[8:16]
    off = middle_mean - mean
    part = few / (few + many)
    spread = spread + middle_spread + (many * part) * (off * off)
    put_stats(stats, middle_mean - part * off, spread, few + many)


def beyond_kernel(ny, nx, x, ends, face, taps, pairs, act, grid):
    edge = x.shape[2]
    wide_face = edge + ny + nx
    depth_at = lax.axis_index("gz")
    behind = depth_at % 2 == 1
    act[...] = ends[...]

    @pl.when(jnp.where(behind, depth_at < lax.axis_size("gz") - 1, depth_at > 0))
    def _():
        blank = jnp.zeros(grid.shape[:1] + grid.shape[2:], grid.dtype)
        grid[:, 0] = blank
        grid[:, edge + 1] = blank
        first = jnp.where(behind, 1, 0)
        for k in range(3):
            grid[first + k, 1 : edge + 1] = face[k * wide_face : k * wide_face + edge]
        own = jnp.where(behind, edge, 1)
        grid[jnp.where(behind, 0, 3), 1 : edge + 1] = x[own, 1 : edge + 1]

        def put(z, new):
            act[pl.ds(jnp.where(behind, 4, 0) + z, new.shape[0])] += new

        convolve(grid, 2, taps, pairs, put)


def merge(mean, spread, rows, other_mean, other_spread):
    off = mean - other_mean
    return 0.5 * (mean + other_mean), spread + other_spread + (0.5 * rows) * (off * off)


def put_stats(stats, mean, spread, rows):
    for step in (1, 2, 4):
        others = pltpu.roll(mean, step, 0), pltpu.roll(spread, step, 0)
        mean, spread = merge(mean, spread, float(rows * step), *others)
    both = jnp.concatenate([mean[0:1], spread[0:1]], axis=0)
    stats[...] = jnp.broadcast_to(both[None], stats.shape)


def read_stats(stats, rows):
    devices, _, channels = stats.shape
    shape = (8, channels)
    means = [jnp.broadcast_to(stats[k, 0:1, :], shape) for k in range(devices)]
    spreads = [jnp.broadcast_to(stats[k, 1:2, :], shape) for k in range(devices)]
    mean = functools.reduce(jnp.add, means) / devices
    spread = functools.reduce(jnp.add, spreads)
    spread = spread + rows * functools.reduce(jnp.add, [(m - mean) * (m - mean) for m in means])
    rows = rows * devices
    lane = lax.broadcasted_iota(jnp.int32, shape, 1)
    step = 1
    while step < channels // GROUPS:
        low = jnp.bitwise_and(lane, step) == 0
        others = [
            jnp.where(low, pltpu.roll(row, channels - step, 1), pltpu.roll(row, step, 1))
            for row in (mean, spread)
        ]
        mean, spread = merge(mean, spread, rows, *others)
        rows, step = 2.0 * rows, 2 * step
    return mean, lax.rsqrt(spread / rows + EPSILON)


def silu_of_double(h):
    return h + h * jnp.tanh(h)


def norm_kernel(ny, nx, inner, ends, stats, gain, offset, out, pooled, *refs):
    y_edges, x_edges, corners, half = refs
    depth, edge = inner.shape[0] + 6, inner.shape[1]
    deep, deep_depth = edge // 2, depth // 2
    f32, bf16 = jnp.float32, jnp.bfloat16
    above, left = Square().low_sides()
    depth_at = lax.axis_index("gz")
    mean, scale = read_stats(stats, float(edge**3))
    scale = scale * (0.5 * gain[...])
    shift = 0.5 * offset[...]
    for k in range(deep_depth):
        value = [
            ends[z] if z < 3 else inner[z - 3] if z < depth - 3 else ends[z - depth + 6]
            for z in (2 * k, 2 * k + 1)
        ]
        value = jnp.stack(value).reshape(edge * edge // 4, 8, 128)
        value = silu_of_double((value - mean) * scale + shift)
        value = value.reshape(2, edge, edge, 128).astype(bf16)
        if 0 < k < deep_depth - 1:
            out[2 * k - 2 : 2 * k] = value
        value = value.astype(f32)
        value = (value[0] + value[1]).reshape(deep, 2, edge, 128)
        half[k] = (value[:, 0] + value[:, 1]).reshape(deep * edge, 128)
        lines = half.at[k]
        pair = lines[pl.ds(0, deep * deep, stride=2), :] + lines[pl.ds(1, deep * deep, stride=2), :]
        pair = (pair * 0.125).astype(bf16).astype(f32).reshape(deep, deep, 128)
        if k == 0 or k == deep_depth - 1:
            inside = depth_at > 0 if k == 0 else depth_at < lax.axis_size("gz") - 1
            pair = jnp.where(inside, pair, 0.0)
        pooled[k] = pair
    lines = pooled.reshape(deep_depth * deep * deep, 128)
    rows = deep_depth * deep
    first_x = lines[pl.ds(0, rows, stride=deep), :]
    last_x = lines[pl.ds(deep - 1, rows, stride=deep), :]
    first_y, last_y = (pooled[:, y].reshape(rows, 128) for y in (0, deep - 1))
    ends = []
    for y in (0, deep - 1):
        for x in (0, deep - 1):
            ends.append(lines[pl.ds(y * deep + x, deep_depth, stride=deep * deep), :])
    if ny == 1:
        above, left = above[0], left[0]
        y_edges[0] = jnp.where(above, first_y, last_y).astype(bf16)
        x_edges[0] = jnp.where(left, first_x, last_x).astype(bf16)
        corners[0, 0:deep_depth] = jnp.where(
            above, jnp.where(left, ends[0], ends[1]), jnp.where(left, ends[2], ends[3])
        )
    else:
        y_edges[0], y_edges[1] = first_y.astype(bf16), last_y.astype(bf16)
        x_edges[0], x_edges[1] = first_x.astype(bf16), last_x.astype(bf16)
        for k in range(4):
            corners[k, 0:deep_depth] = ends[k]


def stack_kernel(*refs):
    out = refs[-1]
    for k in range(out.shape[0]):
        out[k] = refs[k][: out.shape[1], : out.shape[2]]


def stack(*arrays, part=None):
    vmem = pl.BlockSpec(memory_space=pltpu.VMEM)
    shape = (part or arrays[0].shape[:2]) + arrays[0].shape[2:]
    return pl.pallas_call(
        stack_kernel,
        out_shape=jax.ShapeDtypeStruct((len(arrays),) + shape, arrays[0].dtype),
        in_specs=[vmem] * len(arrays),
        out_specs=vmem,
        compiler_params=pltpu.CompilerParams(vmem_limit_bytes=VMEM_BYTES),
    )(*arrays)


def place_weights(own, held, out):
    tile = lax.axis_index("yx")
    out[tile] = own[...]
    if len(held) == 1:
        pieces, others, size = held[0].shape[:3]
        for piece in range(pieces):
            at = jnp.minimum(jnp.bitwise_xor(Riders.mine(), piece) * size, own.shape[0] - size)
            for k in range(others):
                out[jnp.bitwise_xor(tile, k + 1), pl.ds(at, size)] = held[0][piece, k]
    else:
        for k, shard in enumerate(held):
            out[lax.rem(tile + len(held) - k, len(held) + 1)] = shard[...]


def tap_rows(weight, taps):
    per = weight.shape[1] // 27
    return jnp.concatenate(
        [weight[:, pl.ds(tap * per, per)].reshape(-1, 128) for tap in taps], axis=1
    )


def dot_rows(left, right):
    return lax.dot_general(
        left, right, (((1,), (1,)), ((), ())), preferred_element_type=jnp.float32
    )


def deep_kernel(pooled, own, *refs):
    *held, act, weight, grid, packed = refs
    depth, deep = pooled.shape[0], pooled.shape[1]
    place_weights(own, held, weight)
    grid[...] = jnp.zeros(grid.shape, jnp.float32)
    grid[:, 1 : deep + 1, 8:16] = pooled[...]
    for dx in range(3):
        plane = grid[:, :, 7 + dx : 15 + dx]
        for y in range(deep + 1):
            both = jnp.concatenate([plane[:, y], plane[:, y + 1]], axis=1)
            packed[:, y // 2, y % 2, :, dx * 128 : dx * 128 + 128] = both.astype(jnp.bfloat16)
    rows = deep**3
    total = None
    for dz in range(3):
        left = jnp.concatenate(
            [
                packed[dz : dz + deep, dy // 2 : dy // 2 + deep // 2, dy % 2].reshape(rows, 384)
                for dy in range(3)
            ],
            axis=1,
        )
        term = dot_rows(left, tap_rows(weight, range(dz * 9, dz * 9 + 9)))
        total = term if total is None else total + term
    for half in range(act.shape[0]):
        act[half] = total[:, half * 128 : half * 128 + 128]


def deep_rim_kernel(ny, nx, own, x_halos, y_halos, corners, weight, act, stats, line):
    depth, deep = line.shape[0], line.shape[1] - 16
    halves = act.shape[0]
    f32 = jnp.float32
    square = deep * deep
    above, left = Square().low_sides()
    act[...] = own[...]
    flat = line.reshape(depth * line.shape[1], 128)

    def shifts():
        return jnp.concatenate(
            [
                line[dz : dz + deep, 7 + d : 7 + d + deep].reshape(square, 128).astype(jnp.bfloat16)
                for dz in range(3)
                for d in range(3)
            ],
            axis=1,
        )

    for i in range(ny):
        line[...] = jnp.zeros(line.shape, f32)
        line[:, 8 : 8 + deep] = y_halos[i].astype(f32).reshape(depth, deep, 128)
        for j in range(nx):
            end = corners[i * nx + j, 0:depth]
            first, last = jnp.where(left[j], end, 0.0), jnp.where(left[j], 0.0, end)
            if nx == 1 or j == 0:
                flat[pl.ds(7, depth, stride=line.shape[1]), :] = first
            if nx == 1 or j == 1:
                flat[pl.ds(8 + deep, depth, stride=line.shape[1]), :] = last
        tap = jnp.where(above[i], 0, 6)
        taps = [tap + dz * 9 + dx for dz in range(3) for dx in range(3)]
        terms = dot_rows(shifts(), tap_rows(weight, taps))
        for half in range(halves):
            rows = act.at[half].reshape(deep, deep, deep, 128)
            term = terms[:, half * 128 : half * 128 + 128].reshape(deep, deep, 128)
            rows[:, jnp.where(above[i], 0, deep - 1)] += term
    for j in range(nx):
        line[...] = jnp.zeros(line.shape, f32)
        line[:, 8 : 8 + deep] = x_halos[j].astype(f32).reshape(depth, deep, 128)
        tap = jnp.where(left[j], 0, 2)
        taps = [tap + dz * 9 + dy * 3 for dz in range(3) for dy in range(3)]
        terms = dot_rows(shifts(), tap_rows(weight, taps))
        first, last = jnp.where(left[j], terms, 0.0), jnp.where(left[j], 0.0, terms)
        for half in range(halves):
            lanes, rows = slice(half * 128, half * 128 + 128), act.at[half]
            if nx == 1 or j == 0:
                rows[pl.ds(0, square, stride=deep), :] += first[:, lanes]
            if nx == 1 or j == 1:
                rows[pl.ds(deep - 1, square, stride=deep), :] += last[:, lanes]

    rows = deep**3 // 8
    means, spreads = [], []
    for half in range(halves):
        total = act[half].reshape(rows, 8, 128)
        means.append(jnp.sum(total, axis=0) / rows)
        off = total - means[-1]
        spreads.append(jnp.sum(off * off, axis=0))
    put_stats(stats, *(jnp.concatenate(part, axis=1) for part in (means, spreads)), rows)


def final_kernel(act, stats, gain, offset, up, mid, out, wide, held, sems):
    edge = mid.shape[0]
    deep = edge // 2
    f32 = jnp.float32
    mean, scale = read_stats(stats, float(deep**3))
    scale = scale * (0.5 * gain[...])
    shift = 0.5 * offset[...]
    planes = 2
    size = planes * deep * deep
    copies = []
    for k in range(0, deep, planes):
        at = slice(k * deep * deep, k * deep * deep + size)
        value = jnp.concatenate([act[half, at] for half in range(act.shape[0])], axis=1)
        value = value.reshape(size // 8, 8, -1)
        value = silu_of_double((value - mean) * scale + shift)
        value = value.reshape(size, -1).astype(jnp.bfloat16)
        lifted = jnp.dot(value, up[...], preferred_element_type=f32)
        lines = wide.at[k // planes]
        lines[pl.ds(0, size, stride=2), :] = lifted
        lines[pl.ds(1, size, stride=2), :] = lifted
        add = lines[...].reshape(planes, 1, deep, 1, edge, 128)
        at = pl.ds(2 * k, 2 * planes)
        old = mid[at].astype(f32).reshape(planes, 2, deep, 2, edge, 128)
        held[at] = (old + add).astype(jnp.bfloat16).reshape(2 * planes, edge, edge, 128)
        copy = pltpu.make_async_copy(held.at[at], out.at[at], sems.at[k // planes])
        copy.start()
        copies.append(copy)
    for copy in copies:
        copy.wait()


def body(
    features, conv_weight, gain_mid, offset_mid, deep_weight, gain_deep, offset_deep, up_weight
):
    f32, bf16 = jnp.float32, jnp.bfloat16
    edge, channels = features.shape[0], features.shape[3]
    deep = edge // 2
    deep_channels = gain_deep.shape[0]
    square = Square()
    tiles = square.tiles
    devices = lax.axis_size("gz") * tiles
    ny, nx = (len(sides) for sides in square.low_sides())
    riders = Riders(deep_weight.shape[4])

    own = jnp.moveaxis(deep_weight, 4, 3).reshape(-1, 16, channels)
    conv_weight = conv_weight.reshape(27, channels, channels)
    *edges, field, conv_weight = call(
        functools.partial(start_kernel, ny, nx, riders.size),
        [
            ((ny, edge + riders.size, edge, channels), bf16),
            ((nx, edge + riders.size, edge, channels), bf16),
            ((ny * nx, 1 + riders.size, edge, channels), bf16),
            ((edge + 2, edge + 2, edge, channels), bf16),
            (conv_weight.shape, bf16),
        ],
        [((nx, edge * edge, 8, channels), f32), pltpu.SemaphoreType.DMA((8,))],
        features,
        conv_weight,
        own,
        nbytes=5 << 20,
        in_hbm=3,
    )
    halos = square.halos(*(list(piece) for piece in edges))
    conv_flops = 54 * channels * channels * edge**3
    act, taps, pairs, own = call(
        conv_kernel,
        [
            ((edge, edge, edge, channels), f32),
            ((9 * channels, 3 * channels), bf16),
            ((12 * channels, 2 * channels), bf16),
            (own.shape, bf16),
        ],
        [pltpu.SemaphoreType.DMA],
        own,
        field,
        conv_weight,
        flops=conv_flops,
        nbytes=6 << 20,
        in_hbm=1,
    )
    (y, x, corner), act = lax.optimization_barrier((halos, act))
    y, x, corner = jnp.stack(y), jnp.stack(x), jnp.stack(corner)
    face = ((3 * (edge + ny + nx) + ny * nx, edge, channels), bf16)
    held = [((4, riders.size, 16, channels), bf16)] if riders.size else []
    outer, inner, *held = call(
        functools.partial(face_kernel, ny, nx, riders.size),
        [((face[0][0] + 2,) + face[0][1:], bf16), face] + held,
        [],
        field,
        y,
        x,
        corner,
    )
    outer, inner = swap_depth(outer, inner)
    if riders.size:
        held = held[0][None]
        other = swap(held, *riders.STEPS[0])
    else:
        held = rotate_shards(own)
    six = ((6, edge, edge, channels), f32)
    column = (edge + 16, channels)
    middle, partial, stats = call(
        functools.partial(side_kernel, ny, nx),
        [
            ((edge - 2, edge, edge, channels), f32),
            ((4, edge, edge, channels), f32),
            ((16, channels), f32),
        ],
        [((edge + 2, edge, edge, channels), f32), ((edge + 4,) + column, f32)],
        act,
        y,
        x,
        corner,
        taps,
    )
    room = [
        ((3, edge, edge, channels), f32),
        ((4, edge + 2, edge, channels), bf16),
        ((5,) + column, f32),
    ]
    (ends,) = call(
        functools.partial(inner_kernel, ny, nx), [six], room, field, partial, inner, taps, pairs
    )
    ends, stats = call(
        functools.partial(outer_kernel, ny, nx),
        [six, ((devices, 2, channels), f32)],
        room,
        field,
        stats,
        ends,
        outer,
        taps,
        pairs,
    )
    if riders.size:
        stats, other = lax.optimization_barrier((stats, other))
        held = stack(held, other, part=(1, 3)).reshape((2, 3) + held.shape[2:])
        other = swap(held, *riders.STEPS[1])
    (ends,) = call(
        functools.partial(beyond_kernel, ny, nx),
        [six],
        room[1:2],
        field,
        ends,
        outer,
        taps,
        pairs,
        flops=conv_flops,
        nbytes=4 << 20,
    )
    stats, ends = lax.optimization_barrier((stats, ends))
    stats = share(stats)
    if riders.size:
        stats, other = lax.optimization_barrier((stats, other))
        held = stack(held, other).reshape((-1,) + held.shape[1:])
        other = swap(held, *riders.STEPS[2])
        held = [stack(held, other).reshape((-1,) + held.shape[1:])]
    out, pooled, *edges = call(
        functools.partial(norm_kernel, ny, nx),
        [
            ((edge, edge, edge, channels), bf16),
            ((deep + 2, deep, deep, channels), f32),
            ((ny, (deep + 2) * deep, channels), bf16),
            ((nx, (deep + 2) * deep, channels), bf16),
            ((ny * nx, 16, channels), f32),
        ],
        [((deep + 2, deep * edge, channels), f32)],
        middle,
        ends,
        stats,
        gain_mid.reshape(1, channels),
        offset_mid.reshape(1, channels),
        flops=20 * channels * edge**3,
        nbytes=3 << 20,
    )
    y, x, corner = square.halos(*(list(piece) for piece in edges))
    halves = ((deep_channels // 128, deep**3, 128), f32)
    deep_act, weight = call(
        deep_kernel,
        [halves, ((tiles,) + own.shape, bf16)],
        [
            ((deep + 2, deep + 2, 24, channels), f32),
            ((deep + 2, deep // 2 + 1, 2, 16, 3 * channels), bf16),
        ],
        pooled,
        own,
        *held,
        flops=54 * channels * deep_channels * deep**3,
        nbytes=4 << 20,
    )
    deep_act, stats = call(
        functools.partial(deep_rim_kernel, ny, nx),
        [halves, ((devices, 2, deep_channels), f32)],
        [((deep + 2, 24, channels), f32)],
        deep_act,
        jnp.stack(x),
        jnp.stack(y),
        jnp.stack(corner),
        weight,
        flops=4 * channels * deep_channels * deep**3,
        nbytes=3 << 20,
    )
    stats = share(stats)
    (decoded,) = call(
        final_kernel,
        [((edge, edge, edge, channels), bf16)],
        [
            ((deep // 2, 4 * deep * deep, channels), f32),
            ((edge, edge, edge, channels), bf16),
            pltpu.SemaphoreType.DMA((deep // 2,)),
        ],
        deep_act,
        stats,
        gain_deep.reshape(1, deep_channels),
        offset_deep.reshape(1, deep_channels),
        up_weight,
        out,
        flops=4 * deep_channels * channels * deep**3,
        nbytes=3 << 20,
        out_hbm=True,
    )
    return decoded


def solution(mesh):
    placed = (
        P(("cand", "gz"), "yx", None, None),
        P(),
        P(),
        P(),
        P(None, None, None, None, "yx"),
        P(),
        P(),
        P(),
    )
    return jax.shard_map(
        body,
        mesh=mesh,
        in_specs=placed,
        out_specs=P(("cand", "gz"), "yx", None, None),
        check_vma=False,
    )
```
